32 devices in a mesh: section: 2 (over core), batch: 16 (over z, y, x).
Axes of the slice: x: 2, y: 2, z: 4, core: 2. Of those that a mesh axis runs over, the one named last changes fastest.
Arguments:
- frames: bfloat16 [4, 84, 84, 4096], P(None, None, None, 'batch'), may hold values from -6 to 6
- destination: int32 [4096], P('batch'), may hold values from 0 to 15, as said below
- options: int32 [3, 4096], P(None, 'batch'), may hold values from 0 to 17
- depth: int32 [4096], P('batch'), may hold values from 1 to 3
- targets: float32 [3, 3, 4096], P(None, None, 'batch'), may hold values from -6 to 6
- conv_one: bfloat16 [256, 16], replicated, may hold values from -0.375 to 0.375
- bias_one: float32 [16], replicated, may hold values from -3 to 3
- conv_two: bfloat16 [256, 32], replicated, may hold values from -0.375 to 0.375
- bias_two: float32 [32], replicated, may hold values from -3 to 3
- linear_w: bfloat16 [2592, 128], replicated, may hold values from -0.125 to 0.125
- linear_b: float32 [128], replicated, may hold values from -3 to 3
- branch_w: bfloat16 [18, 128, 128], replicated, may hold values from -0.5 to 0.5
- branch_b: float32 [18, 128], replicated, may hold values from -3 to 3
- head_w: bfloat16 [128, 2], replicated, may hold values from -0.5 to 0.5
- head_b: float32 [2], replicated, may hold values from -3 to 3
- value_w: bfloat16 [128, 128], replicated, may hold values from -0.5 to 0.5
- value_b: float32 [128], replicated, may hold values from -3 to 3
- out_w: bfloat16 [128, 1], replicated, may hold values from -0.5 to 0.5
- out_b: float32 [1], replicated, may hold values from -3 to 3
Outputs:
- loss: float32 [], replicated
- frames_grad: float32 [4, 84, 84, 4096], P('section', None, None, 'batch')
- conv_one_grad: float32 [256, 16], replicated
- bias_one_grad: float32 [16], replicated
- conv_two_grad: float32 [256, 32], replicated
- bias_two_grad: float32 [32], replicated
- linear_w_grad: float32 [2592, 128], replicated
- linear_b_grad: float32 [128], replicated
- branch_w_grad: float32 [18, 128, 128], replicated
- branch_b_grad: float32 [18, 128], replicated
- head_w_grad: float32 [128, 2], replicated
- head_b_grad: float32 [2], replicated
- value_w_grad: float32 [128, 128], replicated
- value_b_grad: float32 [128], replicated
- out_w_grad: float32 [128, 1], replicated
- out_b_grad: float32 [1], replicated
The draws below stay inside these ranges and needn't reach their ends.
Inputs may be any that keep to these rules, and one draw needn't show every extreme that they name: `destination`: among the 256 frames of each batch index, every planner index appears exactly 16 times.
All inputs are finite; a program needn't handle non-finite values.
Results may differ from the reference program's by a relative error of at most 0.013.
Values may be sent and summed in bfloat16 or wider, within the bound.
No kernel may reach another device: no remote copies, remote signals or barrier semaphores. Data moves between devices by JAX's collectives and lax.ppermute only.
A program may use at most 256 MiB of HBM per device.

```python
import jax
import jax.numpy as jnp
from jax import lax

D = 128
HV = 128
K1 = 16
K2 = 32
STACK = 4
G1 = 20
OPTIONS = 18
DEPTH = 3
FR_DEV = 256
IMG = 84
G2 = 9
C_PAIR = 16
FRAMES = 4096
N_BATCH = 16


def draw_destination(key, part):
    key = jax.random.fold_in(key, 11)
    block_keys = jax.random.split(key, FRAMES // FR_DEV)

    def one_block(block_key):
        return (jax.random.permutation(block_key, FR_DEV) // C_PAIR).astype(jnp.int32)
    return jax.vmap(one_block)(block_keys).reshape(FRAMES).astype(jnp.int32)


def place_ends(values, stream_key, low, high):
    longest = values.shape.index(max(values.shape))
    spots = []
    for shift in (0, 1):
        where = [jax.random.randint(jax.random.fold_in(stream_key, axis), (), 0, length) for axis, length in enumerate(values.shape)]
        where[longest] = (where[longest] + shift) % values.shape[longest]
        spots.append(tuple(where))
    return values.at[spots[0]].set(low).at[spots[1]].set(high)


def steps_of(stream_key, dims, shards, least, top_value):
    def one(axis_at, blocks):
        draws = jax.random.uniform(jax.random.fold_in(jax.random.fold_in(stream_key, 6), axis_at), (blocks,), jnp.float32, least / len(shards), top_value / len(shards))
        return jnp.repeat(jnp.exp(draws), dims[axis_at] // blocks).reshape((-1,) + (1,) * (len(dims) - axis_at - 1))

    gain = one(*shards[0])
    for cut in shards[1:]:
        gain = gain * one(*cut)
    return gain


def normal_values(key, extent, scale, limit, cuts=(), kind=jnp.bfloat16):
    values = jax.random.normal(key, extent, jnp.float32) * scale
    if len(cuts) > 0:
        values = steps_of(key, extent, cuts, -0.22, 0.18) * values
    return jnp.clip(values, min=-limit, max=limit).astype(kind)


def setup_inputs(seed: int = 0) -> dict:
    seeds = jax.random.split(jax.random.key(seed), 20)
    return {
        "frames": normal_values(seeds[0], (STACK, IMG, IMG, FRAMES), 1.0, 6.0, ((3, 16),)),
        "destination": draw_destination(jax.random.fold_in(seeds[19], 71), 0),
        "options": place_ends(jax.random.randint(seeds[2], (DEPTH, FRAMES), 0, OPTIONS), jax.random.fold_in(seeds[2], 1), 0, OPTIONS - 1).astype(jnp.int32),
        "depth": place_ends(jax.random.randint(seeds[3], (FRAMES,), 1, 4), jax.random.fold_in(seeds[3], 1), 1, 3).astype(jnp.int32),
        "targets": normal_values(seeds[4], (3, DEPTH, FRAMES), 1.0, 6.0, ((2, 16),), jnp.float32),
        "conv_one": normal_values(seeds[5], (64 * STACK, K1), (64 * STACK) ** -0.5, 0.375),
        "bias_one": normal_values(seeds[6], (K1,), 0.5, 3.0, (), jnp.float32),
        "conv_two": normal_values(seeds[7], (16 * K1, K2), (16 * K1) ** -0.5, 0.375),
        "bias_two": normal_values(seeds[8], (K2,), 0.5, 3.0, (), jnp.float32),
        "linear_w": normal_values(seeds[9], (G2 * G2 * K2, D), (G2 * G2 * K2) ** -0.5, 0.125),
        "linear_b": normal_values(seeds[10], (D,), 0.5, 3.0, (), jnp.float32),
        "branch_w": normal_values(seeds[11], (OPTIONS, D, D), D ** -0.5, 0.5),
        "branch_b": normal_values(seeds[12], (OPTIONS, D), 0.5, 3.0, (), jnp.float32),
        "head_w": normal_values(seeds[13], (D, 2), D ** -0.5, 0.5),
        "head_b": normal_values(seeds[14], (2,), 0.5, 3.0, (), jnp.float32),
        "value_w": normal_values(seeds[15], (D, HV), D ** -0.5, 0.5),
        "value_b": normal_values(seeds[16], (HV,), 0.5, 3.0, (), jnp.float32),
        "out_w": normal_values(seeds[17], (HV, 1), HV ** -0.5, 0.5),
        "out_b": normal_values(seeds[18], (1,), 0.5, 3.0, (), jnp.float32),
    }


@jax.custom_vjp
def low(v):
    return lax.optimization_barrier(v.astype(jnp.bfloat16)).astype(jnp.float32)

@jax.custom_vjp
def low_back(v):
    return v

def low_keep(v):
    return (low(v), None)

def low_pass(kept, grad):
    return (grad,)

def back_keep(v):
    return (v, None)

def back_low(kept, grad):
    return (low(grad),)
low.defvjp(low_keep, low_pass)
low_back.defvjp(back_keep, back_low)
full_precision = lax.Precision.HIGHEST

def patches_first(x):
    frame_count = x.shape[0]
    channels = x.shape[1]
    grid_side = x.shape[2] // 4 - 1
    blocks = x.reshape(frame_count, channels, grid_side + 1, 4, grid_side + 1, 4)
    stacked = jnp.stack([jnp.stack([blocks[:, :, a:a + grid_side, :, b:b + grid_side, :] for b in (0, 1)], 0) for a in (0, 1)], 0)
    return stacked.transpose(2, 4, 6, 3, 0, 5, 1, 7).reshape(frame_count, grid_side * grid_side, channels * 64)

def patches_second(h):
    frame_count = h.shape[0]
    grid_half = h.shape[1] // 2
    inner_side = grid_half - 1
    channels = h.shape[3]
    blocks = h.reshape(frame_count, grid_half, 2, grid_half, 2, channels)
    stacked = jnp.stack([jnp.stack([blocks[:, a:a + inner_side, :, b:b + inner_side, :, :] for b in (0, 1)], 0) for a in (0, 1)], 0)
    return stacked.transpose(2, 3, 5, 0, 4, 1, 6, 7).reshape(frame_count, inner_side * inner_side, 16 * channels)

def encode(frames_in, conv_one, bias_one, conv_two, bias_two, linear_w, linear_b):
    frame_count = frames_in.shape[0]
    patch_one = patches_first(frames_in)
    pre_one = jnp.einsum('fpk,kc->fpc', patch_one, conv_one, precision=full_precision) + bias_one
    hidden_one = low(jax.nn.softplus(low_back(pre_one)))
    patch_two = patches_second(hidden_one.reshape(frame_count, G1, G1, K1))
    pre_two = jnp.einsum('fpk,kc->fpc', patch_two, conv_two, precision=full_precision) + bias_two
    hidden_two = low(jax.nn.softplus(low_back(pre_two))).reshape(frame_count, G2 * G2 * K2)
    pre_three = jnp.dot(hidden_two, linear_w, precision=full_precision) + linear_b
    return low_back(low(jax.nn.softplus(low_back(pre_three))))

def plan_loss(states, options_in, depth_in, targets_in, branch_w, branch_b, head_w, head_b, value_w, value_b, out_w, out_b):
    current = states
    loss_total = jnp.zeros((), jnp.float32)
    labels = jnp.arange(OPTIONS, dtype=jnp.int32)
    for tree_level in range(DEPTH):
        rounded = low(current)
        pre_branch = jnp.einsum('ik,okn->ion', rounded, branch_w, precision=full_precision) + branch_b
        moved_state = current[:, None, :] + jax.nn.silu(low_back(pre_branch))
        moved_low = low(moved_state)
        head_out = low_back(jnp.einsum('iok,kc->ioc', moved_low, head_w, precision=full_precision) + head_b)
        reward = head_out[:, :, 0]
        discount = jax.nn.sigmoid(head_out[:, :, 1])
        hidden = low(jax.nn.silu(low_back(jnp.einsum('iok,kh->ioh', moved_low, value_w, precision=full_precision) + value_b)))
        values = low_back(jnp.einsum('ioh,hc->ioc', hidden, out_w, precision=full_precision)[:, :, 0] + out_b[0])
        quality = reward + discount * values
        top_q = lax.optimization_barrier(jnp.max(quality, axis=1))
        planned_value = top_q + jnp.log(lax.optimization_barrier(jnp.sum(jnp.exp(quality - top_q[:, None]), axis=1)))
        picked = (options_in[tree_level][:, None] == labels[None, :]).astype(jnp.float32)
        live_mask = (depth_in > tree_level).astype(jnp.float32)
        reward_gap = live_mask * (lax.optimization_barrier(jnp.sum(picked * reward, axis=1)) - targets_in[0, tree_level])
        discount_gap = live_mask * (lax.optimization_barrier(jnp.sum(picked * discount, axis=1)) - targets_in[1, tree_level])
        plan_gap = live_mask * (planned_value - targets_in[2, tree_level])
        loss_total = loss_total + 0.5 * jnp.sum(reward_gap * reward_gap + discount_gap * discount_gap + plan_gap * plan_gap)
        current = lax.optimization_barrier(jnp.sum(picked[:, :, None] * moved_state, axis=1))
    return loss_total

def slot_of(destination):
    grid_dest = destination.reshape(N_BATCH, FR_DEV)
    onehot = (grid_dest[:, :, None] == jnp.arange(N_BATCH, dtype=jnp.int32)[None, None, :]).astype(jnp.int32)
    before = jnp.cumsum(onehot, axis=1) - onehot
    rank_in = lax.optimization_barrier(jnp.sum(before * onehot, axis=2))
    source = jnp.arange(N_BATCH, dtype=jnp.int32)[:, None]
    return (grid_dest * FR_DEV + source * C_PAIR + rank_in).reshape(FRAMES).astype(jnp.int32)

def reference(frames, destination, options, depth, targets, conv_one, bias_one, conv_two, bias_two, linear_w, linear_b, branch_w, branch_b, head_w, head_b, value_w, value_b, out_w, out_b):
    frames_f = frames.astype(jnp.float32).transpose(3, 0, 1, 2)
    encoder_f = tuple((p.astype(jnp.float32) for p in (conv_one, bias_one, conv_two, bias_two, linear_w, linear_b)))
    planner_f = tuple((p.astype(jnp.float32) for p in (branch_w, branch_b, head_w, head_b, value_w, value_b, out_w, out_b)))
    slots = slot_of(destination)
    anchor = jnp.zeros((FRAMES,), jnp.int32).at[slots].set(jnp.arange(FRAMES, dtype=jnp.int32))
    option_blocks = options.reshape(DEPTH, N_BATCH, FR_DEV).transpose(1, 0, 2)
    depth_blocks = depth.reshape(N_BATCH, FR_DEV)
    target_blocks = targets.astype(jnp.float32).reshape(3, DEPTH, N_BATCH, FR_DEV).transpose(2, 0, 1, 3)

    def whole(frames_all, encoder_all, planner_all):
        frame_blocks = frames_all.reshape(N_BATCH, FR_DEV, STACK, IMG, IMG)

        def encode_block(frame_block):
            return encode(frame_block, *encoder_all)
        states = lax.map(jax.checkpoint(encode_block), frame_blocks).reshape(FRAMES, D)
        planned = states[anchor].reshape(N_BATCH, FR_DEV, D)

        def plan_block(pieces):
            return plan_loss(pieces[0], pieces[1], pieces[2], pieces[3], *planner_all)
        losses = lax.map(jax.checkpoint(plan_block), (planned, option_blocks, depth_blocks, target_blocks))
        return jnp.sum(losses)
    loss, pullback = jax.vjp(whole, frames_f, encoder_f, planner_f)
    frames_grad, encoder_grads, planner_grads = pullback(jnp.ones((), jnp.float32))
    frames_grad = frames_grad.transpose(1, 2, 3, 0)
    return (loss, frames_grad, encoder_grads[0], encoder_grads[1], encoder_grads[2], encoder_grads[3], encoder_grads[4], encoder_grads[5], planner_grads[0], planner_grads[1], planner_grads[2], planner_grads[3], planner_grads[4], planner_grads[5], planner_grads[6], planner_grads[7])
```

```python
import functools
import math

import jax
import jax.numpy as jnp
from jax import lax
from jax.experimental import pallas as pl
from jax.experimental.pallas import tpu as pltpu
from jax.sharding import PartitionSpec as P

BF16 = jnp.bfloat16
F32 = jnp.float32
EXACT = lax.Precision.HIGHEST
LANES = 128
VMEM_BYTES = 48 * 1024 * 1024
TILE = 16
REACH = 5
STEP = 3


def dot(a, b, precision=None):
    return jnp.dot(a, b, preferred_element_type=F32, precision=precision)


def dot_rows(a, b, precision=None):
    return lax.dot_general(
        a, b, (((0,), (0,)), ((), ())), preferred_element_type=F32, precision=precision
    )


def dot_lanes(a, b, precision=None):
    return lax.dot_general(
        a, b, (((1,), (1,)), ((), ())), preferred_element_type=F32, precision=precision
    )


def iota(shape, axis):
    return lax.broadcasted_iota(jnp.int32, shape, axis)


def column(row):
    n = row.shape[1]
    wide = jnp.broadcast_to(row, (n, n))
    return jnp.sum(jnp.where(iota((n, n), 0) == iota((n, n), 1), wide, 0.0), axis=1, keepdims=True)


def row_of(col):
    n = col.shape[0]
    wide = jnp.broadcast_to(col, (n, n))
    return jnp.sum(jnp.where(iota((n, n), 0) == iota((n, n), 1), wide, 0.0), axis=0, keepdims=True)


def soft(x):
    e = jnp.exp(-jnp.abs(x))
    r = 1.0 / (1.0 + e)
    return jnp.maximum(x, 0.0) + jnp.log(1.0 + e), jnp.where(x >= 0.0, r, e * r)


def silu_pair(x):
    s = 1.0 / (1.0 + jnp.exp(-x))
    act = x * s
    return act, s + act * (1.0 - s)


def tap_map(half, place):
    tap, pix = iota((256, 256), 0), iota((256, 256), 1)
    hit = (
        ((tap >> 6) == (pix >> 6))
        & (((tap >> 3) & 7) == ((pix >> 4) & 3) + 4 * half)
        & ((tap & 7) == (pix & 15) - 4 * (place - 1))
    )
    return hit.astype(F32)


def encode_kernel(
    section,
    frames,
    w1,
    b1,
    w2,
    b2,
    lw,
    lb,
    h1,
    s1,
    h2,
    s2,
    enc,
    s3,
    band,
    w2t,
    bias1,
    bias2,
    tail,
    held,
):
    g = pl.program_id(0)
    side = h1.shape[1]
    tiles = frames.shape[2] // TILE
    rest = frames.shape[2] - tiles * TILE
    k1, k2 = w1.shape[1], w2.shape[1]
    reach_rows = REACH * k1

    @pl.when(g == 0)
    def _():
        for half in range(2):
            for place in range(REACH):
                at = half * reach_rows + place * k1
                taps = dot_rows(w1[...], tap_map(half, place).astype(BF16))
                band[at : at + k1, :] = taps.astype(BF16)
        eye = (iota((256, 256), 0) == iota((256, 256), 1)).astype(F32).astype(BF16)
        w2t[...] = dot_rows(w2[...], eye).astype(BF16)
        bias1[...] = jnp.broadcast_to(column(b1[...]), bias1.shape)
        bias2[...] = jnp.broadcast_to(column(b2[...]), bias2.shape)
        tail[...] = jnp.zeros_like(tail)
        held[...] = jnp.zeros_like(held)

    for r in range(STEP):
        rows = slice(4 * r, 4 * r + 4)
        tail[r, :, :, 0:rest, :] = frames[:, rows, tiles * TILE :, :]
        low, high = {}, {}
        done = 0
        for pair in range((tiles + 1) // 2):
            cut = []
            for j in (2 * pair, 2 * pair + 1):
                if j < tiles:
                    cut.append(frames[:, rows, j * TILE : (j + 1) * TILE, :].reshape(256, LANES))
                else:
                    cut.append(tail[r].reshape(256, LANES))
            got = dot(band[...], jnp.concatenate(cut, axis=1))
            for k in range(2):
                for place in range(REACH):
                    x = 4 * (2 * pair + k) - 1 + place
                    if 0 <= x < side:
                        at = place * k1
                        one = got[at : at + k1, k * LANES : (k + 1) * LANES]
                        two = got[
                            reach_rows + at : reach_rows + at + k1, k * LANES : (k + 1) * LANES
                        ]
                        low[x] = low[x] + one if x in low else one
                        high[x] = high[x] + two if x in high else two
            ready = min(8 * pair + 7, side)
            for x in range(done, ready):
                value, slope = soft(held[x] + high[x] + bias1[...])
                held[x] = low[x]
                h1[STEP * g + r, x] = value.astype(BF16)
                s1[r, x] = slope.astype(BF16)
            done = ready

    @pl.when(g == pl.num_programs(0) - 1)
    def _():
        inner = side // 2 - 1
        row_len = inner * k2

        def one_row(y, carry):
            for first in range(0, inner, 2):
                xs = [x for x in (first, first + 1) if x < inner]
                cut = [
                    h1[pl.ds(2 * y + 1, 4), 2 * x : 2 * x + 4].reshape(256, LANES) for x in xs
                ]
                patch = cut[0] if len(cut) == 1 else jnp.concatenate(cut, axis=1)
                got = dot(w2t[...], patch)
                for k, x in enumerate(xs):
                    value, slope = soft(got[:, k * LANES : (k + 1) * LANES] + bias2[...])
                    at = pl.ds(pl.multiple_of(y * row_len + x * k2, k2), k2)
                    h2[at, :] = value.astype(BF16)
                    s2[at, :] = slope.astype(BF16)
            return carry

        lax.fori_loop(0, inner, one_row, 0)
        value, slope = soft(dot_rows(lw[...], h2[...]) + column(lb[...]))
        enc[...] = value.astype(BF16)
        s3[...] = slope


def plan_kernel(
    section,
    destination,
    slots,
    enc,
    s3,
    h2,
    branch_w,
    branch_b,
    head_w,
    head_b,
    value_w,
    value_b,
    out_w,
    out_b,
    big,
    small,
    g3,
    bwt,
    bb,
    vht,
    vhw,
    vb,
    ow,
    mine,
    dbr,
    dval,
    low,
    hid,
    gb,
    states,
    pick,
    rew,
    disc,
    val,
    soft_q,
    gaps,
    rows_g,
    vgrad,
    outacc,
    vbacc,
    rowacc,
    *,
    per_pair,
):
    width = enc.shape[0]
    options = branch_w.shape[0]
    depth = states.shape[0] - 1
    pairs = options // 2
    two = 2 * width
    sec = section[0]

    dest = destination[...].astype(F32)
    count = dest.shape[1]
    own = jnp.where(sec == 0, dest[:, :LANES], dest[:, LANES:])
    others = jnp.transpose(jnp.broadcast_to(dest, (LANES, count)))
    index = iota((count, LANES), 1) + sec * LANES
    earlier = (others == own) & (iota((count, LANES), 0) < index)
    rank = jnp.sum(earlier.astype(F32), axis=0, keepdims=True)
    bucket = own * float(per_pair) + rank
    chosen = (iota((count, LANES), 0).astype(F32) == bucket).astype(F32)
    mine[...] = dot(slots[...], chosen, EXACT)

    for o in range(options):
        at = slice(o * width, (o + 1) * width)
        bwt[at, :] = jnp.transpose(branch_w[o].astype(F32)).astype(BF16)
        bb[at, :] = jnp.broadcast_to(column(branch_b[o : o + 1, :]), (width, LANES))
    vht[...] = jnp.zeros_like(vht)
    vht[0:width, :] = jnp.transpose(value_w[...].astype(F32)).astype(BF16)
    pick_head = (iota((16, 2), 0) == iota((16, 2), 1)).astype(F32).astype(BF16)
    vht[width : width + 16, :] = dot_lanes(pick_head, head_w[...]).astype(BF16)
    vhw[:, 0:width] = value_w[...]
    vhw[:, width:] = dot_lanes(head_w[...], pick_head).astype(BF16)
    vb[...] = jnp.broadcast_to(column(value_b[...]), (width, LANES))
    ow[...] = jnp.broadcast_to(out_w[...].astype(F32), (width, LANES))

    vgrad[...] = jnp.zeros_like(vgrad)
    outacc[...] = jnp.zeros_like(outacc)
    vbacc[...] = jnp.zeros_like(vbacc)
    rowacc[...] = jnp.zeros_like(rowacc)
    states[0] = enc[...].astype(F32)

    def wide(ref):
        return jnp.concatenate([ref[...], ref[...]], axis=1)

    def ahead(level, carry):
        labels = iota((options, LANES), 0).astype(F32)
        picked = (labels == mine[pl.ds(level, 1), :]).astype(F32)
        pick[level] = picked
        states[level + 1] = jnp.zeros((width, LANES), F32)

        def one_pair(t, inside):
            at = pl.ds(pl.multiple_of(t * two, two), two)
            state = states[level]
            act, slope = silu_pair(dot(bwt[at, :], state.astype(BF16)) + bb[at, :])
            dbr[level, at, :] = slope
            left = state + act[:width]
            right = state + act[width:]
            states[level + 1] += (
                pick[level, pl.ds(2 * t, 1), :] * left + pick[level, pl.ds(2 * t + 1, 1), :] * right
            )
            both = jnp.concatenate([left.astype(BF16), right.astype(BF16)], axis=1)
            low[level, t] = both
            got = dot(vht[...], both)
            act, slope = silu_pair(got[:width] + wide(vb))
            dval[level, t] = slope
            hidden = act.astype(BF16)
            hid[level, t] = hidden
            worth = jnp.sum(hidden.astype(F32) * wide(ow), axis=0, keepdims=True)
            for k in range(2):
                spot = pl.ds(2 * t + k, 1)
                span = slice(k * LANES, (k + 1) * LANES)
                val[spot, :] = worth[:, span]
                rew[spot, :] = got[width : width + 1, span]
                disc[spot, :] = got[width + 1 : width + 2, span]
            return inside

        lax.fori_loop(0, pairs, one_pair, 0, unroll=3)
        reward = rew[...] + head_b[:, 0:1]
        discount = jax.nn.sigmoid(disc[...] + head_b[:, 1:2])
        value = val[...] + out_b[...]
        quality = reward + discount * value
        top = jnp.max(quality, axis=0, keepdims=True)
        shifted = jnp.exp(quality - top)
        total = jnp.sum(shifted, axis=0, keepdims=True)
        soft_q[level] = shifted / total
        rows_g[level, 0] = discount
        rows_g[level, 1] = value
        live = (mine[pl.ds(depth, 1), :] > level.astype(F32)).astype(F32)

        def target(kind):
            return mine[pl.ds(depth + 1 + kind * depth + level, 1), :]

        gaps[level, 0:1, :] = live * (jnp.sum(picked * reward, axis=0, keepdims=True) - target(0))
        gaps[level, 1:2, :] = live * (jnp.sum(picked * discount, axis=0, keepdims=True) - target(1))
        gaps[level, 2:3, :] = live * (top + jnp.log(total) - target(2))
        return carry

    lax.fori_loop(0, depth, ahead, 0)

    states[depth] = jnp.zeros((width, LANES), F32)

    def behind(turn, carry):
        level = depth - 1 - turn
        picked = pick[level]
        grad_quality = gaps[level, 2:3, :] * soft_q[level]
        discount = rows_g[level, 0]
        value = rows_g[level, 1]
        head_one = (picked * gaps[level, 0:1, :] + grad_quality).astype(BF16).astype(F32)
        head_two = picked * gaps[level, 1:2, :] + grad_quality * value
        head_two = (head_two * discount * (1.0 - discount)).astype(BF16).astype(F32)
        grad_value = (grad_quality * discount).astype(BF16).astype(F32)
        rew[...] = head_one
        disc[...] = head_two
        val[...] = grad_value
        rowacc[0] += head_one
        rowacc[1] += head_two
        rowacc[2] += grad_value
        grad_next = states[depth]
        states[depth] = jnp.zeros((width, LANES), F32)

        def one_pair(t, inside):
            at = pl.ds(pl.multiple_of(t * two, two), two)

            def across(ref):
                return jnp.concatenate(
                    [ref[pl.ds(2 * t, 1), :], ref[pl.ds(2 * t + 1, 1), :]], axis=1
                )

            worth = across(val)
            grad_hidden = worth * wide(ow)
            grad_pre = (grad_hidden * dval[level, t]).astype(BF16)
            outacc[...] += hid[level, t].astype(F32) * worth
            vbacc[...] += grad_pre.astype(F32)
            line = iota((16, two), 0)
            heads = jnp.where(line == 0, across(rew), jnp.where(line == 1, across(disc), 0.0))
            stacked = jnp.concatenate([grad_pre, heads.astype(BF16)], axis=0)
            vgrad[...] += dot_lanes(stacked, low[level, t])
            moved = dot(vhw[...], stacked)
            left = moved[:, :LANES] + pick[level, pl.ds(2 * t, 1), :] * grad_next
            right = moved[:, LANES:] + pick[level, pl.ds(2 * t + 1, 1), :] * grad_next
            grad_branch = jnp.concatenate([left, right], axis=0) * dbr[level, at, :]
            grad_branch = grad_branch.astype(BF16)
            gb[level, at, :] = grad_branch
            weights = jnp.concatenate([branch_w[2 * t], branch_w[2 * t + 1]], axis=1)
            states[depth] += left + right + dot(weights, grad_branch)
            return inside

        lax.fori_loop(0, pairs, one_pair, 0, unroll=3)
        return carry

    lax.fori_loop(0, depth, behind, 0)

    linear_rows = h2.shape[0]
    ones = jnp.ones((16, depth * LANES), F32).astype(BF16)
    rounded = jnp.concatenate([states[level].astype(BF16) for level in range(depth)], axis=1)
    rounded = jnp.concatenate([rounded, ones], axis=0)
    small[...] = jnp.zeros_like(small)

    def one_option(o, carry):
        at = pl.ds(pl.multiple_of(o * width, width), width)
        grads = jnp.concatenate([gb[level, at, :] for level in range(depth)], axis=1)
        got = dot_lanes(rounded, grads)
        big[pl.ds(pl.multiple_of(linear_rows + o * width, 32), width), :] = got[:width].astype(
            big.dtype
        )
        small[pl.ds(o, 1), :] = got[width : width + 1]
        return carry

    lax.fori_loop(0, options, one_option, 0, unroll=2)
    after = linear_rows + options * width
    big[after : after + width, :] = jnp.transpose(vgrad[0:width, :]).astype(big.dtype)

    grad_three = (states[depth].astype(BF16).astype(F32) * s3[...]).astype(BF16)
    g3[...] = grad_three
    chunk = linear_rows // 9

    def one_chunk(i, carry):
        at = pl.ds(pl.multiple_of(i * chunk, chunk), chunk)
        big[at, :] = dot_lanes(h2[at, :], grad_three).astype(big.dtype)
        return carry

    lax.fori_loop(0, 9, one_chunk, 0, unroll=3)

    at = options
    small[at : at + 1, :] = row_of(jnp.sum(vbacc[...], axis=1, keepdims=True))
    small[at + 1 : at + 2, :] = row_of(jnp.sum(outacc[...], axis=1, keepdims=True))
    small[at + 2 : at + 4, :] = vgrad[width : width + 2, :]
    small[at + 4 : at + 5, :] = row_of(jnp.sum(grad_three.astype(F32), axis=1, keepdims=True))
    gap = gaps[...]
    loss = 0.5 * jnp.sum(jnp.sum(gap * gap, axis=0), axis=0, keepdims=True)
    lines = [loss] + [jnp.sum(rowacc[k], axis=0, keepdims=True) for k in range(3)]
    lane = iota((1, LANES), 1)
    scalars = jnp.zeros((1, LANES), F32)
    for k, line in enumerate(lines):
        scalars = jnp.where(lane == k, jnp.sum(line, axis=1, keepdims=True), scalars)
    small[at + 5 : at + 6, :] = scalars


def back_kernel(g3, lw, s2, h1, s1, w2, g1, c2, sums, g2, t2, b1acc, b2acc):
    side = h1.shape[1]
    k1, k2 = h1.shape[2], w2.shape[1]
    inner = side // 2 - 1
    row_len = inner * k2
    tap, pix = iota((256, LANES), 0), iota((256, LANES), 1)
    for yrel in range(2):
        for p in range(3):
            hit = (
                ((tap & 15) == (pix & 15))
                & ((tap >> 6) == (pix >> 6) + 2 * (1 - yrel))
                & (((tap >> 4) & 3) == ((pix >> 4) & 3) + 2 - 2 * p)
            )
            at = (yrel * 3 + p) * k2
            t2[:, at : at + k2] = dot_rows(hit.astype(F32).astype(BF16), w2[...]).astype(BF16)
    g2[0] = jnp.zeros(g2.shape[1:], BF16)
    g2[inner + 1] = jnp.zeros(g2.shape[1:], BF16)
    g1[0] = jnp.zeros(g1.shape[1:], BF16)
    g1[side + 1] = jnp.zeros(g1.shape[1:], BF16)
    b1acc[...] = jnp.zeros_like(b1acc)
    b2acc[...] = jnp.zeros_like(b2acc)
    c2[...] = jnp.zeros_like(c2)

    def out_row(y, carry):
        at = pl.ds(pl.multiple_of(y * row_len, row_len), row_len)
        grad = dot(lw[at, :], g3[...]) * s2[at, :].astype(F32)
        grad = grad.astype(BF16).reshape(inner, k2, LANES)
        g2[y + 1] = grad
        b2acc[...] += jnp.sum(grad.astype(F32), axis=0)
        grads = jnp.concatenate([grad[x] for x in range(inner)], axis=1)
        patches = jnp.concatenate(
            [h1[pl.ds(2 * y + 1, 4), 2 * x : 2 * x + 4].reshape(256, LANES) for x in range(inner)],
            axis=1,
        )
        c2[...] += dot_lanes(grads, patches)
        return carry

    lax.fori_loop(0, inner, out_row, 0)

    def in_rows(b, carry):
        zero = jnp.zeros((k2, LANES), BF16)
        cut = []
        for j in range(side // 4):
            pieces = []
            for yrel in range(2):
                for p in range(3):
                    x = 2 * j - 1 + p
                    pieces.append(g2[b + yrel, x] if 0 <= x < inner else zero)
            cut.append(jnp.concatenate(pieces, axis=0))
        got = dot(t2[...], jnp.concatenate(cut, axis=1))
        total = b1acc[...]
        for u in range(2):
            for j in range(side // 4):
                part = got[u * 64 : (u + 1) * 64, j * LANES : (j + 1) * LANES]
                slope = s1[2 * b + u + 1, 4 * j : 4 * j + 4].astype(F32)
                grad = (part.reshape(4, k1, LANES) * slope).astype(BF16)
                g1[2 * b + u + 1, 4 * j : 4 * j + 4] = grad
                total = total + jnp.sum(grad.astype(F32), axis=0)
        b1acc[...] = total
        return carry

    lax.fori_loop(0, side // 2, in_rows, 0)
    sums[...] = jnp.zeros_like(sums)
    sums[0:1, 0:k1] = row_of(jnp.sum(b1acc[...], axis=1, keepdims=True))
    sums[1:2, 0:k2] = row_of(jnp.sum(b2acc[...], axis=1, keepdims=True))


def first_kernel(section, frames, g1, c2, sums, small, packed, acc, tail):
    g = pl.program_id(0)
    side, k1 = g1.shape[1], g1.shape[2]
    k2 = c2.shape[0]
    tiles = frames.shape[2] // TILE
    rest = frames.shape[2] - tiles * TILE

    @pl.when(g == 0)
    def _():
        acc[...] = jnp.zeros_like(acc)
        tail[...] = jnp.zeros_like(tail)

    zero = jnp.zeros((k1, LANES), BF16)
    total = acc[...]
    for r in range(STEP):
        rows = slice(4 * r, 4 * r + 4)
        tail[r, :, :, 0:rest, :] = frames[:, rows, tiles * TILE :, :]
        pixels, grads = [], []
        for j in range(tiles + 1):
            if j < tiles:
                pixels.append(frames[:, rows, j * TILE : (j + 1) * TILE, :].reshape(256, LANES))
            else:
                pixels.append(tail[r].reshape(256, LANES))
            pieces = []
            for half in range(2):
                for place in range(REACH):
                    x = 4 * j - 1 + place
                    pieces.append(g1[STEP * g + r + 1 - half, x] if 0 <= x < side else zero)
            grads.append(jnp.concatenate(pieces, axis=0))
        total = total + dot_lanes(
            jnp.concatenate(grads, axis=1), jnp.concatenate(pixels, axis=1)
        )
    acc[...] = total

    @pl.when(g == pl.num_programs(0) - 1)
    def _():
        grad = jnp.zeros((k1, 256), F32)
        for half in range(2):
            for place in range(REACH):
                at = (half * REACH + place) * k1
                grad = grad + dot_lanes(acc[at : at + k1, :], tap_map(half, place), EXACT)
        at = small.shape[0]
        packed[0:at, :] = small[...]
        for part, size in ((c2[...], k2), (grad, k1)):
            for half in range(2):
                packed[at : at + size, :] = part[:, half * LANES : (half + 1) * LANES]
                at += size
        packed[at : at + 8, :] = sums[...]


def pixels_kernel(section, w1, mine, other, out, band):
    g = pl.program_id(0)
    side, k1 = mine.shape[1], mine.shape[2]
    channels = out.shape[0]
    cols = 8
    reach = 3
    sec = section[0]
    size = STEP * channels * 4 * cols

    @pl.when(g == 0)
    def _():
        tap, pix = iota((256, size), 0), iota((256, size), 1)
        r = pix // (channels * 4 * cols)
        c = (pix // (4 * cols)) % channels + sec * channels
        u4 = (pix // cols) % 4
        xx = pix % cols
        for yrel in range(STEP + 1):
            for p in range(reach):
                hit = (
                    ((tap >> 6) == c)
                    & (((tap >> 3) & 7) == 4 * (r + 1 - yrel) + u4)
                    & ((tap & 7) == xx + 4 - 4 * p)
                )
                at = (yrel * reach + p) * k1
                band[:, at : at + k1] = dot_rows(hit.astype(F32).astype(BF16), w1[...]).astype(BF16)

    zero = jnp.zeros((k1, 2 * LANES), BF16)
    here = pl.ds(pl.multiple_of(sec * LANES, LANES), LANES)
    there = pl.ds(pl.multiple_of((1 - sec) * LANES, LANES), LANES)
    for j in range((out.shape[2] + cols - 1) // cols):
        pieces = []
        for yrel in range(STEP + 1):
            for p in range(reach):
                x = 2 * j - 1 + p
                if 0 <= x < side:
                    y = STEP * g + yrel
                    pieces.append(jnp.concatenate([mine[y, x], other[y, x]], axis=1))
                else:
                    pieces.append(zero)
        got = dot(band[...], jnp.concatenate(pieces, axis=0))
        keep = min(cols, out.shape[2] - j * cols)
        for r in range(STEP):
            for c in range(channels):
                for u in range(4):
                    at = ((r * channels + c) * 4 + u) * cols
                    span = slice(j * cols, j * cols + keep)
                    out[c, 4 * r + u, span, here] = got[at : at + keep, :LANES]
                    out[c, 4 * r + u, span, there] = got[at : at + keep, LANES:]


def unpack_kernel(
    big, packed, loss, c1, b1, c2, b2, lw, lb, bw, bb, hw, hb, vw, vb, ow, ob
):
    width = lw.shape[1]
    options = bw.shape[0]
    k1, k2 = c1.shape[1], c2.shape[1]
    rows = lw.shape[0]
    lw[...] = big[0:rows, :].astype(F32)
    for o in range(options):
        bw[o] = big[rows + o * width : rows + (o + 1) * width, :].astype(F32)
    at = rows + options * width
    vw[...] = big[at : at + width, :].astype(F32)
    at = options
    bb[...] = packed[0:at, :]
    vb[...] = packed[at : at + 1, :]
    ow[...] = column(packed[at + 1 : at + 2, :])
    hw[...] = jnp.concatenate(
        [column(packed[at + 2 : at + 3, :]), column(packed[at + 3 : at + 4, :])], axis=1
    )
    lb[...] = packed[at + 4 : at + 5, :]
    scalars = packed[at + 5 : at + 6, :]
    loss[...] = scalars[:, 0:1]
    hb[...] = scalars[:, 1:3]
    ob[...] = scalars[:, 3:4]
    at = 32
    for ref, size in ((c2, k2), (c1, k1)):
        for half in range(2):
            part = packed[at : at + size, :]
            ref[half * LANES : (half + 1) * LANES, :] = jnp.transpose(part)
            at += size
    b1[...] = packed[at : at + 1, 0:k1]
    b2[...] = packed[at + 1 : at + 2, 0:k2]


def whole(shape):
    zeros = (0,) * len(shape)
    return pl.BlockSpec(shape, lambda *_: zeros)


def params():
    return pltpu.CompilerParams(vmem_limit_bytes=VMEM_BYTES)


def shape_of(*shape, dtype=F32):
    return jax.ShapeDtypeStruct(shape, dtype)


def cost(flops, moved, transcendentals=0):
    return pl.CostEstimate(
        flops=int(flops), bytes_accessed=int(moved), transcendentals=int(transcendentals)
    )


def encode(section, frames, w1, b1, w2, b2, lw, lb):
    stack, img = frames.shape[0], frames.shape[1]
    blocks = img // 4
    side = blocks - 1
    k1, k2, width = w1.shape[1], w2.shape[1], lw.shape[1]
    flat = lw.shape[0]
    outs = (
        shape_of(blocks, side, k1, LANES, dtype=BF16),
        shape_of(blocks, side, k1, LANES, dtype=BF16),
        shape_of(flat, LANES, dtype=BF16),
        shape_of(flat, LANES, dtype=BF16),
        shape_of(width, LANES, dtype=BF16),
        shape_of(width, LANES),
    )
    weights = (w1, b1[None, :], w2, b2[None, :], lw, lb[None, :])
    out_specs = [whole(o.shape) for o in outs]
    out_specs[1] = pl.BlockSpec((STEP, side, k1, LANES), lambda g, s: (g, 0, 0, 0))
    return pl.pallas_call(
        encode_kernel,
        grid_spec=pltpu.PrefetchScalarGridSpec(
            num_scalar_prefetch=1,
            grid=(blocks // STEP,),
            in_specs=[
                pl.BlockSpec((stack, 4 * STEP, img, LANES), lambda g, s: (0, g, 0, s[0])),
                *[whole(w.shape) for w in weights],
            ],
            out_specs=out_specs,
            scratch_shapes=[
                pltpu.VMEM((2 * REACH * k1, 256), BF16),
                pltpu.VMEM((k2, 256), BF16),
                pltpu.VMEM((k1, LANES), F32),
                pltpu.VMEM((k2, LANES), F32),
                pltpu.VMEM((STEP, stack, 4, TILE, LANES), BF16),
                pltpu.VMEM((side, k1, LANES), F32),
            ],
        ),
        out_shape=outs,
        compiler_params=params(),
        cost_estimate=cost(2 * 128 * 5.2e6, 1.3e7, 2.5e6),
        name="encode",
    )(section, frames, *weights)


def plan(section, destination, slots, enc, s3, h2, weights, per_pair, depth):
    branch_w, branch_b, head_w, head_b, value_w, value_b, out_w, out_b = weights
    width = enc.shape[0]
    options = branch_w.shape[0]
    flat = h2.shape[0]
    two = 2 * width
    pairs = options // 2
    outs = (
        shape_of(flat + options * width + width, LANES, dtype=BF16),
        shape_of(32, LANES),
        shape_of(width, LANES, dtype=BF16),
    )
    operands = (
        destination[None, :],
        slots,
        enc,
        s3,
        h2,
        branch_w,
        branch_b,
        head_w,
        head_b[None, :],
        value_w,
        value_b[None, :],
        out_w,
        out_b[None, :],
    )
    vmem = pltpu.VMEM
    return pl.pallas_call(
        functools.partial(plan_kernel, per_pair=per_pair),
        grid_spec=pltpu.PrefetchScalarGridSpec(
            num_scalar_prefetch=1,
            grid=(1,),
            in_specs=[whole(o.shape) for o in operands],
            out_specs=[whole(o.shape) for o in outs],
            scratch_shapes=[
                vmem((options * width, width), BF16),
                vmem((options * width, LANES), F32),
                vmem((width + 16, width), BF16),
                vmem((width, width + 16), BF16),
                vmem((width, LANES), F32),
                vmem((width, LANES), F32),
                vmem((slots.shape[0], LANES), F32),
                vmem((depth, options * width, LANES), F32),
                vmem((depth, pairs, width, 2 * LANES), F32),
                vmem((depth, pairs, width, 2 * LANES), BF16),
                vmem((depth, pairs, width, 2 * LANES), BF16),
                vmem((depth, options * width, LANES), BF16),
                vmem((depth + 1, width, LANES), F32),
                vmem((depth, options, LANES), F32),
                vmem((options, LANES), F32),
                vmem((options, LANES), F32),
                vmem((options, LANES), F32),
                vmem((depth, options, LANES), F32),
                vmem((depth, 3, LANES), F32),
                vmem((depth, 2, options, LANES), F32),
                vmem((width + 16, LANES), F32),
                vmem((width, 2 * LANES), F32),
                vmem((width, 2 * LANES), F32),
                vmem((3, options, LANES), F32),
            ],
        ),
        out_shape=outs,
        compiler_params=params(),
        cost_estimate=cost(2 * 3 * 2304 * 6 * 128 * 128, 4e6, 3e6),
        name="plan",
    )(section, *operands)


def back(g3, lw, s2, h1, s1, w2):
    blocks, side, k1 = h1.shape[:3]
    k2 = w2.shape[1]
    inner = side // 2 - 1
    outs = (
        shape_of(side + 2, side, k1, LANES, dtype=BF16),
        shape_of(k2, 256),
        shape_of(8, LANES),
    )
    return pl.pallas_call(
        back_kernel,
        out_shape=outs,
        scratch_shapes=[
            pltpu.VMEM((inner + 2, inner, k2, LANES), BF16),
            pltpu.VMEM((LANES, 6 * k2), BF16),
            pltpu.VMEM((k1, LANES), F32),
            pltpu.VMEM((k2, LANES), F32),
        ],
        compiler_params=params(),
        cost_estimate=cost(2 * 128 * 3e6, 7e6),
        name="back",
    )(g3, lw, s2, h1, s1, w2)


def first(section, frames, g1, c2, sums, small):
    stack, img = frames.shape[0], frames.shape[1]
    blocks = img // 4
    k1, k2 = g1.shape[2], c2.shape[0]
    total = small.shape[0] + 2 * k2 + 2 * k1 + sums.shape[0]
    rest = (g1, c2, sums, small)
    return pl.pallas_call(
        first_kernel,
        grid_spec=pltpu.PrefetchScalarGridSpec(
            num_scalar_prefetch=1,
            grid=(blocks // STEP,),
            in_specs=[
                pl.BlockSpec((stack, 4 * STEP, img, LANES), lambda g, s: (0, g, 0, s[0])),
                *[whole(w.shape) for w in rest],
            ],
            out_specs=whole((total, LANES)),
            scratch_shapes=[
                pltpu.VMEM((2 * REACH * k1, 256), F32),
                pltpu.VMEM((STEP, stack, 4, TILE, LANES), BF16),
            ],
        ),
        out_shape=shape_of(total, LANES),
        compiler_params=params(),
        cost_estimate=cost(2 * 128 * 5e6, 1e7),
        name="first",
    )(section, frames, *rest)


def pixels(section, w1, mine, other, img, channels):
    blocks = img // 4
    k1 = mine.shape[2]
    return pl.pallas_call(
        pixels_kernel,
        grid_spec=pltpu.PrefetchScalarGridSpec(
            num_scalar_prefetch=1,
            grid=(blocks // STEP,),
            in_specs=[whole(w.shape) for w in (w1, mine, other)],
            out_specs=pl.BlockSpec(
                (channels, 4 * STEP, img, 2 * LANES), lambda g, s: (0, g, 0, 0)
            ),
            scratch_shapes=[
                pltpu.VMEM((STEP * channels * 32, (STEP + 1) * 3 * k1), BF16),
            ],
        ),
        out_shape=shape_of(channels, img, img, 2 * LANES),
        compiler_params=params(),
        cost_estimate=cost(2 * 256 * 5e6, 1.9e7),
        name="pixels",
    )(section, w1, mine, other)


def unpack(big, packed, like):
    shapes = [p if len(p) > 1 else (1,) + p for p in like]
    outs = [shape_of(1, 1)] + [shape_of(*s) for s in shapes]
    got = pl.pallas_call(
        unpack_kernel,
        out_shape=outs,
        compiler_params=params(),
        cost_estimate=cost(1e6, 5e6),
        name="unpack",
    )(big, packed)
    return [got[0].reshape(())] + [v.reshape(s) for v, s in zip(got[1:], like)]


def local(
    frames,
    destination,
    options,
    depth,
    targets,
    conv_one,
    bias_one,
    conv_two,
    bias_two,
    linear_w,
    linear_b,
    branch_w,
    branch_b,
    head_w,
    head_b,
    value_w,
    value_b,
    out_w,
    out_b,
):
    section_index = lax.axis_index("section")
    section = section_index.astype(jnp.int32)[None]
    peer_count = lax.axis_size("batch")
    frame_count = frames.shape[3]
    per_pair = frame_count // peer_count
    levels = options.shape[0]
    encoder_params = (conv_one, bias_one, conv_two, bias_two, linear_w, linear_b)
    planner_params = (branch_w, branch_b, head_w, head_b, value_w, value_b, out_w, out_b)

    numbers = jnp.concatenate(
        [options.astype(F32), depth.astype(F32)[None], targets.reshape(3 * levels, frame_count)]
    )
    lines = numbers.shape[0]
    sent = numbers.reshape(lines, peer_count, per_pair).transpose(1, 0, 2)
    arrived = lax.all_to_all(sent, "batch", split_axis=0, concat_axis=0, tiled=True)
    slots = arrived.transpose(1, 0, 2).reshape(lines, frame_count)
    slots = jnp.pad(slots, ((0, 16 - lines), (0, 0)))

    h1, s1, h2, s2, enc, s3 = encode(section, frames, *encoder_params)
    big, small, g3 = plan(
        section, destination, slots, enc, s3, h2, planner_params, per_pair, levels
    )
    big = lax.psum(big, ("section", "batch"))
    g1, c2, sums = back(g3, linear_w, s2, h1, s1, conv_two)
    other = lax.ppermute(g1, "section", [(0, 1), (1, 0)])
    packed = first(section, frames, g1, c2, sums, small)
    packed = lax.psum(packed, ("section", "batch"))
    channels = frames.shape[0] // lax.axis_size("section")
    frames_grad = pixels(section, conv_one, g1, other, frames.shape[1], channels)
    shapes = [p.shape for p in encoder_params + planner_params]
    rest = unpack(big, packed, shapes)
    return (rest[0], frames_grad, *rest[1:])


def solution(mesh):
    placed = (
        P(None, None, None, "batch"),
        P("batch"),
        P(None, "batch"),
        P("batch"),
        P(None, None, "batch"),
    ) + (P(),) * 14
    return jax.shard_map(
        local,
        mesh=mesh,
        in_specs=placed,
        out_specs=(P(), P("section", None, None, "batch")) + (P(),) * 14,
        check_vma=False,
    )
```

```python
import functools
import math

import jax
import jax.numpy as jnp
from jax import lax
from jax.experimental import pallas as pl
from jax.experimental.pallas import tpu as pltpu
from jax.sharding import PartitionSpec as P

BF16 = jnp.bfloat16
F32 = jnp.float32
EXACT = lax.Precision.HIGHEST
LANES = 128
VMEM_BYTES = 48 * 1024 * 1024
TILE = 16
REACH = 5
STEP = 3


def dot(a, b, precision=None):
    return jnp.dot(a, b, preferred_element_type=F32, precision=precision)


def dot_rows(a, b, precision=None):
    return lax.dot_general(
        a, b, (((0,), (0,)), ((), ())), preferred_element_type=F32, precision=precision
    )


def dot_lanes(a, b, precision=None):
    return lax.dot_general(
        a, b, (((1,), (1,)), ((), ())), preferred_element_type=F32, precision=precision
    )


def iota(shape, axis):
    return lax.broadcasted_iota(jnp.int32, shape, axis)


def column(row):
    n = row.shape[1]
    wide = jnp.broadcast_to(row, (n, n))
    return jnp.sum(jnp.where(iota((n, n), 0) == iota((n, n), 1), wide, 0.0), axis=1, keepdims=True)


def row_of(col):
    n = col.shape[0]
    wide = jnp.broadcast_to(col, (n, n))
    return jnp.sum(jnp.where(iota((n, n), 0) == iota((n, n), 1), wide, 0.0), axis=0, keepdims=True)


def soft(x):
    e = jnp.exp(-jnp.abs(x))
    r = 1.0 / (1.0 + e)
    return jnp.maximum(x, 0.0) + jnp.log(1.0 + e), jnp.where(x >= 0.0, r, e * r)


def silu_pair(x):
    s = 1.0 / (1.0 + jnp.exp(-x))
    act = x * s
    return act, s + act * (1.0 - s)


def tap_map(half, place):
    tap, pix = iota((256, 256), 0), iota((256, 256), 1)
    hit = (
        ((tap >> 6) == (pix & 3))
        & (((tap >> 3) & 7) == (pix >> 6) + 4 * half)
        & ((tap & 7) == ((pix >> 2) & 15) - 4 * (place - 1))
    )
    return hit.astype(F32)


def tile_rows(frames, r, j):
    channels = frames.shape[2]
    flat = frames.reshape(frames.shape[0], frames.shape[1] * channels, LANES)
    size = TILE * channels
    end = min((j + 1) * size, flat.shape[1])
    return flat[4 * r : 4 * r + 4, j * size : end, :].reshape(4 * (end - j * size), LANES)


def encode_kernel(
    section,
    frames,
    w1t,
    b1,
    w2t,
    b2,
    lw,
    lb,
    h1,
    s1,
    h2,
    s2,
    enc,
    s3,
    band,
    edge,
    bias1,
    bias2,
    held,
):
    g = pl.program_id(0)
    side = h1.shape[1]
    tiles = frames.shape[1] // TILE
    k1, k2 = w1t.shape[0], w2t.shape[0]
    reach_rows = REACH * k1

    @pl.when(g == 0)
    def _():
        for half in range(2):
            for place in range(REACH):
                at = half * reach_rows + place * k1
                taps = dot(w1t[...], tap_map(half, place).astype(BF16))
                band[at : at + k1, :] = taps.astype(BF16)
            tap, pix = iota((256, 64), 0), iota((256, 64), 1)
            hit = (
                ((tap >> 6) == (pix & 3))
                & (((tap >> 3) & 7) == (pix >> 4) + 4 * half)
                & ((tap & 7) == ((pix >> 2) & 3) + 4)
            )
            taps = dot(w1t[...], hit.astype(F32).astype(BF16))
            edge[half * k1 : (half + 1) * k1, :] = taps.astype(BF16)
        bias1[...] = jnp.broadcast_to(column(b1[...]), bias1.shape)
        bias2[...] = jnp.broadcast_to(column(b2[...]), bias2.shape)
        held[...] = jnp.zeros_like(held)

    for r in range(STEP):
        low, high = {}, {}

        def add(x, one, two):
            low[x] = low[x] + one if x in low else one
            high[x] = high[x] + two if x in high else two

        last = dot(edge[...], tile_rows(frames, r, tiles))
        add(side - 1, last[:k1], last[k1:])
        done = 0
        for first in range(0, tiles, 2):
            js = [j for j in (first, first + 1) if j < tiles]
            cut = [tile_rows(frames, r, j) for j in js]
            got = dot(band[...], cut[0] if len(cut) == 1 else jnp.concatenate(cut, axis=1))
            for k, j in enumerate(js):
                for place in range(REACH):
                    x = 4 * j - 1 + place
                    if 0 <= x < side:
                        at = place * k1
                        span = slice(k * LANES, (k + 1) * LANES)
                        add(
                            x,
                            got[at : at + k1, span],
                            got[reach_rows + at : reach_rows + at + k1, span],
                        )
            ready = side if js[-1] == tiles - 1 else 4 * js[-1] + 3
            for x in range(done, ready):
                value, slope = soft(held[x] + high[x] + bias1[...])
                held[x] = low[x]
                h1[STEP * g + r, x] = value.astype(BF16)
                s1[r, x] = slope.astype(BF16)
            done = ready

    @pl.when(g == pl.num_programs(0) - 1)
    def _():
        inner = side // 2 - 1
        row_len = inner * k2

        def one_row(y, carry):
            for first in range(0, inner, 2):
                xs = [x for x in (first, first + 1) if x < inner]
                cut = [
                    h1[pl.ds(2 * y + 1, 4), 2 * x : 2 * x + 4].reshape(256, LANES) for x in xs
                ]
                patch = cut[0] if len(cut) == 1 else jnp.concatenate(cut, axis=1)
                got = dot(w2t[...], patch)
                for k, x in enumerate(xs):
                    value, slope = soft(got[:, k * LANES : (k + 1) * LANES] + bias2[...])
                    at = pl.ds(pl.multiple_of(y * row_len + x * k2, k2), k2)
                    h2[at, :] = value.astype(BF16)
                    s2[at, :] = slope.astype(BF16)
            return carry

        lax.fori_loop(0, inner, one_row, 0)
        value, slope = soft(dot_rows(lw[...], h2[...]) + column(lb[...]))
        enc[...] = value.astype(BF16)
        s3[...] = slope


def plan_kernel(
    section,
    destination,
    slots,
    enc,
    s3,
    h2,
    branch_w,
    branch_b,
    head_w,
    head_b,
    value_w,
    value_b,
    out_w,
    out_b,
    keep,
    send,
    small,
    g3,
    parts,
    bwt,
    bb,
    vht,
    vhw,
    vb,
    ow,
    mine,
    dbr,
    dval,
    low,
    hid,
    gb,
    states,
    pick,
    rew,
    disc,
    val,
    soft_q,
    gaps,
    rows_g,
    vgrad,
    outacc,
    vbacc,
    rowacc,
    *,
    per_pair,
):
    width = enc.shape[0]
    options = branch_w.shape[0]
    depth = states.shape[0] - 1
    pairs = options // 2
    two = 2 * width
    sec = section[0]

    dest = destination[...].astype(F32)
    count = dest.shape[1]
    own = jnp.where(sec == 0, dest[:, :LANES], dest[:, LANES:])
    others = jnp.transpose(jnp.broadcast_to(dest, (LANES, count)))
    index = iota((count, LANES), 1) + sec * LANES
    earlier = (others == own) & (iota((count, LANES), 0) < index)
    rank = jnp.sum(earlier.astype(F32), axis=0, keepdims=True)
    bucket = own * float(per_pair) + rank
    chosen = (iota((count, LANES), 0).astype(F32) == bucket).astype(F32)
    mine[...] = dot_rows(slots[...], chosen, EXACT)[: mine.shape[0]]

    for o in range(options):
        at = slice(o * width, (o + 1) * width)
        bwt[at, :] = jnp.transpose(branch_w[o].astype(F32)).astype(BF16)
        bb[at, :] = jnp.broadcast_to(column(branch_b[o : o + 1, :]), (width, LANES))
    vht[...] = jnp.zeros_like(vht)
    vht[0:width, :] = jnp.transpose(value_w[...].astype(F32)).astype(BF16)
    pick_head = (iota((16, 2), 0) == iota((16, 2), 1)).astype(F32).astype(BF16)
    vht[width : width + 16, :] = dot(pick_head, head_w[...]).astype(BF16)
    vhw[:, 0:width] = value_w[...]
    vhw[:, width:] = dot_rows(
        head_w[...], (iota((2, 16), 0) == iota((2, 16), 1)).astype(F32).astype(BF16)
    ).astype(BF16)
    vb[...] = jnp.broadcast_to(column(value_b[...]), (width, LANES))
    ow[...] = jnp.broadcast_to(column(out_w[...].astype(F32)), (width, LANES))

    vgrad[...] = jnp.zeros_like(vgrad)
    outacc[...] = jnp.zeros_like(outacc)
    vbacc[...] = jnp.zeros_like(vbacc)
    rowacc[...] = jnp.zeros_like(rowacc)
    states[0] = enc[...].astype(F32)

    def wide(ref):
        return jnp.concatenate([ref[...], ref[...]], axis=1)

    def ahead(level, carry):
        labels = iota((options, LANES), 0).astype(F32)
        picked = (labels == mine[pl.ds(level, 1), :]).astype(F32)
        pick[level] = picked
        states[level + 1] = jnp.zeros((width, LANES), F32)

        def one_pair(t, inside):
            at = pl.ds(pl.multiple_of(t * two, two), two)
            state = states[level]
            act, slope = silu_pair(dot(bwt[at, :], state.astype(BF16)) + bb[at, :])
            dbr[level, at, :] = slope
            left = state + act[:width]
            right = state + act[width:]
            states[level + 1] += (
                pick[level, pl.ds(2 * t, 1), :] * left + pick[level, pl.ds(2 * t + 1, 1), :] * right
            )
            both = jnp.concatenate([left.astype(BF16), right.astype(BF16)], axis=1)
            low[level, t] = both
            got = dot(vht[...], both)
            act, slope = silu_pair(got[:width] + wide(vb))
            dval[level, t] = slope
            hidden = act.astype(BF16)
            hid[level, t] = hidden
            worth = jnp.sum(hidden.astype(F32) * wide(ow), axis=0, keepdims=True)
            for k in range(2):
                spot = pl.ds(2 * t + k, 1)
                span = slice(k * LANES, (k + 1) * LANES)
                val[spot, :] = worth[:, span]
                rew[spot, :] = got[width : width + 1, span]
                disc[spot, :] = got[width + 1 : width + 2, span]
            return inside

        lax.fori_loop(0, pairs, one_pair, 0, unroll=3)
        reward = rew[...] + head_b[:, 0:1]
        discount = jax.nn.sigmoid(disc[...] + head_b[:, 1:2])
        value = val[...] + out_b[...]
        quality = reward + discount * value
        top = jnp.max(quality, axis=0, keepdims=True)
        shifted = jnp.exp(quality - top)
        total = jnp.sum(shifted, axis=0, keepdims=True)
        soft_q[level] = shifted / total
        rows_g[level, 0] = discount
        rows_g[level, 1] = value
        live = (mine[pl.ds(depth, 1), :] > level.astype(F32)).astype(F32)

        def target(kind):
            return mine[pl.ds(depth + 1 + kind * depth + level, 1), :]

        gaps[level, 0:1, :] = live * (jnp.sum(picked * reward, axis=0, keepdims=True) - target(0))
        gaps[level, 1:2, :] = live * (jnp.sum(picked * discount, axis=0, keepdims=True) - target(1))
        gaps[level, 2:3, :] = live * (top + jnp.log(total) - target(2))
        return carry

    lax.fori_loop(0, depth, ahead, 0)

    states[depth] = jnp.zeros((width, LANES), F32)

    def behind(turn, carry):
        level = depth - 1 - turn
        picked = pick[level]
        grad_quality = gaps[level, 2:3, :] * soft_q[level]
        discount = rows_g[level, 0]
        value = rows_g[level, 1]
        head_one = (picked * gaps[level, 0:1, :] + grad_quality).astype(BF16).astype(F32)
        head_two = picked * gaps[level, 1:2, :] + grad_quality * value
        head_two = (head_two * discount * (1.0 - discount)).astype(BF16).astype(F32)
        grad_value = (grad_quality * discount).astype(BF16).astype(F32)
        rew[...] = head_one
        disc[...] = head_two
        val[...] = grad_value
        rowacc[0] += head_one
        rowacc[1] += head_two
        rowacc[2] += grad_value
        grad_next = states[depth]
        states[depth] = jnp.zeros((width, LANES), F32)

        def one_pair(t, inside):
            at = pl.ds(pl.multiple_of(t * two, two), two)

            def across(ref):
                return jnp.concatenate(
                    [ref[pl.ds(2 * t, 1), :], ref[pl.ds(2 * t + 1, 1), :]], axis=1
                )

            worth = across(val)
            grad_hidden = worth * wide(ow)
            grad_pre = (grad_hidden * dval[level, t]).astype(BF16)
            outacc[...] += hid[level, t].astype(F32) * worth
            vbacc[...] += grad_pre.astype(F32)
            line = iota((16, two), 0)
            heads = jnp.where(line == 0, across(rew), jnp.where(line == 1, across(disc), 0.0))
            stacked = jnp.concatenate([grad_pre, heads.astype(BF16)], axis=0)
            vgrad[...] += dot_lanes(stacked, low[level, t])
            moved = dot(vhw[...], stacked)
            left = moved[:, :LANES] + pick[level, pl.ds(2 * t, 1), :] * grad_next
            right = moved[:, LANES:] + pick[level, pl.ds(2 * t + 1, 1), :] * grad_next
            grad_branch = jnp.concatenate([left, right], axis=0) * dbr[level, at, :]
            grad_branch = grad_branch.astype(BF16)
            gb[level, at, :] = grad_branch
            weights = jnp.concatenate([branch_w[2 * t], branch_w[2 * t + 1]], axis=1)
            states[depth] += left + right + dot(weights, grad_branch)
            return inside

        lax.fori_loop(0, pairs, one_pair, 0, unroll=3)
        return carry

    lax.fori_loop(0, depth, behind, 0)

    linear_rows = h2.shape[0]
    half = (linear_rows + options * width + width) // 2
    rest = linear_rows - half
    ones = jnp.ones((16, depth * LANES), F32).astype(BF16)
    rounded = jnp.concatenate([states[level].astype(BF16) for level in range(depth)], axis=1)
    rounded = jnp.concatenate([rounded, ones], axis=0)
    small[...] = jnp.zeros_like(small)
    if half < keep.shape[0]:
        for k in range(2):
            parts[k, half:, :] = jnp.zeros((keep.shape[0] - half, LANES), BF16)

    def one_option(o, carry):
        at = pl.ds(pl.multiple_of(o * width, width), width)
        grads = jnp.concatenate([gb[level, at, :] for level in range(depth)], axis=1)
        got = dot_lanes(rounded, grads)
        at = pl.ds(pl.multiple_of(rest + o * width, 16), width)
        parts[1 - sec, at, :] = got[:width].astype(BF16)
        small[pl.ds(o, 1), :] = got[width : width + 1]
        return carry

    lax.fori_loop(0, options, one_option, 0, unroll=2)
    after = rest + options * width
    parts[1 - sec, after : after + width, :] = jnp.transpose(vgrad[0:width, :]).astype(BF16)

    grad_three = (states[depth].astype(BF16).astype(F32) * s3[...]).astype(BF16)
    g3[...] = grad_three
    chunk = linear_rows // 9

    def one_chunk(i, carry):
        at = pl.ds(pl.multiple_of(i * chunk, chunk), chunk)
        parts[sec, at, :] = dot_lanes(h2[at, :], grad_three).astype(BF16)
        return carry

    lax.fori_loop(0, 8, one_chunk, 0, unroll=4)
    last = dot_lanes(h2[8 * chunk :, :], grad_three).astype(BF16)
    parts[sec, 8 * chunk : half, :] = last[: half - 8 * chunk]
    parts[1 - sec, 0:rest, :] = last[half - 8 * chunk :]
    keep[...] = parts[0]
    send[...] = parts[1]

    at = options
    small[at : at + 1, :] = row_of(jnp.sum(vbacc[...], axis=1, keepdims=True))
    small[at + 1 : at + 2, :] = row_of(jnp.sum(outacc[...], axis=1, keepdims=True))
    small[at + 2 : at + 4, :] = vgrad[width : width + 2, :]
    small[at + 4 : at + 5, :] = row_of(jnp.sum(grad_three.astype(F32), axis=1, keepdims=True))
    gap = gaps[...]
    loss = 0.5 * jnp.sum(jnp.sum(gap * gap, axis=0), axis=0, keepdims=True)
    lines = [loss] + [jnp.sum(rowacc[k], axis=0, keepdims=True) for k in range(3)]
    lane = iota((1, LANES), 1)
    scalars = jnp.zeros((1, LANES), F32)
    for k, line in enumerate(lines):
        scalars = jnp.where(lane == k, jnp.sum(line, axis=1, keepdims=True), scalars)
    small[at + 5 : at + 6, :] = scalars


def back_kernel(g3, lw, s2, h1, s1, w2t, g1, c2, sums, g2, t2, b1acc, b2acc):
    side = h1.shape[1]
    k1, k2 = h1.shape[2], w2t.shape[0]
    inner = side // 2 - 1
    row_len = inner * k2
    tap, pix = iota((LANES, 256), 1), iota((LANES, 256), 0)
    for yrel in range(2):
        for p in range(3):
            hit = (
                ((tap & 15) == (pix & 15))
                & ((tap >> 6) == (pix >> 6) + 2 * (1 - yrel))
                & (((tap >> 4) & 3) == ((pix >> 4) & 3) + 2 - 2 * p)
            )
            at = (yrel * 3 + p) * k2
            t2[:, at : at + k2] = dot_lanes(hit.astype(F32).astype(BF16), w2t[...]).astype(BF16)
    g2[0] = jnp.zeros(g2.shape[1:], BF16)
    g2[inner + 1] = jnp.zeros(g2.shape[1:], BF16)
    g1[0] = jnp.zeros(g1.shape[1:], BF16)
    g1[side + 1] = jnp.zeros(g1.shape[1:], BF16)
    b1acc[...] = jnp.zeros_like(b1acc)
    b2acc[...] = jnp.zeros_like(b2acc)
    c2[...] = jnp.zeros_like(c2)

    def out_row(y, carry):
        at = pl.ds(pl.multiple_of(y * row_len, row_len), row_len)
        grad = dot(lw[at, :], g3[...]) * s2[at, :].astype(F32)
        grad = grad.astype(BF16).reshape(inner, k2, LANES)
        g2[y + 1] = grad
        b2acc[...] += jnp.sum(grad.astype(F32), axis=0)
        grads = jnp.concatenate([grad[x] for x in range(inner)], axis=1)
        patches = jnp.concatenate(
            [h1[pl.ds(2 * y + 1, 4), 2 * x : 2 * x + 4].reshape(256, LANES) for x in range(inner)],
            axis=1,
        )
        c2[...] += dot_lanes(grads, patches)
        return carry

    lax.fori_loop(0, inner, out_row, 0)

    def in_rows(b, carry):
        zero = jnp.zeros((k2, LANES), BF16)
        cut = []
        for j in range(side // 4):
            pieces = []
            for yrel in range(2):
                for p in range(3):
                    x = 2 * j - 1 + p
                    pieces.append(g2[b + yrel, x] if 0 <= x < inner else zero)
            cut.append(jnp.concatenate(pieces, axis=0))
        got = dot(t2[...], jnp.concatenate(cut, axis=1))
        total = b1acc[...]
        for u in range(2):
            for j in range(side // 4):
                part = got[u * 64 : (u + 1) * 64, j * LANES : (j + 1) * LANES]
                slope = s1[2 * b + u + 1, 4 * j : 4 * j + 4].astype(F32)
                grad = (part.reshape(4, k1, LANES) * slope).astype(BF16)
                g1[2 * b + u + 1, 4 * j : 4 * j + 4] = grad
                total = total + jnp.sum(grad.astype(F32), axis=0)
        b1acc[...] = total
        return carry

    lax.fori_loop(0, side // 2, in_rows, 0)
    sums[...] = jnp.zeros_like(sums)
    sums[0:1, 0:k1] = row_of(jnp.sum(b1acc[...], axis=1, keepdims=True))
    sums[1:2, 0:k2] = row_of(jnp.sum(b2acc[...], axis=1, keepdims=True))


def first_kernel(section, frames, g1, c1, acc, side_acc):
    g = pl.program_id(0)
    side, k1 = g1.shape[1], g1.shape[2]
    tiles = frames.shape[1] // TILE

    @pl.when(g == 0)
    def _():
        acc[...] = jnp.zeros_like(acc)
        side_acc[...] = jnp.zeros_like(side_acc)

    zero = jnp.zeros((k1, LANES), BF16)
    total = acc[...]
    edges, edge_grads = [], []
    for r in range(STEP):
        pixels, grads = [], []
        for j in range(tiles):
            pixels.append(tile_rows(frames, r, j))
            pieces = []
            for half in range(2):
                for place in range(REACH):
                    x = 4 * j - 1 + place
                    pieces.append(g1[STEP * g + r + 1 - half, x] if 0 <= x < side else zero)
            grads.append(jnp.concatenate(pieces, axis=0))
        total = total + dot_lanes(
            jnp.concatenate(grads, axis=1), jnp.concatenate(pixels, axis=1)
        )
        edges.append(tile_rows(frames, r, tiles))
        edge_grads.append(
            jnp.concatenate([g1[STEP * g + r + 1 - half, side - 1] for half in range(2)], axis=0)
        )
    acc[...] = total
    side_acc[...] += dot_lanes(
        jnp.concatenate(edge_grads, axis=1), jnp.concatenate(edges, axis=1)
    )

    @pl.when(g == pl.num_programs(0) - 1)
    def _():
        grad = jnp.zeros((k1, 256), F32)
        for half in range(2):
            for place in range(REACH):
                at = (half * REACH + place) * k1
                grad = grad + dot_lanes(acc[at : at + k1, :], tap_map(half, place), EXACT)
            tap, pix = iota((256, 64), 0), iota((256, 64), 1)
            hit = (
                ((tap >> 6) == (pix & 3))
                & (((tap >> 3) & 7) == (pix >> 4) + 4 * half)
                & ((tap & 7) == ((pix >> 2) & 3) + 4)
            )
            grad = grad + dot_lanes(
                side_acc[half * k1 : (half + 1) * k1, :], hit.astype(F32), EXACT
            )
        for half in range(2):
            c1[half * k1 : (half + 1) * k1, :] = grad[:, half * LANES : (half + 1) * LANES].astype(
                BF16
            )


def pixels_kernel(section, w1t, mine, other, out, band, later):
    g, part = pl.program_id(0), pl.program_id(1)
    side, k1 = mine.shape[1], mine.shape[2]
    img, channels = out.shape[1], out.shape[2]
    cols = 8
    reach = 3
    sec = section[0]
    line = cols * channels
    size = STEP * 4 * line
    flat = out.reshape(out.shape[0], img * channels, LANES)

    @pl.when((g == 0) & (part == 0))
    def _():
        tap, pix = iota((size, 256), 1), iota((size, 256), 0)
        r = pix // (4 * line)
        u4 = (pix // line) % 4
        xx = (pix // channels) % cols
        c = pix % channels + sec * channels
        for yrel in range(STEP + 1):
            for p in range(reach):
                hit = (
                    ((tap >> 6) == c)
                    & (((tap >> 3) & 7) == 4 * (r + 1 - yrel) + u4)
                    & ((tap & 7) == xx + 4 - 4 * p)
                )
                at = (yrel * reach + p) * k1
                band[:, at : at + k1] = dot_lanes(hit.astype(F32).astype(BF16), w1t[...]).astype(
                    BF16
                )

    @pl.when(part == 0)
    def _():
        zero = jnp.zeros((k1, 2 * LANES), BF16)
        for j in range((img + cols - 1) // cols):
            pieces = []
            for yrel in range(STEP + 1):
                for p in range(reach):
                    x = 2 * j - 1 + p
                    if 0 <= x < side:
                        y = STEP * g + yrel
                        pieces.append(jnp.concatenate([mine[y, x], other[y, x]], axis=1))
                    else:
                        pieces.append(zero)
            got = dot(band[...], jnp.concatenate(pieces, axis=0))
            keep = min(line, img * channels - j * line)
            for k in range(4 * STEP):
                at = k * line
                flat[k, j * line : j * line + keep, :] = got[at : at + keep, :LANES]
                later[k, j * line : j * line + keep, :] = got[at : at + keep, LANES:]

    @pl.when(part == 1)
    def _():
        flat[...] = later[...]


def merge_kernel(keep, recv, small, c2, sums, out, lines):
    peers, rows = out.shape[0], out.shape[1]
    short = lines.shape[0] // peers
    chunk = rows - 2 * short
    k2 = c2.shape[0]
    lines[...] = jnp.zeros_like(lines)
    at = small.shape[0]
    lines[0:at, :] = small[...]
    for half in range(2):
        lines[at : at + k2, :] = c2[:, half * LANES : (half + 1) * LANES]
        at += k2
    lines[at : at + sums.shape[0], :] = sums[...]
    for p in range(peers):
        rows_p = slice(p * chunk, (p + 1) * chunk)
        both = keep[rows_p, :].astype(F32) + recv[rows_p, :].astype(F32)
        out[p, 0:chunk, :] = both.astype(BF16)
        out[p, chunk:, :] = two_parts(lines[p * short : (p + 1) * short, :])


def two_parts(value):
    high = value.astype(BF16).astype(F32)
    return jnp.concatenate([high, value - high], axis=0).astype(BF16)


def total_kernel(got, c1, out):
    peers, rows = got.shape[0], got.shape[1]
    extra = c1.shape[0]
    chunk = rows - 16
    for at in range(0, rows, 16):
        total = jnp.zeros((16, LANES), F32)
        for p in range(peers):
            total = total + got[p, at : at + 16, :].astype(F32)
        if at < chunk:
            total = total.astype(BF16)
        else:
            total = two_parts(total[0:8] + total[8:16])
        for p in range(peers):
            out[p, at : at + 16, :] = total
    for p in range(peers):
        out[p, rows : rows + extra, :] = c1[...]


def unpack_kernel(
    section, mine, other, loss, c1, b1, c2, b2, lw, lb, bw, bb, hw, hb, vw, vb, ow, ob, halves, lines
):
    width = lw.shape[1]
    options = bw.shape[0]
    k1, k2 = c1.shape[0], c2.shape[0]
    linear_rows = lw.shape[0]
    peers = mine.shape[0]
    chunk = halves.shape[1] // peers
    sec = section[0]
    half = (linear_rows + options * width + width) // 2
    rest = linear_rows - half
    for p in range(peers):
        rows_p = slice(p * chunk, (p + 1) * chunk)
        halves[sec, rows_p, :] = mine[p, 0:chunk, :]
        halves[1 - sec, rows_p, :] = other[p, 0:chunk, :]
        both = mine[p, chunk : chunk + 16, :].astype(F32) + other[p, chunk : chunk + 16, :].astype(
            F32
        )
        lines[p * 8 : (p + 1) * 8, :] = both[0:8] + both[8:16]
    lw[0:half, :] = halves[0, 0:half, :].astype(F32)
    lw[half:, :] = halves[1, 0:rest, :].astype(F32)
    for o in range(options):
        at = rest + o * width
        bw[o] = halves[1, at : at + width, :].astype(F32)
    at = rest + options * width
    vw[...] = halves[1, at : at + width, :].astype(F32)
    at = options
    bb[...] = lines[0:at, :]
    vb[...] = lines[at : at + 1, :]
    ow[...] = lines[at + 1 : at + 2, :]
    hw[...] = lines[at + 2 : at + 4, :]
    lb[...] = lines[at + 4 : at + 5, :]
    scalars = lines[at + 5 : at + 6, :]
    loss[...] = scalars[:, 0:1]
    hb[...] = scalars[:, 1:3]
    ob[...] = scalars[:, 3:4]
    at = 32
    for part in range(2):
        c2[:, part * LANES : (part + 1) * LANES] = lines[at : at + k2, :]
        at += k2
    b1[...] = lines[at : at + 1, 0:k1]
    b2[...] = lines[at + 1 : at + 2, 0:k2]
    for part in range(2):
        total = jnp.zeros((k1, LANES), F32)
        at = chunk + 16 + part * k1
        for p in range(peers):
            total = total + mine[p, at : at + k1, :].astype(F32)
            total = total + other[p, at : at + k1, :].astype(F32)
        c1[:, part * LANES : (part + 1) * LANES] = total


def numbers_kernel(options, depth, targets, out):
    levels, kinds = options.shape[0], targets.shape[0]
    slots = depth.shape[1]
    rows = [options[...].astype(F32), depth[...].astype(F32)]
    rows += [targets[k] for k in range(kinds)]
    rows.append(jnp.zeros((LANES - levels - 1 - kinds * levels, slots), F32))
    out[...] = jnp.transpose(jnp.concatenate(rows, axis=0))


def whole(shape):
    zeros = (0,) * len(shape)
    return pl.BlockSpec(shape, lambda *_: zeros)


def params():
    return pltpu.CompilerParams(vmem_limit_bytes=VMEM_BYTES)


def shape_of(*shape, dtype=F32):
    return jax.ShapeDtypeStruct(shape, dtype)


def cost(flops, moved, transcendentals=0):
    return pl.CostEstimate(
        flops=int(flops), bytes_accessed=int(moved), transcendentals=int(transcendentals)
    )


def frame_block(frames):
    _, img, stack, _ = frames.shape
    return pl.BlockSpec((4 * STEP, img, stack, LANES), lambda g, s: (g, 0, 0, s[0]))


def encode(section, frames, w1t, b1, w2t, b2, lw, lb):
    img = frames.shape[0]
    blocks = img // 4
    side = blocks - 1
    k1, k2, width = w1t.shape[0], w2t.shape[0], lw.shape[1]
    flat = lw.shape[0]
    outs = (
        shape_of(blocks, side, k1, LANES, dtype=BF16),
        shape_of(blocks, side, k1, LANES, dtype=BF16),
        shape_of(flat, LANES, dtype=BF16),
        shape_of(flat, LANES, dtype=BF16),
        shape_of(width, LANES, dtype=BF16),
        shape_of(width, LANES),
    )
    weights = (w1t, b1[None, :], w2t, b2[None, :], lw, lb[None, :])
    out_specs = [whole(o.shape) for o in outs]
    out_specs[1] = pl.BlockSpec((STEP, side, k1, LANES), lambda g, s: (g, 0, 0, 0))
    return pl.pallas_call(
        encode_kernel,
        grid_spec=pltpu.PrefetchScalarGridSpec(
            num_scalar_prefetch=1,
            grid=(blocks // STEP,),
            in_specs=[frame_block(frames), *[whole(w.shape) for w in weights]],
            out_specs=out_specs,
            scratch_shapes=[
                pltpu.VMEM((2 * REACH * k1, 256), BF16),
                pltpu.VMEM((2 * k1, 64), BF16),
                pltpu.VMEM((k1, LANES), F32),
                pltpu.VMEM((k2, LANES), F32),
                pltpu.VMEM((side, k1, LANES), F32),
            ],
        ),
        out_shape=outs,
        compiler_params=params(),
        cost_estimate=cost(2 * 128 * 5.2e6, 1.3e7, 2.5e6),
        name="encode",
    )(section, frames, *weights)


def plan(section, destination, slots, enc, s3, h2, weights, per_pair, depth, half_rows):
    branch_w, branch_b, head_w, head_b, value_w, value_b, out_w, out_b = weights
    width = enc.shape[0]
    options = branch_w.shape[0]
    two = 2 * width
    pairs = options // 2
    outs = (
        shape_of(half_rows, LANES, dtype=BF16),
        shape_of(half_rows, LANES, dtype=BF16),
        shape_of(32, LANES),
        shape_of(width, LANES, dtype=BF16),
    )
    operands = (
        destination[None, :],
        slots,
        enc,
        s3,
        h2,
        branch_w,
        branch_b,
        head_w,
        head_b[None, :],
        value_w,
        value_b[None, :],
        out_w,
        out_b[None, :],
    )
    vmem = pltpu.VMEM
    return pl.pallas_call(
        functools.partial(plan_kernel, per_pair=per_pair),
        grid_spec=pltpu.PrefetchScalarGridSpec(
            num_scalar_prefetch=1,
            grid=(1,),
            in_specs=[whole(o.shape) for o in operands],
            out_specs=[whole(o.shape) for o in outs],
            scratch_shapes=[
                vmem((2, half_rows, LANES), BF16),
                vmem((options * width, width), BF16),
                vmem((options * width, LANES), F32),
                vmem((width + 16, width), BF16),
                vmem((width, width + 16), BF16),
                vmem((width, LANES), F32),
                vmem((width, LANES), F32),
                vmem((16, LANES), F32),
                vmem((depth, options * width, LANES), F32),
                vmem((depth, pairs, width, 2 * LANES), F32),
                vmem((depth, pairs, width, 2 * LANES), BF16),
                vmem((depth, pairs, width, 2 * LANES), BF16),
                vmem((depth, options * width, LANES), BF16),
                vmem((depth + 1, width, LANES), F32),
                vmem((depth, options, LANES), F32),
                vmem((options, LANES), F32),
                vmem((options, LANES), F32),
                vmem((options, LANES), F32),
                vmem((depth, options, LANES), F32),
                vmem((depth, 3, LANES), F32),
                vmem((depth, 2, options, LANES), F32),
                vmem((width + 16, LANES), F32),
                vmem((width, 2 * LANES), F32),
                vmem((width, 2 * LANES), F32),
                vmem((3, options, LANES), F32),
            ],
        ),
        out_shape=outs,
        compiler_params=params(),
        cost_estimate=cost(2 * 3 * 2304 * 6 * 128 * 128, 4e6, 3e6),
        name="plan",
    )(section, *operands)


def back(g3, lw, s2, h1, s1, w2t):
    blocks, side, k1 = h1.shape[:3]
    k2 = w2t.shape[0]
    inner = side // 2 - 1
    outs = (
        shape_of(side + 2, side, k1, LANES, dtype=BF16),
        shape_of(k2, 256),
        shape_of(8, LANES),
    )
    return pl.pallas_call(
        back_kernel,
        out_shape=outs,
        scratch_shapes=[
            pltpu.VMEM((inner + 2, inner, k2, LANES), BF16),
            pltpu.VMEM((LANES, 6 * k2), BF16),
            pltpu.VMEM((k1, LANES), F32),
            pltpu.VMEM((k2, LANES), F32),
        ],
        compiler_params=params(),
        cost_estimate=cost(2 * 128 * 3e6, 7e6),
        name="back",
    )(g3, lw, s2, h1, s1, w2t)


def first(section, frames, g1):
    blocks = frames.shape[0] // 4
    k1 = g1.shape[2]
    return pl.pallas_call(
        first_kernel,
        grid_spec=pltpu.PrefetchScalarGridSpec(
            num_scalar_prefetch=1,
            grid=(blocks // STEP,),
            in_specs=[frame_block(frames), whole(g1.shape)],
            out_specs=whole((2 * k1, LANES)),
            scratch_shapes=[
                pltpu.VMEM((2 * REACH * k1, 256), F32),
                pltpu.VMEM((2 * k1, 64), F32),
            ],
        ),
        out_shape=shape_of(2 * k1, LANES, dtype=BF16),
        compiler_params=params(),
        cost_estimate=cost(2 * 128 * 5e6, 1e7),
        name="first",
    )(section, frames, g1)


def pixels(section, w1t, mine, other, img, channels):
    blocks = img // 4
    k1 = mine.shape[2]
    block = (4 * STEP, img, channels, LANES)
    return pl.pallas_call(
        pixels_kernel,
        grid_spec=pltpu.PrefetchScalarGridSpec(
            num_scalar_prefetch=1,
            grid=(blocks // STEP, 2),
            in_specs=[whole(w.shape) for w in (w1t, mine, other)],
            out_specs=pl.BlockSpec(block, lambda g, p, s: (g, 0, 0, (s[0] + p) % 2)),
            scratch_shapes=[
                pltpu.VMEM((STEP * channels * 32, (STEP + 1) * 3 * k1), BF16),
                pltpu.VMEM((4 * STEP, img * channels, LANES), F32),
            ],
        ),
        out_shape=shape_of(img, img, channels, 2 * LANES),
        compiler_params=params(),
        cost_estimate=cost(2 * 256 * 5e6, 1.9e7),
        name="pixels",
    )(section, w1t, mine, other)


def small_call(kernel, outs, operands, scratch=(), name=None):
    return pl.pallas_call(
        kernel,
        out_shape=outs,
        scratch_shapes=list(scratch),
        compiler_params=params(),
        cost_estimate=cost(1e6, 4e6),
        name=name,
    )(*operands)


def unpack(section, mine, other, shapes, half_rows):
    shapes = [s if len(s) > 1 else (1,) + s for s in shapes]
    outs = [shape_of(1, 1)] + [shape_of(*s) for s in shapes]
    operands = (section, mine, other)
    return pl.pallas_call(
        unpack_kernel,
        in_specs=[pl.BlockSpec(memory_space=pltpu.SMEM)]
        + [pl.BlockSpec(memory_space=pltpu.VMEM)] * 2,
        out_shape=outs,
        scratch_shapes=[
            pltpu.VMEM((2, half_rows, LANES), BF16),
            pltpu.VMEM((mine.shape[0] * 8, LANES), F32),
        ],
        compiler_params=params(),
        cost_estimate=cost(1e6, 5e6),
        name="unpack",
    )(*operands)


def round_up(value, step):
    return -(-value // step) * step


def swapped(value):
    return lax.ppermute(value, "section", [(0, 1), (1, 0)])


def exchanged(value):
    return lax.all_to_all(value, "batch", split_axis=0, concat_axis=0, tiled=True)


def local(
    frames,
    destination,
    options,
    depth,
    targets,
    conv_one,
    bias_one,
    conv_two,
    bias_two,
    linear_w,
    linear_b,
    branch_w,
    branch_b,
    head_w,
    head_b,
    value_w,
    value_b,
    out_w,
    out_b,
):
    section = lax.axis_index("section").astype(jnp.int32)[None]
    peers = lax.axis_size("batch")
    frame_count = frames.shape[3]
    per_pair = frame_count // peers
    levels = options.shape[0]
    frames = frames.transpose(1, 2, 0, 3)
    w1t, w2t = conv_one.T, conv_two.T
    encoder_params = (w1t, bias_one, w2t, bias_two, linear_w, linear_b)
    planner_params = (branch_w, branch_b, head_w.T, head_b, value_w, value_b, out_w.T, out_b)
    width = linear_w.shape[1]
    big_rows = linear_w.shape[0] + (branch_w.shape[0] + 1) * width
    chunk = round_up(-(-big_rows // (2 * peers)), 16)
    half_rows = chunk * peers

    numbers = small_call(
        numbers_kernel,
        shape_of(frame_count, LANES),
        (options, depth[None, :], targets),
        name="numbers",
    )
    slots = exchanged(numbers.reshape(peers, per_pair, LANES)).reshape(frame_count, LANES)

    h1, s1, h2, s2, enc, s3 = encode(section, frames, *encoder_params)
    keep, send, small, g3 = plan(
        section, destination, slots, enc, s3, h2, planner_params, per_pair, levels, half_rows
    )
    recv = swapped(send)
    g1, c2, sums = back(g3, linear_w, s2, h1, s1, w2t)
    other = swapped(g1)
    short = 8
    cut = small_call(
        merge_kernel,
        shape_of(peers, chunk + 2 * short, LANES, dtype=BF16),
        (keep, recv, small, c2, sums),
        [pltpu.VMEM((peers * short, LANES), F32)],
        name="merge",
    )
    got = exchanged(cut)
    c1 = first(section, frames, g1)
    summed = small_call(
        total_kernel,
        shape_of(peers, chunk + 2 * short + c1.shape[0], LANES, dtype=BF16),
        (got, c1),
        name="total",
    )
    summed = exchanged(summed)
    channels = frames.shape[2] // lax.axis_size("section")
    frames_grad = pixels(section, w1t, g1, other, frames.shape[0], channels)
    summed_other = swapped(summed)
    shapes = [p.shape for p in encoder_params + planner_params]
    rest = list(unpack(section, summed, summed_other, shapes, half_rows))
    rest = [v.reshape(s) for v, s in zip(rest, [()] + shapes)]
    for at in (1, 3, 9, 13):
        rest[at] = rest[at].T
    return (rest[0], frames_grad.transpose(2, 0, 1, 3), *rest[1:])


def solution(mesh):
    placed = (
        P(None, None, None, "batch"),
        P("batch"),
        P(None, "batch"),
        P("batch"),
        P(None, None, "batch"),
    ) + (P(),) * 14
    return jax.shard_map(
        local,
        mesh=mesh,
        in_specs=placed,
        out_specs=(P(), P("section", None, None, "batch")) + (P(),) * 14,
        check_vma=False,
    )
```

```python
import functools
import math

import jax
import jax.numpy as jnp
from jax import lax
from jax.experimental import pallas as pl
from jax.experimental.pallas import tpu as pltpu
from jax.sharding import PartitionSpec as P

BF16 = jnp.bfloat16
F32 = jnp.float32
EXACT = lax.Precision.HIGHEST
LANES = 128
VMEM_BYTES = 60 * 1024 * 1024
WORK_BYTES = 52 * 1024 * 1024
TILE = 16
REACH = 5
STEP = 3
AT_VB, AT_OW, AT_HW, AT_LB, AT_SCALARS, AT_B1, AT_B2, AT_DEST = (
    slice(18, 19),
    slice(19, 20),
    slice(20, 22),
    slice(22, 23),
    slice(23, 24),
    slice(24, 25),
    slice(25, 26),
    26,
)
TABLE = 32
PLANE = 4


def dot(a, b, precision=None):
    return jnp.dot(a, b, preferred_element_type=F32, precision=precision)


def dot_rows(a, b, precision=None):
    return lax.dot_general(
        a, b, (((0,), (0,)), ((), ())), preferred_element_type=F32, precision=precision
    )


def dot_lanes(a, b, precision=None):
    return lax.dot_general(
        a, b, (((1,), (1,)), ((), ())), preferred_element_type=F32, precision=precision
    )


def iota(shape, axis):
    return lax.broadcasted_iota(jnp.int32, shape, axis)


def column(row):
    n = row.shape[1]
    wide = jnp.broadcast_to(row, (n, n))
    return jnp.sum(jnp.where(iota((n, n), 0) == iota((n, n), 1), wide, 0.0), axis=1, keepdims=True)


def row_of(col):
    n = col.shape[0]
    wide = jnp.broadcast_to(col, (n, n))
    return jnp.sum(jnp.where(iota((n, n), 0) == iota((n, n), 1), wide, 0.0), axis=0, keepdims=True)


def soft(x):
    e = jnp.exp(-jnp.abs(x))
    r = 1.0 / (1.0 + e)
    return jnp.maximum(x, 0.0) + jnp.log(1.0 + e), jnp.where(x >= 0.0, r, e * r)


def silu_pair(x):
    s = 1.0 / (1.0 + jnp.exp(-x))
    act = x * s
    return act, s + act * (1.0 - s)


def tap_map(half, place):
    tap, pix = iota((256, 256), 0), iota((256, 256), 1)
    hit = (
        ((tap >> 6) == (pix & 3))
        & (((tap >> 3) & 7) == (pix >> 6) + 4 * half)
        & ((tap & 7) == ((pix >> 2) & 15) - 4 * (place - 1))
    )
    return hit.astype(F32)


def tile_rows(frames, r, j):
    channels = frames.shape[2]
    flat = frames.reshape(frames.shape[0], frames.shape[1] * channels, LANES)
    size = TILE * channels
    end = min((j + 1) * size, flat.shape[1])
    return flat[4 * r : 4 * r + 4, j * size : end, :].reshape(4 * (end - j * size), LANES)


def encode_kernel(
    section,
    frames,
    w1t,
    w2t,
    lw,
    table,
    h1,
    s1,
    h2,
    s2,
    enc,
    s3,
    band,
    edge,
    bias1,
    bias2,
    held,
):
    g = pl.program_id(0)
    side = h1.shape[1]
    tiles = frames.shape[1] // TILE
    k1, k2 = w1t.shape[0], w2t.shape[0]
    reach_rows = REACH * k1

    @pl.when(g == 0)
    def _():
        for half in range(2):
            for place in range(REACH):
                at = half * reach_rows + place * k1
                taps = dot(w1t[...], tap_map(half, place).astype(BF16))
                band[at : at + k1, :] = taps.astype(BF16)
            tap, pix = iota((256, 64), 0), iota((256, 64), 1)
            hit = (
                ((tap >> 6) == (pix & 3))
                & (((tap >> 3) & 7) == (pix >> 4) + 4 * half)
                & ((tap & 7) == ((pix >> 2) & 3) + 4)
            )
            taps = dot(w1t[...], hit.astype(F32).astype(BF16))
            edge[half * k1 : (half + 1) * k1, :] = taps.astype(BF16)
        bias1[...] = jnp.broadcast_to(column(table[AT_B1, 0:k1]), bias1.shape)
        bias2[...] = jnp.broadcast_to(column(table[AT_B2, 0:k2]), bias2.shape)
        held[...] = jnp.zeros_like(held)

    for r in range(STEP):
        low, high = {}, {}

        def add(x, one, two):
            low[x] = low[x] + one if x in low else one
            high[x] = high[x] + two if x in high else two

        last = dot(edge[...], tile_rows(frames, r, tiles))
        add(side - 1, last[:k1], last[k1:])
        done = 0
        for first in range(0, tiles, 2):
            js = [j for j in (first, first + 1) if j < tiles]
            cut = [tile_rows(frames, r, j) for j in js]
            got = dot(band[...], cut[0] if len(cut) == 1 else jnp.concatenate(cut, axis=1))
            for k, j in enumerate(js):
                for place in range(REACH):
                    x = 4 * j - 1 + place
                    if 0 <= x < side:
                        at = place * k1
                        span = slice(k * LANES, (k + 1) * LANES)
                        add(
                            x,
                            got[at : at + k1, span],
                            got[reach_rows + at : reach_rows + at + k1, span],
                        )
            ready = side if js[-1] == tiles - 1 else 4 * js[-1] + 3
            for x in range(done, ready):
                value, slope = soft(held[x] + high[x] + bias1[...])
                held[x] = low[x]
                h1[STEP * g + r, x] = value.astype(BF16)
                s1[r, x] = slope.astype(BF16)
            done = ready

    @pl.when(g == pl.num_programs(0) - 1)
    def _():
        inner = side // 2 - 1
        row_len = inner * k2

        def one_row(y, carry):
            for first in range(0, inner, 2):
                xs = [x for x in (first, first + 1) if x < inner]
                cut = [
                    h1[pl.ds(2 * y + 1, 4), 2 * x : 2 * x + 4].reshape(256, LANES) for x in xs
                ]
                patch = cut[0] if len(cut) == 1 else jnp.concatenate(cut, axis=1)
                got = dot(w2t[...], patch)
                for k, x in enumerate(xs):
                    value, slope = soft(got[:, k * LANES : (k + 1) * LANES] + bias2[...])
                    at = pl.ds(pl.multiple_of(y * row_len + x * k2, k2), k2)
                    h2[at, :] = value.astype(BF16)
                    s2[at, :] = slope.astype(BF16)
            return carry

        lax.fori_loop(0, inner, one_row, 0)
        value, slope = soft(dot_rows(lw[...], h2[...]) + column(table[AT_LB, :]))
        enc[...] = value.astype(BF16)
        s3[...] = slope


def plan_kernel(
    section,
    slots,
    enc,
    s3,
    h2,
    branch_w,
    value_w,
    table,
    keep,
    send,
    small,
    g3,
    parts,
    bwt,
    bb,
    vht,
    vhw,
    vb,
    ow,
    mine,
    dbr,
    dval,
    low,
    hid,
    gb,
    states,
    pick,
    rew,
    disc,
    val,
    soft_q,
    gaps,
    rows_g,
    vgrad,
    outacc,
    vbacc,
    rowacc,
    *,
    per_pair,
):
    width = enc.shape[0]
    options = branch_w.shape[0]
    depth = states.shape[0] - 1
    pairs = options // 2
    two = 2 * width
    sec = section[0]

    count = slots.shape[0]
    dest = jnp.concatenate(
        [table[AT_DEST + k : AT_DEST + k + 1, :] for k in range(count // LANES)], axis=1
    )
    own = jnp.where(sec == 0, dest[:, :LANES], dest[:, LANES:])
    others = jnp.transpose(jnp.broadcast_to(dest, (LANES, count)))
    index = iota((count, LANES), 1) + sec * LANES
    earlier = (others == own) & (iota((count, LANES), 0) < index)
    rank = jnp.sum(earlier.astype(F32), axis=0, keepdims=True)
    bucket = own * float(per_pair) + rank
    chosen = (iota((count, LANES), 0).astype(F32) == bucket).astype(F32)
    mine[...] = dot_rows(slots[...], chosen, EXACT)[: mine.shape[0]]

    for o in range(options):
        at = slice(o * width, (o + 1) * width)
        bwt[at, :] = jnp.transpose(branch_w[o].astype(F32)).astype(BF16)
        bb[at, :] = jnp.broadcast_to(column(table[o : o + 1, :]), (width, LANES))
    vht[...] = jnp.zeros_like(vht)
    vht[0:width, :] = jnp.transpose(value_w[...].astype(F32)).astype(BF16)
    pick_head = (iota((16, 2), 0) == iota((16, 2), 1)).astype(F32).astype(BF16)
    head_w = table[AT_HW, :].astype(BF16)
    vht[width : width + 16, :] = dot(pick_head, head_w).astype(BF16)
    vhw[:, 0:width] = value_w[...]
    vhw[:, width:] = dot_rows(
        head_w, (iota((2, 16), 0) == iota((2, 16), 1)).astype(F32).astype(BF16)
    ).astype(BF16)
    vb[...] = jnp.broadcast_to(column(table[AT_VB, :]), (width, LANES))
    ow[...] = jnp.broadcast_to(column(table[AT_OW, :]), (width, LANES))

    vgrad[...] = jnp.zeros_like(vgrad)
    outacc[...] = jnp.zeros_like(outacc)
    vbacc[...] = jnp.zeros_like(vbacc)
    rowacc[...] = jnp.zeros_like(rowacc)
    states[0] = enc[...].astype(F32)

    def wide(ref):
        return jnp.concatenate([ref[...], ref[...]], axis=1)

    def ahead(level, carry):
        labels = iota((options, LANES), 0).astype(F32)
        picked = (labels == mine[pl.ds(level, 1), :]).astype(F32)
        pick[level] = picked
        states[level + 1] = jnp.zeros((width, LANES), F32)

        def one_pair(t, inside):
            at = pl.ds(pl.multiple_of(t * two, two), two)
            state = states[level]
            act, slope = silu_pair(dot(bwt[at, :], state.astype(BF16)) + bb[at, :])
            dbr[level, at, :] = slope
            left = state + act[:width]
            right = state + act[width:]
            states[level + 1] += (
                pick[level, pl.ds(2 * t, 1), :] * left + pick[level, pl.ds(2 * t + 1, 1), :] * right
            )
            both = jnp.concatenate([left.astype(BF16), right.astype(BF16)], axis=1)
            low[level, t] = both
            got = dot(vht[...], both)
            act, slope = silu_pair(got[:width] + wide(vb))
            dval[level, t] = slope
            hidden = act.astype(BF16)
            hid[level, t] = hidden
            worth = jnp.sum(hidden.astype(F32) * wide(ow), axis=0, keepdims=True)
            for k in range(2):
                spot = pl.ds(2 * t + k, 1)
                span = slice(k * LANES, (k + 1) * LANES)
                val[spot, :] = worth[:, span]
                rew[spot, :] = got[width : width + 1, span]
                disc[spot, :] = got[width + 1 : width + 2, span]
            return inside

        lax.fori_loop(0, pairs, one_pair, 0, unroll=3)
        scalars = table[AT_SCALARS, :]
        reward = rew[...] + scalars[:, 1:2]
        discount = jax.nn.sigmoid(disc[...] + scalars[:, 2:3])
        value = val[...] + scalars[:, 3:4]
        quality = reward + discount * value
        top = jnp.max(quality, axis=0, keepdims=True)
        shifted = jnp.exp(quality - top)
        total = jnp.sum(shifted, axis=0, keepdims=True)
        soft_q[level] = shifted / total
        rows_g[level, 0] = discount
        rows_g[level, 1] = value
        live = (mine[pl.ds(depth, 1), :] > level.astype(F32)).astype(F32)

        def target(kind):
            return mine[pl.ds(depth + 1 + kind * depth + level, 1), :]

        gaps[level, 0:1, :] = live * (jnp.sum(picked * reward, axis=0, keepdims=True) - target(0))
        gaps[level, 1:2, :] = live * (jnp.sum(picked * discount, axis=0, keepdims=True) - target(1))
        gaps[level, 2:3, :] = live * (top + jnp.log(total) - target(2))
        return carry

    lax.fori_loop(0, depth, ahead, 0)

    states[depth] = jnp.zeros((width, LANES), F32)

    def behind(turn, carry):
        level = depth - 1 - turn
        picked = pick[level]
        grad_quality = gaps[level, 2:3, :] * soft_q[level]
        discount = rows_g[level, 0]
        value = rows_g[level, 1]
        head_one = (picked * gaps[level, 0:1, :] + grad_quality).astype(BF16).astype(F32)
        head_two = picked * gaps[level, 1:2, :] + grad_quality * value
        head_two = (head_two * discount * (1.0 - discount)).astype(BF16).astype(F32)
        grad_value = (grad_quality * discount).astype(BF16).astype(F32)
        rew[...] = head_one
        disc[...] = head_two
        val[...] = grad_value
        rowacc[0] += head_one
        rowacc[1] += head_two
        rowacc[2] += grad_value
        grad_next = states[depth]
        states[depth] = jnp.zeros((width, LANES), F32)

        def one_pair(t, inside):
            at = pl.ds(pl.multiple_of(t * two, two), two)

            def across(ref):
                return jnp.concatenate(
                    [ref[pl.ds(2 * t, 1), :], ref[pl.ds(2 * t + 1, 1), :]], axis=1
                )

            worth = across(val)
            grad_hidden = worth * wide(ow)
            grad_pre = (grad_hidden * dval[level, t]).astype(BF16)
            outacc[...] += hid[level, t].astype(F32) * worth
            vbacc[...] += grad_pre.astype(F32)
            line = iota((16, two), 0)
            heads = jnp.where(line == 0, across(rew), jnp.where(line == 1, across(disc), 0.0))
            stacked = jnp.concatenate([grad_pre, heads.astype(BF16)], axis=0)
            vgrad[...] += dot_lanes(stacked, low[level, t])
            moved = dot(vhw[...], stacked)
            left = moved[:, :LANES] + pick[level, pl.ds(2 * t, 1), :] * grad_next
            right = moved[:, LANES:] + pick[level, pl.ds(2 * t + 1, 1), :] * grad_next
            grad_branch = jnp.concatenate([left, right], axis=0) * dbr[level, at, :]
            grad_branch = grad_branch.astype(BF16)
            gb[level, at, :] = grad_branch
            weights = jnp.concatenate([branch_w[2 * t], branch_w[2 * t + 1]], axis=1)
            states[depth] += left + right + dot(weights, grad_branch)
            return inside

        lax.fori_loop(0, pairs, one_pair, 0, unroll=3)
        return carry

    lax.fori_loop(0, depth, behind, 0)

    linear_rows = h2.shape[0]
    half = (linear_rows + options * width + width) // 2
    rest = linear_rows - half
    ones = jnp.ones((16, depth * LANES), F32).astype(BF16)
    rounded = jnp.concatenate([states[level].astype(BF16) for level in range(depth)], axis=1)
    rounded = jnp.concatenate([rounded, ones], axis=0)
    small[...] = jnp.zeros_like(small)
    if half < keep.shape[0]:
        for k in range(2):
            parts[k, half:, :] = jnp.zeros((keep.shape[0] - half, LANES), BF16)

    def one_option(o, carry):
        at = pl.ds(pl.multiple_of(o * width, width), width)
        grads = jnp.concatenate([gb[level, at, :] for level in range(depth)], axis=1)
        got = dot_lanes(rounded, grads)
        at = pl.ds(pl.multiple_of(rest + o * width, 16), width)
        parts[1 - sec, at, :] = got[:width].astype(BF16)
        small[pl.ds(o, 1), :] = got[width : width + 1]
        return carry

    lax.fori_loop(0, options, one_option, 0, unroll=2)
    after = rest + options * width
    parts[1 - sec, after : after + width, :] = jnp.transpose(vgrad[0:width, :]).astype(BF16)

    grad_three = (states[depth].astype(BF16).astype(F32) * s3[...]).astype(BF16)
    g3[...] = grad_three
    chunk = linear_rows // 9

    def one_chunk(i, carry):
        at = pl.ds(pl.multiple_of(i * chunk, chunk), chunk)
        parts[sec, at, :] = dot_lanes(h2[at, :], grad_three).astype(BF16)
        return carry

    lax.fori_loop(0, 8, one_chunk, 0, unroll=4)
    last = dot_lanes(h2[8 * chunk :, :], grad_three).astype(BF16)
    parts[sec, 8 * chunk : half, :] = last[: half - 8 * chunk]
    parts[1 - sec, 0:rest, :] = last[half - 8 * chunk :]
    keep[...] = parts[0]
    send[...] = parts[1]

    small[AT_VB, :] = row_of(jnp.sum(vbacc[...], axis=1, keepdims=True))
    small[AT_OW, :] = row_of(jnp.sum(outacc[...], axis=1, keepdims=True))
    small[AT_HW, :] = vgrad[width : width + 2, :]
    small[AT_LB, :] = row_of(jnp.sum(grad_three.astype(F32), axis=1, keepdims=True))
    gap = gaps[...]
    loss = 0.5 * jnp.sum(jnp.sum(gap * gap, axis=0), axis=0, keepdims=True)
    lines = [loss] + [jnp.sum(rowacc[k], axis=0, keepdims=True) for k in range(3)]
    lane = iota((1, LANES), 1)
    scalars = jnp.zeros((1, LANES), F32)
    for k, line in enumerate(lines):
        scalars = jnp.where(lane == k, jnp.sum(line, axis=1, keepdims=True), scalars)
    small[AT_SCALARS, :] = scalars


def back_kernel(g3, lw, s2, h1, s1, w2t, g1, c2, sums, g2, t2, b1acc, b2acc):
    side = h1.shape[1]
    k1, k2 = h1.shape[2], w2t.shape[0]
    inner = side // 2 - 1
    row_len = inner * k2
    tap, pix = iota((LANES, 256), 1), iota((LANES, 256), 0)
    for yrel in range(2):
        for p in range(3):
            hit = (
                ((tap & 15) == (pix & 15))
                & ((tap >> 6) == (pix >> 6) + 2 * (1 - yrel))
                & (((tap >> 4) & 3) == ((pix >> 4) & 3) + 2 - 2 * p)
            )
            at = (yrel * 3 + p) * k2
            t2[:, at : at + k2] = dot_lanes(hit.astype(F32).astype(BF16), w2t[...]).astype(BF16)
    g2[0] = jnp.zeros(g2.shape[1:], BF16)
    g2[inner + 1] = jnp.zeros(g2.shape[1:], BF16)
    g1[0] = jnp.zeros(g1.shape[1:], BF16)
    g1[side + 1] = jnp.zeros(g1.shape[1:], BF16)
    b1acc[...] = jnp.zeros_like(b1acc)
    b2acc[...] = jnp.zeros_like(b2acc)
    c2[...] = jnp.zeros_like(c2)

    def out_row(y, carry):
        at = pl.ds(pl.multiple_of(y * row_len, row_len), row_len)
        grad = dot(lw[at, :], g3[...]) * s2[at, :].astype(F32)
        grad = grad.astype(BF16).reshape(inner, k2, LANES)
        g2[y + 1] = grad
        b2acc[...] += jnp.sum(grad.astype(F32), axis=0)
        grads = jnp.concatenate([grad[x] for x in range(inner)], axis=1)
        patches = jnp.concatenate(
            [h1[pl.ds(2 * y + 1, 4), 2 * x : 2 * x + 4].reshape(256, LANES) for x in range(inner)],
            axis=1,
        )
        c2[...] += dot_lanes(grads, patches)
        return carry

    lax.fori_loop(0, inner, out_row, 0)

    def in_rows(b, carry):
        zero = jnp.zeros((k2, LANES), BF16)
        cut = []
        for j in range(side // 4):
            pieces = []
            for yrel in range(2):
                for p in range(3):
                    x = 2 * j - 1 + p
                    pieces.append(g2[b + yrel, x] if 0 <= x < inner else zero)
            cut.append(jnp.concatenate(pieces, axis=0))
        got = dot(t2[...], jnp.concatenate(cut, axis=1))
        total = b1acc[...]
        for u in range(2):
            for j in range(side // 4):
                part = got[u * 64 : (u + 1) * 64, j * LANES : (j + 1) * LANES]
                slope = s1[2 * b + u + 1, 4 * j : 4 * j + 4].astype(F32)
                grad = (part.reshape(4, k1, LANES) * slope).astype(BF16)
                g1[2 * b + u + 1, 4 * j : 4 * j + 4] = grad
                total = total + jnp.sum(grad.astype(F32), axis=0)
        b1acc[...] = total
        return carry

    lax.fori_loop(0, side // 2, in_rows, 0)
    sums[...] = jnp.zeros_like(sums)
    sums[0:1, 0:k1] = row_of(jnp.sum(b1acc[...], axis=1, keepdims=True))
    sums[1:2, 0:k2] = row_of(jnp.sum(b2acc[...], axis=1, keepdims=True))


def first_kernel(section, frames, g1, after, c1, acc, side_acc):
    g = pl.program_id(0)
    side, k1 = g1.shape[1], g1.shape[2]
    tiles = frames.shape[1] // TILE

    @pl.when(g == 0)
    def _():
        acc[...] = jnp.zeros_like(acc)
        side_acc[...] = jnp.zeros_like(side_acc)

    zero = jnp.zeros((k1, LANES), BF16)
    total = acc[...]
    edges, edge_grads = [], []
    for r in range(STEP):
        pixels, grads = [], []
        for j in range(tiles):
            pixels.append(tile_rows(frames, r, j))
            pieces = []
            for half in range(2):
                for place in range(REACH):
                    x = 4 * j - 1 + place
                    pieces.append(g1[r + 1 - half, x] if 0 <= x < side else zero)
            grads.append(jnp.concatenate(pieces, axis=0))
        total = total + dot_lanes(
            jnp.concatenate(grads, axis=1), jnp.concatenate(pixels, axis=1)
        )
        edges.append(tile_rows(frames, r, tiles))
        edge_grads.append(
            jnp.concatenate([g1[r + 1 - half, side - 1] for half in range(2)], axis=0)
        )
    acc[...] = total
    side_acc[...] += dot_lanes(
        jnp.concatenate(edge_grads, axis=1), jnp.concatenate(edges, axis=1)
    )

    @pl.when(g == pl.num_programs(0) - 1)
    def _():
        grad = jnp.zeros((k1, 256), F32)
        for half in range(2):
            for place in range(REACH):
                at = (half * REACH + place) * k1
                grad = grad + dot_lanes(acc[at : at + k1, :], tap_map(half, place), EXACT)
            tap, pix = iota((256, 64), 0), iota((256, 64), 1)
            hit = (
                ((tap >> 6) == (pix & 3))
                & (((tap >> 3) & 7) == (pix >> 4) + 4 * half)
                & ((tap & 7) == ((pix >> 2) & 3) + 4)
            )
            grad = grad + dot_lanes(
                side_acc[half * k1 : (half + 1) * k1, :], hit.astype(F32), EXACT
            )
        for half in range(2):
            c1[half * k1 : (half + 1) * k1, :] = grad[:, half * LANES : (half + 1) * LANES].astype(
                BF16
            )


def pixels_kernel(section, w1t, mine, other, *rest):
    out, token, band, later = rest[-4:]
    g, part = pl.program_id(0), pl.program_id(1)
    side, k1 = mine.shape[1], mine.shape[2]
    img, channels = out.shape[1], out.shape[2]
    cols = 8
    reach = 3
    sec = section[0]
    line = cols * channels
    size = STEP * 4 * line
    flat = out.reshape(out.shape[0], img * channels, LANES)

    @pl.when((g == 0) & (part == 0))
    def _():
        token[...] = jnp.zeros_like(token)
        tap, pix = iota((size, 256), 1), iota((size, 256), 0)
        r = pix // (4 * line)
        u4 = (pix // line) % 4
        xx = (pix // channels) % cols
        c = pix % channels + sec * channels
        for yrel in range(STEP + 1):
            for p in range(reach):
                hit = (
                    ((tap >> 6) == c)
                    & (((tap >> 3) & 7) == 4 * (r + 1 - yrel) + u4)
                    & ((tap & 7) == xx + 4 - 4 * p)
                )
                at = (yrel * reach + p) * k1
                band[:, at : at + k1] = dot_lanes(hit.astype(F32).astype(BF16), w1t[...]).astype(
                    BF16
                )

    @pl.when(part == 0)
    def _():
        zero = jnp.zeros((k1, 2 * LANES), BF16)
        for j in range((img + cols - 1) // cols):
            pieces = []
            for yrel in range(STEP + 1):
                for p in range(reach):
                    x = 2 * j - 1 + p
                    if 0 <= x < side:
                        pieces.append(jnp.concatenate([mine[yrel, x], other[yrel, x]], axis=1))
                    else:
                        pieces.append(zero)
            got = dot(band[...], jnp.concatenate(pieces, axis=0))
            keep = min(line, img * channels - j * line)
            for k in range(4 * STEP):
                at = k * line
                flat[k, j * line : j * line + keep, :] = got[at : at + keep, :LANES]
                later[k, j * line : j * line + keep, :] = got[at : at + keep, LANES:]

    @pl.when(part == 1)
    def _():
        flat[...] = later[...]


def two_parts(value):
    high = value.astype(BF16).astype(F32)
    return jnp.concatenate([high, value - high], axis=0).astype(BF16)


def one_part(pair):
    rows = pair.shape[0] // 2
    pair = pair.astype(F32)
    return pair[:rows] + pair[rows:]


def merge_kernel(section, batch, keep, recv, small, c2, sums, *rest):
    outs, lines = rest[:-1], rest[-1]
    me = batch[0] % PLANE
    short = lines.shape[0] // PLANE
    size = keep.shape[0] // PLANE
    k2 = c2.shape[0]
    lines[...] = jnp.zeros_like(lines)
    at = small.shape[0]
    lines[0:at, :] = small[...]
    for half in range(2):
        lines[at : at + k2, :] = c2[:, half * LANES : (half + 1) * LANES]
        at += k2
    lines[at : at + sums.shape[0], :] = sums[...]
    for k, out in enumerate(outs):
        whose = me ^ k
        at = pl.ds(pl.multiple_of(whose * size, size), size)
        out[0:size, :] = (keep[at, :].astype(F32) + recv[at, :].astype(F32)).astype(BF16)
        out[size:, :] = two_parts(lines[pl.ds(pl.multiple_of(whose * short, short), short), :])


def plane_kernel(section, batch, *refs, depth):
    parts = refs[:PLANE]
    outs, total, lines = refs[-2 - depth : -2], refs[-2], refs[-1]
    me = batch[0] // PLANE
    size = total.shape[0]
    chunk = size // depth
    total[...] = sum(p[0:size, :].astype(F32) for p in parts).astype(BF16)
    lines[...] = sum(one_part(p[size:, :]) for p in parts)
    for k, out in enumerate(outs):
        whose = me ^ k
        out[0:chunk, :] = total[pl.ds(pl.multiple_of(whose * chunk, chunk), chunk), :]
        out[chunk:, :] = two_parts(lines[pl.ds(pl.multiple_of(whose * 8, 8), 8), :])


def depth_kernel(*refs, depth):
    parts, c1, out = refs[:depth], refs[depth], refs[-1]
    chunk = parts[0].shape[0] - 16
    out[0:chunk, :] = sum(p[0:chunk, :].astype(F32) for p in parts).astype(BF16)
    out[chunk : chunk + 16, :] = two_parts(sum(one_part(p[chunk:, :]) for p in parts))
    out[chunk + 16 :, :] = c1[...]


def gather_kernel(section, batch, *refs, depth):
    parts, out = refs[:depth], refs[-1]
    me = batch[0] // PLANE
    chunk = (out.shape[0] - 32) // depth - 16
    for k, part in enumerate(parts):
        whose = me ^ k
        at = pl.ds(pl.multiple_of(whose * chunk, chunk), chunk)
        out[at, :] = part[0:chunk, :]
        at = pl.ds(pl.multiple_of(depth * chunk + whose * 16, 16), 16)
        out[at, :] = part[chunk : chunk + 16, :]
    out[depth * (chunk + 16) :, :] = sum(p[chunk + 16 :, :].astype(F32) for p in parts).astype(BF16)


def unpack_kernel(section, batch, *refs):
    mine, other = refs[:PLANE], refs[PLANE : 2 * PLANE]
    loss, c1, b1, c2, b2, lw, lb, bw, bb, hw, hb, vw, vb, ow, ob, halves, lines = refs[-17:]
    width = lw.shape[1]
    options = bw.shape[0]
    k1, k2 = c1.shape[0], c2.shape[0]
    linear_rows = lw.shape[0]
    me, sec = batch[0] % PLANE, section[0]
    size = halves.shape[1] // PLANE
    short = lines.shape[0] // PLANE
    half = (linear_rows + options * width + width) // 2
    rest = linear_rows - half
    grad = [jnp.zeros((k1, LANES), F32) for _ in range(2)]
    for k in range(PLANE):
        at = pl.ds(pl.multiple_of((me ^ k) * size, size), size)
        halves[sec, at, :] = mine[k][0:size, :]
        halves[1 - sec, at, :] = other[k][0:size, :]
        for z in range(short // 8):
            pair = slice(size + 16 * z, size + 16 * z + 16)
            line = pl.ds(pl.multiple_of((me ^ k) * short + 8 * z, 8), 8)
            lines[line, :] = one_part(mine[k][pair, :]) + one_part(other[k][pair, :])
        at = size + 2 * short
        for part in range(2):
            span = slice(at + part * k1, at + (part + 1) * k1)
            grad[part] += mine[k][span, :].astype(F32) + other[k][span, :].astype(F32)
    for part in range(2):
        c1[:, part * LANES : (part + 1) * LANES] = grad[part]
    lw[0:half, :] = halves[0, 0:half, :].astype(F32)
    lw[half:, :] = halves[1, 0:rest, :].astype(F32)
    for o in range(options):
        at = rest + o * width
        bw[o] = halves[1, at : at + width, :].astype(F32)
    at = rest + options * width
    vw[...] = halves[1, at : at + width, :].astype(F32)
    bb[...] = lines[0:options, :]
    vb[...] = lines[AT_VB, :]
    ow[...] = lines[AT_OW, :]
    hw[...] = lines[AT_HW, :]
    lb[...] = lines[AT_LB, :]
    scalars = lines[AT_SCALARS, :]
    loss[...] = scalars[:, 0:1]
    hb[...] = scalars[:, 1:3]
    ob[...] = scalars[:, 3:4]
    at = TABLE
    for part in range(2):
        c2[:, part * LANES : (part + 1) * LANES] = lines[at : at + k2, :]
        at += k2
    b1[...] = lines[at : at + 1, 0:k1]
    b2[...] = lines[at + 1 : at + 2, 0:k2]


def numbers_kernel(
    options,
    depth,
    targets,
    destination,
    b1,
    b2,
    lb,
    bb,
    hw,
    vb,
    ow,
    hb,
    ob,
    out,
    table,
):
    levels, kinds = options.shape[0], targets.shape[0]
    slots = depth.shape[1]
    rows = [options[...].astype(F32), depth[...].astype(F32)]
    rows += [targets[k] for k in range(kinds)]
    rows.append(jnp.zeros((LANES - levels - 1 - kinds * levels, slots), F32))
    out[...] = jnp.transpose(jnp.concatenate(rows, axis=0))
    table[...] = jnp.zeros_like(table)
    table[0 : bb.shape[0], :] = bb[...]
    table[AT_VB, :] = vb[...]
    table[AT_OW, :] = ow[...].astype(F32)
    table[AT_HW, :] = hw[...].astype(F32)
    table[AT_LB, :] = lb[...]
    table[AT_B1, 0 : b1.shape[1]] = b1[...]
    table[AT_B2, 0 : b2.shape[1]] = b2[...]
    lane = iota((1, LANES), 1)
    scalars = jnp.zeros((1, LANES), F32)
    for k, value in ((1, hb[0]), (2, hb[1]), (3, ob[0])):
        scalars = jnp.where(lane == k, value, scalars)
    table[AT_SCALARS, :] = scalars
    for k in range(slots // LANES):
        part = destination[:, k * LANES : (k + 1) * LANES]
        table[AT_DEST + k : AT_DEST + k + 1, :] = part.astype(F32)


def whole(shape):
    zeros = (0,) * len(shape)
    return pl.BlockSpec(shape, lambda *_: zeros)


def params(size=VMEM_BYTES):
    return pltpu.CompilerParams(vmem_limit_bytes=size)


def shape_of(*shape, dtype=F32):
    return jax.ShapeDtypeStruct(shape, dtype)


def cost(flops, moved, transcendentals=0):
    return pl.CostEstimate(
        flops=int(flops), bytes_accessed=int(moved), transcendentals=int(transcendentals)
    )


def frame_block(frames):
    _, img, stack, _ = frames.shape
    return pl.BlockSpec((4 * STEP, img, stack, LANES), lambda g, s: (g, 0, 0, s[0]))


def encode(section, frames, w1t, w2t, lw, table):
    img = frames.shape[0]
    blocks = img // 4
    side = blocks - 1
    k1, k2, width = w1t.shape[0], w2t.shape[0], lw.shape[1]
    flat = lw.shape[0]
    outs = (
        shape_of(blocks, side, k1, LANES, dtype=BF16),
        shape_of(blocks, side, k1, LANES, dtype=BF16),
        shape_of(flat, LANES, dtype=BF16),
        shape_of(flat, LANES, dtype=BF16),
        shape_of(width, LANES, dtype=BF16),
        shape_of(width, LANES),
    )
    weights = (w1t, w2t, lw, table)
    out_specs = [whole(o.shape) for o in outs]
    out_specs[1] = pl.BlockSpec((STEP, side, k1, LANES), lambda g, s: (g, 0, 0, 0))
    return pl.pallas_call(
        encode_kernel,
        grid_spec=pltpu.PrefetchScalarGridSpec(
            num_scalar_prefetch=1,
            grid=(blocks // STEP,),
            in_specs=[frame_block(frames), *[whole(w.shape) for w in weights]],
            out_specs=out_specs,
            scratch_shapes=[
                pltpu.VMEM((2 * REACH * k1, 256), BF16),
                pltpu.VMEM((2 * k1, 64), BF16),
                pltpu.VMEM((k1, LANES), F32),
                pltpu.VMEM((k2, LANES), F32),
                pltpu.VMEM((side, k1, LANES), F32),
            ],
        ),
        out_shape=outs,
        compiler_params=params(),
        cost_estimate=cost(2 * 128 * 5.2e6, 1.3e7, 2.5e6),
        name="encode",
    )(section, frames, *weights)


def plan(section, slots, enc, s3, h2, branch_w, value_w, table, per_pair, depth, half_rows):
    width = enc.shape[0]
    options = branch_w.shape[0]
    two = 2 * width
    pairs = options // 2
    outs = (
        shape_of(half_rows, LANES, dtype=BF16),
        shape_of(half_rows, LANES, dtype=BF16),
        shape_of(TABLE, LANES),
        shape_of(width, LANES, dtype=BF16),
    )
    operands = (slots, enc, s3, h2, branch_w, value_w, table)
    vmem = pltpu.VMEM
    return pl.pallas_call(
        functools.partial(plan_kernel, per_pair=per_pair),
        grid_spec=pltpu.PrefetchScalarGridSpec(
            num_scalar_prefetch=1,
            grid=(1,),
            in_specs=[whole(o.shape) for o in operands],
            out_specs=[whole(o.shape) for o in outs],
            scratch_shapes=[
                vmem((2, half_rows, LANES), BF16),
                vmem((options * width, width), BF16),
                vmem((options * width, LANES), F32),
                vmem((width + 16, width), BF16),
                vmem((width, width + 16), BF16),
                vmem((width, LANES), F32),
                vmem((width, LANES), F32),
                vmem((16, LANES), F32),
                vmem((depth, options * width, LANES), F32),
                vmem((depth, pairs, width, 2 * LANES), F32),
                vmem((depth, pairs, width, 2 * LANES), BF16),
                vmem((depth, pairs, width, 2 * LANES), BF16),
                vmem((depth, options * width, LANES), BF16),
                vmem((depth + 1, width, LANES), F32),
                vmem((depth, options, LANES), F32),
                vmem((options, LANES), F32),
                vmem((options, LANES), F32),
                vmem((options, LANES), F32),
                vmem((depth, options, LANES), F32),
                vmem((depth, 3, LANES), F32),
                vmem((depth, 2, options, LANES), F32),
                vmem((width + 16, LANES), F32),
                vmem((width, 2 * LANES), F32),
                vmem((width, 2 * LANES), F32),
                vmem((3, options, LANES), F32),
            ],
        ),
        out_shape=outs,
        compiler_params=params(),
        cost_estimate=cost(2 * 3 * 2304 * 6 * 128 * 128, 4e6, 3e6),
        name="plan",
    )(section, *operands)


def back(g3, lw, s2, h1, s1, w2t):
    blocks, side, k1 = h1.shape[:3]
    k2 = w2t.shape[0]
    inner = side // 2 - 1
    outs = (
        shape_of(side + 2, side, k1, LANES, dtype=BF16),
        shape_of(k2, 256),
        shape_of(8, LANES),
    )
    return pl.pallas_call(
        back_kernel,
        out_shape=outs,
        scratch_shapes=[
            pltpu.VMEM((inner + 2, inner, k2, LANES), BF16),
            pltpu.VMEM((LANES, 6 * k2), BF16),
            pltpu.VMEM((k1, LANES), F32),
            pltpu.VMEM((k2, LANES), F32),
        ],
        compiler_params=params(WORK_BYTES),
        cost_estimate=cost(2 * 128 * 3e6, 7e6),
        name="back",
    )(g3, lw, s2, h1, s1, w2t)


ANYWHERE = pl.BlockSpec(memory_space=pl.ANY)


def row_window(g1, start):
    block = (pl.Element(STEP + 1),) + tuple(pl.Element(n) for n in g1.shape[1:])
    return pl.BlockSpec(block, lambda g, *_: (STEP * (start + g), 0, 0, 0))


def first(section, frames, g1, after):
    blocks = frames.shape[0] // 4
    k1 = g1.shape[2]
    return pl.pallas_call(
        first_kernel,
        grid_spec=pltpu.PrefetchScalarGridSpec(
            num_scalar_prefetch=1,
            grid=(blocks // STEP,),
            in_specs=[frame_block(frames), row_window(g1, 0), ANYWHERE],
            out_specs=whole((2 * k1, LANES)),
            scratch_shapes=[
                pltpu.VMEM((2 * REACH * k1, 256), F32),
                pltpu.VMEM((2 * k1, 64), F32),
            ],
        ),
        out_shape=shape_of(2 * k1, LANES, dtype=BF16),
        compiler_params=params(WORK_BYTES),
        cost_estimate=cost(2 * 128 * 5e6, 1e7),
        name="first",
    )(section, frames, g1, after)


def pixels(section, w1t, mine, other, img, channels, start, steps, after, done):
    k1 = mine.shape[2]
    block = (4 * STEP, img, channels, LANES)
    operands = (w1t, mine, other, after)
    specs = [whole(w1t.shape), row_window(mine, start), row_window(other, start), ANYWHERE]
    aliases = {}
    if done is not None:
        operands += (done,)
        specs.append(ANYWHERE)
        aliases = {len(operands): 0}
    return pl.pallas_call(
        pixels_kernel,
        grid_spec=pltpu.PrefetchScalarGridSpec(
            num_scalar_prefetch=1,
            grid=(steps, 2),
            in_specs=specs,
            out_specs=[
                pl.BlockSpec(block, lambda g, p, s: (start + g, 0, 0, (s[0] + p) % 2)),
                whole((8, LANES)),
            ],
            scratch_shapes=[
                pltpu.VMEM((STEP * channels * 32, (STEP + 1) * 3 * k1), BF16),
                pltpu.VMEM((4 * STEP, img * channels, LANES), F32),
            ],
        ),
        out_shape=[shape_of(img, img, channels, 2 * LANES), shape_of(8, LANES)],
        input_output_aliases=aliases,
        compiler_params=params(WORK_BYTES),
        cost_estimate=cost(2 * 256 * 5e6 * steps / 7, 1.9e7 * steps / 7),
        name="pixels",
    )(section, *operands)


def small_call(
    kernel, outs, operands, scratch=(), name=None, place=None, after=(), vmem=16 * 1024 * 1024
):
    specs = [pl.BlockSpec(memory_space=pltpu.VMEM)] * len(operands)
    if place is not None:
        operands = (*place, *operands)
        specs = [pl.BlockSpec(memory_space=pltpu.SMEM)] * len(place) + specs
    return pl.pallas_call(
        kernel,
        in_specs=specs + [ANYWHERE] * len(after),
        out_shape=outs,
        scratch_shapes=list(scratch),
        compiler_params=params(vmem),
        cost_estimate=cost(1e6, 4e6),
        name=name,
    )(*operands, *after)


def round_up(value, step):
    return -(-value // step) * step


def swapped(value):
    return lax.ppermute(value, "section", [(0, 1), (1, 0)])


def exchanged(value):
    return lax.all_to_all(value, "batch", split_axis=0, concat_axis=0, tiled=True)


def partner(value, distance):
    count = lax.axis_size("batch")
    return lax.ppermute(value, "batch", [(b, b ^ distance) for b in range(count)])


def local(
    frames,
    destination,
    options,
    depth,
    targets,
    conv_one,
    bias_one,
    conv_two,
    bias_two,
    linear_w,
    linear_b,
    branch_w,
    branch_b,
    head_w,
    head_b,
    value_w,
    value_b,
    out_w,
    out_b,
):
    section = lax.axis_index("section").astype(jnp.int32)[None]
    peers = lax.axis_size("batch")
    frame_count = frames.shape[3]
    per_pair = frame_count // peers
    levels = options.shape[0]
    frames = frames.transpose(1, 2, 0, 3)
    w1t, w2t = conv_one.T, conv_two.T
    encoder_params = (w1t, bias_one, w2t, bias_two, linear_w, linear_b)
    planner_params = (branch_w, branch_b, head_w.T, head_b, value_w, value_b, out_w.T, out_b)
    width = linear_w.shape[1]
    big_rows = linear_w.shape[0] + (branch_w.shape[0] + 1) * width
    chunk = round_up(-(-big_rows // (2 * peers)), 16)
    half_rows = chunk * peers

    scalars = pl.BlockSpec(memory_space=pltpu.SMEM)
    tiny = (bias_one, bias_two, linear_b, branch_b, head_w.T, value_b, out_w.T)
    tiny = [v if v.ndim > 1 else v[None, :] for v in tiny]
    numbers, table = pl.pallas_call(
        numbers_kernel,
        in_specs=[pl.BlockSpec(memory_space=pltpu.VMEM)] * (4 + len(tiny)) + [scalars] * 2,
        out_shape=[shape_of(frame_count, LANES), shape_of(TABLE, LANES)],
        compiler_params=params(),
        cost_estimate=cost(1e5, 2e5),
        name="numbers",
    )(options, depth[None, :], targets, destination[None, :], *tiny, head_b, out_b)
    slots = exchanged(numbers.reshape(peers, per_pair, LANES)).reshape(frame_count, LANES)

    h1, s1, h2, s2, enc, s3 = encode(section, frames, w1t, w2t, linear_w, table)
    keep, send, small, g3 = plan(
        section, slots, enc, s3, h2, branch_w, value_w, table, per_pair, levels, half_rows
    )
    recv = swapped(send)
    g1, c2, sums = back(g3, linear_w, s2, h1, s1, w2t)
    other = swapped(g1)
    place = (section, lax.axis_index("batch").astype(jnp.int32)[None])
    planes = peers // PLANE
    short = 8 * planes
    size = chunk * planes
    small_shape = functools.partial(shape_of, dtype=BF16)
    pieces = small_call(
        merge_kernel,
        [small_shape(size + 2 * short, LANES)] * PLANE,
        (keep, recv, small, c2, sums),
        [pltpu.VMEM((PLANE * short, LANES), F32)],
        name="merge",
        place=place,
    )
    pieces = [pieces[0]] + [partner(pieces[k], k) for k in range(1, PLANE)]
    c1 = first(section, frames, g1, pieces[0])
    pieces = small_call(
        functools.partial(plane_kernel, depth=planes),
        [small_shape(chunk + 16, LANES)] * planes,
        pieces,
        [pltpu.VMEM((size, LANES), BF16), pltpu.VMEM((short, LANES), F32)],
        name="plane",
        place=place,
        after=(c1,),
    )
    channels = frames.shape[2] // lax.axis_size("section")
    draw = functools.partial(pixels, section, w1t, g1, other, frames.shape[0], channels)
    frames_grad, token = draw(0, 2, pieces[0], None)
    pieces = [pieces[0]] + [partner(pieces[k], PLANE * k) for k in range(1, planes)]
    summed = small_call(
        functools.partial(depth_kernel, depth=planes),
        small_shape(chunk + 16 + c1.shape[0], LANES),
        (*pieces, c1),
        name="depth",
        after=(token,),
    )
    frames_grad, token = draw(2, 2, summed, frames_grad)
    pieces = [summed] + [partner(summed, PLANE * k) for k in range(1, planes)]
    summed = small_call(
        functools.partial(gather_kernel, depth=planes),
        small_shape(size + 2 * short + c1.shape[0], LANES),
        pieces,
        name="gather",
        place=place,
        after=(token,),
    )
    frames_grad, token = draw(4, 3, summed, frames_grad)
    pieces = [summed] + [partner(summed, k) for k in range(1, PLANE)]
    pieces += [swapped(p) for p in pieces]
    shapes = [p.shape for p in encoder_params + planner_params]
    flat = [s if len(s) > 1 else (1,) + s for s in shapes]
    rest = small_call(
        unpack_kernel,
        [shape_of(1, 1)] + [shape_of(*s) for s in flat],
        pieces,
        [pltpu.VMEM((2, half_rows, LANES), BF16), pltpu.VMEM((PLANE * short, LANES), F32)],
        name="unpack",
        place=place,
        after=(token,),
    )
    rest = [v.reshape(s) for v, s in zip(rest, [()] + shapes)]
    for at in (1, 3, 9, 13):
        rest[at] = rest[at].T
    return (rest[0], frames_grad.transpose(2, 0, 1, 3), *rest[1:])


def solution(mesh):
    placed = (
        P(None, None, None, "batch"),
        P("batch"),
        P(None, "batch"),
        P("batch"),
        P(None, None, "batch"),
    ) + (P(),) * 14
    return jax.shard_map(
        local,
        mesh=mesh,
        in_specs=placed,
        out_specs=(P(), P("section", None, None, "batch")) + (P(),) * 14,
        check_vma=False,
    )
```

```python
import functools
import math

import jax
import jax.numpy as jnp
from jax import lax
from jax.experimental import pallas as pl
from jax.experimental.pallas import tpu as pltpu
from jax.sharding import PartitionSpec as P

BF16 = jnp.bfloat16
F32 = jnp.float32
EXACT = lax.Precision.HIGHEST
LANES = 128
VMEM_BYTES = 32 * 1024 * 1024
TILE = 16
REACH = 5
STEP = 3
COLS = 8
AT_VB, AT_OW, AT_HW, AT_LB, AT_SCALARS, AT_B1, AT_B2, AT_DEST = (
    slice(18, 19),
    slice(19, 20),
    slice(20, 22),
    slice(22, 23),
    slice(23, 24),
    slice(24, 25),
    slice(25, 26),
    26,
)
TABLE = 32
PLANE = 4


def dot(a, b, precision=None):
    return jnp.dot(a, b, preferred_element_type=F32, precision=precision)


def dot_rows(a, b, precision=None):
    return lax.dot_general(
        a, b, (((0,), (0,)), ((), ())), preferred_element_type=F32, precision=precision
    )


def dot_lanes(a, b, precision=None):
    return lax.dot_general(
        a, b, (((1,), (1,)), ((), ())), preferred_element_type=F32, precision=precision
    )


def iota(shape, axis):
    return lax.broadcasted_iota(jnp.int32, shape, axis)


def column(row):
    n = row.shape[1]
    wide = jnp.broadcast_to(row, (n, n))
    return jnp.sum(jnp.where(iota((n, n), 0) == iota((n, n), 1), wide, 0.0), axis=1, keepdims=True)


def row_of(col):
    n = col.shape[0]
    wide = jnp.broadcast_to(col, (n, n))
    return jnp.sum(jnp.where(iota((n, n), 0) == iota((n, n), 1), wide, 0.0), axis=0, keepdims=True)


def soft(x):
    t = jnp.tanh(0.5 * x)
    return jnp.maximum(x, 0.0) - jnp.log(0.5 + 0.5 * jnp.abs(t)), 0.5 + 0.5 * t


def silu_pair(x):
    s = 0.5 + 0.5 * jnp.tanh(0.5 * x)
    act = x * s
    return act, s + act * (1.0 - s)


def tap_map(half, place):
    tap, pix = iota((256, 256), 0), iota((256, 256), 1)
    hit = (
        ((tap >> 6) == (pix & 3))
        & (((tap >> 3) & 7) == (pix >> 6) + 4 * half)
        & ((tap & 7) == ((pix >> 2) & 15) - 4 * (place - 1))
    )
    return hit.astype(F32)


def tile_rows(frames, r, j):
    channels = frames.shape[2]
    flat = frames.reshape(frames.shape[0], frames.shape[1] * channels, LANES)
    size = TILE * channels
    end = min((j + 1) * size, flat.shape[1])
    return flat[4 * r : 4 * r + 4, j * size : end, :].reshape(4 * (end - j * size), LANES)


def encode_kernel(
    section,
    frames,
    w1t,
    w2t,
    lw,
    table,
    h1,
    s1,
    h2,
    s2,
    enc,
    s3,
    band,
    edge,
    bias1,
    bias2,
    held,
):
    g = pl.program_id(0)
    side = h1.shape[1]
    tiles = frames.shape[1] // TILE
    k1, k2 = w1t.shape[0], w2t.shape[0]
    reach_rows = REACH * k1

    @pl.when(g == 0)
    def _():
        for half in range(2):
            for place in range(REACH):
                at = half * reach_rows + place * k1
                taps = dot(w1t[...], tap_map(half, place).astype(BF16))
                band[at : at + k1, :] = taps.astype(BF16)
            tap, pix = iota((256, 64), 0), iota((256, 64), 1)
            hit = (
                ((tap >> 6) == (pix & 3))
                & (((tap >> 3) & 7) == (pix >> 4) + 4 * half)
                & ((tap & 7) == ((pix >> 2) & 3) + 4)
            )
            taps = dot(w1t[...], hit.astype(F32).astype(BF16))
            edge[half * k1 : (half + 1) * k1, :] = taps.astype(BF16)
        bias1[...] = jnp.broadcast_to(column(table[AT_B1, 0:k1]), bias1.shape)
        bias2[...] = jnp.broadcast_to(column(table[AT_B2, 0:k2]), bias2.shape)
        held[...] = jnp.zeros_like(held)
        h1[...] = jnp.zeros_like(h1)

    inner = side // 2 - 1
    row_len = inner * k2

    def second_row(y):
        for first in range(0, inner, 2):
            xs = [x for x in (first, first + 1) if x < inner]
            cut = [h1[pl.ds(2 * y + 1, 4), 2 * x : 2 * x + 4].reshape(256, LANES) for x in xs]
            patch = cut[0] if len(cut) == 1 else jnp.concatenate(cut, axis=1)
            got = dot(w2t[...], patch)
            for k, x in enumerate(xs):
                value, slope = soft(got[:, k * LANES : (k + 1) * LANES] + bias2[...])
                at = pl.ds(pl.multiple_of(y * row_len + x * k2, k2), k2)
                h2[at, :] = value.astype(BF16)
                s2[at, :] = slope.astype(BF16)

    ready_row = jnp.maximum((STEP * g - 6) // 2, 0)
    second_row(ready_row)
    second_row(ready_row + 1)

    for r in range(STEP):
        low, high = {}, {}

        def add(x, one, two):
            low[x] = low[x] + one if x in low else one
            high[x] = high[x] + two if x in high else two

        last = dot(edge[...], tile_rows(frames, r, tiles))
        add(side - 1, last[:k1], last[k1:])
        done = 0
        for first in range(0, tiles, 2):
            js = [j for j in (first, first + 1) if j < tiles]
            cut = [tile_rows(frames, r, j) for j in js]
            got = dot(band[...], cut[0] if len(cut) == 1 else jnp.concatenate(cut, axis=1))
            for k, j in enumerate(js):
                for place in range(REACH):
                    x = 4 * j - 1 + place
                    if 0 <= x < side:
                        at = place * k1
                        span = slice(k * LANES, (k + 1) * LANES)
                        add(
                            x,
                            got[at : at + k1, span],
                            got[reach_rows + at : reach_rows + at + k1, span],
                        )
            ready = side if js[-1] == tiles - 1 else 4 * js[-1] + 3
            for x in range(done, ready):
                value, slope = soft(held[x] + high[x] + bias1[...])
                held[x] = low[x]
                h1[STEP * g + r, x] = value.astype(BF16)
                s1[r, x] = slope.astype(BF16)
            done = ready

    @pl.when(g == pl.num_programs(0) - 1)
    def _():
        for y in range(inner - 2, inner):
            second_row(y)
        value, slope = soft(dot_rows(lw[...], h2[...]) + column(table[AT_LB, :]))
        enc[...] = value.astype(BF16)
        s3[...] = slope


def plan_kernel(
    section,
    slots,
    enc,
    s3,
    h2,
    branch_w,
    value_w,
    table,
    keep,
    send,
    small,
    g3,
    parts,
    bwt,
    bb,
    vht,
    vhw,
    vb,
    ow,
    mine,
    dbr,
    dval,
    low,
    hid,
    gb,
    states,
    pick,
    rew,
    disc,
    val,
    soft_q,
    gaps,
    rows_g,
    vgrad,
    outacc,
    vbacc,
    rowacc,
    *,
    per_pair,
):
    width = enc.shape[0]
    options = branch_w.shape[0]
    depth = states.shape[0] - 1
    pairs = options // 2
    two = 2 * width
    sec = section[0]

    count = slots.shape[0]
    dest = jnp.concatenate(
        [table[AT_DEST + k : AT_DEST + k + 1, :] for k in range(count // LANES)], axis=1
    )
    own = jnp.where(sec == 0, dest[:, :LANES], dest[:, LANES:])
    others = jnp.transpose(jnp.broadcast_to(dest, (LANES, count)))
    index = iota((count, LANES), 1) + sec * LANES
    earlier = (others == own) & (iota((count, LANES), 0) < index)
    rank = jnp.sum(earlier.astype(F32), axis=0, keepdims=True)
    bucket = own * float(per_pair) + rank
    chosen = (iota((count, LANES), 0).astype(F32) == bucket).astype(F32)
    mine[...] = dot_rows(slots[...], chosen, EXACT)[: mine.shape[0]]

    for o in range(options):
        at = slice(o * width, (o + 1) * width)
        bwt[at, :] = jnp.transpose(branch_w[o].astype(F32)).astype(BF16)
        bb[at, :] = jnp.broadcast_to(column(table[o : o + 1, :]), (width, LANES))
    vht[...] = jnp.zeros_like(vht)
    vht[0:width, :] = jnp.transpose(value_w[...].astype(F32)).astype(BF16)
    pick_head = (iota((16, 2), 0) == iota((16, 2), 1)).astype(F32).astype(BF16)
    head_w = table[AT_HW, :].astype(BF16)
    vht[width : width + 16, :] = dot(pick_head, head_w).astype(BF16)
    vhw[:, 0:width] = value_w[...]
    vhw[:, width:] = dot_rows(
        head_w, (iota((2, 16), 0) == iota((2, 16), 1)).astype(F32).astype(BF16)
    ).astype(BF16)
    vb[...] = jnp.broadcast_to(column(table[AT_VB, :]), (width, LANES))
    ow[...] = jnp.broadcast_to(column(table[AT_OW, :]), (width, LANES))

    vgrad[...] = jnp.zeros_like(vgrad)
    outacc[...] = jnp.zeros_like(outacc)
    vbacc[...] = jnp.zeros_like(vbacc)
    rowacc[...] = jnp.zeros_like(rowacc)
    states[0] = enc[...].astype(F32)

    def wide(ref):
        return jnp.concatenate([ref[...], ref[...]], axis=1)

    def ahead(level, carry):
        labels = iota((options, LANES), 0).astype(F32)
        picked = (labels == mine[pl.ds(level, 1), :]).astype(F32)
        pick[level] = picked
        states[level + 1] = jnp.zeros((width, LANES), F32)

        def one_pair(t, inside):
            at = slice(t * two, (t + 1) * two)
            state = states[level]
            act, slope = silu_pair(dot(bwt[at, :], state.astype(BF16)) + bb[at, :])
            dbr[level, at, :] = slope
            left = state + act[:width]
            right = state + act[width:]
            states[level + 1] += (
                pick[level, 2 * t : 2 * t + 1, :] * left
                + pick[level, 2 * t + 1 : 2 * t + 2, :] * right
            )
            both = jnp.concatenate([left.astype(BF16), right.astype(BF16)], axis=1)
            low[level, t] = both
            got = dot(vht[...], both)
            act, slope = silu_pair(got[:width] + wide(vb))
            dval[level, t] = slope
            hidden = act.astype(BF16)
            hid[level, t] = hidden
            worth = jnp.sum(hidden.astype(F32) * wide(ow), axis=0, keepdims=True)
            for k in range(2):
                spot = slice(2 * t + k, 2 * t + k + 1)
                span = slice(k * LANES, (k + 1) * LANES)
                val[spot, :] = worth[:, span]
                rew[spot, :] = got[width : width + 1, span]
                disc[spot, :] = got[width + 1 : width + 2, span]
            return inside

        for t in range(pairs):
            one_pair(t, 0)
        scalars = table[AT_SCALARS, :]
        reward = rew[...] + scalars[:, 1:2]
        discount = jax.nn.sigmoid(disc[...] + scalars[:, 2:3])
        value = val[...] + scalars[:, 3:4]
        quality = reward + discount * value
        top = jnp.max(quality, axis=0, keepdims=True)
        shifted = jnp.exp(quality - top)
        total = jnp.sum(shifted, axis=0, keepdims=True)
        soft_q[level] = shifted / total
        rows_g[level, 0] = discount
        rows_g[level, 1] = value
        live = (mine[pl.ds(depth, 1), :] > level.astype(F32)).astype(F32)

        def target(kind):
            return mine[pl.ds(depth + 1 + kind * depth + level, 1), :]

        gaps[level, 0:1, :] = live * (jnp.sum(picked * reward, axis=0, keepdims=True) - target(0))
        gaps[level, 1:2, :] = live * (jnp.sum(picked * discount, axis=0, keepdims=True) - target(1))
        gaps[level, 2:3, :] = live * (top + jnp.log(total) - target(2))
        return carry

    lax.fori_loop(0, depth, ahead, 0)

    states[depth] = jnp.zeros((width, LANES), F32)

    def behind(turn, carry):
        level = depth - 1 - turn
        picked = pick[level]
        grad_quality = gaps[level, 2:3, :] * soft_q[level]
        discount = rows_g[level, 0]
        value = rows_g[level, 1]
        head_one = (picked * gaps[level, 0:1, :] + grad_quality).astype(BF16).astype(F32)
        head_two = picked * gaps[level, 1:2, :] + grad_quality * value
        head_two = (head_two * discount * (1.0 - discount)).astype(BF16).astype(F32)
        grad_value = (grad_quality * discount).astype(BF16).astype(F32)
        rew[...] = head_one
        disc[...] = head_two
        val[...] = grad_value
        rowacc[0] += head_one
        rowacc[1] += head_two
        rowacc[2] += grad_value
        grad_next = states[depth]
        states[depth] = jnp.zeros((width, LANES), F32)

        def one_pair(t, inside):
            at = slice(t * two, (t + 1) * two)

            def across(ref):
                return jnp.concatenate([ref[2 * t : 2 * t + 1], ref[2 * t + 1 : 2 * t + 2]], axis=1)

            worth = across(val)
            grad_hidden = worth * wide(ow)
            grad_pre = (grad_hidden * dval[level, t]).astype(BF16)
            outacc[...] += hid[level, t].astype(F32) * worth
            vbacc[...] += grad_pre.astype(F32)
            line = iota((16, two), 0)
            heads = jnp.where(line == 0, across(rew), jnp.where(line == 1, across(disc), 0.0))
            stacked = jnp.concatenate([grad_pre, heads.astype(BF16)], axis=0)
            vgrad[...] += dot_lanes(stacked, low[level, t])
            moved = dot(vhw[...], stacked)
            left = moved[:, :LANES] + pick[level, 2 * t : 2 * t + 1, :] * grad_next
            right = moved[:, LANES:] + pick[level, 2 * t + 1 : 2 * t + 2, :] * grad_next
            grad_branch = jnp.concatenate([left, right], axis=0) * dbr[level, at, :]
            grad_branch = grad_branch.astype(BF16)
            gb[level, at, :] = grad_branch
            weights = jnp.concatenate([branch_w[2 * t], branch_w[2 * t + 1]], axis=1)
            states[depth] += left + right + dot(weights, grad_branch)
            return inside

        for t in range(pairs):
            one_pair(t, 0)
        return carry

    lax.fori_loop(0, depth, behind, 0)

    linear_rows = h2.shape[0]
    half = (linear_rows + options * width + width) // 2
    rest = linear_rows - half
    ones = jnp.ones((16, depth * LANES), F32).astype(BF16)
    rounded = jnp.concatenate([states[level].astype(BF16) for level in range(depth)], axis=1)
    rounded = jnp.concatenate([rounded, ones], axis=0)
    small[...] = jnp.zeros_like(small)
    if half < keep.shape[0]:
        for k in range(2):
            parts[k, half:, :] = jnp.zeros((keep.shape[0] - half, LANES), BF16)

    def one_option(o, carry):
        at = pl.ds(pl.multiple_of(o * width, width), width)
        grads = jnp.concatenate([gb[level, at, :] for level in range(depth)], axis=1)
        got = dot_lanes(rounded, grads)
        at = pl.ds(pl.multiple_of(rest + o * width, 16), width)
        parts[1 - sec, at, :] = got[:width].astype(BF16)
        small[pl.ds(o, 1), :] = got[width : width + 1]
        return carry

    lax.fori_loop(0, options, one_option, 0, unroll=2)
    after = rest + options * width
    parts[1 - sec, after : after + width, :] = jnp.transpose(vgrad[0:width, :]).astype(BF16)

    grad_three = (states[depth].astype(BF16).astype(F32) * s3[...]).astype(BF16)
    g3[...] = grad_three
    chunk = linear_rows // 9

    def one_chunk(i, carry):
        at = pl.ds(pl.multiple_of(i * chunk, chunk), chunk)
        parts[sec, at, :] = dot_lanes(h2[at, :], grad_three).astype(BF16)
        return carry

    lax.fori_loop(0, 8, one_chunk, 0, unroll=4)
    last = dot_lanes(h2[8 * chunk :, :], grad_three).astype(BF16)
    parts[sec, 8 * chunk : half, :] = last[: half - 8 * chunk]
    parts[1 - sec, 0:rest, :] = last[half - 8 * chunk :]
    keep[...] = parts[0]
    send[...] = parts[1]

    small[AT_VB, :] = row_of(jnp.sum(vbacc[...], axis=1, keepdims=True))
    small[AT_OW, :] = row_of(jnp.sum(outacc[...], axis=1, keepdims=True))
    small[AT_HW, :] = vgrad[width : width + 2, :]
    small[AT_LB, :] = row_of(jnp.sum(grad_three.astype(F32), axis=1, keepdims=True))
    gap = gaps[...]
    loss = 0.5 * jnp.sum(jnp.sum(gap * gap, axis=0), axis=0, keepdims=True)
    lines = [loss] + [jnp.sum(rowacc[k], axis=0, keepdims=True) for k in range(3)]
    lane = iota((1, LANES), 1)
    scalars = jnp.zeros((1, LANES), F32)
    for k, line in enumerate(lines):
        scalars = jnp.where(lane == k, jnp.sum(line, axis=1, keepdims=True), scalars)
    small[AT_SCALARS, :] = scalars


def back_kernel(section, g3, lw, s2, s1, w1t, w2t, g1, g2, sums, band, t2, b1acc, b2acc):
    side, k1 = s1.shape[1], s1.shape[2]
    k2 = w2t.shape[0]
    inner = side // 2 - 1
    row_len = inner * k2
    tap, pix = iota((LANES, 256), 1), iota((LANES, 256), 0)
    for yrel in range(2):
        for p in range(3):
            hit = (
                ((tap & 15) == (pix & 15))
                & ((tap >> 6) == (pix >> 6) + 2 * (1 - yrel))
                & (((tap >> 4) & 3) == ((pix >> 4) & 3) + 2 - 2 * p)
            )
            at = (yrel * 3 + p) * k2
            t2[:, at : at + k2] = dot_lanes(hit.astype(F32).astype(BF16), w2t[...]).astype(BF16)
    g2[0] = jnp.zeros(g2.shape[1:], BF16)
    g2[inner + 1] = jnp.zeros(g2.shape[1:], BF16)
    g1[0] = jnp.zeros(g1.shape[1:], BF16)
    g1[side + 1] = jnp.zeros(g1.shape[1:], BF16)
    zero = jnp.zeros((k2, LANES), BF16)
    total_one = jnp.zeros((k1, LANES), F32)
    total_two = jnp.zeros((k2, LANES), F32)
    for b in range(side // 2):
        if b < inner:
            at = slice(b * row_len, (b + 1) * row_len)
            grad = dot(lw[at, :], g3[...]) * s2[at, :].astype(F32)
            grad = grad.astype(BF16).reshape(inner, k2, LANES)
            g2[b + 1] = grad
            total_two = total_two + jnp.sum(grad.astype(F32), axis=0)
        cut = []
        for j in range(side // 4):
            pieces = []
            for yrel in range(2):
                for p in range(3):
                    x = 2 * j - 1 + p
                    pieces.append(g2[b + yrel, x] if 0 <= x < inner else zero)
            cut.append(jnp.concatenate(pieces, axis=0))
        got = dot(t2[...], jnp.concatenate(cut, axis=1))
        for u in range(2):
            for j in range(side // 4):
                part = got[u * 64 : (u + 1) * 64, j * LANES : (j + 1) * LANES]
                slope = s1[2 * b + u + 1, 4 * j : 4 * j + 4].astype(F32)
                grad = (part.reshape(4, k1, LANES) * slope).astype(BF16)
                g1[2 * b + u + 1, 4 * j : 4 * j + 4] = grad
                total_one = total_one + jnp.sum(grad.astype(F32), axis=0)
    sums[...] = jnp.zeros_like(sums)
    sums[0:1, 0:k1] = row_of(jnp.sum(total_one, axis=1, keepdims=True))
    sums[1:2, 0:k2] = row_of(jnp.sum(total_two, axis=1, keepdims=True))
    pixel_band(section[0], w1t, band)


def pixel_band(sec, w1t, band):
    k1 = w1t.shape[0]
    size = band.shape[0]
    channels = size // (STEP * 4 * COLS)
    line = COLS * channels
    tap, pix = iota((size, 256), 1), iota((size, 256), 0)
    r = pix // (4 * line)
    u4 = (pix // line) % 4
    xx = (pix // channels) % COLS
    c = pix % channels + sec * channels
    for yrel in range(STEP + 1):
        for p in range(3):
            hit = (
                ((tap >> 6) == c)
                & (((tap >> 3) & 7) == 4 * (r + 1 - yrel) + u4)
                & ((tap & 7) == xx + 4 - 4 * p)
            )
            at = (yrel * 3 + p) * k1
            band[:, at : at + k1] = dot_lanes(hit.astype(F32).astype(BF16), w1t[...]).astype(BF16)


def second_kernel(h1, g2, after, c2):
    side = h1.shape[1]
    inner = side // 2 - 1
    total = jnp.zeros(c2.shape, F32)
    for y in range(inner):
        grads = jnp.concatenate([g2[y + 1, x] for x in range(inner)], axis=1)
        patches = jnp.concatenate(
            [h1[2 * y + 1 : 2 * y + 5, 2 * x : 2 * x + 4].reshape(256, LANES) for x in range(inner)],
            axis=1,
        )
        total = total + dot_lanes(grads, patches)
    c2[...] = total


def first_kernel(section, frames, g1, after, c1, acc, side_acc):
    g = pl.program_id(0)
    side, k1 = g1.shape[1], g1.shape[2]
    tiles = frames.shape[1] // TILE

    @pl.when(g == 0)
    def _():
        acc[...] = jnp.zeros_like(acc)
        side_acc[...] = jnp.zeros_like(side_acc)

    zero = jnp.zeros((k1, LANES), BF16)
    total = acc[...]
    edges, edge_grads = [], []
    for r in range(STEP):
        pixels, grads = [], []
        for j in range(tiles):
            pixels.append(tile_rows(frames, r, j))
            pieces = []
            for half in range(2):
                for place in range(REACH):
                    x = 4 * j - 1 + place
                    pieces.append(g1[r + 1 - half, x] if 0 <= x < side else zero)
            grads.append(jnp.concatenate(pieces, axis=0))
        total = total + dot_lanes(
            jnp.concatenate(grads, axis=1), jnp.concatenate(pixels, axis=1)
        )
        edges.append(tile_rows(frames, r, tiles))
        edge_grads.append(
            jnp.concatenate([g1[r + 1 - half, side - 1] for half in range(2)], axis=0)
        )
    acc[...] = total
    side_acc[...] += dot_lanes(
        jnp.concatenate(edge_grads, axis=1), jnp.concatenate(edges, axis=1)
    )

    @pl.when(g == pl.num_programs(0) - 1)
    def _():
        grad = jnp.zeros((k1, 256), F32)
        for half in range(2):
            for place in range(REACH):
                at = (half * REACH + place) * k1
                grad = grad + dot_lanes(acc[at : at + k1, :], tap_map(half, place), EXACT)
            tap, pix = iota((256, 64), 0), iota((256, 64), 1)
            hit = (
                ((tap >> 6) == (pix & 3))
                & (((tap >> 3) & 7) == (pix >> 4) + 4 * half)
                & ((tap & 7) == ((pix >> 2) & 3) + 4)
            )
            grad = grad + dot_lanes(
                side_acc[half * k1 : (half + 1) * k1, :], hit.astype(F32), EXACT
            )
        for half in range(2):
            c1[half * k1 : (half + 1) * k1, :] = grad[:, half * LANES : (half + 1) * LANES].astype(
                BF16
            )


def pixels_kernel(section, band, mine, other, *rest, start):
    out, token, held, sems = rest[-4:]
    g = pl.program_id(0)
    steps = pl.num_programs(0)
    side, k1 = mine.shape[1], mine.shape[2]
    img, channels = out.shape[1], out.shape[2]
    sec = section[0]
    line = COLS * channels
    flat = held.reshape(2, 2, 4 * STEP, img * channels, LANES)
    slot = g % 2

    def writes(step, at):
        rows = pl.ds(pl.multiple_of(4 * STEP * (start + step), 4), 4 * STEP)
        places = (sec * LANES, (1 - sec) * LANES)
        return [
            pltpu.make_async_copy(
                held.at[at, k],
                out.at[rows, :, :, pl.ds(pl.multiple_of(places[k], LANES), LANES)],
                sems.at[at, k],
            )
            for k in range(2)
        ]

    @pl.when(g >= 2)
    def _():
        for copy in writes(g - 2, slot):
            copy.wait()

    zero = jnp.zeros((k1, 2 * LANES), BF16)
    for j in range((img + COLS - 1) // COLS):
        pieces = []
        for yrel in range(STEP + 1):
            for p in range(3):
                x = 2 * j - 1 + p
                if 0 <= x < side:
                    pieces.append(jnp.concatenate([mine[yrel, x], other[yrel, x]], axis=1))
                else:
                    pieces.append(zero)
        got = dot(band[...], jnp.concatenate(pieces, axis=0))
        keep = min(line, img * channels - j * line)
        for k in range(4 * STEP):
            at = k * line
            span = slice(j * line, j * line + keep)
            flat[slot, 0, k, span, :] = got[at : at + keep, :LANES]
            flat[slot, 1, k, span, :] = got[at : at + keep, LANES:]
    for copy in writes(g, slot):
        copy.start()
    token[...] = jnp.zeros_like(token)

    @pl.when(g == steps - 1)
    def _():
        @pl.when(g >= 1)
        def _():
            for copy in writes(g - 1, 1 - slot):
                copy.wait()

        for copy in writes(g, slot):
            copy.wait()


def two_parts(value):
    high = value.astype(BF16).astype(F32)
    return jnp.concatenate([high, value - high], axis=0).astype(BF16)


def one_part(pair):
    rows = pair.shape[0] // 2
    pair = pair.astype(F32)
    return pair[:rows] + pair[rows:]


def merge_kernel(keep, recv, after, out):
    size = out.shape[1]
    for k in range(out.shape[0]):
        at = slice(k * size, (k + 1) * size)
        out[k] = (keep[at, :].astype(F32) + recv[at, :].astype(F32)).astype(BF16)


def plane_kernel(got, after, out):
    size = out.shape[1]
    for k in range(out.shape[0]):
        at = slice(k * size, (k + 1) * size)
        out[k] = sum(got[p, at, :].astype(F32) for p in range(got.shape[0])).astype(BF16)


def depth_kernel(got, c1, c2, small, sums, after, out):
    planes, chunk = got.shape[0], got.shape[1]
    total = sum(got[p].astype(F32) for p in range(planes)).astype(BF16)
    late = jnp.concatenate(
        [c1[...], c2[:, :LANES].astype(BF16), c2[:, LANES:].astype(BF16)]
        + [two_parts(jnp.concatenate([small[...], sums[...]], axis=0))],
        axis=0,
    )
    for p in range(planes):
        out[p, 0:chunk, :] = total
        out[p, chunk:, :] = late


def gather_kernel(got, after, out, *, late):
    planes = got.shape[0]
    chunk = got.shape[1] - late
    part = TABLE + 8
    plain = late - 2 * part
    sums = sum(got[p, chunk : chunk + plain, :].astype(F32) for p in range(planes)).astype(BF16)
    fine = sum(one_part(got[p, chunk + plain :, :]) for p in range(planes))
    tail = jnp.concatenate([sums, two_parts(fine)], axis=0)
    for k in range(out.shape[0]):
        for p in range(planes):
            out[k, p * chunk : (p + 1) * chunk, :] = got[p, 0:chunk, :]
        out[k, planes * chunk :, :] = tail


def relay_kernel(got, after, out):
    out[...] = got[...]


def unpack_kernel(section, mine, other, after, *refs):
    loss, c1, b1, c2, b2, lw, lb, bw, bb, hw, hb, vw, vb, ow, ob, halves = refs
    width = lw.shape[1]
    options = bw.shape[0]
    k1, k2 = c1.shape[0], c2.shape[0]
    linear_rows = lw.shape[0]
    sec = section[0]
    size = halves.shape[1] // PLANE
    half = (linear_rows + options * width + width) // 2
    rest = linear_rows - half
    for k in range(PLANE):
        at = slice(k * size, (k + 1) * size)
        halves[sec, at, :] = mine[k, 0:size, :]
        halves[1 - sec, at, :] = other[k, 0:size, :]
    lw[0:half, :] = halves[0, 0:half, :].astype(F32)
    lw[half:, :] = halves[1, 0:rest, :].astype(F32)
    for o in range(options):
        at = rest + o * width
        bw[o] = halves[1, at : at + width, :].astype(F32)
    at = rest + options * width
    vw[...] = halves[1, at : at + width, :].astype(F32)

    def summed(start, count):
        span = slice(size + start, size + start + count)
        return sum(v[k, span, :].astype(F32) for v in (mine, other) for k in range(PLANE))

    at = 0
    for ref, count in ((c1, k1), (c2, k2)):
        for part in range(2):
            ref[:, part * LANES : (part + 1) * LANES] = summed(at, count)
            at += count
    lines = summed(at, 2 * (TABLE + 8))
    lines = lines[: TABLE + 8] + lines[TABLE + 8 :]
    bb[...] = lines[0:options, :]
    vb[...] = lines[AT_VB, :]
    ow[...] = lines[AT_OW, :]
    hw[...] = lines[AT_HW, :]
    lb[...] = lines[AT_LB, :]
    scalars = lines[AT_SCALARS, :]
    loss[...] = scalars[:, 0:1]
    hb[...] = scalars[:, 1:3]
    ob[...] = scalars[:, 3:4]
    b1[...] = lines[TABLE : TABLE + 1, 0:k1]
    b2[...] = lines[TABLE + 1 : TABLE + 2, 0:k2]


def numbers_kernel(
    options,
    depth,
    targets,
    destination,
    b1,
    b2,
    lb,
    bb,
    hw,
    vb,
    ow,
    hb,
    ob,
    out,
    table,
):
    levels, kinds = options.shape[0], targets.shape[0]
    slots = depth.shape[1]
    rows = [options[...].astype(F32), depth[...].astype(F32)]
    rows += [targets[k] for k in range(kinds)]
    rows.append(jnp.zeros((LANES - levels - 1 - kinds * levels, slots), F32))
    out[...] = jnp.transpose(jnp.concatenate(rows, axis=0))
    table[...] = jnp.zeros_like(table)
    table[0 : bb.shape[0], :] = bb[...]
    table[AT_VB, :] = vb[...]
    table[AT_OW, :] = ow[...].astype(F32)
    table[AT_HW, :] = hw[...].astype(F32)
    table[AT_LB, :] = lb[...]
    table[AT_B1, 0 : b1.shape[1]] = b1[...]
    table[AT_B2, 0 : b2.shape[1]] = b2[...]
    lane = iota((1, LANES), 1)
    scalars = jnp.zeros((1, LANES), F32)
    for k, value in ((1, hb[0]), (2, hb[1]), (3, ob[0])):
        scalars = jnp.where(lane == k, value, scalars)
    table[AT_SCALARS, :] = scalars
    for k in range(slots // LANES):
        part = destination[:, k * LANES : (k + 1) * LANES]
        table[AT_DEST + k : AT_DEST + k + 1, :] = part.astype(F32)


def whole(shape):
    zeros = (0,) * len(shape)
    return pl.BlockSpec(shape, lambda *_: zeros)


def params():
    return pltpu.CompilerParams(vmem_limit_bytes=VMEM_BYTES)


def shape_of(*shape, dtype=F32):
    return jax.ShapeDtypeStruct(shape, dtype)


def cost(microseconds):
    return pl.CostEstimate(
        flops=int(1.1e9 * microseconds), bytes_accessed=int(3.6e6 * microseconds), transcendentals=0
    )


def stays(value):
    return pltpu.with_memory_space_constraint(value, pltpu.HBM)


def frame_block(frames):
    _, img, stack, _ = frames.shape
    return pl.BlockSpec((4 * STEP, img, stack, LANES), lambda g, s: (g, 0, 0, s[0]))


def encode(section, frames, w1t, w2t, lw, table):
    img = frames.shape[0]
    blocks = img // 4
    side = blocks - 1
    k1, k2, width = w1t.shape[0], w2t.shape[0], lw.shape[1]
    flat = lw.shape[0]
    outs = (
        shape_of(blocks, side, k1, LANES, dtype=BF16),
        shape_of(blocks, side, k1, LANES, dtype=BF16),
        shape_of(flat, LANES, dtype=BF16),
        shape_of(flat, LANES, dtype=BF16),
        shape_of(width, LANES, dtype=BF16),
        shape_of(width, LANES),
    )
    weights = (w1t, w2t, lw, table)
    out_specs = [whole(o.shape) for o in outs]
    out_specs[1] = pl.BlockSpec((STEP, side, k1, LANES), lambda g, s: (g, 0, 0, 0))
    return pl.pallas_call(
        encode_kernel,
        grid_spec=pltpu.PrefetchScalarGridSpec(
            num_scalar_prefetch=1,
            grid=(blocks // STEP,),
            in_specs=[frame_block(frames), *[whole(w.shape) for w in weights]],
            out_specs=out_specs,
            scratch_shapes=[
                pltpu.VMEM((2 * REACH * k1, 256), BF16),
                pltpu.VMEM((2 * k1, 64), BF16),
                pltpu.VMEM((k1, LANES), F32),
                pltpu.VMEM((k2, LANES), F32),
                pltpu.VMEM((side, k1, LANES), F32),
            ],
        ),
        out_shape=outs,
        compiler_params=params(),
        cost_estimate=cost(9),
        name="encode",
    )(section, frames, *weights)


def plan(section, slots, enc, s3, h2, branch_w, value_w, table, per_pair, depth, half_rows):
    width = enc.shape[0]
    options = branch_w.shape[0]
    two = 2 * width
    pairs = options // 2
    outs = (
        shape_of(half_rows, LANES, dtype=BF16),
        shape_of(half_rows, LANES, dtype=BF16),
        shape_of(TABLE, LANES),
        shape_of(width, LANES, dtype=BF16),
    )
    operands = (slots, enc, s3, h2, branch_w, value_w, table)
    vmem = pltpu.VMEM
    return pl.pallas_call(
        functools.partial(plan_kernel, per_pair=per_pair),
        grid_spec=pltpu.PrefetchScalarGridSpec(
            num_scalar_prefetch=1,
            grid=(1,),
            in_specs=[whole(o.shape) for o in operands],
            out_specs=[whole(o.shape) for o in outs],
            scratch_shapes=[
                vmem((2, half_rows, LANES), BF16),
                vmem((options * width, width), BF16),
                vmem((options * width, LANES), F32),
                vmem((width + 16, width), BF16),
                vmem((width, width + 16), BF16),
                vmem((width, LANES), F32),
                vmem((width, LANES), F32),
                vmem((16, LANES), F32),
                vmem((depth, options * width, LANES), F32),
                vmem((depth, pairs, width, 2 * LANES), F32),
                vmem((depth, pairs, width, 2 * LANES), BF16),
                vmem((depth, pairs, width, 2 * LANES), BF16),
                vmem((depth, options * width, LANES), BF16),
                vmem((depth + 1, width, LANES), F32),
                vmem((depth, options, LANES), F32),
                vmem((options, LANES), F32),
                vmem((options, LANES), F32),
                vmem((options, LANES), F32),
                vmem((depth, options, LANES), F32),
                vmem((depth, 3, LANES), F32),
                vmem((depth, 2, options, LANES), F32),
                vmem((width + 16, LANES), F32),
                vmem((width, 2 * LANES), F32),
                vmem((width, 2 * LANES), F32),
                vmem((3, options, LANES), F32),
            ],
        ),
        out_shape=outs,
        compiler_params=params(),
        cost_estimate=cost(13),
        name="plan",
    )(section, *operands)


def back(section, g3, lw, s2, s1, w1t, w2t, channels):
    _, side, k1 = s1.shape[:3]
    k2 = w2t.shape[0]
    inner = side // 2 - 1
    outs = (
        shape_of(side + 2, side, k1, LANES, dtype=BF16),
        shape_of(inner + 2, inner, k2, LANES, dtype=BF16),
        shape_of(8, LANES),
        shape_of(STEP * channels * 4 * COLS, (STEP + 1) * 3 * k1, dtype=BF16),
    )
    return small_call(
        back_kernel,
        outs,
        (g3, lw, s2, s1, w1t, w2t),
        [
            pltpu.VMEM((LANES, 6 * k2), BF16),
            pltpu.VMEM((k1, LANES), F32),
            pltpu.VMEM((k2, LANES), F32),
        ],
        name="back",
        place=(section,),
        weight=5,
    )


ANYWHERE = pl.BlockSpec(memory_space=pl.ANY)


def row_window(g1, start):
    block = (pl.Element(STEP + 1),) + tuple(pl.Element(n) for n in g1.shape[1:])
    return pl.BlockSpec(block, lambda g, *_: (STEP * (start + g), 0, 0, 0))


def first(section, frames, g1, after):
    blocks = frames.shape[0] // 4
    k1 = g1.shape[2]
    return pl.pallas_call(
        first_kernel,
        grid_spec=pltpu.PrefetchScalarGridSpec(
            num_scalar_prefetch=1,
            grid=(blocks // STEP,),
            in_specs=[frame_block(frames), row_window(g1, 0), ANYWHERE],
            out_specs=whole((2 * k1, LANES)),
            scratch_shapes=[
                pltpu.VMEM((2 * REACH * k1, 256), F32),
                pltpu.VMEM((2 * k1, 64), F32),
            ],
        ),
        out_shape=shape_of(2 * k1, LANES, dtype=BF16),
        compiler_params=params(),
        cost_estimate=cost(9),
        name="first",
    )(section, frames, g1, after)


def pixels(section, band, mine, other, img, channels, start, steps, after, done):
    operands = (band, mine, other, after)
    specs = [whole(band.shape), row_window(mine, start), row_window(other, start), ANYWHERE]
    aliases = {}
    if done is not None:
        operands += (done,)
        specs.append(ANYWHERE)
        aliases = {len(operands): 0}
    return pl.pallas_call(
        functools.partial(pixels_kernel, start=start),
        grid_spec=pltpu.PrefetchScalarGridSpec(
            num_scalar_prefetch=1,
            grid=(steps,),
            in_specs=specs,
            out_specs=[ANYWHERE, whole((8, LANES))],
            scratch_shapes=[
                pltpu.VMEM((2, 2, 4 * STEP, img, channels, LANES), F32),
                pltpu.SemaphoreType.DMA((2, 2)),
            ],
        ),
        out_shape=[shape_of(img, img, channels, 2 * LANES), shape_of(8, LANES)],
        input_output_aliases=aliases,
        compiler_params=params(),
        cost_estimate=cost(1.6 * steps),
        name="pixels",
    )(section, *operands)


def small_call(
    kernel, outs, operands, scratch=(), name=None, place=None, after=(), weight=0.3
):
    specs = [pl.BlockSpec(memory_space=pltpu.VMEM)] * len(operands)
    if place is not None:
        operands = (*place, *operands)
        specs = [pl.BlockSpec(memory_space=pltpu.SMEM)] * len(place) + specs
    return pl.pallas_call(
        kernel,
        in_specs=specs + [ANYWHERE] * len(after),
        out_shape=outs,
        scratch_shapes=list(scratch),
        compiler_params=params(),
        cost_estimate=cost(weight),
        name=name,
    )(*operands, *after)


def round_up(value, step):
    return -(-value // step) * step


def swapped(value):
    return lax.ppermute(value, "section", [(0, 1), (1, 0)])


def exchanged(value, groups=None):
    return lax.all_to_all(
        value, "batch", split_axis=0, concat_axis=0, axis_index_groups=groups, tiled=True
    )


def local(
    frames,
    destination,
    options,
    depth,
    targets,
    conv_one,
    bias_one,
    conv_two,
    bias_two,
    linear_w,
    linear_b,
    branch_w,
    branch_b,
    head_w,
    head_b,
    value_w,
    value_b,
    out_w,
    out_b,
):
    section = lax.axis_index("section").astype(jnp.int32)[None]
    peers = lax.axis_size("batch")
    frame_count = frames.shape[3]
    per_pair = frame_count // peers
    levels = options.shape[0]
    frames = stays(frames.transpose(1, 2, 0, 3))
    w1t, w2t = stays(conv_one.T), stays(conv_two.T)
    linear_w, branch_w, value_w = stays(linear_w), stays(branch_w), stays(value_w)
    encoder_params = (w1t, bias_one, w2t, bias_two, linear_w, linear_b)
    planner_params = (branch_w, branch_b, head_w.T, head_b, value_w, value_b, out_w.T, out_b)
    width = linear_w.shape[1]
    big_rows = linear_w.shape[0] + (branch_w.shape[0] + 1) * width
    chunk = round_up(-(-big_rows // (2 * peers)), 16)
    half_rows = chunk * peers

    scalars = pl.BlockSpec(memory_space=pltpu.SMEM)
    tiny = (bias_one, bias_two, linear_b, branch_b, head_w.T, value_b, out_w.T)
    tiny = [stays(v if v.ndim > 1 else v[None, :]) for v in tiny]
    numbers, table = pl.pallas_call(
        numbers_kernel,
        in_specs=[pl.BlockSpec(memory_space=pltpu.VMEM)] * (4 + len(tiny)) + [scalars] * 2,
        out_shape=[shape_of(frame_count, LANES), shape_of(TABLE, LANES)],
        compiler_params=params(),
        cost_estimate=cost(1),
        name="numbers",
    )(
        stays(options),
        stays(depth[None, :]),
        stays(targets),
        stays(destination[None, :]),
        *tiny,
        head_b,
        out_b,
    )
    slots = exchanged(numbers.reshape(peers, per_pair, LANES)).reshape(frame_count, LANES)

    h1, s1, h2, s2, enc, s3 = encode(section, frames, w1t, w2t, linear_w, table)
    keep, send, small, g3 = plan(
        section, slots, enc, s3, h2, branch_w, value_w, table, per_pair, levels, half_rows
    )
    recv = swapped(send)
    channels = frames.shape[2] // lax.axis_size("section")
    g1, g2, sums, band = back(section, g3, linear_w, s2, s1, w1t, w2t, channels)
    other = swapped(g1)
    planes = peers // PLANE
    size = chunk * planes
    in_plane = [list(range(p * PLANE, (p + 1) * PLANE)) for p in range(planes)]
    across = [list(range(m, peers, PLANE)) for m in range(PLANE)]
    bf16 = functools.partial(shape_of, dtype=BF16)
    pieces = small_call(
        merge_kernel, bf16(PLANE, size, LANES), (keep, recv), name="merge", after=(sums,)
    )
    got = exchanged(pieces, in_plane)
    c1 = first(section, frames, g1, pieces)
    pieces = small_call(
        plane_kernel, bf16(planes, chunk, LANES), (got,), name="plane", after=(c1,)
    )
    got = exchanged(pieces, across)
    c2 = small_call(
        second_kernel,
        shape_of(w2t.shape[0], 256),
        (h1, g2),
        name="second",
        after=(pieces,),
        weight=2,
    )
    draw = functools.partial(pixels, section, band, g1, other, frames.shape[0], channels)
    frames_grad, token = draw(0, 1, c2, None)
    late = 2 * (w1t.shape[0] + w2t.shape[0] + TABLE + 8)
    pieces = small_call(
        depth_kernel,
        bf16(planes, chunk + late, LANES),
        (got, c1, c2, small, sums),
        name="depth",
        after=(token,),
    )
    got = exchanged(pieces, across)
    frames_grad, token = draw(1, 2, pieces, frames_grad)
    pieces = small_call(
        functools.partial(gather_kernel, late=late),
        bf16(PLANE, size + late, LANES),
        (got,),
        name="gather",
        after=(token,),
    )
    got = exchanged(pieces, in_plane)
    frames_grad, token = draw(3, 3, pieces, frames_grad)
    got = small_call(relay_kernel, bf16(*got.shape), (got,), name="relay", after=(token,))
    got_other = swapped(got)
    frames_grad, token = draw(6, 1, got, frames_grad)
    shapes = [p.shape for p in encoder_params + planner_params]
    flat = [s if len(s) > 1 else (1,) + s for s in shapes]
    rest = small_call(
        unpack_kernel,
        [shape_of(1, 1)] + [shape_of(*s) for s in flat],
        (got, got_other),
        [pltpu.VMEM((2, half_rows, LANES), BF16)],
        name="unpack",
        place=(section,),
        after=(token,),
    )
    rest = [v.reshape(s) for v, s in zip(rest, [()] + shapes)]
    for at in (1, 3, 9, 13):
        rest[at] = rest[at].T
    return (rest[0], frames_grad.transpose(2, 0, 1, 3), *rest[1:])


def solution(mesh):
    placed = (
        P(None, None, None, "batch"),
        P("batch"),
        P(None, "batch"),
        P("batch"),
        P(None, None, "batch"),
    ) + (P(),) * 14
    return jax.shard_map(
        local,
        mesh=mesh,
        in_specs=placed,
        out_specs=(P(), P("section", None, None, "batch")) + (P(),) * 14,
        check_vma=False,
    )
```

```python
import functools
import math

import jax
import jax.numpy as jnp
from jax import lax
from jax.experimental import pallas as pl
from jax.experimental.pallas import tpu as pltpu
from jax.sharding import PartitionSpec as P

BF16 = jnp.bfloat16
F32 = jnp.float32
EXACT = lax.Precision.HIGHEST
LANES = 128
VMEM_BYTES = 32 * 1024 * 1024
TILE = 16
REACH = 5
STEP = 3
COLS = 8
AT_VB, AT_OW, AT_HW, AT_LB, AT_SCALARS, AT_B1, AT_B2, AT_DEST = (
    slice(18, 19),
    slice(19, 20),
    slice(20, 22),
    slice(22, 23),
    slice(23, 24),
    slice(24, 25),
    slice(25, 26),
    26,
)
TABLE = 32
PLANE = 4
SHORT = 32


def dot(a, b, precision=None):
    return jnp.dot(a, b, preferred_element_type=F32, precision=precision)


def dot_rows(a, b, precision=None):
    return lax.dot_general(
        a, b, (((0,), (0,)), ((), ())), preferred_element_type=F32, precision=precision
    )


def dot_lanes(a, b, precision=None):
    return lax.dot_general(
        a, b, (((1,), (1,)), ((), ())), preferred_element_type=F32, precision=precision
    )


def iota(shape, axis):
    return lax.broadcasted_iota(jnp.int32, shape, axis)


def column(row):
    n = row.shape[1]
    wide = jnp.broadcast_to(row, (n, n))
    return jnp.sum(jnp.where(iota((n, n), 0) == iota((n, n), 1), wide, 0.0), axis=1, keepdims=True)


def row_of(col):
    n = col.shape[0]
    wide = jnp.broadcast_to(col, (n, n))
    return jnp.sum(jnp.where(iota((n, n), 0) == iota((n, n), 1), wide, 0.0), axis=0, keepdims=True)


def soft(x):
    t = jnp.tanh(0.5 * x)
    return jnp.maximum(x, 0.0) - jnp.log(0.5 + 0.5 * jnp.abs(t)), 0.5 + 0.5 * t


def silu_pair(x):
    s = 0.5 + 0.5 * jnp.tanh(0.5 * x)
    act = x * s
    return act, s + act * (1.0 - s)


def tap_map(half, place):
    tap, pix = iota((256, 256), 0), iota((256, 256), 1)
    hit = (
        ((tap >> 6) == (pix & 3))
        & (((tap >> 3) & 7) == (pix >> 6) + 4 * half)
        & ((tap & 7) == ((pix >> 2) & 15) - 4 * (place - 1))
    )
    return hit.astype(F32)


def tile_rows(frames, r, j):
    channels = frames.shape[2]
    flat = frames.reshape(frames.shape[0], frames.shape[1] * channels, LANES)
    size = TILE * channels
    end = min((j + 1) * size, flat.shape[1])
    return flat[4 * r : 4 * r + 4, j * size : end, :].reshape(4 * (end - j * size), LANES)


def encode_kernel(
    section,
    frames,
    w1t,
    w2t,
    lw,
    table,
    h1,
    s1,
    h2,
    s2,
    enc,
    s3,
    band,
    edge,
    bias1,
    bias2,
    held,
):
    g = pl.program_id(0)
    side = h1.shape[1]
    tiles = frames.shape[1] // TILE
    k1, k2 = w1t.shape[0], w2t.shape[0]
    reach_rows = REACH * k1

    @pl.when(g == 0)
    def _():
        for half in range(2):
            for place in range(REACH):
                at = half * reach_rows + place * k1
                taps = dot(w1t[...], tap_map(half, place).astype(BF16))
                band[at : at + k1, :] = taps.astype(BF16)
            tap, pix = iota((256, 64), 0), iota((256, 64), 1)
            hit = (
                ((tap >> 6) == (pix & 3))
                & (((tap >> 3) & 7) == (pix >> 4) + 4 * half)
                & ((tap & 7) == ((pix >> 2) & 3) + 4)
            )
            taps = dot(w1t[...], hit.astype(F32).astype(BF16))
            edge[half * k1 : (half + 1) * k1, :] = taps.astype(BF16)
        bias1[...] = jnp.broadcast_to(column(table[AT_B1, 0:k1]), bias1.shape)
        bias2[...] = jnp.broadcast_to(column(table[AT_B2, 0:k2]), bias2.shape)
        held[...] = jnp.zeros_like(held)
        h1[...] = jnp.zeros_like(h1)

    inner = side // 2 - 1
    row_len = inner * k2

    def second_row(y):
        for first in range(0, inner, 2):
            xs = [x for x in (first, first + 1) if x < inner]
            cut = [h1[pl.ds(2 * y + 1, 4), 2 * x : 2 * x + 4].reshape(256, LANES) for x in xs]
            patch = cut[0] if len(cut) == 1 else jnp.concatenate(cut, axis=1)
            got = dot(w2t[...], patch)
            for k, x in enumerate(xs):
                value, slope = soft(got[:, k * LANES : (k + 1) * LANES] + bias2[...])
                at = pl.ds(pl.multiple_of(y * row_len + x * k2, k2), k2)
                h2[at, :] = value.astype(BF16)
                s2[at, :] = slope.astype(BF16)

    ready_row = jnp.maximum((STEP * g - 6) // 2, 0)
    second_row(ready_row)
    second_row(ready_row + 1)

    for r in range(STEP):
        low, high = {}, {}

        def add(x, one, two):
            low[x] = low[x] + one if x in low else one
            high[x] = high[x] + two if x in high else two

        last = dot(edge[...], tile_rows(frames, r, tiles))
        add(side - 1, last[:k1], last[k1:])
        done = 0
        for first in range(0, tiles, 2):
            js = [j for j in (first, first + 1) if j < tiles]
            cut = [tile_rows(frames, r, j) for j in js]
            got = dot(band[...], cut[0] if len(cut) == 1 else jnp.concatenate(cut, axis=1))
            for k, j in enumerate(js):
                for place in range(REACH):
                    x = 4 * j - 1 + place
                    if 0 <= x < side:
                        at = place * k1
                        span = slice(k * LANES, (k + 1) * LANES)
                        add(
                            x,
                            got[at : at + k1, span],
                            got[reach_rows + at : reach_rows + at + k1, span],
                        )
            ready = side if js[-1] == tiles - 1 else 4 * js[-1] + 3
            for x in range(done, ready):
                value, slope = soft(held[x] + high[x] + bias1[...])
                held[x] = low[x]
                h1[STEP * g + r, x] = value.astype(BF16)
                s1[r, x] = slope.astype(BF16)
            done = ready

    @pl.when(g == pl.num_programs(0) - 1)
    def _():
        for y in range(inner - 2, inner):
            second_row(y)
        value, slope = soft(dot_rows(lw[...], h2[...]) + column(table[AT_LB, :]))
        enc[...] = value.astype(BF16)
        s3[...] = slope


def plan_kernel(
    section,
    slots,
    enc,
    s3,
    h2,
    branch_w,
    value_w,
    table,
    keep,
    send,
    small,
    g3,
    parts,
    bwt,
    bb,
    vht,
    vhw,
    vb,
    ow,
    mine,
    dbr,
    dval,
    low,
    hid,
    gb,
    states,
    pick,
    rew,
    disc,
    val,
    soft_q,
    gaps,
    rows_g,
    vgrad,
    outacc,
    vbacc,
    rowacc,
    *,
    per_pair,
):
    width = enc.shape[0]
    options = branch_w.shape[0]
    depth = states.shape[0] - 1
    pairs = options // 2
    two = 2 * width
    sec = section[0]

    count = slots.shape[0]
    dest = jnp.concatenate(
        [table[AT_DEST + k : AT_DEST + k + 1, :] for k in range(count // LANES)], axis=1
    )
    own = jnp.where(sec == 0, dest[:, :LANES], dest[:, LANES:])
    others = jnp.transpose(jnp.broadcast_to(dest, (LANES, count)))
    index = iota((count, LANES), 1) + sec * LANES
    earlier = (others == own) & (iota((count, LANES), 0) < index)
    rank = jnp.sum(earlier.astype(F32), axis=0, keepdims=True)
    bucket = own * float(per_pair) + rank
    chosen = (iota((count, LANES), 0).astype(F32) == bucket).astype(F32)
    mine[...] = dot_rows(slots[...], chosen, EXACT)[: mine.shape[0]]

    for o in range(options):
        at = slice(o * width, (o + 1) * width)
        bwt[at, :] = jnp.transpose(branch_w[o].astype(F32)).astype(BF16)
        bb[at, :] = jnp.broadcast_to(column(table[o : o + 1, :]), (width, LANES))
    vht[...] = jnp.zeros_like(vht)
    vht[0:width, :] = jnp.transpose(value_w[...].astype(F32)).astype(BF16)
    pick_head = (iota((16, 2), 0) == iota((16, 2), 1)).astype(F32).astype(BF16)
    head_w = table[AT_HW, :].astype(BF16)
    vht[width : width + 16, :] = dot(pick_head, head_w).astype(BF16)
    vhw[:, 0:width] = value_w[...]
    vhw[:, width:] = dot_rows(
        head_w, (iota((2, 16), 0) == iota((2, 16), 1)).astype(F32).astype(BF16)
    ).astype(BF16)
    vb[...] = jnp.broadcast_to(column(table[AT_VB, :]), (width, LANES))
    ow[...] = jnp.broadcast_to(column(table[AT_OW, :]), (width, LANES))

    vgrad[...] = jnp.zeros_like(vgrad)
    outacc[...] = jnp.zeros_like(outacc)
    vbacc[...] = jnp.zeros_like(vbacc)
    rowacc[...] = jnp.zeros_like(rowacc)
    states[0] = enc[...].astype(F32)

    def wide(ref):
        return jnp.concatenate([ref[...], ref[...]], axis=1)

    def ahead(level, carry):
        labels = iota((options, LANES), 0).astype(F32)
        picked = (labels == mine[pl.ds(level, 1), :]).astype(F32)
        pick[level] = picked
        state = states[level]
        rounded = state.astype(BF16)

        def one_pair(t, following):
            at = slice(t * two, (t + 1) * two)
            act, slope = silu_pair(dot(bwt[at, :], rounded) + bb[at, :])
            dbr[level, at, :] = slope
            left = state + act[:width]
            right = state + act[width:]
            following = jnp.where(picked[2 * t : 2 * t + 1] > 0.0, left, following)
            following = jnp.where(picked[2 * t + 1 : 2 * t + 2] > 0.0, right, following)
            both = jnp.concatenate([left.astype(BF16), right.astype(BF16)], axis=1)
            low[level, t] = both
            got = dot(vht[...], both)
            act, slope = silu_pair(got[:width] + wide(vb))
            dval[level, t] = slope
            hidden = act.astype(BF16)
            hid[level, t] = hidden
            worth = jnp.sum(hidden.astype(F32) * wide(ow), axis=0, keepdims=True)
            for k in range(2):
                spot = slice(2 * t + k, 2 * t + k + 1)
                span = slice(k * LANES, (k + 1) * LANES)
                val[spot, :] = worth[:, span]
                rew[spot, :] = got[width : width + 1, span]
                disc[spot, :] = got[width + 1 : width + 2, span]
            return following

        following = state
        for t in range(pairs):
            following = one_pair(t, following)
        states[level + 1] = following
        scalars = table[AT_SCALARS, :]
        reward = rew[...] + scalars[:, 1:2]
        discount = jax.nn.sigmoid(disc[...] + scalars[:, 2:3])
        value = val[...] + scalars[:, 3:4]
        quality = reward + discount * value
        top = jnp.max(quality, axis=0, keepdims=True)
        shifted = jnp.exp(quality - top)
        total = jnp.sum(shifted, axis=0, keepdims=True)
        soft_q[level] = shifted / total
        rows_g[level, 0] = discount
        rows_g[level, 1] = value
        live = (mine[pl.ds(depth, 1), :] > level.astype(F32)).astype(F32)

        def target(kind):
            return mine[pl.ds(depth + 1 + kind * depth + level, 1), :]

        gaps[level, 0:1, :] = live * (jnp.sum(picked * reward, axis=0, keepdims=True) - target(0))
        gaps[level, 1:2, :] = live * (jnp.sum(picked * discount, axis=0, keepdims=True) - target(1))
        gaps[level, 2:3, :] = live * (top + jnp.log(total) - target(2))
        return carry

    lax.fori_loop(0, depth, ahead, 0)

    def behind(turn, grad_next):
        level = depth - 1 - turn
        picked = pick[level]
        grad_quality = gaps[level, 2:3, :] * soft_q[level]
        discount = rows_g[level, 0]
        value = rows_g[level, 1]
        head_one = (picked * gaps[level, 0:1, :] + grad_quality).astype(BF16).astype(F32)
        head_two = picked * gaps[level, 1:2, :] + grad_quality * value
        head_two = (head_two * discount * (1.0 - discount)).astype(BF16).astype(F32)
        grad_value = (grad_quality * discount).astype(BF16).astype(F32)
        rew[...] = head_one
        disc[...] = head_two
        val[...] = grad_value
        rowacc[0] += head_one
        rowacc[1] += head_two
        rowacc[2] += grad_value

        def one_pair(t, total):
            at = slice(t * two, (t + 1) * two)

            def across(ref):
                return jnp.concatenate([ref[2 * t : 2 * t + 1], ref[2 * t + 1 : 2 * t + 2]], axis=1)

            worth = across(val)
            grad_hidden = worth * wide(ow)
            grad_pre = (grad_hidden * dval[level, t]).astype(BF16)
            outacc[...] += hid[level, t].astype(F32) * worth
            vbacc[...] += grad_pre.astype(F32)
            line = iota((16, two), 0)
            heads = jnp.where(line == 0, across(rew), jnp.where(line == 1, across(disc), 0.0))
            stacked = jnp.concatenate([grad_pre, heads.astype(BF16)], axis=0)
            vgrad[...] += dot_lanes(stacked, low[level, t])
            moved = dot(vhw[...], stacked)
            left = moved[:, :LANES] + pick[level, 2 * t : 2 * t + 1, :] * grad_next
            right = moved[:, LANES:] + pick[level, 2 * t + 1 : 2 * t + 2, :] * grad_next
            grad_branch = jnp.concatenate([left, right], axis=0) * dbr[level, at, :]
            grad_branch = grad_branch.astype(BF16)
            gb[level, at, :] = grad_branch
            weights = jnp.concatenate([branch_w[2 * t], branch_w[2 * t + 1]], axis=1)
            return total + (left + right + dot(weights, grad_branch))

        total = jnp.zeros((width, LANES), F32)
        for t in range(pairs):
            total = one_pair(t, total)
        return total

    grad_planned = lax.fori_loop(0, depth, behind, jnp.zeros((width, LANES), F32))

    linear_rows = h2.shape[0]
    half = (linear_rows + options * width + width) // 2
    rest = linear_rows - half
    ones = jnp.ones((16, depth * LANES), F32).astype(BF16)
    rounded = jnp.concatenate([states[level].astype(BF16) for level in range(depth)], axis=1)
    rounded = jnp.concatenate([rounded, ones], axis=0)
    small[...] = jnp.zeros_like(small)
    if half < keep.shape[0]:
        for k in range(2):
            parts[k, half:, :] = jnp.zeros((keep.shape[0] - half, LANES), BF16)

    def one_option(o, carry):
        at = pl.ds(pl.multiple_of(o * width, width), width)
        grads = jnp.concatenate([gb[level, at, :] for level in range(depth)], axis=1)
        got = dot_lanes(rounded, grads)
        at = pl.ds(pl.multiple_of(rest + o * width, 16), width)
        parts[1 - sec, at, :] = got[:width].astype(BF16)
        small[pl.ds(o, 1), :] = got[width : width + 1]
        return carry

    lax.fori_loop(0, options, one_option, 0, unroll=2)
    after = rest + options * width
    parts[1 - sec, after : after + width, :] = jnp.transpose(vgrad[0:width, :]).astype(BF16)

    grad_three = (grad_planned.astype(BF16).astype(F32) * s3[...]).astype(BF16)
    g3[...] = grad_three
    chunk = linear_rows // 9

    def one_chunk(i, carry):
        at = pl.ds(pl.multiple_of(i * chunk, chunk), chunk)
        parts[sec, at, :] = dot_lanes(h2[at, :], grad_three).astype(BF16)
        return carry

    lax.fori_loop(0, 8, one_chunk, 0, unroll=4)
    last = dot_lanes(h2[8 * chunk :, :], grad_three).astype(BF16)
    parts[sec, 8 * chunk : half, :] = last[: half - 8 * chunk]
    parts[1 - sec, 0:rest, :] = last[half - 8 * chunk :]
    keep[...] = parts[0]
    send[...] = parts[1]

    small[AT_VB, :] = row_of(jnp.sum(vbacc[...], axis=1, keepdims=True))
    small[AT_OW, :] = row_of(jnp.sum(outacc[...], axis=1, keepdims=True))
    small[AT_HW, :] = vgrad[width : width + 2, :]
    small[AT_LB, :] = row_of(jnp.sum(grad_three.astype(F32), axis=1, keepdims=True))
    gap = gaps[...]
    loss = 0.5 * jnp.sum(jnp.sum(gap * gap, axis=0), axis=0, keepdims=True)
    lines = [loss] + [jnp.sum(rowacc[k], axis=0, keepdims=True) for k in range(3)]
    lane = iota((1, LANES), 1)
    scalars = jnp.zeros((1, LANES), F32)
    for k, line in enumerate(lines):
        scalars = jnp.where(lane == k, jnp.sum(line, axis=1, keepdims=True), scalars)
    small[AT_SCALARS, :] = scalars


def back_kernel(section, g3, lw, s2, s1, w1t, w2t, g1, g2, sums, band, t2, b1acc, b2acc):
    side, k1 = s1.shape[1], s1.shape[2]
    k2 = w2t.shape[0]
    inner = side // 2 - 1
    row_len = inner * k2
    tap, pix = iota((LANES, 256), 1), iota((LANES, 256), 0)
    for yrel in range(2):
        for p in range(3):
            hit = (
                ((tap & 15) == (pix & 15))
                & ((tap >> 6) == (pix >> 6) + 2 * (1 - yrel))
                & (((tap >> 4) & 3) == ((pix >> 4) & 3) + 2 - 2 * p)
            )
            at = (yrel * 3 + p) * k2
            t2[:, at : at + k2] = dot_lanes(hit.astype(F32).astype(BF16), w2t[...]).astype(BF16)
    g2[0] = jnp.zeros(g2.shape[1:], BF16)
    g2[inner + 1] = jnp.zeros(g2.shape[1:], BF16)
    g1[0] = jnp.zeros(g1.shape[1:], BF16)
    g1[side + 1] = jnp.zeros(g1.shape[1:], BF16)
    zero = jnp.zeros((k2, LANES), BF16)
    total_one = jnp.zeros((k1, LANES), F32)
    total_two = jnp.zeros((k2, LANES), F32)
    for b in range(side // 2):
        if b < inner:
            at = slice(b * row_len, (b + 1) * row_len)
            grad = dot(lw[at, :], g3[...]) * s2[at, :].astype(F32)
            grad = grad.astype(BF16).reshape(inner, k2, LANES)
            g2[b + 1] = grad
            total_two = total_two + jnp.sum(grad.astype(F32), axis=0)
        cut = []
        for j in range(side // 4):
            pieces = []
            for yrel in range(2):
                for p in range(3):
                    x = 2 * j - 1 + p
                    pieces.append(g2[b + yrel, x] if 0 <= x < inner else zero)
            cut.append(jnp.concatenate(pieces, axis=0))
        got = dot(t2[...], jnp.concatenate(cut, axis=1))
        for u in range(2):
            for j in range(side // 4):
                part = got[u * 64 : (u + 1) * 64, j * LANES : (j + 1) * LANES]
                slope = s1[2 * b + u + 1, 4 * j : 4 * j + 4].astype(F32)
                grad = (part.reshape(4, k1, LANES) * slope).astype(BF16)
                g1[2 * b + u + 1, 4 * j : 4 * j + 4] = grad
                total_one = total_one + jnp.sum(grad.astype(F32), axis=0)
    sums[...] = jnp.zeros_like(sums)
    sums[0:1, 0:k1] = row_of(jnp.sum(total_one, axis=1, keepdims=True))
    sums[1:2, 0:k2] = row_of(jnp.sum(total_two, axis=1, keepdims=True))
    pixel_band(section[0], w1t, band)


def pixel_band(sec, w1t, band):
    k1 = w1t.shape[0]
    size = band.shape[0]
    channels = size // (STEP * 4 * COLS)
    line = COLS * channels
    tap, pix = iota((size, 256), 1), iota((size, 256), 0)
    r = pix // (4 * line)
    u4 = (pix // line) % 4
    xx = (pix // channels) % COLS
    c = pix % channels + sec * channels
    for yrel in range(STEP + 1):
        for p in range(3):
            hit = (
                ((tap >> 6) == c)
                & (((tap >> 3) & 7) == 4 * (r + 1 - yrel) + u4)
                & ((tap & 7) == xx + 4 - 4 * p)
            )
            at = (yrel * 3 + p) * k1
            band[:, at : at + k1] = dot_lanes(hit.astype(F32).astype(BF16), w1t[...]).astype(BF16)


def second_kernel(h1, g2, c2):
    side = h1.shape[1]
    inner = side // 2 - 1
    total = jnp.zeros(c2.shape, F32)
    for y in range(inner):
        grads = jnp.concatenate([g2[y + 1, x] for x in range(inner)], axis=1)
        patches = jnp.concatenate(
            [h1[2 * y + 1 : 2 * y + 5, 2 * x : 2 * x + 4].reshape(256, LANES) for x in range(inner)],
            axis=1,
        )
        total = total + dot_lanes(grads, patches)
    c2[...] = total


def first_kernel(section, frames, g1, after, c1, acc, side_acc):
    g = pl.program_id(0)
    side, k1 = g1.shape[1], g1.shape[2]
    tiles = frames.shape[1] // TILE

    @pl.when(g == 0)
    def _():
        acc[...] = jnp.zeros_like(acc)
        side_acc[...] = jnp.zeros_like(side_acc)

    zero = jnp.zeros((k1, LANES), BF16)
    pixels, grads, edges, edge_grads = [], [], [], []
    for r in range(STEP):
        for j in range(tiles):
            pixels.append(tile_rows(frames, r, j))
            pieces = []
            for half in range(2):
                for place in range(REACH):
                    x = 4 * j - 1 + place
                    pieces.append(g1[r + 1 - half, x] if 0 <= x < side else zero)
            grads.append(jnp.concatenate(pieces, axis=0))
        edges.append(tile_rows(frames, r, tiles))
        edge_grads.append(
            jnp.concatenate([g1[r + 1 - half, side - 1] for half in range(2)], axis=0)
        )
    acc[...] += dot_lanes(jnp.concatenate(pixels, axis=1), jnp.concatenate(grads, axis=1))
    side_acc[...] += dot_lanes(
        jnp.concatenate(edges, axis=1), jnp.concatenate(edge_grads, axis=1)
    )

    @pl.when(g == pl.num_programs(0) - 1)
    def _():
        grad = jnp.zeros((k1, 256), F32)
        total, edge = jnp.transpose(acc[...]), jnp.transpose(side_acc[...])
        for half in range(2):
            for place in range(REACH):
                at = (half * REACH + place) * k1
                grad = grad + dot_lanes(
                    total[at : at + k1], tap_map(half, place), EXACT
                )
            tap, pix = iota((256, 64), 0), iota((256, 64), 1)
            hit = (
                ((tap >> 6) == (pix & 3))
                & (((tap >> 3) & 7) == (pix >> 4) + 4 * half)
                & ((tap & 7) == ((pix >> 2) & 3) + 4)
            )
            grad = grad + dot_lanes(
                edge[half * k1 : (half + 1) * k1], hit.astype(F32), EXACT
            )
        for half in range(2):
            c1[half * k1 : (half + 1) * k1, :] = grad[:, half * LANES : (half + 1) * LANES].astype(
                BF16
            )


def pixels_kernel(section, band, mine, other, after, out, token, held, sems):
    g = pl.program_id(0)
    steps = pl.num_programs(0)
    side, k1 = mine.shape[1], mine.shape[2]
    img, channels = out.shape[1], out.shape[2]
    sec = section[0]
    line = COLS * channels
    flat = held.reshape(2, 2, 4 * STEP, img * channels, LANES)
    slot = g % 2

    def writes(step, at):
        rows = pl.ds(pl.multiple_of(4 * STEP * step, 4), 4 * STEP)
        places = (sec * LANES, (1 - sec) * LANES)
        return [
            pltpu.make_async_copy(
                held.at[at, k],
                out.at[rows, :, :, pl.ds(pl.multiple_of(places[k], LANES), LANES)],
                sems.at[at, k],
            )
            for k in range(2)
        ]

    @pl.when(g >= 2)
    def _():
        for copy in writes(g - 2, slot):
            copy.wait()

    zero = jnp.zeros((k1, 2 * LANES), BF16)
    for j in range((img + COLS - 1) // COLS):
        pieces = []
        for yrel in range(STEP + 1):
            for p in range(3):
                x = 2 * j - 1 + p
                if 0 <= x < side:
                    pieces.append(jnp.concatenate([mine[yrel, x], other[yrel, x]], axis=1))
                else:
                    pieces.append(zero)
        got = dot(band[...], jnp.concatenate(pieces, axis=0))
        keep = min(line, img * channels - j * line)
        for k in range(4 * STEP):
            at = k * line
            span = slice(j * line, j * line + keep)
            flat[slot, 0, k, span, :] = got[at : at + keep, :LANES]
            flat[slot, 1, k, span, :] = got[at : at + keep, LANES:]
    for copy in writes(g, slot):
        copy.start()
    token[...] = jnp.zeros_like(token)

    @pl.when(g == steps - 1)
    def _():
        @pl.when(g >= 1)
        def _():
            for copy in writes(g - 1, 1 - slot):
                copy.wait()

        for copy in writes(g, slot):
            copy.wait()


def two_parts(value):
    high = value.astype(BF16).astype(F32)
    return jnp.concatenate([high, value - high], axis=0).astype(BF16)


def one_part(pair):
    rows = pair.shape[0] // 2
    pair = pair.astype(F32)
    return pair[:rows] + pair[rows:]


def merge_kernel(section, batch, keep, recv, small, c2, sums, *rest):
    outs, lines = rest[:-1], rest[-1]
    me = batch[0] % PLANE
    short = lines.shape[0] // PLANE
    size = keep.shape[0] // PLANE
    k2 = c2.shape[0]
    lines[...] = jnp.zeros_like(lines)
    at = small.shape[0]
    lines[0:at, :] = small[...]
    for half in range(2):
        lines[at : at + k2, :] = c2[:, half * LANES : (half + 1) * LANES]
        at += k2
    lines[at : at + sums.shape[0], :] = sums[...]
    for k, out in enumerate(outs):
        whose = me ^ k
        at = pl.ds(pl.multiple_of(whose * size, size), size)
        out[0:size, :] = (keep[at, :].astype(F32) + recv[at, :].astype(F32)).astype(BF16)
        out[size:, :] = two_parts(lines[pl.ds(pl.multiple_of(whose * short, short), short), :])


def plane_kernel(section, batch, *refs):
    parts, c1 = refs[:PLANE], refs[PLANE]
    keep, send, total, lines = refs[PLANE + 1 :]
    size, short = total.shape[0], lines.shape[0]
    total[...] = sum(p[0:size, :].astype(F32) for p in parts).astype(BF16)
    lines[...] = sum(one_part(p[size:, :]) for p in parts)
    mine = (batch[0] // PLANE) % 2
    for out, half in ((keep, mine), (send, 1 - mine)):
        at = 0
        for ref, count in ((total, size // 2), (lines, short // 2), (c1, c1.shape[0] // 2)):
            part = ref[pl.ds(pl.multiple_of(half * count, count), count), :]
            part = two_parts(part) if ref is lines else part
            out[at : at + part.shape[0], :] = part
            at += part.shape[0]


def added(a, b, short):
    fine = a.shape[0] - 16 - 2 * short
    spans = (slice(0, fine), slice(fine, fine + 2 * short), slice(fine + 2 * short, None))
    big, last = ((a[k, :].astype(F32) + b[k, :].astype(F32)).astype(BF16) for k in spans[::2])
    middle = two_parts(one_part(a[spans[1], :]) + one_part(b[spans[1], :]))
    return jnp.concatenate([big, middle, last], axis=0)


def add_kernel(a, b, out, *, short):
    out[...] = added(a[...], b[...], short)


def join_kernel(section, batch, a, b, out):
    mine = (batch[0] // PLANE) % 2
    out[mine] = a[...]
    out[1 - mine] = b[...]


def relay_kernel(section, batch, *refs):
    parts, out = refs[:PLANE], refs[-1]
    me = batch[0] % PLANE
    for k, part in enumerate(parts):
        out[me ^ k] = part[...]


def unpack_kernel(section, mine, other, *refs):
    loss, c1, b1, c2, b2, lw, lb, bw, bb, hw, hb, vw, vb, ow, ob, halves, lines = refs
    width = lw.shape[1]
    options = bw.shape[0]
    k1, k2 = c1.shape[0], c2.shape[0]
    linear_rows = lw.shape[0]
    sec = section[0]
    size = halves.shape[1] // (2 * PLANE)
    short = lines.shape[0] // (2 * PLANE)
    half = (linear_rows + options * width + width) // 2
    rest = linear_rows - half
    grad = [jnp.zeros((k1, LANES), F32) for _ in range(2)]
    for k in range(PLANE):
        for h in range(2):
            at = (2 * k + h) * size
            halves[sec, at : at + size, :] = mine[k, h, 0:size, :]
            halves[1 - sec, at : at + size, :] = other[k, h, 0:size, :]
            pair = slice(size, size + 2 * short)
            at = (2 * k + h) * short
            lines[at : at + short, :] = one_part(mine[k, h, pair, :]) + one_part(
                other[k, h, pair, :]
            )
            for ref in (mine, other):
                grad[h] += ref[k, h, size + 2 * short :, :].astype(F32)
    for part in range(2):
        c1[:, part * LANES : (part + 1) * LANES] = grad[part]
    lw[0:half, :] = halves[0, 0:half, :].astype(F32)
    lw[half:, :] = halves[1, 0:rest, :].astype(F32)
    for o in range(options):
        at = rest + o * width
        bw[o] = halves[1, at : at + width, :].astype(F32)
    at = rest + options * width
    vw[...] = halves[1, at : at + width, :].astype(F32)
    bb[...] = lines[0:options, :]
    vb[...] = lines[AT_VB, :]
    ow[...] = lines[AT_OW, :]
    hw[...] = lines[AT_HW, :]
    lb[...] = lines[AT_LB, :]
    scalars = lines[AT_SCALARS, :]
    loss[...] = scalars[:, 0:1]
    hb[...] = scalars[:, 1:3]
    ob[...] = scalars[:, 3:4]
    at = TABLE
    for part in range(2):
        c2[:, part * LANES : (part + 1) * LANES] = lines[at : at + k2, :]
        at += k2
    b1[...] = lines[at : at + 1, 0:k1]
    b2[...] = lines[at + 1 : at + 2, 0:k2]


def numbers_kernel(
    options,
    depth,
    targets,
    destination,
    b1,
    b2,
    lb,
    bb,
    hw,
    vb,
    ow,
    hb,
    ob,
    out,
    table,
):
    levels, kinds = options.shape[0], targets.shape[0]
    slots = depth.shape[1]
    rows = [options[...].astype(F32), depth[...].astype(F32)]
    rows += [targets[k] for k in range(kinds)]
    rows.append(jnp.zeros((LANES - levels - 1 - kinds * levels, slots), F32))
    out[...] = jnp.transpose(jnp.concatenate(rows, axis=0))
    table[...] = jnp.zeros_like(table)
    table[0 : bb.shape[0], :] = bb[...]
    table[AT_VB, :] = vb[...]
    table[AT_OW, :] = ow[...].astype(F32)
    table[AT_HW, :] = hw[...].astype(F32)
    table[AT_LB, :] = lb[...]
    table[AT_B1, 0 : b1.shape[1]] = b1[...]
    table[AT_B2, 0 : b2.shape[1]] = b2[...]
    lane = iota((1, LANES), 1)
    scalars = jnp.zeros((1, LANES), F32)
    for k, value in ((1, hb[:, 0:1]), (2, hb[:, 1:2]), (3, ob[...])):
        scalars = jnp.where(lane == k, value, scalars)
    table[AT_SCALARS, :] = scalars
    for k in range(slots // LANES):
        part = destination[:, k * LANES : (k + 1) * LANES]
        table[AT_DEST + k : AT_DEST + k + 1, :] = part.astype(F32)


def whole(shape):
    zeros = (0,) * len(shape)
    return pl.BlockSpec(shape, lambda *_: zeros)


def params():
    return pltpu.CompilerParams(vmem_limit_bytes=VMEM_BYTES)


def shape_of(*shape, dtype=F32):
    return jax.ShapeDtypeStruct(shape, dtype)


def near(*shape, dtype=BF16):
    return pltpu.VMEM(shape, dtype)


def cost(microseconds):
    return pl.CostEstimate(
        flops=int(1.1e9 * microseconds), bytes_accessed=int(3.6e6 * microseconds), transcendentals=0
    )


def stays(value):
    return pltpu.with_memory_space_constraint(value, pltpu.HBM)


def frame_block(frames):
    _, img, stack, _ = frames.shape
    return pl.BlockSpec((4 * STEP, img, stack, LANES), lambda g, s: (g, 0, 0, s[0]))


def encode(section, frames, w1t, w2t, lw, table):
    img = frames.shape[0]
    blocks = img // 4
    side = blocks - 1
    k1, k2, width = w1t.shape[0], w2t.shape[0], lw.shape[1]
    flat = lw.shape[0]
    outs = (
        near(blocks, side, k1, LANES),
        near(blocks, side, k1, LANES),
        near(flat, LANES),
        near(flat, LANES),
        near(width, LANES),
        near(width, LANES, dtype=F32),
    )
    weights = (w1t, w2t, lw, table)
    out_specs = [whole(o.shape) for o in outs]
    out_specs[1] = pl.BlockSpec((STEP, side, k1, LANES), lambda g, s: (g, 0, 0, 0))
    return pl.pallas_call(
        encode_kernel,
        grid_spec=pltpu.PrefetchScalarGridSpec(
            num_scalar_prefetch=1,
            grid=(blocks // STEP,),
            in_specs=[frame_block(frames), *[whole(w.shape) for w in weights]],
            out_specs=out_specs,
            scratch_shapes=[
                pltpu.VMEM((2 * REACH * k1, 256), BF16),
                pltpu.VMEM((2 * k1, 64), BF16),
                pltpu.VMEM((k1, LANES), F32),
                pltpu.VMEM((k2, LANES), F32),
                pltpu.VMEM((side, k1, LANES), F32),
            ],
        ),
        out_shape=outs,
        compiler_params=params(),
        cost_estimate=cost(9),
        name="encode",
    )(section, frames, *weights)


def plan(section, slots, enc, s3, h2, branch_w, value_w, table, per_pair, depth, half_rows):
    width = enc.shape[0]
    options = branch_w.shape[0]
    two = 2 * width
    pairs = options // 2
    outs = (
        shape_of(half_rows, LANES, dtype=BF16),
        shape_of(half_rows, LANES, dtype=BF16),
        shape_of(TABLE, LANES),
        shape_of(width, LANES, dtype=BF16),
    )
    operands = (slots, enc, s3, h2, branch_w, value_w, table)
    vmem = pltpu.VMEM
    return pl.pallas_call(
        functools.partial(plan_kernel, per_pair=per_pair),
        grid_spec=pltpu.PrefetchScalarGridSpec(
            num_scalar_prefetch=1,
            grid=(1,),
            in_specs=[whole(o.shape) for o in operands],
            out_specs=[whole(o.shape) for o in outs],
            scratch_shapes=[
                vmem((2, half_rows, LANES), BF16),
                vmem((options * width, width), BF16),
                vmem((options * width, LANES), F32),
                vmem((width + 16, width), BF16),
                vmem((width, width + 16), BF16),
                vmem((width, LANES), F32),
                vmem((width, LANES), F32),
                vmem((16, LANES), F32),
                vmem((depth, options * width, LANES), F32),
                vmem((depth, pairs, width, 2 * LANES), F32),
                vmem((depth, pairs, width, 2 * LANES), BF16),
                vmem((depth, pairs, width, 2 * LANES), BF16),
                vmem((depth, options * width, LANES), BF16),
                vmem((depth + 1, width, LANES), F32),
                vmem((depth, options, LANES), F32),
                vmem((options, LANES), F32),
                vmem((options, LANES), F32),
                vmem((options, LANES), F32),
                vmem((depth, options, LANES), F32),
                vmem((depth, 3, LANES), F32),
                vmem((depth, 2, options, LANES), F32),
                vmem((width + 16, LANES), F32),
                vmem((width, 2 * LANES), F32),
                vmem((width, 2 * LANES), F32),
                vmem((3, options, LANES), F32),
            ],
        ),
        out_shape=outs,
        compiler_params=params(),
        cost_estimate=cost(13),
        name="plan",
    )(section, *operands)


def back(section, g3, lw, s2, s1, w1t, w2t, channels):
    _, side, k1 = s1.shape[:3]
    k2 = w2t.shape[0]
    inner = side // 2 - 1
    outs = (
        shape_of(side + 2, side, k1, LANES, dtype=BF16),
        shape_of(inner + 2, inner, k2, LANES, dtype=BF16),
        shape_of(8, LANES),
        shape_of(STEP * channels * 4 * COLS, (STEP + 1) * 3 * k1, dtype=BF16),
    )
    return small_call(
        back_kernel,
        outs,
        (g3, lw, s2, s1, w1t, w2t),
        [
            pltpu.VMEM((LANES, 6 * k2), BF16),
            pltpu.VMEM((k1, LANES), F32),
            pltpu.VMEM((k2, LANES), F32),
        ],
        name="back",
        place=(section,),
        weight=5,
    )


ANYWHERE = pl.BlockSpec(memory_space=pl.ANY)


def row_window(g1):
    block = (pl.Element(STEP + 1),) + tuple(pl.Element(n) for n in g1.shape[1:])
    return pl.BlockSpec(block, lambda g, *_: (STEP * g, 0, 0, 0))


def first(section, frames, g1, after):
    blocks = frames.shape[0] // 4
    k1 = g1.shape[2]
    return pl.pallas_call(
        first_kernel,
        grid_spec=pltpu.PrefetchScalarGridSpec(
            num_scalar_prefetch=1,
            grid=(blocks // STEP,),
            in_specs=[frame_block(frames), row_window(g1), ANYWHERE],
            out_specs=whole((2 * k1, LANES)),
            scratch_shapes=[
                pltpu.VMEM((256, 2 * REACH * k1), F32),
                pltpu.VMEM((64, 2 * k1), F32),
            ],
        ),
        out_shape=shape_of(2 * k1, LANES, dtype=BF16),
        compiler_params=params(),
        cost_estimate=cost(9),
        name="first",
    )(section, frames, g1, after)


def pixels(section, band, mine, other, img, channels, after):
    steps = img // 4 // STEP
    return pl.pallas_call(
        pixels_kernel,
        grid_spec=pltpu.PrefetchScalarGridSpec(
            num_scalar_prefetch=1,
            grid=(steps,),
            in_specs=[whole(band.shape), row_window(mine), row_window(other), ANYWHERE],
            out_specs=[ANYWHERE, whole((8, LANES))],
            scratch_shapes=[
                pltpu.VMEM((2, 2, 4 * STEP, img, channels, LANES), F32),
                pltpu.SemaphoreType.DMA((2, 2)),
            ],
        ),
        out_shape=[shape_of(img, img, channels, 2 * LANES), shape_of(8, LANES)],
        compiler_params=params(),
        cost_estimate=cost(8),
        name="pixels",
    )(section, band, mine, other, after)


def small_call(
    kernel, outs, operands, scratch=(), name=None, place=None, after=(), weight=0.3
):
    specs = [pl.BlockSpec(memory_space=pltpu.VMEM)] * len(operands)
    if place is not None:
        operands = (*place, *operands)
        specs = [pl.BlockSpec(memory_space=pltpu.SMEM)] * len(place) + specs
    return pl.pallas_call(
        kernel,
        in_specs=specs + [ANYWHERE] * len(after),
        out_shape=outs,
        scratch_shapes=list(scratch),
        compiler_params=params(),
        cost_estimate=cost(weight),
        name=name,
    )(*operands, *after)


def round_up(value, step):
    return -(-value // step) * step


def swapped(value):
    return lax.ppermute(value, "section", [(0, 1), (1, 0)])


def exchanged(value):
    return lax.all_to_all(value, "batch", split_axis=0, concat_axis=0, tiled=True)


def partner(value, distance):
    count = lax.axis_size("batch")
    return lax.ppermute(value, "batch", [(b, b ^ distance) for b in range(count)])


def local(
    frames,
    destination,
    options,
    depth,
    targets,
    conv_one,
    bias_one,
    conv_two,
    bias_two,
    linear_w,
    linear_b,
    branch_w,
    branch_b,
    head_w,
    head_b,
    value_w,
    value_b,
    out_w,
    out_b,
):
    section = lax.axis_index("section").astype(jnp.int32)[None]
    peers = lax.axis_size("batch")
    frame_count = frames.shape[3]
    per_pair = frame_count // peers
    levels = options.shape[0]
    frames = stays(frames.transpose(1, 2, 0, 3))
    w1t, w2t = stays(conv_one.T), stays(conv_two.T)
    linear_w, branch_w, value_w = stays(linear_w), stays(branch_w), stays(value_w)
    encoder_params = (w1t, bias_one, w2t, bias_two, linear_w, linear_b)
    planner_params = (branch_w, branch_b, head_w.T, head_b, value_w, value_b, out_w.T, out_b)
    width = linear_w.shape[1]
    big_rows = linear_w.shape[0] + (branch_w.shape[0] + 1) * width
    size = round_up(-(-big_rows // (2 * PLANE)), 32)

    tiny = (bias_one, bias_two, linear_b, branch_b, head_w.T, value_b, out_w.T)
    tiny = [stays(v if v.ndim > 1 else v[None, :]) for v in tiny]
    numbers, table = pl.pallas_call(
        numbers_kernel,
        in_specs=[pl.BlockSpec(memory_space=pltpu.VMEM)] * (6 + len(tiny)),
        out_shape=[shape_of(frame_count, LANES), shape_of(TABLE, LANES)],
        compiler_params=params(),
        cost_estimate=cost(1),
        name="numbers",
    )(
        stays(options),
        stays(depth[None, :]),
        stays(targets),
        stays(destination[None, :]),
        *tiny,
        stays(head_b[None, :]),
        out_b[None, :],
    )
    slots = exchanged(numbers.reshape(peers, per_pair, LANES)).reshape(frame_count, LANES)

    acts = encode(section, frames, w1t, w2t, linear_w, table)
    h1, s1, h2, s2, enc, s3 = (
        pltpu.with_memory_space_constraint(v, pltpu.VMEM) for v in acts
    )
    keep, send, small, g3 = plan(
        section, slots, enc, s3, h2, branch_w, value_w, table, per_pair, levels, PLANE * size
    )
    recv = swapped(send)
    channels = frames.shape[2] // lax.axis_size("section")
    g1, g2, sums, band = back(section, g3, linear_w, s2, s1, w1t, w2t, channels)
    other = swapped(g1)
    c2 = small_call(
        second_kernel,
        shape_of(w2t.shape[0], 256),
        (h1, g2),
        name="second",
        weight=2,
    )
    place = (section, lax.axis_index("batch").astype(jnp.int32)[None])
    bf16 = functools.partial(shape_of, dtype=BF16)
    pieces = small_call(
        merge_kernel,
        [bf16(size + 2 * SHORT, LANES)] * PLANE,
        (keep, recv, small, c2, sums),
        [pltpu.VMEM((PLANE * SHORT, LANES), F32)],
        name="merge",
        place=place,
    )
    parts = [pieces[0]] + [partner(pieces[k], k) for k in range(1, PLANE)]
    c1 = first(section, frames, g1, pieces[0])
    half = bf16(size // 2 + SHORT + c1.shape[0] // 2, LANES)
    keep, send = small_call(
        plane_kernel,
        [half, half],
        (*parts, c1),
        [pltpu.VMEM((size, LANES), BF16), pltpu.VMEM((SHORT, LANES), F32)],
        name="plane",
        place=place,
    )
    recv = partner(send, PLANE)
    distance = PLANE
    while distance < peers:
        keep = small_call(
            functools.partial(add_kernel, short=SHORT // 2), half, (keep, recv), name="add"
        )
        distance *= 2
        if distance < peers:
            recv = partner(keep, distance)
    recv = partner(keep, PLANE)
    whole_piece = small_call(
        join_kernel, bf16(2, *half.shape), (keep, recv), name="join", place=place
    )
    parts = [whole_piece] + [partner(whole_piece, k) for k in range(1, PLANE)]
    frames_grad, token = pixels(section, band, g1, other, frames.shape[0], channels, whole_piece)
    got = small_call(
        relay_kernel,
        bf16(PLANE, 2, *half.shape),
        parts,
        name="relay",
        place=place,
        after=(token,),
    )
    shapes = [p.shape for p in encoder_params + planner_params]
    flat = [s if len(s) > 1 else (1,) + s for s in shapes]
    rest = small_call(
        unpack_kernel,
        [shape_of(1, 1)] + [shape_of(*s) for s in flat],
        (got, swapped(got)),
        [
            pltpu.VMEM((2, PLANE * size, LANES), BF16),
            pltpu.VMEM((PLANE * SHORT, LANES), F32),
        ],
        name="unpack",
        place=(section,),
    )
    rest = [v.reshape(s) for v, s in zip(rest, [()] + shapes)]
    for at in (1, 3, 9, 13):
        rest[at] = rest[at].T
    return (rest[0], frames_grad.transpose(2, 0, 1, 3), *rest[1:])


def solution(mesh):
    placed = (
        P(None, None, None, "batch"),
        P("batch"),
        P(None, "batch"),
        P("batch"),
        P(None, None, "batch"),
    ) + (P(),) * 14
    return jax.shard_map(
        local,
        mesh=mesh,
        in_specs=placed,
        out_specs=(P(), P("section", None, None, "batch")) + (P(),) * 14,
        check_vma=False,
    )
```

```python
import functools
import math

import jax
import jax.numpy as jnp
from jax import lax
from jax.experimental import pallas as pl
from jax.experimental.pallas import tpu as pltpu
from jax.sharding import PartitionSpec as P

BF16 = jnp.bfloat16
F32 = jnp.float32
EXACT = lax.Precision.HIGHEST
LANES = 128
VMEM_BYTES = 32 * 1024 * 1024
TILE = 16
REACH = 5
STEP = 3
COLS = 12
NEAR = 4
PARTS = 6
AT_VB, AT_OW, AT_HW, AT_LB, AT_SCALARS, AT_B1, AT_B2, AT_DEST = (
    slice(18, 19),
    slice(19, 20),
    slice(20, 22),
    slice(22, 23),
    slice(23, 24),
    slice(24, 25),
    slice(25, 26),
    26,
)
TABLE = 32
PLANE = 4
SHORT = 32


def dot(a, b, precision=None):
    return jnp.dot(a, b, preferred_element_type=F32, precision=precision)


def dot_rows(a, b, precision=None):
    return lax.dot_general(
        a, b, (((0,), (0,)), ((), ())), preferred_element_type=F32, precision=precision
    )


def dot_lanes(a, b, precision=None):
    return lax.dot_general(
        a, b, (((1,), (1,)), ((), ())), preferred_element_type=F32, precision=precision
    )


def iota(shape, axis):
    return lax.broadcasted_iota(jnp.int32, shape, axis)


def column(row):
    n = row.shape[1]
    wide = jnp.broadcast_to(row, (n, n))
    return jnp.sum(jnp.where(iota((n, n), 0) == iota((n, n), 1), wide, 0.0), axis=1, keepdims=True)


def row_of(col):
    n = col.shape[0]
    wide = jnp.broadcast_to(col, (n, n))
    return jnp.sum(jnp.where(iota((n, n), 0) == iota((n, n), 1), wide, 0.0), axis=0, keepdims=True)


def soft(x):
    t = jnp.tanh(0.5 * x)
    return jnp.maximum(x, 0.0) - jnp.log(0.5 + 0.5 * jnp.abs(t)), 0.5 + 0.5 * t


def silu_pair(x):
    s = 0.5 + 0.5 * jnp.tanh(0.5 * x)
    act = x * s
    return act, s + act * (1.0 - s)


def tap_map(half, place):
    tap, pix = iota((256, 256), 0), iota((256, 256), 1)
    hit = (
        ((tap >> 6) == (pix & 3))
        & (((tap >> 3) & 7) == (pix >> 6) + 4 * half)
        & ((tap & 7) == ((pix >> 2) & 15) - 4 * (place - 1))
    )
    return hit.astype(F32)


def tile_rows(frames, r, j, cols):
    per = 4 * STEP // len(frames)
    parts = []
    for k in range(4 // per):
        ref = frames[4 // per * r + k]
        channels = ref.shape[2]
        flat = ref.reshape(per, ref.shape[1] * channels, LANES)
        size = cols * channels
        end = min((j + 1) * size, flat.shape[1])
        parts.append(flat[:, j * size : end, :].reshape(per * (end - j * size), LANES))
    return jnp.concatenate(parts, axis=0)


def encode_kernel(section, *refs):
    frames = refs[:PARTS]
    w1t, w2t, lw, table, h1_out, s1, h2, s2, enc, s3 = refs[PARTS : PARTS + 10]
    band, edge, bias1, bias2, held, h1 = refs[PARTS + 10 :]
    g = pl.program_id(0)
    side = h1.shape[1]
    tiles = frames[0].shape[1] // TILE
    k1, k2 = w1t.shape[0], w2t.shape[0]
    reach_rows = REACH * k1

    @pl.when(g == 0)
    def _():
        for half in range(2):
            for place in range(REACH):
                at = half * reach_rows + place * k1
                taps = dot(w1t[...], tap_map(half, place).astype(BF16))
                band[at : at + k1, :] = taps.astype(BF16)
            tap, pix = iota((256, 64), 0), iota((256, 64), 1)
            hit = (
                ((tap >> 6) == (pix & 3))
                & (((tap >> 3) & 7) == (pix >> 4) + 4 * half)
                & ((tap & 7) == ((pix >> 2) & 3) + 4)
            )
            taps = dot(w1t[...], hit.astype(F32).astype(BF16))
            edge[half * k1 : (half + 1) * k1, :] = taps.astype(BF16)
        bias1[...] = jnp.broadcast_to(column(table[AT_B1, 0:k1]), bias1.shape)
        bias2[...] = jnp.broadcast_to(column(table[AT_B2, 0:k2]), bias2.shape)
        held[...] = jnp.zeros_like(held)
        h1[...] = jnp.zeros_like(h1)

    inner = side // 2 - 1
    row_len = inner * k2

    def second_row(y):
        for first in range(0, inner, 2):
            xs = [x for x in (first, first + 1) if x < inner]
            cut = [h1[pl.ds(2 * y + 1, 4), 2 * x : 2 * x + 4].reshape(256, LANES) for x in xs]
            patch = cut[0] if len(cut) == 1 else jnp.concatenate(cut, axis=1)
            got = dot(w2t[...], patch)
            for k, x in enumerate(xs):
                value, slope = soft(got[:, k * LANES : (k + 1) * LANES] + bias2[...])
                at = pl.ds(pl.multiple_of(y * row_len + x * k2, k2), k2)
                h2[at, :] = value.astype(BF16)
                s2[at, :] = slope.astype(BF16)

    ready_row = jnp.maximum((STEP * g - 6) // 2, 0)
    second_row(ready_row)
    second_row(ready_row + 1)

    for r in range(STEP):
        low, high = {}, {}

        def add(x, one, two):
            low[x] = low[x] + one if x in low else one
            high[x] = high[x] + two if x in high else two

        last = dot(edge[...], tile_rows(frames, r, tiles, TILE))
        add(side - 1, last[:k1], last[k1:])
        done = 0
        for first in range(0, tiles, 2):
            js = [j for j in (first, first + 1) if j < tiles]
            cut = [tile_rows(frames, r, j, TILE) for j in js]
            got = dot(band[...], cut[0] if len(cut) == 1 else jnp.concatenate(cut, axis=1))
            for k, j in enumerate(js):
                for place in range(REACH):
                    x = 4 * j - 1 + place
                    if 0 <= x < side:
                        at = place * k1
                        span = slice(k * LANES, (k + 1) * LANES)
                        add(
                            x,
                            got[at : at + k1, span],
                            got[reach_rows + at : reach_rows + at + k1, span],
                        )
            ready = side if js[-1] == tiles - 1 else 4 * js[-1] + 3
            for x in range(done, ready):
                value, slope = soft(held[x] + high[x] + bias1[...])
                held[x] = low[x]
                value = value.astype(BF16)
                h1[STEP * g + r, x] = value
                h1_out[r, x] = value
                s1[r, x] = slope.astype(BF16)
            done = ready

    @pl.when(g == pl.num_programs(0) - 1)
    def _():
        for y in range(inner - 2, inner):
            second_row(y)
        value, slope = soft(dot_rows(lw[...], h2[...]) + column(table[AT_LB, :]))
        enc[...] = value.astype(BF16)
        s3[...] = slope


def three_parts(row):
    high = row.astype(BF16).astype(F32)
    middle = (row - high).astype(BF16).astype(F32)
    return jnp.concatenate([high, middle, row - high - middle], axis=0)


def with_ones(value):
    return jnp.concatenate([value, ones_rows(value.shape[1])], axis=0)


def ones_rows(lanes):
    return (iota((16, lanes), 0) < 3).astype(F32).astype(BF16)


def plan_kernel(
    section,
    slots,
    enc,
    s3,
    h2,
    branch_w,
    value_w,
    table,
    keep,
    send,
    small,
    g3,
    parts,
    bwt,
    vht,
    vhw,
    ow,
    mine,
    pre,
    dbr,
    dval,
    low,
    hid,
    gb,
    h2_here,
    sem,
    *,
    per_pair,
    depth,
):
    width = enc.shape[0]
    options = branch_w.shape[0]
    pairs = options // 2
    two = 2 * width
    sec = section[0]
    h2_copy = pltpu.make_async_copy(h2, h2_here, sem)
    h2_copy.start()

    count = slots.shape[0]
    dest = jnp.concatenate(
        [table[AT_DEST + k : AT_DEST + k + 1, :] for k in range(count // LANES)], axis=1
    )
    own = jnp.where(sec == 0, dest[:, :LANES], dest[:, LANES:])
    others = jnp.transpose(jnp.broadcast_to(dest, (LANES, count)))
    index = iota((count, LANES), 1) + sec * LANES
    earlier = (others == own) & (iota((count, LANES), 0) < index)
    rank = jnp.sum(earlier.astype(F32), axis=0, keepdims=True)
    bucket = own * float(per_pair) + rank
    chosen = (iota((count, LANES), 0).astype(F32) == bucket).astype(F32)
    mine[...] = dot_rows(slots[...], chosen, EXACT)[: mine.shape[0]]

    pad = jnp.zeros((13, width), F32)
    for o in range(options):
        rows = [branch_w[o].astype(F32), three_parts(table[o : o + 1, :]), pad]
        bwt[o * width : (o + 1) * width, :] = jnp.transpose(
            jnp.concatenate(rows, axis=0)
        ).astype(BF16)
    scalars = table[AT_SCALARS, :]
    head_w = table[AT_HW, :]
    rows = [value_w[...].astype(F32), three_parts(table[AT_VB, :]), pad]
    vht[0:width, :] = jnp.transpose(jnp.concatenate(rows, axis=0)).astype(BF16)
    vht[width:, :] = jnp.zeros((16, width + 16), BF16)
    lane = iota((1, 16), 1)
    for k in range(2):
        bias = three_parts(jnp.broadcast_to(scalars[:, 1 + k : 2 + k], (1, 16)))
        bias = sum(jnp.where(lane == j, bias[j : j + 1], 0.0) for j in range(3))
        vht[width + k : width + k + 1, 0:width] = head_w[k : k + 1].astype(BF16)
        vht[width + k : width + k + 1, width:] = bias.astype(BF16)
    vhw[:, 0:width] = value_w[...]
    vhw[:, width:] = jnp.transpose(
        jnp.concatenate([head_w, jnp.zeros((14, width), F32)], axis=0)
    ).astype(BF16)
    ow[...] = jnp.broadcast_to(column(table[AT_OW, :]), (width, LANES))
    wide_ow = jnp.concatenate([ow[...], ow[...]], axis=1)

    labels = iota((options, LANES), 0).astype(F32)
    state = enc[...].astype(F32)
    rounded_all, saved = [], []
    for level in range(depth):
        picked = labels == mine[level : level + 1, :]
        rounded = state.astype(BF16)
        rounded_all.append(rounded)
        pre[...] = dot(bwt[...], with_ones(rounded))
        following = state
        reward, discount, value = [], [], []
        for t in range(pairs):
            at = slice(t * two, (t + 1) * two)
            act, slope = silu_pair(pre[at, :])
            dbr[level, at, :] = slope
            left = state + act[:width]
            right = state + act[width:]
            following = jnp.where(picked[2 * t : 2 * t + 1], left, following)
            following = jnp.where(picked[2 * t + 1 : 2 * t + 2], right, following)
            both = with_ones(jnp.concatenate([left.astype(BF16), right.astype(BF16)], axis=1))
            low[level, t] = both
            got = dot(vht[...], both)
            act, slope = silu_pair(got[:width])
            dval[level, t] = slope
            hidden = act.astype(BF16)
            hid[level, t] = hidden
            worth = jnp.sum(hidden.astype(F32) * wide_ow, axis=0, keepdims=True)
            for k in range(2):
                span = slice(k * LANES, (k + 1) * LANES)
                value.append(worth[:, span])
                reward.append(got[width : width + 1, span])
                discount.append(got[width + 1 : width + 2, span])
        reward = jnp.concatenate(reward, axis=0)
        discount = jax.nn.sigmoid(jnp.concatenate(discount, axis=0))
        value = jnp.concatenate(value, axis=0) + scalars[:, 3:4]
        quality = reward + discount * value
        top = jnp.max(quality, axis=0, keepdims=True)
        shifted = jnp.exp(quality - top)
        total = jnp.sum(shifted, axis=0, keepdims=True)
        live = (mine[depth : depth + 1, :] > level).astype(F32)
        chosen = picked.astype(F32)

        def target(kind):
            at = depth + 1 + kind * depth + level
            return mine[at : at + 1, :]

        reward_gap = live * (jnp.sum(chosen * reward, axis=0, keepdims=True) - target(0))
        discount_gap = live * (jnp.sum(chosen * discount, axis=0, keepdims=True) - target(1))
        plan_gap = live * (top + jnp.log(total) - target(2))
        grad_quality = plan_gap * (shifted / total)
        head_two = (chosen * discount_gap + grad_quality * value) * discount * (1.0 - discount)
        saved.append(
            (
                picked,
                (chosen * reward_gap + grad_quality).astype(BF16).astype(F32),
                head_two.astype(BF16).astype(F32),
                (grad_quality * discount).astype(BF16).astype(F32),
                reward_gap * reward_gap + discount_gap * discount_gap + plan_gap * plan_gap,
            )
        )
        state = following

    out_sum = jnp.zeros((width, two), F32)
    value_sum = jnp.zeros((width + 16, width + 16), F32)
    grad_next = jnp.zeros((width, LANES), F32)
    line = iota((16, two), 0)
    for level in reversed(range(depth)):
        picked, head_one, head_two, grad_value, _ = saved[level]
        upward = jnp.zeros((width, LANES), F32)
        for t in range(pairs):
            at = slice(t * two, (t + 1) * two)

            def across(rows):
                return jnp.concatenate(
                    [rows[2 * t : 2 * t + 1], rows[2 * t + 1 : 2 * t + 2]], axis=1
                )

            worth = across(grad_value)
            grad_pre = (worth * wide_ow * dval[level, t]).astype(BF16)
            out_sum = out_sum + hid[level, t].astype(F32) * worth
            heads = jnp.where(line == 0, across(head_one), 0.0)
            heads = jnp.where(line == 1, across(head_two), heads)
            heads = jnp.where(line == 2, worth, heads)
            stacked = jnp.concatenate([grad_pre, heads.astype(BF16)], axis=0)
            value_sum = value_sum + dot_lanes(stacked, low[level, t])
            moved = dot(vhw[...], stacked)
            left = moved[:, :LANES] + jnp.where(picked[2 * t : 2 * t + 1], grad_next, 0.0)
            right = moved[:, LANES:] + jnp.where(picked[2 * t + 1 : 2 * t + 2], grad_next, 0.0)
            grad_branch = jnp.concatenate([left, right], axis=0) * dbr[level, at, :]
            grad_branch = grad_branch.astype(BF16)
            gb[level, at, :] = grad_branch
            weights = jnp.concatenate([branch_w[2 * t], branch_w[2 * t + 1]], axis=1)
            upward = upward + (left + right + dot(weights, grad_branch))
        grad_next = upward

    linear_rows = h2.shape[0]
    half = (linear_rows + options * width + width) // 2
    rest = linear_rows - half
    rounded = with_ones(jnp.concatenate(rounded_all, axis=1))
    small[...] = jnp.zeros_like(small)
    if half < keep.shape[0]:
        for k in range(2):
            parts[k, half:, :] = jnp.zeros((keep.shape[0] - half, LANES), BF16)
    for o in range(options):
        at = slice(o * width, (o + 1) * width)
        grads = jnp.concatenate([gb[level, at, :] for level in range(depth)], axis=1)
        got = dot_lanes(rounded, grads)
        parts[1 - sec, rest + o * width : rest + (o + 1) * width, :] = got[:width].astype(BF16)
        small[o : o + 1, :] = got[width : width + 1]
    after = rest + options * width
    parts[1 - sec, after : after + width, :] = jnp.transpose(value_sum[:width, :width]).astype(BF16)

    grad_three = (grad_next.astype(BF16).astype(F32) * s3[...]).astype(BF16)
    g3[...] = grad_three
    h2_copy.wait()
    chunk = linear_rows // 9
    for i in range(8):
        at = slice(i * chunk, (i + 1) * chunk)
        parts[sec, at, :] = dot_lanes(h2_here[at, :], grad_three).astype(BF16)
    last = dot_lanes(h2_here[8 * chunk :, :], grad_three).astype(BF16)
    parts[sec, 8 * chunk : half, :] = last[: half - 8 * chunk]
    parts[1 - sec, 0:rest, :] = last[half - 8 * chunk :]
    keep[...] = parts[0]
    send[...] = parts[1]

    small[AT_VB, :] = row_of(value_sum[:width, width : width + 1])
    small[AT_OW, :] = row_of(jnp.sum(out_sum, axis=1, keepdims=True))
    small[AT_HW, :] = value_sum[width : width + 2, :width]
    small[AT_LB, :] = row_of(jnp.sum(grad_three.astype(F32), axis=1, keepdims=True))
    loss = 0.5 * jnp.sum(sum(kept[4] for kept in saved), axis=1, keepdims=True)
    ends = [loss] + [value_sum[width + k : width + k + 1, width : width + 1] for k in range(3)]
    lane = iota((1, LANES), 1)
    line = jnp.zeros((1, LANES), F32)
    for k, end in enumerate(ends):
        line = jnp.where(lane == k, end, line)
    small[AT_SCALARS, :] = line


def back_kernel(g3, lw, s2, s1_far, h1_far, w2t, g1, c2, sums, t2, g2, s1, h1, sems):
    side, k1 = s1.shape[1], s1.shape[2]
    k2 = w2t.shape[0]
    inner = side // 2 - 1
    row_len = inner * k2
    copies = [
        pltpu.make_async_copy(s1_far, s1, sems.at[0]),
        pltpu.make_async_copy(h1_far, h1, sems.at[1]),
    ]
    for copy in copies:
        copy.start()
    tap, pix = iota((LANES, 256), 1), iota((LANES, 256), 0)
    for yrel in range(2):
        for p in range(3):
            hit = (
                ((tap & 15) == (pix & 15))
                & ((tap >> 6) == (pix >> 6) + 2 * (1 - yrel))
                & (((tap >> 4) & 3) == ((pix >> 4) & 3) + 2 - 2 * p)
            )
            at = (yrel * 3 + p) * k2
            t2[:, at : at + k2] = dot_lanes(hit.astype(F32).astype(BF16), w2t[...]).astype(BF16)
    g2[0] = jnp.zeros(g2.shape[1:], BF16)
    g2[inner + 1] = jnp.zeros(g2.shape[1:], BF16)
    g1[0] = jnp.zeros(g1.shape[1:], BF16)
    g1[side + 1] = jnp.zeros(g1.shape[1:], BF16)
    zero = jnp.zeros((k2, LANES), BF16)
    total_one = jnp.zeros((k1, LANES), F32)
    total_two = jnp.zeros((k2, LANES), F32)
    for y in range(inner):
        at = slice(y * row_len, (y + 1) * row_len)
        grad = dot(lw[at, :], g3[...]) * s2[at, :].astype(F32)
        grad = grad.astype(BF16).reshape(inner, k2, LANES)
        g2[y + 1] = grad
        total_two = total_two + jnp.sum(grad.astype(F32), axis=0)
    for copy in copies:
        copy.wait()
    total = jnp.zeros(c2.shape, F32)
    for b in range(side // 2):
        cut = []
        for j in range(side // 4):
            pieces = []
            for yrel in range(2):
                for p in range(3):
                    x = 2 * j - 1 + p
                    pieces.append(g2[b + yrel, x] if 0 <= x < inner else zero)
            cut.append(jnp.concatenate(pieces, axis=0))
        got = dot(t2[...], jnp.concatenate(cut, axis=1))
        for u in range(2):
            for j in range(side // 4):
                part = got[u * 64 : (u + 1) * 64, j * LANES : (j + 1) * LANES]
                slope = s1[2 * b + u + 1, 4 * j : 4 * j + 4].astype(F32)
                grad = (part.reshape(4, k1, LANES) * slope).astype(BF16)
                g1[2 * b + u + 1, 4 * j : 4 * j + 4] = grad
                total_one = total_one + jnp.sum(grad.astype(F32), axis=0)
        if b < inner:
            grads = jnp.concatenate([g2[b + 1, x] for x in range(inner)], axis=1)
            patches = [
                h1[2 * b + 1 : 2 * b + 5, 2 * x : 2 * x + 4].reshape(256, LANES)
                for x in range(inner)
            ]
            total = total + dot_lanes(grads, jnp.concatenate(patches, axis=1))
    c2[...] = total
    sums[...] = jnp.zeros_like(sums)
    sums[0:1, 0:k1] = row_of(jnp.sum(total_one, axis=1, keepdims=True))
    sums[1:2, 0:k2] = row_of(jnp.sum(total_two, axis=1, keepdims=True))


def band_kernel(section, w1t, after, band):
    k1 = w1t.shape[0]
    size = band.shape[0]
    channels = size // (STEP * 4 * COLS)
    line = COLS * channels
    tap, pix = iota((size, 256), 1), iota((size, 256), 0)
    r = pix // (4 * line)
    u4 = (pix // line) % 4
    xx = (pix // channels) % COLS
    c = pix % channels + section[0] * channels
    for yrel in range(STEP + 1):
        for p in range(NEAR):
            hit = (
                ((tap >> 6) == c)
                & (((tap >> 3) & 7) == 4 * (r + 1 - yrel) + u4)
                & ((tap & 7) == xx + 4 - 4 * p)
            )
            at = (yrel * NEAR + p) * k1
            band[:, at : at + k1] = dot_lanes(hit.astype(F32).astype(BF16), w1t[...]).astype(BF16)


def first_kernel(section, *refs):
    frames = refs[:PARTS]
    g1, after, c1, acc = refs[PARTS:]
    g = pl.program_id(0)
    side, k1 = g1.shape[1], g1.shape[2]
    img, channels = frames[0].shape[1], frames[0].shape[2]

    @pl.when(g == 0)
    def _():
        acc[...] = jnp.zeros_like(acc)

    zero = jnp.zeros((k1, LANES), BF16)
    pixels, grads = [], []
    for j in range(img // COLS):
        pixels.append(
            jnp.concatenate([tile_rows(frames, r, j, COLS) for r in range(STEP)], axis=0)
        )
        pieces = []
        for yrel in range(STEP + 1):
            for p in range(NEAR):
                x = 3 * j - 1 + p
                pieces.append(g1[yrel, x] if 0 <= x < side else zero)
        grads.append(jnp.concatenate(pieces, axis=0))
    acc[...] += dot_lanes(jnp.concatenate(pixels, axis=1), jnp.concatenate(grads, axis=1))

    @pl.when(g == pl.num_programs(0) - 1)
    def _():
        line = COLS * channels
        step = 4 * channels
        taps = []
        for half in range(2):
            total = sum(
                acc[r * 4 * line : (r + 1) * 4 * line, :][
                    :, (r + 1 - half) * NEAR * k1 : (r + 2 - half) * NEAR * k1
                ]
                for r in range(STEP)
            )
            for u in range(4):
                part = total[u * line : (u + 1) * line]
                cols = [part[:, p * k1 : (p + 1) * k1] for p in range(NEAR)]
                taps.append(cols[1][0:step] + cols[2][step : 2 * step] + cols[3][2 * step :])
                taps.append(cols[0][0:step] + cols[1][step : 2 * step] + cols[2][2 * step :])
        row, col = iota((256, 256), 0), iota((256, 256), 1)
        moves = ((row & 3) == (col >> 6)) & ((row >> 2) == (col & 63))
        grad = dot_rows(jnp.concatenate(taps, axis=0), moves.astype(F32), EXACT)
        for half in range(2):
            c1[half * k1 : (half + 1) * k1, :] = grad[:, half * LANES : (half + 1) * LANES].astype(
                BF16
            )


def pixels_kernel(section, band, mine, other, after, out, token, held, sems):
    g = pl.program_id(0)
    steps = pl.num_programs(0)
    side, k1 = mine.shape[1], mine.shape[2]
    img, channels = out.shape[1], out.shape[2]
    sec = section[0]
    line = COLS * channels
    flat = held.reshape(2, 2, 4 * STEP, img * channels, LANES)
    slot = g % 2

    def writes(step, at):
        rows = pl.ds(pl.multiple_of(4 * STEP * step, 4), 4 * STEP)
        places = (sec * LANES, (1 - sec) * LANES)
        return [
            pltpu.make_async_copy(
                held.at[at, k],
                out.at[rows, :, :, pl.ds(pl.multiple_of(places[k], LANES), LANES)],
                sems.at[at, k],
            )
            for k in range(2)
        ]

    @pl.when(g >= 2)
    def _():
        for copy in writes(g - 2, slot):
            copy.wait()

    zero = jnp.zeros((k1, 2 * LANES), BF16)
    for j in range(img // COLS):
        pieces = []
        for yrel in range(STEP + 1):
            for p in range(NEAR):
                x = 3 * j - 1 + p
                if 0 <= x < side:
                    pieces.append(jnp.concatenate([mine[yrel, x], other[yrel, x]], axis=1))
                else:
                    pieces.append(zero)
        got = dot(band[...], jnp.concatenate(pieces, axis=0))
        for k in range(4 * STEP):
            at = slice(k * line, (k + 1) * line)
            span = slice(j * line, (j + 1) * line)
            flat[slot, 0, k, span, :] = got[at, :LANES]
            flat[slot, 1, k, span, :] = got[at, LANES:]
    for copy in writes(g, slot):
        copy.start()
    token[...] = jnp.zeros_like(token)

    @pl.when(g == steps - 1)
    def _():
        @pl.when(g >= 1)
        def _():
            for copy in writes(g - 1, 1 - slot):
                copy.wait()

        for copy in writes(g, slot):
            copy.wait()


def two_parts(value):
    high = value.astype(BF16).astype(F32)
    return jnp.concatenate([high, value - high], axis=0).astype(BF16)


def one_part(pair):
    rows = pair.shape[0] // 2
    pair = pair.astype(F32)
    return pair[:rows] + pair[rows:]


def merge_kernel(section, batch, keep, recv, small, c2, sums, *rest):
    outs, lines = rest[:-1], rest[-1]
    me = batch[0] % PLANE
    short = lines.shape[0] // PLANE
    size = keep.shape[0] // PLANE
    k2 = c2.shape[0]
    lines[...] = jnp.zeros_like(lines)
    at = small.shape[0]
    lines[0:at, :] = small[...]
    for half in range(2):
        lines[at : at + k2, :] = c2[:, half * LANES : (half + 1) * LANES]
        at += k2
    lines[at : at + sums.shape[0], :] = sums[...]
    for k, out in enumerate(outs):
        whose = me ^ k
        at = pl.ds(pl.multiple_of(whose * size, size), size)
        out[0:size, :] = (keep[at, :].astype(F32) + recv[at, :].astype(F32)).astype(BF16)
        out[size:, :] = two_parts(lines[pl.ds(pl.multiple_of(whose * short, short), short), :])


def plane_kernel(section, batch, *refs):
    parts, c1 = refs[:PLANE], refs[PLANE]
    keep, send, total, lines = refs[PLANE + 1 :]
    size, short = total.shape[0], lines.shape[0]
    total[...] = sum(p[0:size, :].astype(F32) for p in parts).astype(BF16)
    lines[...] = sum(one_part(p[size:, :]) for p in parts)
    mine = (batch[0] // PLANE) % 2
    for out, half in ((keep, mine), (send, 1 - mine)):
        at = 0
        for ref, count in ((total, size // 2), (lines, short // 2), (c1, c1.shape[0] // 2)):
            part = ref[pl.ds(pl.multiple_of(half * count, count), count), :]
            part = two_parts(part) if ref is lines else part
            out[at : at + part.shape[0], :] = part
            at += part.shape[0]


def added(a, b, short):
    fine = a.shape[0] - 16 - 2 * short
    spans = (slice(0, fine), slice(fine, fine + 2 * short), slice(fine + 2 * short, None))
    big, last = ((a[k, :].astype(F32) + b[k, :].astype(F32)).astype(BF16) for k in spans[::2])
    middle = two_parts(one_part(a[spans[1], :]) + one_part(b[spans[1], :]))
    return jnp.concatenate([big, middle, last], axis=0)


def add_kernel(a, b, out, *, short):
    out[...] = added(a[...], b[...], short)


def join_kernel(section, batch, a, b, out):
    mine = (batch[0] // PLANE) % 2
    out[mine] = a[...]
    out[1 - mine] = b[...]


def relay_kernel(section, batch, *refs):
    parts, out = refs[:PLANE], refs[-1]
    me = batch[0] % PLANE
    for k, part in enumerate(parts):
        out[me ^ k] = part[...]


def unpack_kernel(section, mine, other, *refs):
    loss, c1, b1, c2, b2, lw, lb, bw, bb, hw, hb, vw, vb, ow, ob, halves, lines = refs
    width = lw.shape[1]
    options = bw.shape[0]
    k1, k2 = c1.shape[0], c2.shape[0]
    linear_rows = lw.shape[0]
    sec = section[0]
    size = halves.shape[1] // (2 * PLANE)
    short = lines.shape[0] // (2 * PLANE)
    half = (linear_rows + options * width + width) // 2
    rest = linear_rows - half
    grad = [jnp.zeros((k1, LANES), F32) for _ in range(2)]
    for k in range(PLANE):
        for h in range(2):
            at = (2 * k + h) * size
            halves[sec, at : at + size, :] = mine[k, h, 0:size, :]
            halves[1 - sec, at : at + size, :] = other[k, h, 0:size, :]
            pair = slice(size, size + 2 * short)
            at = (2 * k + h) * short
            lines[at : at + short, :] = one_part(mine[k, h, pair, :]) + one_part(
                other[k, h, pair, :]
            )
            for ref in (mine, other):
                grad[h] += ref[k, h, size + 2 * short :, :].astype(F32)
    for part in range(2):
        c1[:, part * LANES : (part + 1) * LANES] = grad[part]
    lw[0:half, :] = halves[0, 0:half, :].astype(F32)
    lw[half:, :] = halves[1, 0:rest, :].astype(F32)
    for o in range(options):
        at = rest + o * width
        bw[o] = halves[1, at : at + width, :].astype(F32)
    at = rest + options * width
    vw[...] = halves[1, at : at + width, :].astype(F32)
    bb[...] = lines[0:options, :]
    vb[...] = lines[AT_VB, :]
    ow[...] = lines[AT_OW, :]
    hw[...] = lines[AT_HW, :]
    lb[...] = lines[AT_LB, :]
    scalars = lines[AT_SCALARS, :]
    loss[...] = scalars[:, 0:1]
    hb[...] = scalars[:, 1:3]
    ob[...] = scalars[:, 3:4]
    at = TABLE
    for part in range(2):
        c2[:, part * LANES : (part + 1) * LANES] = lines[at : at + k2, :]
        at += k2
    b1[...] = lines[at : at + 1, 0:k1]
    b2[...] = lines[at + 1 : at + 2, 0:k2]


def numbers_kernel(
    options,
    depth,
    targets,
    destination,
    b1,
    b2,
    lb,
    bb,
    hw,
    vb,
    ow,
    hb,
    ob,
    out,
    table,
):
    levels, kinds = options.shape[0], targets.shape[0]
    slots = depth.shape[1]
    rows = [options[...].astype(F32), depth[...].astype(F32)]
    rows += [targets[k] for k in range(kinds)]
    rows.append(jnp.zeros((LANES - levels - 1 - kinds * levels, slots), F32))
    out[...] = jnp.transpose(jnp.concatenate(rows, axis=0))
    table[...] = jnp.zeros_like(table)
    table[0 : bb.shape[0], :] = bb[...]
    table[AT_VB, :] = vb[...]
    table[AT_OW, :] = ow[...].astype(F32)
    table[AT_HW, :] = hw[...].astype(F32)
    table[AT_LB, :] = lb[...]
    table[AT_B1, 0 : b1.shape[1]] = b1[...]
    table[AT_B2, 0 : b2.shape[1]] = b2[...]
    lane = iota((1, LANES), 1)
    scalars = jnp.zeros((1, LANES), F32)
    for k, value in ((1, hb[:, 0:1]), (2, hb[:, 1:2]), (3, ob[...])):
        scalars = jnp.where(lane == k, value, scalars)
    table[AT_SCALARS, :] = scalars
    for k in range(slots // LANES):
        part = destination[:, k * LANES : (k + 1) * LANES]
        table[AT_DEST + k : AT_DEST + k + 1, :] = part.astype(F32)


def whole(shape):
    zeros = (0,) * len(shape)
    return pl.BlockSpec(shape, lambda *_: zeros)


def params():
    return pltpu.CompilerParams(vmem_limit_bytes=VMEM_BYTES)


def shape_of(*shape, dtype=F32):
    return jax.ShapeDtypeStruct(shape, dtype)


def cost(microseconds):
    return pl.CostEstimate(
        flops=int(1.1e9 * microseconds), bytes_accessed=int(3.6e6 * microseconds), transcendentals=0
    )


def stays(value):
    return pltpu.with_memory_space_constraint(value, pltpu.HBM)


def frame_blocks(frames):
    _, img, stack, _ = frames.shape
    block = (4 * STEP // PARTS, img, stack, LANES)

    def spec(k):
        return pl.BlockSpec(block, lambda g, s: (PARTS * g + k, 0, 0, s[0]))

    return [spec(k) for k in range(PARTS)]


def encode(section, frames, w1t, w2t, lw, table):
    img = frames.shape[0]
    blocks = img // 4
    side = blocks - 1
    k1, k2, width = w1t.shape[0], w2t.shape[0], lw.shape[1]
    flat = lw.shape[0]
    outs = (
        pltpu.HBM((blocks, side, k1, LANES), BF16),
        pltpu.HBM((blocks, side, k1, LANES), BF16),
        shape_of(flat, LANES, dtype=BF16),
        shape_of(flat, LANES, dtype=BF16),
        shape_of(width, LANES, dtype=BF16),
        shape_of(width, LANES),
    )
    weights = (w1t, w2t, lw, table)
    out_specs = [whole(o.shape) for o in outs]
    for k in range(2):
        out_specs[k] = pl.BlockSpec((STEP, side, k1, LANES), lambda g, s: (g, 0, 0, 0))
    return pl.pallas_call(
        encode_kernel,
        grid_spec=pltpu.PrefetchScalarGridSpec(
            num_scalar_prefetch=1,
            grid=(blocks // STEP,),
            in_specs=[*frame_blocks(frames), *[whole(w.shape) for w in weights]],
            out_specs=out_specs,
            scratch_shapes=[
                pltpu.VMEM((2 * REACH * k1, 256), BF16),
                pltpu.VMEM((2 * k1, 64), BF16),
                pltpu.VMEM((k1, LANES), F32),
                pltpu.VMEM((k2, LANES), F32),
                pltpu.VMEM((side, k1, LANES), F32),
                pltpu.VMEM((blocks, side, k1, LANES), BF16),
            ],
        ),
        out_shape=outs,
        compiler_params=params(),
        cost_estimate=cost(9),
        name="encode",
    )(section, *[frames] * PARTS, *weights)


def plan(section, slots, enc, s3, h2, branch_w, value_w, table, per_pair, depth, half_rows):
    width = enc.shape[0]
    options = branch_w.shape[0]
    two = 2 * width
    pairs = options // 2
    outs = (
        shape_of(half_rows, LANES, dtype=BF16),
        shape_of(half_rows, LANES, dtype=BF16),
        shape_of(TABLE, LANES),
        shape_of(width, LANES, dtype=BF16),
    )
    operands = (slots, enc, s3, h2, branch_w, value_w, table)
    specs = [whole(o.shape) for o in operands]
    specs[3] = ANYWHERE
    vmem = pltpu.VMEM
    return pl.pallas_call(
        functools.partial(plan_kernel, per_pair=per_pair, depth=depth),
        grid_spec=pltpu.PrefetchScalarGridSpec(
            num_scalar_prefetch=1,
            grid=(1,),
            in_specs=specs,
            out_specs=[whole(o.shape) for o in outs],
            scratch_shapes=[
                vmem((2, half_rows, LANES), BF16),
                vmem((options * width, width + 16), BF16),
                vmem((width + 16, width + 16), BF16),
                vmem((width, width + 16), BF16),
                vmem((width, LANES), F32),
                vmem((16, LANES), F32),
                vmem((options * width, LANES), F32),
                vmem((depth, options * width, LANES), F32),
                vmem((depth, pairs, width, two), F32),
                vmem((depth, pairs, width + 16, two), BF16),
                vmem((depth, pairs, width, two), BF16),
                vmem((depth, options * width, LANES), BF16),
                vmem(h2.shape, BF16),
                pltpu.SemaphoreType.DMA,
            ],
        ),
        out_shape=outs,
        compiler_params=params(),
        cost_estimate=cost(13),
        name="plan",
    )(section, *operands)


def back(g3, lw, s2, s1, h1, w2t):
    _, side, k1 = s1.shape[:3]
    k2 = w2t.shape[0]
    inner = side // 2 - 1
    outs = (
        shape_of(side + 2, side, k1, LANES, dtype=BF16),
        shape_of(k2, 256),
        shape_of(8, LANES),
    )
    near = pl.BlockSpec(memory_space=pltpu.VMEM)
    return pl.pallas_call(
        back_kernel,
        in_specs=[near, near, near, ANYWHERE, ANYWHERE, near],
        out_shape=outs,
        scratch_shapes=[
            pltpu.VMEM((LANES, 6 * k2), BF16),
            pltpu.VMEM((inner + 2, inner, k2, LANES), BF16),
            pltpu.VMEM(s1.shape, BF16),
            pltpu.VMEM(h1.shape, BF16),
            pltpu.SemaphoreType.DMA((2,)),
        ],
        compiler_params=params(),
        cost_estimate=cost(5),
        name="back",
    )(g3, lw, s2, s1, h1, w2t)


ANYWHERE = pl.BlockSpec(memory_space=pl.ANY)


def row_window(g1):
    block = (pl.Element(STEP + 1),) + tuple(pl.Element(n) for n in g1.shape[1:])
    return pl.BlockSpec(block, lambda g, *_: (STEP * g, 0, 0, 0))


def first(section, frames, g1, after):
    blocks = frames.shape[0] // 4
    k1 = g1.shape[2]
    return pl.pallas_call(
        first_kernel,
        grid_spec=pltpu.PrefetchScalarGridSpec(
            num_scalar_prefetch=1,
            grid=(blocks // STEP,),
            in_specs=[*frame_blocks(frames), row_window(g1), ANYWHERE],
            out_specs=whole((2 * k1, LANES)),
            scratch_shapes=[
                pltpu.VMEM(
                    (STEP * 4 * COLS * frames.shape[2], (STEP + 1) * NEAR * k1), F32
                ),
            ],
        ),
        out_shape=shape_of(2 * k1, LANES, dtype=BF16),
        compiler_params=params(),
        cost_estimate=cost(9),
        name="first",
    )(section, *[frames] * PARTS, g1, after)


def pixels(section, band, mine, other, img, channels, after):
    steps = img // 4 // STEP
    return pl.pallas_call(
        pixels_kernel,
        grid_spec=pltpu.PrefetchScalarGridSpec(
            num_scalar_prefetch=1,
            grid=(steps,),
            in_specs=[whole(band.shape), row_window(mine), row_window(other), ANYWHERE],
            out_specs=[ANYWHERE, whole((8, LANES))],
            scratch_shapes=[
                pltpu.VMEM((2, 2, 4 * STEP, img, channels, LANES), F32),
                pltpu.SemaphoreType.DMA((2, 2)),
            ],
        ),
        out_shape=[shape_of(img, img, channels, 2 * LANES), shape_of(8, LANES)],
        compiler_params=params(),
        cost_estimate=cost(8),
        name="pixels",
    )(section, band, mine, other, after)


def small_call(
    kernel, outs, operands, scratch=(), name=None, place=None, after=(), weight=0.3
):
    specs = [pl.BlockSpec(memory_space=pltpu.VMEM)] * len(operands)
    if place is not None:
        operands = (*place, *operands)
        specs = [pl.BlockSpec(memory_space=pltpu.SMEM)] * len(place) + specs
    return pl.pallas_call(
        kernel,
        in_specs=specs + [ANYWHERE] * len(after),
        out_shape=outs,
        scratch_shapes=list(scratch),
        compiler_params=params(),
        cost_estimate=cost(weight),
        name=name,
    )(*operands, *after)


def round_up(value, step):
    return -(-value // step) * step


def swapped(value):
    return lax.ppermute(value, "section", [(0, 1), (1, 0)])


def exchanged(value):
    return lax.all_to_all(value, "batch", split_axis=0, concat_axis=0, tiled=True)


def partner(value, distance):
    count = lax.axis_size("batch")
    return lax.ppermute(value, "batch", [(b, b ^ distance) for b in range(count)])


def local(
    frames,
    destination,
    options,
    depth,
    targets,
    conv_one,
    bias_one,
    conv_two,
    bias_two,
    linear_w,
    linear_b,
    branch_w,
    branch_b,
    head_w,
    head_b,
    value_w,
    value_b,
    out_w,
    out_b,
):
    section = lax.axis_index("section").astype(jnp.int32)[None]
    peers = lax.axis_size("batch")
    frame_count = frames.shape[3]
    per_pair = frame_count // peers
    levels = options.shape[0]
    frames = stays(frames.transpose(1, 2, 0, 3))
    w1t, w2t = stays(conv_one.T), stays(conv_two.T)
    linear_w, branch_w, value_w = stays(linear_w), stays(branch_w), stays(value_w)
    encoder_params = (w1t, bias_one, w2t, bias_two, linear_w, linear_b)
    planner_params = (branch_w, branch_b, head_w.T, head_b, value_w, value_b, out_w.T, out_b)
    width = linear_w.shape[1]
    big_rows = linear_w.shape[0] + (branch_w.shape[0] + 1) * width
    size = round_up(-(-big_rows // (2 * PLANE)), 32)

    tiny = (bias_one, bias_two, linear_b, branch_b, head_w.T, value_b, out_w.T)
    tiny = [stays(v if v.ndim > 1 else v[None, :]) for v in tiny]
    numbers, table = pl.pallas_call(
        numbers_kernel,
        in_specs=[pl.BlockSpec(memory_space=pltpu.VMEM)] * (6 + len(tiny)),
        out_shape=[shape_of(frame_count, LANES), shape_of(TABLE, LANES)],
        compiler_params=params(),
        cost_estimate=cost(1),
        name="numbers",
    )(
        stays(options),
        stays(depth[None, :]),
        stays(targets),
        stays(destination[None, :]),
        *tiny,
        stays(head_b[None, :]),
        out_b[None, :],
    )
    slots = exchanged(numbers.reshape(peers, per_pair, LANES)).reshape(frame_count, LANES)

    h1, s1, h2, s2, enc, s3 = encode(section, frames, w1t, w2t, linear_w, table)
    h1, s1 = stays(h1), stays(s1)
    keep, send, small, g3 = plan(
        section, slots, enc, s3, h2, branch_w, value_w, table, per_pair, levels, PLANE * size
    )
    recv = swapped(send)
    channels = frames.shape[2] // lax.axis_size("section")
    g1, c2, sums = back(g3, linear_w, s2, s1, h1, w2t)
    other = swapped(g1)
    place = (section, lax.axis_index("batch").astype(jnp.int32)[None])
    bf16 = functools.partial(shape_of, dtype=BF16)
    pieces = small_call(
        merge_kernel,
        [bf16(size + 2 * SHORT, LANES)] * PLANE,
        (keep, recv, small, c2, sums),
        [pltpu.VMEM((PLANE * SHORT, LANES), F32)],
        name="merge",
        place=place,
    )
    parts = [pieces[0]] + [partner(pieces[k], k) for k in range(1, PLANE)]
    c1 = first(section, frames, g1, pieces[0])
    half = bf16(size // 2 + SHORT + c1.shape[0] // 2, LANES)
    keep, send = small_call(
        plane_kernel,
        [half, half],
        (*parts, c1),
        [pltpu.VMEM((size, LANES), BF16), pltpu.VMEM((SHORT, LANES), F32)],
        name="plane",
        place=place,
    )
    recv = partner(send, PLANE)
    k1 = w1t.shape[0]
    band = small_call(
        band_kernel,
        bf16(STEP * 4 * COLS * channels, (STEP + 1) * NEAR * k1),
        (w1t,),
        name="band",
        place=(section,),
        after=(send,),
        weight=2,
    )
    distance = PLANE
    while distance < peers:
        keep = small_call(
            functools.partial(add_kernel, short=SHORT // 2), half, (keep, recv), name="add"
        )
        distance *= 2
        if distance < peers:
            recv = partner(keep, distance)
    recv = partner(keep, PLANE)
    whole_piece = small_call(
        join_kernel, bf16(2, *half.shape), (keep, recv), name="join", place=place
    )
    parts = [whole_piece] + [partner(whole_piece, k) for k in range(1, PLANE)]
    frames_grad, token = pixels(section, band, g1, other, frames.shape[0], channels, whole_piece)
    got = small_call(
        relay_kernel,
        bf16(PLANE, 2, *half.shape),
        parts,
        name="relay",
        place=place,
        after=(token,),
    )
    shapes = [p.shape for p in encoder_params + planner_params]
    flat = [s if len(s) > 1 else (1,) + s for s in shapes]
    rest = small_call(
        unpack_kernel,
        [shape_of(1, 1)] + [shape_of(*s) for s in flat],
        (got, swapped(got)),
        [
            pltpu.VMEM((2, PLANE * size, LANES), BF16),
            pltpu.VMEM((PLANE * SHORT, LANES), F32),
        ],
        name="unpack",
        place=(section,),
    )
    rest = [v.reshape(s) for v, s in zip(rest, [()] + shapes)]
    for at in (1, 3, 9, 13):
        rest[at] = rest[at].T
    return (rest[0], frames_grad.transpose(2, 0, 1, 3), *rest[1:])


def solution(mesh):
    placed = (
        P(None, None, None, "batch"),
        P("batch"),
        P(None, "batch"),
        P("batch"),
        P(None, None, "batch"),
    ) + (P(),) * 14
    return jax.shard_map(
        local,
        mesh=mesh,
        in_specs=placed,
        out_specs=(P(), P("section", None, None, "batch")) + (P(),) * 14,
        check_vma=False,
    )
```

```python
import functools
import math

import jax
import jax.numpy as jnp
from jax import lax
from jax.experimental import pallas as pl
from jax.experimental.pallas import tpu as pltpu
from jax.sharding import PartitionSpec as P

BF16 = jnp.bfloat16
F32 = jnp.float32
EXACT = lax.Precision.HIGHEST
LANES = 128
VMEM_BYTES = 32 * 1024 * 1024
TILE = 16
REACH = 5
STEP = 3
COLS = 12
NEAR = 4
PARTS = 3
AT_VB, AT_OW, AT_HW, AT_LB, AT_SCALARS, AT_B1, AT_B2, AT_DEST = (
    slice(18, 19),
    slice(19, 20),
    slice(20, 22),
    slice(22, 23),
    slice(23, 24),
    slice(24, 25),
    slice(25, 26),
    26,
)
TABLE = 32
PLANE = 4
SHORT = 32


def dot(a, b, precision=None):
    return jnp.dot(a, b, preferred_element_type=F32, precision=precision)


def dot_rows(a, b, precision=None):
    return lax.dot_general(
        a, b, (((0,), (0,)), ((), ())), preferred_element_type=F32, precision=precision
    )


def dot_lanes(a, b, precision=None):
    return lax.dot_general(
        a, b, (((1,), (1,)), ((), ())), preferred_element_type=F32, precision=precision
    )


def iota(shape, axis):
    return lax.broadcasted_iota(jnp.int32, shape, axis)


def column(row):
    n = row.shape[1]
    wide = jnp.broadcast_to(row, (n, n))
    return jnp.sum(jnp.where(iota((n, n), 0) == iota((n, n), 1), wide, 0.0), axis=1, keepdims=True)


def row_of(col):
    n = col.shape[0]
    wide = jnp.broadcast_to(col, (n, n))
    return jnp.sum(jnp.where(iota((n, n), 0) == iota((n, n), 1), wide, 0.0), axis=0, keepdims=True)


def soft(x):
    t = jnp.tanh(0.5 * x)
    return jnp.maximum(x, 0.0) - jnp.log(0.5 + 0.5 * jnp.abs(t)), 0.5 + 0.5 * t


def silu_pair(x):
    s = 0.5 + 0.5 * jnp.tanh(0.5 * x)
    act = x * s
    return act, s + act * (1.0 - s)


def pixel_order(w1t):
    tap, pix = iota((256, 256), 0), iota((256, 256), 1)
    moves = ((tap >> 6) == (pix & 3)) & ((tap & 63) == (pix >> 2))
    return dot(w1t, moves.astype(F32).astype(BF16))


def tile_rows(frames, r, j, cols):
    per = 4 * STEP // len(frames)
    parts = []
    for k in range(4 // per):
        ref = frames[4 // per * r + k]
        channels = ref.shape[2]
        flat = ref.reshape(per, ref.shape[1] * channels, LANES)
        size = cols * channels
        end = min((j + 1) * size, flat.shape[1])
        parts.append(flat[:, j * size : end, :].reshape(per * (end - j * size), LANES))
    return jnp.concatenate(parts, axis=0)


def encode_kernel(section, *refs):
    frames = refs[:PARTS]
    w1t, w2t, lw, table, h1_out, s1, h2, s2, enc, s3 = refs[PARTS : PARTS + 10]
    band, edge, band2, bias1, bias2, held, held2, h1 = refs[PARTS + 10 :]
    g = pl.program_id(0)
    side = h1.shape[1]
    tiles = frames[0].shape[1] // TILE
    k1, k2 = w1t.shape[0], w2t.shape[0]
    reach_rows = REACH * k1

    inner = side // 2 - 1
    row_len = inner * k2
    two = 2 * k2 * 3

    @pl.when(g == 0)
    def _():
        taps = pixel_order(w1t[...])
        edges = []
        for half in range(2):
            lines = [taps[:, 32 * (4 * half + u) : 32 * (4 * half + u + 1)] for u in range(4)]
            for place in range(REACH):
                pieces = []
                for line in lines:
                    start = 16 * (place - 1)
                    cut = line[:, max(0, -start) : min(32, 64 - start)]
                    start = max(start, 0)
                    pieces += [jnp.zeros((k1, start), F32)] if start else []
                    pieces.append(cut)
                    rest = 64 - start - cut.shape[1]
                    pieces += [jnp.zeros((k1, rest), F32)] if rest else []
                at = half * reach_rows + place * k1
                band[at : at + k1, :] = jnp.concatenate(pieces, axis=1).astype(BF16)
            edges.append(jnp.concatenate([line[:, 16:] for line in lines], axis=1))
        edge[...] = jnp.concatenate(edges, axis=0).astype(BF16)
        tap, pix = iota((256, LANES), 0), iota((256, LANES), 1)
        for half in range(2):
            for place in range(3):
                hit = (
                    ((tap & 15) == (pix & 15))
                    & ((tap >> 6) == (pix >> 6) + 2 * half)
                    & (((tap >> 4) & 3) == ((pix >> 4) & 3) + 2 - 2 * place)
                )
                at = (half * 3 + place) * k2
                taps = dot(w2t[...], hit.astype(F32).astype(BF16))
                band2[at : at + k2, :] = taps.astype(BF16)
        bias1[...] = jnp.broadcast_to(column(table[AT_B1, 0:k1]), bias1.shape)
        bias2[...] = jnp.broadcast_to(column(table[AT_B2, 0:k2]), bias2.shape)
        held[...] = jnp.zeros_like(held)
        held2[...] = jnp.zeros_like(held2)
        h1[...] = jnp.zeros_like(h1)

    def added(sums, x, value):
        sums[x] = sums[x] + value if x in sums else value

    def second_rows(b):
        tiles = [
            h1[pl.ds(2 * b + 1, 2), 4 * j : 4 * j + 4].reshape(LANES, LANES)
            for j in range(side // 4)
        ]
        got = dot(band2[...], jnp.concatenate(tiles, axis=1))
        low, high = {}, {}
        for j in range(side // 4):
            for place in range(3):
                x = 2 * j - 1 + place
                if 0 <= x < inner:
                    span = slice(j * LANES, (j + 1) * LANES)
                    at = place * k2
                    added(low, x, got[at : at + k2, span])
                    added(high, x, got[two // 2 + at : two // 2 + at + k2, span])
        row = jnp.maximum(b - 1, 0) * row_len
        for x in range(inner):
            value, slope = soft(held2[x] + high[x] + bias2[...])
            held2[x] = low[x]
            at = pl.ds(pl.multiple_of(row + x * k2, k2), k2)
            h2[at, :] = value.astype(BF16)
            s2[at, :] = slope.astype(BF16)

    second_rows(jnp.maximum(g - 1, 0))

    last = dot(
        edge[...], jnp.concatenate([tile_rows(frames, r, tiles, TILE) for r in range(STEP)], axis=1)
    )
    odd = {}
    for r in range(STEP):
        low, high = {}, {}

        def place_tile(j, got):
            for place in range(REACH):
                x = 4 * j - 1 + place
                if 0 <= x < side:
                    at = place * k1
                    added(low, x, got[at : at + k1])
                    added(high, x, got[reach_rows + at : reach_rows + at + k1])

        if r not in odd:
            rows = [k for k in (r, r + 1) if k < STEP]
            cut = [tile_rows(frames, k, tiles - 1, TILE) for k in rows]
            got = dot(band[...], jnp.concatenate(cut, axis=1))
            odd.update({k: got[:, i * LANES : (i + 1) * LANES] for i, k in enumerate(rows)})
        place_tile(tiles - 1, odd[r])
        added(low, side - 1, last[:k1, r * LANES : (r + 1) * LANES])
        added(high, side - 1, last[k1:, r * LANES : (r + 1) * LANES])
        done = 0
        for j in range(0, tiles - 1, 2):
            cut = [tile_rows(frames, r, j + k, TILE) for k in range(2)]
            got = dot(band[...], jnp.concatenate(cut, axis=1))
            for k in range(2):
                place_tile(j + k, got[:, k * LANES : (k + 1) * LANES])
            ready = side if j + 2 == tiles - 1 else 4 * j + 7
            for x in range(done, ready):
                value, slope = soft(held[x] + high[x] + bias1[...])
                held[x] = low[x]
                value = value.astype(BF16)
                h1[STEP * g + r, x] = value
                h1_out[r, x] = value
                s1[r, x] = slope.astype(BF16)
            done = ready

    @pl.when(g == pl.num_programs(0) - 1)
    def _():
        for b in range(h1.shape[0] // STEP - 1, side // 2):
            second_rows(b)
        value, slope = soft(dot_rows(lw[...], h2[...]) + column(table[AT_LB, :]))
        enc[...] = value.astype(BF16)
        s3[...] = slope


def three_parts(row):
    high = row.astype(BF16).astype(F32)
    middle = (row - high).astype(BF16).astype(F32)
    return jnp.concatenate([high, middle, row - high - middle], axis=0)


def with_ones(value):
    return jnp.concatenate([value, ones_rows(value.shape[1])], axis=0)


def ones_rows(lanes):
    return (iota((16, lanes), 0) < 3).astype(F32).astype(BF16)


def plan_kernel(
    section,
    slots,
    enc,
    s3,
    h2,
    branch_w,
    value_w,
    table,
    keep,
    send,
    small,
    g3,
    parts,
    bwt,
    vht,
    vhw,
    ow,
    mine,
    pre,
    dbr,
    dval,
    low,
    hid,
    gb,
    h2_here,
    sem,
    *,
    per_pair,
    depth,
):
    width = enc.shape[0]
    options = branch_w.shape[0]
    pairs = options // 2
    two = 2 * width
    sec = section[0]
    h2_copy = pltpu.make_async_copy(h2, h2_here, sem)
    h2_copy.start()

    count = slots.shape[0]
    dest = jnp.concatenate(
        [table[AT_DEST + k : AT_DEST + k + 1, :] for k in range(count // LANES)], axis=1
    )
    own = jnp.where(sec == 0, dest[:, :LANES], dest[:, LANES:])
    others = jnp.transpose(jnp.broadcast_to(dest, (LANES, count)))
    index = iota((count, LANES), 1) + sec * LANES
    earlier = (others == own) & (iota((count, LANES), 0) < index)
    rank = jnp.sum(earlier.astype(F32), axis=0, keepdims=True)
    bucket = own * float(per_pair) + rank
    chosen = (iota((count, LANES), 0).astype(F32) == bucket).astype(F32)
    mine[...] = dot_rows(slots[...], chosen, EXACT)[: mine.shape[0]]

    pad = jnp.zeros((13, width), F32)
    for o in range(options):
        rows = [branch_w[o].astype(F32), three_parts(table[o : o + 1, :]), pad]
        bwt[o * width : (o + 1) * width, :] = jnp.transpose(
            jnp.concatenate(rows, axis=0)
        ).astype(BF16)
    scalars = table[AT_SCALARS, :]
    head_w = table[AT_HW, :]
    rows = [value_w[...].astype(F32), three_parts(table[AT_VB, :]), pad]
    vht[0:width, :] = jnp.transpose(jnp.concatenate(rows, axis=0)).astype(BF16)
    vht[width:, :] = jnp.zeros((16, width + 16), BF16)
    lane = iota((1, 16), 1)
    for k in range(2):
        bias = three_parts(jnp.broadcast_to(scalars[:, 1 + k : 2 + k], (1, 16)))
        bias = sum(jnp.where(lane == j, bias[j : j + 1], 0.0) for j in range(3))
        vht[width + k : width + k + 1, 0:width] = head_w[k : k + 1].astype(BF16)
        vht[width + k : width + k + 1, width:] = bias.astype(BF16)
    vhw[:, 0:width] = value_w[...]
    vhw[:, width:] = jnp.transpose(
        jnp.concatenate([head_w, jnp.zeros((14, width), F32)], axis=0)
    ).astype(BF16)
    ow[...] = jnp.broadcast_to(column(table[AT_OW, :]), (width, LANES))
    wide_ow = jnp.concatenate([ow[...], ow[...]], axis=1)

    labels = iota((options, LANES), 0).astype(F32)
    state = enc[...].astype(F32)
    rounded_all, saved = [], []
    for level in range(depth):
        picked = labels == mine[level : level + 1, :]
        rounded = state.astype(BF16)
        rounded_all.append(rounded)
        pre[...] = dot(bwt[...], with_ones(rounded))
        following = state
        reward, discount, value = [], [], []
        for t in range(pairs):
            at = slice(t * two, (t + 1) * two)
            act, slope = silu_pair(pre[at, :])
            dbr[level, at, :] = slope
            left = state + act[:width]
            right = state + act[width:]
            following = jnp.where(picked[2 * t : 2 * t + 1], left, following)
            following = jnp.where(picked[2 * t + 1 : 2 * t + 2], right, following)
            both = with_ones(jnp.concatenate([left.astype(BF16), right.astype(BF16)], axis=1))
            low[level, t] = both
            got = dot(vht[...], both)
            act, slope = silu_pair(got[:width])
            dval[level, t] = slope
            hidden = act.astype(BF16)
            hid[level, t] = hidden
            worth = jnp.sum(hidden.astype(F32) * wide_ow, axis=0, keepdims=True)
            for k in range(2):
                span = slice(k * LANES, (k + 1) * LANES)
                value.append(worth[:, span])
                reward.append(got[width : width + 1, span])
                discount.append(got[width + 1 : width + 2, span])
        reward = jnp.concatenate(reward, axis=0)
        discount = jax.nn.sigmoid(jnp.concatenate(discount, axis=0))
        value = jnp.concatenate(value, axis=0) + scalars[:, 3:4]
        quality = reward + discount * value
        top = jnp.max(quality, axis=0, keepdims=True)
        shifted = jnp.exp(quality - top)
        total = jnp.sum(shifted, axis=0, keepdims=True)
        live = (mine[depth : depth + 1, :] > level).astype(F32)
        chosen = picked.astype(F32)

        def target(kind):
            at = depth + 1 + kind * depth + level
            return mine[at : at + 1, :]

        reward_gap = live * (jnp.sum(chosen * reward, axis=0, keepdims=True) - target(0))
        discount_gap = live * (jnp.sum(chosen * discount, axis=0, keepdims=True) - target(1))
        plan_gap = live * (top + jnp.log(total) - target(2))
        grad_quality = plan_gap * (shifted / total)
        head_two = (chosen * discount_gap + grad_quality * value) * discount * (1.0 - discount)
        saved.append(
            (
                picked,
                (chosen * reward_gap + grad_quality).astype(BF16).astype(F32),
                head_two.astype(BF16).astype(F32),
                (grad_quality * discount).astype(BF16).astype(F32),
                reward_gap * reward_gap + discount_gap * discount_gap + plan_gap * plan_gap,
            )
        )
        state = following

    out_sum = jnp.zeros((width, two), F32)
    value_sum = jnp.zeros((width + 16, width + 16), F32)
    grad_next = jnp.zeros((width, LANES), F32)
    line = iota((16, two), 0)
    for level in reversed(range(depth)):
        picked, head_one, head_two, grad_value, _ = saved[level]
        upward = jnp.zeros((width, LANES), F32)
        for t in range(pairs):
            at = slice(t * two, (t + 1) * two)

            def across(rows):
                return jnp.concatenate(
                    [rows[2 * t : 2 * t + 1], rows[2 * t + 1 : 2 * t + 2]], axis=1
                )

            worth = across(grad_value)
            grad_pre = (worth * wide_ow * dval[level, t]).astype(BF16)
            out_sum = out_sum + hid[level, t].astype(F32) * worth
            heads = jnp.where(line == 0, across(head_one), 0.0)
            heads = jnp.where(line == 1, across(head_two), heads)
            heads = jnp.where(line == 2, worth, heads)
            stacked = jnp.concatenate([grad_pre, heads.astype(BF16)], axis=0)
            value_sum = value_sum + dot_lanes(stacked, low[level, t])
            moved = dot(vhw[...], stacked)
            left = moved[:, :LANES] + jnp.where(picked[2 * t : 2 * t + 1], grad_next, 0.0)
            right = moved[:, LANES:] + jnp.where(picked[2 * t + 1 : 2 * t + 2], grad_next, 0.0)
            grad_branch = jnp.concatenate([left, right], axis=0) * dbr[level, at, :]
            grad_branch = grad_branch.astype(BF16)
            gb[level, at, :] = grad_branch
            weights = jnp.concatenate([branch_w[2 * t], branch_w[2 * t + 1]], axis=1)
            upward = upward + (left + right + dot(weights, grad_branch))
        grad_next = upward

    linear_rows = h2.shape[0]
    half = (linear_rows + options * width + width) // 2
    rest = linear_rows - half
    rounded = with_ones(jnp.concatenate(rounded_all, axis=1))
    small[...] = jnp.zeros_like(small)
    if half < keep.shape[0]:
        for k in range(2):
            parts[k, half:, :] = jnp.zeros((keep.shape[0] - half, LANES), BF16)
    for t in range(pairs):
        at = slice(t * two, (t + 1) * two)
        grads = jnp.concatenate([gb[level, at, :] for level in range(depth)], axis=1)
        got = dot_lanes(rounded, grads)
        for k in range(2):
            o = 2 * t + k
            span = slice(k * width, (k + 1) * width)
            rows = slice(rest + o * width, rest + (o + 1) * width)
            parts[1 - sec, rows, :] = got[:width, span].astype(BF16)
            small[o : o + 1, :] = got[width : width + 1, span]
    after = rest + options * width
    parts[1 - sec, after : after + width, :] = jnp.transpose(value_sum[:width, :width]).astype(BF16)

    grad_three = (grad_next.astype(BF16).astype(F32) * s3[...]).astype(BF16)
    g3[...] = grad_three
    h2_copy.wait()
    chunk = linear_rows // 9
    for i in range(8):
        at = slice(i * chunk, (i + 1) * chunk)
        parts[sec, at, :] = dot_lanes(h2_here[at, :], grad_three).astype(BF16)
    last = dot_lanes(h2_here[8 * chunk :, :], grad_three).astype(BF16)
    parts[sec, 8 * chunk : half, :] = last[: half - 8 * chunk]
    parts[1 - sec, 0:rest, :] = last[half - 8 * chunk :]
    keep[...] = parts[0]
    send[...] = parts[1]

    small[AT_VB, :] = row_of(value_sum[:width, width : width + 1])
    small[AT_OW, :] = row_of(jnp.sum(out_sum, axis=1, keepdims=True))
    small[AT_HW, :] = value_sum[width : width + 2, :width]
    small[AT_LB, :] = row_of(jnp.sum(grad_three.astype(F32), axis=1, keepdims=True))
    loss = 0.5 * jnp.sum(sum(kept[4] for kept in saved), axis=1, keepdims=True)
    ends = [loss] + [value_sum[width + k : width + k + 1, width : width + 1] for k in range(3)]
    lane = iota((1, LANES), 1)
    line = jnp.zeros((1, LANES), F32)
    for k, end in enumerate(ends):
        line = jnp.where(lane == k, end, line)
    small[AT_SCALARS, :] = line


def back_kernel(g3, lw, s2_far, s1_far, h1_far, w2t, g1, c2, sums, t2, g2, s2, s1, h1, sems):
    side, k1 = s1.shape[1], s1.shape[2]
    k2 = w2t.shape[0]
    inner = side // 2 - 1
    row_len = inner * k2
    copies = [
        pltpu.make_async_copy(s2_far, s2, sems.at[0]),
        pltpu.make_async_copy(s1_far, s1, sems.at[1]),
        pltpu.make_async_copy(h1_far, h1, sems.at[2]),
    ]
    for copy in copies:
        copy.start()
    tap, pix = iota((LANES, 256), 1), iota((LANES, 256), 0)
    for yrel in range(2):
        for p in range(3):
            hit = (
                ((tap & 15) == (pix & 15))
                & ((tap >> 6) == (pix >> 6) + 2 * (1 - yrel))
                & (((tap >> 4) & 3) == ((pix >> 4) & 3) + 2 - 2 * p)
            )
            at = (yrel * 3 + p) * k2
            t2[:, at : at + k2] = dot_lanes(hit.astype(F32).astype(BF16), w2t[...]).astype(BF16)
    g2[0] = jnp.zeros(g2.shape[1:], BF16)
    g2[inner + 1] = jnp.zeros(g2.shape[1:], BF16)
    g1[0] = jnp.zeros(g1.shape[1:], BF16)
    g1[side + 1] = jnp.zeros(g1.shape[1:], BF16)
    zero = jnp.zeros((k2, LANES), BF16)
    total_one = jnp.zeros((k1, LANES), F32)
    total_two = jnp.zeros((k2, LANES), F32)
    copies[0].wait()
    for y in range(inner):
        at = slice(y * row_len, (y + 1) * row_len)
        grad = dot(lw[at, :], g3[...]) * s2[at, :].astype(F32)
        grad = grad.astype(BF16).reshape(inner, k2, LANES)
        g2[y + 1] = grad
        total_two = total_two + jnp.sum(grad.astype(F32), axis=0)
    for copy in copies[1:]:
        copy.wait()
    total = jnp.zeros(c2.shape, F32)
    for b in range(side // 2):
        cut = []
        for j in range(side // 4):
            pieces = []
            for yrel in range(2):
                for p in range(3):
                    x = 2 * j - 1 + p
                    pieces.append(g2[b + yrel, x] if 0 <= x < inner else zero)
            cut.append(jnp.concatenate(pieces, axis=0))
        got = dot(t2[...], jnp.concatenate(cut, axis=1))
        for u in range(2):
            for j in range(side // 4):
                part = got[u * 64 : (u + 1) * 64, j * LANES : (j + 1) * LANES]
                slope = s1[2 * b + u + 1, 4 * j : 4 * j + 4].astype(F32)
                grad = (part.reshape(4, k1, LANES) * slope).astype(BF16)
                g1[2 * b + u + 1, 4 * j : 4 * j + 4] = grad
                total_one = total_one + jnp.sum(grad.astype(F32), axis=0)
        if b < inner:
            grads = jnp.concatenate([g2[b + 1, x] for x in range(inner)], axis=1)
            patches = [
                h1[2 * b + 1 : 2 * b + 5, 2 * x : 2 * x + 4].reshape(256, LANES)
                for x in range(inner)
            ]
            total = total + dot_lanes(grads, jnp.concatenate(patches, axis=1))
    c2[...] = total
    sums[...] = jnp.zeros_like(sums)
    sums[0:1, 0:k1] = row_of(jnp.sum(total_one, axis=1, keepdims=True))
    sums[1:2, 0:k2] = row_of(jnp.sum(total_two, axis=1, keepdims=True))


def pixel_band(sec, w1t, channels):
    k1 = w1t.shape[0]
    rows = 64 * channels
    row, tap = iota((rows, 256), 0), iota((rows, 256), 1)
    moves = ((tap >> 6) == row % channels + sec * channels) & ((tap & 63) == row // channels)
    taps = dot_lanes(moves.astype(F32).astype(BF16), w1t)
    line, span = COLS * channels, 8 * channels
    blocks = {}
    for half in range(2):
        for p in range(NEAR):
            pieces = []
            for u in range(4):
                at = (4 * half + u) * span
                start = 4 * (p - 1) * channels
                cut = taps[at + max(0, -start) : at + min(span, line - start)]
                start = max(start, 0)
                pieces += [jnp.zeros((start, k1), F32)] if start else []
                pieces.append(cut)
                rest = line - start - cut.shape[0]
                pieces += [jnp.zeros((rest, k1), F32)] if rest else []
            blocks[half, p] = jnp.concatenate(pieces, axis=0)
    zero = jnp.zeros((4 * line, k1), F32)
    lines = []
    for r in range(STEP):
        cols = [
            blocks.get((r + 1 - yrel, p), zero) for yrel in range(STEP + 1) for p in range(NEAR)
        ]
        lines.append(jnp.concatenate(cols, axis=1))
    return jnp.concatenate(lines, axis=0).astype(BF16)


def first_kernel(section, *refs):
    frames = refs[:PARTS]
    g1, after, c1, acc = refs[PARTS:]
    g = pl.program_id(0)
    side, k1 = g1.shape[1], g1.shape[2]
    img, channels = frames[0].shape[1], frames[0].shape[2]

    @pl.when(g == 0)
    def _():
        acc[...] = jnp.zeros_like(acc)

    zero = jnp.zeros((k1, LANES), BF16)
    pixels, grads = [], []
    for j in range(img // COLS):
        pixels.append(
            jnp.concatenate([tile_rows(frames, r, j, COLS) for r in range(STEP)], axis=0)
        )
        pieces = []
        for yrel in range(STEP + 1):
            for p in range(NEAR):
                x = 3 * j - 1 + p
                pieces.append(g1[yrel, x] if 0 <= x < side else zero)
        grads.append(jnp.concatenate(pieces, axis=0))
    acc[...] += dot_lanes(jnp.concatenate(pixels, axis=1), jnp.concatenate(grads, axis=1))

    @pl.when(g == pl.num_programs(0) - 1)
    def _():
        line = COLS * channels
        step = 4 * channels
        taps = []
        for half in range(2):
            total = sum(
                acc[r * 4 * line : (r + 1) * 4 * line, :][
                    :, (r + 1 - half) * NEAR * k1 : (r + 2 - half) * NEAR * k1
                ]
                for r in range(STEP)
            )
            for u in range(4):
                part = total[u * line : (u + 1) * line]
                cols = [part[:, p * k1 : (p + 1) * k1] for p in range(NEAR)]
                taps.append(cols[1][0:step] + cols[2][step : 2 * step] + cols[3][2 * step :])
                taps.append(cols[0][0:step] + cols[1][step : 2 * step] + cols[2][2 * step :])
        row, col = iota((256, 256), 0), iota((256, 256), 1)
        moves = ((row & 3) == (col >> 6)) & ((row >> 2) == (col & 63))
        grad = dot_rows(jnp.concatenate(taps, axis=0), moves.astype(F32), EXACT)
        for half in range(2):
            c1[half * k1 : (half + 1) * k1, :] = grad[:, half * LANES : (half + 1) * LANES].astype(
                BF16
            )


def pixels_kernel(section, weights, mine, other, after, *refs, start, begins):
    out, token, band_out, band, held, sems = refs[-6:]
    g = pl.program_id(0)
    steps = pl.num_programs(0)
    side, k1 = mine.shape[1], mine.shape[2]
    img, channels = out.shape[1], out.shape[2]
    sec = section[0]
    line = COLS * channels
    flat = held.reshape(2, 2, 4 * STEP, img * channels, LANES)
    slot = g % 2

    def writes(step, at, cols):
        rows = pl.ds(pl.multiple_of(4 * STEP * (start + step), 4), 4 * STEP)
        places = (sec * LANES, (1 - sec) * LANES)
        return [
            pltpu.make_async_copy(
                held.at[at, k, :, cols],
                out.at[rows, cols, :, pl.ds(pl.multiple_of(places[k], LANES), LANES)],
                sems.at[at, k],
            )
            for k in range(2)
        ]

    @pl.when(g == 0)
    def _():
        if begins:
            band[...] = pixel_band(sec, weights[...], channels)
            band_out[...] = band[...]
        else:
            band[...] = weights[...]
            band_out[...] = jnp.zeros_like(band_out)

    everything = pl.ds(0, img)

    @pl.when(g >= 2)
    def _():
        for copy in writes(g - 2, slot, everything):
            copy.wait()

    zero = jnp.zeros((k1, 2 * LANES), BF16)
    for j in range(img // COLS):
        pieces = []
        for yrel in range(STEP + 1):
            for p in range(NEAR):
                x = 3 * j - 1 + p
                if 0 <= x < side:
                    pieces.append(jnp.concatenate([mine[yrel, x], other[yrel, x]], axis=1))
                else:
                    pieces.append(zero)
        got = dot(band[...], jnp.concatenate(pieces, axis=0))
        for k in range(4 * STEP):
            at = slice(k * line, (k + 1) * line)
            span = slice(j * line, (j + 1) * line)
            flat[slot, 0, k, span, :] = got[at, :LANES]
            flat[slot, 1, k, span, :] = got[at, LANES:]
        for copy in writes(g, slot, pl.ds(j * COLS, COLS)):
            copy.start()
    token[...] = jnp.zeros_like(token)

    @pl.when(g == steps - 1)
    def _():
        @pl.when(g >= 1)
        def _():
            for copy in writes(g - 1, 1 - slot, everything):
                copy.wait()

        for copy in writes(g, slot, everything):
            copy.wait()


def two_parts(value):
    high = value.astype(BF16).astype(F32)
    return jnp.concatenate([high, value - high], axis=0).astype(BF16)


def one_part(pair):
    rows = pair.shape[0] // 2
    pair = pair.astype(F32)
    return pair[:rows] + pair[rows:]


def merge_kernel(section, batch, keep, recv, small, c2, sums, *rest):
    outs, lines = rest[:-1], rest[-1]
    me = batch[0] % PLANE
    short = lines.shape[0] // PLANE
    size = keep.shape[0] // PLANE
    k2 = c2.shape[0]
    lines[...] = jnp.zeros_like(lines)
    at = small.shape[0]
    lines[0:at, :] = small[...]
    for half in range(2):
        lines[at : at + k2, :] = c2[:, half * LANES : (half + 1) * LANES]
        at += k2
    lines[at : at + sums.shape[0], :] = sums[...]
    for k, out in enumerate(outs):
        whose = me ^ k
        at = pl.ds(pl.multiple_of(whose * size, size), size)
        out[0:size, :] = (keep[at, :].astype(F32) + recv[at, :].astype(F32)).astype(BF16)
        out[size:, :] = two_parts(lines[pl.ds(pl.multiple_of(whose * short, short), short), :])


def plane_kernel(section, batch, *refs):
    parts, c1 = refs[:PLANE], refs[PLANE]
    keep, send, total, lines = refs[PLANE + 1 :]
    size, short = total.shape[0], lines.shape[0]
    total[...] = sum(p[0:size, :].astype(F32) for p in parts).astype(BF16)
    lines[...] = sum(one_part(p[size:, :]) for p in parts)
    mine = (batch[0] // PLANE) % 2
    for out, half in ((keep, mine), (send, 1 - mine)):
        at = 0
        for ref, count in ((total, size // 2), (lines, short // 2), (c1, c1.shape[0] // 2)):
            part = ref[pl.ds(pl.multiple_of(half * count, count), count), :]
            part = two_parts(part) if ref is lines else part
            out[at : at + part.shape[0], :] = part
            at += part.shape[0]


def added(a, b, short):
    fine = a.shape[0] - 16 - 2 * short
    spans = (slice(0, fine), slice(fine, fine + 2 * short), slice(fine + 2 * short, None))
    big, last = ((a[k, :].astype(F32) + b[k, :].astype(F32)).astype(BF16) for k in spans[::2])
    middle = two_parts(one_part(a[spans[1], :]) + one_part(b[spans[1], :]))
    return jnp.concatenate([big, middle, last], axis=0)


def add_kernel(a, b, after, out, *, short):
    out[...] = added(a[...], b[...], short)


def join_kernel(section, batch, a, b, out):
    mine = (batch[0] // PLANE) % 2
    out[mine] = a[...]
    out[1 - mine] = b[...]


def relay_kernel(section, batch, *refs):
    parts, out = refs[:PLANE], refs[-1]
    me = batch[0] % PLANE
    for k, part in enumerate(parts):
        out[me ^ k] = part[...]


def unpack_kernel(section, mine, other, *refs):
    loss, c1, b1, c2, b2, lw, lb, bw, bb, hw, hb, vw, vb, ow, ob, halves, lines = refs
    width = lw.shape[1]
    options = bw.shape[0]
    k1, k2 = c1.shape[0], c2.shape[0]
    linear_rows = lw.shape[0]
    sec = section[0]
    size = halves.shape[1] // (2 * PLANE)
    short = lines.shape[0] // (2 * PLANE)
    half = (linear_rows + options * width + width) // 2
    rest = linear_rows - half
    grad = [jnp.zeros((k1, LANES), F32) for _ in range(2)]
    for k in range(PLANE):
        for h in range(2):
            at = (2 * k + h) * size
            halves[sec, at : at + size, :] = mine[k, h, 0:size, :]
            halves[1 - sec, at : at + size, :] = other[k, h, 0:size, :]
            pair = slice(size, size + 2 * short)
            at = (2 * k + h) * short
            lines[at : at + short, :] = one_part(mine[k, h, pair, :]) + one_part(
                other[k, h, pair, :]
            )
            for ref in (mine, other):
                grad[h] += ref[k, h, size + 2 * short :, :].astype(F32)
    for part in range(2):
        c1[:, part * LANES : (part + 1) * LANES] = grad[part]
    lw[0:half, :] = halves[0, 0:half, :].astype(F32)
    lw[half:, :] = halves[1, 0:rest, :].astype(F32)
    for o in range(options):
        at = rest + o * width
        bw[o] = halves[1, at : at + width, :].astype(F32)
    at = rest + options * width
    vw[...] = halves[1, at : at + width, :].astype(F32)
    bb[...] = lines[0:options, :]
    vb[...] = lines[AT_VB, :]
    ow[...] = lines[AT_OW, :]
    hw[...] = lines[AT_HW, :]
    lb[...] = lines[AT_LB, :]
    scalars = lines[AT_SCALARS, :]
    loss[...] = scalars[:, 0:1]
    hb[...] = scalars[:, 1:3]
    ob[...] = scalars[:, 3:4]
    at = TABLE
    for part in range(2):
        c2[:, part * LANES : (part + 1) * LANES] = lines[at : at + k2, :]
        at += k2
    b1[...] = lines[at : at + 1, 0:k1]
    b2[...] = lines[at + 1 : at + 2, 0:k2]


def numbers_kernel(
    options,
    depth,
    targets,
    destination,
    b1,
    b2,
    lb,
    bb,
    hw,
    vb,
    ow,
    hb,
    ob,
    out,
    table,
):
    levels, kinds = options.shape[0], targets.shape[0]
    slots = depth.shape[1]
    rows = [options[...].astype(F32), depth[...].astype(F32)]
    rows += [targets[k] for k in range(kinds)]
    rows.append(jnp.zeros((LANES - levels - 1 - kinds * levels, slots), F32))
    out[...] = jnp.transpose(jnp.concatenate(rows, axis=0))
    table[...] = jnp.zeros_like(table)
    table[0 : bb.shape[0], :] = bb[...]
    table[AT_VB, :] = vb[...]
    table[AT_OW, :] = ow[...].astype(F32)
    table[AT_HW, :] = hw[...].astype(F32)
    table[AT_LB, :] = lb[...]
    table[AT_B1, 0 : b1.shape[1]] = b1[...]
    table[AT_B2, 0 : b2.shape[1]] = b2[...]
    lane = iota((1, LANES), 1)
    scalars = jnp.zeros((1, LANES), F32)
    for k, value in ((1, hb[:, 0:1]), (2, hb[:, 1:2]), (3, ob[...])):
        scalars = jnp.where(lane == k, value, scalars)
    table[AT_SCALARS, :] = scalars
    for k in range(slots // LANES):
        part = destination[:, k * LANES : (k + 1) * LANES]
        table[AT_DEST + k : AT_DEST + k + 1, :] = part.astype(F32)


def whole(shape):
    zeros = (0,) * len(shape)
    return pl.BlockSpec(shape, lambda *_: zeros)


def params():
    return pltpu.CompilerParams(vmem_limit_bytes=VMEM_BYTES)


def shape_of(*shape, dtype=F32):
    return jax.ShapeDtypeStruct(shape, dtype)


def cost(microseconds):
    return pl.CostEstimate(
        flops=int(1.1e9 * microseconds), bytes_accessed=int(3.6e6 * microseconds), transcendentals=0
    )


def stays(value):
    return pltpu.with_memory_space_constraint(value, pltpu.HBM)


def frame_blocks(frames):
    _, img, stack, _ = frames.shape
    block = (4 * STEP // PARTS, img, stack, LANES)

    def spec(k):
        return pl.BlockSpec(block, lambda g, s: (PARTS * g + k, 0, 0, s[0]))

    return [spec(k) for k in range(PARTS)]


def encode(section, frames, w1t, w2t, lw, table):
    img = frames.shape[0]
    blocks = img // 4
    side = blocks - 1
    k1, k2, width = w1t.shape[0], w2t.shape[0], lw.shape[1]
    flat = lw.shape[0]
    outs = (
        pltpu.HBM((blocks, side, k1, LANES), BF16),
        pltpu.HBM((blocks, side, k1, LANES), BF16),
        pltpu.HBM((flat, LANES), BF16),
        pltpu.HBM((flat, LANES), BF16),
        shape_of(width, LANES, dtype=BF16),
        shape_of(width, LANES),
    )
    weights = (w1t, w2t, lw, table)
    out_specs = [whole(o.shape) for o in outs]
    for k in range(2):
        out_specs[k] = pl.BlockSpec((STEP, side, k1, LANES), lambda g, s: (g, 0, 0, 0))
    return pl.pallas_call(
        encode_kernel,
        grid_spec=pltpu.PrefetchScalarGridSpec(
            num_scalar_prefetch=1,
            grid=(blocks // STEP,),
            in_specs=[*frame_blocks(frames), *[whole(w.shape) for w in weights]],
            out_specs=out_specs,
            scratch_shapes=[
                pltpu.VMEM((2 * REACH * k1, 256), BF16),
                pltpu.VMEM((2 * k1, 64), BF16),
                pltpu.VMEM((6 * k2, LANES), BF16),
                pltpu.VMEM((k1, LANES), F32),
                pltpu.VMEM((k2, LANES), F32),
                pltpu.VMEM((side, k1, LANES), F32),
                pltpu.VMEM((side // 2 - 1, k2, LANES), F32),
                pltpu.VMEM((blocks, side, k1, LANES), BF16),
            ],
        ),
        out_shape=outs,
        compiler_params=params(),
        cost_estimate=cost(9),
        name="encode",
    )(section, *[frames] * PARTS, *weights)


def plan(section, slots, enc, s3, h2, branch_w, value_w, table, per_pair, depth, half_rows):
    width = enc.shape[0]
    options = branch_w.shape[0]
    two = 2 * width
    pairs = options // 2
    outs = (
        shape_of(half_rows, LANES, dtype=BF16),
        shape_of(half_rows, LANES, dtype=BF16),
        shape_of(TABLE, LANES),
        shape_of(width, LANES, dtype=BF16),
    )
    operands = (slots, enc, s3, h2, branch_w, value_w, table)
    specs = [whole(o.shape) for o in operands]
    specs[3] = ANYWHERE
    vmem = pltpu.VMEM
    return pl.pallas_call(
        functools.partial(plan_kernel, per_pair=per_pair, depth=depth),
        grid_spec=pltpu.PrefetchScalarGridSpec(
            num_scalar_prefetch=1,
            grid=(1,),
            in_specs=specs,
            out_specs=[whole(o.shape) for o in outs],
            scratch_shapes=[
                vmem((2, half_rows, LANES), BF16),
                vmem((options * width, width + 16), BF16),
                vmem((width + 16, width + 16), BF16),
                vmem((width, width + 16), BF16),
                vmem((width, LANES), F32),
                vmem((16, LANES), F32),
                vmem((options * width, LANES), F32),
                vmem((depth, options * width, LANES), F32),
                vmem((depth, pairs, width, two), F32),
                vmem((depth, pairs, width + 16, two), BF16),
                vmem((depth, pairs, width, two), BF16),
                vmem((depth, options * width, LANES), BF16),
                vmem(h2.shape, BF16),
                pltpu.SemaphoreType.DMA,
            ],
        ),
        out_shape=outs,
        compiler_params=params(),
        cost_estimate=cost(13),
        name="plan",
    )(section, *operands)


def back(g3, lw, s2, s1, h1, w2t):
    _, side, k1 = s1.shape[:3]
    k2 = w2t.shape[0]
    inner = side // 2 - 1
    outs = (
        shape_of(side + 2, side, k1, LANES, dtype=BF16),
        shape_of(k2, 256),
        shape_of(8, LANES),
    )
    near = pl.BlockSpec(memory_space=pltpu.VMEM)
    return pl.pallas_call(
        back_kernel,
        in_specs=[near, near, ANYWHERE, ANYWHERE, ANYWHERE, near],
        out_shape=outs,
        scratch_shapes=[
            pltpu.VMEM((LANES, 6 * k2), BF16),
            pltpu.VMEM((inner + 2, inner, k2, LANES), BF16),
            pltpu.VMEM(s2.shape, BF16),
            pltpu.VMEM(s1.shape, BF16),
            pltpu.VMEM(h1.shape, BF16),
            pltpu.SemaphoreType.DMA((3,)),
        ],
        compiler_params=params(),
        cost_estimate=cost(5),
        name="back",
    )(g3, lw, s2, s1, h1, w2t)


ANYWHERE = pl.BlockSpec(memory_space=pl.ANY)


def row_window(g1, start=0):
    block = (pl.Element(STEP + 1),) + tuple(pl.Element(n) for n in g1.shape[1:])
    return pl.BlockSpec(block, lambda g, *_: (STEP * (start + g), 0, 0, 0))


def first(section, frames, g1, after):
    blocks = frames.shape[0] // 4
    k1 = g1.shape[2]
    return pl.pallas_call(
        first_kernel,
        grid_spec=pltpu.PrefetchScalarGridSpec(
            num_scalar_prefetch=1,
            grid=(blocks // STEP,),
            in_specs=[*frame_blocks(frames), row_window(g1), ANYWHERE],
            out_specs=whole((2 * k1, LANES)),
            scratch_shapes=[
                pltpu.VMEM(
                    (STEP * 4 * COLS * frames.shape[2], (STEP + 1) * NEAR * k1), F32
                ),
            ],
        ),
        out_shape=shape_of(2 * k1, LANES, dtype=BF16),
        compiler_params=params(),
        cost_estimate=cost(9),
        name="first",
    )(section, *[frames] * PARTS, g1, after)


def pixels(section, weights, mine, other, shape, start, steps, after, done=None):
    img, _, channels, _ = shape
    k1 = mine.shape[2]
    band = (STEP * 4 * COLS * channels, (STEP + 1) * NEAR * k1)
    operands = (weights, mine, other, after)
    specs = [whole(weights.shape), row_window(mine, start), row_window(other, start), ANYWHERE]
    aliases = {}
    if done is not None:
        operands += (done,)
        specs.append(ANYWHERE)
        aliases = {len(operands): 0}
    outs = [shape_of(*shape), shape_of(8, LANES), shape_of(*band, dtype=BF16)]
    return pl.pallas_call(
        functools.partial(pixels_kernel, start=start, begins=done is None),
        grid_spec=pltpu.PrefetchScalarGridSpec(
            num_scalar_prefetch=1,
            grid=(steps,),
            in_specs=specs,
            out_specs=[ANYWHERE] + [whole(o.shape) for o in outs[1:]],
            scratch_shapes=[
                pltpu.VMEM(band, BF16),
                pltpu.VMEM((2, 2, 4 * STEP, img, channels, LANES), F32),
                pltpu.SemaphoreType.DMA((2, 2)),
            ],
        ),
        out_shape=outs,
        input_output_aliases=aliases,
        compiler_params=params(),
        cost_estimate=cost(2 + 0.8 * steps),
        name="pixels",
    )(section, *operands)


def small_call(
    kernel, outs, operands, scratch=(), name=None, place=None, after=(), weight=0.3
):
    specs = [pl.BlockSpec(memory_space=pltpu.VMEM)] * len(operands)
    if place is not None:
        operands = (*place, *operands)
        specs = [pl.BlockSpec(memory_space=pltpu.SMEM)] * len(place) + specs
    return pl.pallas_call(
        kernel,
        in_specs=specs + [ANYWHERE] * len(after),
        out_shape=outs,
        scratch_shapes=list(scratch),
        compiler_params=params(),
        cost_estimate=cost(weight),
        name=name,
    )(*operands, *after)


def round_up(value, step):
    return -(-value // step) * step


def swapped(value):
    return lax.ppermute(value, "section", [(0, 1), (1, 0)])


def exchanged(value):
    return lax.all_to_all(value, "batch", split_axis=0, concat_axis=0, tiled=True)


def partner(value, distance):
    count = lax.axis_size("batch")
    return lax.ppermute(value, "batch", [(b, b ^ distance) for b in range(count)])


def local(
    frames,
    destination,
    options,
    depth,
    targets,
    conv_one,
    bias_one,
    conv_two,
    bias_two,
    linear_w,
    linear_b,
    branch_w,
    branch_b,
    head_w,
    head_b,
    value_w,
    value_b,
    out_w,
    out_b,
):
    section = lax.axis_index("section").astype(jnp.int32)[None]
    peers = lax.axis_size("batch")
    frame_count = frames.shape[3]
    per_pair = frame_count // peers
    levels = options.shape[0]
    frames = stays(frames.transpose(1, 2, 0, 3))
    w1t, w2t = stays(conv_one.T), stays(conv_two.T)
    linear_w, branch_w, value_w = stays(linear_w), stays(branch_w), stays(value_w)
    encoder_params = (w1t, bias_one, w2t, bias_two, linear_w, linear_b)
    planner_params = (branch_w, branch_b, head_w.T, head_b, value_w, value_b, out_w.T, out_b)
    width = linear_w.shape[1]
    big_rows = linear_w.shape[0] + (branch_w.shape[0] + 1) * width
    size = round_up(-(-big_rows // (2 * PLANE)), 32)

    tiny = (bias_one, bias_two, linear_b, branch_b, head_w.T, value_b, out_w.T)
    tiny = [stays(v if v.ndim > 1 else v[None, :]) for v in tiny]
    numbers, table = pl.pallas_call(
        numbers_kernel,
        in_specs=[pl.BlockSpec(memory_space=pltpu.VMEM)] * (6 + len(tiny)),
        out_shape=[shape_of(frame_count, LANES), shape_of(TABLE, LANES)],
        compiler_params=params(),
        cost_estimate=cost(1),
        name="numbers",
    )(
        stays(options),
        stays(depth[None, :]),
        stays(targets),
        stays(destination[None, :]),
        *tiny,
        stays(head_b[None, :]),
        out_b[None, :],
    )
    slots = exchanged(numbers.reshape(peers, per_pair, LANES)).reshape(frame_count, LANES)

    h1, s1, h2, s2, enc, s3 = encode(section, frames, w1t, w2t, linear_w, table)
    h1, s1, h2, s2 = (stays(v) for v in (h1, s1, h2, s2))
    keep, send, small, g3 = plan(
        section, slots, enc, s3, h2, branch_w, value_w, table, per_pair, levels, PLANE * size
    )
    recv = swapped(send)
    channels = frames.shape[2] // lax.axis_size("section")
    g1, c2, sums = back(g3, linear_w, s2, s1, h1, w2t)
    other = swapped(g1)
    place = (section, lax.axis_index("batch").astype(jnp.int32)[None])
    bf16 = functools.partial(shape_of, dtype=BF16)
    pieces = small_call(
        merge_kernel,
        [bf16(size + 2 * SHORT, LANES)] * PLANE,
        (keep, recv, small, c2, sums),
        [pltpu.VMEM((PLANE * SHORT, LANES), F32)],
        name="merge",
        place=place,
    )
    parts = [pieces[0]] + [partner(pieces[k], k) for k in range(1, PLANE)]
    c1 = first(section, frames, g1, pieces[0])
    half = bf16(size // 2 + SHORT + c1.shape[0] // 2, LANES)
    keep, send = small_call(
        plane_kernel,
        [half, half],
        (*parts, c1),
        [pltpu.VMEM((size, LANES), BF16), pltpu.VMEM((SHORT, LANES), F32)],
        name="plane",
        place=place,
    )
    img = frames.shape[0]
    draw = functools.partial(
        pixels, section, mine=g1, other=other, shape=(img, img, channels, 2 * LANES)
    )
    steps = img // 4 // STEP
    recv = partner(send, PLANE)
    frames_grad, token, band = draw(weights=w1t, start=0, steps=1, after=send)
    distance = PLANE
    while distance < peers:
        keep = small_call(
            functools.partial(add_kernel, short=SHORT // 2),
            half,
            (keep, recv),
            name="add",
            after=(token,),
        )
        distance *= 2
        if distance < peers:
            recv = partner(keep, distance)
        if distance == 2 * PLANE:
            frames_grad, token, _ = draw(
                weights=band, start=1, steps=1, after=keep, done=frames_grad
            )
    recv = partner(keep, PLANE)
    whole_piece = small_call(
        join_kernel, bf16(2, *half.shape), (keep, recv), name="join", place=place
    )
    parts = [whole_piece] + [partner(whole_piece, k) for k in range(1, PLANE)]
    frames_grad, token, _ = draw(
        weights=band, start=2, steps=steps - 2, after=whole_piece, done=frames_grad
    )
    got = small_call(
        relay_kernel,
        bf16(PLANE, 2, *half.shape),
        parts,
        name="relay",
        place=place,
        after=(token,),
    )
    shapes = [p.shape for p in encoder_params + planner_params]
    flat = [s if len(s) > 1 else (1,) + s for s in shapes]
    rest = small_call(
        unpack_kernel,
        [shape_of(1, 1)] + [shape_of(*s) for s in flat],
        (got, swapped(got)),
        [
            pltpu.VMEM((2, PLANE * size, LANES), BF16),
            pltpu.VMEM((PLANE * SHORT, LANES), F32),
        ],
        name="unpack",
        place=(section,),
    )
    rest = [v.reshape(s) for v, s in zip(rest, [()] + shapes)]
    for at in (1, 3, 9, 13):
        rest[at] = rest[at].T
    return (rest[0], frames_grad.transpose(2, 0, 1, 3), *rest[1:])


def solution(mesh):
    placed = (
        P(None, None, None, "batch"),
        P("batch"),
        P(None, "batch"),
        P("batch"),
        P(None, None, "batch"),
    ) + (P(),) * 14
    return jax.shard_map(
        local,
        mesh=mesh,
        in_specs=placed,
        out_specs=(P(), P("section", None, None, "batch")) + (P(),) * 14,
        check_vma=False,
    )
```

```python
import functools
import math

import jax
import jax.numpy as jnp
from jax import lax
from jax.experimental import pallas as pl
from jax.experimental.pallas import tpu as pltpu
from jax.sharding import PartitionSpec as P

BF16 = jnp.bfloat16
F32 = jnp.float32
EXACT = lax.Precision.HIGHEST
LANES = 128
VMEM_BYTES = 32 * 1024 * 1024
TILE = 16
REACH = 5
STEP = 3
COLS = 12
NEAR = 4
AT_VB, AT_OW, AT_HW, AT_LB, AT_SCALARS, AT_B1, AT_B2, AT_DEST = (
    slice(18, 19),
    slice(19, 20),
    slice(20, 22),
    slice(22, 23),
    slice(23, 24),
    slice(24, 25),
    slice(25, 26),
    26,
)
TABLE = 32
PLANE = 4
SHORT = 32


def dot(a, b, precision=None):
    return jnp.dot(a, b, preferred_element_type=F32, precision=precision)


def dot_rows(a, b, precision=None):
    return lax.dot_general(
        a, b, (((0,), (0,)), ((), ())), preferred_element_type=F32, precision=precision
    )


def dot_lanes(a, b, precision=None):
    return lax.dot_general(
        a, b, (((1,), (1,)), ((), ())), preferred_element_type=F32, precision=precision
    )


def iota(shape, axis):
    return lax.broadcasted_iota(jnp.int32, shape, axis)


def column(row):
    n = row.shape[1]
    wide = jnp.broadcast_to(row, (n, n))
    return jnp.sum(jnp.where(iota((n, n), 0) == iota((n, n), 1), wide, 0.0), axis=1, keepdims=True)


def row_of(col):
    n = col.shape[0]
    wide = jnp.broadcast_to(col, (n, n))
    return jnp.sum(jnp.where(iota((n, n), 0) == iota((n, n), 1), wide, 0.0), axis=0, keepdims=True)


def soft(x):
    t = jnp.tanh(0.5 * x)
    return jnp.maximum(x, 0.0) - jnp.log(0.5 + 0.5 * jnp.abs(t)), 0.5 + 0.5 * t


def silu_pair(x):
    s = 0.5 + 0.5 * jnp.tanh(0.5 * x)
    act = x * s
    return act, s + act * (1.0 - s)


def pixel_order(w1t):
    tap, pix = iota((256, 256), 0), iota((256, 256), 1)
    moves = ((tap >> 6) == (pix & 3)) & ((tap & 63) == (pix >> 2))
    return dot(w1t, moves.astype(F32).astype(BF16))


def frame_copies(section, far, here, sems):
    lanes = pl.ds(pl.multiple_of(section[0] * LANES, LANES), LANES)
    size = 4 * STEP

    def copy(g):
        rows = pl.ds(pl.multiple_of(g * size, size), size)
        return pltpu.make_async_copy(far.at[rows, :, :, lanes], here.at[rows], sems.at[g])

    return copy


def tile_rows(frames, row, j, cols):
    img, _, channels, _ = frames.shape
    flat = frames.reshape(img, img * channels, LANES)
    size = cols * channels
    end = min((j + 1) * size, img * channels)
    part = flat[pl.ds(row, 4), j * size : end, :]
    return part.reshape(4 * (end - j * size), LANES)


def encode_kernel(
    section,
    frames_far,
    w1t,
    w2t,
    lw_far,
    table,
    h1_far,
    s1_far,
    h2_far,
    s2_far,
    enc,
    s3,
    frames,
    lw,
    h1,
    s1,
    h2,
    s2,
    band,
    edge,
    band2,
    bias1,
    bias2,
    held,
    held2,
    sems,
):
    blocks, side = h1.shape[:2]
    steps = blocks // STEP
    tiles = frames.shape[1] // TILE
    k1, k2 = w1t.shape[0], w2t.shape[0]
    reach_rows = REACH * k1
    arrives = frame_copies(section, frames_far, frames, sems.at[0])
    for g in range(steps):
        arrives(g).start()
    last_copies = [
        pltpu.make_async_copy(lw_far, lw, sems.at[3, 0]),
        pltpu.make_async_copy(h2, h2_far, sems.at[3, 1]),
        pltpu.make_async_copy(s2, s2_far, sems.at[3, 2]),
    ]
    last_copies[0].start()

    def leaves(g):
        rows = pl.ds(g * STEP, STEP)
        return [
            pltpu.make_async_copy(h1.at[rows], h1_far.at[rows], sems.at[1, g]),
            pltpu.make_async_copy(s1.at[rows], s1_far.at[rows], sems.at[2, g]),
        ]

    inner = side // 2 - 1
    row_len = inner * k2
    two = 2 * k2 * 3

    def prepare():
        taps = pixel_order(w1t[...])
        edges = []
        for half in range(2):
            lines = [taps[:, 32 * (4 * half + u) : 32 * (4 * half + u + 1)] for u in range(4)]
            for place in range(REACH):
                pieces = []
                for line in lines:
                    start = 16 * (place - 1)
                    cut = line[:, max(0, -start) : min(32, 64 - start)]
                    start = max(start, 0)
                    pieces += [jnp.zeros((k1, start), F32)] if start else []
                    pieces.append(cut)
                    rest = 64 - start - cut.shape[1]
                    pieces += [jnp.zeros((k1, rest), F32)] if rest else []
                at = half * reach_rows + place * k1
                band[at : at + k1, :] = jnp.concatenate(pieces, axis=1).astype(BF16)
            edges.append(jnp.concatenate([line[:, 16:] for line in lines], axis=1))
        edge[...] = jnp.concatenate(edges, axis=0).astype(BF16)
        tap, pix = iota((256, LANES), 0), iota((256, LANES), 1)
        for half in range(2):
            for place in range(3):
                hit = (
                    ((tap & 15) == (pix & 15))
                    & ((tap >> 6) == (pix >> 6) + 2 * half)
                    & (((tap >> 4) & 3) == ((pix >> 4) & 3) + 2 - 2 * place)
                )
                at = (half * 3 + place) * k2
                taps = dot(w2t[...], hit.astype(F32).astype(BF16))
                band2[at : at + k2, :] = taps.astype(BF16)
        bias1[...] = jnp.broadcast_to(column(table[AT_B1, 0:k1]), bias1.shape)
        bias2[...] = jnp.broadcast_to(column(table[AT_B2, 0:k2]), bias2.shape)
        held[...] = jnp.zeros_like(held)
        held2[...] = jnp.zeros_like(held2)
        h1[...] = jnp.zeros_like(h1)

    def added(sums, x, value):
        sums[x] = sums[x] + value if x in sums else value

    def second_rows(b):
        tiles = [
            h1[pl.ds(2 * b + 1, 2), 4 * j : 4 * j + 4].reshape(LANES, LANES)
            for j in range(side // 4)
        ]
        got = dot(band2[...], jnp.concatenate(tiles, axis=1))
        low, high = {}, {}
        for j in range(side // 4):
            for place in range(3):
                x = 2 * j - 1 + place
                if 0 <= x < inner:
                    span = slice(j * LANES, (j + 1) * LANES)
                    at = place * k2
                    added(low, x, got[at : at + k2, span])
                    added(high, x, got[two // 2 + at : two // 2 + at + k2, span])
        row = jnp.maximum(b - 1, 0) * row_len
        for x in range(inner):
            value, slope = soft(held2[x] + high[x] + bias2[...])
            held2[x] = low[x]
            at = pl.ds(pl.multiple_of(row + x * k2, k2), k2)
            h2[at, :] = value.astype(BF16)
            s2[at, :] = slope.astype(BF16)

    def one_step(g, carry):
        def row(r):
            return pl.multiple_of(4 * (STEP * g + r), 4)

        arrives(g).wait()
        second_rows(jnp.maximum(g - 1, 0))

        last = dot(
            edge[...], jnp.concatenate([tile_rows(frames, row(r), tiles, TILE) for r in range(STEP)], axis=1)
        )
        odd = {}
        for r in range(STEP):
            low, high = {}, {}

            def place_tile(j, got):
                for place in range(REACH):
                    x = 4 * j - 1 + place
                    if 0 <= x < side:
                        at = place * k1
                        added(low, x, got[at : at + k1])
                        added(high, x, got[reach_rows + at : reach_rows + at + k1])

            if r not in odd:
                rows = [k for k in (r, r + 1) if k < STEP]
                cut = [tile_rows(frames, row(k), tiles - 1, TILE) for k in rows]
                got = dot(band[...], jnp.concatenate(cut, axis=1))
                odd.update({k: got[:, i * LANES : (i + 1) * LANES] for i, k in enumerate(rows)})
            place_tile(tiles - 1, odd[r])
            added(low, side - 1, last[:k1, r * LANES : (r + 1) * LANES])
            added(high, side - 1, last[k1:, r * LANES : (r + 1) * LANES])
            done = 0
            for j in range(0, tiles - 1, 2):
                cut = [tile_rows(frames, row(r), j + k, TILE) for k in range(2)]
                got = dot(band[...], jnp.concatenate(cut, axis=1))
                for k in range(2):
                    place_tile(j + k, got[:, k * LANES : (k + 1) * LANES])
                ready = side if j + 2 == tiles - 1 else 4 * j + 7
                for x in range(done, ready):
                    value, slope = soft(held[x] + high[x] + bias1[...])
                    held[x] = low[x]
                    value = value.astype(BF16)
                    h1[STEP * g + r, x] = value
                    s1[STEP * g + r, x] = slope.astype(BF16)
                done = ready
        for copy in leaves(g):
            copy.start()
        return carry

    prepare()
    lax.fori_loop(0, steps, one_step, 0)
    for b in range(steps - 1, side // 2):
        second_rows(b)
    for copy in last_copies[1:]:
        copy.start()
    last_copies[0].wait()
    value, slope = soft(dot_rows(lw[...], h2[...]) + column(table[AT_LB, :]))
    enc[...] = value.astype(BF16)
    s3[...] = slope
    for g in range(steps):
        for copy in leaves(g):
            copy.wait()
    for copy in last_copies[1:]:
        copy.wait()


def three_parts(row):
    high = row.astype(BF16).astype(F32)
    middle = (row - high).astype(BF16).astype(F32)
    return jnp.concatenate([high, middle, row - high - middle], axis=0)


def with_ones(value):
    return jnp.concatenate([value, ones_rows(value.shape[1])], axis=0)


def ones_rows(lanes):
    return (iota((16, lanes), 0) < 3).astype(F32).astype(BF16)


def plan_kernel(
    section,
    slots,
    enc,
    s3,
    h2,
    branch_far,
    value_w,
    table,
    keep,
    send,
    small,
    g3,
    parts,
    bwt,
    vht,
    vhw,
    ow,
    mine,
    pre,
    dbr,
    dval,
    low,
    hid,
    gb,
    h2_here,
    branch_w,
    sems,
    *,
    per_pair,
    depth,
):
    width = enc.shape[0]
    options = branch_w.shape[0]
    pairs = options // 2
    two = 2 * width
    sec = section[0]
    branch_copy = pltpu.make_async_copy(branch_far, branch_w, sems.at[0])
    branch_copy.start()
    h2_copy = pltpu.make_async_copy(h2, h2_here, sems.at[1])
    h2_copy.start()

    count = slots.shape[0]
    dest = jnp.concatenate(
        [table[AT_DEST + k : AT_DEST + k + 1, :] for k in range(count // LANES)], axis=1
    )
    own = jnp.where(sec == 0, dest[:, :LANES], dest[:, LANES:])
    others = jnp.transpose(jnp.broadcast_to(dest, (LANES, count)))
    index = iota((count, LANES), 1) + sec * LANES
    earlier = (others == own) & (iota((count, LANES), 0) < index)
    rank = jnp.sum(earlier.astype(F32), axis=0, keepdims=True)
    bucket = own * float(per_pair) + rank
    chosen = (iota((count, LANES), 0).astype(F32) == bucket).astype(F32)
    mine[...] = dot_rows(slots[...], chosen, EXACT)[: mine.shape[0]]

    pad = jnp.zeros((13, width), F32)
    branch_copy.wait()
    for o in range(options):
        rows = [branch_w[o].astype(F32), three_parts(table[o : o + 1, :]), pad]
        bwt[o * width : (o + 1) * width, :] = jnp.transpose(
            jnp.concatenate(rows, axis=0)
        ).astype(BF16)
    scalars = table[AT_SCALARS, :]
    head_w = table[AT_HW, :]
    rows = [value_w[...].astype(F32), three_parts(table[AT_VB, :]), pad]
    vht[0:width, :] = jnp.transpose(jnp.concatenate(rows, axis=0)).astype(BF16)
    vht[width:, :] = jnp.zeros((16, width + 16), BF16)
    lane = iota((1, 16), 1)
    for k in range(2):
        bias = three_parts(jnp.broadcast_to(scalars[:, 1 + k : 2 + k], (1, 16)))
        bias = sum(jnp.where(lane == j, bias[j : j + 1], 0.0) for j in range(3))
        vht[width + k : width + k + 1, 0:width] = head_w[k : k + 1].astype(BF16)
        vht[width + k : width + k + 1, width:] = bias.astype(BF16)
    vhw[:, 0:width] = value_w[...]
    vhw[:, width:] = jnp.transpose(
        jnp.concatenate([head_w, jnp.zeros((14, width), F32)], axis=0)
    ).astype(BF16)
    ow[...] = jnp.broadcast_to(column(table[AT_OW, :]), (width, LANES))
    wide_ow = jnp.concatenate([ow[...], ow[...]], axis=1)

    labels = iota((options, LANES), 0).astype(F32)
    state = enc[...].astype(F32)
    rounded_all, saved = [], []
    for level in range(depth):
        picked = labels == mine[level : level + 1, :]
        rounded = state.astype(BF16)
        rounded_all.append(rounded)
        pre[...] = dot(bwt[...], with_ones(rounded))
        following = state
        reward, discount, value = [], [], []
        for t in range(pairs):
            at = slice(t * two, (t + 1) * two)
            act, slope = silu_pair(pre[at, :])
            dbr[level, at, :] = slope
            left = state + act[:width]
            right = state + act[width:]
            following = jnp.where(picked[2 * t : 2 * t + 1], left, following)
            following = jnp.where(picked[2 * t + 1 : 2 * t + 2], right, following)
            both = with_ones(jnp.concatenate([left.astype(BF16), right.astype(BF16)], axis=1))
            low[level, t] = both
            got = dot(vht[...], both)
            act, slope = silu_pair(got[:width])
            dval[level, t] = slope
            hidden = act.astype(BF16)
            hid[level, t] = hidden
            worth = jnp.sum(hidden.astype(F32) * wide_ow, axis=0, keepdims=True)
            for k in range(2):
                span = slice(k * LANES, (k + 1) * LANES)
                value.append(worth[:, span])
                reward.append(got[width : width + 1, span])
                discount.append(got[width + 1 : width + 2, span])
        reward = jnp.concatenate(reward, axis=0)
        discount = jax.nn.sigmoid(jnp.concatenate(discount, axis=0))
        value = jnp.concatenate(value, axis=0) + scalars[:, 3:4]
        quality = reward + discount * value
        top = jnp.max(quality, axis=0, keepdims=True)
        shifted = jnp.exp(quality - top)
        total = jnp.sum(shifted, axis=0, keepdims=True)
        live = (mine[depth : depth + 1, :] > level).astype(F32)
        chosen = picked.astype(F32)

        def target(kind):
            at = depth + 1 + kind * depth + level
            return mine[at : at + 1, :]

        reward_gap = live * (jnp.sum(chosen * reward, axis=0, keepdims=True) - target(0))
        discount_gap = live * (jnp.sum(chosen * discount, axis=0, keepdims=True) - target(1))
        plan_gap = live * (top + jnp.log(total) - target(2))
        grad_quality = plan_gap * (shifted / total)
        head_two = (chosen * discount_gap + grad_quality * value) * discount * (1.0 - discount)
        saved.append(
            (
                picked,
                (chosen * reward_gap + grad_quality).astype(BF16).astype(F32),
                head_two.astype(BF16).astype(F32),
                (grad_quality * discount).astype(BF16).astype(F32),
                reward_gap * reward_gap + discount_gap * discount_gap + plan_gap * plan_gap,
            )
        )
        state = following

    out_sum = jnp.zeros((width, two), F32)
    value_sum = jnp.zeros((width + 16, width + 16), F32)
    grad_next = jnp.zeros((width, LANES), F32)
    line = iota((16, two), 0)
    for level in reversed(range(depth)):
        picked, head_one, head_two, grad_value, _ = saved[level]
        upward = jnp.zeros((width, LANES), F32)
        for t in range(pairs):
            at = slice(t * two, (t + 1) * two)

            def across(rows):
                return jnp.concatenate(
                    [rows[2 * t : 2 * t + 1], rows[2 * t + 1 : 2 * t + 2]], axis=1
                )

            worth = across(grad_value)
            grad_pre = (worth * wide_ow * dval[level, t]).astype(BF16)
            out_sum = out_sum + hid[level, t].astype(F32) * worth
            heads = jnp.where(line == 0, across(head_one), 0.0)
            heads = jnp.where(line == 1, across(head_two), heads)
            heads = jnp.where(line == 2, worth, heads)
            stacked = jnp.concatenate([grad_pre, heads.astype(BF16)], axis=0)
            value_sum = value_sum + dot_lanes(stacked, low[level, t])
            moved = dot(vhw[...], stacked)
            left = moved[:, :LANES] + jnp.where(picked[2 * t : 2 * t + 1], grad_next, 0.0)
            right = moved[:, LANES:] + jnp.where(picked[2 * t + 1 : 2 * t + 2], grad_next, 0.0)
            grad_branch = jnp.concatenate([left, right], axis=0) * dbr[level, at, :]
            grad_branch = grad_branch.astype(BF16)
            gb[level, at, :] = grad_branch
            weights = jnp.concatenate([branch_w[2 * t], branch_w[2 * t + 1]], axis=1)
            upward = upward + (left + right + dot(weights, grad_branch))
        grad_next = upward

    linear_rows = h2.shape[0]
    half = (linear_rows + options * width + width) // 2
    rest = linear_rows - half
    rounded = with_ones(jnp.concatenate(rounded_all, axis=1))
    small[...] = jnp.zeros_like(small)
    if half < keep.shape[0]:
        for k in range(2):
            parts[k, half:, :] = jnp.zeros((keep.shape[0] - half, LANES), BF16)
    for t in range(pairs):
        at = slice(t * two, (t + 1) * two)
        grads = jnp.concatenate([gb[level, at, :] for level in range(depth)], axis=1)
        got = dot_lanes(rounded, grads)
        for k in range(2):
            o = 2 * t + k
            span = slice(k * width, (k + 1) * width)
            rows = slice(rest + o * width, rest + (o + 1) * width)
            parts[1 - sec, rows, :] = got[:width, span].astype(BF16)
            small[o : o + 1, :] = got[width : width + 1, span]
    after = rest + options * width
    parts[1 - sec, after : after + width, :] = jnp.transpose(value_sum[:width, :width]).astype(BF16)

    grad_three = (grad_next.astype(BF16).astype(F32) * s3[...]).astype(BF16)
    g3[...] = grad_three
    h2_copy.wait()
    chunk = linear_rows // 9
    for i in range(8):
        at = slice(i * chunk, (i + 1) * chunk)
        parts[sec, at, :] = dot_lanes(h2_here[at, :], grad_three).astype(BF16)
    last = dot_lanes(h2_here[8 * chunk :, :], grad_three).astype(BF16)
    parts[sec, 8 * chunk : half, :] = last[: half - 8 * chunk]
    parts[1 - sec, 0:rest, :] = last[half - 8 * chunk :]
    keep[...] = parts[0]
    send[...] = parts[1]

    small[AT_VB, :] = row_of(value_sum[:width, width : width + 1])
    small[AT_OW, :] = row_of(jnp.sum(out_sum, axis=1, keepdims=True))
    small[AT_HW, :] = value_sum[width : width + 2, :width]
    small[AT_LB, :] = row_of(jnp.sum(grad_three.astype(F32), axis=1, keepdims=True))
    loss = 0.5 * jnp.sum(sum(kept[4] for kept in saved), axis=1, keepdims=True)
    ends = [loss] + [value_sum[width + k : width + k + 1, width : width + 1] for k in range(3)]
    lane = iota((1, LANES), 1)
    line = jnp.zeros((1, LANES), F32)
    for k, end in enumerate(ends):
        line = jnp.where(lane == k, end, line)
    small[AT_SCALARS, :] = line


def back_kernel(g3, lw, s2_far, s1_far, h1_far, w2t, g1, c2, sums, t2, g2, s2, s1, h1, sems):
    side, k1 = s1.shape[1], s1.shape[2]
    k2 = w2t.shape[0]
    inner = side // 2 - 1
    row_len = inner * k2
    copies = [
        pltpu.make_async_copy(s2_far, s2, sems.at[0]),
        pltpu.make_async_copy(s1_far, s1, sems.at[1]),
        pltpu.make_async_copy(h1_far, h1, sems.at[2]),
    ]
    for copy in copies:
        copy.start()
    tap, pix = iota((LANES, 256), 1), iota((LANES, 256), 0)
    for yrel in range(2):
        for p in range(3):
            hit = (
                ((tap & 15) == (pix & 15))
                & ((tap >> 6) == (pix >> 6) + 2 * (1 - yrel))
                & (((tap >> 4) & 3) == ((pix >> 4) & 3) + 2 - 2 * p)
            )
            at = (yrel * 3 + p) * k2
            t2[:, at : at + k2] = dot_lanes(hit.astype(F32).astype(BF16), w2t[...]).astype(BF16)
    g2[0] = jnp.zeros(g2.shape[1:], BF16)
    g2[inner + 1] = jnp.zeros(g2.shape[1:], BF16)
    g1[0] = jnp.zeros(g1.shape[1:], BF16)
    g1[side + 1] = jnp.zeros(g1.shape[1:], BF16)
    zero = jnp.zeros((k2, LANES), BF16)
    total_one = jnp.zeros((k1, LANES), F32)
    total_two = jnp.zeros((k2, LANES), F32)
    copies[0].wait()
    for y in range(inner):
        at = slice(y * row_len, (y + 1) * row_len)
        grad = dot(lw[at, :], g3[...]) * s2[at, :].astype(F32)
        grad = grad.astype(BF16).reshape(inner, k2, LANES)
        g2[y + 1] = grad
        total_two = total_two + jnp.sum(grad.astype(F32), axis=0)
    for copy in copies[1:]:
        copy.wait()
    total = jnp.zeros(c2.shape, F32)
    for b in range(side // 2):
        cut = []
        for j in range(side // 4):
            pieces = []
            for yrel in range(2):
                for p in range(3):
                    x = 2 * j - 1 + p
                    pieces.append(g2[b + yrel, x] if 0 <= x < inner else zero)
            cut.append(jnp.concatenate(pieces, axis=0))
        got = dot(t2[...], jnp.concatenate(cut, axis=1))
        for u in range(2):
            for j in range(side // 4):
                part = got[u * 64 : (u + 1) * 64, j * LANES : (j + 1) * LANES]
                slope = s1[2 * b + u + 1, 4 * j : 4 * j + 4].astype(F32)
                grad = (part.reshape(4, k1, LANES) * slope).astype(BF16)
                g1[2 * b + u + 1, 4 * j : 4 * j + 4] = grad
                total_one = total_one + jnp.sum(grad.astype(F32), axis=0)
        if b < inner:
            grads = jnp.concatenate([g2[b + 1, x] for x in range(inner)], axis=1)
            patches = [
                h1[2 * b + 1 : 2 * b + 5, 2 * x : 2 * x + 4].reshape(256, LANES)
                for x in range(inner)
            ]
            total = total + dot_lanes(grads, jnp.concatenate(patches, axis=1))
    c2[...] = total
    sums[...] = jnp.zeros_like(sums)
    sums[0:1, 0:k1] = row_of(jnp.sum(total_one, axis=1, keepdims=True))
    sums[1:2, 0:k2] = row_of(jnp.sum(total_two, axis=1, keepdims=True))


def pixel_band(sec, w1t, channels):
    k1 = w1t.shape[0]
    rows = 64 * channels
    row, tap = iota((rows, 256), 0), iota((rows, 256), 1)
    moves = ((tap >> 6) == row % channels + sec * channels) & ((tap & 63) == row // channels)
    taps = dot_lanes(moves.astype(F32).astype(BF16), w1t)
    line, span = COLS * channels, 8 * channels
    blocks = {}
    for half in range(2):
        for p in range(NEAR):
            pieces = []
            for u in range(4):
                at = (4 * half + u) * span
                start = 4 * (p - 1) * channels
                cut = taps[at + max(0, -start) : at + min(span, line - start)]
                start = max(start, 0)
                pieces += [jnp.zeros((start, k1), F32)] if start else []
                pieces.append(cut)
                rest = line - start - cut.shape[0]
                pieces += [jnp.zeros((rest, k1), F32)] if rest else []
            blocks[half, p] = jnp.concatenate(pieces, axis=0)
    zero = jnp.zeros((4 * line, k1), F32)
    lines = []
    for r in range(STEP):
        cols = [
            blocks.get((r + 1 - yrel, p), zero) for yrel in range(STEP + 1) for p in range(NEAR)
        ]
        lines.append(jnp.concatenate(cols, axis=1))
    return jnp.concatenate(lines, axis=0).astype(BF16)


def first_kernel(section, frames_far, g1, after, c1, frames, acc, sems):
    side, k1 = g1.shape[1], g1.shape[2]
    img, _, channels, _ = frames.shape
    steps = img // 4 // STEP
    arrives = frame_copies(section, frames_far, frames, sems)
    for g in range(steps):
        arrives(g).start()
    acc[...] = jnp.zeros_like(acc)
    zero = jnp.zeros((k1, LANES), BF16)

    def one_step(g, carry):
        arrives(g).wait()
        pixels, grads = [], []
        for j in range(img // COLS):
            rows = [pl.multiple_of(4 * (STEP * g + r), 4) for r in range(STEP)]
            pixels.append(
                jnp.concatenate([tile_rows(frames, row, j, COLS) for row in rows], axis=0)
            )
            pieces = []
            for yrel in range(STEP + 1):
                for p in range(NEAR):
                    x = 3 * j - 1 + p
                    pieces.append(g1[STEP * g + yrel, x] if 0 <= x < side else zero)
            grads.append(jnp.concatenate(pieces, axis=0))
        acc[...] += dot_lanes(jnp.concatenate(pixels, axis=1), jnp.concatenate(grads, axis=1))
        return carry

    lax.fori_loop(0, steps, one_step, 0)
    fold_first(acc, c1, channels, k1)


def fold_first(acc, c1, channels, k1):
    line = COLS * channels
    step = 4 * channels
    taps = []
    for half in range(2):
        total = sum(
            acc[r * 4 * line : (r + 1) * 4 * line, :][
                :, (r + 1 - half) * NEAR * k1 : (r + 2 - half) * NEAR * k1
            ]
            for r in range(STEP)
        )
        for u in range(4):
            part = total[u * line : (u + 1) * line]
            cols = [part[:, p * k1 : (p + 1) * k1] for p in range(NEAR)]
            taps.append(cols[1][0:step] + cols[2][step : 2 * step] + cols[3][2 * step :])
            taps.append(cols[0][0:step] + cols[1][step : 2 * step] + cols[2][2 * step :])
    row, col = iota((256, 256), 0), iota((256, 256), 1)
    moves = ((row & 3) == (col >> 6)) & ((row >> 2) == (col & 63))
    grad = dot_rows(jnp.concatenate(taps, axis=0), moves.astype(F32), EXACT)
    for half in range(2):
        c1[half * k1 : (half + 1) * k1, :] = grad[:, half * LANES : (half + 1) * LANES].astype(BF16)


def pixels_kernel(section, weights, mine, other, after, *refs, start, steps, begins):
    out, token, band_out, held, sems = refs[-5:]
    side, k1 = mine.shape[1], mine.shape[2]
    img, channels = out.shape[1], out.shape[2]
    sec = section[0]
    line = COLS * channels
    flat = held.reshape(2, 2, 4 * STEP, img * channels, LANES)
    if begins:
        band_out[...] = pixel_band(sec, weights[...], channels)
        band = band_out
    else:
        band = weights
        band_out[...] = jnp.zeros_like(band_out)
    token[...] = jnp.zeros_like(token)

    def writes(g):
        rows = slice(4 * STEP * (start + g), 4 * STEP * (start + g + 1))
        places = (sec * LANES, (1 - sec) * LANES)
        return [
            pltpu.make_async_copy(
                held.at[g % 2, k],
                out.at[rows, :, :, pl.ds(pl.multiple_of(places[k], LANES), LANES)],
                sems.at[g % 2, k],
            )
            for k in range(2)
        ]

    zero = jnp.zeros((k1, 2 * LANES), BF16)
    for g in range(steps):
        if g >= 2:
            for copy in writes(g - 2):
                copy.wait()
        for j in range(img // COLS):
            pieces = []
            for yrel in range(STEP + 1):
                for p in range(NEAR):
                    x, y = 3 * j - 1 + p, STEP * (start + g) + yrel
                    if 0 <= x < side:
                        pieces.append(jnp.concatenate([mine[y, x], other[y, x]], axis=1))
                    else:
                        pieces.append(zero)
            got = dot(band[...], jnp.concatenate(pieces, axis=0))
            for k in range(4 * STEP):
                at = slice(k * line, (k + 1) * line)
                span = slice(j * line, (j + 1) * line)
                flat[g % 2, 0, k, span, :] = got[at, :LANES]
                flat[g % 2, 1, k, span, :] = got[at, LANES:]
        for copy in writes(g):
            copy.start()
    for g in range(max(steps - 2, 0), steps):
        for copy in writes(g):
            copy.wait()


def two_parts(value):
    high = value.astype(BF16).astype(F32)
    return jnp.concatenate([high, value - high], axis=0).astype(BF16)


def one_part(pair):
    rows = pair.shape[0] // 2
    pair = pair.astype(F32)
    return pair[:rows] + pair[rows:]


def plane_bits(section):
    return 1 + section[0], 2 - section[0]


def merge_kernel(section, batch, keep, recv, small, c2, sums, stay, go, lines):
    me = batch[0] % PLANE
    one, two = plane_bits(section)
    short = lines.shape[0] // PLANE
    size = keep.shape[0] // PLANE
    k2 = c2.shape[0]
    lines[...] = jnp.zeros_like(lines)
    at = small.shape[0]
    lines[0:at, :] = small[...]
    for half in range(2):
        lines[at : at + k2, :] = c2[:, half * LANES : (half + 1) * LANES]
        at += k2
    lines[at : at + sums.shape[0], :] = sums[...]
    for out, whose in ((stay, me), (go, me ^ one)):
        for k in range(2):
            member = whose ^ two if k else whose
            at = pl.ds(pl.multiple_of(member * size, size), size)
            out[k, 0:size, :] = (keep[at, :].astype(F32) + recv[at, :].astype(F32)).astype(BF16)
            at = pl.ds(pl.multiple_of(member * short, short), short)
            out[k, size:, :] = two_parts(lines[at, :])


def fold_kernel(mine, got, after, stay, go):
    for k, out in enumerate((stay, go)):
        out[...] = added(mine[k], got[k], SHORT)


def plane_kernel(section, batch, mine, got, c1, after, keep, send, total, lines):
    size, short = total.shape[0], lines.shape[0]
    total[...] = (mine[0:size, :].astype(F32) + got[0:size, :].astype(F32)).astype(BF16)
    lines[...] = one_part(mine[size:, :]) + one_part(got[size:, :])
    half_kept = own_half(section, batch)
    for out, half in ((keep, half_kept), (send, 1 - half_kept)):
        at = 0
        for ref, count in ((total, size // 2), (lines, short // 2), (c1, c1.shape[0] // 2)):
            part = ref[pl.ds(pl.multiple_of(half * count, count), count), :]
            part = two_parts(part) if ref is lines else part
            out[at : at + part.shape[0], :] = part
            at += part.shape[0]


def own_half(section, batch):
    plane = batch[0] // PLANE
    return jnp.where(section[0] == 0, plane % 2, (plane // 2) % 2)


def added(a, b, short, rest=0):
    fine = a.shape[0] - 2 * short - rest
    pieces = [(a[0:fine].astype(F32) + b[0:fine].astype(F32)).astype(BF16)]
    pieces.append(
        two_parts(one_part(a[fine : fine + 2 * short]) + one_part(b[fine : fine + 2 * short]))
    )
    if rest:
        at = fine + 2 * short
        pieces.append((a[at:].astype(F32) + b[at:].astype(F32)).astype(BF16))
    return jnp.concatenate(pieces, axis=0)


def add_kernel(a, b, after, out, *, rest):
    out[...] = added(a[...], b[...], SHORT // 2, rest)


def join_kernel(section, batch, a, b, after, out):
    mine = own_half(section, batch)
    out[mine] = a[...]
    out[1 - mine] = b[...]


def pair_kernel(a, b, out):
    out[0] = a[...]
    out[1] = b[...]


def relay_kernel(section, batch, mine, got, after, out):
    me = batch[0] % PLANE
    one, two = plane_bits(section)
    for pair, whose in ((mine, me), (got, me ^ one)):
        out[whose] = pair[0]
        out[whose ^ two] = pair[1]


def unpack_kernel(section, mine, other, *refs):
    loss, c1, b1, c2, b2, lw, lb, bw, bb, hw, hb, vw, vb, ow, ob, halves, lines = refs
    width = lw.shape[1]
    options = bw.shape[0]
    k1, k2 = c1.shape[0], c2.shape[0]
    linear_rows = lw.shape[0]
    sec = section[0]
    size = halves.shape[1] // (2 * PLANE)
    short = lines.shape[0] // (2 * PLANE)
    half = (linear_rows + options * width + width) // 2
    rest = linear_rows - half
    grad = [jnp.zeros((k1, LANES), F32) for _ in range(2)]
    for k in range(PLANE):
        for h in range(2):
            at = (2 * k + h) * size
            halves[sec, at : at + size, :] = mine[k, h, 0:size, :]
            halves[1 - sec, at : at + size, :] = other[k, h, 0:size, :]
            pair = slice(size, size + 2 * short)
            at = (2 * k + h) * short
            lines[at : at + short, :] = one_part(mine[k, h, pair, :]) + one_part(
                other[k, h, pair, :]
            )
            for ref in (mine, other):
                grad[h] += ref[k, h, size + 2 * short :, :].astype(F32)
    for part in range(2):
        c1[:, part * LANES : (part + 1) * LANES] = grad[part]
    lw[0:half, :] = halves[0, 0:half, :].astype(F32)
    lw[half:, :] = halves[1, 0:rest, :].astype(F32)
    for o in range(options):
        at = rest + o * width
        bw[o] = halves[1, at : at + width, :].astype(F32)
    at = rest + options * width
    vw[...] = halves[1, at : at + width, :].astype(F32)
    bb[...] = lines[0:options, :]
    vb[...] = lines[AT_VB, :]
    ow[...] = lines[AT_OW, :]
    hw[...] = lines[AT_HW, :]
    lb[...] = lines[AT_LB, :]
    scalars = lines[AT_SCALARS, :]
    loss[...] = scalars[:, 0:1]
    hb[...] = scalars[:, 1:3]
    ob[...] = scalars[:, 3:4]
    at = TABLE
    for part in range(2):
        c2[:, part * LANES : (part + 1) * LANES] = lines[at : at + k2, :]
        at += k2
    b1[...] = lines[at : at + 1, 0:k1]
    b2[...] = lines[at + 1 : at + 2, 0:k2]


def numbers_kernel(
    options,
    depth,
    targets,
    destination,
    b1,
    b2,
    lb,
    bb,
    hw,
    vb,
    ow,
    hb,
    ob,
    out,
    table,
):
    levels, kinds = options.shape[0], targets.shape[0]
    slots = depth.shape[1]
    rows = [options[...].astype(F32), depth[...].astype(F32)]
    rows += [targets[k] for k in range(kinds)]
    rows.append(jnp.zeros((LANES - levels - 1 - kinds * levels, slots), F32))
    out[...] = jnp.transpose(jnp.concatenate(rows, axis=0))
    table[...] = jnp.zeros_like(table)
    table[0 : bb.shape[0], :] = bb[...]
    table[AT_VB, :] = vb[...]
    table[AT_OW, :] = ow[...].astype(F32)
    table[AT_HW, :] = hw[...].astype(F32)
    table[AT_LB, :] = lb[...]
    table[AT_B1, 0 : b1.shape[1]] = b1[...]
    table[AT_B2, 0 : b2.shape[1]] = b2[...]
    lane = iota((1, LANES), 1)
    scalars = jnp.zeros((1, LANES), F32)
    for k, value in ((1, hb[:, 0:1]), (2, hb[:, 1:2]), (3, ob[...])):
        scalars = jnp.where(lane == k, value, scalars)
    table[AT_SCALARS, :] = scalars
    for k in range(slots // LANES):
        part = destination[:, k * LANES : (k + 1) * LANES]
        table[AT_DEST + k : AT_DEST + k + 1, :] = part.astype(F32)


def whole(shape):
    zeros = (0,) * len(shape)
    return pl.BlockSpec(shape, lambda *_: zeros)


ANYWHERE = pl.BlockSpec(memory_space=pl.ANY)
SCALARS = pl.BlockSpec(memory_space=pltpu.SMEM)


def params():
    return pltpu.CompilerParams(vmem_limit_bytes=VMEM_BYTES)


def shape_of(*shape, dtype=F32):
    return jax.ShapeDtypeStruct(shape, dtype)


def cost(microseconds):
    return pl.CostEstimate(
        flops=int(5e9 * microseconds), bytes_accessed=int(1.8e7 * microseconds), transcendentals=0
    )


def stays(value):
    return pltpu.with_memory_space_constraint(value, pltpu.HBM)


def held_near(value):
    return pltpu.with_memory_space_constraint(value, pltpu.VMEM)


def encode(section, frames, w1t, w2t, lw, table):
    img = frames.shape[0]
    blocks = img // 4
    side = blocks - 1
    k1, k2, width = w1t.shape[0], w2t.shape[0], lw.shape[1]
    flat = lw.shape[0]
    vmem = pltpu.VMEM
    near = pl.BlockSpec(memory_space=vmem)
    grid_one = (blocks, side, k1, LANES)
    return pl.pallas_call(
        encode_kernel,
        in_specs=[SCALARS, ANYWHERE, near, near, ANYWHERE, near],
        out_specs=[ANYWHERE] * 4 + [near] * 2,
        out_shape=(
            pltpu.HBM(grid_one, BF16),
            pltpu.HBM(grid_one, BF16),
            pltpu.HBM((flat, LANES), BF16),
            pltpu.HBM((flat, LANES), BF16),
            shape_of(width, LANES, dtype=BF16),
            shape_of(width, LANES),
        ),
        scratch_shapes=[
            vmem((img, img, frames.shape[2], LANES), BF16),
            vmem(lw.shape, BF16),
            vmem(grid_one, BF16),
            vmem(grid_one, BF16),
            vmem((flat, LANES), BF16),
            vmem((flat, LANES), BF16),
            vmem((2 * REACH * k1, 256), BF16),
            vmem((2 * k1, 64), BF16),
            vmem((6 * k2, LANES), BF16),
            vmem((k1, LANES), F32),
            vmem((k2, LANES), F32),
            vmem((side, k1, LANES), F32),
            vmem((side // 2 - 1, k2, LANES), F32),
            pltpu.SemaphoreType.DMA((4, max(blocks // STEP, 3))),
        ],
        compiler_params=params(),
        cost_estimate=cost(9),
        name="encode",
    )(section, frames, w1t, w2t, lw, table)


def plan(section, slots, enc, s3, h2, branch_w, value_w, table, per_pair, depth, half_rows):
    width = enc.shape[0]
    options = branch_w.shape[0]
    two = 2 * width
    pairs = options // 2
    outs = (
        shape_of(half_rows, LANES, dtype=BF16),
        shape_of(half_rows, LANES, dtype=BF16),
        shape_of(TABLE, LANES),
        shape_of(width, LANES, dtype=BF16),
    )
    vmem = pltpu.VMEM
    near = pl.BlockSpec(memory_space=vmem)
    return pl.pallas_call(
        functools.partial(plan_kernel, per_pair=per_pair, depth=depth),
        in_specs=[SCALARS, near, near, near, ANYWHERE, ANYWHERE, near, near],
        out_shape=outs,
        scratch_shapes=[
            vmem((2, half_rows, LANES), BF16),
            vmem((options * width, width + 16), BF16),
            vmem((width + 16, width + 16), BF16),
            vmem((width, width + 16), BF16),
            vmem((width, LANES), F32),
            vmem((16, LANES), F32),
            vmem((options * width, LANES), F32),
            vmem((depth, options * width, LANES), F32),
            vmem((depth, pairs, width, two), F32),
            vmem((depth, pairs, width + 16, two), BF16),
            vmem((depth, pairs, width, two), BF16),
            vmem((depth, options * width, LANES), BF16),
            vmem(h2.shape, BF16),
            vmem(branch_w.shape, BF16),
            pltpu.SemaphoreType.DMA((2,)),
        ],
        compiler_params=params(),
        cost_estimate=cost(11),
        name="plan",
    )(section, slots, enc, s3, h2, branch_w, value_w, table)


def back(g3, lw, s2, s1, h1, w2t):
    _, side, k1 = s1.shape[:3]
    k2 = w2t.shape[0]
    inner = side // 2 - 1
    outs = (
        shape_of(side + 2, side, k1, LANES, dtype=BF16),
        shape_of(k2, 256),
        shape_of(8, LANES),
    )
    near = pl.BlockSpec(memory_space=pltpu.VMEM)
    return pl.pallas_call(
        back_kernel,
        in_specs=[near, near, ANYWHERE, ANYWHERE, ANYWHERE, near],
        out_shape=outs,
        scratch_shapes=[
            pltpu.VMEM((LANES, 6 * k2), BF16),
            pltpu.VMEM((inner + 2, inner, k2, LANES), BF16),
            pltpu.VMEM(s2.shape, BF16),
            pltpu.VMEM(s1.shape, BF16),
            pltpu.VMEM(h1.shape, BF16),
            pltpu.SemaphoreType.DMA((3,)),
        ],
        compiler_params=params(),
        cost_estimate=cost(5),
        name="back",
    )(g3, lw, s2, s1, h1, w2t)


def first(section, frames, g1, after):
    img, _, channels, _ = frames.shape
    k1 = g1.shape[2]
    near = pl.BlockSpec(memory_space=pltpu.VMEM)
    return pl.pallas_call(
        first_kernel,
        in_specs=[SCALARS, ANYWHERE, near, ANYWHERE],
        out_shape=shape_of(2 * k1, LANES, dtype=BF16),
        scratch_shapes=[
            pltpu.VMEM((img, img, channels, LANES), BF16),
            pltpu.VMEM((STEP * 4 * COLS * channels, (STEP + 1) * NEAR * k1), F32),
            pltpu.SemaphoreType.DMA((img // 4 // STEP,)),
        ],
        compiler_params=params(),
        cost_estimate=cost(9),
        name="first",
    )(section, frames, g1, after)


def pixels(section, weights, mine, other, shape, start, steps, after, done=None):
    img, _, channels, _ = shape
    k1 = mine.shape[2]
    band = (STEP * 4 * COLS * channels, (STEP + 1) * NEAR * k1)
    near = pl.BlockSpec(memory_space=pltpu.VMEM)
    operands = (section, weights, mine, other, after)
    specs = [SCALARS, near, near, near, ANYWHERE]
    aliases = {}
    if done is not None:
        aliases = {len(operands): 0}
        operands += (done,)
        specs.append(ANYWHERE)
    outs = [shape_of(*shape), shape_of(8, LANES), shape_of(*band, dtype=BF16)]
    return pl.pallas_call(
        functools.partial(pixels_kernel, start=start, steps=steps, begins=done is None),
        in_specs=specs,
        out_specs=[ANYWHERE, near, near],
        out_shape=outs,
        scratch_shapes=[
            pltpu.VMEM((2, 2, 4 * STEP, img, channels, LANES), F32),
            pltpu.SemaphoreType.DMA((2, 2)),
        ],
        input_output_aliases=aliases,
        compiler_params=params(),
        cost_estimate=cost(2 + 0.8 * steps),
        name="pixels",
    )(*operands)


def small_call(
    kernel, outs, operands, scratch=(), name=None, place=None, after=(), weight=0.3
):
    specs = [pl.BlockSpec(memory_space=pltpu.VMEM)] * len(operands)
    if place is not None:
        operands = (*place, *operands)
        specs = [pl.BlockSpec(memory_space=pltpu.SMEM)] * len(place) + specs
    return pl.pallas_call(
        kernel,
        in_specs=specs + [ANYWHERE] * len(after),
        out_shape=outs,
        scratch_shapes=list(scratch),
        compiler_params=params(),
        cost_estimate=cost(weight),
        name=name,
    )(*operands, *after)


def round_up(value, step):
    return -(-value // step) * step


def swapped(value):
    return lax.ppermute(value, "section", [(0, 1), (1, 0)])


def exchanged(value):
    return lax.all_to_all(value, "batch", split_axis=0, concat_axis=0, tiled=True)


def partner(value, distances):
    count = lax.axis_size("batch")
    pairs = [
        (s * count + b, s * count + (b ^ distances[s])) for s in range(2) for b in range(count)
    ]
    return lax.ppermute(value, ("section", "batch"), pairs)


def local(
    frames,
    destination,
    options,
    depth,
    targets,
    conv_one,
    bias_one,
    conv_two,
    bias_two,
    linear_w,
    linear_b,
    branch_w,
    branch_b,
    head_w,
    head_b,
    value_w,
    value_b,
    out_w,
    out_b,
):
    section = lax.axis_index("section").astype(jnp.int32)[None]
    peers = lax.axis_size("batch")
    frame_count = frames.shape[3]
    per_pair = frame_count // peers
    levels = options.shape[0]
    frames = stays(frames.transpose(1, 2, 0, 3))
    w1t, w2t = stays(conv_one.T), stays(conv_two.T)
    linear_w, branch_w, value_w = stays(linear_w), stays(branch_w), stays(value_w)
    encoder_params = (w1t, bias_one, w2t, bias_two, linear_w, linear_b)
    planner_params = (branch_w, branch_b, head_w.T, head_b, value_w, value_b, out_w.T, out_b)
    width = linear_w.shape[1]
    big_rows = linear_w.shape[0] + (branch_w.shape[0] + 1) * width
    size = round_up(-(-big_rows // (2 * PLANE)), 32)

    tiny = (bias_one, bias_two, linear_b, branch_b, head_w.T, value_b, out_w.T)
    tiny = [stays(v if v.ndim > 1 else v[None, :]) for v in tiny]
    numbers, table = pl.pallas_call(
        numbers_kernel,
        in_specs=[pl.BlockSpec(memory_space=pltpu.VMEM)] * (6 + len(tiny)),
        out_shape=[shape_of(frame_count, LANES), shape_of(TABLE, LANES)],
        compiler_params=params(),
        cost_estimate=cost(1),
        name="numbers",
    )(
        stays(options),
        stays(depth[None, :]),
        stays(targets),
        stays(destination[None, :]),
        *tiny,
        stays(head_b[None, :]),
        out_b[None, :],
    )
    slots = exchanged(numbers.reshape(peers, per_pair, LANES)).reshape(frame_count, LANES)

    h1, s1, h2, s2, enc, s3 = encode(section, frames, w1t, w2t, linear_w, table)
    h1, s1, h2, s2 = (stays(v) for v in (h1, s1, h2, s2))
    keep, send, small, g3 = plan(
        section, slots, enc, s3, h2, branch_w, value_w, table, per_pair, levels, PLANE * size
    )
    recv = swapped(send)
    channels = frames.shape[2] // lax.axis_size("section")
    g1, c2, sums = back(g3, linear_w, s2, s1, h1, w2t)
    other = held_near(swapped(g1))
    g1 = held_near(g1)
    place = (section, lax.axis_index("batch").astype(jnp.int32)[None])
    bf16 = functools.partial(shape_of, dtype=BF16)
    pieces = bf16(2, size + 2 * SHORT, LANES)
    keep, send = small_call(
        merge_kernel,
        [pieces] * 2,
        (keep, recv, small, c2, sums),
        [pltpu.VMEM((PLANE * SHORT, LANES), F32)],
        name="merge",
        place=place,
    )
    recv = partner(send, (1, 2))
    c1 = first(section, frames, g1, send)
    keep, send = small_call(
        fold_kernel, [bf16(*pieces.shape[1:])] * 2, (keep, recv), name="fold", after=(c1,)
    )
    recv = partner(send, (2, 1))
    img = frames.shape[0]
    steps = img // 4 // STEP
    draw = functools.partial(
        pixels, section, mine=g1, other=other, shape=(img, img, channels, 2 * LANES)
    )
    frames_grad, token, band = draw(weights=w1t, start=0, steps=1, after=send)
    extra = c1.shape[0] // 2
    half = bf16(size // 2 + SHORT + extra, LANES)
    keep, send = small_call(
        plane_kernel,
        [half, half],
        (keep, recv, c1),
        [pltpu.VMEM((size, LANES), BF16), pltpu.VMEM((SHORT, LANES), F32)],
        name="plane",
        place=place,
        after=(token,),
    )
    orders = ([PLANE, 2 * PLANE], [2 * PLANE, PLANE])
    distance = 4 * PLANE
    while distance < peers:
        orders[0].append(distance)
        orders[1].append(distance)
        distance *= 2
    for at, distances in enumerate(zip(*orders)):
        recv = partner(send if at == 0 else keep, distances)
        if at < 2:
            frames_grad, token, _ = draw(
                weights=band,
                start=1 + at,
                steps=1,
                after=send if at == 0 else keep,
                done=frames_grad,
            )
        keep = small_call(
            functools.partial(add_kernel, rest=extra),
            half,
            (keep, recv),
            name="add",
            after=(token,),
        )
    recv = partner(keep, (orders[0][0], orders[1][0]))
    frames_grad, token, _ = draw(weights=band, start=3, steps=1, after=keep, done=frames_grad)
    piece = bf16(2, *half.shape)
    mine = small_call(
        join_kernel, piece, (keep, recv), name="join", place=place, after=(token,)
    )
    mine = small_call(
        pair_kernel, bf16(2, *piece.shape), (mine, partner(mine, (2, 1))), name="pair"
    )
    recv = partner(mine, (1, 2))
    frames_grad, token, _ = draw(
        weights=band, start=4, steps=steps - 4, after=mine, done=frames_grad
    )
    got = small_call(
        relay_kernel,
        bf16(PLANE, *piece.shape),
        (mine, recv),
        name="relay",
        place=place,
        after=(token,),
    )
    shapes = [p.shape for p in encoder_params + planner_params]
    flat = [s if len(s) > 1 else (1,) + s for s in shapes]
    rest = small_call(
        unpack_kernel,
        [shape_of(1, 1)] + [shape_of(*s) for s in flat],
        (got, swapped(got)),
        [
            pltpu.VMEM((2, PLANE * size, LANES), BF16),
            pltpu.VMEM((PLANE * SHORT, LANES), F32),
        ],
        name="unpack",
        place=(section,),
    )
    rest = [v.reshape(s) for v, s in zip(rest, [()] + shapes)]
    for at in (1, 3, 9, 13):
        rest[at] = rest[at].T
    return (rest[0], frames_grad.transpose(2, 0, 1, 3), *rest[1:])


def solution(mesh):
    placed = (
        P(None, None, None, "batch"),
        P("batch"),
        P(None, "batch"),
        P("batch"),
        P(None, None, "batch"),
    ) + (P(),) * 14
    return jax.shard_map(
        local,
        mesh=mesh,
        in_specs=placed,
        out_specs=(P(), P("section", None, None, "batch")) + (P(),) * 14,
        check_vma=False,
    )
```

```python
import functools
import math

import jax
import jax.numpy as jnp
from jax import lax
from jax.experimental import pallas as pl
from jax.experimental.pallas import tpu as pltpu
from jax.sharding import PartitionSpec as P

BF16 = jnp.bfloat16
F32 = jnp.float32
EXACT = lax.Precision.HIGHEST
LANES = 128
VMEM_BYTES = 32 * 1024 * 1024
TILE = 16
REACH = 5
STEP = 3
COLS = 12
NEAR = 4
AT_VB, AT_OW, AT_HW, AT_LB, AT_SCALARS, AT_B1, AT_B2, AT_DEST = (
    slice(18, 19),
    slice(19, 20),
    slice(20, 22),
    slice(22, 23),
    slice(23, 24),
    slice(24, 25),
    slice(25, 26),
    26,
)
TABLE = 32
CUBE = 8
SHORT = 16


def dot(a, b, precision=None):
    return jnp.dot(a, b, preferred_element_type=F32, precision=precision)


def dot_rows(a, b, precision=None):
    return lax.dot_general(
        a, b, (((0,), (0,)), ((), ())), preferred_element_type=F32, precision=precision
    )


def dot_lanes(a, b, precision=None):
    return lax.dot_general(
        a, b, (((1,), (1,)), ((), ())), preferred_element_type=F32, precision=precision
    )


def iota(shape, axis):
    return lax.broadcasted_iota(jnp.int32, shape, axis)


def column(row):
    n = row.shape[1]
    wide = jnp.broadcast_to(row, (n, n))
    return jnp.sum(jnp.where(iota((n, n), 0) == iota((n, n), 1), wide, 0.0), axis=1, keepdims=True)


def row_of(col):
    n = col.shape[0]
    wide = jnp.broadcast_to(col, (n, n))
    return jnp.sum(jnp.where(iota((n, n), 0) == iota((n, n), 1), wide, 0.0), axis=0, keepdims=True)


def soft(x):
    t = jnp.tanh(0.5 * x)
    return jnp.maximum(x, 0.0) - jnp.log(0.5 + 0.5 * jnp.abs(t)), 0.5 + 0.5 * t


def silu_pair(x):
    s = 0.5 + 0.5 * jnp.tanh(0.5 * x)
    act = x * s
    return act, s + act * (1.0 - s)


def pixel_order(w1t):
    tap, pix = iota((256, 256), 0), iota((256, 256), 1)
    moves = ((tap >> 6) == (pix & 3)) & ((tap & 63) == (pix >> 2))
    return dot(w1t, moves.astype(F32).astype(BF16))


def frame_copies(section, far, here, sems):
    lanes = pl.ds(pl.multiple_of(section[0] * LANES, LANES), LANES)
    size = 4 * STEP

    def copy(g):
        rows = pl.ds(pl.multiple_of(g * size, size), size)
        return pltpu.make_async_copy(far.at[rows, :, :, lanes], here.at[rows], sems.at[g])

    return copy


def tile_rows(frames, row, j, cols):
    img, _, channels, _ = frames.shape
    flat = frames.reshape(img, img * channels, LANES)
    size = cols * channels
    end = min((j + 1) * size, img * channels)
    part = flat[pl.ds(row, 4), j * size : end, :]
    return part.reshape(4 * (end - j * size), LANES)


def encode_kernel(
    section,
    frames_far,
    w1t,
    w2t,
    lw_far,
    table,
    h1_far,
    s1_far,
    h2_far,
    s2_far,
    enc,
    s3,
    frames,
    lw,
    h1,
    s1,
    h2,
    s2,
    band,
    edge,
    band2,
    bias1,
    bias2,
    held,
    held2,
    sems,
):
    blocks, side = h1.shape[:2]
    steps = blocks // STEP
    tiles = frames.shape[1] // TILE
    k1, k2 = w1t.shape[0], w2t.shape[0]
    reach_rows = REACH * k1
    arrives = frame_copies(section, frames_far, frames, sems.at[0])
    for g in range(steps):
        arrives(g).start()
    last_copies = [
        pltpu.make_async_copy(lw_far, lw, sems.at[3, 0]),
        pltpu.make_async_copy(h2, h2_far, sems.at[3, 1]),
        pltpu.make_async_copy(s2, s2_far, sems.at[3, 2]),
    ]
    last_copies[0].start()

    def leaves(g):
        rows = pl.ds(g * STEP, STEP)
        return [
            pltpu.make_async_copy(h1.at[rows], h1_far.at[rows], sems.at[1, g]),
            pltpu.make_async_copy(s1.at[rows], s1_far.at[rows], sems.at[2, g]),
        ]

    inner = side // 2 - 1
    row_len = inner * k2
    two = 2 * k2 * 3

    def prepare():
        taps = pixel_order(w1t[...])
        edges = []
        for half in range(2):
            lines = [taps[:, 32 * (4 * half + u) : 32 * (4 * half + u + 1)] for u in range(4)]
            for place in range(REACH):
                pieces = []
                for line in lines:
                    start = 16 * (place - 1)
                    cut = line[:, max(0, -start) : min(32, 64 - start)]
                    start = max(start, 0)
                    pieces += [jnp.zeros((k1, start), F32)] if start else []
                    pieces.append(cut)
                    rest = 64 - start - cut.shape[1]
                    pieces += [jnp.zeros((k1, rest), F32)] if rest else []
                at = half * reach_rows + place * k1
                band[at : at + k1, :] = jnp.concatenate(pieces, axis=1).astype(BF16)
            edges.append(jnp.concatenate([line[:, 16:] for line in lines], axis=1))
        edge[...] = jnp.concatenate(edges, axis=0).astype(BF16)
        tap, pix = iota((256, LANES), 0), iota((256, LANES), 1)
        for half in range(2):
            for place in range(3):
                hit = (
                    ((tap & 15) == (pix & 15))
                    & ((tap >> 6) == (pix >> 6) + 2 * half)
                    & (((tap >> 4) & 3) == ((pix >> 4) & 3) + 2 - 2 * place)
                )
                at = (half * 3 + place) * k2
                taps = dot(w2t[...], hit.astype(F32).astype(BF16))
                band2[at : at + k2, :] = taps.astype(BF16)
        bias1[...] = jnp.broadcast_to(column(table[AT_B1, 0:k1]), bias1.shape)
        bias2[...] = jnp.broadcast_to(column(table[AT_B2, 0:k2]), bias2.shape)
        held[...] = jnp.zeros_like(held)
        held2[...] = jnp.zeros_like(held2)
        h1[...] = jnp.zeros_like(h1)

    def added(sums, x, value):
        sums[x] = sums[x] + value if x in sums else value

    def second_rows(b):
        tiles = [
            h1[pl.ds(2 * b + 1, 2), 4 * j : 4 * j + 4].reshape(LANES, LANES)
            for j in range(side // 4)
        ]
        got = dot(band2[...], jnp.concatenate(tiles, axis=1))
        low, high = {}, {}
        for j in range(side // 4):
            for place in range(3):
                x = 2 * j - 1 + place
                if 0 <= x < inner:
                    span = slice(j * LANES, (j + 1) * LANES)
                    at = place * k2
                    added(low, x, got[at : at + k2, span])
                    added(high, x, got[two // 2 + at : two // 2 + at + k2, span])
        row = jnp.maximum(b - 1, 0) * row_len
        for x in range(inner):
            value, slope = soft(held2[x] + high[x] + bias2[...])
            held2[x] = low[x]
            at = pl.ds(pl.multiple_of(row + x * k2, k2), k2)
            h2[at, :] = value.astype(BF16)
            s2[at, :] = slope.astype(BF16)

    def one_step(g, carry):
        def row(r):
            return pl.multiple_of(4 * (STEP * g + r), 4)

        arrives(g).wait()
        second_rows(jnp.maximum(g - 1, 0))

        last = dot(
            edge[...], jnp.concatenate([tile_rows(frames, row(r), tiles, TILE) for r in range(STEP)], axis=1)
        )
        odd = {}
        for r in range(STEP):
            low, high = {}, {}

            def place_tile(j, got):
                for place in range(REACH):
                    x = 4 * j - 1 + place
                    if 0 <= x < side:
                        at = place * k1
                        added(low, x, got[at : at + k1])
                        added(high, x, got[reach_rows + at : reach_rows + at + k1])

            if r not in odd:
                rows = [k for k in (r, r + 1) if k < STEP]
                cut = [tile_rows(frames, row(k), tiles - 1, TILE) for k in rows]
                got = dot(band[...], jnp.concatenate(cut, axis=1))
                odd.update({k: got[:, i * LANES : (i + 1) * LANES] for i, k in enumerate(rows)})
            place_tile(tiles - 1, odd[r])
            added(low, side - 1, last[:k1, r * LANES : (r + 1) * LANES])
            added(high, side - 1, last[k1:, r * LANES : (r + 1) * LANES])
            done = 0
            for j in range(0, tiles - 1, 2):
                cut = [tile_rows(frames, row(r), j + k, TILE) for k in range(2)]
                got = dot(band[...], jnp.concatenate(cut, axis=1))
                for k in range(2):
                    place_tile(j + k, got[:, k * LANES : (k + 1) * LANES])
                ready = side if j + 2 == tiles - 1 else 4 * j + 7
                for x in range(done, ready):
                    value, slope = soft(held[x] + high[x] + bias1[...])
                    held[x] = low[x]
                    value = value.astype(BF16)
                    h1[STEP * g + r, x] = value
                    s1[STEP * g + r, x] = slope.astype(BF16)
                done = ready
        for copy in leaves(g):
            copy.start()
        return carry

    prepare()
    lax.fori_loop(0, steps, one_step, 0)
    for b in range(steps - 1, side // 2):
        second_rows(b)
    for copy in last_copies[1:]:
        copy.start()
    last_copies[0].wait()
    value, slope = soft(dot_rows(lw[...], h2[...]) + column(table[AT_LB, :]))
    enc[...] = value.astype(BF16)
    s3[...] = slope
    for g in range(steps):
        for copy in leaves(g):
            copy.wait()
    for copy in last_copies[1:]:
        copy.wait()


def three_parts(row):
    high = row.astype(BF16).astype(F32)
    middle = (row - high).astype(BF16).astype(F32)
    return jnp.concatenate([high, middle, row - high - middle], axis=0)


def with_ones(value):
    return jnp.concatenate([value, ones_rows(value.shape[1])], axis=0)


def ones_rows(lanes):
    return (iota((16, lanes), 0) < 3).astype(F32).astype(BF16)


def plan_kernel(
    section,
    slots,
    enc,
    s3,
    h2,
    branch_far,
    value_w,
    table,
    keep,
    send,
    small,
    g3,
    parts,
    bwt,
    vht,
    vhw,
    ow,
    mine,
    pre,
    dbr,
    dval,
    low,
    hid,
    gb,
    h2_here,
    branch_w,
    sems,
    *,
    per_pair,
    depth,
):
    width = enc.shape[0]
    options = branch_w.shape[0]
    pairs = options // 2
    two = 2 * width
    sec = section[0]
    branch_copy = pltpu.make_async_copy(branch_far, branch_w, sems.at[0])
    branch_copy.start()
    h2_copy = pltpu.make_async_copy(h2, h2_here, sems.at[1])
    h2_copy.start()

    count = slots.shape[0]
    dest = jnp.concatenate(
        [table[AT_DEST + k : AT_DEST + k + 1, :] for k in range(count // LANES)], axis=1
    )
    own = jnp.where(sec == 0, dest[:, :LANES], dest[:, LANES:])
    others = jnp.transpose(jnp.broadcast_to(dest, (LANES, count)))
    index = iota((count, LANES), 1) + sec * LANES
    earlier = (others == own) & (iota((count, LANES), 0) < index)
    rank = jnp.sum(earlier.astype(F32), axis=0, keepdims=True)
    bucket = own * float(per_pair) + rank
    chosen = (iota((count, LANES), 0).astype(F32) == bucket).astype(F32)
    mine[...] = dot_rows(slots[...], chosen, EXACT)[: mine.shape[0]]

    pad = jnp.zeros((13, width), F32)
    branch_copy.wait()
    for o in range(options):
        rows = [branch_w[o].astype(F32), three_parts(table[o : o + 1, :]), pad]
        bwt[o * width : (o + 1) * width, :] = jnp.transpose(
            jnp.concatenate(rows, axis=0)
        ).astype(BF16)
    scalars = table[AT_SCALARS, :]
    head_w = table[AT_HW, :]
    rows = [value_w[...].astype(F32), three_parts(table[AT_VB, :]), pad]
    vht[0:width, :] = jnp.transpose(jnp.concatenate(rows, axis=0)).astype(BF16)
    vht[width:, :] = jnp.zeros((16, width + 16), BF16)
    lane = iota((1, 16), 1)
    for k in range(2):
        bias = three_parts(jnp.broadcast_to(scalars[:, 1 + k : 2 + k], (1, 16)))
        bias = sum(jnp.where(lane == j, bias[j : j + 1], 0.0) for j in range(3))
        vht[width + k : width + k + 1, 0:width] = head_w[k : k + 1].astype(BF16)
        vht[width + k : width + k + 1, width:] = bias.astype(BF16)
    vhw[:, 0:width] = value_w[...]
    vhw[:, width:] = jnp.transpose(
        jnp.concatenate([head_w, jnp.zeros((14, width), F32)], axis=0)
    ).astype(BF16)
    ow[...] = jnp.broadcast_to(column(table[AT_OW, :]), (width, LANES))
    wide_ow = jnp.concatenate([ow[...], ow[...]], axis=1)

    labels = iota((options, LANES), 0).astype(F32)
    state = enc[...].astype(F32)
    rounded_all, saved = [], []
    for level in range(depth):
        picked = labels == mine[level : level + 1, :]
        rounded = state.astype(BF16)
        rounded_all.append(rounded)
        pre[...] = dot(bwt[...], with_ones(rounded))
        following = state
        reward, discount, value = [], [], []
        for t in range(pairs):
            at = slice(t * two, (t + 1) * two)
            act, slope = silu_pair(pre[at, :])
            dbr[level, at, :] = slope
            left = state + act[:width]
            right = state + act[width:]
            following = jnp.where(picked[2 * t : 2 * t + 1], left, following)
            following = jnp.where(picked[2 * t + 1 : 2 * t + 2], right, following)
            both = with_ones(jnp.concatenate([left.astype(BF16), right.astype(BF16)], axis=1))
            low[level, t] = both
            got = dot(vht[...], both)
            act, slope = silu_pair(got[:width])
            dval[level, t] = slope
            hidden = act.astype(BF16)
            hid[level, t] = hidden
            worth = jnp.sum(hidden.astype(F32) * wide_ow, axis=0, keepdims=True)
            for k in range(2):
                span = slice(k * LANES, (k + 1) * LANES)
                value.append(worth[:, span])
                reward.append(got[width : width + 1, span])
                discount.append(got[width + 1 : width + 2, span])
        reward = jnp.concatenate(reward, axis=0)
        discount = jax.nn.sigmoid(jnp.concatenate(discount, axis=0))
        value = jnp.concatenate(value, axis=0) + scalars[:, 3:4]
        quality = reward + discount * value
        top = jnp.max(quality, axis=0, keepdims=True)
        shifted = jnp.exp(quality - top)
        total = jnp.sum(shifted, axis=0, keepdims=True)
        live = (mine[depth : depth + 1, :] > level).astype(F32)
        chosen = picked.astype(F32)

        def target(kind):
            at = depth + 1 + kind * depth + level
            return mine[at : at + 1, :]

        reward_gap = live * (jnp.sum(chosen * reward, axis=0, keepdims=True) - target(0))
        discount_gap = live * (jnp.sum(chosen * discount, axis=0, keepdims=True) - target(1))
        plan_gap = live * (top + jnp.log(total) - target(2))
        grad_quality = plan_gap * (shifted / total)
        head_two = (chosen * discount_gap + grad_quality * value) * discount * (1.0 - discount)
        saved.append(
            (
                picked,
                (chosen * reward_gap + grad_quality).astype(BF16).astype(F32),
                head_two.astype(BF16).astype(F32),
                (grad_quality * discount).astype(BF16).astype(F32),
                reward_gap * reward_gap + discount_gap * discount_gap + plan_gap * plan_gap,
            )
        )
        state = following

    out_sum = jnp.zeros((width, two), F32)
    value_sum = jnp.zeros((width + 16, width + 16), F32)
    grad_next = jnp.zeros((width, LANES), F32)
    line = iota((16, two), 0)
    for level in reversed(range(depth)):
        picked, head_one, head_two, grad_value, _ = saved[level]
        upward = jnp.zeros((width, LANES), F32)
        for t in range(pairs):
            at = slice(t * two, (t + 1) * two)

            def across(rows):
                return jnp.concatenate(
                    [rows[2 * t : 2 * t + 1], rows[2 * t + 1 : 2 * t + 2]], axis=1
                )

            worth = across(grad_value)
            grad_pre = (worth * wide_ow * dval[level, t]).astype(BF16)
            out_sum = out_sum + hid[level, t].astype(F32) * worth
            heads = jnp.where(line == 0, across(head_one), 0.0)
            heads = jnp.where(line == 1, across(head_two), heads)
            heads = jnp.where(line == 2, worth, heads)
            stacked = jnp.concatenate([grad_pre, heads.astype(BF16)], axis=0)
            value_sum = value_sum + dot_lanes(stacked, low[level, t])
            moved = dot(vhw[...], stacked)
            left = moved[:, :LANES] + jnp.where(picked[2 * t : 2 * t + 1], grad_next, 0.0)
            right = moved[:, LANES:] + jnp.where(picked[2 * t + 1 : 2 * t + 2], grad_next, 0.0)
            grad_branch = jnp.concatenate([left, right], axis=0) * dbr[level, at, :]
            grad_branch = grad_branch.astype(BF16)
            gb[level, at, :] = grad_branch
            weights = jnp.concatenate([branch_w[2 * t], branch_w[2 * t + 1]], axis=1)
            upward = upward + (left + right + dot(weights, grad_branch))
        grad_next = upward

    linear_rows = h2.shape[0]
    half = (linear_rows + options * width + width) // 2
    rest = linear_rows - half
    rounded = with_ones(jnp.concatenate(rounded_all, axis=1))
    small[...] = jnp.zeros_like(small)
    if half < keep.shape[0]:
        for k in range(2):
            parts[k, half:, :] = jnp.zeros((keep.shape[0] - half, LANES), BF16)
    for t in range(pairs):
        at = slice(t * two, (t + 1) * two)
        grads = jnp.concatenate([gb[level, at, :] for level in range(depth)], axis=1)
        got = dot_lanes(rounded, grads)
        for k in range(2):
            o = 2 * t + k
            span = slice(k * width, (k + 1) * width)
            rows = slice(rest + o * width, rest + (o + 1) * width)
            parts[1 - sec, rows, :] = got[:width, span].astype(BF16)
            small[o : o + 1, :] = got[width : width + 1, span]
    after = rest + options * width
    parts[1 - sec, after : after + width, :] = jnp.transpose(value_sum[:width, :width]).astype(BF16)

    grad_three = (grad_next.astype(BF16).astype(F32) * s3[...]).astype(BF16)
    g3[...] = grad_three
    h2_copy.wait()
    chunk = linear_rows // 9
    for i in range(8):
        at = slice(i * chunk, (i + 1) * chunk)
        parts[sec, at, :] = dot_lanes(h2_here[at, :], grad_three).astype(BF16)
    last = dot_lanes(h2_here[8 * chunk :, :], grad_three).astype(BF16)
    parts[sec, 8 * chunk : half, :] = last[: half - 8 * chunk]
    parts[1 - sec, 0:rest, :] = last[half - 8 * chunk :]
    keep[...] = parts[0]
    send[...] = parts[1]

    small[AT_VB, :] = row_of(value_sum[:width, width : width + 1])
    small[AT_OW, :] = row_of(jnp.sum(out_sum, axis=1, keepdims=True))
    small[AT_HW, :] = value_sum[width : width + 2, :width]
    small[AT_LB, :] = row_of(jnp.sum(grad_three.astype(F32), axis=1, keepdims=True))
    loss = 0.5 * jnp.sum(sum(kept[4] for kept in saved), axis=1, keepdims=True)
    ends = [loss] + [value_sum[width + k : width + k + 1, width : width + 1] for k in range(3)]
    lane = iota((1, LANES), 1)
    line = jnp.zeros((1, LANES), F32)
    for k, end in enumerate(ends):
        line = jnp.where(lane == k, end, line)
    small[AT_SCALARS, :] = line


def back_kernel(g3, lw, s2, s1, h1, w2t, g1_far, c2, sums, t2, g2, g1, sems):
    side, k1 = s1.shape[1], s1.shape[2]
    k2 = w2t.shape[0]
    inner = side // 2 - 1
    row_len = inner * k2
    tap, pix = iota((LANES, 256), 1), iota((LANES, 256), 0)
    for yrel in range(2):
        for p in range(3):
            hit = (
                ((tap & 15) == (pix & 15))
                & ((tap >> 6) == (pix >> 6) + 2 * (1 - yrel))
                & (((tap >> 4) & 3) == ((pix >> 4) & 3) + 2 - 2 * p)
            )
            at = (yrel * 3 + p) * k2
            t2[:, at : at + k2] = dot_lanes(hit.astype(F32).astype(BF16), w2t[...]).astype(BF16)
    g2[0] = jnp.zeros(g2.shape[1:], BF16)
    g2[inner + 1] = jnp.zeros(g2.shape[1:], BF16)
    g1[0] = jnp.zeros(g1.shape[1:], BF16)
    g1[side + 1] = jnp.zeros(g1.shape[1:], BF16)
    zero = jnp.zeros((k2, LANES), BF16)
    total_one = jnp.zeros((k1, LANES), F32)
    total_two = jnp.zeros((k2, LANES), F32)
    for y in range(inner):
        at = slice(y * row_len, (y + 1) * row_len)
        grad = dot(lw[at, :], g3[...]) * s2[at, :].astype(F32)
        grad = grad.astype(BF16).reshape(inner, k2, LANES)
        g2[y + 1] = grad
        total_two = total_two + jnp.sum(grad.astype(F32), axis=0)
    ends = (0, side // 2 + 1, side + 2)
    copies = [
        pltpu.make_async_copy(g1.at[a:b], g1_far.at[a:b], sems.at[k])
        for k, (a, b) in enumerate(zip(ends, ends[1:]))
    ]
    reach, cols = 5, 8
    total = jnp.zeros((2 * reach * k2, 2 * cols * k1), F32)
    grads, tiles = [], []
    for b in range(side // 2):
        cut = []
        for j in range(side // 4):
            pieces = []
            for yrel in range(2):
                for p in range(3):
                    x = 2 * j - 1 + p
                    pieces.append(g2[b + yrel, x] if 0 <= x < inner else zero)
            cut.append(jnp.concatenate(pieces, axis=0))
        got = dot(t2[...], jnp.concatenate(cut, axis=1))
        for u in range(2):
            for j in range(side // 4):
                part = got[u * 64 : (u + 1) * 64, j * LANES : (j + 1) * LANES]
                slope = s1[2 * b + u + 1, 4 * j : 4 * j + 4].astype(F32)
                grad = (part.reshape(4, k1, LANES) * slope).astype(BF16)
                g1[2 * b + u + 1, 4 * j : 4 * j + 4] = grad
                total_one = total_one + jnp.sum(grad.astype(F32), axis=0)
        if 2 * b + 3 == ends[1]:
            copies[0].start()
        for j in range(-(-side // cols)):
            end = min((j + 1) * cols, side)
            tile = h1[2 * b + 1 : 2 * b + 3, j * cols : end]
            if end < (j + 1) * cols:
                rest = jnp.zeros((2, (j + 1) * cols - end, k1, LANES), BF16)
                tile = jnp.concatenate([tile, rest], axis=1)
            tiles.append(tile.reshape(2 * cols * k1, LANES))
            pieces = []
            for half in range(2):
                for p in range(reach):
                    x = 4 * j - 1 + p
                    pieces.append(g2[b + 1 - half, x] if 0 <= x < inner else zero)
            grads.append(jnp.concatenate(pieces, axis=0))
        if b % 2:
            total = total + dot_lanes(
                jnp.concatenate(grads, axis=1), jnp.concatenate(tiles, axis=1)
            )
            grads, tiles = [], []
    copies[1].start()
    line = 4 * k1
    for half in range(2):
        for u in range(2):
            tap_row = jnp.zeros((k2, line), F32)
            for p in range(reach):
                at = (half * reach + p) * k2
                part = total[at : at + k2, u * 2 * line : (u + 1) * 2 * line]
                start = 2 * k1 * (p - 1)
                piece = part[:, max(start, 0) : min(start + line, 2 * line)]
                if start < 0:
                    piece = jnp.concatenate([jnp.zeros((k2, -start), F32), piece], axis=1)
                if start + line > 2 * line:
                    rest = jnp.zeros((k2, start - line), F32)
                    piece = jnp.concatenate([piece, rest], axis=1)
                tap_row = tap_row + piece
            at = (2 * half + u) * line
            c2[:, at : at + line] = tap_row
    sums[...] = jnp.zeros_like(sums)
    sums[0:1, 0:k1] = row_of(jnp.sum(total_one, axis=1, keepdims=True))
    sums[1:2, 0:k2] = row_of(jnp.sum(total_two, axis=1, keepdims=True))
    for copy in copies:
        copy.wait()


def pixel_band(sec, w1t, channels):
    k1 = w1t.shape[0]
    rows = 64 * channels
    row, tap = iota((rows, 256), 0), iota((rows, 256), 1)
    moves = ((tap >> 6) == row % channels + sec * channels) & ((tap & 63) == row // channels)
    taps = dot_lanes(moves.astype(F32).astype(BF16), w1t)
    line, span = COLS * channels, 8 * channels
    blocks = {}
    for half in range(2):
        for p in range(NEAR):
            pieces = []
            for u in range(4):
                at = (4 * half + u) * span
                start = 4 * (p - 1) * channels
                cut = taps[at + max(0, -start) : at + min(span, line - start)]
                start = max(start, 0)
                pieces += [jnp.zeros((start, k1), F32)] if start else []
                pieces.append(cut)
                rest = line - start - cut.shape[0]
                pieces += [jnp.zeros((rest, k1), F32)] if rest else []
            blocks[half, p] = jnp.concatenate(pieces, axis=0)
    zero = jnp.zeros((4 * line, k1), F32)
    lines = []
    for r in range(STEP):
        cols = [
            blocks.get((r + 1 - yrel, p), zero) for yrel in range(STEP + 1) for p in range(NEAR)
        ]
        lines.append(jnp.concatenate(cols, axis=1))
    return jnp.concatenate(lines, axis=0).astype(BF16)


def first_kernel(section, frames_far, g1_far, after, c1, frames, g1, acc, sems):
    side, k1 = g1.shape[1], g1.shape[2]
    img, _, channels, _ = frames.shape
    steps = img // 4 // STEP
    arrives = frame_copies(section, frames_far, frames, sems)
    g1_copy = pltpu.make_async_copy(g1_far, g1, sems.at[steps])
    arrives(0).start()
    g1_copy.start()
    for g in range(1, steps):
        arrives(g).start()
    acc[...] = jnp.zeros_like(acc)
    zero = jnp.zeros((k1, LANES), BF16)
    g1_copy.wait()

    def one_step(g, carry):
        arrives(g).wait()
        pixels, grads = [], []
        for j in range(img // COLS):
            rows = [pl.multiple_of(4 * (STEP * g + r), 4) for r in range(STEP)]
            pixels.append(
                jnp.concatenate([tile_rows(frames, row, j, COLS) for row in rows], axis=0)
            )
            pieces = []
            for yrel in range(STEP + 1):
                for p in range(NEAR):
                    x = 3 * j - 1 + p
                    pieces.append(g1[STEP * g + yrel, x] if 0 <= x < side else zero)
            grads.append(jnp.concatenate(pieces, axis=0))
        acc[...] += dot_lanes(jnp.concatenate(pixels, axis=1), jnp.concatenate(grads, axis=1))
        return carry

    lax.fori_loop(0, steps, one_step, 0)
    fold_first(acc, c1, channels, k1)


def fold_first(acc, c1, channels, k1):
    line = COLS * channels
    step = 4 * channels
    taps = []
    for half in range(2):
        total = sum(
            acc[r * 4 * line : (r + 1) * 4 * line, :][
                :, (r + 1 - half) * NEAR * k1 : (r + 2 - half) * NEAR * k1
            ]
            for r in range(STEP)
        )
        for u in range(4):
            part = total[u * line : (u + 1) * line]
            cols = [part[:, p * k1 : (p + 1) * k1] for p in range(NEAR)]
            taps.append(cols[1][0:step] + cols[2][step : 2 * step] + cols[3][2 * step :])
            taps.append(cols[0][0:step] + cols[1][step : 2 * step] + cols[2][2 * step :])
    row, col = iota((256, 256), 0), iota((256, 256), 1)
    moves = ((row & 3) == (col >> 6)) & ((row >> 2) == (col & 63))
    grad = dot_rows(jnp.concatenate(taps, axis=0), moves.astype(F32), EXACT)
    for half in range(2):
        c1[half * k1 : (half + 1) * k1, :] = grad[:, half * LANES : (half + 1) * LANES].astype(BF16)


def pixels_kernel(section, weights, mine_far, other_far, after, *refs, start, steps, begins):
    out, token, band_out, held, mine, other, sems = refs[-7:]
    side, k1 = mine.shape[1], mine.shape[2]
    rows = slice(STEP * start, STEP * (start + steps) + 1)
    fetches = [
        pltpu.make_async_copy(far.at[rows], here, sems.at[2, k])
        for k, (far, here) in enumerate(((mine_far, mine), (other_far, other)))
    ]
    for fetch in fetches:
        fetch.start()
    img, channels = out.shape[1], out.shape[2]
    sec = section[0]
    line = COLS * channels
    flat = held.reshape(2, 2, 4 * STEP, img * channels, LANES)
    if begins:
        band_out[...] = pixel_band(sec, weights[...], channels)
        band = band_out
    else:
        band = weights
        band_out[...] = jnp.zeros_like(band_out)
    token[...] = jnp.zeros_like(token)

    def writes(g):
        rows = slice(4 * STEP * (start + g), 4 * STEP * (start + g + 1))
        places = (sec * LANES, (1 - sec) * LANES)
        return [
            pltpu.make_async_copy(
                held.at[g % 2, k],
                out.at[rows, :, :, pl.ds(pl.multiple_of(places[k], LANES), LANES)],
                sems.at[g % 2, k],
            )
            for k in range(2)
        ]

    zero = jnp.zeros((k1, 2 * LANES), BF16)
    for fetch in fetches:
        fetch.wait()
    for g in range(steps):
        if g >= 2:
            for copy in writes(g - 2):
                copy.wait()
        for j in range(img // COLS):
            pieces = []
            for yrel in range(STEP + 1):
                for p in range(NEAR):
                    x, y = 3 * j - 1 + p, STEP * g + yrel
                    if 0 <= x < side:
                        pieces.append(jnp.concatenate([mine[y, x], other[y, x]], axis=1))
                    else:
                        pieces.append(zero)
            got = dot(band[...], jnp.concatenate(pieces, axis=0))
            for k in range(4 * STEP):
                at = slice(k * line, (k + 1) * line)
                span = slice(j * line, (j + 1) * line)
                flat[g % 2, 0, k, span, :] = got[at, :LANES]
                flat[g % 2, 1, k, span, :] = got[at, LANES:]
        for copy in writes(g):
            copy.start()
    for g in range(max(steps - 2, 0), steps):
        for copy in writes(g):
            copy.wait()


def two_parts(value):
    high = value.astype(BF16).astype(F32)
    return jnp.concatenate([high, value - high], axis=0).astype(BF16)


def one_part(pair):
    rows = pair.shape[0] // 2
    pair = pair.astype(F32)
    return pair[:rows] + pair[rows:]


def merge_kernel(keep, recv, small, c2, sums, out, lines):
    members = out.shape[0]
    size = keep.shape[0] // members
    k2 = c2.shape[0]
    lines[...] = jnp.zeros_like(lines)
    at = small.shape[0]
    lines[0:at, :] = small[...]
    for half in range(2):
        lines[at : at + k2, :] = c2[:, half * LANES : (half + 1) * LANES]
        at += k2
    lines[at : at + sums.shape[0], :] = sums[...]
    for k in range(members):
        at = slice(k * size, (k + 1) * size)
        out[k, 0:size, :] = (keep[at, :].astype(F32) + recv[at, :].astype(F32)).astype(BF16)
        out[k, size:, :] = two_parts(lines[k * SHORT : (k + 1) * SHORT, :])


def cube_kernel(got, c1, after, out):
    members = got.shape[0]
    size = got.shape[1] - 2 * SHORT
    out[0:size, :] = sum(got[k, 0:size, :].astype(F32) for k in range(members)).astype(BF16)
    total = sum(one_part(got[k, size:, :]) for k in range(members))
    out[size : size + 2 * SHORT, :] = two_parts(total)
    out[size + 2 * SHORT :, :] = c1[...]


def add_kernel(a, b, after, out):
    size = a.shape[0] - 2 * SHORT - 32
    spans = (slice(0, size), slice(size, size + 2 * SHORT), slice(size + 2 * SHORT, None))
    first, last = ((a[k, :].astype(F32) + b[k, :].astype(F32)).astype(BF16) for k in spans[::2])
    middle = two_parts(one_part(a[spans[1], :]) + one_part(b[spans[1], :]))
    for k in range(out.shape[0]):
        for span, part in zip(spans, (first, middle, last)):
            out[k, span, :] = part


def relay_kernel(got, after, out):
    out[...] = got[...]


def unpack_kernel(section, mine, other, *refs):
    loss, c1, b1, c2, b2, lw, lb, bw, bb, hw, hb, vw, vb, ow, ob, halves, lines = refs
    width = lw.shape[1]
    options = bw.shape[0]
    k1, k2 = c1.shape[0], c2.shape[0]
    linear_rows = lw.shape[0]
    sec = section[0]
    size = halves.shape[1] // CUBE
    half = (linear_rows + options * width + width) // 2
    rest = linear_rows - half
    grad = [jnp.zeros((k1, LANES), F32) for _ in range(2)]
    for k in range(CUBE):
        at = slice(k * size, (k + 1) * size)
        halves[sec, at, :] = mine[k, 0:size, :]
        halves[1 - sec, at, :] = other[k, 0:size, :]
        pair = slice(size, size + 2 * SHORT)
        at = slice(k * SHORT, (k + 1) * SHORT)
        lines[at, :] = one_part(mine[k, pair, :]) + one_part(other[k, pair, :])
        for ref in (mine, other):
            for h in range(2):
                at = size + 2 * SHORT + h * k1
                grad[h] += ref[k, at : at + k1, :].astype(F32)
    for part in range(2):
        c1[:, part * LANES : (part + 1) * LANES] = grad[part]
    lw[0:half, :] = halves[0, 0:half, :].astype(F32)
    lw[half:, :] = halves[1, 0:rest, :].astype(F32)
    for o in range(options):
        at = rest + o * width
        bw[o] = halves[1, at : at + width, :].astype(F32)
    at = rest + options * width
    vw[...] = halves[1, at : at + width, :].astype(F32)
    bb[...] = lines[0:options, :]
    vb[...] = lines[AT_VB, :]
    ow[...] = lines[AT_OW, :]
    hw[...] = lines[AT_HW, :]
    lb[...] = lines[AT_LB, :]
    scalars = lines[AT_SCALARS, :]
    loss[...] = scalars[:, 0:1]
    hb[...] = scalars[:, 1:3]
    ob[...] = scalars[:, 3:4]
    at = TABLE
    for part in range(2):
        c2[:, part * LANES : (part + 1) * LANES] = lines[at : at + k2, :]
        at += k2
    b1[...] = lines[at : at + 1, 0:k1]
    b2[...] = lines[at + 1 : at + 2, 0:k2]


def numbers_kernel(
    options,
    depth,
    targets,
    destination,
    b1,
    b2,
    lb,
    bb,
    hw,
    vb,
    ow,
    hb,
    ob,
    out,
    table,
):
    levels, kinds = options.shape[0], targets.shape[0]
    slots = depth.shape[1]
    rows = [options[...].astype(F32), depth[...].astype(F32)]
    rows += [targets[k] for k in range(kinds)]
    rows.append(jnp.zeros((LANES - levels - 1 - kinds * levels, slots), F32))
    out[...] = jnp.transpose(jnp.concatenate(rows, axis=0))
    table[...] = jnp.zeros_like(table)
    table[0 : bb.shape[0], :] = bb[...]
    table[AT_VB, :] = vb[...]
    table[AT_OW, :] = ow[...].astype(F32)
    table[AT_HW, :] = hw[...].astype(F32)
    table[AT_LB, :] = lb[...]
    table[AT_B1, 0 : b1.shape[1]] = b1[...]
    table[AT_B2, 0 : b2.shape[1]] = b2[...]
    lane = iota((1, LANES), 1)
    scalars = jnp.zeros((1, LANES), F32)
    for k, value in ((1, hb[:, 0:1]), (2, hb[:, 1:2]), (3, ob[...])):
        scalars = jnp.where(lane == k, value, scalars)
    table[AT_SCALARS, :] = scalars
    for k in range(slots // LANES):
        part = destination[:, k * LANES : (k + 1) * LANES]
        table[AT_DEST + k : AT_DEST + k + 1, :] = part.astype(F32)


def whole(shape):
    zeros = (0,) * len(shape)
    return pl.BlockSpec(shape, lambda *_: zeros)


ANYWHERE = pl.BlockSpec(memory_space=pl.ANY)
SCALARS = pl.BlockSpec(memory_space=pltpu.SMEM)


def params():
    return pltpu.CompilerParams(vmem_limit_bytes=VMEM_BYTES)


def shape_of(*shape, dtype=F32):
    return jax.ShapeDtypeStruct(shape, dtype)


def cost(microseconds):
    return pl.CostEstimate(
        flops=int(5e9 * microseconds), bytes_accessed=int(1.8e7 * microseconds), transcendentals=0
    )


def stays(value):
    return pltpu.with_memory_space_constraint(value, pltpu.HBM)


def encode(section, frames, w1t, w2t, lw, table):
    img = frames.shape[0]
    blocks = img // 4
    side = blocks - 1
    k1, k2, width = w1t.shape[0], w2t.shape[0], lw.shape[1]
    flat = lw.shape[0]
    vmem = pltpu.VMEM
    near = pl.BlockSpec(memory_space=vmem)
    grid_one = (blocks, side, k1, LANES)
    return pl.pallas_call(
        encode_kernel,
        in_specs=[SCALARS, ANYWHERE, near, near, ANYWHERE, near],
        out_specs=[ANYWHERE] * 4 + [near] * 2,
        out_shape=(
            pltpu.HBM(grid_one, BF16),
            pltpu.HBM(grid_one, BF16),
            pltpu.HBM((flat, LANES), BF16),
            pltpu.HBM((flat, LANES), BF16),
            shape_of(width, LANES, dtype=BF16),
            shape_of(width, LANES),
        ),
        scratch_shapes=[
            vmem((img, img, frames.shape[2], LANES), BF16),
            vmem(lw.shape, BF16),
            vmem(grid_one, BF16),
            vmem(grid_one, BF16),
            vmem((flat, LANES), BF16),
            vmem((flat, LANES), BF16),
            vmem((2 * REACH * k1, 256), BF16),
            vmem((2 * k1, 64), BF16),
            vmem((6 * k2, LANES), BF16),
            vmem((k1, LANES), F32),
            vmem((k2, LANES), F32),
            vmem((side, k1, LANES), F32),
            vmem((side // 2 - 1, k2, LANES), F32),
            pltpu.SemaphoreType.DMA((4, max(blocks // STEP, 3))),
        ],
        compiler_params=params(),
        cost_estimate=cost(9),
        name="encode",
    )(section, frames, w1t, w2t, lw, table)


def plan(section, slots, enc, s3, h2, branch_w, value_w, table, per_pair, depth, half_rows):
    width = enc.shape[0]
    options = branch_w.shape[0]
    two = 2 * width
    pairs = options // 2
    outs = (
        shape_of(half_rows, LANES, dtype=BF16),
        shape_of(half_rows, LANES, dtype=BF16),
        shape_of(TABLE, LANES),
        shape_of(width, LANES, dtype=BF16),
    )
    vmem = pltpu.VMEM
    near = pl.BlockSpec(memory_space=vmem)
    return pl.pallas_call(
        functools.partial(plan_kernel, per_pair=per_pair, depth=depth),
        in_specs=[SCALARS, near, near, near, ANYWHERE, ANYWHERE, near, near],
        out_shape=outs,
        scratch_shapes=[
            vmem((2, half_rows, LANES), BF16),
            vmem((options * width, width + 16), BF16),
            vmem((width + 16, width + 16), BF16),
            vmem((width, width + 16), BF16),
            vmem((width, LANES), F32),
            vmem((16, LANES), F32),
            vmem((options * width, LANES), F32),
            vmem((depth, options * width, LANES), F32),
            vmem((depth, pairs, width, two), F32),
            vmem((depth, pairs, width + 16, two), BF16),
            vmem((depth, pairs, width, two), BF16),
            vmem((depth, options * width, LANES), BF16),
            vmem(h2.shape, BF16),
            vmem(branch_w.shape, BF16),
            pltpu.SemaphoreType.DMA((2,)),
        ],
        compiler_params=params(),
        cost_estimate=cost(11),
        name="plan",
    )(section, slots, enc, s3, h2, branch_w, value_w, table)


def back(g3, lw, s2, s1, h1, w2t):
    _, side, k1 = s1.shape[:3]
    k2 = w2t.shape[0]
    inner = side // 2 - 1
    padded = (side + 2, side, k1, LANES)
    near = pl.BlockSpec(memory_space=pltpu.VMEM)
    return pl.pallas_call(
        back_kernel,
        in_specs=[near] * 6,
        out_specs=[ANYWHERE, near, near],
        out_shape=(pltpu.HBM(padded, BF16), shape_of(k2, 256), shape_of(8, LANES)),
        scratch_shapes=[
            pltpu.VMEM((LANES, 6 * k2), BF16),
            pltpu.VMEM((inner + 2, inner, k2, LANES), BF16),
            pltpu.VMEM(padded, BF16),
            pltpu.SemaphoreType.DMA((2,)),
        ],
        compiler_params=params(),
        cost_estimate=cost(5),
        name="back",
    )(g3, lw, s2, s1, h1, w2t)


def first(section, frames, g1, after):
    img, _, channels, _ = frames.shape
    k1 = g1.shape[2]
    return pl.pallas_call(
        first_kernel,
        in_specs=[SCALARS, ANYWHERE, ANYWHERE, ANYWHERE],
        out_shape=shape_of(2 * k1, LANES, dtype=BF16),
        scratch_shapes=[
            pltpu.VMEM((img, img, channels, LANES), BF16),
            pltpu.VMEM(g1.shape, BF16),
            pltpu.VMEM((STEP * 4 * COLS * channels, (STEP + 1) * NEAR * k1), F32),
            pltpu.SemaphoreType.DMA((img // 4 // STEP + 1,)),
        ],
        compiler_params=params(),
        cost_estimate=cost(9),
        name="first",
    )(section, frames, g1, after)


def pixels(section, weights, mine, other, shape, start, steps, after, done=None):
    img, _, channels, _ = shape
    k1 = mine.shape[2]
    band = (STEP * 4 * COLS * channels, (STEP + 1) * NEAR * k1)
    near = pl.BlockSpec(memory_space=pltpu.VMEM)
    operands = (section, weights, mine, other, after)
    specs = [SCALARS, near, ANYWHERE, ANYWHERE, ANYWHERE]
    window = pltpu.VMEM((STEP * steps + 1,) + mine.shape[1:], BF16)
    aliases = {}
    if done is not None:
        aliases = {len(operands): 0}
        operands += (done,)
        specs.append(ANYWHERE)
    outs = [shape_of(*shape), shape_of(8, LANES), shape_of(*band, dtype=BF16)]
    return pl.pallas_call(
        functools.partial(pixels_kernel, start=start, steps=steps, begins=done is None),
        in_specs=specs,
        out_specs=[ANYWHERE, near, near],
        out_shape=outs,
        scratch_shapes=[
            pltpu.VMEM((2, 2, 4 * STEP, img, channels, LANES), F32),
            window,
            window,
            pltpu.SemaphoreType.DMA((3, 2)),
        ],
        input_output_aliases=aliases,
        compiler_params=params(),
        cost_estimate=cost(2 + 0.8 * steps),
        name="pixels",
    )(*operands)


def small_call(
    kernel, outs, operands, scratch=(), name=None, place=None, after=(), weight=0.3
):
    specs = [pl.BlockSpec(memory_space=pltpu.VMEM)] * len(operands)
    if place is not None:
        operands = (*place, *operands)
        specs = [pl.BlockSpec(memory_space=pltpu.SMEM)] * len(place) + specs
    return pl.pallas_call(
        kernel,
        in_specs=specs + [ANYWHERE] * len(after),
        out_shape=outs,
        scratch_shapes=list(scratch),
        compiler_params=params(),
        cost_estimate=cost(weight),
        name=name,
    )(*operands, *after)


def round_up(value, step):
    return -(-value // step) * step


def swapped(value):
    return lax.ppermute(value, "section", [(0, 1), (1, 0)])


def exchanged(value, groups=None):
    return lax.all_to_all(
        value, "batch", split_axis=0, concat_axis=0, axis_index_groups=groups, tiled=True
    )


def partner(value, distance):
    count = lax.axis_size("batch")
    return lax.ppermute(value, "batch", [(b, b ^ distance) for b in range(count)])


def local(
    frames,
    destination,
    options,
    depth,
    targets,
    conv_one,
    bias_one,
    conv_two,
    bias_two,
    linear_w,
    linear_b,
    branch_w,
    branch_b,
    head_w,
    head_b,
    value_w,
    value_b,
    out_w,
    out_b,
):
    section = lax.axis_index("section").astype(jnp.int32)[None]
    peers = lax.axis_size("batch")
    frame_count = frames.shape[3]
    per_pair = frame_count // peers
    levels = options.shape[0]
    frames = stays(frames.transpose(1, 2, 0, 3))
    w1t, w2t = stays(conv_one.T), stays(conv_two.T)
    branch_w, value_w = stays(branch_w), stays(value_w)
    encoder_params = (w1t, bias_one, w2t, bias_two, linear_w, linear_b)
    planner_params = (branch_w, branch_b, head_w.T, head_b, value_w, value_b, out_w.T, out_b)
    width = linear_w.shape[1]
    big_rows = linear_w.shape[0] + (branch_w.shape[0] + 1) * width
    size = round_up(-(-big_rows // (2 * CUBE)), 16)

    tiny = (bias_one, bias_two, linear_b, branch_b, head_w.T, value_b, out_w.T)
    tiny = [stays(v if v.ndim > 1 else v[None, :]) for v in tiny]
    numbers, table = pl.pallas_call(
        numbers_kernel,
        in_specs=[pl.BlockSpec(memory_space=pltpu.VMEM)] * (6 + len(tiny)),
        out_shape=[shape_of(frame_count, LANES), shape_of(TABLE, LANES)],
        compiler_params=params(),
        cost_estimate=cost(1),
        name="numbers",
    )(
        stays(options),
        stays(depth[None, :]),
        stays(targets),
        stays(destination[None, :]),
        *tiny,
        stays(head_b[None, :]),
        out_b[None, :],
    )
    slots = exchanged(numbers.reshape(peers, per_pair, LANES)).reshape(frame_count, LANES)

    h1, s1, h2, s2, enc, s3 = encode(section, frames, w1t, w2t, stays(linear_w), table)
    h2 = stays(h2)
    keep, send, small, g3 = plan(
        section, slots, enc, s3, h2, branch_w, value_w, table, per_pair, levels, CUBE * size
    )
    recv = swapped(send)
    channels = frames.shape[2] // lax.axis_size("section")
    g1, c2, sums = back(g3, linear_w, s2, s1, h1, w2t)
    other = swapped(g1)
    g1 = stays(g1)
    cubes = [list(range(c, c + CUBE)) for c in range(0, peers, CUBE)]
    bf16 = functools.partial(shape_of, dtype=BF16)
    pieces = small_call(
        merge_kernel,
        bf16(CUBE, size + 2 * SHORT, LANES),
        (keep, recv, small, c2, sums),
        [pltpu.VMEM((CUBE * SHORT, LANES), F32)],
        name="merge",
    )
    got = exchanged(pieces, cubes)
    c1 = first(section, frames, g1, pieces)
    img = frames.shape[0]
    steps = img // 4 // STEP
    draw = functools.partial(
        pixels, section, mine=g1, other=other, shape=(img, img, channels, 2 * LANES)
    )
    frames_grad, token, band = draw(weights=w1t, start=0, steps=1, after=c1)
    piece = bf16(1, size + 2 * SHORT + c1.shape[0], LANES)
    keep = small_call(cube_kernel, bf16(*piece.shape[1:]), (got, c1), name="cube", after=(token,))
    distance = CUBE
    while distance < peers:
        recv = partner(keep, distance)
        if distance == CUBE:
            frames_grad, token, _ = draw(
                weights=band, start=1, steps=1, after=keep, done=frames_grad
            )
        distance *= 2
        copies = 1 if distance < peers else CUBE
        keep = small_call(
            add_kernel,
            bf16(copies, *piece.shape[1:]),
            (keep, recv),
            name="add",
            after=(token,),
        )
        keep = keep[0] if copies == 1 else keep
    got = exchanged(keep, cubes)
    frames_grad, token, _ = draw(
        weights=band, start=2, steps=steps - 2, after=keep, done=frames_grad
    )
    got = small_call(relay_kernel, bf16(*got.shape), (got,), name="relay", after=(token,))
    shapes = [p.shape for p in encoder_params + planner_params]
    flat = [s if len(s) > 1 else (1,) + s for s in shapes]
    rest = small_call(
        unpack_kernel,
        [shape_of(1, 1)] + [shape_of(*s) for s in flat],
        (got, swapped(got)),
        [
            pltpu.VMEM((2, CUBE * size, LANES), BF16),
            pltpu.VMEM((CUBE * SHORT, LANES), F32),
        ],
        name="unpack",
        place=(section,),
    )
    rest = [v.reshape(s) for v, s in zip(rest, [()] + shapes)]
    for at in (1, 3, 9, 13):
        rest[at] = rest[at].T
    return (rest[0], frames_grad.transpose(2, 0, 1, 3), *rest[1:])


def solution(mesh):
    placed = (
        P(None, None, None, "batch"),
        P("batch"),
        P(None, "batch"),
        P("batch"),
        P(None, None, "batch"),
    ) + (P(),) * 14
    return jax.shard_map(
        local,
        mesh=mesh,
        in_specs=placed,
        out_specs=(P(), P("section", None, None, "batch")) + (P(),) * 14,
        check_vma=False,
    )
```

```python
import functools
import math

import jax
import jax.numpy as jnp
from jax import lax
from jax.experimental import pallas as pl
from jax.experimental.pallas import tpu as pltpu
from jax.sharding import PartitionSpec as P

BF16 = jnp.bfloat16
F32 = jnp.float32
EXACT = lax.Precision.HIGHEST
LANES = 128
VMEM_BYTES = 32 * 1024 * 1024
TILE = 16
REACH = 5
STEP = 3
COLS = 12
NEAR = 4
AT_VB, AT_OW, AT_HW, AT_LB, AT_SCALARS, AT_B1, AT_B2, AT_DEST = (
    slice(18, 19),
    slice(19, 20),
    slice(20, 22),
    slice(22, 23),
    slice(23, 24),
    slice(24, 25),
    slice(25, 26),
    26,
)
TABLE = 32
CUBE = 8
SHORT = 16


def dot(a, b, precision=None):
    return jnp.dot(a, b, preferred_element_type=F32, precision=precision)


def dot_rows(a, b, precision=None):
    return lax.dot_general(
        a, b, (((0,), (0,)), ((), ())), preferred_element_type=F32, precision=precision
    )


def dot_lanes(a, b, precision=None):
    return lax.dot_general(
        a, b, (((1,), (1,)), ((), ())), preferred_element_type=F32, precision=precision
    )


def iota(shape, axis):
    return lax.broadcasted_iota(jnp.int32, shape, axis)


def column(row):
    n = row.shape[1]
    wide = jnp.broadcast_to(row, (n, n))
    return jnp.sum(jnp.where(iota((n, n), 0) == iota((n, n), 1), wide, 0.0), axis=1, keepdims=True)


def row_of(col):
    n = col.shape[0]
    wide = jnp.broadcast_to(col, (n, n))
    return jnp.sum(jnp.where(iota((n, n), 0) == iota((n, n), 1), wide, 0.0), axis=0, keepdims=True)


def soft(x):
    t = jnp.tanh(0.5 * x)
    return jnp.maximum(x, 0.0) - jnp.log(0.5 + 0.5 * jnp.abs(t)), 0.5 + 0.5 * t


def silu_pair(x):
    s = 0.5 + 0.5 * jnp.tanh(0.5 * x)
    act = x * s
    return act, s + act * (1.0 - s)


def pixel_order(w1t):
    tap, pix = iota((256, 256), 0), iota((256, 256), 1)
    moves = ((tap >> 6) == (pix & 3)) & ((tap & 63) == (pix >> 2))
    return dot(w1t, moves.astype(F32).astype(BF16))


def frame_copies(section, far, here, sems):
    lanes = pl.ds(pl.multiple_of(section[0] * LANES, LANES), LANES)
    size = 4 * STEP

    def copy(g):
        rows = pl.ds(pl.multiple_of(g * size, size), size)
        return pltpu.make_async_copy(far.at[rows, :, :, lanes], here.at[rows], sems.at[g])

    return copy


def tile_rows(frames, row, j, cols):
    img, _, channels, _ = frames.shape
    flat = frames.reshape(img, img * channels, LANES)
    size = cols * channels
    end = min((j + 1) * size, img * channels)
    part = flat[pl.ds(row, 4), j * size : end, :]
    return part.reshape(4 * (end - j * size), LANES)


def encode_kernel(
    section,
    frames_far,
    w1t,
    w2t,
    lw_far,
    table,
    h1_far,
    s1_far,
    s2_far,
    h2,
    enc,
    s3,
    frames,
    lw,
    h1,
    s1,
    s2,
    band,
    edge,
    band2,
    bias1,
    bias2,
    held,
    held2,
    sems,
):
    blocks, side = h1.shape[:2]
    steps = blocks // STEP
    tiles = frames.shape[1] // TILE
    k1, k2 = w1t.shape[0], w2t.shape[0]
    reach_rows = REACH * k1
    arrives = frame_copies(section, frames_far, frames, sems.at[0])
    for g in range(steps):
        arrives(g).start()
    last_copies = [
        pltpu.make_async_copy(lw_far, lw, sems.at[3, 0]),
        pltpu.make_async_copy(s2, s2_far, sems.at[3, 1]),
    ]
    last_copies[0].start()

    def leaves(g):
        rows = pl.ds(g * STEP, STEP)
        return [
            pltpu.make_async_copy(h1.at[rows], h1_far.at[rows], sems.at[1, g]),
            pltpu.make_async_copy(s1.at[rows], s1_far.at[rows], sems.at[2, g]),
        ]

    inner = side // 2 - 1
    row_len = inner * k2
    two = 2 * k2 * 3

    def prepare():
        taps = pixel_order(w1t[...])
        edges = []
        for half in range(2):
            lines = [taps[:, 32 * (4 * half + u) : 32 * (4 * half + u + 1)] for u in range(4)]
            for place in range(REACH):
                pieces = []
                for line in lines:
                    start = 16 * (place - 1)
                    cut = line[:, max(0, -start) : min(32, 64 - start)]
                    start = max(start, 0)
                    pieces += [jnp.zeros((k1, start), F32)] if start else []
                    pieces.append(cut)
                    rest = 64 - start - cut.shape[1]
                    pieces += [jnp.zeros((k1, rest), F32)] if rest else []
                at = half * reach_rows + place * k1
                band[at : at + k1, :] = jnp.concatenate(pieces, axis=1).astype(BF16)
            edges.append(jnp.concatenate([line[:, 16:] for line in lines], axis=1))
        edge[...] = jnp.concatenate(edges, axis=0).astype(BF16)
        tap, pix = iota((256, LANES), 0), iota((256, LANES), 1)
        for half in range(2):
            for place in range(3):
                hit = (
                    ((tap & 15) == (pix & 15))
                    & ((tap >> 6) == (pix >> 6) + 2 * half)
                    & (((tap >> 4) & 3) == ((pix >> 4) & 3) + 2 - 2 * place)
                )
                at = (half * 3 + place) * k2
                taps = dot(w2t[...], hit.astype(F32).astype(BF16))
                band2[at : at + k2, :] = taps.astype(BF16)
        bias1[...] = jnp.broadcast_to(column(table[AT_B1, 0:k1]), bias1.shape)
        bias2[...] = jnp.broadcast_to(column(table[AT_B2, 0:k2]), bias2.shape)
        held[...] = jnp.zeros_like(held)
        held2[...] = jnp.zeros_like(held2)
        h1[...] = jnp.zeros_like(h1)

    def added(sums, x, value):
        sums[x] = sums[x] + value if x in sums else value

    def second_rows(b):
        tiles = [
            h1[pl.ds(2 * b + 1, 2), 4 * j : 4 * j + 4].reshape(LANES, LANES)
            for j in range(side // 4)
        ]
        got = dot(band2[...], jnp.concatenate(tiles, axis=1))
        low, high = {}, {}
        for j in range(side // 4):
            for place in range(3):
                x = 2 * j - 1 + place
                if 0 <= x < inner:
                    span = slice(j * LANES, (j + 1) * LANES)
                    at = place * k2
                    added(low, x, got[at : at + k2, span])
                    added(high, x, got[two // 2 + at : two // 2 + at + k2, span])
        row = jnp.maximum(b - 1, 0) * row_len
        for x in range(inner):
            value, slope = soft(held2[x] + high[x] + bias2[...])
            held2[x] = low[x]
            at = pl.ds(pl.multiple_of(row + x * k2, k2), k2)
            h2[at, :] = value.astype(BF16)
            s2[at, :] = slope.astype(BF16)

    def one_step(g, carry):
        def row(r):
            return pl.multiple_of(4 * (STEP * g + r), 4)

        arrives(g).wait()
        second_rows(jnp.maximum(g - 1, 0))

        last = dot(
            edge[...], jnp.concatenate([tile_rows(frames, row(r), tiles, TILE) for r in range(STEP)], axis=1)
        )
        odd = {}
        for r in range(STEP):
            low, high = {}, {}

            def place_tile(j, got):
                for place in range(REACH):
                    x = 4 * j - 1 + place
                    if 0 <= x < side:
                        at = place * k1
                        added(low, x, got[at : at + k1])
                        added(high, x, got[reach_rows + at : reach_rows + at + k1])

            if r not in odd:
                rows = [k for k in (r, r + 1) if k < STEP]
                cut = [tile_rows(frames, row(k), tiles - 1, TILE) for k in rows]
                got = dot(band[...], jnp.concatenate(cut, axis=1))
                odd.update({k: got[:, i * LANES : (i + 1) * LANES] for i, k in enumerate(rows)})
            place_tile(tiles - 1, odd[r])
            added(low, side - 1, last[:k1, r * LANES : (r + 1) * LANES])
            added(high, side - 1, last[k1:, r * LANES : (r + 1) * LANES])
            done = 0
            for j in range(0, tiles - 1, 2):
                cut = [tile_rows(frames, row(r), j + k, TILE) for k in range(2)]
                got = dot(band[...], jnp.concatenate(cut, axis=1))
                for k in range(2):
                    place_tile(j + k, got[:, k * LANES : (k + 1) * LANES])
                ready = side if j + 2 == tiles - 1 else 4 * j + 7
                for x in range(done, ready):
                    value, slope = soft(held[x] + high[x] + bias1[...])
                    held[x] = low[x]
                    value = value.astype(BF16)
                    h1[STEP * g + r, x] = value
                    s1[STEP * g + r, x] = slope.astype(BF16)
                done = ready
        for copy in leaves(g):
            copy.start()
        return carry

    prepare()
    lax.fori_loop(0, steps, one_step, 0)
    for b in range(steps - 1, side // 2):
        second_rows(b)
    for copy in last_copies[1:]:
        copy.start()
    last_copies[0].wait()
    value, slope = soft(dot_rows(lw[...], h2[...]) + column(table[AT_LB, :]))
    enc[...] = value.astype(BF16)
    s3[...] = slope
    for g in range(steps):
        for copy in leaves(g):
            copy.wait()
    for copy in last_copies[1:]:
        copy.wait()


def three_parts(row):
    high = row.astype(BF16).astype(F32)
    middle = (row - high).astype(BF16).astype(F32)
    return jnp.concatenate([high, middle, row - high - middle], axis=0)


def with_ones(value):
    return jnp.concatenate([value, ones_rows(value.shape[1])], axis=0)


def ones_rows(lanes):
    return (iota((16, lanes), 0) < 3).astype(F32).astype(BF16)


def plan_kernel(
    section,
    slots,
    enc,
    s3,
    h2,
    branch_far,
    value_w,
    table,
    keep,
    send,
    small,
    g3,
    parts,
    bwt,
    vht,
    vhw,
    ow,
    mine,
    pre,
    dbr,
    dval,
    low,
    hid,
    gb,
    branch_w,
    sem,
    *,
    per_pair,
    depth,
):
    width = enc.shape[0]
    options = branch_w.shape[0]
    pairs = options // 2
    two = 2 * width
    sec = section[0]
    branch_copy = pltpu.make_async_copy(branch_far, branch_w, sem)
    branch_copy.start()

    count = slots.shape[0]
    dest = jnp.concatenate(
        [table[AT_DEST + k : AT_DEST + k + 1, :] for k in range(count // LANES)], axis=1
    )
    own = jnp.where(sec == 0, dest[:, :LANES], dest[:, LANES:])
    others = jnp.transpose(jnp.broadcast_to(dest, (LANES, count)))
    index = iota((count, LANES), 1) + sec * LANES
    earlier = (others == own) & (iota((count, LANES), 0) < index)
    rank = jnp.sum(earlier.astype(F32), axis=0, keepdims=True)
    bucket = own * float(per_pair) + rank
    chosen = (iota((count, LANES), 0).astype(F32) == bucket).astype(F32)
    mine[...] = dot_rows(slots[...], chosen, EXACT)[: mine.shape[0]]

    pad = jnp.zeros((13, width), F32)
    branch_copy.wait()
    for o in range(options):
        rows = [branch_w[o].astype(F32), three_parts(table[o : o + 1, :]), pad]
        bwt[o * width : (o + 1) * width, :] = jnp.transpose(
            jnp.concatenate(rows, axis=0)
        ).astype(BF16)
    scalars = table[AT_SCALARS, :]
    head_w = table[AT_HW, :]
    rows = [value_w[...].astype(F32), three_parts(table[AT_VB, :]), pad]
    vht[0:width, :] = jnp.transpose(jnp.concatenate(rows, axis=0)).astype(BF16)
    vht[width:, :] = jnp.zeros((16, width + 16), BF16)
    lane = iota((1, 16), 1)
    for k in range(2):
        bias = three_parts(jnp.broadcast_to(scalars[:, 1 + k : 2 + k], (1, 16)))
        bias = sum(jnp.where(lane == j, bias[j : j + 1], 0.0) for j in range(3))
        vht[width + k : width + k + 1, 0:width] = head_w[k : k + 1].astype(BF16)
        vht[width + k : width + k + 1, width:] = bias.astype(BF16)
    vhw[:, 0:width] = value_w[...]
    vhw[:, width:] = jnp.transpose(
        jnp.concatenate([head_w, jnp.zeros((14, width), F32)], axis=0)
    ).astype(BF16)
    ow[...] = jnp.broadcast_to(column(table[AT_OW, :]), (width, LANES))
    wide_ow = jnp.concatenate([ow[...], ow[...]], axis=1)

    labels = iota((options, LANES), 0).astype(F32)
    state = enc[...].astype(F32)
    rounded_all, saved = [], []
    for level in range(depth):
        picked = labels == mine[level : level + 1, :]
        rounded = state.astype(BF16)
        rounded_all.append(rounded)
        pre[...] = dot(bwt[...], with_ones(rounded))
        following = state
        reward, discount, value = [], [], []
        for t in range(pairs):
            at = slice(t * two, (t + 1) * two)
            act, slope = silu_pair(pre[at, :])
            dbr[level, at, :] = slope
            left = state + act[:width]
            right = state + act[width:]
            following = jnp.where(picked[2 * t : 2 * t + 1], left, following)
            following = jnp.where(picked[2 * t + 1 : 2 * t + 2], right, following)
            both = with_ones(jnp.concatenate([left.astype(BF16), right.astype(BF16)], axis=1))
            low[level, t] = both
            got = dot(vht[...], both)
            act, slope = silu_pair(got[:width])
            dval[level, t] = slope
            hidden = act.astype(BF16)
            hid[level, t] = hidden
            worth = jnp.sum(hidden.astype(F32) * wide_ow, axis=0, keepdims=True)
            for k in range(2):
                span = slice(k * LANES, (k + 1) * LANES)
                value.append(worth[:, span])
                reward.append(got[width : width + 1, span])
                discount.append(got[width + 1 : width + 2, span])
        reward = jnp.concatenate(reward, axis=0)
        discount = jax.nn.sigmoid(jnp.concatenate(discount, axis=0))
        value = jnp.concatenate(value, axis=0) + scalars[:, 3:4]
        quality = reward + discount * value
        top = jnp.max(quality, axis=0, keepdims=True)
        shifted = jnp.exp(quality - top)
        total = jnp.sum(shifted, axis=0, keepdims=True)
        live = (mine[depth : depth + 1, :] > level).astype(F32)
        chosen = picked.astype(F32)

        def target(kind):
            at = depth + 1 + kind * depth + level
            return mine[at : at + 1, :]

        reward_gap = live * (jnp.sum(chosen * reward, axis=0, keepdims=True) - target(0))
        discount_gap = live * (jnp.sum(chosen * discount, axis=0, keepdims=True) - target(1))
        plan_gap = live * (top + jnp.log(total) - target(2))
        grad_quality = plan_gap * (shifted / total)
        head_two = (chosen * discount_gap + grad_quality * value) * discount * (1.0 - discount)
        saved.append(
            (
                picked,
                (chosen * reward_gap + grad_quality).astype(BF16).astype(F32),
                head_two.astype(BF16).astype(F32),
                (grad_quality * discount).astype(BF16).astype(F32),
                reward_gap * reward_gap + discount_gap * discount_gap + plan_gap * plan_gap,
            )
        )
        state = following

    out_sum = jnp.zeros((width, two), F32)
    value_sum = jnp.zeros((width + 16, width + 16), F32)
    grad_next = jnp.zeros((width, LANES), F32)
    line = iota((16, two), 0)
    for level in reversed(range(depth)):
        picked, head_one, head_two, grad_value, _ = saved[level]
        upward = jnp.zeros((width, LANES), F32)
        for t in range(pairs):
            at = slice(t * two, (t + 1) * two)

            def across(rows):
                return jnp.concatenate(
                    [rows[2 * t : 2 * t + 1], rows[2 * t + 1 : 2 * t + 2]], axis=1
                )

            worth = across(grad_value)
            grad_pre = (worth * wide_ow * dval[level, t]).astype(BF16)
            out_sum = out_sum + hid[level, t].astype(F32) * worth
            heads = jnp.where(line == 0, across(head_one), 0.0)
            heads = jnp.where(line == 1, across(head_two), heads)
            heads = jnp.where(line == 2, worth, heads)
            stacked = jnp.concatenate([grad_pre, heads.astype(BF16)], axis=0)
            value_sum = value_sum + dot_lanes(stacked, low[level, t])
            moved = dot(vhw[...], stacked)
            left = moved[:, :LANES] + jnp.where(picked[2 * t : 2 * t + 1], grad_next, 0.0)
            right = moved[:, LANES:] + jnp.where(picked[2 * t + 1 : 2 * t + 2], grad_next, 0.0)
            grad_branch = jnp.concatenate([left, right], axis=0) * dbr[level, at, :]
            grad_branch = grad_branch.astype(BF16)
            gb[level, at, :] = grad_branch
            weights = jnp.concatenate([branch_w[2 * t], branch_w[2 * t + 1]], axis=1)
            upward = upward + (left + right + dot(weights, grad_branch))
        grad_next = upward

    linear_rows = h2.shape[0]
    half = (linear_rows + options * width + width) // 2
    rest = linear_rows - half
    rounded = with_ones(jnp.concatenate(rounded_all, axis=1))
    small[...] = jnp.zeros_like(small)
    if half < keep.shape[0]:
        for k in range(2):
            parts[k, half:, :] = jnp.zeros((keep.shape[0] - half, LANES), BF16)
    for t in range(pairs):
        at = slice(t * two, (t + 1) * two)
        grads = jnp.concatenate([gb[level, at, :] for level in range(depth)], axis=1)
        got = dot_lanes(rounded, grads)
        for k in range(2):
            o = 2 * t + k
            span = slice(k * width, (k + 1) * width)
            rows = slice(rest + o * width, rest + (o + 1) * width)
            parts[1 - sec, rows, :] = got[:width, span].astype(BF16)
            small[o : o + 1, :] = got[width : width + 1, span]
    after = rest + options * width
    parts[1 - sec, after : after + width, :] = jnp.transpose(value_sum[:width, :width]).astype(BF16)

    grad_three = (grad_next.astype(BF16).astype(F32) * s3[...]).astype(BF16)
    g3[...] = grad_three
    chunk = linear_rows // 9
    for i in range(8):
        at = slice(i * chunk, (i + 1) * chunk)
        parts[sec, at, :] = dot_lanes(h2[at, :], grad_three).astype(BF16)
    last = dot_lanes(h2[8 * chunk :, :], grad_three).astype(BF16)
    parts[sec, 8 * chunk : half, :] = last[: half - 8 * chunk]
    parts[1 - sec, 0:rest, :] = last[half - 8 * chunk :]
    keep[...] = parts[0]
    send[...] = parts[1]

    small[AT_VB, :] = row_of(value_sum[:width, width : width + 1])
    small[AT_OW, :] = row_of(jnp.sum(out_sum, axis=1, keepdims=True))
    small[AT_HW, :] = value_sum[width : width + 2, :width]
    small[AT_LB, :] = row_of(jnp.sum(grad_three.astype(F32), axis=1, keepdims=True))
    loss = 0.5 * jnp.sum(sum(kept[4] for kept in saved), axis=1, keepdims=True)
    ends = [loss] + [value_sum[width + k : width + k + 1, width : width + 1] for k in range(3)]
    lane = iota((1, LANES), 1)
    line = jnp.zeros((1, LANES), F32)
    for k, end in enumerate(ends):
        line = jnp.where(lane == k, end, line)
    small[AT_SCALARS, :] = line


def back_kernel(g3, lw, s2, s1, h1, w2t, g1_far, c2, sums, t2, g2, g1, sems):
    side, k1 = s1.shape[1], s1.shape[2]
    k2 = w2t.shape[0]
    inner = side // 2 - 1
    row_len = inner * k2
    tap, pix = iota((LANES, 256), 1), iota((LANES, 256), 0)
    for yrel in range(2):
        for p in range(3):
            hit = (
                ((tap & 15) == (pix & 15))
                & ((tap >> 6) == (pix >> 6) + 2 * (1 - yrel))
                & (((tap >> 4) & 3) == ((pix >> 4) & 3) + 2 - 2 * p)
            )
            at = (yrel * 3 + p) * k2
            t2[:, at : at + k2] = dot_lanes(hit.astype(F32).astype(BF16), w2t[...]).astype(BF16)
    g2[0] = jnp.zeros(g2.shape[1:], BF16)
    g2[inner + 1] = jnp.zeros(g2.shape[1:], BF16)
    g1[0] = jnp.zeros(g1.shape[1:], BF16)
    g1[side + 1] = jnp.zeros(g1.shape[1:], BF16)
    zero = jnp.zeros((k2, LANES), BF16)
    total_one = jnp.zeros((k1, LANES), F32)
    total_two = jnp.zeros((k2, LANES), F32)
    for y in range(inner):
        at = slice(y * row_len, (y + 1) * row_len)
        grad = dot(lw[at, :], g3[...]) * s2[at, :].astype(F32)
        grad = grad.astype(BF16).reshape(inner, k2, LANES)
        g2[y + 1] = grad
        total_two = total_two + jnp.sum(grad.astype(F32), axis=0)
    ends = (0, side // 2 + 1, side + 2)
    copies = [
        pltpu.make_async_copy(g1.at[a:b], g1_far.at[a:b], sems.at[k])
        for k, (a, b) in enumerate(zip(ends, ends[1:]))
    ]
    reach, cols = 5, 8
    total = jnp.zeros((2 * reach * k2, 2 * cols * k1), F32)
    grads, tiles = [], []
    for b in range(side // 2):
        cut = []
        for j in range(side // 4):
            pieces = []
            for yrel in range(2):
                for p in range(3):
                    x = 2 * j - 1 + p
                    pieces.append(g2[b + yrel, x] if 0 <= x < inner else zero)
            cut.append(jnp.concatenate(pieces, axis=0))
        got = dot(t2[...], jnp.concatenate(cut, axis=1))
        for u in range(2):
            for j in range(side // 4):
                part = got[u * 64 : (u + 1) * 64, j * LANES : (j + 1) * LANES]
                slope = s1[2 * b + u + 1, 4 * j : 4 * j + 4].astype(F32)
                grad = (part.reshape(4, k1, LANES) * slope).astype(BF16)
                g1[2 * b + u + 1, 4 * j : 4 * j + 4] = grad
                total_one = total_one + jnp.sum(grad.astype(F32), axis=0)
        if 2 * b + 3 == ends[1]:
            copies[0].start()
        for j in range(-(-side // cols)):
            end = min((j + 1) * cols, side)
            tile = h1[2 * b + 1 : 2 * b + 3, j * cols : end]
            if end < (j + 1) * cols:
                rest = jnp.zeros((2, (j + 1) * cols - end, k1, LANES), BF16)
                tile = jnp.concatenate([tile, rest], axis=1)
            tiles.append(tile.reshape(2 * cols * k1, LANES))
            pieces = []
            for half in range(2):
                for p in range(reach):
                    x = 4 * j - 1 + p
                    pieces.append(g2[b + 1 - half, x] if 0 <= x < inner else zero)
            grads.append(jnp.concatenate(pieces, axis=0))
        if b % 2:
            total = total + dot_lanes(
                jnp.concatenate(grads, axis=1), jnp.concatenate(tiles, axis=1)
            )
            grads, tiles = [], []
    copies[1].start()
    line = 4 * k1
    for half in range(2):
        for u in range(2):
            tap_row = jnp.zeros((k2, line), F32)
            for p in range(reach):
                at = (half * reach + p) * k2
                part = total[at : at + k2, u * 2 * line : (u + 1) * 2 * line]
                start = 2 * k1 * (p - 1)
                piece = part[:, max(start, 0) : min(start + line, 2 * line)]
                if start < 0:
                    piece = jnp.concatenate([jnp.zeros((k2, -start), F32), piece], axis=1)
                if start + line > 2 * line:
                    rest = jnp.zeros((k2, start - line), F32)
                    piece = jnp.concatenate([piece, rest], axis=1)
                tap_row = tap_row + piece
            at = (2 * half + u) * line
            c2[:, at : at + line] = tap_row
    sums[...] = jnp.zeros_like(sums)
    sums[0:1, 0:k1] = row_of(jnp.sum(total_one, axis=1, keepdims=True))
    sums[1:2, 0:k2] = row_of(jnp.sum(total_two, axis=1, keepdims=True))
    for copy in copies:
        copy.wait()


def pixel_band(sec, w1t, channels):
    k1 = w1t.shape[0]
    rows = 64 * channels
    row, tap = iota((rows, 256), 0), iota((rows, 256), 1)
    moves = ((tap >> 6) == row % channels + sec * channels) & ((tap & 63) == row // channels)
    taps = dot_lanes(moves.astype(F32).astype(BF16), w1t)
    line, span = COLS * channels, 8 * channels
    blocks = {}
    for half in range(2):
        for p in range(NEAR):
            pieces = []
            for u in range(4):
                at = (4 * half + u) * span
                start = 4 * (p - 1) * channels
                cut = taps[at + max(0, -start) : at + min(span, line - start)]
                start = max(start, 0)
                pieces += [jnp.zeros((start, k1), F32)] if start else []
                pieces.append(cut)
                rest = line - start - cut.shape[0]
                pieces += [jnp.zeros((rest, k1), F32)] if rest else []
            blocks[half, p] = jnp.concatenate(pieces, axis=0)
    zero = jnp.zeros((4 * line, k1), F32)
    lines = []
    for r in range(STEP):
        cols = [
            blocks.get((r + 1 - yrel, p), zero) for yrel in range(STEP + 1) for p in range(NEAR)
        ]
        lines.append(jnp.concatenate(cols, axis=1))
    return jnp.concatenate(lines, axis=0).astype(BF16)


def first_kernel(section, frames_far, g1_far, after, c1, frames, g1, acc, sems):
    side, k1 = g1.shape[1], g1.shape[2]
    img, _, channels, _ = frames.shape
    steps = img // 4 // STEP
    arrives = frame_copies(section, frames_far, frames, sems)
    g1_copy = pltpu.make_async_copy(g1_far, g1, sems.at[steps])
    arrives(0).start()
    g1_copy.start()
    for g in range(1, steps):
        arrives(g).start()
    acc[...] = jnp.zeros_like(acc)
    zero = jnp.zeros((k1, LANES), BF16)
    g1_copy.wait()

    def one_step(g, carry):
        arrives(g).wait()
        pixels, grads = [], []
        for j in range(img // COLS):
            rows = [pl.multiple_of(4 * (STEP * g + r), 4) for r in range(STEP)]
            pixels.append(
                jnp.concatenate([tile_rows(frames, row, j, COLS) for row in rows], axis=0)
            )
            pieces = []
            for yrel in range(STEP + 1):
                for p in range(NEAR):
                    x = 3 * j - 1 + p
                    pieces.append(g1[STEP * g + yrel, x] if 0 <= x < side else zero)
            grads.append(jnp.concatenate(pieces, axis=0))
        acc[...] += dot_lanes(jnp.concatenate(pixels, axis=1), jnp.concatenate(grads, axis=1))
        return carry

    lax.fori_loop(0, steps, one_step, 0)
    fold_first(acc, c1, channels, k1)


def fold_first(acc, c1, channels, k1):
    line = COLS * channels
    step = 4 * channels
    taps = []
    for half in range(2):
        total = sum(
            acc[r * 4 * line : (r + 1) * 4 * line, :][
                :, (r + 1 - half) * NEAR * k1 : (r + 2 - half) * NEAR * k1
            ]
            for r in range(STEP)
        )
        for u in range(4):
            part = total[u * line : (u + 1) * line]
            cols = [part[:, p * k1 : (p + 1) * k1] for p in range(NEAR)]
            taps.append(cols[1][0:step] + cols[2][step : 2 * step] + cols[3][2 * step :])
            taps.append(cols[0][0:step] + cols[1][step : 2 * step] + cols[2][2 * step :])
    row, col = iota((256, 256), 0), iota((256, 256), 1)
    moves = ((row & 3) == (col >> 6)) & ((row >> 2) == (col & 63))
    grad = dot_rows(jnp.concatenate(taps, axis=0), moves.astype(F32), EXACT)
    for half in range(2):
        c1[half * k1 : (half + 1) * k1, :] = grad[:, half * LANES : (half + 1) * LANES].astype(BF16)


def pixels_kernel(section, weights, mine_far, other_far, after, *refs, start, steps, begins):
    out, token, band_out, held, mine, other, sems = refs[-7:]
    side, k1 = mine.shape[1], mine.shape[2]


    def fetches(g):
        first, end = (STEP * g + 1 if g else 0), STEP * (g + 1) + 1
        pairs = ((mine_far, mine), (other_far, other))
        return [
            pltpu.make_async_copy(
                far.at[STEP * start + first : STEP * start + end],
                here.at[first:end],
                sems.at[2 + g, k],
            )
            for k, (far, here) in enumerate(pairs)
        ]

    for g in range(steps):
        for fetch in fetches(g):
            fetch.start()
    img, channels = out.shape[1], out.shape[2]
    sec = section[0]
    line = COLS * channels
    flat = held.reshape(2, 2, 4 * STEP, img * channels, LANES)
    if begins:
        band_out[...] = pixel_band(sec, weights[...], channels)
        band = band_out
    else:
        band = weights
        band_out[...] = jnp.zeros_like(band_out)
    token[...] = jnp.zeros_like(token)

    def writes(g):
        rows = slice(4 * STEP * (start + g), 4 * STEP * (start + g + 1))
        places = (sec * LANES, (1 - sec) * LANES)
        return [
            pltpu.make_async_copy(
                held.at[g % 2, k],
                out.at[rows, :, :, pl.ds(pl.multiple_of(places[k], LANES), LANES)],
                sems.at[g % 2, k],
            )
            for k in range(2)
        ]

    zero = jnp.zeros((k1, 2 * LANES), BF16)
    for g in range(steps):
        for fetch in fetches(g):
            fetch.wait()
        if g >= 2:
            for copy in writes(g - 2):
                copy.wait()
        for j in range(img // COLS):
            pieces = []
            for yrel in range(STEP + 1):
                for p in range(NEAR):
                    x, y = 3 * j - 1 + p, STEP * g + yrel
                    if 0 <= x < side:
                        pieces.append(jnp.concatenate([mine[y, x], other[y, x]], axis=1))
                    else:
                        pieces.append(zero)
            got = dot(band[...], jnp.concatenate(pieces, axis=0))
            for k in range(4 * STEP):
                at = slice(k * line, (k + 1) * line)
                span = slice(j * line, (j + 1) * line)
                flat[g % 2, 0, k, span, :] = got[at, :LANES]
                flat[g % 2, 1, k, span, :] = got[at, LANES:]
        for copy in writes(g):
            copy.start()
    for g in range(max(steps - 2, 0), steps):
        for copy in writes(g):
            copy.wait()


def two_parts(value):
    high = value.astype(BF16).astype(F32)
    return jnp.concatenate([high, value - high], axis=0).astype(BF16)


def one_part(pair):
    rows = pair.shape[0] // 2
    pair = pair.astype(F32)
    return pair[:rows] + pair[rows:]


def merge_kernel(keep, recv, small, c2, sums, out_far, lines, out, sems):
    members = out.shape[0]
    size = keep.shape[0] // members
    k2 = c2.shape[0]
    lines[...] = jnp.zeros_like(lines)
    at = small.shape[0]
    lines[0:at, :] = small[...]
    for half in range(2):
        lines[at : at + k2, :] = c2[:, half * LANES : (half + 1) * LANES]
        at += k2
    lines[at : at + sums.shape[0], :] = sums[...]
    for k in range(members):
        at = slice(k * size, (k + 1) * size)
        out[k, 0:size, :] = (keep[at, :].astype(F32) + recv[at, :].astype(F32)).astype(BF16)
        out[k, size:, :] = two_parts(lines[k * SHORT : (k + 1) * SHORT, :])
        pltpu.make_async_copy(out.at[k], out_far.at[k], sems.at[k]).start()
    for k in range(members):
        pltpu.make_async_copy(out.at[k], out_far.at[k], sems.at[k]).wait()


def cube_kernel(got, c1, after, out):
    members = got.shape[0]
    size = got.shape[1] - 2 * SHORT
    out[0:size, :] = sum(got[k, 0:size, :].astype(F32) for k in range(members)).astype(BF16)
    total = sum(one_part(got[k, size:, :]) for k in range(members))
    out[size : size + 2 * SHORT, :] = two_parts(total)
    out[size + 2 * SHORT :, :] = c1[...]


def added(a, b):
    size = a.shape[0] - 2 * SHORT - 32
    spans = (slice(0, size), slice(size, size + 2 * SHORT), slice(size + 2 * SHORT, None))
    first, last = ((a[k, :].astype(F32) + b[k, :].astype(F32)).astype(BF16) for k in spans[::2])
    middle = two_parts(one_part(a[spans[1], :]) + one_part(b[spans[1], :]))
    return jnp.concatenate([first, middle, last], axis=0)


def add_kernel(a, b, after, out):
    out[...] = added(a[...], b[...])


def spread_kernel(a, b, after, out_far, out, sems):
    out[...] = added(a[...], b[...])
    copies = [
        pltpu.make_async_copy(out, out_far.at[k], sems.at[k]) for k in range(out_far.shape[0])
    ]
    for copy in copies:
        copy.start()
    for copy in copies:
        copy.wait()


def relay_kernel(got, after, out):
    out[...] = got[...]


def unpack_half(which, got, lw, bw, vw, stage, stage_b, sems):
    members = got.shape[0]
    size = stage.shape[0] // members
    linear_rows, width = lw.shape
    options = bw.shape[0]
    half = (linear_rows + options * width + width) // 2
    rest = linear_rows - half

    @pl.when(which == 0)
    def _():
        copies = []
        for k in range(members):
            start, end = k * size, min((k + 1) * size, half)
            stage[start:end, :] = got[k, 0 : end - start, :].astype(F32)
            copies.append(
                pltpu.make_async_copy(stage.at[start:end], lw.at[start:end], sems.at[k])
            )
            copies[-1].start()
        for copy in copies:
            copy.wait()

    @pl.when(which == 1)
    def _():
        def rows(start, end):
            parts = []
            while start < end:
                k, at = start // size, start % size
                count = min(size - at, end - start)
                parts.append(got[k, at : at + count, :])
                start += count
            value = parts[0] if len(parts) == 1 else jnp.concatenate(parts, axis=0)
            return value.astype(F32)

        stage[0:rest, :] = rows(0, rest)
        copies = [pltpu.make_async_copy(stage.at[0:rest], lw.at[half:], sems.at[0])]
        copies[0].start()
        group = options // 3
        for o in range(options):
            stage_b[o] = rows(rest + o * width, rest + (o + 1) * width)
            if o % group == group - 1:
                part = slice(o + 1 - group, o + 1)
                copy = pltpu.make_async_copy(
                    stage_b.at[part], bw.at[part], sems.at[1 + o // group]
                )
                copy.start()
                copies.append(copy)
        at = rest + options * width
        stage[rest : rest + width, :] = rows(at, at + width)
        copies.append(
            pltpu.make_async_copy(stage.at[rest : rest + width], vw, sems.at[1 + options // group])
        )
        copies[-1].start()
        for copy in copies:
            copy.wait()


def own_kernel(section, mine, lw, bw, vw, stage, stage_b, sems):
    unpack_half(section[0], mine, lw, bw, vw, stage, stage_b, sems)


def unpack_kernel(section, mine, other, *refs):
    refs = refs[3:]
    lw, bw, vw, loss, c1, b1, c2, b2, lb, bb, hw, hb, vb, ow, ob, stage, stage_b, lines, sems = refs
    options = bw.shape[0]
    k1, k2 = c1.shape[0], c2.shape[0]
    size = stage.shape[0] // CUBE
    unpack_half(1 - section[0], other, lw, bw, vw, stage, stage_b, sems)
    grad = [jnp.zeros((k1, LANES), F32) for _ in range(2)]
    for k in range(CUBE):
        pair = slice(size, size + 2 * SHORT)
        at = slice(k * SHORT, (k + 1) * SHORT)
        lines[at, :] = one_part(mine[k, pair, :]) + one_part(other[k, pair, :])
        for ref in (mine, other):
            for h in range(2):
                at = size + 2 * SHORT + h * k1
                grad[h] += ref[k, at : at + k1, :].astype(F32)
    for part in range(2):
        c1[:, part * LANES : (part + 1) * LANES] = grad[part]
    bb[...] = lines[0:options, :]
    vb[...] = lines[AT_VB, :]
    ow[...] = lines[AT_OW, :]
    hw[...] = lines[AT_HW, :]
    lb[...] = lines[AT_LB, :]
    scalars = lines[AT_SCALARS, :]
    loss[...] = scalars[:, 0:1]
    hb[...] = scalars[:, 1:3]
    ob[...] = scalars[:, 3:4]
    at = TABLE
    for part in range(2):
        c2[:, part * LANES : (part + 1) * LANES] = lines[at : at + k2, :]
        at += k2
    b1[...] = lines[at : at + 1, 0:k1]
    b2[...] = lines[at + 1 : at + 2, 0:k2]


def numbers_kernel(
    options,
    depth,
    targets,
    destination,
    b1,
    b2,
    lb,
    bb,
    hw,
    vb,
    ow,
    hb,
    ob,
    out,
    table,
):
    levels, kinds = options.shape[0], targets.shape[0]
    slots = depth.shape[1]
    rows = [options[...].astype(F32), depth[...].astype(F32)]
    rows += [targets[k] for k in range(kinds)]
    rows.append(jnp.zeros((LANES - levels - 1 - kinds * levels, slots), F32))
    out[...] = jnp.transpose(jnp.concatenate(rows, axis=0))
    table[...] = jnp.zeros_like(table)
    table[0 : bb.shape[0], :] = bb[...]
    table[AT_VB, :] = vb[...]
    table[AT_OW, :] = ow[...].astype(F32)
    table[AT_HW, :] = hw[...].astype(F32)
    table[AT_LB, :] = lb[...]
    table[AT_B1, 0 : b1.shape[1]] = b1[...]
    table[AT_B2, 0 : b2.shape[1]] = b2[...]
    lane = iota((1, LANES), 1)
    scalars = jnp.zeros((1, LANES), F32)
    for k, value in ((1, hb[:, 0:1]), (2, hb[:, 1:2]), (3, ob[...])):
        scalars = jnp.where(lane == k, value, scalars)
    table[AT_SCALARS, :] = scalars
    for k in range(slots // LANES):
        part = destination[:, k * LANES : (k + 1) * LANES]
        table[AT_DEST + k : AT_DEST + k + 1, :] = part.astype(F32)


def whole(shape):
    zeros = (0,) * len(shape)
    return pl.BlockSpec(shape, lambda *_: zeros)


ANYWHERE = pl.BlockSpec(memory_space=pl.ANY)
SCALARS = pl.BlockSpec(memory_space=pltpu.SMEM)


def params():
    return pltpu.CompilerParams(vmem_limit_bytes=VMEM_BYTES)


def shape_of(*shape, dtype=F32):
    return jax.ShapeDtypeStruct(shape, dtype)


def cost(microseconds):
    return pl.CostEstimate(
        flops=int(1.1e9 * microseconds), bytes_accessed=int(3.6e6 * microseconds), transcendentals=0
    )


def stays(value):
    return pltpu.with_memory_space_constraint(value, pltpu.HBM)


def encode(section, frames, w1t, w2t, lw, table):
    img = frames.shape[0]
    blocks = img // 4
    side = blocks - 1
    k1, k2, width = w1t.shape[0], w2t.shape[0], lw.shape[1]
    flat = lw.shape[0]
    vmem = pltpu.VMEM
    near = pl.BlockSpec(memory_space=vmem)
    grid_one = (blocks, side, k1, LANES)
    return pl.pallas_call(
        encode_kernel,
        in_specs=[SCALARS, ANYWHERE, near, near, ANYWHERE, near],
        out_specs=[ANYWHERE] * 3 + [near] * 3,
        out_shape=(
            pltpu.HBM(grid_one, BF16),
            pltpu.HBM(grid_one, BF16),
            pltpu.HBM((flat, LANES), BF16),
            shape_of(flat, LANES, dtype=BF16),
            shape_of(width, LANES, dtype=BF16),
            shape_of(width, LANES),
        ),
        scratch_shapes=[
            vmem((img, img, frames.shape[2], LANES), BF16),
            vmem(lw.shape, BF16),
            vmem(grid_one, BF16),
            vmem(grid_one, BF16),
            vmem((flat, LANES), BF16),
            vmem((2 * REACH * k1, 256), BF16),
            vmem((2 * k1, 64), BF16),
            vmem((6 * k2, LANES), BF16),
            vmem((k1, LANES), F32),
            vmem((k2, LANES), F32),
            vmem((side, k1, LANES), F32),
            vmem((side // 2 - 1, k2, LANES), F32),
            pltpu.SemaphoreType.DMA((4, max(blocks // STEP, 3))),
        ],
        compiler_params=params(),
        cost_estimate=cost(9),
        name="encode",
    )(section, frames, w1t, w2t, lw, table)


def plan(section, slots, enc, s3, h2, branch_w, value_w, table, per_pair, depth, half_rows):
    width = enc.shape[0]
    options = branch_w.shape[0]
    two = 2 * width
    pairs = options // 2
    outs = (
        shape_of(half_rows, LANES, dtype=BF16),
        shape_of(half_rows, LANES, dtype=BF16),
        shape_of(TABLE, LANES),
        shape_of(width, LANES, dtype=BF16),
    )
    vmem = pltpu.VMEM
    near = pl.BlockSpec(memory_space=vmem)
    return pl.pallas_call(
        functools.partial(plan_kernel, per_pair=per_pair, depth=depth),
        in_specs=[SCALARS, near, near, near, near, ANYWHERE, near, near],
        out_shape=outs,
        scratch_shapes=[
            vmem((2, half_rows, LANES), BF16),
            vmem((options * width, width + 16), BF16),
            vmem((width + 16, width + 16), BF16),
            vmem((width, width + 16), BF16),
            vmem((width, LANES), F32),
            vmem((16, LANES), F32),
            vmem((options * width, LANES), F32),
            vmem((depth, options * width, LANES), F32),
            vmem((depth, pairs, width, two), F32),
            vmem((depth, pairs, width + 16, two), BF16),
            vmem((depth, pairs, width, two), BF16),
            vmem((depth, options * width, LANES), BF16),
            vmem(branch_w.shape, BF16),
            pltpu.SemaphoreType.DMA,
        ],
        compiler_params=params(),
        cost_estimate=cost(11),
        name="plan",
    )(section, slots, enc, s3, h2, branch_w, value_w, table)


def back(g3, lw, s2, s1, h1, w2t):
    _, side, k1 = s1.shape[:3]
    k2 = w2t.shape[0]
    inner = side // 2 - 1
    padded = (side + 2, side, k1, LANES)
    near = pl.BlockSpec(memory_space=pltpu.VMEM)
    return pl.pallas_call(
        back_kernel,
        in_specs=[near] * 6,
        out_specs=[ANYWHERE, near, near],
        out_shape=(pltpu.HBM(padded, BF16), shape_of(k2, 256), shape_of(8, LANES)),
        scratch_shapes=[
            pltpu.VMEM((LANES, 6 * k2), BF16),
            pltpu.VMEM((inner + 2, inner, k2, LANES), BF16),
            pltpu.VMEM(padded, BF16),
            pltpu.SemaphoreType.DMA((2,)),
        ],
        compiler_params=params(),
        cost_estimate=cost(25),
        name="back",
    )(g3, lw, s2, s1, h1, w2t)


def first(section, frames, g1, after):
    img, _, channels, _ = frames.shape
    k1 = g1.shape[2]
    return pl.pallas_call(
        first_kernel,
        in_specs=[SCALARS, ANYWHERE, ANYWHERE, ANYWHERE],
        out_shape=shape_of(2 * k1, LANES, dtype=BF16),
        scratch_shapes=[
            pltpu.VMEM((img, img, channels, LANES), BF16),
            pltpu.VMEM(g1.shape, BF16),
            pltpu.VMEM((STEP * 4 * COLS * channels, (STEP + 1) * NEAR * k1), F32),
            pltpu.SemaphoreType.DMA((img // 4 // STEP + 1,)),
        ],
        compiler_params=params(),
        cost_estimate=cost(45),
        name="first",
    )(section, frames, g1, after)


def pixels(section, weights, mine, other, shape, start, steps, after, done=None):
    img, _, channels, _ = shape
    k1 = mine.shape[2]
    band = (STEP * 4 * COLS * channels, (STEP + 1) * NEAR * k1)
    near = pl.BlockSpec(memory_space=pltpu.VMEM)
    operands = (section, weights, mine, other, after)
    specs = [SCALARS, near, ANYWHERE, ANYWHERE, ANYWHERE]
    window = pltpu.VMEM((STEP * steps + 1,) + mine.shape[1:], BF16)
    aliases = {}
    if done is not None:
        aliases = {len(operands): 0}
        operands += (done,)
        specs.append(ANYWHERE)
    outs = [shape_of(*shape), shape_of(8, LANES), shape_of(*band, dtype=BF16)]
    return pl.pallas_call(
        functools.partial(pixels_kernel, start=start, steps=steps, begins=done is None),
        in_specs=specs,
        out_specs=[ANYWHERE, near, near],
        out_shape=outs,
        scratch_shapes=[
            pltpu.VMEM((2, 2, 4 * STEP, img, channels, LANES), F32),
            window,
            window,
            pltpu.SemaphoreType.DMA((2 + steps, 2)),
        ],
        input_output_aliases=aliases,
        compiler_params=params(),
        cost_estimate=cost(2 + 0.8 * steps),
        name="pixels",
    )(*operands)


def small_call(
    kernel, outs, operands, scratch=(), name=None, place=None, after=(), weight=0.3, far=False
):
    specs = [pl.BlockSpec(memory_space=pltpu.VMEM)] * len(operands)
    if place is not None:
        operands = (*place, *operands)
        specs = [pl.BlockSpec(memory_space=pltpu.SMEM)] * len(place) + specs
    return pl.pallas_call(
        kernel,
        in_specs=specs + [ANYWHERE] * len(after),
        out_specs=jax.tree.map(
            lambda _: ANYWHERE if far else pl.BlockSpec(memory_space=pltpu.VMEM), outs
        ),
        out_shape=outs,
        scratch_shapes=list(scratch),
        compiler_params=params(),
        cost_estimate=cost(weight),
        name=name,
    )(*operands, *after)


def round_up(value, step):
    return -(-value // step) * step


def swapped(value):
    return lax.ppermute(value, "section", [(0, 1), (1, 0)])


def exchanged(value, groups=None):
    return lax.all_to_all(
        value, "batch", split_axis=0, concat_axis=0, axis_index_groups=groups, tiled=True
    )


def partner(value, distance):
    count = lax.axis_size("batch")
    return lax.ppermute(value, "batch", [(b, b ^ distance) for b in range(count)])


def local(
    frames,
    destination,
    options,
    depth,
    targets,
    conv_one,
    bias_one,
    conv_two,
    bias_two,
    linear_w,
    linear_b,
    branch_w,
    branch_b,
    head_w,
    head_b,
    value_w,
    value_b,
    out_w,
    out_b,
):
    section = lax.axis_index("section").astype(jnp.int32)[None]
    peers = lax.axis_size("batch")
    frame_count = frames.shape[3]
    per_pair = frame_count // peers
    levels = options.shape[0]
    frames = stays(frames.transpose(1, 2, 0, 3))
    w1t, w2t = stays(conv_one.T), stays(conv_two.T)
    branch_w, value_w = stays(branch_w), stays(value_w)
    encoder_params = (w1t, bias_one, w2t, bias_two, linear_w, linear_b)
    planner_params = (branch_w, branch_b, head_w.T, head_b, value_w, value_b, out_w.T, out_b)
    width = linear_w.shape[1]
    big_rows = linear_w.shape[0] + (branch_w.shape[0] + 1) * width
    size = round_up(-(-big_rows // (2 * CUBE)), 16)

    tiny = (bias_one, bias_two, linear_b, branch_b, head_w.T, value_b, out_w.T)
    tiny = [stays(v if v.ndim > 1 else v[None, :]) for v in tiny]
    numbers, table = pl.pallas_call(
        numbers_kernel,
        in_specs=[pl.BlockSpec(memory_space=pltpu.VMEM)] * (6 + len(tiny)),
        out_shape=[shape_of(frame_count, LANES), shape_of(TABLE, LANES)],
        compiler_params=params(),
        cost_estimate=cost(1),
        name="numbers",
    )(
        stays(options),
        stays(depth[None, :]),
        stays(targets),
        stays(destination[None, :]),
        *tiny,
        stays(head_b[None, :]),
        out_b[None, :],
    )
    slots = exchanged(numbers.reshape(peers, per_pair, LANES)).reshape(frame_count, LANES)

    h1, s1, s2, h2, enc, s3 = encode(section, frames, w1t, w2t, stays(linear_w), table)
    keep, send, small, g3 = plan(
        section, slots, enc, s3, h2, branch_w, value_w, table, per_pair, levels, CUBE * size
    )
    recv = swapped(send)
    channels = frames.shape[2] // lax.axis_size("section")
    g1, c2, sums = back(g3, linear_w, s2, s1, h1, w2t)
    other = swapped(g1)
    g1 = stays(g1)
    cubes = [list(range(c, c + CUBE)) for c in range(0, peers, CUBE)]
    bf16 = functools.partial(shape_of, dtype=BF16)
    pieces = small_call(
        merge_kernel,
        bf16(CUBE, size + 2 * SHORT, LANES),
        (keep, recv, small, c2, sums),
        [
            pltpu.VMEM((CUBE * SHORT, LANES), F32),
            pltpu.VMEM((CUBE, size + 2 * SHORT, LANES), BF16),
            pltpu.SemaphoreType.DMA((CUBE,)),
        ],
        name="merge",
        far=True,
    )
    got = exchanged(pieces, cubes)
    c1 = first(section, frames, g1, pieces)
    img = frames.shape[0]
    steps = img // 4 // STEP
    draw = functools.partial(
        pixels, section, mine=g1, other=other, shape=(img, img, channels, 2 * LANES)
    )
    frames_grad, token, band = draw(weights=w1t, start=0, steps=1, after=c1)
    piece = bf16(size + 2 * SHORT + c1.shape[0], LANES)
    keep = small_call(cube_kernel, piece, (got, c1), name="cube", after=(token,))
    distance = CUBE
    while distance < peers:
        recv = partner(keep, distance)
        if distance == CUBE:
            frames_grad, token, _ = draw(
                weights=band, start=1, steps=1, after=keep, done=frames_grad
            )
        distance *= 2
        if distance < peers:
            keep = small_call(add_kernel, piece, (keep, recv), name="add", after=(token,))
        else:
            keep = small_call(
                spread_kernel,
                bf16(CUBE, *piece.shape),
                (keep, recv),
                [pltpu.VMEM(piece.shape, BF16), pltpu.SemaphoreType.DMA((CUBE,))],
                name="spread",
                after=(token,),
                far=True,
            )
    got = exchanged(keep, cubes)
    frames_grad, token, _ = draw(
        weights=band, start=2, steps=steps - 2, after=keep, done=frames_grad
    )
    got = small_call(relay_kernel, bf16(*got.shape), (got,), name="relay", after=(token,))
    got_other = swapped(got)
    shapes = [p.shape for p in encoder_params + planner_params]
    near = pl.BlockSpec(memory_space=pltpu.VMEM)
    flat = [shape_of(*(v if len(v) > 1 else (1,) + v)) for v in [(1, 1)] + shapes]
    large = [flat[k] for k in (5, 7, 11)]
    stages = [
        pltpu.VMEM((CUBE * size, LANES), F32),
        pltpu.VMEM(branch_w.shape, F32),
    ]
    sems = pltpu.SemaphoreType.DMA((CUBE,))
    begun = pl.pallas_call(
        own_kernel,
        in_specs=[SCALARS, near],
        out_specs=[ANYWHERE] * 3,
        out_shape=large,
        scratch_shapes=[*stages, sems],
        compiler_params=params(),
        cost_estimate=cost(1),
        name="own",
    )(section, got)
    little = [v for k, v in enumerate(flat) if k not in (5, 7, 11)]
    ends = pl.pallas_call(
        unpack_kernel,
        in_specs=[SCALARS, near, near] + [ANYWHERE] * 3,
        out_specs=[ANYWHERE] * 3 + [near] * len(little),
        out_shape=large + little,
        scratch_shapes=[*stages, pltpu.VMEM((CUBE * SHORT, LANES), F32), sems],
        input_output_aliases={3: 0, 4: 1, 5: 2},
        compiler_params=params(),
        cost_estimate=cost(1.5),
        name="unpack",
    )(section, got, got_other, *begun)
    rest = list(ends[3:])
    for k, at in enumerate((5, 7, 11)):
        rest.insert(at, ends[k])
    rest = [v.reshape(s) for v, s in zip(rest, [()] + shapes)]
    for at in (1, 3, 9, 13):
        rest[at] = rest[at].T
    return (rest[0], frames_grad.transpose(2, 0, 1, 3), *rest[1:])


def solution(mesh):
    placed = (
        P(None, None, None, "batch"),
        P("batch"),
        P(None, "batch"),
        P("batch"),
        P(None, None, "batch"),
    ) + (P(),) * 14
    return jax.shard_map(
        local,
        mesh=mesh,
        in_specs=placed,
        out_specs=(P(), P("section", None, None, "batch")) + (P(),) * 14,
        check_vma=False,
    )
```

```python
import functools
import math

import jax
import jax.numpy as jnp
from jax import lax
from jax.experimental import pallas as pl
from jax.experimental.pallas import tpu as pltpu
from jax.sharding import PartitionSpec as P

BF16 = jnp.bfloat16
F32 = jnp.float32
EXACT = lax.Precision.HIGHEST
LANES = 128
VMEM_BYTES = 32 * 1024 * 1024
TILE = 16
REACH = 5
STEP = 3
COLS = 12
NEAR = 4
AT_VB, AT_OW, AT_HW, AT_LB, AT_SCALARS, AT_B1, AT_B2, AT_DEST = (
    slice(18, 19),
    slice(19, 20),
    slice(20, 22),
    slice(22, 23),
    slice(23, 24),
    slice(24, 25),
    slice(25, 26),
    26,
)
TABLE = 32
CUBE = 8
SHORT = 16


def dot(a, b, precision=None):
    return jnp.dot(a, b, preferred_element_type=F32, precision=precision)


def dot_rows(a, b, precision=None):
    return lax.dot_general(
        a, b, (((0,), (0,)), ((), ())), preferred_element_type=F32, precision=precision
    )


def dot_lanes(a, b, precision=None):
    return lax.dot_general(
        a, b, (((1,), (1,)), ((), ())), preferred_element_type=F32, precision=precision
    )


def iota(shape, axis):
    return lax.broadcasted_iota(jnp.int32, shape, axis)


def column(row):
    n = row.shape[1]
    wide = jnp.broadcast_to(row, (n, n))
    return jnp.sum(jnp.where(iota((n, n), 0) == iota((n, n), 1), wide, 0.0), axis=1, keepdims=True)


def row_of(col):
    n = col.shape[0]
    wide = jnp.broadcast_to(col, (n, n))
    return jnp.sum(jnp.where(iota((n, n), 0) == iota((n, n), 1), wide, 0.0), axis=0, keepdims=True)


def soft(x):
    t = jnp.tanh(0.5 * x)
    return jnp.maximum(x, 0.0) - jnp.log(0.5 + 0.5 * jnp.abs(t)), 0.5 + 0.5 * t


def silu_pair(x):
    s = 0.5 + 0.5 * jnp.tanh(0.5 * x)
    act = x * s
    return act, s + act * (1.0 - s)


def pixel_order(w1t):
    tap, pix = iota((256, 256), 0), iota((256, 256), 1)
    moves = ((tap >> 6) == (pix & 3)) & ((tap & 63) == (pix >> 2))
    return dot(w1t, moves.astype(F32).astype(BF16))


def frame_copies(section, far, here, sems):
    lanes = pl.ds(pl.multiple_of(section[0] * LANES, LANES), LANES)
    size = 4 * STEP

    def copy(g):
        rows = pl.ds(pl.multiple_of(g * size, size), size)
        return pltpu.make_async_copy(far.at[rows, :, :, lanes], here.at[rows], sems.at[g])

    return copy


def tile_rows(frames, row, j, cols):
    img, _, channels, _ = frames.shape
    flat = frames.reshape(img, img * channels, LANES)
    size = cols * channels
    end = min((j + 1) * size, img * channels)
    part = flat[pl.ds(row, 4), j * size : end, :]
    return part.reshape(4 * (end - j * size), LANES)


def encode_kernel(
    section,
    frames_far,
    w1t,
    w2t,
    lw_far,
    branch_far,
    table,
    h1_far,
    s1_far,
    s2_far,
    h2,
    enc,
    s3,
    bwt,
    frames,
    lw,
    branch_w,
    h1,
    s1,
    s2,
    band,
    edge,
    band2,
    bias1,
    bias2,
    held,
    held2,
    sems,
):
    blocks, side = h1.shape[:2]
    steps = blocks // STEP
    tiles = frames.shape[1] // TILE
    k1, k2 = w1t.shape[0], w2t.shape[0]
    reach_rows = REACH * k1
    arrives = frame_copies(section, frames_far, frames, sems.at[0])
    for g in range(steps):
        arrives(g).start()
    last_copies = [
        pltpu.make_async_copy(lw_far, lw, sems.at[3, 0]),
        pltpu.make_async_copy(s2, s2_far, sems.at[3, 1]),
    ]
    branch_copy = pltpu.make_async_copy(branch_far, branch_w, sems.at[3, 2])
    branch_copy.start()
    last_copies[0].start()
    options, width, _ = branch_w.shape
    turns = -(-options // steps)

    def turn(o):
        rows = [branch_w[o].astype(F32), three_parts(table[pl.ds(o, 1), :])]
        rows.append(jnp.zeros((13, width), F32))
        value = jnp.transpose(jnp.concatenate(rows, axis=0)).astype(BF16)
        bwt[pl.ds(pl.multiple_of(o * width, width), width), :] = value

    def leaves(g):
        rows = pl.ds(g * STEP, STEP)
        return [
            pltpu.make_async_copy(h1.at[rows], h1_far.at[rows], sems.at[1, g]),
            pltpu.make_async_copy(s1.at[rows], s1_far.at[rows], sems.at[2, g]),
        ]

    inner = side // 2 - 1
    row_len = inner * k2
    two = 2 * k2 * 3

    def prepare():
        taps = pixel_order(w1t[...])
        edges = []
        for half in range(2):
            lines = [taps[:, 32 * (4 * half + u) : 32 * (4 * half + u + 1)] for u in range(4)]
            for place in range(REACH):
                pieces = []
                for line in lines:
                    start = 16 * (place - 1)
                    cut = line[:, max(0, -start) : min(32, 64 - start)]
                    start = max(start, 0)
                    pieces += [jnp.zeros((k1, start), F32)] if start else []
                    pieces.append(cut)
                    rest = 64 - start - cut.shape[1]
                    pieces += [jnp.zeros((k1, rest), F32)] if rest else []
                at = half * reach_rows + place * k1
                band[at : at + k1, :] = jnp.concatenate(pieces, axis=1).astype(BF16)
            edges.append(jnp.concatenate([line[:, 16:] for line in lines], axis=1))
        edge[...] = jnp.concatenate(edges, axis=0).astype(BF16)
        tap, pix = iota((256, LANES), 0), iota((256, LANES), 1)
        for half in range(2):
            for place in range(3):
                hit = (
                    ((tap & 15) == (pix & 15))
                    & ((tap >> 6) == (pix >> 6) + 2 * half)
                    & (((tap >> 4) & 3) == ((pix >> 4) & 3) + 2 - 2 * place)
                )
                at = (half * 3 + place) * k2
                taps = dot(w2t[...], hit.astype(F32).astype(BF16))
                band2[at : at + k2, :] = taps.astype(BF16)
        bias1[...] = jnp.broadcast_to(column(table[AT_B1, 0:k1]), bias1.shape)
        bias2[...] = jnp.broadcast_to(column(table[AT_B2, 0:k2]), bias2.shape)
        held[...] = jnp.zeros_like(held)
        held2[...] = jnp.zeros_like(held2)
        h1[...] = jnp.zeros_like(h1)

    def added(sums, x, value):
        sums[x] = sums[x] + value if x in sums else value

    def second_rows(b):
        tiles = [
            h1[pl.ds(2 * b + 1, 2), 4 * j : 4 * j + 4].reshape(LANES, LANES)
            for j in range(side // 4)
        ]
        got = dot(band2[...], jnp.concatenate(tiles, axis=1))
        low, high = {}, {}
        for j in range(side // 4):
            for place in range(3):
                x = 2 * j - 1 + place
                if 0 <= x < inner:
                    span = slice(j * LANES, (j + 1) * LANES)
                    at = place * k2
                    added(low, x, got[at : at + k2, span])
                    added(high, x, got[two // 2 + at : two // 2 + at + k2, span])
        row = jnp.maximum(b - 1, 0) * row_len
        for x in range(inner):
            value, slope = soft(held2[x] + high[x] + bias2[...])
            held2[x] = low[x]
            at = pl.ds(pl.multiple_of(row + x * k2, k2), k2)
            h2[at, :] = value.astype(BF16)
            s2[at, :] = slope.astype(BF16)

    def one_step(g, carry):
        def row(r):
            return pl.multiple_of(4 * (STEP * g + r), 4)

        arrives(g).wait()
        for k in range(turns):
            turn(jnp.minimum(turns * g + k, options - 1))
        second_rows(jnp.maximum(g - 1, 0))

        last = dot(
            edge[...], jnp.concatenate([tile_rows(frames, row(r), tiles, TILE) for r in range(STEP)], axis=1)
        )
        odd = {}
        for r in range(STEP):
            low, high = {}, {}

            def place_tile(j, got):
                for place in range(REACH):
                    x = 4 * j - 1 + place
                    if 0 <= x < side:
                        at = place * k1
                        added(low, x, got[at : at + k1])
                        added(high, x, got[reach_rows + at : reach_rows + at + k1])

            if r not in odd:
                rows = [k for k in (r, r + 1) if k < STEP]
                cut = [tile_rows(frames, row(k), tiles - 1, TILE) for k in rows]
                got = dot(band[...], jnp.concatenate(cut, axis=1))
                odd.update({k: got[:, i * LANES : (i + 1) * LANES] for i, k in enumerate(rows)})
            place_tile(tiles - 1, odd[r])
            added(low, side - 1, last[:k1, r * LANES : (r + 1) * LANES])
            added(high, side - 1, last[k1:, r * LANES : (r + 1) * LANES])
            done = 0
            for j in range(0, tiles - 1, 2):
                cut = [tile_rows(frames, row(r), j + k, TILE) for k in range(2)]
                got = dot(band[...], jnp.concatenate(cut, axis=1))
                for k in range(2):
                    place_tile(j + k, got[:, k * LANES : (k + 1) * LANES])
                ready = side if j + 2 == tiles - 1 else 4 * j + 7
                for x in range(done, ready):
                    value, slope = soft(held[x] + high[x] + bias1[...])
                    held[x] = low[x]
                    value = value.astype(BF16)
                    h1[STEP * g + r, x] = value
                    s1[STEP * g + r, x] = slope.astype(BF16)
                done = ready
        for copy in leaves(g):
            copy.start()
        return carry

    prepare()
    branch_copy.wait()
    lax.fori_loop(0, steps, one_step, 0)
    for b in range(steps - 1, side // 2):
        second_rows(b)
    for copy in last_copies[1:]:
        copy.start()
    last_copies[0].wait()
    value, slope = soft(dot_rows(lw[...], h2[...]) + column(table[AT_LB, :]))
    enc[...] = value.astype(BF16)
    s3[...] = slope
    for g in range(steps):
        for copy in leaves(g):
            copy.wait()
    for copy in last_copies[1:]:
        copy.wait()


def three_parts(row):
    high = row.astype(BF16).astype(F32)
    middle = (row - high).astype(BF16).astype(F32)
    return jnp.concatenate([high, middle, row - high - middle], axis=0)


def with_ones(value):
    return jnp.concatenate([value, ones_rows(value.shape[1])], axis=0)


def ones_rows(lanes):
    return (iota((16, lanes), 0) < 3).astype(F32).astype(BF16)


def plan_kernel(
    section,
    slots,
    enc,
    s3,
    h2,
    bwt,
    branch_far,
    value_w,
    table,
    keep,
    send,
    small,
    g3,
    parts,
    vht,
    vhw,
    ow,
    mine,
    pre,
    dbr,
    dval,
    low,
    hid,
    gb,
    branch_w,
    sem,
    *,
    per_pair,
    depth,
):
    width = enc.shape[0]
    options = branch_w.shape[0]
    pairs = options // 2
    two = 2 * width
    sec = section[0]
    branch_copy = pltpu.make_async_copy(branch_far, branch_w, sem)
    branch_copy.start()

    count = slots.shape[0]
    dest = jnp.concatenate(
        [table[AT_DEST + k : AT_DEST + k + 1, :] for k in range(count // LANES)], axis=1
    )
    own = jnp.where(sec == 0, dest[:, :LANES], dest[:, LANES:])
    others = jnp.transpose(jnp.broadcast_to(dest, (LANES, count)))
    index = iota((count, LANES), 1) + sec * LANES
    earlier = (others == own) & (iota((count, LANES), 0) < index)
    rank = jnp.sum(earlier.astype(F32), axis=0, keepdims=True)
    bucket = own * float(per_pair) + rank
    chosen = (iota((count, LANES), 0).astype(F32) == bucket).astype(F32).astype(BF16)
    numbers = slots[...]
    high = numbers.astype(BF16)
    middle = (numbers - high.astype(F32)).astype(BF16)
    rest = (numbers - high.astype(F32) - middle.astype(F32)).astype(BF16)
    mine[...] = sum(dot_rows(v, chosen) for v in (rest, middle, high))[: mine.shape[0]]

    pad = jnp.zeros((13, width), F32)
    scalars = table[AT_SCALARS, :]
    head_w = table[AT_HW, :]
    rows = [value_w[...].astype(F32), three_parts(table[AT_VB, :]), pad]
    vht[0:width, :] = jnp.transpose(jnp.concatenate(rows, axis=0)).astype(BF16)
    vht[width:, :] = jnp.zeros((16, width + 16), BF16)
    lane = iota((1, 16), 1)
    for k in range(2):
        bias = three_parts(jnp.broadcast_to(scalars[:, 1 + k : 2 + k], (1, 16)))
        bias = sum(jnp.where(lane == j, bias[j : j + 1], 0.0) for j in range(3))
        vht[width + k : width + k + 1, 0:width] = head_w[k : k + 1].astype(BF16)
        vht[width + k : width + k + 1, width:] = bias.astype(BF16)
    vhw[:, 0:width] = value_w[...]
    vhw[:, width:] = jnp.transpose(
        jnp.concatenate([head_w, jnp.zeros((14, width), F32)], axis=0)
    ).astype(BF16)
    ow[...] = jnp.broadcast_to(column(table[AT_OW, :]), (width, LANES))
    wide_ow = jnp.concatenate([ow[...], ow[...]], axis=1)

    labels = iota((options, LANES), 0).astype(F32)
    state = enc[...].astype(F32)
    rounded_all, saved = [], []
    for level in range(depth):
        picked = labels == mine[level : level + 1, :]
        rounded = state.astype(BF16)
        rounded_all.append(rounded)
        pre[...] = dot(bwt[...], with_ones(rounded))
        following = state
        reward, discount, value = [], [], []
        for t in range(pairs):
            at = slice(t * two, (t + 1) * two)
            act, slope = silu_pair(pre[at, :])
            dbr[level, at, :] = slope
            left = state + act[:width]
            right = state + act[width:]
            following = jnp.where(picked[2 * t : 2 * t + 1], left, following)
            following = jnp.where(picked[2 * t + 1 : 2 * t + 2], right, following)
            both = with_ones(jnp.concatenate([left.astype(BF16), right.astype(BF16)], axis=1))
            low[level, t] = both
            got = dot(vht[...], both)
            act, slope = silu_pair(got[:width])
            dval[level, t] = slope
            hidden = act.astype(BF16)
            hid[level, t] = hidden
            worth = jnp.sum(hidden.astype(F32) * wide_ow, axis=0, keepdims=True)
            for k in range(2):
                span = slice(k * LANES, (k + 1) * LANES)
                value.append(worth[:, span])
                reward.append(got[width : width + 1, span])
                discount.append(got[width + 1 : width + 2, span])
        reward = jnp.concatenate(reward, axis=0)
        discount = jax.nn.sigmoid(jnp.concatenate(discount, axis=0))
        value = jnp.concatenate(value, axis=0) + scalars[:, 3:4]
        quality = reward + discount * value
        top = jnp.max(quality, axis=0, keepdims=True)
        shifted = jnp.exp(quality - top)
        total = jnp.sum(shifted, axis=0, keepdims=True)
        live = (mine[depth : depth + 1, :] > level).astype(F32)
        chosen = picked.astype(F32)

        def target(kind):
            at = depth + 1 + kind * depth + level
            return mine[at : at + 1, :]

        reward_gap = live * (jnp.sum(chosen * reward, axis=0, keepdims=True) - target(0))
        discount_gap = live * (jnp.sum(chosen * discount, axis=0, keepdims=True) - target(1))
        plan_gap = live * (top + jnp.log(total) - target(2))
        grad_quality = plan_gap * (shifted / total)
        head_two = (chosen * discount_gap + grad_quality * value) * discount * (1.0 - discount)
        saved.append(
            (
                picked,
                (chosen * reward_gap + grad_quality).astype(BF16).astype(F32),
                head_two.astype(BF16).astype(F32),
                (grad_quality * discount).astype(BF16).astype(F32),
                reward_gap * reward_gap + discount_gap * discount_gap + plan_gap * plan_gap,
            )
        )
        state = following

    branch_copy.wait()
    out_sum = jnp.zeros((width, two), F32)
    value_sum = jnp.zeros((width + 16, width + 16), F32)
    grad_next = jnp.zeros((width, LANES), F32)
    line = iota((16, two), 0)
    for level in reversed(range(depth)):
        picked, head_one, head_two, grad_value, _ = saved[level]
        upward = jnp.zeros((width, LANES), F32)
        for t in range(pairs):
            at = slice(t * two, (t + 1) * two)

            def across(rows):
                return jnp.concatenate(
                    [rows[2 * t : 2 * t + 1], rows[2 * t + 1 : 2 * t + 2]], axis=1
                )

            worth = across(grad_value)
            grad_pre = (worth * wide_ow * dval[level, t]).astype(BF16)
            out_sum = out_sum + hid[level, t].astype(F32) * worth
            heads = jnp.where(line == 0, across(head_one), 0.0)
            heads = jnp.where(line == 1, across(head_two), heads)
            heads = jnp.where(line == 2, worth, heads)
            stacked = jnp.concatenate([grad_pre, heads.astype(BF16)], axis=0)
            value_sum = value_sum + dot_lanes(stacked, low[level, t])
            moved = dot(vhw[...], stacked)
            left = moved[:, :LANES] + jnp.where(picked[2 * t : 2 * t + 1], grad_next, 0.0)
            right = moved[:, LANES:] + jnp.where(picked[2 * t + 1 : 2 * t + 2], grad_next, 0.0)
            grad_branch = jnp.concatenate([left, right], axis=0) * dbr[level, at, :]
            grad_branch = grad_branch.astype(BF16)
            gb[level, at, :] = grad_branch
            weights = jnp.concatenate([branch_w[2 * t], branch_w[2 * t + 1]], axis=1)
            upward = upward + (left + right + dot(weights, grad_branch))
        grad_next = upward

    linear_rows = h2.shape[0]
    half = (linear_rows + options * width + width) // 2
    rest = linear_rows - half
    rounded = with_ones(jnp.concatenate(rounded_all, axis=1))
    small[...] = jnp.zeros_like(small)
    if half < keep.shape[0]:
        for k in range(2):
            parts[k, half:, :] = jnp.zeros((keep.shape[0] - half, LANES), BF16)
    for t in range(pairs):
        at = slice(t * two, (t + 1) * two)
        grads = jnp.concatenate([gb[level, at, :] for level in range(depth)], axis=1)
        got = dot_lanes(rounded, grads)
        for k in range(2):
            o = 2 * t + k
            span = slice(k * width, (k + 1) * width)
            rows = slice(rest + o * width, rest + (o + 1) * width)
            parts[1 - sec, rows, :] = got[:width, span].astype(BF16)
            small[o : o + 1, :] = got[width : width + 1, span]
    after = rest + options * width
    parts[1 - sec, after : after + width, :] = jnp.transpose(value_sum[:width, :width]).astype(BF16)

    grad_three = (grad_next.astype(BF16).astype(F32) * s3[...]).astype(BF16)
    g3[...] = grad_three
    chunk = linear_rows // 9
    for i in range(8):
        at = slice(i * chunk, (i + 1) * chunk)
        parts[sec, at, :] = dot_lanes(h2[at, :], grad_three).astype(BF16)
    last = dot_lanes(h2[8 * chunk :, :], grad_three).astype(BF16)
    parts[sec, 8 * chunk : half, :] = last[: half - 8 * chunk]
    parts[1 - sec, 0:rest, :] = last[half - 8 * chunk :]
    keep[...] = parts[0]
    send[...] = parts[1]

    small[AT_VB, :] = row_of(value_sum[:width, width : width + 1])
    small[AT_OW, :] = row_of(jnp.sum(out_sum, axis=1, keepdims=True))
    small[AT_HW, :] = value_sum[width : width + 2, :width]
    small[AT_LB, :] = row_of(jnp.sum(grad_three.astype(F32), axis=1, keepdims=True))
    loss = 0.5 * jnp.sum(sum(kept[4] for kept in saved), axis=1, keepdims=True)
    ends = [loss] + [value_sum[width + k : width + k + 1, width : width + 1] for k in range(3)]
    lane = iota((1, LANES), 1)
    line = jnp.zeros((1, LANES), F32)
    for k, end in enumerate(ends):
        line = jnp.where(lane == k, end, line)
    small[AT_SCALARS, :] = line


def back_kernel(g3, lw, s2, s1, h1, w2t, g1_far, c2, sums, t2, g2, g1, sems):
    side, k1 = s1.shape[1], s1.shape[2]
    k2 = w2t.shape[0]
    inner = side // 2 - 1
    row_len = inner * k2
    tap, pix = iota((LANES, 256), 1), iota((LANES, 256), 0)
    for yrel in range(2):
        for p in range(3):
            hit = (
                ((tap & 15) == (pix & 15))
                & ((tap >> 6) == (pix >> 6) + 2 * (1 - yrel))
                & (((tap >> 4) & 3) == ((pix >> 4) & 3) + 2 - 2 * p)
            )
            at = (yrel * 3 + p) * k2
            t2[:, at : at + k2] = dot_lanes(hit.astype(F32).astype(BF16), w2t[...]).astype(BF16)
    g2[0] = jnp.zeros(g2.shape[1:], BF16)
    g2[inner + 1] = jnp.zeros(g2.shape[1:], BF16)
    g1[0] = jnp.zeros(g1.shape[1:], BF16)
    g1[side + 1] = jnp.zeros(g1.shape[1:], BF16)
    zero = jnp.zeros((k2, LANES), BF16)
    total_one = jnp.zeros((k1, LANES), F32)
    total_two = jnp.zeros((k2, LANES), F32)
    for y in range(inner):
        at = slice(y * row_len, (y + 1) * row_len)
        grad = dot(lw[at, :], g3[...]) * s2[at, :].astype(F32)
        grad = grad.astype(BF16).reshape(inner, k2, LANES)
        g2[y + 1] = grad
        total_two = total_two + jnp.sum(grad.astype(F32), axis=0)
    ends = (0, side // 2 + 1, side + 2)
    copies = [
        pltpu.make_async_copy(g1.at[a:b], g1_far.at[a:b], sems.at[k])
        for k, (a, b) in enumerate(zip(ends, ends[1:]))
    ]
    reach, cols = 5, 8
    total = jnp.zeros((2 * reach * k2, 2 * cols * k1), F32)
    grads, tiles = [], []
    for b in range(side // 2):
        cut = []
        for j in range(side // 4):
            pieces = []
            for yrel in range(2):
                for p in range(3):
                    x = 2 * j - 1 + p
                    pieces.append(g2[b + yrel, x] if 0 <= x < inner else zero)
            cut.append(jnp.concatenate(pieces, axis=0))
        got = dot(t2[...], jnp.concatenate(cut, axis=1))
        for u in range(2):
            for j in range(side // 4):
                part = got[u * 64 : (u + 1) * 64, j * LANES : (j + 1) * LANES]
                slope = s1[2 * b + u + 1, 4 * j : 4 * j + 4].astype(F32)
                grad = (part.reshape(4, k1, LANES) * slope).astype(BF16)
                g1[2 * b + u + 1, 4 * j : 4 * j + 4] = grad
                total_one = total_one + jnp.sum(grad.astype(F32), axis=0)
        if 2 * b + 3 == ends[1]:
            copies[0].start()
        for j in range(-(-side // cols)):
            end = min((j + 1) * cols, side)
            tile = h1[2 * b + 1 : 2 * b + 3, j * cols : end]
            if end < (j + 1) * cols:
                rest = jnp.zeros((2, (j + 1) * cols - end, k1, LANES), BF16)
                tile = jnp.concatenate([tile, rest], axis=1)
            tiles.append(tile.reshape(2 * cols * k1, LANES))
            pieces = []
            for half in range(2):
                for p in range(reach):
                    x = 4 * j - 1 + p
                    pieces.append(g2[b + 1 - half, x] if 0 <= x < inner else zero)
            grads.append(jnp.concatenate(pieces, axis=0))
        if b % 2:
            total = total + dot_lanes(
                jnp.concatenate(grads, axis=1), jnp.concatenate(tiles, axis=1)
            )
            grads, tiles = [], []
    copies[1].start()
    line = 4 * k1
    for half in range(2):
        for u in range(2):
            tap_row = jnp.zeros((k2, line), F32)
            for p in range(reach):
                at = (half * reach + p) * k2
                part = total[at : at + k2, u * 2 * line : (u + 1) * 2 * line]
                start = 2 * k1 * (p - 1)
                piece = part[:, max(start, 0) : min(start + line, 2 * line)]
                if start < 0:
                    piece = jnp.concatenate([jnp.zeros((k2, -start), F32), piece], axis=1)
                if start + line > 2 * line:
                    rest = jnp.zeros((k2, start - line), F32)
                    piece = jnp.concatenate([piece, rest], axis=1)
                tap_row = tap_row + piece
            at = (2 * half + u) * line
            c2[:, at : at + line] = tap_row
    sums[...] = jnp.zeros_like(sums)
    sums[0:1, 0:k1] = row_of(jnp.sum(total_one, axis=1, keepdims=True))
    sums[1:2, 0:k2] = row_of(jnp.sum(total_two, axis=1, keepdims=True))
    for copy in copies:
        copy.wait()


def pixel_band(sec, w1t, channels):
    k1 = w1t.shape[0]
    rows = 64 * channels
    row, tap = iota((rows, 256), 0), iota((rows, 256), 1)
    moves = ((tap >> 6) == row % channels + sec * channels) & ((tap & 63) == row // channels)
    taps = dot_lanes(moves.astype(F32).astype(BF16), w1t)
    line, span = COLS * channels, 8 * channels
    blocks = {}
    for half in range(2):
        for p in range(NEAR):
            pieces = []
            for u in range(4):
                at = (4 * half + u) * span
                start = 4 * (p - 1) * channels
                cut = taps[at + max(0, -start) : at + min(span, line - start)]
                start = max(start, 0)
                pieces += [jnp.zeros((start, k1), F32)] if start else []
                pieces.append(cut)
                rest = line - start - cut.shape[0]
                pieces += [jnp.zeros((rest, k1), F32)] if rest else []
            blocks[half, p] = jnp.concatenate(pieces, axis=0)
    zero = jnp.zeros((4 * line, k1), F32)
    lines = []
    for r in range(STEP):
        cols = [
            blocks.get((r + 1 - yrel, p), zero) for yrel in range(STEP + 1) for p in range(NEAR)
        ]
        lines.append(jnp.concatenate(cols, axis=1))
    return jnp.concatenate(lines, axis=0).astype(BF16)


def first_kernel(section, frames_far, g1_far, after, c1, frames, g1, acc, sems):
    side, k1 = g1.shape[1], g1.shape[2]
    img, _, channels, _ = frames.shape
    steps = img // 4 // STEP
    arrives = frame_copies(section, frames_far, frames, sems)
    g1_copy = pltpu.make_async_copy(g1_far, g1, sems.at[steps])
    arrives(0).start()
    g1_copy.start()
    for g in range(1, steps):
        arrives(g).start()
    acc[...] = jnp.zeros_like(acc)
    zero = jnp.zeros((k1, LANES), BF16)
    g1_copy.wait()

    def one_step(g, carry):
        arrives(g).wait()
        pixels, grads = [], []
        for j in range(img // COLS):
            rows = [pl.multiple_of(4 * (STEP * g + r), 4) for r in range(STEP)]
            pixels.append(
                jnp.concatenate([tile_rows(frames, row, j, COLS) for row in rows], axis=0)
            )
            pieces = []
            for yrel in range(STEP + 1):
                for p in range(NEAR):
                    x = 3 * j - 1 + p
                    pieces.append(g1[STEP * g + yrel, x] if 0 <= x < side else zero)
            grads.append(jnp.concatenate(pieces, axis=0))
        acc[...] += dot_lanes(jnp.concatenate(pixels, axis=1), jnp.concatenate(grads, axis=1))
        return carry

    lax.fori_loop(0, steps, one_step, 0)
    fold_first(acc, c1, channels, k1)


def fold_first(acc, c1, channels, k1):
    line = COLS * channels
    step = 4 * channels
    taps = []
    for half in range(2):
        total = sum(
            acc[r * 4 * line : (r + 1) * 4 * line, :][
                :, (r + 1 - half) * NEAR * k1 : (r + 2 - half) * NEAR * k1
            ]
            for r in range(STEP)
        )
        for u in range(4):
            part = total[u * line : (u + 1) * line]
            cols = [part[:, p * k1 : (p + 1) * k1] for p in range(NEAR)]
            taps.append(cols[1][0:step] + cols[2][step : 2 * step] + cols[3][2 * step :])
            taps.append(cols[0][0:step] + cols[1][step : 2 * step] + cols[2][2 * step :])
    row, col = iota((256, 256), 0), iota((256, 256), 1)
    moves = ((row & 3) == (col >> 6)) & ((row >> 2) == (col & 63))
    grad = dot_rows(jnp.concatenate(taps, axis=0), moves.astype(F32), EXACT)
    for half in range(2):
        c1[half * k1 : (half + 1) * k1, :] = grad[:, half * LANES : (half + 1) * LANES].astype(BF16)


def pixels_kernel(section, weights, mine_far, other_far, after, *refs, start, steps, begins):
    out, token, band_out, held, mine, other, sems = refs[-7:]
    side, k1 = mine.shape[1], mine.shape[2]


    def fetches(g):
        first, end = (STEP * g + 1 if g else 0), STEP * (g + 1) + 1
        pairs = ((mine_far, mine), (other_far, other))
        return [
            pltpu.make_async_copy(
                far.at[STEP * start + first : STEP * start + end],
                here.at[first:end],
                sems.at[2 + g, k],
            )
            for k, (far, here) in enumerate(pairs)
        ]

    for g in range(steps):
        for fetch in fetches(g):
            fetch.start()
    img, channels = out.shape[1], out.shape[2]
    sec = section[0]
    line = COLS * channels
    flat = held.reshape(2, 2, 4 * STEP, img * channels, LANES)
    if begins:
        band_out[...] = pixel_band(sec, weights[...], channels)
        band = band_out
    else:
        band = weights
        band_out[...] = jnp.zeros_like(band_out)
    token[...] = jnp.zeros_like(token)

    def writes(g):
        rows = slice(4 * STEP * (start + g), 4 * STEP * (start + g + 1))
        places = (sec * LANES, (1 - sec) * LANES)
        return [
            pltpu.make_async_copy(
                held.at[g % 2, k],
                out.at[rows, :, :, pl.ds(pl.multiple_of(places[k], LANES), LANES)],
                sems.at[g % 2, k],
            )
            for k in range(2)
        ]

    zero = jnp.zeros((k1, 2 * LANES), BF16)
    for g in range(steps):
        for fetch in fetches(g):
            fetch.wait()
        if g >= 2:
            for copy in writes(g - 2):
                copy.wait()
        for j in range(img // COLS):
            pieces = []
            for yrel in range(STEP + 1):
                for p in range(NEAR):
                    x, y = 3 * j - 1 + p, STEP * g + yrel
                    if 0 <= x < side:
                        pieces.append(jnp.concatenate([mine[y, x], other[y, x]], axis=1))
                    else:
                        pieces.append(zero)
            got = dot(band[...], jnp.concatenate(pieces, axis=0))
            for k in range(4 * STEP):
                at = slice(k * line, (k + 1) * line)
                span = slice(j * line, (j + 1) * line)
                flat[g % 2, 0, k, span, :] = got[at, :LANES]
                flat[g % 2, 1, k, span, :] = got[at, LANES:]
        for copy in writes(g):
            copy.start()
    for g in range(max(steps - 2, 0), steps):
        for copy in writes(g):
            copy.wait()


def two_parts(value):
    high = value.astype(BF16).astype(F32)
    return jnp.concatenate([high, value - high], axis=0).astype(BF16)


def one_part(pair):
    rows = pair.shape[0] // 2
    pair = pair.astype(F32)
    return pair[:rows] + pair[rows:]


def merge_kernel(keep, recv, small, c2, sums, out_far, lines, out, sems):
    members = out.shape[0]
    size = keep.shape[0] // members
    k2 = c2.shape[0]
    lines[...] = jnp.zeros_like(lines)
    at = small.shape[0]
    lines[0:at, :] = small[...]
    for half in range(2):
        lines[at : at + k2, :] = c2[:, half * LANES : (half + 1) * LANES]
        at += k2
    lines[at : at + sums.shape[0], :] = sums[...]
    for k in range(members):
        at = slice(k * size, (k + 1) * size)
        out[k, 0:size, :] = (keep[at, :].astype(F32) + recv[at, :].astype(F32)).astype(BF16)
        out[k, size:, :] = two_parts(lines[k * SHORT : (k + 1) * SHORT, :])
        pltpu.make_async_copy(out.at[k], out_far.at[k], sems.at[k]).start()
    for k in range(members):
        pltpu.make_async_copy(out.at[k], out_far.at[k], sems.at[k]).wait()


def cube_kernel(got, c1, after, out):
    members = got.shape[0]
    size = got.shape[1] - 2 * SHORT
    out[0:size, :] = sum(got[k, 0:size, :].astype(F32) for k in range(members)).astype(BF16)
    total = sum(one_part(got[k, size:, :]) for k in range(members))
    out[size : size + 2 * SHORT, :] = two_parts(total)
    out[size + 2 * SHORT :, :] = c1[...]


def added(a, b):
    size = a.shape[0] - 2 * SHORT - 32
    spans = (slice(0, size), slice(size, size + 2 * SHORT), slice(size + 2 * SHORT, None))
    first, last = ((a[k, :].astype(F32) + b[k, :].astype(F32)).astype(BF16) for k in spans[::2])
    middle = two_parts(one_part(a[spans[1], :]) + one_part(b[spans[1], :]))
    return jnp.concatenate([first, middle, last], axis=0)


def add_kernel(a, b, out):
    out[...] = added(a[...], b[...])


def spread_kernel(a, b, out_far, out, sems):
    out[...] = added(a[...], b[...])
    copies = [
        pltpu.make_async_copy(out, out_far.at[k], sems.at[k]) for k in range(out_far.shape[0])
    ]
    for copy in copies:
        copy.start()
    for copy in copies:
        copy.wait()


def relay_kernel(got, after, out):
    out[...] = got[...]


def unpack_half(which, got, lw, bw, vw, stage, stage_b, sems):
    members = got.shape[0]
    size = stage.shape[0] // members
    linear_rows, width = lw.shape
    options = bw.shape[0]
    half = (linear_rows + options * width + width) // 2
    rest = linear_rows - half

    @pl.when(which == 0)
    def _():
        copies = []
        for k in range(members):
            start, end = k * size, min((k + 1) * size, half)
            stage[start:end, :] = got[k, 0 : end - start, :].astype(F32)
            copies.append(
                pltpu.make_async_copy(stage.at[start:end], lw.at[start:end], sems.at[k])
            )
            copies[-1].start()
        for copy in copies:
            copy.wait()

    @pl.when(which == 1)
    def _():
        def rows(start, end):
            parts = []
            while start < end:
                k, at = start // size, start % size
                count = min(size - at, end - start)
                parts.append(got[k, at : at + count, :])
                start += count
            value = parts[0] if len(parts) == 1 else jnp.concatenate(parts, axis=0)
            return value.astype(F32)

        stage[0:rest, :] = rows(0, rest)
        copies = [pltpu.make_async_copy(stage.at[0:rest], lw.at[half:], sems.at[0])]
        copies[0].start()
        group = options // 3
        for o in range(options):
            stage_b[o] = rows(rest + o * width, rest + (o + 1) * width)
            if o % group == group - 1:
                part = slice(o + 1 - group, o + 1)
                copy = pltpu.make_async_copy(
                    stage_b.at[part], bw.at[part], sems.at[1 + o // group]
                )
                copy.start()
                copies.append(copy)
        at = rest + options * width
        stage[rest : rest + width, :] = rows(at, at + width)
        copies.append(
            pltpu.make_async_copy(stage.at[rest : rest + width], vw, sems.at[1 + options // group])
        )
        copies[-1].start()
        for copy in copies:
            copy.wait()


def own_kernel(section, mine, lw, bw, vw, stage, stage_b, sems):
    unpack_half(section[0], mine, lw, bw, vw, stage, stage_b, sems)


def unpack_kernel(section, mine, other, *refs):
    lw, bw, vw = refs[3:6]
    little = (len(refs) - 10) // 2
    far, near = refs[6 : 6 + little], refs[6 + little : 6 + 2 * little]
    loss, c1, b1, c2, b2, lb, bb, hw, hb, vb, ow, ob = near
    stage, stage_b, lines, sems = refs[-4:]
    options = bw.shape[0]
    k1, k2 = c1.shape[0], c2.shape[0]
    size = stage.shape[0] // CUBE
    grad = [jnp.zeros((k1, LANES), F32) for _ in range(2)]
    for k in range(CUBE):
        pair = slice(size, size + 2 * SHORT)
        at = slice(k * SHORT, (k + 1) * SHORT)
        lines[at, :] = one_part(mine[k, pair, :]) + one_part(other[k, pair, :])
        for ref in (mine, other):
            for h in range(2):
                at = size + 2 * SHORT + h * k1
                grad[h] += ref[k, at : at + k1, :].astype(F32)
    for part in range(2):
        c1[:, part * LANES : (part + 1) * LANES] = grad[part]
    bb[...] = lines[0:options, :]
    vb[...] = lines[AT_VB, :]
    ow[...] = lines[AT_OW, :]
    hw[...] = lines[AT_HW, :]
    lb[...] = lines[AT_LB, :]
    scalars = lines[AT_SCALARS, :]
    loss[...] = scalars[:, 0:1]
    hb[...] = scalars[:, 1:3]
    ob[...] = scalars[:, 3:4]
    at = TABLE
    for part in range(2):
        c2[:, part * LANES : (part + 1) * LANES] = lines[at : at + k2, :]
        at += k2
    b1[...] = lines[at : at + 1, 0:k1]
    b2[...] = lines[at + 1 : at + 2, 0:k2]
    copies = [
        pltpu.make_async_copy(a, b, sems.at[CUBE + k]) for k, (a, b) in enumerate(zip(near, far))
    ]
    for copy in copies:
        copy.start()
    unpack_half(1 - section[0], other, lw, bw, vw, stage, stage_b, sems)
    for copy in copies:
        copy.wait()


def numbers_kernel(*refs):
    given = (len(refs) - 3) // 2
    out, table = refs[given : given + 2]
    here, sems = refs[given + 2 : -1], refs[-1]
    copies = [
        pltpu.make_async_copy(far, near, sems.at[k])
        for k, (far, near) in enumerate(zip(refs[:given], here))
    ]
    for copy in copies:
        copy.start()
    options, depth, targets, destination, b1, b2, lb, bb, hw, vb, ow, hb, ob = here
    for copy in copies:
        copy.wait()
    levels, kinds = options.shape[0], targets.shape[0]
    slots = depth.shape[1]
    rows = [options[...].astype(F32), depth[...].astype(F32)]
    rows += [targets[k] for k in range(kinds)]
    rows.append(jnp.zeros((LANES - levels - 1 - kinds * levels, slots), F32))
    out[...] = jnp.transpose(jnp.concatenate(rows, axis=0))
    table[...] = jnp.zeros_like(table)
    table[0 : bb.shape[0], :] = bb[...]
    table[AT_VB, :] = vb[...]
    table[AT_OW, :] = ow[...].astype(F32)
    table[AT_HW, :] = hw[...].astype(F32)
    table[AT_LB, :] = lb[...]
    table[AT_B1, 0 : b1.shape[1]] = b1[...]
    table[AT_B2, 0 : b2.shape[1]] = b2[...]
    lane = iota((1, LANES), 1)
    scalars = jnp.zeros((1, LANES), F32)
    for k, value in ((1, hb[:, 0:1]), (2, hb[:, 1:2]), (3, ob[...])):
        scalars = jnp.where(lane == k, value, scalars)
    table[AT_SCALARS, :] = scalars
    for k in range(slots // LANES):
        part = destination[:, k * LANES : (k + 1) * LANES]
        table[AT_DEST + k : AT_DEST + k + 1, :] = part.astype(F32)


def whole(shape):
    zeros = (0,) * len(shape)
    return pl.BlockSpec(shape, lambda *_: zeros)


ANYWHERE = pl.BlockSpec(memory_space=pl.ANY)
SCALARS = pl.BlockSpec(memory_space=pltpu.SMEM)


def params():
    return pltpu.CompilerParams(vmem_limit_bytes=VMEM_BYTES)


def shape_of(*shape, dtype=F32):
    return jax.ShapeDtypeStruct(shape, dtype)


def cost(microseconds):
    return pl.CostEstimate(
        flops=int(1.1e9 * microseconds), bytes_accessed=int(3.6e6 * microseconds), transcendentals=0
    )


def stays(value):
    return pltpu.with_memory_space_constraint(value, pltpu.HBM)


def encode(section, frames, w1t, w2t, lw, branch_w, table):
    options = branch_w.shape[0]
    img = frames.shape[0]
    blocks = img // 4
    side = blocks - 1
    k1, k2, width = w1t.shape[0], w2t.shape[0], lw.shape[1]
    flat = lw.shape[0]
    vmem = pltpu.VMEM
    near = pl.BlockSpec(memory_space=vmem)
    grid_one = (blocks, side, k1, LANES)
    return pl.pallas_call(
        encode_kernel,
        in_specs=[SCALARS, ANYWHERE, near, near, ANYWHERE, ANYWHERE, near],
        out_specs=[ANYWHERE] * 3 + [near] * 4,
        out_shape=(
            pltpu.HBM(grid_one, BF16),
            pltpu.HBM(grid_one, BF16),
            pltpu.HBM((flat, LANES), BF16),
            shape_of(flat, LANES, dtype=BF16),
            shape_of(width, LANES, dtype=BF16),
            shape_of(width, LANES),
            shape_of(options * width, width + 16, dtype=BF16),
        ),
        scratch_shapes=[
            vmem((img, img, frames.shape[2], LANES), BF16),
            vmem(lw.shape, BF16),
            vmem(branch_w.shape, BF16),
            vmem(grid_one, BF16),
            vmem(grid_one, BF16),
            vmem((flat, LANES), BF16),
            vmem((2 * REACH * k1, 256), BF16),
            vmem((2 * k1, 64), BF16),
            vmem((6 * k2, LANES), BF16),
            vmem((k1, LANES), F32),
            vmem((k2, LANES), F32),
            vmem((side, k1, LANES), F32),
            vmem((side // 2 - 1, k2, LANES), F32),
            pltpu.SemaphoreType.DMA((4, max(blocks // STEP, 3))),
        ],
        compiler_params=params(),
        cost_estimate=cost(9),
        name="encode",
    )(section, frames, w1t, w2t, lw, branch_w, table)


def plan(
    section, slots, enc, s3, h2, bwt, branch_w, value_w, table, per_pair, depth, half_rows
):
    width = enc.shape[0]
    options = branch_w.shape[0]
    two = 2 * width
    pairs = options // 2
    outs = (
        shape_of(half_rows, LANES, dtype=BF16),
        shape_of(half_rows, LANES, dtype=BF16),
        shape_of(TABLE, LANES),
        shape_of(width, LANES, dtype=BF16),
    )
    vmem = pltpu.VMEM
    near = pl.BlockSpec(memory_space=vmem)
    return pl.pallas_call(
        functools.partial(plan_kernel, per_pair=per_pair, depth=depth),
        in_specs=[SCALARS, near, near, near, near, near, ANYWHERE, near, near],
        out_shape=outs,
        scratch_shapes=[
            vmem((2, half_rows, LANES), BF16),
            vmem((width + 16, width + 16), BF16),
            vmem((width, width + 16), BF16),
            vmem((width, LANES), F32),
            vmem((16, LANES), F32),
            vmem((options * width, LANES), F32),
            vmem((depth, options * width, LANES), F32),
            vmem((depth, pairs, width, two), F32),
            vmem((depth, pairs, width + 16, two), BF16),
            vmem((depth, pairs, width, two), BF16),
            vmem((depth, options * width, LANES), BF16),
            vmem(branch_w.shape, BF16),
            pltpu.SemaphoreType.DMA,
        ],
        compiler_params=params(),
        cost_estimate=cost(11),
        name="plan",
    )(section, slots, enc, s3, h2, bwt, branch_w, value_w, table)


def back(g3, lw, s2, s1, h1, w2t):
    _, side, k1 = s1.shape[:3]
    k2 = w2t.shape[0]
    inner = side // 2 - 1
    padded = (side + 2, side, k1, LANES)
    near = pl.BlockSpec(memory_space=pltpu.VMEM)
    return pl.pallas_call(
        back_kernel,
        in_specs=[near] * 6,
        out_specs=[ANYWHERE, near, near],
        out_shape=(pltpu.HBM(padded, BF16), shape_of(k2, 256), shape_of(8, LANES)),
        scratch_shapes=[
            pltpu.VMEM((LANES, 6 * k2), BF16),
            pltpu.VMEM((inner + 2, inner, k2, LANES), BF16),
            pltpu.VMEM(padded, BF16),
            pltpu.SemaphoreType.DMA((2,)),
        ],
        compiler_params=params(),
        cost_estimate=cost(25),
        name="back",
    )(g3, lw, s2, s1, h1, w2t)


def first(section, frames, g1, after):
    img, _, channels, _ = frames.shape
    k1 = g1.shape[2]
    return pl.pallas_call(
        first_kernel,
        in_specs=[SCALARS, ANYWHERE, ANYWHERE, ANYWHERE],
        out_shape=shape_of(2 * k1, LANES, dtype=BF16),
        scratch_shapes=[
            pltpu.VMEM((img, img, channels, LANES), BF16),
            pltpu.VMEM(g1.shape, BF16),
            pltpu.VMEM((STEP * 4 * COLS * channels, (STEP + 1) * NEAR * k1), F32),
            pltpu.SemaphoreType.DMA((img // 4 // STEP + 1,)),
        ],
        compiler_params=params(),
        cost_estimate=cost(45),
        name="first",
    )(section, frames, g1, after)


def pixels(section, weights, mine, other, shape, start, steps, after, done=None):
    img, _, channels, _ = shape
    k1 = mine.shape[2]
    band = (STEP * 4 * COLS * channels, (STEP + 1) * NEAR * k1)
    near = pl.BlockSpec(memory_space=pltpu.VMEM)
    operands = (section, weights, mine, other, after)
    specs = [SCALARS, near, ANYWHERE, ANYWHERE, ANYWHERE]
    window = pltpu.VMEM((STEP * steps + 1,) + mine.shape[1:], BF16)
    aliases = {}
    if done is not None:
        aliases = {len(operands): 0}
        operands += (done,)
        specs.append(ANYWHERE)
    outs = [shape_of(*shape), shape_of(8, LANES), shape_of(*band, dtype=BF16)]
    return pl.pallas_call(
        functools.partial(pixels_kernel, start=start, steps=steps, begins=done is None),
        in_specs=specs,
        out_specs=[ANYWHERE, near, near],
        out_shape=outs,
        scratch_shapes=[
            pltpu.VMEM((2, 2, 4 * STEP, img, channels, LANES), F32),
            window,
            window,
            pltpu.SemaphoreType.DMA((2 + steps, 2)),
        ],
        input_output_aliases=aliases,
        compiler_params=params(),
        cost_estimate=cost(2 + 0.8 * steps),
        name="pixels",
    )(*operands)


def small_call(
    kernel, outs, operands, scratch=(), name=None, place=None, after=(), weight=0.3, far=False
):
    specs = [pl.BlockSpec(memory_space=pltpu.VMEM)] * len(operands)
    if place is not None:
        operands = (*place, *operands)
        specs = [pl.BlockSpec(memory_space=pltpu.SMEM)] * len(place) + specs
    return pl.pallas_call(
        kernel,
        in_specs=specs + [ANYWHERE] * len(after),
        out_specs=jax.tree.map(
            lambda _: ANYWHERE if far else pl.BlockSpec(memory_space=pltpu.VMEM), outs
        ),
        out_shape=outs,
        scratch_shapes=list(scratch),
        compiler_params=params(),
        cost_estimate=cost(weight),
        name=name,
    )(*operands, *after)


def round_up(value, step):
    return -(-value // step) * step


def swapped(value):
    return lax.ppermute(value, "section", [(0, 1), (1, 0)])


def exchanged(value):
    return lax.all_to_all(value, "batch", split_axis=0, concat_axis=0, tiled=True)


def cube_bits(section):
    bits = range((lax.axis_size("batch") - 1).bit_length())
    inside = (0, 1, 2 + section)
    return inside, [bit for bit in bits if bit not in inside]


def in_cube(value):
    count = lax.axis_size("batch")
    groups = []
    for section in range(2):
        inside, outside = cube_bits(section)
        for base in range(count):
            if not any(base >> bit & 1 for bit in inside):
                members = [
                    base + sum((k >> i & 1) << bit for i, bit in enumerate(inside))
                    for k in range(CUBE)
                ]
                groups.append([section * count + member for member in members])
    return lax.all_to_all(
        value,
        ("section", "batch"),
        split_axis=0,
        concat_axis=0,
        axis_index_groups=groups,
        tiled=True,
    )


def across_cubes(value, stage):
    count = lax.axis_size("batch")
    pairs = []
    for section in range(2):
        bit = cube_bits(section)[1][stage]
        pairs += [(section * count + b, section * count + (b ^ 1 << bit)) for b in range(count)]
    return lax.ppermute(value, ("section", "batch"), pairs)


def local(
    frames,
    destination,
    options,
    depth,
    targets,
    conv_one,
    bias_one,
    conv_two,
    bias_two,
    linear_w,
    linear_b,
    branch_w,
    branch_b,
    head_w,
    head_b,
    value_w,
    value_b,
    out_w,
    out_b,
):
    section = lax.axis_index("section").astype(jnp.int32)[None]
    peers = lax.axis_size("batch")
    frame_count = frames.shape[3]
    per_pair = frame_count // peers
    levels = options.shape[0]
    frames = stays(frames.transpose(1, 2, 0, 3))
    w1t, w2t = stays(conv_one.T), stays(conv_two.T)
    branch_w, value_w = stays(branch_w), stays(value_w)
    encoder_params = (w1t, bias_one, w2t, bias_two, linear_w, linear_b)
    planner_params = (branch_w, branch_b, head_w.T, head_b, value_w, value_b, out_w.T, out_b)
    width = linear_w.shape[1]
    big_rows = linear_w.shape[0] + (branch_w.shape[0] + 1) * width
    size = round_up(-(-big_rows // (2 * CUBE)), 16)

    given = [options, depth[None, :], targets, destination[None, :]]
    given += [bias_one, bias_two, linear_b, branch_b, head_w.T, value_b, out_w.T, head_b, out_b]
    given = [v if v.ndim > 1 else v[None, :] for v in given]
    numbers, table = pl.pallas_call(
        numbers_kernel,
        in_specs=[ANYWHERE] * len(given),
        out_shape=[shape_of(frame_count, LANES), shape_of(TABLE, LANES)],
        scratch_shapes=[pltpu.VMEM(v.shape, v.dtype) for v in given]
        + [pltpu.SemaphoreType.DMA((len(given),))],
        compiler_params=params(),
        cost_estimate=cost(1),
        name="numbers",
    )(*[stays(v) if v.size > 1 else v for v in given])
    slots = exchanged(numbers.reshape(peers, per_pair, LANES)).reshape(frame_count, LANES)

    h1, s1, s2, h2, enc, s3, bwt = encode(
        section, frames, w1t, w2t, stays(linear_w), branch_w, table
    )
    keep, send, small, g3 = plan(
        section, slots, enc, s3, h2, bwt, branch_w, value_w, table, per_pair, levels, CUBE * size
    )
    recv = swapped(send)
    channels = frames.shape[2] // lax.axis_size("section")
    g1, c2, sums = back(g3, linear_w, s2, s1, h1, w2t)
    other = swapped(g1)
    g1 = stays(g1)
    bf16 = functools.partial(shape_of, dtype=BF16)
    pieces = small_call(
        merge_kernel,
        bf16(CUBE, size + 2 * SHORT, LANES),
        (keep, recv, small, c2, sums),
        [
            pltpu.VMEM((CUBE * SHORT, LANES), F32),
            pltpu.VMEM((CUBE, size + 2 * SHORT, LANES), BF16),
            pltpu.SemaphoreType.DMA((CUBE,)),
        ],
        name="merge",
        far=True,
    )
    got = in_cube(pieces)
    c1 = first(section, frames, g1, pieces)
    img = frames.shape[0]
    steps = img // 4 // STEP
    draw = functools.partial(
        pixels, section, mine=g1, other=other, shape=(img, img, channels, 2 * LANES)
    )
    frames_grad, token, band = draw(weights=w1t, start=0, steps=1, after=c1)
    piece = bf16(size + 2 * SHORT + c1.shape[0], LANES)
    keep = small_call(cube_kernel, piece, (got, c1), name="cube", after=(token,))
    stages = len(cube_bits(0)[1])
    for stage in range(stages - 1):
        keep = small_call(add_kernel, piece, (keep, across_cubes(keep, stage)), name="add")
    keep = small_call(
        spread_kernel,
        bf16(CUBE, *piece.shape),
        (keep, across_cubes(keep, stages - 1)),
        [pltpu.VMEM(piece.shape, BF16), pltpu.SemaphoreType.DMA((CUBE,))],
        name="spread",
        far=True,
    )
    got = in_cube(keep)
    frames_grad, token, _ = draw(
        weights=band, start=1, steps=steps - 1, after=keep, done=frames_grad
    )
    got = small_call(relay_kernel, bf16(*got.shape), (got,), name="relay", after=(token,))
    got_other = swapped(got)
    shapes = [p.shape for p in encoder_params + planner_params]
    near = pl.BlockSpec(memory_space=pltpu.VMEM)
    flat = [shape_of(*(v if len(v) > 1 else (1,) + v)) for v in [(1, 1)] + shapes]
    large = [flat[k] for k in (5, 7, 11)]
    staged = [
        pltpu.VMEM((CUBE * size, LANES), F32),
        pltpu.VMEM(branch_w.shape, F32),
    ]
    little = [v for k, v in enumerate(flat) if k not in (5, 7, 11)]
    sems = pltpu.SemaphoreType.DMA((CUBE + len(little),))
    begun = pl.pallas_call(
        own_kernel,
        in_specs=[SCALARS, near],
        out_specs=[ANYWHERE] * 3,
        out_shape=large,
        scratch_shapes=[*staged, sems],
        compiler_params=params(),
        cost_estimate=cost(1),
        name="own",
    )(section, got)
    ends = pl.pallas_call(
        unpack_kernel,
        in_specs=[SCALARS, near, near] + [ANYWHERE] * 3,
        out_specs=[ANYWHERE] * (3 + len(little)),
        out_shape=large + little,
        scratch_shapes=[pltpu.VMEM(v.shape, F32) for v in little]
        + [*staged, pltpu.VMEM((CUBE * SHORT, LANES), F32), sems],
        input_output_aliases={3: 0, 4: 1, 5: 2},
        compiler_params=params(),
        cost_estimate=cost(1.5),
        name="unpack",
    )(section, got, got_other, *begun)
    rest = list(ends[3:])
    for k, at in enumerate((5, 7, 11)):
        rest.insert(at, ends[k])
    rest = [v.reshape(s) for v, s in zip(rest, [()] + shapes)]
    for at in (1, 3, 9, 13):
        rest[at] = rest[at].T
    return (rest[0], frames_grad.transpose(2, 0, 1, 3), *rest[1:])


def solution(mesh):
    placed = (
        P(None, None, None, "batch"),
        P("batch"),
        P(None, "batch"),
        P("batch"),
        P(None, None, "batch"),
    ) + (P(),) * 14
    return jax.shard_map(
        local,
        mesh=mesh,
        in_specs=placed,
        out_specs=(P(), P("section", None, None, "batch")) + (P(),) * 14,
        check_vma=False,
    )
```

```python
import functools
import math

import jax
import jax.numpy as jnp
from jax import lax
from jax.experimental import pallas as pl
from jax.experimental.pallas import tpu as pltpu
from jax.sharding import PartitionSpec as P

BF16 = jnp.bfloat16
F32 = jnp.float32
EXACT = lax.Precision.HIGHEST
LANES = 128
VMEM_BYTES = 32 * 1024 * 1024
TILE = 16
REACH = 5
STEP = 3
COLS = 12
NEAR = 4
AT_VB, AT_OW, AT_HW, AT_LB, AT_SCALARS, AT_B1, AT_B2, AT_DEST = (
    slice(18, 19),
    slice(19, 20),
    slice(20, 22),
    slice(22, 23),
    slice(23, 24),
    slice(24, 25),
    slice(25, 26),
    26,
)
TABLE = 32
CUBE = 8
SHORT = 16


def dot(a, b, precision=None):
    return jnp.dot(a, b, preferred_element_type=F32, precision=precision)


def dot_rows(a, b, precision=None):
    return lax.dot_general(
        a, b, (((0,), (0,)), ((), ())), preferred_element_type=F32, precision=precision
    )


def dot_lanes(a, b, precision=None):
    return lax.dot_general(
        a, b, (((1,), (1,)), ((), ())), preferred_element_type=F32, precision=precision
    )


def iota(shape, axis):
    return lax.broadcasted_iota(jnp.int32, shape, axis)


def column(row):
    n = row.shape[1]
    wide = jnp.broadcast_to(row, (n, n))
    return jnp.sum(jnp.where(iota((n, n), 0) == iota((n, n), 1), wide, 0.0), axis=1, keepdims=True)


def row_of(col):
    n = col.shape[0]
    wide = jnp.broadcast_to(col, (n, n))
    return jnp.sum(jnp.where(iota((n, n), 0) == iota((n, n), 1), wide, 0.0), axis=0, keepdims=True)


def soft(x):
    t = jnp.tanh(0.5 * x)
    return jnp.maximum(x, 0.0) - jnp.log(0.5 + 0.5 * jnp.abs(t)), 0.5 + 0.5 * t


def silu_pair(x):
    s = 0.5 + 0.5 * jnp.tanh(0.5 * x)
    act = x * s
    return act, s + act * (1.0 - s)


def pixel_order(w1t):
    tap, pix = iota((256, 256), 0), iota((256, 256), 1)
    moves = ((tap >> 6) == (pix & 3)) & ((tap & 63) == (pix >> 2))
    return dot(w1t, moves.astype(F32).astype(BF16))


def frame_copies(section, far, here, sems):
    lanes = pl.ds(pl.multiple_of(section[0] * LANES, LANES), LANES)
    size = 4 * STEP

    def copy(g):
        rows = pl.ds(pl.multiple_of(g * size, size), size)
        return pltpu.make_async_copy(far.at[rows, :, :, lanes], here.at[rows], sems.at[g])

    return copy


def tile_rows(frames, row, j, cols):
    img, _, channels, _ = frames.shape
    flat = frames.reshape(img, img * channels, LANES)
    size = cols * channels
    end = min((j + 1) * size, img * channels)
    part = flat[pl.ds(row, 4), j * size : end, :]
    return part.reshape(4 * (end - j * size), LANES)


def encode_kernel(
    section,
    frames_far,
    w1t,
    w2t,
    lw_far,
    table,
    h1_far,
    s1_far,
    s2_far,
    h2,
    enc,
    s3,
    frames,
    lw,
    h1,
    s1,
    s2,
    band,
    edge,
    band2,
    bias1,
    bias2,
    held,
    held2,
    sems,
):
    blocks, side = h1.shape[:2]
    steps = blocks // STEP
    tiles = frames.shape[1] // TILE
    k1, k2 = w1t.shape[0], w2t.shape[0]
    reach_rows = REACH * k1
    arrives = frame_copies(section, frames_far, frames, sems.at[0])
    for g in range(steps):
        arrives(g).start()
    last_copies = [
        pltpu.make_async_copy(lw_far, lw, sems.at[3, 0]),
        pltpu.make_async_copy(s2, s2_far, sems.at[3, 1]),
    ]
    last_copies[0].start()

    def leaves(g):
        rows = pl.ds(g * STEP, STEP)
        return [
            pltpu.make_async_copy(h1.at[rows], h1_far.at[rows], sems.at[1, g]),
            pltpu.make_async_copy(s1.at[rows], s1_far.at[rows], sems.at[2, g]),
        ]

    inner = side // 2 - 1
    row_len = inner * k2
    two = 2 * k2 * 3

    def prepare():
        taps = pixel_order(w1t[...])
        edges = []
        for half in range(2):
            lines = [taps[:, 32 * (4 * half + u) : 32 * (4 * half + u + 1)] for u in range(4)]
            for place in range(REACH):
                pieces = []
                for line in lines:
                    start = 16 * (place - 1)
                    cut = line[:, max(0, -start) : min(32, 64 - start)]
                    start = max(start, 0)
                    pieces += [jnp.zeros((k1, start), F32)] if start else []
                    pieces.append(cut)
                    rest = 64 - start - cut.shape[1]
                    pieces += [jnp.zeros((k1, rest), F32)] if rest else []
                at = half * reach_rows + place * k1
                band[at : at + k1, :] = jnp.concatenate(pieces, axis=1).astype(BF16)
            edges.append(jnp.concatenate([line[:, 16:] for line in lines], axis=1))
        edge[...] = jnp.concatenate(edges, axis=0).astype(BF16)
        tap, pix = iota((256, LANES), 0), iota((256, LANES), 1)
        for half in range(2):
            for place in range(3):
                hit = (
                    ((tap & 15) == (pix & 15))
                    & ((tap >> 6) == (pix >> 6) + 2 * half)
                    & (((tap >> 4) & 3) == ((pix >> 4) & 3) + 2 - 2 * place)
                )
                at = (half * 3 + place) * k2
                taps = dot(w2t[...], hit.astype(F32).astype(BF16))
                band2[at : at + k2, :] = taps.astype(BF16)
        bias1[...] = jnp.broadcast_to(column(table[AT_B1, 0:k1]), bias1.shape)
        bias2[...] = jnp.broadcast_to(column(table[AT_B2, 0:k2]), bias2.shape)
        held[...] = jnp.zeros_like(held)
        held2[...] = jnp.zeros_like(held2)
        h1[...] = jnp.zeros_like(h1)

    def added(sums, x, value):
        sums[x] = sums[x] + value if x in sums else value

    def second_rows(b):
        tiles = [
            h1[pl.ds(2 * b + 1, 2), 4 * j : 4 * j + 4].reshape(LANES, LANES)
            for j in range(side // 4)
        ]
        got = dot(band2[...], jnp.concatenate(tiles, axis=1))
        low, high = {}, {}
        for j in range(side // 4):
            for place in range(3):
                x = 2 * j - 1 + place
                if 0 <= x < inner:
                    span = slice(j * LANES, (j + 1) * LANES)
                    at = place * k2
                    added(low, x, got[at : at + k2, span])
                    added(high, x, got[two // 2 + at : two // 2 + at + k2, span])
        row = jnp.maximum(b - 1, 0) * row_len
        for x in range(inner):
            value, slope = soft(held2[x] + high[x] + bias2[...])
            held2[x] = low[x]
            at = pl.ds(pl.multiple_of(row + x * k2, k2), k2)
            h2[at, :] = value.astype(BF16)
            s2[at, :] = slope.astype(BF16)

    def one_step(g, carry):
        def row(r):
            return pl.multiple_of(4 * (STEP * g + r), 4)

        arrives(g).wait()
        second_rows(jnp.maximum(g - 1, 0))

        last = dot(
            edge[...], jnp.concatenate([tile_rows(frames, row(r), tiles, TILE) for r in range(STEP)], axis=1)
        )
        odd = {}
        for r in range(STEP):
            low, high = {}, {}

            def place_tile(j, got):
                for place in range(REACH):
                    x = 4 * j - 1 + place
                    if 0 <= x < side:
                        at = place * k1
                        added(low, x, got[at : at + k1])
                        added(high, x, got[reach_rows + at : reach_rows + at + k1])

            if r not in odd:
                rows = [k for k in (r, r + 1) if k < STEP]
                cut = [tile_rows(frames, row(k), tiles - 1, TILE) for k in rows]
                got = dot(band[...], jnp.concatenate(cut, axis=1))
                odd.update({k: got[:, i * LANES : (i + 1) * LANES] for i, k in enumerate(rows)})
            place_tile(tiles - 1, odd[r])
            added(low, side - 1, last[:k1, r * LANES : (r + 1) * LANES])
            added(high, side - 1, last[k1:, r * LANES : (r + 1) * LANES])
            done = 0
            for j in range(0, tiles - 1, 2):
                cut = [tile_rows(frames, row(r), j + k, TILE) for k in range(2)]
                got = dot(band[...], jnp.concatenate(cut, axis=1))
                for k in range(2):
                    place_tile(j + k, got[:, k * LANES : (k + 1) * LANES])
                ready = side if j + 2 == tiles - 1 else 4 * j + 7
                for x in range(done, ready):
                    value, slope = soft(held[x] + high[x] + bias1[...])
                    held[x] = low[x]
                    value = value.astype(BF16)
                    h1[STEP * g + r, x] = value
                    s1[STEP * g + r, x] = slope.astype(BF16)
                done = ready
        for copy in leaves(g):
            copy.start()
        return carry

    prepare()
    lax.fori_loop(0, steps, one_step, 0)
    for b in range(steps - 1, side // 2):
        second_rows(b)
    for copy in last_copies[1:]:
        copy.start()
    last_copies[0].wait()
    value, slope = soft(dot_rows(lw[...], h2[...]) + column(table[AT_LB, :]))
    enc[...] = value.astype(BF16)
    s3[...] = slope
    for g in range(steps):
        for copy in leaves(g):
            copy.wait()
    for copy in last_copies[1:]:
        copy.wait()


def three_parts(row):
    high = row.astype(BF16).astype(F32)
    middle = (row - high).astype(BF16).astype(F32)
    return jnp.concatenate([high, middle, row - high - middle], axis=0)


def with_ones(value):
    return jnp.concatenate([value, ones_rows(value.shape[1])], axis=0)


def ones_rows(lanes):
    return (iota((16, lanes), 0) < 3).astype(F32).astype(BF16)


def plan_kernel(
    section,
    slots,
    enc,
    s3,
    h2,
    branch_far,
    value_w,
    table,
    keep,
    send,
    small,
    g3,
    parts,
    bwt,
    vht,
    vhw,
    ow,
    mine,
    pre,
    dbr,
    dval,
    low,
    hid,
    gb,
    branch_w,
    sem,
    *,
    per_pair,
    depth,
):
    width = enc.shape[0]
    options = branch_w.shape[0]
    pairs = options // 2
    two = 2 * width
    sec = section[0]
    branch_copy = pltpu.make_async_copy(branch_far, branch_w, sem)
    branch_copy.start()

    count = slots.shape[0]
    dest = jnp.concatenate(
        [table[AT_DEST + k : AT_DEST + k + 1, :] for k in range(count // LANES)], axis=1
    )
    own = jnp.where(sec == 0, dest[:, :LANES], dest[:, LANES:])
    others = jnp.transpose(jnp.broadcast_to(dest, (LANES, count)))
    index = iota((count, LANES), 1) + sec * LANES
    earlier = (others == own) & (iota((count, LANES), 0) < index)
    rank = jnp.sum(earlier.astype(F32), axis=0, keepdims=True)
    bucket = own * float(per_pair) + rank
    chosen = (iota((count, LANES), 0).astype(F32) == bucket).astype(F32).astype(BF16)
    numbers = slots[...]
    high = numbers.astype(BF16)
    middle = (numbers - high.astype(F32)).astype(BF16)
    rest = (numbers - high.astype(F32) - middle.astype(F32)).astype(BF16)
    mine[...] = sum(dot_rows(v, chosen) for v in (rest, middle, high))[: mine.shape[0]]

    pad = jnp.zeros((13, width), F32)
    branch_copy.wait()
    for o in range(options):
        rows = [branch_w[o].astype(F32), three_parts(table[o : o + 1, :]), pad]
        bwt[o * width : (o + 1) * width, :] = jnp.transpose(
            jnp.concatenate(rows, axis=0)
        ).astype(BF16)
    scalars = table[AT_SCALARS, :]
    head_w = table[AT_HW, :]
    rows = [value_w[...].astype(F32), three_parts(table[AT_VB, :]), pad]
    vht[0:width, :] = jnp.transpose(jnp.concatenate(rows, axis=0)).astype(BF16)
    vht[width:, :] = jnp.zeros((16, width + 16), BF16)
    lane = iota((1, 16), 1)
    for k in range(2):
        bias = three_parts(jnp.broadcast_to(scalars[:, 1 + k : 2 + k], (1, 16)))
        bias = sum(jnp.where(lane == j, bias[j : j + 1], 0.0) for j in range(3))
        vht[width + k : width + k + 1, 0:width] = head_w[k : k + 1].astype(BF16)
        vht[width + k : width + k + 1, width:] = bias.astype(BF16)
    vhw[:, 0:width] = value_w[...]
    vhw[:, width:] = jnp.transpose(
        jnp.concatenate([head_w, jnp.zeros((14, width), F32)], axis=0)
    ).astype(BF16)
    ow[...] = jnp.broadcast_to(column(table[AT_OW, :]), (width, LANES))
    wide_ow = jnp.concatenate([ow[...], ow[...]], axis=1)

    labels = iota((options, LANES), 0).astype(F32)
    state = enc[...].astype(F32)
    rounded_all, saved = [], []
    for level in range(depth):
        picked = labels == mine[level : level + 1, :]
        rounded = state.astype(BF16)
        rounded_all.append(rounded)
        pre[...] = dot(bwt[...], with_ones(rounded))
        following = state
        reward, discount, value = [], [], []
        for t in range(pairs):
            at = slice(t * two, (t + 1) * two)
            act, slope = silu_pair(pre[at, :])
            dbr[level, at, :] = slope
            left = state + act[:width]
            right = state + act[width:]
            following = jnp.where(picked[2 * t : 2 * t + 1], left, following)
            following = jnp.where(picked[2 * t + 1 : 2 * t + 2], right, following)
            both = with_ones(jnp.concatenate([left.astype(BF16), right.astype(BF16)], axis=1))
            low[level, t] = both
            got = dot(vht[...], both)
            act, slope = silu_pair(got[:width])
            dval[level, t] = slope
            hidden = act.astype(BF16)
            hid[level, t] = hidden
            worth = jnp.sum(hidden.astype(F32) * wide_ow, axis=0, keepdims=True)
            for k in range(2):
                span = slice(k * LANES, (k + 1) * LANES)
                value.append(worth[:, span])
                reward.append(got[width : width + 1, span])
                discount.append(got[width + 1 : width + 2, span])
        reward = jnp.concatenate(reward, axis=0)
        discount = jax.nn.sigmoid(jnp.concatenate(discount, axis=0))
        value = jnp.concatenate(value, axis=0) + scalars[:, 3:4]
        quality = reward + discount * value
        top = jnp.max(quality, axis=0, keepdims=True)
        shifted = jnp.exp(quality - top)
        total = jnp.sum(shifted, axis=0, keepdims=True)
        live = (mine[depth : depth + 1, :] > level).astype(F32)
        chosen = picked.astype(F32)

        def target(kind):
            at = depth + 1 + kind * depth + level
            return mine[at : at + 1, :]

        reward_gap = live * (jnp.sum(chosen * reward, axis=0, keepdims=True) - target(0))
        discount_gap = live * (jnp.sum(chosen * discount, axis=0, keepdims=True) - target(1))
        plan_gap = live * (top + jnp.log(total) - target(2))
        grad_quality = plan_gap * (shifted / total)
        head_two = (chosen * discount_gap + grad_quality * value) * discount * (1.0 - discount)
        saved.append(
            (
                picked,
                (chosen * reward_gap + grad_quality).astype(BF16).astype(F32),
                head_two.astype(BF16).astype(F32),
                (grad_quality * discount).astype(BF16).astype(F32),
                reward_gap * reward_gap + discount_gap * discount_gap + plan_gap * plan_gap,
            )
        )
        state = following

    out_sum = jnp.zeros((width, two), F32)
    value_sum = jnp.zeros((width + 16, width + 16), F32)
    grad_next = jnp.zeros((width, LANES), F32)
    line = iota((16, two), 0)
    for level in reversed(range(depth)):
        picked, head_one, head_two, grad_value, _ = saved[level]
        upward = jnp.zeros((width, LANES), F32)
        for t in range(pairs):
            at = slice(t * two, (t + 1) * two)

            def across(rows):
                return jnp.concatenate(
                    [rows[2 * t : 2 * t + 1], rows[2 * t + 1 : 2 * t + 2]], axis=1
                )

            worth = across(grad_value)
            grad_pre = (worth * wide_ow * dval[level, t]).astype(BF16)
            out_sum = out_sum + hid[level, t].astype(F32) * worth
            heads = jnp.where(line == 0, across(head_one), 0.0)
            heads = jnp.where(line == 1, across(head_two), heads)
            heads = jnp.where(line == 2, worth, heads)
            stacked = jnp.concatenate([grad_pre, heads.astype(BF16)], axis=0)
            value_sum = value_sum + dot_lanes(stacked, low[level, t])
            moved = dot(vhw[...], stacked)
            left = moved[:, :LANES] + jnp.where(picked[2 * t : 2 * t + 1], grad_next, 0.0)
            right = moved[:, LANES:] + jnp.where(picked[2 * t + 1 : 2 * t + 2], grad_next, 0.0)
            grad_branch = jnp.concatenate([left, right], axis=0) * dbr[level, at, :]
            grad_branch = grad_branch.astype(BF16)
            gb[level, at, :] = grad_branch
            weights = jnp.concatenate([branch_w[2 * t], branch_w[2 * t + 1]], axis=1)
            upward = upward + (left + right + dot(weights, grad_branch))
        grad_next = upward

    linear_rows = h2.shape[0]
    half = (linear_rows + options * width + width) // 2
    rest = linear_rows - half
    rounded = with_ones(jnp.concatenate(rounded_all, axis=1))
    small[...] = jnp.zeros_like(small)
    if half < keep.shape[0]:
        for k in range(2):
            parts[k, half:, :] = jnp.zeros((keep.shape[0] - half, LANES), BF16)
    for t in range(pairs):
        at = slice(t * two, (t + 1) * two)
        grads = jnp.concatenate([gb[level, at, :] for level in range(depth)], axis=1)
        got = dot_lanes(rounded, grads)
        for k in range(2):
            o = 2 * t + k
            span = slice(k * width, (k + 1) * width)
            rows = slice(rest + o * width, rest + (o + 1) * width)
            parts[1 - sec, rows, :] = got[:width, span].astype(BF16)
            small[o : o + 1, :] = got[width : width + 1, span]
    after = rest + options * width
    parts[1 - sec, after : after + width, :] = jnp.transpose(value_sum[:width, :width]).astype(BF16)

    grad_three = (grad_next.astype(BF16).astype(F32) * s3[...]).astype(BF16)
    g3[...] = grad_three
    chunk = linear_rows // 9
    for i in range(8):
        at = slice(i * chunk, (i + 1) * chunk)
        parts[sec, at, :] = dot_lanes(h2[at, :], grad_three).astype(BF16)
    last = dot_lanes(h2[8 * chunk :, :], grad_three).astype(BF16)
    parts[sec, 8 * chunk : half, :] = last[: half - 8 * chunk]
    parts[1 - sec, 0:rest, :] = last[half - 8 * chunk :]
    keep[...] = parts[0]
    send[...] = parts[1]

    small[AT_VB, :] = row_of(value_sum[:width, width : width + 1])
    small[AT_OW, :] = row_of(jnp.sum(out_sum, axis=1, keepdims=True))
    small[AT_HW, :] = value_sum[width : width + 2, :width]
    small[AT_LB, :] = row_of(jnp.sum(grad_three.astype(F32), axis=1, keepdims=True))
    loss = 0.5 * jnp.sum(sum(kept[4] for kept in saved), axis=1, keepdims=True)
    ends = [loss] + [value_sum[width + k : width + k + 1, width : width + 1] for k in range(3)]
    lane = iota((1, LANES), 1)
    line = jnp.zeros((1, LANES), F32)
    for k, end in enumerate(ends):
        line = jnp.where(lane == k, end, line)
    small[AT_SCALARS, :] = line


def back_kernel(g3, lw, s2, s1, h1, w2t, g1, c2, sums, t2, g2):
    side, k1 = s1.shape[1], s1.shape[2]
    k2 = w2t.shape[0]
    inner = side // 2 - 1
    row_len = inner * k2
    tap, pix = iota((LANES, 256), 1), iota((LANES, 256), 0)
    for yrel in range(2):
        for p in range(3):
            hit = (
                ((tap & 15) == (pix & 15))
                & ((tap >> 6) == (pix >> 6) + 2 * (1 - yrel))
                & (((tap >> 4) & 3) == ((pix >> 4) & 3) + 2 - 2 * p)
            )
            at = (yrel * 3 + p) * k2
            t2[:, at : at + k2] = dot_lanes(hit.astype(F32).astype(BF16), w2t[...]).astype(BF16)
    g2[0] = jnp.zeros(g2.shape[1:], BF16)
    g2[inner + 1] = jnp.zeros(g2.shape[1:], BF16)
    g1[0] = jnp.zeros(g1.shape[1:], BF16)
    g1[side + 1] = jnp.zeros(g1.shape[1:], BF16)
    zero = jnp.zeros((k2, LANES), BF16)
    total_one = jnp.zeros((k1, LANES), F32)
    total_two = jnp.zeros((k2, LANES), F32)
    for y in range(inner):
        at = slice(y * row_len, (y + 1) * row_len)
        grad = dot(lw[at, :], g3[...]) * s2[at, :].astype(F32)
        grad = grad.astype(BF16).reshape(inner, k2, LANES)
        g2[y + 1] = grad
        total_two = total_two + jnp.sum(grad.astype(F32), axis=0)
    reach, cols = 5, 8
    total = jnp.zeros((2 * reach * k2, 2 * cols * k1), F32)
    grads, tiles = [], []
    for b in range(side // 2):
        cut = []
        for j in range(side // 4):
            pieces = []
            for yrel in range(2):
                for p in range(3):
                    x = 2 * j - 1 + p
                    pieces.append(g2[b + yrel, x] if 0 <= x < inner else zero)
            cut.append(jnp.concatenate(pieces, axis=0))
        got = dot(t2[...], jnp.concatenate(cut, axis=1))
        for u in range(2):
            for j in range(side // 4):
                part = got[u * 64 : (u + 1) * 64, j * LANES : (j + 1) * LANES]
                slope = s1[2 * b + u + 1, 4 * j : 4 * j + 4].astype(F32)
                grad = (part.reshape(4, k1, LANES) * slope).astype(BF16)
                g1[2 * b + u + 1, 4 * j : 4 * j + 4] = grad
                total_one = total_one + jnp.sum(grad.astype(F32), axis=0)
        for j in range(-(-side // cols)):
            end = min((j + 1) * cols, side)
            tile = h1[2 * b + 1 : 2 * b + 3, j * cols : end]
            if end < (j + 1) * cols:
                rest = jnp.zeros((2, (j + 1) * cols - end, k1, LANES), BF16)
                tile = jnp.concatenate([tile, rest], axis=1)
            tiles.append(tile.reshape(2 * cols * k1, LANES))
            pieces = []
            for half in range(2):
                for p in range(reach):
                    x = 4 * j - 1 + p
                    pieces.append(g2[b + 1 - half, x] if 0 <= x < inner else zero)
            grads.append(jnp.concatenate(pieces, axis=0))
        if b % 2:
            total = total + dot_lanes(
                jnp.concatenate(grads, axis=1), jnp.concatenate(tiles, axis=1)
            )
            grads, tiles = [], []
    line = 4 * k1
    for half in range(2):
        for u in range(2):
            tap_row = jnp.zeros((k2, line), F32)
            for p in range(reach):
                at = (half * reach + p) * k2
                part = total[at : at + k2, u * 2 * line : (u + 1) * 2 * line]
                start = 2 * k1 * (p - 1)
                piece = part[:, max(start, 0) : min(start + line, 2 * line)]
                if start < 0:
                    piece = jnp.concatenate([jnp.zeros((k2, -start), F32), piece], axis=1)
                if start + line > 2 * line:
                    rest = jnp.zeros((k2, start - line), F32)
                    piece = jnp.concatenate([piece, rest], axis=1)
                tap_row = tap_row + piece
            at = (2 * half + u) * line
            c2[:, at : at + line] = tap_row
    sums[...] = jnp.zeros_like(sums)
    sums[0:1, 0:k1] = row_of(jnp.sum(total_one, axis=1, keepdims=True))
    sums[1:2, 0:k2] = row_of(jnp.sum(total_two, axis=1, keepdims=True))


def pixel_band(sec, w1t, channels):
    k1 = w1t.shape[0]
    rows = 64 * channels
    row, tap = iota((rows, 256), 0), iota((rows, 256), 1)
    moves = ((tap >> 6) == row % channels + sec * channels) & ((tap & 63) == row // channels)
    taps = dot_lanes(moves.astype(F32).astype(BF16), w1t)
    line, span = COLS * channels, 8 * channels
    blocks = {}
    for half in range(2):
        for p in range(NEAR):
            pieces = []
            for u in range(4):
                at = (4 * half + u) * span
                start = 4 * (p - 1) * channels
                cut = taps[at + max(0, -start) : at + min(span, line - start)]
                start = max(start, 0)
                pieces += [jnp.zeros((start, k1), F32)] if start else []
                pieces.append(cut)
                rest = line - start - cut.shape[0]
                pieces += [jnp.zeros((rest, k1), F32)] if rest else []
            blocks[half, p] = jnp.concatenate(pieces, axis=0)
    zero = jnp.zeros((4 * line, k1), F32)
    lines = []
    for r in range(STEP):
        cols = [
            blocks.get((r + 1 - yrel, p), zero) for yrel in range(STEP + 1) for p in range(NEAR)
        ]
        lines.append(jnp.concatenate(cols, axis=1))
    return jnp.concatenate(lines, axis=0).astype(BF16)


def first_kernel(section, frames_far, g1, after, c1, frames, acc, sems):
    side, k1 = g1.shape[1], g1.shape[2]
    img, _, channels, _ = frames.shape
    steps = img // 4 // STEP
    arrives = frame_copies(section, frames_far, frames, sems)
    for g in range(steps):
        arrives(g).start()
    acc[...] = jnp.zeros_like(acc)
    zero = jnp.zeros((k1, LANES), BF16)

    def one_step(g, carry):
        arrives(g).wait()
        pixels, grads = [], []
        for j in range(img // COLS):
            rows = [pl.multiple_of(4 * (STEP * g + r), 4) for r in range(STEP)]
            pixels.append(
                jnp.concatenate([tile_rows(frames, row, j, COLS) for row in rows], axis=0)
            )
            pieces = []
            for yrel in range(STEP + 1):
                for p in range(NEAR):
                    x = 3 * j - 1 + p
                    pieces.append(g1[STEP * g + yrel, x] if 0 <= x < side else zero)
            grads.append(jnp.concatenate(pieces, axis=0))
        acc[...] += dot_lanes(jnp.concatenate(pixels, axis=1), jnp.concatenate(grads, axis=1))
        return carry

    lax.fori_loop(0, steps, one_step, 0)
    fold_first(acc, c1, channels, k1)


def fold_first(acc, c1, channels, k1):
    line = COLS * channels
    step = 4 * channels
    taps = []
    for half in range(2):
        total = sum(
            acc[r * 4 * line : (r + 1) * 4 * line, :][
                :, (r + 1 - half) * NEAR * k1 : (r + 2 - half) * NEAR * k1
            ]
            for r in range(STEP)
        )
        for u in range(4):
            part = total[u * line : (u + 1) * line]
            cols = [part[:, p * k1 : (p + 1) * k1] for p in range(NEAR)]
            taps.append(cols[1][0:step] + cols[2][step : 2 * step] + cols[3][2 * step :])
            taps.append(cols[0][0:step] + cols[1][step : 2 * step] + cols[2][2 * step :])
    row, col = iota((256, 256), 0), iota((256, 256), 1)
    moves = ((row & 3) == (col >> 6)) & ((row >> 2) == (col & 63))
    grad = dot_rows(jnp.concatenate(taps, axis=0), moves.astype(F32), EXACT)
    for half in range(2):
        c1[half * k1 : (half + 1) * k1, :] = grad[:, half * LANES : (half + 1) * LANES].astype(BF16)


def pixels_kernel(section, weights, mine, other, after, *refs, start, steps, begins):
    out, token, band_out, held, sems = refs[-5:]
    side, k1 = mine.shape[1], mine.shape[2]
    img, channels = out.shape[1], out.shape[2]
    sec = section[0]
    line = COLS * channels
    flat = held.reshape(2, 2, 4 * STEP, img * channels, LANES)
    if begins:
        band_out[...] = pixel_band(sec, weights[...], channels)
        band = band_out
    else:
        band = weights
        band_out[...] = jnp.zeros_like(band_out)
    token[...] = jnp.zeros_like(token)

    def writes(g):
        rows = slice(4 * STEP * (start + g), 4 * STEP * (start + g + 1))
        places = (sec * LANES, (1 - sec) * LANES)
        return [
            pltpu.make_async_copy(
                held.at[g % 2, k],
                out.at[rows, :, :, pl.ds(pl.multiple_of(places[k], LANES), LANES)],
                sems.at[g % 2, k],
            )
            for k in range(2)
        ]

    zero = jnp.zeros((k1, 2 * LANES), BF16)
    for g in range(steps):
        if g >= 2:
            for copy in writes(g - 2):
                copy.wait()
        for j in range(img // COLS):
            pieces = []
            for yrel in range(STEP + 1):
                for p in range(NEAR):
                    x, y = 3 * j - 1 + p, STEP * (start + g) + yrel
                    if 0 <= x < side:
                        pieces.append(jnp.concatenate([mine[y, x], other[y, x]], axis=1))
                    else:
                        pieces.append(zero)
            got = dot(band[...], jnp.concatenate(pieces, axis=0))
            for k in range(4 * STEP):
                at = slice(k * line, (k + 1) * line)
                span = slice(j * line, (j + 1) * line)
                flat[g % 2, 0, k, span, :] = got[at, :LANES]
                flat[g % 2, 1, k, span, :] = got[at, LANES:]
        for copy in writes(g):
            copy.start()
    for g in range(max(steps - 2, 0), steps):
        for copy in writes(g):
            copy.wait()


def two_parts(value):
    high = value.astype(BF16).astype(F32)
    return jnp.concatenate([high, value - high], axis=0).astype(BF16)


def one_part(pair):
    rows = pair.shape[0] // 2
    pair = pair.astype(F32)
    return pair[:rows] + pair[rows:]


def merge_kernel(batch, keep, recv, small, c2, sums, *rest):
    outs, lines = rest[:-1], rest[-1]
    me = batch[0] % CUBE
    size = keep.shape[0] // CUBE
    k2 = c2.shape[0]
    lines[...] = jnp.zeros_like(lines)
    at = small.shape[0]
    lines[0:at, :] = small[...]
    for half in range(2):
        lines[at : at + k2, :] = c2[:, half * LANES : (half + 1) * LANES]
        at += k2
    lines[at : at + sums.shape[0], :] = sums[...]
    for k, out in enumerate(outs):
        member = me ^ k
        at = pl.ds(pl.multiple_of(member * size, size), size)
        out[0:size, :] = (keep[at, :].astype(F32) + recv[at, :].astype(F32)).astype(BF16)
        at = pl.ds(pl.multiple_of(member * SHORT, SHORT), SHORT)
        out[size:, :] = two_parts(lines[at, :])


def cube_kernel(*refs):
    parts, c1, out = refs[:CUBE], refs[CUBE], refs[-1]
    size = parts[0].shape[0] - 2 * SHORT
    out[0:size, :] = sum(p[0:size, :].astype(F32) for p in parts).astype(BF16)
    out[size : size + 2 * SHORT, :] = two_parts(sum(one_part(p[size:, :]) for p in parts))
    out[size + 2 * SHORT :, :] = c1[...]


def add_kernel(a, b, after, out):
    size = a.shape[0] - 2 * SHORT - 32
    middle = slice(size, size + 2 * SHORT)
    for span in (slice(0, size), slice(size + 2 * SHORT, a.shape[0])):
        out[span, :] = (a[span, :].astype(F32) + b[span, :].astype(F32)).astype(BF16)
    out[middle, :] = two_parts(one_part(a[middle, :]) + one_part(b[middle, :]))


def relay_kernel(batch, *refs):
    parts, out = refs[:CUBE], refs[-1]
    me = batch[0] % CUBE
    for k, part in enumerate(parts):
        out[me ^ k] = part[...]


def unpack_half(which, got, lw, bw, vw, stage, stage_b, sems):
    members = got.shape[0]
    size = stage.shape[0] // members
    linear_rows, width = lw.shape
    options = bw.shape[0]
    half = (linear_rows + options * width + width) // 2
    rest = linear_rows - half

    @pl.when(which == 0)
    def _():
        copies = []
        for k in range(members):
            start, end = k * size, min((k + 1) * size, half)
            stage[start:end, :] = got[k, 0 : end - start, :].astype(F32)
            copies.append(
                pltpu.make_async_copy(stage.at[start:end], lw.at[start:end], sems.at[k])
            )
            copies[-1].start()
        for copy in copies:
            copy.wait()

    @pl.when(which == 1)
    def _():
        def rows(start, end):
            parts = []
            while start < end:
                k, at = start // size, start % size
                count = min(size - at, end - start)
                parts.append(got[k, at : at + count, :])
                start += count
            value = parts[0] if len(parts) == 1 else jnp.concatenate(parts, axis=0)
            return value.astype(F32)

        stage[0:rest, :] = rows(0, rest)
        copies = [pltpu.make_async_copy(stage.at[0:rest], lw.at[half:], sems.at[0])]
        copies[0].start()
        group = options // 3
        for o in range(options):
            stage_b[o] = rows(rest + o * width, rest + (o + 1) * width)
            if o % group == group - 1:
                part = slice(o + 1 - group, o + 1)
                copy = pltpu.make_async_copy(
                    stage_b.at[part], bw.at[part], sems.at[1 + o // group]
                )
                copy.start()
                copies.append(copy)
        at = rest + options * width
        stage[rest : rest + width, :] = rows(at, at + width)
        copies.append(
            pltpu.make_async_copy(stage.at[rest : rest + width], vw, sems.at[1 + options // group])
        )
        copies[-1].start()
        for copy in copies:
            copy.wait()


def own_kernel(section, mine, lw, bw, vw, stage, stage_b, sems):
    unpack_half(section[0], mine, lw, bw, vw, stage, stage_b, sems)


def unpack_kernel(section, mine, other, *refs):
    lw, bw, vw = refs[3:6]
    little = (len(refs) - 10) // 2
    far, near = refs[6 : 6 + little], refs[6 + little : 6 + 2 * little]
    loss, c1, b1, c2, b2, lb, bb, hw, hb, vb, ow, ob = near
    stage, stage_b, lines, sems = refs[-4:]
    options = bw.shape[0]
    k1, k2 = c1.shape[0], c2.shape[0]
    size = stage.shape[0] // CUBE
    grad = [jnp.zeros((k1, LANES), F32) for _ in range(2)]
    for k in range(CUBE):
        pair = slice(size, size + 2 * SHORT)
        at = slice(k * SHORT, (k + 1) * SHORT)
        lines[at, :] = one_part(mine[k, pair, :]) + one_part(other[k, pair, :])
        for ref in (mine, other):
            for h in range(2):
                at = size + 2 * SHORT + h * k1
                grad[h] += ref[k, at : at + k1, :].astype(F32)
    for part in range(2):
        c1[:, part * LANES : (part + 1) * LANES] = grad[part]
    bb[...] = lines[0:options, :]
    vb[...] = lines[AT_VB, :]
    ow[...] = lines[AT_OW, :]
    hw[...] = lines[AT_HW, :]
    lb[...] = lines[AT_LB, :]
    scalars = lines[AT_SCALARS, :]
    loss[...] = scalars[:, 0:1]
    hb[...] = scalars[:, 1:3]
    ob[...] = scalars[:, 3:4]
    at = TABLE
    for part in range(2):
        c2[:, part * LANES : (part + 1) * LANES] = lines[at : at + k2, :]
        at += k2
    b1[...] = lines[at : at + 1, 0:k1]
    b2[...] = lines[at + 1 : at + 2, 0:k2]
    copies = [
        pltpu.make_async_copy(a, b, sems.at[CUBE + k]) for k, (a, b) in enumerate(zip(near, far))
    ]
    for copy in copies:
        copy.start()
    unpack_half(1 - section[0], other, lw, bw, vw, stage, stage_b, sems)
    for copy in copies:
        copy.wait()


def numbers_kernel(
    options,
    depth,
    targets,
    destination,
    b1,
    b2,
    lb,
    bb,
    hw,
    vb,
    ow,
    hb,
    ob,
    out,
    table,
):
    levels, kinds = options.shape[0], targets.shape[0]
    slots = depth.shape[1]
    rows = [options[...].astype(F32), depth[...].astype(F32)]
    rows += [targets[k] for k in range(kinds)]
    rows.append(jnp.zeros((LANES - levels - 1 - kinds * levels, slots), F32))
    out[...] = jnp.transpose(jnp.concatenate(rows, axis=0))
    table[...] = jnp.zeros_like(table)
    table[0 : bb.shape[0], :] = bb[...]
    table[AT_VB, :] = vb[...]
    table[AT_OW, :] = ow[...].astype(F32)
    table[AT_HW, :] = hw[...].astype(F32)
    table[AT_LB, :] = lb[...]
    table[AT_B1, 0 : b1.shape[1]] = b1[...]
    table[AT_B2, 0 : b2.shape[1]] = b2[...]
    lane = iota((1, LANES), 1)
    scalars = jnp.zeros((1, LANES), F32)
    for k, value in ((1, hb[:, 0:1]), (2, hb[:, 1:2]), (3, ob[...])):
        scalars = jnp.where(lane == k, value, scalars)
    table[AT_SCALARS, :] = scalars
    for k in range(slots // LANES):
        part = destination[:, k * LANES : (k + 1) * LANES]
        table[AT_DEST + k : AT_DEST + k + 1, :] = part.astype(F32)


def whole(shape):
    zeros = (0,) * len(shape)
    return pl.BlockSpec(shape, lambda *_: zeros)


ANYWHERE = pl.BlockSpec(memory_space=pl.ANY)
SCALARS = pl.BlockSpec(memory_space=pltpu.SMEM)


def params():
    return pltpu.CompilerParams(vmem_limit_bytes=VMEM_BYTES)


def shape_of(*shape, dtype=F32):
    return jax.ShapeDtypeStruct(shape, dtype)


def cost(microseconds):
    return pl.CostEstimate(
        flops=int(1.1e9 * microseconds), bytes_accessed=int(3.6e6 * microseconds), transcendentals=0
    )


def stays(value):
    return pltpu.with_memory_space_constraint(value, pltpu.HBM)


def held_near(value):
    return pltpu.with_memory_space_constraint(value, pltpu.VMEM)


def encode(section, frames, w1t, w2t, lw, table):
    img = frames.shape[0]
    blocks = img // 4
    side = blocks - 1
    k1, k2, width = w1t.shape[0], w2t.shape[0], lw.shape[1]
    flat = lw.shape[0]
    vmem = pltpu.VMEM
    near = pl.BlockSpec(memory_space=vmem)
    grid_one = (blocks, side, k1, LANES)
    return pl.pallas_call(
        encode_kernel,
        in_specs=[SCALARS, ANYWHERE, near, near, ANYWHERE, near],
        out_specs=[ANYWHERE] * 3 + [near] * 3,
        out_shape=(
            pltpu.HBM(grid_one, BF16),
            pltpu.HBM(grid_one, BF16),
            pltpu.HBM((flat, LANES), BF16),
            shape_of(flat, LANES, dtype=BF16),
            shape_of(width, LANES, dtype=BF16),
            shape_of(width, LANES),
        ),
        scratch_shapes=[
            vmem((img, img, frames.shape[2], LANES), BF16),
            vmem(lw.shape, BF16),
            vmem(grid_one, BF16),
            vmem(grid_one, BF16),
            vmem((flat, LANES), BF16),
            vmem((2 * REACH * k1, 256), BF16),
            vmem((2 * k1, 64), BF16),
            vmem((6 * k2, LANES), BF16),
            vmem((k1, LANES), F32),
            vmem((k2, LANES), F32),
            vmem((side, k1, LANES), F32),
            vmem((side // 2 - 1, k2, LANES), F32),
            pltpu.SemaphoreType.DMA((4, max(blocks // STEP, 3))),
        ],
        compiler_params=params(),
        cost_estimate=cost(9),
        name="encode",
    )(section, frames, w1t, w2t, lw, table)


def plan(section, slots, enc, s3, h2, branch_w, value_w, table, per_pair, depth, half_rows):
    width = enc.shape[0]
    options = branch_w.shape[0]
    two = 2 * width
    pairs = options // 2
    outs = (
        shape_of(half_rows, LANES, dtype=BF16),
        shape_of(half_rows, LANES, dtype=BF16),
        shape_of(TABLE, LANES),
        shape_of(width, LANES, dtype=BF16),
    )
    vmem = pltpu.VMEM
    near = pl.BlockSpec(memory_space=vmem)
    return pl.pallas_call(
        functools.partial(plan_kernel, per_pair=per_pair, depth=depth),
        in_specs=[SCALARS, near, near, near, near, ANYWHERE, near, near],
        out_shape=outs,
        scratch_shapes=[
            vmem((2, half_rows, LANES), BF16),
            vmem((options * width, width + 16), BF16),
            vmem((width + 16, width + 16), BF16),
            vmem((width, width + 16), BF16),
            vmem((width, LANES), F32),
            vmem((16, LANES), F32),
            vmem((options * width, LANES), F32),
            vmem((depth, options * width, LANES), F32),
            vmem((depth, pairs, width, two), F32),
            vmem((depth, pairs, width + 16, two), BF16),
            vmem((depth, pairs, width, two), BF16),
            vmem((depth, options * width, LANES), BF16),
            vmem(branch_w.shape, BF16),
            pltpu.SemaphoreType.DMA,
        ],
        compiler_params=params(),
        cost_estimate=cost(11),
        name="plan",
    )(section, slots, enc, s3, h2, branch_w, value_w, table)


def back(g3, lw, s2, s1, h1, w2t):
    _, side, k1 = s1.shape[:3]
    k2 = w2t.shape[0]
    inner = side // 2 - 1
    padded = (side + 2, side, k1, LANES)
    near = pl.BlockSpec(memory_space=pltpu.VMEM)
    return pl.pallas_call(
        back_kernel,
        in_specs=[near] * 6,
        out_shape=(shape_of(*padded, dtype=BF16), shape_of(k2, 256), shape_of(8, LANES)),
        scratch_shapes=[
            pltpu.VMEM((LANES, 6 * k2), BF16),
            pltpu.VMEM((inner + 2, inner, k2, LANES), BF16),
        ],
        compiler_params=params(),
        cost_estimate=cost(25),
        name="back",
    )(g3, lw, s2, s1, h1, w2t)


def first(section, frames, g1, after):
    img, _, channels, _ = frames.shape
    k1 = g1.shape[2]
    return pl.pallas_call(
        first_kernel,
        in_specs=[SCALARS, ANYWHERE, pl.BlockSpec(memory_space=pltpu.VMEM), ANYWHERE],
        out_shape=shape_of(2 * k1, LANES, dtype=BF16),
        scratch_shapes=[
            pltpu.VMEM((img, img, channels, LANES), BF16),
            pltpu.VMEM((STEP * 4 * COLS * channels, (STEP + 1) * NEAR * k1), F32),
            pltpu.SemaphoreType.DMA((img // 4 // STEP,)),
        ],
        compiler_params=params(),
        cost_estimate=cost(45),
        name="first",
    )(section, frames, g1, after)


def pixels(section, weights, mine, other, shape, start, steps, after, done=None):
    img, _, channels, _ = shape
    k1 = mine.shape[2]
    band = (STEP * 4 * COLS * channels, (STEP + 1) * NEAR * k1)
    near = pl.BlockSpec(memory_space=pltpu.VMEM)
    operands = (section, weights, mine, other, after)
    specs = [SCALARS, near, near, near, ANYWHERE]
    aliases = {}
    if done is not None:
        aliases = {len(operands): 0}
        operands += (done,)
        specs.append(ANYWHERE)
    outs = [shape_of(*shape), shape_of(8, LANES), shape_of(*band, dtype=BF16)]
    return pl.pallas_call(
        functools.partial(pixels_kernel, start=start, steps=steps, begins=done is None),
        in_specs=specs,
        out_specs=[ANYWHERE, near, near],
        out_shape=outs,
        scratch_shapes=[
            pltpu.VMEM((2, 2, 4 * STEP, img, channels, LANES), F32),
            pltpu.SemaphoreType.DMA((2, 2)),
        ],
        input_output_aliases=aliases,
        compiler_params=params(),
        cost_estimate=cost(2 + 0.8 * steps),
        name="pixels",
    )(*operands)


def small_call(
    kernel, outs, operands, scratch=(), name=None, place=None, after=(), weight=0.3, far=False
):
    specs = [pl.BlockSpec(memory_space=pltpu.VMEM)] * len(operands)
    if place is not None:
        operands = (*place, *operands)
        specs = [pl.BlockSpec(memory_space=pltpu.SMEM)] * len(place) + specs
    return pl.pallas_call(
        kernel,
        in_specs=specs + [ANYWHERE] * len(after),
        out_specs=jax.tree.map(
            lambda _: ANYWHERE if far else pl.BlockSpec(memory_space=pltpu.VMEM), outs
        ),
        out_shape=outs,
        scratch_shapes=list(scratch),
        compiler_params=params(),
        cost_estimate=cost(weight),
        name=name,
    )(*operands, *after)


def round_up(value, step):
    return -(-value // step) * step


def swapped(value):
    return lax.ppermute(value, "section", [(0, 1), (1, 0)])


def exchanged(value):
    return lax.all_to_all(value, "batch", split_axis=0, concat_axis=0, tiled=True)


def partner(value, distance):
    count = lax.axis_size("batch")
    return lax.ppermute(value, "batch", [(b, b ^ distance) for b in range(count)])


def local(
    frames,
    destination,
    options,
    depth,
    targets,
    conv_one,
    bias_one,
    conv_two,
    bias_two,
    linear_w,
    linear_b,
    branch_w,
    branch_b,
    head_w,
    head_b,
    value_w,
    value_b,
    out_w,
    out_b,
):
    section = lax.axis_index("section").astype(jnp.int32)[None]
    peers = lax.axis_size("batch")
    frame_count = frames.shape[3]
    per_pair = frame_count // peers
    levels = options.shape[0]
    frames = stays(frames.transpose(1, 2, 0, 3))
    w1t, w2t = stays(conv_one.T), stays(conv_two.T)
    branch_w, value_w = stays(branch_w), stays(value_w)
    encoder_params = (w1t, bias_one, w2t, bias_two, linear_w, linear_b)
    planner_params = (branch_w, branch_b, head_w.T, head_b, value_w, value_b, out_w.T, out_b)
    width = linear_w.shape[1]
    big_rows = linear_w.shape[0] + (branch_w.shape[0] + 1) * width
    size = round_up(-(-big_rows // (2 * CUBE)), 16)

    tiny = (bias_one, bias_two, linear_b, branch_b, head_w.T, value_b, out_w.T)
    tiny = [stays(v if v.ndim > 1 else v[None, :]) for v in tiny]
    numbers, table = pl.pallas_call(
        numbers_kernel,
        in_specs=[pl.BlockSpec(memory_space=pltpu.VMEM)] * (6 + len(tiny)),
        out_shape=[shape_of(frame_count, LANES), shape_of(TABLE, LANES)],
        compiler_params=params(),
        cost_estimate=cost(1),
        name="numbers",
    )(
        stays(options),
        stays(depth[None, :]),
        stays(targets),
        stays(destination[None, :]),
        *tiny,
        stays(head_b[None, :]),
        out_b[None, :],
    )
    slots = exchanged(numbers.reshape(peers, per_pair, LANES)).reshape(frame_count, LANES)

    h1, s1, s2, h2, enc, s3 = encode(section, frames, w1t, w2t, stays(linear_w), table)
    keep, send, small, g3 = plan(
        section, slots, enc, s3, h2, branch_w, value_w, table, per_pair, levels, CUBE * size
    )
    recv = swapped(send)
    channels = frames.shape[2] // lax.axis_size("section")
    g1, c2, sums = back(g3, linear_w, s2, s1, h1, w2t)
    other = held_near(swapped(g1))
    g1 = held_near(g1)
    place = (lax.axis_index("batch").astype(jnp.int32)[None],)
    bf16 = functools.partial(shape_of, dtype=BF16)
    pieces = small_call(
        merge_kernel,
        [bf16(size + 2 * SHORT, LANES)] * CUBE,
        (keep, recv, small, c2, sums),
        [pltpu.VMEM((CUBE * SHORT, LANES), F32)],
        name="merge",
        place=place,
    )
    parts = [pieces[0]] + [partner(pieces[k], k) for k in range(1, CUBE)]
    c1 = first(section, frames, g1, pieces[0])
    piece = bf16(size + 2 * SHORT + c1.shape[0], LANES)
    keep = small_call(cube_kernel, piece, (*parts, c1), name="cube")
    img = frames.shape[0]
    steps = img // 4 // STEP
    draw = functools.partial(
        pixels, section, mine=g1, other=other, shape=(img, img, channels, 2 * LANES)
    )
    distance = CUBE
    while distance < peers:
        recv = partner(keep, distance)
        if distance == CUBE:
            frames_grad, token, band = draw(weights=w1t, start=0, steps=4, after=keep)
        distance *= 2
        keep = small_call(add_kernel, piece, (keep, recv), name="add", after=(token,))
    parts = [keep] + [partner(keep, k) for k in range(1, CUBE)]
    frames_grad, token, _ = draw(
        weights=band, start=4, steps=steps - 4, after=keep, done=frames_grad
    )
    got = small_call(
        relay_kernel, bf16(CUBE, *piece.shape), parts, name="relay", place=place, after=(token,)
    )
    got_other = swapped(got)
    shapes = [p.shape for p in encoder_params + planner_params]
    near = pl.BlockSpec(memory_space=pltpu.VMEM)
    flat = [shape_of(*(v if len(v) > 1 else (1,) + v)) for v in [(1, 1)] + shapes]
    large = [flat[k] for k in (5, 7, 11)]
    staged = [
        pltpu.VMEM((CUBE * size, LANES), F32),
        pltpu.VMEM(branch_w.shape, F32),
    ]
    little = [v for k, v in enumerate(flat) if k not in (5, 7, 11)]
    sems = pltpu.SemaphoreType.DMA((CUBE + len(little),))
    begun = pl.pallas_call(
        own_kernel,
        in_specs=[SCALARS, near],
        out_specs=[ANYWHERE] * 3,
        out_shape=large,
        scratch_shapes=[*staged, sems],
        compiler_params=params(),
        cost_estimate=cost(1),
        name="own",
    )(section, got)
    ends = pl.pallas_call(
        unpack_kernel,
        in_specs=[SCALARS, near, near] + [ANYWHERE] * 3,
        out_specs=[ANYWHERE] * (3 + len(little)),
        out_shape=large + little,
        scratch_shapes=[pltpu.VMEM(v.shape, F32) for v in little]
        + [*staged, pltpu.VMEM((CUBE * SHORT, LANES), F32), sems],
        input_output_aliases={3: 0, 4: 1, 5: 2},
        compiler_params=params(),
        cost_estimate=cost(1.5),
        name="unpack",
    )(section, got, got_other, *begun)
    rest = list(ends[3:])
    for k, at in enumerate((5, 7, 11)):
        rest.insert(at, ends[k])
    rest = [v.reshape(s) for v, s in zip(rest, [()] + shapes)]
    for at in (1, 3, 9, 13):
        rest[at] = rest[at].T
    return (rest[0], frames_grad.transpose(2, 0, 1, 3), *rest[1:])


def solution(mesh):
    placed = (
        P(None, None, None, "batch"),
        P("batch"),
        P(None, "batch"),
        P("batch"),
        P(None, None, "batch"),
    ) + (P(),) * 14
    return jax.shard_map(
        local,
        mesh=mesh,
        in_specs=placed,
        out_specs=(P(), P("section", None, None, "batch")) + (P(),) * 14,
        check_vma=False,
    )
```

```python
import functools
import math

import jax
import jax.numpy as jnp
from jax import lax
from jax.experimental import pallas as pl
from jax.experimental.pallas import tpu as pltpu
from jax.sharding import PartitionSpec as P

BF16 = jnp.bfloat16
F32 = jnp.float32
EXACT = lax.Precision.HIGHEST
LANES = 128
VMEM_BYTES = 32 * 1024 * 1024
TILE = 16
REACH = 5
STEP = 3
COLS = 12
NEAR = 4
AT_VB, AT_OW, AT_HW, AT_LB, AT_SCALARS, AT_B1, AT_B2, AT_DEST = (
    slice(18, 19),
    slice(19, 20),
    slice(20, 22),
    slice(22, 23),
    slice(23, 24),
    slice(24, 25),
    slice(25, 26),
    26,
)
TABLE = 32
CUBE = 8
DRAW = 4
SHORT = 16


def dot(a, b, precision=None):
    return jnp.dot(a, b, preferred_element_type=F32, precision=precision)


def dot_rows(a, b, precision=None):
    return lax.dot_general(
        a, b, (((0,), (0,)), ((), ())), preferred_element_type=F32, precision=precision
    )


def dot_lanes(a, b, precision=None):
    return lax.dot_general(
        a, b, (((1,), (1,)), ((), ())), preferred_element_type=F32, precision=precision
    )


def iota(shape, axis):
    return lax.broadcasted_iota(jnp.int32, shape, axis)


def column(row):
    n = row.shape[1]
    wide = jnp.broadcast_to(row, (n, n))
    return jnp.sum(jnp.where(iota((n, n), 0) == iota((n, n), 1), wide, 0.0), axis=1, keepdims=True)


def row_of(col):
    n = col.shape[0]
    wide = jnp.broadcast_to(col, (n, n))
    return jnp.sum(jnp.where(iota((n, n), 0) == iota((n, n), 1), wide, 0.0), axis=0, keepdims=True)


def soft(x):
    t = jnp.tanh(0.5 * x)
    return jnp.maximum(x, 0.0) - jnp.log(0.5 + 0.5 * jnp.abs(t)), 0.5 + 0.5 * t


def silu_pair(x):
    s = 0.5 + 0.5 * jnp.tanh(0.5 * x)
    act = x * s
    return act, s + act * (1.0 - s)


def pixel_order(w1t):
    tap, pix = iota((256, 256), 0), iota((256, 256), 1)
    moves = ((tap >> 6) == (pix & 3)) & ((tap & 63) == (pix >> 2))
    return dot(w1t, moves.astype(F32).astype(BF16))


def frame_copies(section, far, here, sems):
    lanes = pl.ds(pl.multiple_of(section[0] * LANES, LANES), LANES)
    size = 4 * STEP

    def copy(g):
        rows = pl.ds(pl.multiple_of(g * size, size), size)
        return pltpu.make_async_copy(far.at[rows, :, :, lanes], here.at[rows], sems.at[g])

    return copy


def tile_rows(frames, row, j, cols):
    img, _, channels, _ = frames.shape
    flat = frames.reshape(img, img * channels, LANES)
    size = cols * channels
    end = min((j + 1) * size, img * channels)
    part = flat[pl.ds(row, 4), j * size : end, :]
    return part.reshape(4 * (end - j * size), LANES)


def encode_kernel(
    section,
    frames_far,
    w1t,
    w2t,
    lw_far,
    table,
    h1_far,
    s1_far,
    s2_far,
    h2,
    enc,
    s3,
    frames,
    lw,
    h1,
    s1,
    s2,
    band,
    edge,
    band2,
    bias1,
    bias2,
    held,
    held2,
    sems,
):
    blocks, side = h1.shape[:2]
    steps = blocks // STEP
    tiles = frames.shape[1] // TILE
    k1, k2 = w1t.shape[0], w2t.shape[0]
    reach_rows = REACH * k1
    arrives = frame_copies(section, frames_far, frames, sems.at[0])
    for g in range(steps):
        arrives(g).start()
    last_copies = [
        pltpu.make_async_copy(lw_far, lw, sems.at[3, 0]),
        pltpu.make_async_copy(s2, s2_far, sems.at[3, 1]),
    ]
    last_copies[0].start()

    def leaves(g):
        rows = pl.ds(g * STEP, STEP)
        return [
            pltpu.make_async_copy(h1.at[rows], h1_far.at[rows], sems.at[1, g]),
            pltpu.make_async_copy(s1.at[rows], s1_far.at[rows], sems.at[2, g]),
        ]

    inner = side // 2 - 1
    row_len = inner * k2
    two = 2 * k2 * 3

    def prepare():
        taps = pixel_order(w1t[...])
        edges = []
        for half in range(2):
            lines = [taps[:, 32 * (4 * half + u) : 32 * (4 * half + u + 1)] for u in range(4)]
            for place in range(REACH):
                pieces = []
                for line in lines:
                    start = 16 * (place - 1)
                    cut = line[:, max(0, -start) : min(32, 64 - start)]
                    start = max(start, 0)
                    pieces += [jnp.zeros((k1, start), F32)] if start else []
                    pieces.append(cut)
                    rest = 64 - start - cut.shape[1]
                    pieces += [jnp.zeros((k1, rest), F32)] if rest else []
                at = half * reach_rows + place * k1
                band[at : at + k1, :] = jnp.concatenate(pieces, axis=1).astype(BF16)
            edges.append(jnp.concatenate([line[:, 16:] for line in lines], axis=1))
        edge[...] = jnp.concatenate(edges, axis=0).astype(BF16)
        tap, pix = iota((256, LANES), 0), iota((256, LANES), 1)
        for half in range(2):
            for place in range(3):
                hit = (
                    ((tap & 15) == (pix & 15))
                    & ((tap >> 6) == (pix >> 6) + 2 * half)
                    & (((tap >> 4) & 3) == ((pix >> 4) & 3) + 2 - 2 * place)
                )
                at = (half * 3 + place) * k2
                taps = dot(w2t[...], hit.astype(F32).astype(BF16))
                band2[at : at + k2, :] = taps.astype(BF16)
        bias1[...] = jnp.broadcast_to(column(table[AT_B1, 0:k1]), bias1.shape)
        bias2[...] = jnp.broadcast_to(column(table[AT_B2, 0:k2]), bias2.shape)
        held[...] = jnp.zeros_like(held)
        held2[...] = jnp.zeros_like(held2)
        h1[...] = jnp.zeros_like(h1)

    def added(sums, x, value):
        sums[x] = sums[x] + value if x in sums else value

    def second_rows(b):
        tiles = [
            h1[pl.ds(2 * b + 1, 2), 4 * j : 4 * j + 4].reshape(LANES, LANES)
            for j in range(side // 4)
        ]
        got = dot(band2[...], jnp.concatenate(tiles, axis=1))
        low, high = {}, {}
        for j in range(side // 4):
            for place in range(3):
                x = 2 * j - 1 + place
                if 0 <= x < inner:
                    span = slice(j * LANES, (j + 1) * LANES)
                    at = place * k2
                    added(low, x, got[at : at + k2, span])
                    added(high, x, got[two // 2 + at : two // 2 + at + k2, span])
        row = jnp.maximum(b - 1, 0) * row_len
        for x in range(inner):
            value, slope = soft(held2[x] + high[x] + bias2[...])
            held2[x] = low[x]
            at = pl.ds(pl.multiple_of(row + x * k2, k2), k2)
            h2[at, :] = value.astype(BF16)
            s2[at, :] = slope.astype(BF16)

    def one_step(g, carry):
        def row(r):
            return pl.multiple_of(4 * (STEP * g + r), 4)

        arrives(g).wait()
        second_rows(jnp.maximum(g - 1, 0))

        last = dot(
            edge[...], jnp.concatenate([tile_rows(frames, row(r), tiles, TILE) for r in range(STEP)], axis=1)
        )
        odd = {}
        for r in range(STEP):
            low, high = {}, {}

            def place_tile(j, got):
                for place in range(REACH):
                    x = 4 * j - 1 + place
                    if 0 <= x < side:
                        at = place * k1
                        added(low, x, got[at : at + k1])
                        added(high, x, got[reach_rows + at : reach_rows + at + k1])

            if r not in odd:
                rows = [k for k in (r, r + 1) if k < STEP]
                cut = [tile_rows(frames, row(k), tiles - 1, TILE) for k in rows]
                got = dot(band[...], jnp.concatenate(cut, axis=1))
                odd.update({k: got[:, i * LANES : (i + 1) * LANES] for i, k in enumerate(rows)})
            place_tile(tiles - 1, odd[r])
            added(low, side - 1, last[:k1, r * LANES : (r + 1) * LANES])
            added(high, side - 1, last[k1:, r * LANES : (r + 1) * LANES])
            done = 0
            for j in range(0, tiles - 1, 2):
                cut = [tile_rows(frames, row(r), j + k, TILE) for k in range(2)]
                got = dot(band[...], jnp.concatenate(cut, axis=1))
                for k in range(2):
                    place_tile(j + k, got[:, k * LANES : (k + 1) * LANES])
                ready = side if j + 2 == tiles - 1 else 4 * j + 7
                for x in range(done, ready):
                    value, slope = soft(held[x] + high[x] + bias1[...])
                    held[x] = low[x]
                    value = value.astype(BF16)
                    h1[STEP * g + r, x] = value
                    s1[STEP * g + r, x] = slope.astype(BF16)
                done = ready
        for copy in leaves(g):
            copy.start()
        return carry

    prepare()
    lax.fori_loop(0, steps, one_step, 0)
    for b in range(steps - 1, side // 2):
        second_rows(b)
    for copy in last_copies[1:]:
        copy.start()
    last_copies[0].wait()
    value, slope = soft(dot_rows(lw[...], h2[...]) + column(table[AT_LB, :]))
    enc[...] = value.astype(BF16)
    s3[...] = slope
    for g in range(steps):
        for copy in leaves(g):
            copy.wait()
    for copy in last_copies[1:]:
        copy.wait()


def three_parts(row):
    high = row.astype(BF16).astype(F32)
    middle = (row - high).astype(BF16).astype(F32)
    return jnp.concatenate([high, middle, row - high - middle], axis=0)


def with_ones(value):
    return jnp.concatenate([value, ones_rows(value.shape[1])], axis=0)


def ones_rows(lanes):
    return (iota((16, lanes), 0) < 3).astype(F32).astype(BF16)


def plan_kernel(
    section,
    slots,
    enc,
    s3,
    h2,
    branch_far,
    value_w,
    table,
    keep,
    send,
    small,
    g3,
    parts,
    bwt,
    bb,
    vht,
    vhw,
    mine,
    pre,
    dbr,
    dval,
    low,
    hid,
    gb,
    branch_w,
    sem,
    *,
    per_pair,
    depth,
):
    width = enc.shape[0]
    options = branch_w.shape[0]
    pairs = options // 2
    two = 2 * width
    sec = section[0]
    branch_copy = pltpu.make_async_copy(branch_far, branch_w, sem)
    branch_copy.start()

    count = slots.shape[0]
    dest = jnp.concatenate(
        [table[AT_DEST + k : AT_DEST + k + 1, :] for k in range(count // LANES)], axis=1
    )
    own = jnp.where(sec == 0, dest[:, :LANES], dest[:, LANES:])
    others = jnp.transpose(jnp.broadcast_to(dest, (LANES, count)))
    index = iota((count, LANES), 1) + sec * LANES
    earlier = (others == own) & (iota((count, LANES), 0) < index)
    rank = jnp.sum(earlier.astype(F32), axis=0, keepdims=True)
    bucket = own * float(per_pair) + rank
    chosen = (iota((count, LANES), 0).astype(F32) == bucket).astype(F32).astype(BF16)
    numbers = slots[...]
    high = numbers.astype(BF16)
    middle = (numbers - high.astype(F32)).astype(BF16)
    rest = (numbers - high.astype(F32) - middle.astype(F32)).astype(BF16)
    mine[...] = sum(dot_rows(v, chosen) for v in (rest, middle, high))[: mine.shape[0]]

    columns = jnp.transpose(
        jnp.concatenate([table[...], jnp.zeros((width - TABLE, width), F32)], axis=0)
    )

    def across_lanes(row):
        return jnp.broadcast_to(columns[:, row : row + 1], (width, LANES))

    branch_copy.wait()
    for o in range(options):
        at = slice(o * width, (o + 1) * width)
        bwt[at, :] = jnp.transpose(branch_w[o].astype(F32)).astype(BF16)
        bb[at, :] = across_lanes(o)
    scalars = table[AT_SCALARS, :]
    head_w = table[AT_HW, :]
    vht[0:width, :] = jnp.transpose(value_w[...].astype(F32)).astype(BF16)
    vht[width:, :] = jnp.concatenate([head_w, jnp.zeros((14, width), F32)], axis=0).astype(BF16)
    vhw[:, 0:width] = value_w[...]
    vhw[:, width:] = jnp.transpose(
        jnp.concatenate([head_w, jnp.zeros((14, width), F32)], axis=0)
    ).astype(BF16)
    wide_ow = jnp.concatenate([across_lanes(AT_OW.start)] * 2, axis=1)
    wide_vb = jnp.concatenate([across_lanes(AT_VB.start)] * 2, axis=1)

    labels = iota((options, LANES), 0).astype(F32)
    state = enc[...].astype(F32)
    rounded_all, saved = [], []
    for level in range(depth):
        picked = labels == mine[level : level + 1, :]
        rounded = state.astype(BF16)
        rounded_all.append(rounded)
        pre[...] = dot(bwt[...], rounded) + bb[...]
        following = state
        reward, discount, value = [], [], []
        for t in range(pairs):
            at = slice(t * two, (t + 1) * two)
            act, slope = silu_pair(pre[at, :])
            dbr[level, at, :] = slope
            left = state + act[:width]
            right = state + act[width:]
            following = jnp.where(picked[2 * t : 2 * t + 1], left, following)
            following = jnp.where(picked[2 * t + 1 : 2 * t + 2], right, following)
            both = jnp.concatenate([left.astype(BF16), right.astype(BF16)], axis=1)
            low[level, t] = with_ones(both)
            got = dot(vht[...], both)
            act, slope = silu_pair(got[:width] + wide_vb)
            dval[level, t] = slope
            hidden = act.astype(BF16)
            hid[level, t] = hidden
            worth = jnp.sum(hidden.astype(F32) * wide_ow, axis=0, keepdims=True)
            for k in range(2):
                span = slice(k * LANES, (k + 1) * LANES)
                value.append(worth[:, span])
                reward.append(got[width : width + 1, span])
                discount.append(got[width + 1 : width + 2, span])
        reward = jnp.concatenate(reward, axis=0) + scalars[:, 1:2]
        discount = jax.nn.sigmoid(jnp.concatenate(discount, axis=0) + scalars[:, 2:3])
        value = jnp.concatenate(value, axis=0) + scalars[:, 3:4]
        quality = reward + discount * value
        top = jnp.max(quality, axis=0, keepdims=True)
        shifted = jnp.exp(quality - top)
        total = jnp.sum(shifted, axis=0, keepdims=True)
        live = (mine[depth : depth + 1, :] > level).astype(F32)
        chosen = picked.astype(F32)

        def target(kind):
            at = depth + 1 + kind * depth + level
            return mine[at : at + 1, :]

        reward_gap = live * (jnp.sum(chosen * reward, axis=0, keepdims=True) - target(0))
        discount_gap = live * (jnp.sum(chosen * discount, axis=0, keepdims=True) - target(1))
        plan_gap = live * (top + jnp.log(total) - target(2))
        grad_quality = plan_gap * (shifted / total)
        head_two = (chosen * discount_gap + grad_quality * value) * discount * (1.0 - discount)
        saved.append(
            (
                picked,
                (chosen * reward_gap + grad_quality).astype(BF16).astype(F32),
                head_two.astype(BF16).astype(F32),
                (grad_quality * discount).astype(BF16).astype(F32),
                reward_gap * reward_gap + discount_gap * discount_gap + plan_gap * plan_gap,
            )
        )
        state = following

    out_sum = jnp.zeros((width, two), F32)
    value_sum = jnp.zeros((width + 16, width + 16), F32)
    grad_next = jnp.zeros((width, LANES), F32)
    line = iota((16, two), 0)
    for level in reversed(range(depth)):
        picked, head_one, head_two, grad_value, _ = saved[level]
        upward = jnp.zeros((width, LANES), F32)
        for t in range(pairs):
            at = slice(t * two, (t + 1) * two)

            def across(rows):
                return jnp.concatenate(
                    [rows[2 * t : 2 * t + 1], rows[2 * t + 1 : 2 * t + 2]], axis=1
                )

            worth = across(grad_value)
            grad_pre = (worth * wide_ow * dval[level, t]).astype(BF16)
            out_sum = out_sum + hid[level, t].astype(F32) * worth
            heads = jnp.where(line == 0, across(head_one), 0.0)
            heads = jnp.where(line == 1, across(head_two), heads)
            heads = jnp.where(line == 2, worth, heads)
            stacked = jnp.concatenate([grad_pre, heads.astype(BF16)], axis=0)
            value_sum = value_sum + dot_lanes(stacked, low[level, t])
            moved = dot(vhw[...], stacked)
            left = moved[:, :LANES] + jnp.where(picked[2 * t : 2 * t + 1], grad_next, 0.0)
            right = moved[:, LANES:] + jnp.where(picked[2 * t + 1 : 2 * t + 2], grad_next, 0.0)
            grad_branch = jnp.concatenate([left, right], axis=0) * dbr[level, at, :]
            grad_branch = grad_branch.astype(BF16)
            gb[level, at, :] = grad_branch
            weights = jnp.concatenate([branch_w[2 * t], branch_w[2 * t + 1]], axis=1)
            upward = upward + (left + right + dot(weights, grad_branch))
        grad_next = upward

    linear_rows = h2.shape[0]
    half = (linear_rows + options * width + width) // 2
    rest = linear_rows - half
    rounded = with_ones(jnp.concatenate(rounded_all, axis=1))
    small[...] = jnp.zeros_like(small)
    if half < keep.shape[0]:
        for k in range(2):
            parts[k, half:, :] = jnp.zeros((keep.shape[0] - half, LANES), BF16)
    for t in range(pairs):
        at = slice(t * two, (t + 1) * two)
        grads = jnp.concatenate([gb[level, at, :] for level in range(depth)], axis=1)
        got = dot_lanes(rounded, grads)
        for k in range(2):
            o = 2 * t + k
            span = slice(k * width, (k + 1) * width)
            rows = slice(rest + o * width, rest + (o + 1) * width)
            parts[1 - sec, rows, :] = got[:width, span].astype(BF16)
            small[o : o + 1, :] = got[width : width + 1, span]
    after = rest + options * width
    parts[1 - sec, after : after + width, :] = jnp.transpose(value_sum[:width, :width]).astype(BF16)

    grad_three = (grad_next.astype(BF16).astype(F32) * s3[...]).astype(BF16)
    g3[...] = grad_three
    chunk = linear_rows // 9
    for i in range(8):
        at = slice(i * chunk, (i + 1) * chunk)
        parts[sec, at, :] = dot_lanes(h2[at, :], grad_three).astype(BF16)
    last = dot_lanes(h2[8 * chunk :, :], grad_three).astype(BF16)
    parts[sec, 8 * chunk : half, :] = last[: half - 8 * chunk]
    parts[1 - sec, 0:rest, :] = last[half - 8 * chunk :]
    keep[...] = parts[0]
    send[...] = parts[1]

    small[AT_VB, :] = row_of(value_sum[:width, width : width + 1])
    small[AT_OW, :] = row_of(jnp.sum(out_sum, axis=1, keepdims=True))
    small[AT_HW, :] = value_sum[width : width + 2, :width]
    small[AT_LB, :] = row_of(jnp.sum(grad_three.astype(F32), axis=1, keepdims=True))
    loss = 0.5 * jnp.sum(sum(kept[4] for kept in saved), axis=1, keepdims=True)
    ends = [loss] + [value_sum[width + k : width + k + 1, width : width + 1] for k in range(3)]
    lane = iota((1, LANES), 1)
    line = jnp.zeros((1, LANES), F32)
    for k, end in enumerate(ends):
        line = jnp.where(lane == k, end, line)
    small[AT_SCALARS, :] = line


def back_kernel(g3, lw, s2, s1, h1, w2t, g1, c2, sums, t2, g2):
    side, k1 = s1.shape[1], s1.shape[2]
    k2 = w2t.shape[0]
    inner = side // 2 - 1
    row_len = inner * k2
    tap, pix = iota((LANES, 256), 1), iota((LANES, 256), 0)
    for yrel in range(2):
        for p in range(3):
            hit = (
                ((tap & 15) == (pix & 15))
                & ((tap >> 6) == (pix >> 6) + 2 * (1 - yrel))
                & (((tap >> 4) & 3) == ((pix >> 4) & 3) + 2 - 2 * p)
            )
            at = (yrel * 3 + p) * k2
            t2[:, at : at + k2] = dot_lanes(hit.astype(F32).astype(BF16), w2t[...]).astype(BF16)
    g2[0] = jnp.zeros(g2.shape[1:], BF16)
    g2[inner + 1] = jnp.zeros(g2.shape[1:], BF16)
    g1[0] = jnp.zeros(g1.shape[1:], BF16)
    g1[side + 1] = jnp.zeros(g1.shape[1:], BF16)
    zero = jnp.zeros((k2, LANES), BF16)
    total_one = jnp.zeros((k1, LANES), F32)
    total_two = jnp.zeros((k2, LANES), F32)
    for y in range(inner):
        at = slice(y * row_len, (y + 1) * row_len)
        grad = dot(lw[at, :], g3[...]) * s2[at, :].astype(F32)
        grad = grad.astype(BF16).reshape(inner, k2, LANES)
        g2[y + 1] = grad
        total_two = total_two + jnp.sum(grad.astype(F32), axis=0)
    reach, cols = 5, 8
    total = jnp.zeros((2 * reach * k2, 2 * cols * k1), F32)
    grads, tiles = [], []
    for b in range(side // 2):
        cut = []
        for j in range(side // 4):
            pieces = []
            for yrel in range(2):
                for p in range(3):
                    x = 2 * j - 1 + p
                    pieces.append(g2[b + yrel, x] if 0 <= x < inner else zero)
            cut.append(jnp.concatenate(pieces, axis=0))
        got = dot(t2[...], jnp.concatenate(cut, axis=1))
        for u in range(2):
            for j in range(side // 4):
                part = got[u * 64 : (u + 1) * 64, j * LANES : (j + 1) * LANES]
                slope = s1[2 * b + u + 1, 4 * j : 4 * j + 4].astype(F32)
                grad = (part.reshape(4, k1, LANES) * slope).astype(BF16)
                g1[2 * b + u + 1, 4 * j : 4 * j + 4] = grad
                total_one = total_one + jnp.sum(grad.astype(F32), axis=0)
        for j in range(-(-side // cols)):
            end = min((j + 1) * cols, side)
            tile = h1[2 * b + 1 : 2 * b + 3, j * cols : end]
            if end < (j + 1) * cols:
                rest = jnp.zeros((2, (j + 1) * cols - end, k1, LANES), BF16)
                tile = jnp.concatenate([tile, rest], axis=1)
            tiles.append(tile.reshape(2 * cols * k1, LANES))
            pieces = []
            for half in range(2):
                for p in range(reach):
                    x = 4 * j - 1 + p
                    pieces.append(g2[b + 1 - half, x] if 0 <= x < inner else zero)
            grads.append(jnp.concatenate(pieces, axis=0))
        if b % 2:
            total = total + dot_lanes(
                jnp.concatenate(grads, axis=1), jnp.concatenate(tiles, axis=1)
            )
            grads, tiles = [], []
    line = 4 * k1
    for half in range(2):
        for u in range(2):
            tap_row = jnp.zeros((k2, line), F32)
            for p in range(reach):
                at = (half * reach + p) * k2
                part = total[at : at + k2, u * 2 * line : (u + 1) * 2 * line]
                start = 2 * k1 * (p - 1)
                piece = part[:, max(start, 0) : min(start + line, 2 * line)]
                if start < 0:
                    piece = jnp.concatenate([jnp.zeros((k2, -start), F32), piece], axis=1)
                if start + line > 2 * line:
                    rest = jnp.zeros((k2, start - line), F32)
                    piece = jnp.concatenate([piece, rest], axis=1)
                tap_row = tap_row + piece
            at = (2 * half + u) * line
            c2[:, at : at + line] = tap_row
    sums[...] = jnp.zeros_like(sums)
    sums[0:1, 0:k1] = row_of(jnp.sum(total_one, axis=1, keepdims=True))
    sums[1:2, 0:k2] = row_of(jnp.sum(total_two, axis=1, keepdims=True))


def pixel_band(sec, w1t, channels):
    k1 = w1t.shape[0]
    rows = 64 * channels
    row, tap = iota((rows, 256), 0), iota((rows, 256), 1)
    moves = ((tap >> 6) == row % channels + sec * channels) & ((tap & 63) == row // channels)
    taps = dot_lanes(moves.astype(F32).astype(BF16), w1t)
    line, span = COLS * channels, 8 * channels
    blocks = {}
    for half in range(2):
        for p in range(NEAR):
            pieces = []
            for u in range(4):
                at = (4 * half + u) * span
                start = 4 * (p - 1) * channels
                cut = taps[at + max(0, -start) : at + min(span, line - start)]
                start = max(start, 0)
                pieces += [jnp.zeros((start, k1), F32)] if start else []
                pieces.append(cut)
                rest = line - start - cut.shape[0]
                pieces += [jnp.zeros((rest, k1), F32)] if rest else []
            blocks[half, p] = jnp.concatenate(pieces, axis=0)
    zero = jnp.zeros((4 * line, k1), F32)
    lines = []
    for r in range(STEP):
        cols = [
            blocks.get((r + 1 - yrel, p), zero) for yrel in range(STEP + 1) for p in range(NEAR)
        ]
        lines.append(jnp.concatenate(cols, axis=1))
    return jnp.concatenate(lines, axis=0).astype(BF16)


def first_kernel(
    section,
    frames_far,
    g1,
    w1t,
    other_far,
    after,
    c1,
    out,
    band,
    frames,
    acc,
    other,
    held,
    sems,
    draw_sems,
    *,
    draw,
):
    side, k1 = g1.shape[1], g1.shape[2]
    img, _, channels, _ = frames.shape
    steps = img // 4 // STEP
    arrives = frame_copies(section, frames_far, frames, sems)
    for g in range(steps):
        arrives(g).start()
    other_copy = pltpu.make_async_copy(
        other_far.at[0 : STEP * draw + 1], other, sems.at[steps]
    )
    other_copy.start()
    acc[...] = jnp.zeros_like(acc)
    zero = jnp.zeros((k1, LANES), BF16)

    def one_step(g, carry):
        arrives(g).wait()
        pixels, grads = [], []
        for j in range(img // COLS):
            rows = [pl.multiple_of(4 * (STEP * g + r), 4) for r in range(STEP)]
            pixels.append(
                jnp.concatenate([tile_rows(frames, row, j, COLS) for row in rows], axis=0)
            )
            pieces = []
            for yrel in range(STEP + 1):
                for p in range(NEAR):
                    x = 3 * j - 1 + p
                    pieces.append(g1[STEP * g + yrel, x] if 0 <= x < side else zero)
            grads.append(jnp.concatenate(pieces, axis=0))
        acc[...] += dot_lanes(jnp.concatenate(pixels, axis=1), jnp.concatenate(grads, axis=1))
        return carry

    lax.fori_loop(0, steps, one_step, 0)
    band[...] = pixel_band(section[0], w1t[...], out.shape[2])
    other_copy.wait()
    finish = draw_steps(section, band, g1, 0, other, 0, out, held, draw_sems, 0, draw)
    fold_first(acc, c1, channels, k1)
    finish()


def fold_first(acc, c1, channels, k1):
    line = COLS * channels
    step = 4 * channels
    taps = []
    for half in range(2):
        total = sum(
            acc[r * 4 * line : (r + 1) * 4 * line, :][
                :, (r + 1 - half) * NEAR * k1 : (r + 2 - half) * NEAR * k1
            ]
            for r in range(STEP)
        )
        for u in range(4):
            part = total[u * line : (u + 1) * line]
            cols = [part[:, p * k1 : (p + 1) * k1] for p in range(NEAR)]
            taps.append(cols[1][0:step] + cols[2][step : 2 * step] + cols[3][2 * step :])
            taps.append(cols[0][0:step] + cols[1][step : 2 * step] + cols[2][2 * step :])
    row, col = iota((256, 256), 0), iota((256, 256), 1)
    moves = ((row & 3) == (col >> 6)) & ((row >> 2) == (col & 63))
    grad = dot_rows(jnp.concatenate(taps, axis=0), moves.astype(F32), EXACT)
    for half in range(2):
        c1[half * k1 : (half + 1) * k1, :] = grad[:, half * LANES : (half + 1) * LANES].astype(BF16)


def draw_steps(section, band, mine, mine_at, other, other_at, out, held, sems, start, steps):
    side, k1 = mine.shape[1], mine.shape[2]
    img, channels = out.shape[1], out.shape[2]
    sec = section[0]
    line = COLS * channels
    flat = held.reshape(2, 2, 4 * STEP, img * channels, LANES)

    def writes(g):
        rows = slice(4 * STEP * (start + g), 4 * STEP * (start + g + 1))
        places = (sec * LANES, (1 - sec) * LANES)
        return [
            pltpu.make_async_copy(
                held.at[g % 2, k],
                out.at[rows, :, :, pl.ds(pl.multiple_of(places[k], LANES), LANES)],
                sems.at[g % 2, k],
            )
            for k in range(2)
        ]

    zero = jnp.zeros((k1, 2 * LANES), BF16)
    for g in range(steps):
        if g >= 2:
            for copy in writes(g - 2):
                copy.wait()
        for j in range(img // COLS):
            pieces = []
            for yrel in range(STEP + 1):
                for p in range(NEAR):
                    x, y = 3 * j - 1 + p, STEP * (start + g) + yrel
                    if 0 <= x < side:
                        pair = [mine[y - mine_at, x], other[y - other_at, x]]
                        pieces.append(jnp.concatenate(pair, axis=1))
                    else:
                        pieces.append(zero)
            got = dot(band[...], jnp.concatenate(pieces, axis=0))
            for k in range(4 * STEP):
                at = slice(k * line, (k + 1) * line)
                span = slice(j * line, (j + 1) * line)
                flat[g % 2, 0, k, span, :] = got[at, :LANES]
                flat[g % 2, 1, k, span, :] = got[at, LANES:]
        for copy in writes(g):
            copy.start()

    def finish():
        for g in range(max(steps - 2, 0), steps):
            for copy in writes(g):
                copy.wait()

    return finish


def pixels_kernel(section, band, mine, other_far, after, done, out, token, held, other, sems, *, start):
    steps = other.shape[0] // STEP
    fetch = pltpu.make_async_copy(
        other_far.at[STEP * start : STEP * (start + steps) + 1], other, sems.at[2, 0]
    )
    fetch.start()
    token[...] = jnp.zeros_like(token)
    fetch.wait()
    draw_steps(
        section, band, mine, 0, other, STEP * start, out, held, sems, start, steps
    )()


def two_parts(value):
    high = value.astype(BF16).astype(F32)
    return jnp.concatenate([high, value - high], axis=0).astype(BF16)


def one_part(pair):
    rows = pair.shape[0] // 2
    pair = pair.astype(F32)
    return pair[:rows] + pair[rows:]


def merge_kernel(keep, recv, small, c2, sums, out_far, lines, out, sems):
    members = out.shape[0]
    size = keep.shape[0] // members
    k2 = c2.shape[0]
    lines[...] = jnp.zeros_like(lines)
    at = small.shape[0]
    lines[0:at, :] = small[...]
    for half in range(2):
        lines[at : at + k2, :] = c2[:, half * LANES : (half + 1) * LANES]
        at += k2
    lines[at : at + sums.shape[0], :] = sums[...]
    for k in range(members):
        at = slice(k * size, (k + 1) * size)
        out[k, 0:size, :] = (keep[at, :].astype(F32) + recv[at, :].astype(F32)).astype(BF16)
        out[k, size:, :] = two_parts(lines[k * SHORT : (k + 1) * SHORT, :])
        pltpu.make_async_copy(out.at[k], out_far.at[k], sems.at[k]).start()
    for k in range(members):
        pltpu.make_async_copy(out.at[k], out_far.at[k], sems.at[k]).wait()


def cube_kernel(got, c1, out):
    members = got.shape[0]
    size = got.shape[1] - 2 * SHORT
    out[0:size, :] = sum(got[k, 0:size, :].astype(F32) for k in range(members)).astype(BF16)
    total = sum(one_part(got[k, size:, :]) for k in range(members))
    out[size : size + 2 * SHORT, :] = two_parts(total)
    out[size + 2 * SHORT :, :] = c1[...]


def add_kernel(a, b, after, out):
    size = a.shape[0] - 2 * SHORT - 32
    middle = slice(size, size + 2 * SHORT)
    for span in (slice(0, size), slice(size + 2 * SHORT, a.shape[0])):
        out[span, :] = (a[span, :].astype(F32) + b[span, :].astype(F32)).astype(BF16)
    out[middle, :] = two_parts(one_part(a[middle, :]) + one_part(b[middle, :]))


def relay_kernel(batch, *refs):
    parts, out = refs[:CUBE], refs[-1]
    me = batch[0] % CUBE
    for k, part in enumerate(parts):
        out[me ^ k] = part[...]


def unpack_half(which, got, lw, bw, vw, stage, stage_b, sems):
    members = got.shape[0]
    size = stage.shape[0] // members
    linear_rows, width = lw.shape
    options = bw.shape[0]
    half = (linear_rows + options * width + width) // 2
    rest = linear_rows - half

    @pl.when(which == 0)
    def _():
        copies = []
        for k in range(members):
            start, end = k * size, min((k + 1) * size, half)
            stage[start:end, :] = got[k, 0 : end - start, :].astype(F32)
            copies.append(
                pltpu.make_async_copy(stage.at[start:end], lw.at[start:end], sems.at[k])
            )
            copies[-1].start()
        for copy in copies:
            copy.wait()

    @pl.when(which == 1)
    def _():
        def rows(start, end):
            parts = []
            while start < end:
                k, at = start // size, start % size
                count = min(size - at, end - start)
                parts.append(got[k, at : at + count, :])
                start += count
            value = parts[0] if len(parts) == 1 else jnp.concatenate(parts, axis=0)
            return value.astype(F32)

        stage[0:rest, :] = rows(0, rest)
        copies = [pltpu.make_async_copy(stage.at[0:rest], lw.at[half:], sems.at[0])]
        copies[0].start()
        group = options // 3
        for o in range(options):
            stage_b[o] = rows(rest + o * width, rest + (o + 1) * width)
            if o % group == group - 1:
                part = slice(o + 1 - group, o + 1)
                copy = pltpu.make_async_copy(
                    stage_b.at[part], bw.at[part], sems.at[1 + o // group]
                )
                copy.start()
                copies.append(copy)
        at = rest + options * width
        stage[rest : rest + width, :] = rows(at, at + width)
        copies.append(
            pltpu.make_async_copy(stage.at[rest : rest + width], vw, sems.at[1 + options // group])
        )
        copies[-1].start()
        for copy in copies:
            copy.wait()


def own_kernel(section, mine, lw, bw, vw, stage, stage_b, sems):
    unpack_half(section[0], mine, lw, bw, vw, stage, stage_b, sems)


def unpack_kernel(section, mine, other, *refs):
    lw, bw, vw = refs[3:6]
    little = (len(refs) - 10) // 2
    far, near = refs[6 : 6 + little], refs[6 + little : 6 + 2 * little]
    loss, c1, b1, c2, b2, lb, bb, hw, hb, vb, ow, ob = near
    stage, stage_b, lines, sems = refs[-4:]
    options = bw.shape[0]
    k1, k2 = c1.shape[0], c2.shape[0]
    size = stage.shape[0] // CUBE
    grad = [jnp.zeros((k1, LANES), F32) for _ in range(2)]
    for k in range(CUBE):
        pair = slice(size, size + 2 * SHORT)
        at = slice(k * SHORT, (k + 1) * SHORT)
        lines[at, :] = one_part(mine[k, pair, :]) + one_part(other[k, pair, :])
        for ref in (mine, other):
            for h in range(2):
                at = size + 2 * SHORT + h * k1
                grad[h] += ref[k, at : at + k1, :].astype(F32)
    for part in range(2):
        c1[:, part * LANES : (part + 1) * LANES] = grad[part]
    bb[...] = lines[0:options, :]
    vb[...] = lines[AT_VB, :]
    ow[...] = lines[AT_OW, :]
    hw[...] = lines[AT_HW, :]
    lb[...] = lines[AT_LB, :]
    scalars = lines[AT_SCALARS, :]
    loss[...] = scalars[:, 0:1]
    hb[...] = scalars[:, 1:3]
    ob[...] = scalars[:, 3:4]
    at = TABLE
    for part in range(2):
        c2[:, part * LANES : (part + 1) * LANES] = lines[at : at + k2, :]
        at += k2
    b1[...] = lines[at : at + 1, 0:k1]
    b2[...] = lines[at + 1 : at + 2, 0:k2]
    copies = [
        pltpu.make_async_copy(a, b, sems.at[CUBE + k]) for k, (a, b) in enumerate(zip(near, far))
    ]
    for copy in copies:
        copy.start()
    unpack_half(1 - section[0], other, lw, bw, vw, stage, stage_b, sems)
    for copy in copies:
        copy.wait()


def numbers_kernel(
    options,
    depth,
    targets,
    destination,
    b1,
    b2,
    lb,
    bb,
    hw,
    vb,
    ow,
    hb,
    ob,
    out,
    table,
):
    levels, kinds = options.shape[0], targets.shape[0]
    slots = depth.shape[1]
    rows = [options[...].astype(F32), depth[...].astype(F32)]
    rows += [targets[k] for k in range(kinds)]
    rows.append(jnp.zeros((LANES - levels - 1 - kinds * levels, slots), F32))
    out[...] = jnp.transpose(jnp.concatenate(rows, axis=0))
    table[...] = jnp.zeros_like(table)
    table[0 : bb.shape[0], :] = bb[...]
    table[AT_VB, :] = vb[...]
    table[AT_OW, :] = ow[...].astype(F32)
    table[AT_HW, :] = hw[...].astype(F32)
    table[AT_LB, :] = lb[...]
    table[AT_B1, 0 : b1.shape[1]] = b1[...]
    table[AT_B2, 0 : b2.shape[1]] = b2[...]
    lane = iota((1, LANES), 1)
    scalars = jnp.zeros((1, LANES), F32)
    for k, value in ((1, hb[:, 0:1]), (2, hb[:, 1:2]), (3, ob[...])):
        scalars = jnp.where(lane == k, value, scalars)
    table[AT_SCALARS, :] = scalars
    for k in range(slots // LANES):
        part = destination[:, k * LANES : (k + 1) * LANES]
        table[AT_DEST + k : AT_DEST + k + 1, :] = part.astype(F32)


def whole(shape):
    zeros = (0,) * len(shape)
    return pl.BlockSpec(shape, lambda *_: zeros)


ANYWHERE = pl.BlockSpec(memory_space=pl.ANY)
SCALARS = pl.BlockSpec(memory_space=pltpu.SMEM)


def params():
    return pltpu.CompilerParams(vmem_limit_bytes=VMEM_BYTES)


def shape_of(*shape, dtype=F32):
    return jax.ShapeDtypeStruct(shape, dtype)


def cost(microseconds):
    return pl.CostEstimate(
        flops=int(1.1e9 * microseconds), bytes_accessed=int(3.6e6 * microseconds), transcendentals=0
    )


def stays(value):
    return pltpu.with_memory_space_constraint(value, pltpu.HBM)


def held_near(value):
    return pltpu.with_memory_space_constraint(value, pltpu.VMEM)


def encode(section, frames, w1t, w2t, lw, table):
    img = frames.shape[0]
    blocks = img // 4
    side = blocks - 1
    k1, k2, width = w1t.shape[0], w2t.shape[0], lw.shape[1]
    flat = lw.shape[0]
    vmem = pltpu.VMEM
    near = pl.BlockSpec(memory_space=vmem)
    grid_one = (blocks, side, k1, LANES)
    return pl.pallas_call(
        encode_kernel,
        in_specs=[SCALARS, ANYWHERE, near, near, ANYWHERE, near],
        out_specs=[ANYWHERE] * 3 + [near] * 3,
        out_shape=(
            pltpu.HBM(grid_one, BF16),
            pltpu.HBM(grid_one, BF16),
            pltpu.HBM((flat, LANES), BF16),
            shape_of(flat, LANES, dtype=BF16),
            shape_of(width, LANES, dtype=BF16),
            shape_of(width, LANES),
        ),
        scratch_shapes=[
            vmem((img, img, frames.shape[2], LANES), BF16),
            vmem(lw.shape, BF16),
            vmem(grid_one, BF16),
            vmem(grid_one, BF16),
            vmem((flat, LANES), BF16),
            vmem((2 * REACH * k1, 256), BF16),
            vmem((2 * k1, 64), BF16),
            vmem((6 * k2, LANES), BF16),
            vmem((k1, LANES), F32),
            vmem((k2, LANES), F32),
            vmem((side, k1, LANES), F32),
            vmem((side // 2 - 1, k2, LANES), F32),
            pltpu.SemaphoreType.DMA((4, max(blocks // STEP, 3))),
        ],
        compiler_params=params(),
        cost_estimate=cost(9),
        name="encode",
    )(section, frames, w1t, w2t, lw, table)


def plan(section, slots, enc, s3, h2, branch_w, value_w, table, per_pair, depth, half_rows):
    width = enc.shape[0]
    options = branch_w.shape[0]
    two = 2 * width
    pairs = options // 2
    outs = (
        shape_of(half_rows, LANES, dtype=BF16),
        shape_of(half_rows, LANES, dtype=BF16),
        shape_of(TABLE, LANES),
        shape_of(width, LANES, dtype=BF16),
    )
    vmem = pltpu.VMEM
    near = pl.BlockSpec(memory_space=vmem)
    return pl.pallas_call(
        functools.partial(plan_kernel, per_pair=per_pair, depth=depth),
        in_specs=[SCALARS, near, near, near, near, ANYWHERE, near, near],
        out_shape=outs,
        scratch_shapes=[
            vmem((2, half_rows, LANES), BF16),
            vmem((options * width, width), BF16),
            vmem((options * width, LANES), F32),
            vmem((width + 16, width), BF16),
            vmem((width, width + 16), BF16),
            vmem((16, LANES), F32),
            vmem((options * width, LANES), F32),
            vmem((depth, options * width, LANES), F32),
            vmem((depth, pairs, width, two), F32),
            vmem((depth, pairs, width + 16, two), BF16),
            vmem((depth, pairs, width, two), BF16),
            vmem((depth, options * width, LANES), BF16),
            vmem(branch_w.shape, BF16),
            pltpu.SemaphoreType.DMA,
        ],
        compiler_params=params(),
        cost_estimate=cost(11),
        name="plan",
    )(section, slots, enc, s3, h2, branch_w, value_w, table)


def back(g3, lw, s2, s1, h1, w2t):
    _, side, k1 = s1.shape[:3]
    k2 = w2t.shape[0]
    inner = side // 2 - 1
    padded = (side + 2, side, k1, LANES)
    near = pl.BlockSpec(memory_space=pltpu.VMEM)
    return pl.pallas_call(
        back_kernel,
        in_specs=[near] * 6,
        out_shape=(shape_of(*padded, dtype=BF16), shape_of(k2, 256), shape_of(8, LANES)),
        scratch_shapes=[
            pltpu.VMEM((LANES, 6 * k2), BF16),
            pltpu.VMEM((inner + 2, inner, k2, LANES), BF16),
        ],
        compiler_params=params(),
        cost_estimate=cost(25),
        name="back",
    )(g3, lw, s2, s1, h1, w2t)


def first(section, frames, g1, w1t, other, after, channels, draw):
    img, _, stack, _ = frames.shape
    k1 = g1.shape[2]
    band = (STEP * 4 * COLS * channels, (STEP + 1) * NEAR * k1)
    near = pl.BlockSpec(memory_space=pltpu.VMEM)
    return pl.pallas_call(
        functools.partial(first_kernel, draw=draw),
        in_specs=[SCALARS, ANYWHERE, near, near, ANYWHERE, ANYWHERE],
        out_specs=[near, ANYWHERE, near],
        out_shape=[
            shape_of(2 * k1, LANES, dtype=BF16),
            shape_of(img, img, channels, 2 * LANES),
            shape_of(*band, dtype=BF16),
        ],
        scratch_shapes=[
            pltpu.VMEM((img, img, stack, LANES), BF16),
            pltpu.VMEM((STEP * 4 * COLS * stack, (STEP + 1) * NEAR * k1), F32),
            pltpu.VMEM((STEP * draw + 1,) + g1.shape[1:], BF16),
            pltpu.VMEM((2, 2, 4 * STEP, img, channels, LANES), F32),
            pltpu.SemaphoreType.DMA((img // 4 // STEP + 1,)),
            pltpu.SemaphoreType.DMA((2, 2)),
        ],
        compiler_params=params(),
        cost_estimate=cost(45),
        name="first",
    )(section, frames, g1, w1t, other, after)


def pixels(section, band, mine, other, after, done, start):
    img, _, channels, _ = done.shape
    steps = img // 4 // STEP - start
    near = pl.BlockSpec(memory_space=pltpu.VMEM)
    return pl.pallas_call(
        functools.partial(pixels_kernel, start=start),
        in_specs=[SCALARS, near, near, ANYWHERE, ANYWHERE, ANYWHERE],
        out_specs=[ANYWHERE, near],
        out_shape=[shape_of(*done.shape), shape_of(8, LANES)],
        scratch_shapes=[
            pltpu.VMEM((2, 2, 4 * STEP, img, channels, LANES), F32),
            pltpu.VMEM((STEP * steps + 1,) + mine.shape[1:], BF16),
            pltpu.SemaphoreType.DMA((3, 2)),
        ],
        input_output_aliases={5: 0},
        compiler_params=params(),
        cost_estimate=cost(1 + 0.9 * steps),
        name="pixels",
    )(section, band, mine, other, after, done)


def small_call(
    kernel, outs, operands, scratch=(), name=None, place=None, after=(), weight=0.3, far=False
):
    specs = [pl.BlockSpec(memory_space=pltpu.VMEM)] * len(operands)
    if place is not None:
        operands = (*place, *operands)
        specs = [pl.BlockSpec(memory_space=pltpu.SMEM)] * len(place) + specs
    return pl.pallas_call(
        kernel,
        in_specs=specs + [ANYWHERE] * len(after),
        out_specs=jax.tree.map(
            lambda _: ANYWHERE if far else pl.BlockSpec(memory_space=pltpu.VMEM), outs
        ),
        out_shape=outs,
        scratch_shapes=list(scratch),
        compiler_params=params(),
        cost_estimate=cost(weight),
        name=name,
    )(*operands, *after)


def round_up(value, step):
    return -(-value // step) * step


def swapped(value):
    return lax.ppermute(value, "section", [(0, 1), (1, 0)])


def exchanged(value, groups=None):
    return lax.all_to_all(
        value, "batch", split_axis=0, concat_axis=0, axis_index_groups=groups, tiled=True
    )


def partner(value, distance):
    count = lax.axis_size("batch")
    return lax.ppermute(value, "batch", [(b, b ^ distance) for b in range(count)])


def local(
    frames,
    destination,
    options,
    depth,
    targets,
    conv_one,
    bias_one,
    conv_two,
    bias_two,
    linear_w,
    linear_b,
    branch_w,
    branch_b,
    head_w,
    head_b,
    value_w,
    value_b,
    out_w,
    out_b,
):
    section = lax.axis_index("section").astype(jnp.int32)[None]
    peers = lax.axis_size("batch")
    frame_count = frames.shape[3]
    per_pair = frame_count // peers
    levels = options.shape[0]
    frames = stays(frames.transpose(1, 2, 0, 3))
    w1t, w2t = stays(conv_one.T), stays(conv_two.T)
    branch_w, value_w = stays(branch_w), stays(value_w)
    encoder_params = (w1t, bias_one, w2t, bias_two, linear_w, linear_b)
    planner_params = (branch_w, branch_b, head_w.T, head_b, value_w, value_b, out_w.T, out_b)
    width = linear_w.shape[1]
    big_rows = linear_w.shape[0] + (branch_w.shape[0] + 1) * width
    size = round_up(-(-big_rows // (2 * CUBE)), 16)

    tiny = (bias_one, bias_two, linear_b, branch_b, head_w.T, value_b, out_w.T)
    tiny = [stays(v if v.ndim > 1 else v[None, :]) for v in tiny]
    numbers, table = pl.pallas_call(
        numbers_kernel,
        in_specs=[pl.BlockSpec(memory_space=pltpu.VMEM)] * (6 + len(tiny)),
        out_shape=[shape_of(frame_count, LANES), shape_of(TABLE, LANES)],
        compiler_params=params(),
        cost_estimate=cost(1),
        name="numbers",
    )(
        stays(options),
        stays(depth[None, :]),
        stays(targets),
        stays(destination[None, :]),
        *tiny,
        stays(head_b[None, :]),
        out_b[None, :],
    )
    slots = exchanged(numbers.reshape(peers, per_pair, LANES)).reshape(frame_count, LANES)

    h1, s1, s2, h2, enc, s3 = encode(section, frames, w1t, w2t, stays(linear_w), table)
    keep, send, small, g3 = plan(
        section, slots, enc, s3, h2, branch_w, value_w, table, per_pair, levels, CUBE * size
    )
    recv = swapped(send)
    channels = frames.shape[2] // lax.axis_size("section")
    g1, c2, sums = back(g3, linear_w, s2, s1, h1, w2t)
    other = swapped(g1)
    g1 = held_near(g1)
    cubes = [list(range(c, c + CUBE)) for c in range(0, peers, CUBE)]
    bf16 = functools.partial(shape_of, dtype=BF16)
    pieces = small_call(
        merge_kernel,
        bf16(CUBE, size + 2 * SHORT, LANES),
        (keep, recv, small, c2, sums),
        [
            pltpu.VMEM((CUBE * SHORT, LANES), F32),
            pltpu.VMEM((CUBE, size + 2 * SHORT, LANES), BF16),
            pltpu.SemaphoreType.DMA((CUBE,)),
        ],
        name="merge",
        far=True,
    )
    got = exchanged(pieces, cubes)
    c1, frames_grad, band = first(section, frames, g1, w1t, other, pieces, channels, DRAW)
    piece = bf16(size + 2 * SHORT + c1.shape[0], LANES)
    keep = small_call(cube_kernel, piece, (got, c1), name="cube")
    distance = CUBE
    while distance < peers:
        recv = partner(keep, distance)
        if distance == CUBE:
            frames_grad, token = pixels(section, band, g1, other, keep, frames_grad, DRAW)
        distance *= 2
        keep = small_call(add_kernel, piece, (keep, recv), name="add", after=(token,))
    parts = [keep] + [partner(keep, k) for k in range(1, CUBE)]
    place = (lax.axis_index("batch").astype(jnp.int32)[None],)
    got = small_call(relay_kernel, bf16(CUBE, *piece.shape), parts, name="relay", place=place)
    got_other = swapped(got)
    shapes = [p.shape for p in encoder_params + planner_params]
    near = pl.BlockSpec(memory_space=pltpu.VMEM)
    flat = [shape_of(*(v if len(v) > 1 else (1,) + v)) for v in [(1, 1)] + shapes]
    large = [flat[k] for k in (5, 7, 11)]
    staged = [
        pltpu.VMEM((CUBE * size, LANES), F32),
        pltpu.VMEM(branch_w.shape, F32),
    ]
    little = [v for k, v in enumerate(flat) if k not in (5, 7, 11)]
    sems = pltpu.SemaphoreType.DMA((CUBE + len(little),))
    begun = pl.pallas_call(
        own_kernel,
        in_specs=[SCALARS, near],
        out_specs=[ANYWHERE] * 3,
        out_shape=large,
        scratch_shapes=[*staged, sems],
        compiler_params=params(),
        cost_estimate=cost(1),
        name="own",
    )(section, got)
    ends = pl.pallas_call(
        unpack_kernel,
        in_specs=[SCALARS, near, near] + [ANYWHERE] * 3,
        out_specs=[ANYWHERE] * (3 + len(little)),
        out_shape=large + little,
        scratch_shapes=[pltpu.VMEM(v.shape, F32) for v in little]
        + [*staged, pltpu.VMEM((CUBE * SHORT, LANES), F32), sems],
        input_output_aliases={3: 0, 4: 1, 5: 2},
        compiler_params=params(),
        cost_estimate=cost(1.5),
        name="unpack",
    )(section, got, got_other, *begun)
    rest = list(ends[3:])
    for k, at in enumerate((5, 7, 11)):
        rest.insert(at, ends[k])
    rest = [v.reshape(s) for v, s in zip(rest, [()] + shapes)]
    for at in (1, 3, 9, 13):
        rest[at] = rest[at].T
    return (rest[0], frames_grad.transpose(2, 0, 1, 3), *rest[1:])


def solution(mesh):
    placed = (
        P(None, None, None, "batch"),
        P("batch"),
        P(None, "batch"),
        P("batch"),
        P(None, None, "batch"),
    ) + (P(),) * 14
    return jax.shard_map(
        local,
        mesh=mesh,
        in_specs=placed,
        out_specs=(P(), P("section", None, None, "batch")) + (P(),) * 14,
        check_vma=False,
    )
```

```python
import functools
import math

import jax
import jax.numpy as jnp
from jax import lax
from jax.experimental import pallas as pl
from jax.experimental.pallas import tpu as pltpu
from jax.sharding import PartitionSpec as P

BF16 = jnp.bfloat16
F32 = jnp.float32
EXACT = lax.Precision.HIGHEST
LANES = 128
VMEM_BYTES = 32 * 1024 * 1024
TILE = 16
REACH = 5
STEP = 3
COLS = 12
NEAR = 4
AT_VB, AT_OW, AT_HW, AT_LB, AT_SCALARS, AT_B1, AT_B2, AT_DEST = (
    slice(18, 19),
    slice(19, 20),
    slice(20, 22),
    slice(22, 23),
    slice(23, 24),
    slice(24, 25),
    slice(25, 26),
    26,
)
TABLE = 32
CUBE = 8
DRAW = 4
SHORT = 16


def dot(a, b, precision=None):
    return jnp.dot(a, b, preferred_element_type=F32, precision=precision)


def dot_rows(a, b, precision=None):
    return lax.dot_general(
        a, b, (((0,), (0,)), ((), ())), preferred_element_type=F32, precision=precision
    )


def dot_lanes(a, b, precision=None):
    return lax.dot_general(
        a, b, (((1,), (1,)), ((), ())), preferred_element_type=F32, precision=precision
    )


def iota(shape, axis):
    return lax.broadcasted_iota(jnp.int32, shape, axis)


def column(row):
    n = row.shape[1]
    wide = jnp.broadcast_to(row, (n, n))
    return jnp.sum(jnp.where(iota((n, n), 0) == iota((n, n), 1), wide, 0.0), axis=1, keepdims=True)


def row_of(col):
    n = col.shape[0]
    wide = jnp.broadcast_to(col, (n, n))
    return jnp.sum(jnp.where(iota((n, n), 0) == iota((n, n), 1), wide, 0.0), axis=0, keepdims=True)


def soft(x):
    t = jnp.tanh(0.5 * x)
    return jnp.maximum(x, 0.0) - jnp.log(0.5 + 0.5 * jnp.abs(t)), 0.5 + 0.5 * t


def silu_pair(x):
    s = 0.5 + 0.5 * jnp.tanh(0.5 * x)
    act = x * s
    return act, s + act * (1.0 - s)


def pixel_order(w1t):
    tap, pix = iota((256, 256), 0), iota((256, 256), 1)
    moves = ((tap >> 6) == (pix & 3)) & ((tap & 63) == (pix >> 2))
    return dot(w1t, moves.astype(F32).astype(BF16))


def frame_copies(section, far, here, sems):
    lanes = pl.ds(pl.multiple_of(section[0] * LANES, LANES), LANES)
    size = 4 * STEP

    def copy(g):
        rows = pl.ds(pl.multiple_of(g * size, size), size)
        return pltpu.make_async_copy(far.at[rows, :, :, lanes], here.at[rows], sems.at[g])

    return copy


def tile_rows(frames, row, j, cols):
    img, _, channels, _ = frames.shape
    flat = frames.reshape(img, img * channels, LANES)
    size = cols * channels
    end = min((j + 1) * size, img * channels)
    part = flat[pl.ds(row, 4), j * size : end, :]
    return part.reshape(4 * (end - j * size), LANES)


def encode_kernel(
    section,
    frames_far,
    w1t,
    w2t,
    lw_far,
    table,
    h1_far,
    s1_far,
    s2_far,
    h2,
    enc,
    s3,
    frames,
    lw,
    h1,
    s1,
    s2,
    band,
    edge,
    band2,
    bias1,
    bias2,
    held,
    held2,
    sems,
):
    blocks, side = h1.shape[:2]
    steps = blocks // STEP
    tiles = frames.shape[1] // TILE
    k1, k2 = w1t.shape[0], w2t.shape[0]
    reach_rows = REACH * k1
    arrives = frame_copies(section, frames_far, frames, sems.at[0])
    for g in range(steps):
        arrives(g).start()
    last_copies = [
        pltpu.make_async_copy(lw_far, lw, sems.at[3, 0]),
        pltpu.make_async_copy(s2, s2_far, sems.at[3, 1]),
    ]
    last_copies[0].start()

    def leaves(g):
        rows = pl.ds(g * STEP, STEP)
        return [
            pltpu.make_async_copy(h1.at[rows], h1_far.at[rows], sems.at[1, g]),
            pltpu.make_async_copy(s1.at[rows], s1_far.at[rows], sems.at[2, g]),
        ]

    inner = side // 2 - 1
    row_len = inner * k2
    two = 2 * k2 * 3

    def prepare():
        taps = pixel_order(w1t[...])
        edges = []
        for half in range(2):
            lines = [taps[:, 32 * (4 * half + u) : 32 * (4 * half + u + 1)] for u in range(4)]
            for place in range(REACH):
                pieces = []
                for line in lines:
                    start = 16 * (place - 1)
                    cut = line[:, max(0, -start) : min(32, 64 - start)]
                    start = max(start, 0)
                    pieces += [jnp.zeros((k1, start), F32)] if start else []
                    pieces.append(cut)
                    rest = 64 - start - cut.shape[1]
                    pieces += [jnp.zeros((k1, rest), F32)] if rest else []
                at = half * reach_rows + place * k1
                band[at : at + k1, :] = jnp.concatenate(pieces, axis=1).astype(BF16)
            edges.append(jnp.concatenate([line[:, 16:] for line in lines], axis=1))
        edge[...] = jnp.concatenate(edges, axis=0).astype(BF16)
        tap, pix = iota((256, LANES), 0), iota((256, LANES), 1)
        for half in range(2):
            for place in range(3):
                hit = (
                    ((tap & 15) == (pix & 15))
                    & ((tap >> 6) == (pix >> 6) + 2 * half)
                    & (((tap >> 4) & 3) == ((pix >> 4) & 3) + 2 - 2 * place)
                )
                at = (half * 3 + place) * k2
                taps = dot(w2t[...], hit.astype(F32).astype(BF16))
                band2[at : at + k2, :] = taps.astype(BF16)
        bias1[...] = jnp.broadcast_to(column(table[AT_B1, 0:k1]), bias1.shape)
        bias2[...] = jnp.broadcast_to(column(table[AT_B2, 0:k2]), bias2.shape)
        held[...] = jnp.zeros_like(held)
        held2[...] = jnp.zeros_like(held2)
        h1[...] = jnp.zeros_like(h1)

    def added(sums, x, value):
        sums[x] = sums[x] + value if x in sums else value

    def second_rows(b):
        tiles = [
            h1[pl.ds(2 * b + 1, 2), 4 * j : 4 * j + 4].reshape(LANES, LANES)
            for j in range(side // 4)
        ]
        got = dot(band2[...], jnp.concatenate(tiles, axis=1))
        low, high = {}, {}
        for j in range(side // 4):
            for place in range(3):
                x = 2 * j - 1 + place
                if 0 <= x < inner:
                    span = slice(j * LANES, (j + 1) * LANES)
                    at = place * k2
                    added(low, x, got[at : at + k2, span])
                    added(high, x, got[two // 2 + at : two // 2 + at + k2, span])
        row = jnp.maximum(b - 1, 0) * row_len
        for x in range(inner):
            value, slope = soft(held2[x] + high[x] + bias2[...])
            held2[x] = low[x]
            at = pl.ds(pl.multiple_of(row + x * k2, k2), k2)
            h2[at, :] = value.astype(BF16)
            s2[at, :] = slope.astype(BF16)

    def one_step(g, carry):
        def row(r):
            return pl.multiple_of(4 * (STEP * g + r), 4)

        arrives(g).wait()
        second_rows(jnp.maximum(g - 1, 0))

        last = dot(
            edge[...], jnp.concatenate([tile_rows(frames, row(r), tiles, TILE) for r in range(STEP)], axis=1)
        )
        odd = {}
        for r in range(STEP):
            low, high = {}, {}

            def place_tile(j, got):
                for place in range(REACH):
                    x = 4 * j - 1 + place
                    if 0 <= x < side:
                        at = place * k1
                        added(low, x, got[at : at + k1])
                        added(high, x, got[reach_rows + at : reach_rows + at + k1])

            if r not in odd:
                rows = [k for k in (r, r + 1) if k < STEP]
                cut = [tile_rows(frames, row(k), tiles - 1, TILE) for k in rows]
                got = dot(band[...], jnp.concatenate(cut, axis=1))
                odd.update({k: got[:, i * LANES : (i + 1) * LANES] for i, k in enumerate(rows)})
            place_tile(tiles - 1, odd[r])
            added(low, side - 1, last[:k1, r * LANES : (r + 1) * LANES])
            added(high, side - 1, last[k1:, r * LANES : (r + 1) * LANES])
            done = 0
            for j in range(0, tiles - 1, 2):
                cut = [tile_rows(frames, row(r), j + k, TILE) for k in range(2)]
                got = dot(band[...], jnp.concatenate(cut, axis=1))
                for k in range(2):
                    place_tile(j + k, got[:, k * LANES : (k + 1) * LANES])
                ready = side if j + 2 == tiles - 1 else 4 * j + 7
                for x in range(done, ready):
                    value, slope = soft(held[x] + high[x] + bias1[...])
                    held[x] = low[x]
                    value = value.astype(BF16)
                    h1[STEP * g + r, x] = value
                    s1[STEP * g + r, x] = slope.astype(BF16)
                done = ready
        for copy in leaves(g):
            copy.start()
        return carry

    prepare()
    lax.fori_loop(0, steps, one_step, 0)
    for b in range(steps - 1, side // 2):
        second_rows(b)
    for copy in last_copies[1:]:
        copy.start()
    last_copies[0].wait()
    value, slope = soft(dot_rows(lw[...], h2[...]) + column(table[AT_LB, :]))
    enc[...] = value.astype(BF16)
    s3[...] = slope
    for g in range(steps):
        for copy in leaves(g):
            copy.wait()
    for copy in last_copies[1:]:
        copy.wait()


def three_parts(row):
    high = row.astype(BF16).astype(F32)
    middle = (row - high).astype(BF16).astype(F32)
    return jnp.concatenate([high, middle, row - high - middle], axis=0)


def with_ones(value):
    return jnp.concatenate([value, ones_rows(value.shape[1])], axis=0)


def ones_rows(lanes):
    return (iota((16, lanes), 0) < 3).astype(F32).astype(BF16)


def plan_kernel(
    section,
    slots,
    enc,
    s3,
    h2,
    branch_far,
    value_w,
    table,
    keep,
    send_one,
    send_two,
    small,
    g3,
    parts,
    bwt,
    vht,
    vhw,
    ow,
    mine,
    pre,
    dbr,
    dval,
    low,
    hid,
    gb,
    branch_w,
    sem,
    *,
    per_pair,
    depth,
):
    width = enc.shape[0]
    options = branch_w.shape[0]
    pairs = options // 2
    two = 2 * width
    sec = section[0]
    branch_copy = pltpu.make_async_copy(branch_far, branch_w, sem)
    branch_copy.start()

    count = slots.shape[0]
    dest = jnp.concatenate(
        [table[AT_DEST + k : AT_DEST + k + 1, :] for k in range(count // LANES)], axis=1
    )
    own = jnp.where(sec == 0, dest[:, :LANES], dest[:, LANES:])
    others = jnp.transpose(jnp.broadcast_to(dest, (LANES, count)))
    index = iota((count, LANES), 1) + sec * LANES
    earlier = (others == own) & (iota((count, LANES), 0) < index)
    rank = jnp.sum(earlier.astype(F32), axis=0, keepdims=True)
    bucket = own * float(per_pair) + rank
    chosen = (iota((count, LANES), 0).astype(F32) == bucket).astype(F32).astype(BF16)
    numbers = slots[...]
    high = numbers.astype(BF16)
    middle = (numbers - high.astype(F32)).astype(BF16)
    rest = (numbers - high.astype(F32) - middle.astype(F32)).astype(BF16)
    mine[...] = sum(dot_rows(v, chosen) for v in (rest, middle, high))[: mine.shape[0]]

    pad = jnp.zeros((13, width), F32)
    branch_copy.wait()
    for o in range(options):
        rows = [branch_w[o].astype(F32), three_parts(table[o : o + 1, :]), pad]
        bwt[o * width : (o + 1) * width, :] = jnp.transpose(
            jnp.concatenate(rows, axis=0)
        ).astype(BF16)
    scalars = table[AT_SCALARS, :]
    head_w = table[AT_HW, :]
    rows = [value_w[...].astype(F32), three_parts(table[AT_VB, :]), pad]
    vht[0:width, :] = jnp.transpose(jnp.concatenate(rows, axis=0)).astype(BF16)
    vht[width:, :] = jnp.zeros((16, width + 16), BF16)
    lane = iota((1, 16), 1)
    for k in range(2):
        bias = three_parts(jnp.broadcast_to(scalars[:, 1 + k : 2 + k], (1, 16)))
        bias = sum(jnp.where(lane == j, bias[j : j + 1], 0.0) for j in range(3))
        vht[width + k : width + k + 1, 0:width] = head_w[k : k + 1].astype(BF16)
        vht[width + k : width + k + 1, width:] = bias.astype(BF16)
    vhw[:, 0:width] = value_w[...]
    vhw[:, width:] = jnp.transpose(
        jnp.concatenate([head_w, jnp.zeros((14, width), F32)], axis=0)
    ).astype(BF16)
    ow[...] = jnp.broadcast_to(column(table[AT_OW, :]), (width, LANES))
    wide_ow = jnp.concatenate([ow[...], ow[...]], axis=1)

    labels = iota((options, LANES), 0).astype(F32)
    state = enc[...].astype(F32)
    rounded_all, saved = [], []
    for level in range(depth):
        picked = labels == mine[level : level + 1, :]
        rounded = state.astype(BF16)
        rounded_all.append(rounded)
        pre[...] = dot(bwt[...], with_ones(rounded))
        following = state
        reward, discount, value = [], [], []
        for t in range(pairs):
            at = slice(t * two, (t + 1) * two)
            act, slope = silu_pair(pre[at, :])
            dbr[level, at, :] = slope
            left = state + act[:width]
            right = state + act[width:]
            following = jnp.where(picked[2 * t : 2 * t + 1], left, following)
            following = jnp.where(picked[2 * t + 1 : 2 * t + 2], right, following)
            both = with_ones(jnp.concatenate([left.astype(BF16), right.astype(BF16)], axis=1))
            low[level, t] = both
            got = dot(vht[...], both)
            act, slope = silu_pair(got[:width])
            dval[level, t] = slope
            hidden = act.astype(BF16)
            hid[level, t] = hidden
            worth = jnp.sum(hidden.astype(F32) * wide_ow, axis=0, keepdims=True)
            for k in range(2):
                span = slice(k * LANES, (k + 1) * LANES)
                value.append(worth[:, span])
                reward.append(got[width : width + 1, span])
                discount.append(got[width + 1 : width + 2, span])
        reward = jnp.concatenate(reward, axis=0)
        discount = jax.nn.sigmoid(jnp.concatenate(discount, axis=0))
        value = jnp.concatenate(value, axis=0) + scalars[:, 3:4]
        quality = reward + discount * value
        top = jnp.max(quality, axis=0, keepdims=True)
        shifted = jnp.exp(quality - top)
        total = jnp.sum(shifted, axis=0, keepdims=True)
        live = (mine[depth : depth + 1, :] > level).astype(F32)
        chosen = picked.astype(F32)

        def target(kind):
            at = depth + 1 + kind * depth + level
            return mine[at : at + 1, :]

        reward_gap = live * (jnp.sum(chosen * reward, axis=0, keepdims=True) - target(0))
        discount_gap = live * (jnp.sum(chosen * discount, axis=0, keepdims=True) - target(1))
        plan_gap = live * (top + jnp.log(total) - target(2))
        grad_quality = plan_gap * (shifted / total)
        head_two = (chosen * discount_gap + grad_quality * value) * discount * (1.0 - discount)
        saved.append(
            (
                picked,
                (chosen * reward_gap + grad_quality).astype(BF16).astype(F32),
                head_two.astype(BF16).astype(F32),
                (grad_quality * discount).astype(BF16).astype(F32),
                reward_gap * reward_gap + discount_gap * discount_gap + plan_gap * plan_gap,
            )
        )
        state = following

    out_sum = jnp.zeros((width, two), F32)
    value_sum = jnp.zeros((width + 16, width + 16), F32)
    grad_next = jnp.zeros((width, LANES), F32)
    line = iota((16, two), 0)
    for level in reversed(range(depth)):
        picked, head_one, head_two, grad_value, _ = saved[level]
        upward = jnp.zeros((width, LANES), F32)
        for t in range(pairs):
            at = slice(t * two, (t + 1) * two)

            def across(rows):
                return jnp.concatenate(
                    [rows[2 * t : 2 * t + 1], rows[2 * t + 1 : 2 * t + 2]], axis=1
                )

            worth = across(grad_value)
            grad_pre = (worth * wide_ow * dval[level, t]).astype(BF16)
            out_sum = out_sum + hid[level, t].astype(F32) * worth
            heads = jnp.where(line == 0, across(head_one), 0.0)
            heads = jnp.where(line == 1, across(head_two), heads)
            heads = jnp.where(line == 2, worth, heads)
            stacked = jnp.concatenate([grad_pre, heads.astype(BF16)], axis=0)
            value_sum = value_sum + dot_lanes(stacked, low[level, t])
            moved = dot(vhw[...], stacked)
            left = moved[:, :LANES] + jnp.where(picked[2 * t : 2 * t + 1], grad_next, 0.0)
            right = moved[:, LANES:] + jnp.where(picked[2 * t + 1 : 2 * t + 2], grad_next, 0.0)
            grad_branch = jnp.concatenate([left, right], axis=0) * dbr[level, at, :]
            grad_branch = grad_branch.astype(BF16)
            gb[level, at, :] = grad_branch
            weights = jnp.concatenate([branch_w[2 * t], branch_w[2 * t + 1]], axis=1)
            upward = upward + (left + right + dot(weights, grad_branch))
        grad_next = upward

    linear_rows = h2.shape[0]
    half = (linear_rows + options * width + width) // 2
    rest = linear_rows - half
    rounded = with_ones(jnp.concatenate(rounded_all, axis=1))
    small[...] = jnp.zeros_like(small)
    if half < keep.shape[0]:
        for k in range(2):
            parts[k, half:, :] = jnp.zeros((keep.shape[0] - half, LANES), BF16)
    for t in range(pairs):
        at = slice(t * two, (t + 1) * two)
        grads = jnp.concatenate([gb[level, at, :] for level in range(depth)], axis=1)
        got = dot_lanes(rounded, grads)
        for k in range(2):
            o = 2 * t + k
            span = slice(k * width, (k + 1) * width)
            rows = slice(rest + o * width, rest + (o + 1) * width)
            parts[1 - sec, rows, :] = got[:width, span].astype(BF16)
            small[o : o + 1, :] = got[width : width + 1, span]
    after = rest + options * width
    parts[1 - sec, after : after + width, :] = jnp.transpose(value_sum[:width, :width]).astype(BF16)

    grad_three = (grad_next.astype(BF16).astype(F32) * s3[...]).astype(BF16)
    g3[...] = grad_three
    chunk = linear_rows // 9
    for i in range(8):
        at = slice(i * chunk, (i + 1) * chunk)
        parts[sec, at, :] = dot_lanes(h2[at, :], grad_three).astype(BF16)
    last = dot_lanes(h2[8 * chunk :, :], grad_three).astype(BF16)
    parts[sec, 8 * chunk : half, :] = last[: half - 8 * chunk]
    parts[1 - sec, 0:rest, :] = last[half - 8 * chunk :]
    keep[...] = parts[0]
    send_one[...] = parts[1, : send_one.shape[0]]
    send_two[...] = parts[1, send_one.shape[0] :]

    small[AT_VB, :] = row_of(value_sum[:width, width : width + 1])
    small[AT_OW, :] = row_of(jnp.sum(out_sum, axis=1, keepdims=True))
    small[AT_HW, :] = value_sum[width : width + 2, :width]
    small[AT_LB, :] = row_of(jnp.sum(grad_three.astype(F32), axis=1, keepdims=True))
    loss = 0.5 * jnp.sum(sum(kept[4] for kept in saved), axis=1, keepdims=True)
    ends = [loss] + [value_sum[width + k : width + k + 1, width : width + 1] for k in range(3)]
    lane = iota((1, LANES), 1)
    line = jnp.zeros((1, LANES), F32)
    for k, end in enumerate(ends):
        line = jnp.where(lane == k, end, line)
    small[AT_SCALARS, :] = line


def back_kernel(g3, lw, s2, s1, h1, w2t, g1, c2, sums, t2, g2):
    side, k1 = s1.shape[1], s1.shape[2]
    k2 = w2t.shape[0]
    inner = side // 2 - 1
    row_len = inner * k2
    tap, pix = iota((LANES, 256), 1), iota((LANES, 256), 0)
    for yrel in range(2):
        for p in range(3):
            hit = (
                ((tap & 15) == (pix & 15))
                & ((tap >> 6) == (pix >> 6) + 2 * (1 - yrel))
                & (((tap >> 4) & 3) == ((pix >> 4) & 3) + 2 - 2 * p)
            )
            at = (yrel * 3 + p) * k2
            t2[:, at : at + k2] = dot_lanes(hit.astype(F32).astype(BF16), w2t[...]).astype(BF16)
    g2[0] = jnp.zeros(g2.shape[1:], BF16)
    g2[inner + 1] = jnp.zeros(g2.shape[1:], BF16)
    g1[0] = jnp.zeros(g1.shape[1:], BF16)
    g1[side + 1] = jnp.zeros(g1.shape[1:], BF16)
    zero = jnp.zeros((k2, LANES), BF16)
    total_one = jnp.zeros((k1, LANES), F32)
    total_two = jnp.zeros((k2, LANES), F32)
    for y in range(inner):
        at = slice(y * row_len, (y + 1) * row_len)
        grad = dot(lw[at, :], g3[...]) * s2[at, :].astype(F32)
        grad = grad.astype(BF16).reshape(inner, k2, LANES)
        g2[y + 1] = grad
        total_two = total_two + jnp.sum(grad.astype(F32), axis=0)
    reach, cols = 5, 8
    total = jnp.zeros((2 * reach * k2, 2 * cols * k1), F32)
    grads, tiles = [], []
    for b in range(side // 2):
        cut = []
        for j in range(side // 4):
            pieces = []
            for yrel in range(2):
                for p in range(3):
                    x = 2 * j - 1 + p
                    pieces.append(g2[b + yrel, x] if 0 <= x < inner else zero)
            cut.append(jnp.concatenate(pieces, axis=0))
        got = dot(t2[...], jnp.concatenate(cut, axis=1))
        for u in range(2):
            for j in range(side // 4):
                part = got[u * 64 : (u + 1) * 64, j * LANES : (j + 1) * LANES]
                slope = s1[2 * b + u + 1, 4 * j : 4 * j + 4].astype(F32)
                grad = (part.reshape(4, k1, LANES) * slope).astype(BF16)
                g1[2 * b + u + 1, 4 * j : 4 * j + 4] = grad
                total_one = total_one + jnp.sum(grad.astype(F32), axis=0)
        for j in range(-(-side // cols)):
            end = min((j + 1) * cols, side)
            tile = h1[2 * b + 1 : 2 * b + 3, j * cols : end]
            if end < (j + 1) * cols:
                rest = jnp.zeros((2, (j + 1) * cols - end, k1, LANES), BF16)
                tile = jnp.concatenate([tile, rest], axis=1)
            tiles.append(tile.reshape(2 * cols * k1, LANES))
            pieces = []
            for half in range(2):
                for p in range(reach):
                    x = 4 * j - 1 + p
                    pieces.append(g2[b + 1 - half, x] if 0 <= x < inner else zero)
            grads.append(jnp.concatenate(pieces, axis=0))
        if b % 2:
            total = total + dot_lanes(
                jnp.concatenate(grads, axis=1), jnp.concatenate(tiles, axis=1)
            )
            grads, tiles = [], []
    line = 4 * k1
    for half in range(2):
        for u in range(2):
            tap_row = jnp.zeros((k2, line), F32)
            for p in range(reach):
                at = (half * reach + p) * k2
                part = total[at : at + k2, u * 2 * line : (u + 1) * 2 * line]
                start = 2 * k1 * (p - 1)
                piece = part[:, max(start, 0) : min(start + line, 2 * line)]
                if start < 0:
                    piece = jnp.concatenate([jnp.zeros((k2, -start), F32), piece], axis=1)
                if start + line > 2 * line:
                    rest = jnp.zeros((k2, start - line), F32)
                    piece = jnp.concatenate([piece, rest], axis=1)
                tap_row = tap_row + piece
            at = (2 * half + u) * line
            c2[:, at : at + line] = tap_row
    sums[...] = jnp.zeros_like(sums)
    sums[0:1, 0:k1] = row_of(jnp.sum(total_one, axis=1, keepdims=True))
    sums[1:2, 0:k2] = row_of(jnp.sum(total_two, axis=1, keepdims=True))


def pixel_band(sec, w1t, channels):
    k1 = w1t.shape[0]
    rows = 64 * channels
    row, tap = iota((rows, 256), 0), iota((rows, 256), 1)
    moves = ((tap >> 6) == row % channels + sec * channels) & ((tap & 63) == row // channels)
    taps = dot_lanes(moves.astype(F32).astype(BF16), w1t)
    line, span = COLS * channels, 8 * channels
    blocks = {}
    for half in range(2):
        for p in range(NEAR):
            pieces = []
            for u in range(4):
                at = (4 * half + u) * span
                start = 4 * (p - 1) * channels
                cut = taps[at + max(0, -start) : at + min(span, line - start)]
                start = max(start, 0)
                pieces += [jnp.zeros((start, k1), F32)] if start else []
                pieces.append(cut)
                rest = line - start - cut.shape[0]
                pieces += [jnp.zeros((rest, k1), F32)] if rest else []
            blocks[half, p] = jnp.concatenate(pieces, axis=0)
    zero = jnp.zeros((4 * line, k1), F32)
    lines = []
    for r in range(STEP):
        cols = [
            blocks.get((r + 1 - yrel, p), zero) for yrel in range(STEP + 1) for p in range(NEAR)
        ]
        lines.append(jnp.concatenate(cols, axis=1))
    return jnp.concatenate(lines, axis=0).astype(BF16)


def first_kernel(
    section,
    frames_far,
    g1,
    w1t,
    other_far,
    after,
    c1,
    out,
    band,
    frames,
    acc,
    other,
    held,
    sems,
    draw_sems,
    *,
    draw,
):
    side, k1 = g1.shape[1], g1.shape[2]
    img, _, channels, _ = frames.shape
    steps = img // 4 // STEP
    arrives = frame_copies(section, frames_far, frames, sems)
    for g in range(steps):
        arrives(g).start()
    other_copy = pltpu.make_async_copy(
        other_far.at[0 : STEP * draw + 1], other, sems.at[steps]
    )
    other_copy.start()
    acc[...] = jnp.zeros_like(acc)
    zero = jnp.zeros((k1, LANES), BF16)

    def one_step(g, carry):
        arrives(g).wait()
        pixels, grads = [], []
        for j in range(img // COLS):
            rows = [pl.multiple_of(4 * (STEP * g + r), 4) for r in range(STEP)]
            pixels.append(
                jnp.concatenate([tile_rows(frames, row, j, COLS) for row in rows], axis=0)
            )
            pieces = []
            for yrel in range(STEP + 1):
                for p in range(NEAR):
                    x = 3 * j - 1 + p
                    pieces.append(g1[STEP * g + yrel, x] if 0 <= x < side else zero)
            grads.append(jnp.concatenate(pieces, axis=0))
        acc[...] += dot_lanes(jnp.concatenate(pixels, axis=1), jnp.concatenate(grads, axis=1))
        return carry

    lax.fori_loop(0, steps, one_step, 0)
    band[...] = pixel_band(section[0], w1t[...], out.shape[2])
    other_copy.wait()
    finish = draw_steps(section, band, g1, 0, other, 0, out, held, draw_sems, 0, draw)
    fold_first(acc, c1, channels, k1)
    finish()


def fold_first(acc, c1, channels, k1):
    line = COLS * channels
    step = 4 * channels
    taps = []
    for half in range(2):
        total = sum(
            acc[r * 4 * line : (r + 1) * 4 * line, :][
                :, (r + 1 - half) * NEAR * k1 : (r + 2 - half) * NEAR * k1
            ]
            for r in range(STEP)
        )
        for u in range(4):
            part = total[u * line : (u + 1) * line]
            cols = [part[:, p * k1 : (p + 1) * k1] for p in range(NEAR)]
            taps.append(cols[1][0:step] + cols[2][step : 2 * step] + cols[3][2 * step :])
            taps.append(cols[0][0:step] + cols[1][step : 2 * step] + cols[2][2 * step :])
    row, col = iota((256, 256), 0), iota((256, 256), 1)
    moves = ((row & 3) == (col >> 6)) & ((row >> 2) == (col & 63))
    grad = dot_rows(jnp.concatenate(taps, axis=0), moves.astype(F32), EXACT)
    for half in range(2):
        c1[half * k1 : (half + 1) * k1, :] = grad[:, half * LANES : (half + 1) * LANES].astype(BF16)


def draw_steps(section, band, mine, mine_at, other, other_at, out, held, sems, start, steps):
    side, k1 = mine.shape[1], mine.shape[2]
    img, channels = out.shape[1], out.shape[2]
    sec = section[0]
    line = COLS * channels
    flat = held.reshape(2, 2, 4 * STEP, img * channels, LANES)

    def writes(g):
        rows = slice(4 * STEP * (start + g), 4 * STEP * (start + g + 1))
        places = (sec * LANES, (1 - sec) * LANES)
        return [
            pltpu.make_async_copy(
                held.at[g % 2, k],
                out.at[rows, :, :, pl.ds(pl.multiple_of(places[k], LANES), LANES)],
                sems.at[g % 2, k],
            )
            for k in range(2)
        ]

    zero = jnp.zeros((k1, 2 * LANES), BF16)
    for g in range(steps):
        if g >= 2:
            for copy in writes(g - 2):
                copy.wait()
        for j in range(img // COLS):
            pieces = []
            for yrel in range(STEP + 1):
                for p in range(NEAR):
                    x, y = 3 * j - 1 + p, STEP * (start + g) + yrel
                    if 0 <= x < side:
                        pair = [mine[y - mine_at, x], other[y - other_at, x]]
                        pieces.append(jnp.concatenate(pair, axis=1))
                    else:
                        pieces.append(zero)
            got = dot(band[...], jnp.concatenate(pieces, axis=0))
            for k in range(4 * STEP):
                at = slice(k * line, (k + 1) * line)
                span = slice(j * line, (j + 1) * line)
                flat[g % 2, 0, k, span, :] = got[at, :LANES]
                flat[g % 2, 1, k, span, :] = got[at, LANES:]
        for copy in writes(g):
            copy.start()

    def finish():
        for g in range(max(steps - 2, 0), steps):
            for copy in writes(g):
                copy.wait()

    return finish


def pixels_kernel(section, band, mine, other_far, after, done, out, token, held, other, sems, *, start):
    steps = other.shape[0] // STEP
    fetch = pltpu.make_async_copy(
        other_far.at[STEP * start : STEP * (start + steps) + 1], other, sems.at[2, 0]
    )
    fetch.start()
    token[...] = jnp.zeros_like(token)
    fetch.wait()
    draw_steps(
        section, band, mine, 0, other, STEP * start, out, held, sems, start, steps
    )()


def two_parts(value):
    high = value.astype(BF16).astype(F32)
    return jnp.concatenate([high, value - high], axis=0).astype(BF16)


def one_part(pair):
    rows = pair.shape[0] // 2
    pair = pair.astype(F32)
    return pair[:rows] + pair[rows:]


def merge_kernel(keep, recv_one, recv_two, small, c2, sums, out_far, lines, out, sems):
    members = out.shape[0]
    size = keep.shape[0] // members
    k2 = c2.shape[0]
    lines[...] = jnp.zeros_like(lines)
    at = small.shape[0]
    lines[0:at, :] = small[...]
    for half in range(2):
        lines[at : at + k2, :] = c2[:, half * LANES : (half + 1) * LANES]
        at += k2
    lines[at : at + sums.shape[0], :] = sums[...]
    for k in range(members):
        at = slice(k * size, (k + 1) * size)
        recv, here = recv_one, k
        if k >= members // 2:
            recv, here = recv_two, k - members // 2
        got = recv[here * size : (here + 1) * size, :]
        out[k, 0:size, :] = (keep[at, :].astype(F32) + got.astype(F32)).astype(BF16)
        out[k, size:, :] = two_parts(lines[k * SHORT : (k + 1) * SHORT, :])
        pltpu.make_async_copy(out.at[k], out_far.at[k], sems.at[k]).start()
    for k in range(members):
        pltpu.make_async_copy(out.at[k], out_far.at[k], sems.at[k]).wait()


def cube_kernel(got, c1, out):
    members = got.shape[0]
    size = got.shape[1] - 2 * SHORT
    out[0:size, :] = sum(got[k, 0:size, :].astype(F32) for k in range(members)).astype(BF16)
    total = sum(one_part(got[k, size:, :]) for k in range(members))
    out[size : size + 2 * SHORT, :] = two_parts(total)
    out[size + 2 * SHORT :, :] = c1[...]


def add_kernel(a, b, after, out):
    size = a.shape[0] - 2 * SHORT - 32
    middle = slice(size, size + 2 * SHORT)
    for span in (slice(0, size), slice(size + 2 * SHORT, a.shape[0])):
        out[span, :] = (a[span, :].astype(F32) + b[span, :].astype(F32)).astype(BF16)
    out[middle, :] = two_parts(one_part(a[middle, :]) + one_part(b[middle, :]))


def relay_kernel(batch, *refs):
    parts, (one, two, out) = refs[:CUBE], refs[CUBE:]
    me = batch[0] % CUBE
    for k, part in enumerate(parts):
        out[me ^ k] = part[...]
    one[...] = out[: CUBE // 2]
    two[...] = out[CUBE // 2 :]


def piece_of(got, k):
    count = got[0].shape[0]
    return got[k // count].at[k % count]


def unpack_half(which, got, lw, bw, vw, stage, stage_b, sems):
    members = 2 * got[0].shape[0]
    size = stage.shape[0] // members
    linear_rows, width = lw.shape
    options = bw.shape[0]
    half = (linear_rows + options * width + width) // 2
    rest = linear_rows - half

    @pl.when(which == 0)
    def _():
        copies = []
        for k in range(members):
            start, end = k * size, min((k + 1) * size, half)
            stage[start:end, :] = piece_of(got, k)[0 : end - start, :].astype(F32)
            copies.append(
                pltpu.make_async_copy(stage.at[start:end], lw.at[start:end], sems.at[k])
            )
            copies[-1].start()
        for copy in copies:
            copy.wait()

    @pl.when(which == 1)
    def _():
        def rows(start, end):
            parts = []
            while start < end:
                k, at = start // size, start % size
                count = min(size - at, end - start)
                parts.append(piece_of(got, k)[at : at + count, :])
                start += count
            value = parts[0] if len(parts) == 1 else jnp.concatenate(parts, axis=0)
            return value.astype(F32)

        stage[0:rest, :] = rows(0, rest)
        copies = [pltpu.make_async_copy(stage.at[0:rest], lw.at[half:], sems.at[0])]
        copies[0].start()
        group = options // 3
        for o in range(options):
            stage_b[o] = rows(rest + o * width, rest + (o + 1) * width)
            if o % group == group - 1:
                part = slice(o + 1 - group, o + 1)
                copy = pltpu.make_async_copy(
                    stage_b.at[part], bw.at[part], sems.at[1 + o // group]
                )
                copy.start()
                copies.append(copy)
        at = rest + options * width
        stage[rest : rest + width, :] = rows(at, at + width)
        copies.append(
            pltpu.make_async_copy(stage.at[rest : rest + width], vw, sems.at[1 + options // group])
        )
        copies[-1].start()
        for copy in copies:
            copy.wait()


def own_kernel(section, one, two, lw, bw, vw, stage, stage_b, sems):
    unpack_half(section[0], (one, two), lw, bw, vw, stage, stage_b, sems)


def unpack_kernel(section, *refs):
    mine, other, refs = refs[0:2], refs[2:4], refs[4:]
    lw, bw, vw = refs[3:6]
    little = (len(refs) - 10) // 2
    far, near = refs[6 : 6 + little], refs[6 + little : 6 + 2 * little]
    loss, c1, b1, c2, b2, lb, bb, hw, hb, vb, ow, ob = near
    stage, stage_b, lines, sems = refs[-4:]
    options = bw.shape[0]
    k1, k2 = c1.shape[0], c2.shape[0]
    size = stage.shape[0] // CUBE
    grad = [jnp.zeros((k1, LANES), F32) for _ in range(2)]
    for k in range(CUBE):
        pair = slice(size, size + 2 * SHORT)
        at = slice(k * SHORT, (k + 1) * SHORT)
        views = piece_of(mine, k), piece_of(other, k)
        lines[at, :] = sum(one_part(v[pair, :]) for v in views)
        for view in views:
            for h in range(2):
                at = size + 2 * SHORT + h * k1
                grad[h] += view[at : at + k1, :].astype(F32)
    for part in range(2):
        c1[:, part * LANES : (part + 1) * LANES] = grad[part]
    bb[...] = lines[0:options, :]
    vb[...] = lines[AT_VB, :]
    ow[...] = lines[AT_OW, :]
    hw[...] = lines[AT_HW, :]
    lb[...] = lines[AT_LB, :]
    scalars = lines[AT_SCALARS, :]
    loss[...] = scalars[:, 0:1]
    hb[...] = scalars[:, 1:3]
    ob[...] = scalars[:, 3:4]
    at = TABLE
    for part in range(2):
        c2[:, part * LANES : (part + 1) * LANES] = lines[at : at + k2, :]
        at += k2
    b1[...] = lines[at : at + 1, 0:k1]
    b2[...] = lines[at + 1 : at + 2, 0:k2]
    copies = [
        pltpu.make_async_copy(a, b, sems.at[CUBE + k]) for k, (a, b) in enumerate(zip(near, far))
    ]
    for copy in copies:
        copy.start()
    unpack_half(1 - section[0], other, lw, bw, vw, stage, stage_b, sems)
    for copy in copies:
        copy.wait()


def numbers_kernel(
    options,
    depth,
    targets,
    destination,
    b1,
    b2,
    lb,
    bb,
    hw,
    vb,
    ow,
    hb,
    ob,
    out,
    table,
):
    levels, kinds = options.shape[0], targets.shape[0]
    slots = depth.shape[1]
    rows = [options[...].astype(F32), depth[...].astype(F32)]
    rows += [targets[k] for k in range(kinds)]
    rows.append(jnp.zeros((LANES - levels - 1 - kinds * levels, slots), F32))
    out[...] = jnp.transpose(jnp.concatenate(rows, axis=0))
    table[...] = jnp.zeros_like(table)
    table[0 : bb.shape[0], :] = bb[...]
    table[AT_VB, :] = vb[...]
    table[AT_OW, :] = ow[...].astype(F32)
    table[AT_HW, :] = hw[...].astype(F32)
    table[AT_LB, :] = lb[...]
    table[AT_B1, 0 : b1.shape[1]] = b1[...]
    table[AT_B2, 0 : b2.shape[1]] = b2[...]
    lane = iota((1, LANES), 1)
    scalars = jnp.zeros((1, LANES), F32)
    for k, value in ((1, hb[:, 0:1]), (2, hb[:, 1:2]), (3, ob[...])):
        scalars = jnp.where(lane == k, value, scalars)
    table[AT_SCALARS, :] = scalars
    for k in range(slots // LANES):
        part = destination[:, k * LANES : (k + 1) * LANES]
        table[AT_DEST + k : AT_DEST + k + 1, :] = part.astype(F32)


def whole(shape):
    zeros = (0,) * len(shape)
    return pl.BlockSpec(shape, lambda *_: zeros)


ANYWHERE = pl.BlockSpec(memory_space=pl.ANY)
SCALARS = pl.BlockSpec(memory_space=pltpu.SMEM)


def params():
    return pltpu.CompilerParams(vmem_limit_bytes=VMEM_BYTES)


def shape_of(*shape, dtype=F32):
    return jax.ShapeDtypeStruct(shape, dtype)


def cost(microseconds):
    return pl.CostEstimate(
        flops=int(1.1e9 * microseconds), bytes_accessed=int(3.6e6 * microseconds), transcendentals=0
    )


def stays(value):
    return pltpu.with_memory_space_constraint(value, pltpu.HBM)


def held_near(value):
    return pltpu.with_memory_space_constraint(value, pltpu.VMEM)


def encode(section, frames, w1t, w2t, lw, table):
    img = frames.shape[0]
    blocks = img // 4
    side = blocks - 1
    k1, k2, width = w1t.shape[0], w2t.shape[0], lw.shape[1]
    flat = lw.shape[0]
    vmem = pltpu.VMEM
    near = pl.BlockSpec(memory_space=vmem)
    grid_one = (blocks, side, k1, LANES)
    return pl.pallas_call(
        encode_kernel,
        in_specs=[SCALARS, ANYWHERE, near, near, ANYWHERE, near],
        out_specs=[ANYWHERE] * 3 + [near] * 3,
        out_shape=(
            pltpu.HBM(grid_one, BF16),
            pltpu.HBM(grid_one, BF16),
            pltpu.HBM((flat, LANES), BF16),
            shape_of(flat, LANES, dtype=BF16),
            shape_of(width, LANES, dtype=BF16),
            shape_of(width, LANES),
        ),
        scratch_shapes=[
            vmem((img, img, frames.shape[2], LANES), BF16),
            vmem(lw.shape, BF16),
            vmem(grid_one, BF16),
            vmem(grid_one, BF16),
            vmem((flat, LANES), BF16),
            vmem((2 * REACH * k1, 256), BF16),
            vmem((2 * k1, 64), BF16),
            vmem((6 * k2, LANES), BF16),
            vmem((k1, LANES), F32),
            vmem((k2, LANES), F32),
            vmem((side, k1, LANES), F32),
            vmem((side // 2 - 1, k2, LANES), F32),
            pltpu.SemaphoreType.DMA((4, max(blocks // STEP, 3))),
        ],
        compiler_params=params(),
        cost_estimate=cost(9),
        name="encode",
    )(section, frames, w1t, w2t, lw, table)


def plan(section, slots, enc, s3, h2, branch_w, value_w, table, per_pair, depth, half_rows):
    width = enc.shape[0]
    options = branch_w.shape[0]
    two = 2 * width
    pairs = options // 2
    outs = (
        shape_of(half_rows, LANES, dtype=BF16),
        shape_of(half_rows // 2, LANES, dtype=BF16),
        shape_of(half_rows // 2, LANES, dtype=BF16),
        shape_of(TABLE, LANES),
        shape_of(width, LANES, dtype=BF16),
    )
    vmem = pltpu.VMEM
    near = pl.BlockSpec(memory_space=vmem)
    return pl.pallas_call(
        functools.partial(plan_kernel, per_pair=per_pair, depth=depth),
        in_specs=[SCALARS, near, near, near, near, ANYWHERE, near, near],
        out_shape=outs,
        scratch_shapes=[
            vmem((2, half_rows, LANES), BF16),
            vmem((options * width, width + 16), BF16),
            vmem((width + 16, width + 16), BF16),
            vmem((width, width + 16), BF16),
            vmem((width, LANES), F32),
            vmem((16, LANES), F32),
            vmem((options * width, LANES), F32),
            vmem((depth, options * width, LANES), F32),
            vmem((depth, pairs, width, two), F32),
            vmem((depth, pairs, width + 16, two), BF16),
            vmem((depth, pairs, width, two), BF16),
            vmem((depth, options * width, LANES), BF16),
            vmem(branch_w.shape, BF16),
            pltpu.SemaphoreType.DMA,
        ],
        compiler_params=params(),
        cost_estimate=cost(11),
        name="plan",
    )(section, slots, enc, s3, h2, branch_w, value_w, table)


def back(g3, lw, s2, s1, h1, w2t):
    _, side, k1 = s1.shape[:3]
    k2 = w2t.shape[0]
    inner = side // 2 - 1
    padded = (side + 2, side, k1, LANES)
    near = pl.BlockSpec(memory_space=pltpu.VMEM)
    return pl.pallas_call(
        back_kernel,
        in_specs=[near] * 6,
        out_shape=(shape_of(*padded, dtype=BF16), shape_of(k2, 256), shape_of(8, LANES)),
        scratch_shapes=[
            pltpu.VMEM((LANES, 6 * k2), BF16),
            pltpu.VMEM((inner + 2, inner, k2, LANES), BF16),
        ],
        compiler_params=params(),
        cost_estimate=cost(25),
        name="back",
    )(g3, lw, s2, s1, h1, w2t)


def first(section, frames, g1, w1t, other, after, channels, draw):
    img, _, stack, _ = frames.shape
    k1 = g1.shape[2]
    band = (STEP * 4 * COLS * channels, (STEP + 1) * NEAR * k1)
    near = pl.BlockSpec(memory_space=pltpu.VMEM)
    return pl.pallas_call(
        functools.partial(first_kernel, draw=draw),
        in_specs=[SCALARS, ANYWHERE, near, near, ANYWHERE, ANYWHERE],
        out_specs=[near, ANYWHERE, near],
        out_shape=[
            shape_of(2 * k1, LANES, dtype=BF16),
            shape_of(img, img, channels, 2 * LANES),
            shape_of(*band, dtype=BF16),
        ],
        scratch_shapes=[
            pltpu.VMEM((img, img, stack, LANES), BF16),
            pltpu.VMEM((STEP * 4 * COLS * stack, (STEP + 1) * NEAR * k1), F32),
            pltpu.VMEM((STEP * draw + 1,) + g1.shape[1:], BF16),
            pltpu.VMEM((2, 2, 4 * STEP, img, channels, LANES), F32),
            pltpu.SemaphoreType.DMA((img // 4 // STEP + 1,)),
            pltpu.SemaphoreType.DMA((2, 2)),
        ],
        compiler_params=params(),
        cost_estimate=cost(45),
        name="first",
    )(section, frames, g1, w1t, other, after)


def pixels(section, band, mine, other, after, done, start):
    img, _, channels, _ = done.shape
    steps = img // 4 // STEP - start
    near = pl.BlockSpec(memory_space=pltpu.VMEM)
    return pl.pallas_call(
        functools.partial(pixels_kernel, start=start),
        in_specs=[SCALARS, near, near, ANYWHERE, ANYWHERE, ANYWHERE],
        out_specs=[ANYWHERE, near],
        out_shape=[shape_of(*done.shape), shape_of(8, LANES)],
        scratch_shapes=[
            pltpu.VMEM((2, 2, 4 * STEP, img, channels, LANES), F32),
            pltpu.VMEM((STEP * steps + 1,) + mine.shape[1:], BF16),
            pltpu.SemaphoreType.DMA((3, 2)),
        ],
        input_output_aliases={5: 0},
        compiler_params=params(),
        cost_estimate=cost(1 + 0.9 * steps),
        name="pixels",
    )(section, band, mine, other, after, done)


def small_call(
    kernel, outs, operands, scratch=(), name=None, place=None, after=(), weight=0.3, far=False
):
    specs = [pl.BlockSpec(memory_space=pltpu.VMEM)] * len(operands)
    if place is not None:
        operands = (*place, *operands)
        specs = [pl.BlockSpec(memory_space=pltpu.SMEM)] * len(place) + specs
    return pl.pallas_call(
        kernel,
        in_specs=specs + [ANYWHERE] * len(after),
        out_specs=jax.tree.map(
            lambda _: ANYWHERE if far else pl.BlockSpec(memory_space=pltpu.VMEM), outs
        ),
        out_shape=outs,
        scratch_shapes=list(scratch),
        compiler_params=params(),
        cost_estimate=cost(weight),
        name=name,
    )(*operands, *after)


def round_up(value, step):
    return -(-value // step) * step


def swapped(value):
    return lax.ppermute(value, "section", [(0, 1), (1, 0)])


def exchanged(value, groups=None):
    return lax.all_to_all(
        value, "batch", split_axis=0, concat_axis=0, axis_index_groups=groups, tiled=True
    )


def partner(value, distance):
    count = lax.axis_size("batch")
    return lax.ppermute(value, "batch", [(b, b ^ distance) for b in range(count)])


def local(
    frames,
    destination,
    options,
    depth,
    targets,
    conv_one,
    bias_one,
    conv_two,
    bias_two,
    linear_w,
    linear_b,
    branch_w,
    branch_b,
    head_w,
    head_b,
    value_w,
    value_b,
    out_w,
    out_b,
):
    section = lax.axis_index("section").astype(jnp.int32)[None]
    peers = lax.axis_size("batch")
    frame_count = frames.shape[3]
    per_pair = frame_count // peers
    levels = options.shape[0]
    frames = stays(frames.transpose(1, 2, 0, 3))
    w1t, w2t = stays(conv_one.T), stays(conv_two.T)
    branch_w, value_w = stays(branch_w), stays(value_w)
    encoder_params = (w1t, bias_one, w2t, bias_two, linear_w, linear_b)
    planner_params = (branch_w, branch_b, head_w.T, head_b, value_w, value_b, out_w.T, out_b)
    width = linear_w.shape[1]
    big_rows = linear_w.shape[0] + (branch_w.shape[0] + 1) * width
    size = round_up(-(-big_rows // (2 * CUBE)), 16)

    tiny = (bias_one, bias_two, linear_b, branch_b, head_w.T, value_b, out_w.T)
    tiny = [stays(v if v.ndim > 1 else v[None, :]) for v in tiny]
    numbers, table = pl.pallas_call(
        numbers_kernel,
        in_specs=[pl.BlockSpec(memory_space=pltpu.VMEM)] * (6 + len(tiny)),
        out_shape=[shape_of(frame_count, LANES), shape_of(TABLE, LANES)],
        compiler_params=params(),
        cost_estimate=cost(1),
        name="numbers",
    )(
        stays(options),
        stays(depth[None, :]),
        stays(targets),
        stays(destination[None, :]),
        *tiny,
        stays(head_b[None, :]),
        out_b[None, :],
    )
    slots = exchanged(numbers.reshape(peers, per_pair, LANES)).reshape(frame_count, LANES)

    h1, s1, s2, h2, enc, s3 = encode(section, frames, w1t, w2t, stays(linear_w), table)
    keep, send_one, send_two, small, g3 = plan(
        section, slots, enc, s3, h2, branch_w, value_w, table, per_pair, levels, CUBE * size
    )
    recv = swapped(send_one), swapped(send_two)
    channels = frames.shape[2] // lax.axis_size("section")
    g1, c2, sums = back(g3, linear_w, s2, s1, h1, w2t)
    other = swapped(g1)
    g1 = held_near(g1)
    cubes = [list(range(c, c + CUBE)) for c in range(0, peers, CUBE)]
    bf16 = functools.partial(shape_of, dtype=BF16)
    pieces = small_call(
        merge_kernel,
        bf16(CUBE, size + 2 * SHORT, LANES),
        (keep, *recv, small, c2, sums),
        [
            pltpu.VMEM((CUBE * SHORT, LANES), F32),
            pltpu.VMEM((CUBE, size + 2 * SHORT, LANES), BF16),
            pltpu.SemaphoreType.DMA((CUBE,)),
        ],
        name="merge",
        far=True,
        weight=30,
    )
    got = exchanged(pieces, cubes)
    c1, frames_grad, band = first(section, frames, g1, w1t, other, pieces, channels, DRAW)
    piece = bf16(size + 2 * SHORT + c1.shape[0], LANES)
    keep = small_call(cube_kernel, piece, (got, c1), name="cube")
    distance = CUBE
    while distance < peers:
        recv = partner(keep, distance)
        if distance == CUBE:
            frames_grad, token = pixels(section, band, g1, other, keep, frames_grad, DRAW)
        distance *= 2
        keep = small_call(add_kernel, piece, (keep, recv), name="add", after=(token,))
    parts = [keep] + [partner(keep, k) for k in range(1, CUBE)]
    place = (lax.axis_index("batch").astype(jnp.int32)[None],)
    got = small_call(
        relay_kernel,
        [bf16(CUBE // 2, *piece.shape)] * 2,
        parts,
        [pltpu.VMEM((CUBE, *piece.shape), BF16)],
        name="relay",
        place=place,
    )
    got_other = [swapped(v) for v in got]
    shapes = [p.shape for p in encoder_params + planner_params]
    near = pl.BlockSpec(memory_space=pltpu.VMEM)
    flat = [shape_of(*(v if len(v) > 1 else (1,) + v)) for v in [(1, 1)] + shapes]
    large = [flat[k] for k in (5, 7, 11)]
    staged = [
        pltpu.VMEM((CUBE * size, LANES), F32),
        pltpu.VMEM(branch_w.shape, F32),
    ]
    little = [v for k, v in enumerate(flat) if k not in (5, 7, 11)]
    sems = pltpu.SemaphoreType.DMA((CUBE + len(little),))
    begun = pl.pallas_call(
        own_kernel,
        in_specs=[SCALARS, near, near],
        out_specs=[ANYWHERE] * 3,
        out_shape=large,
        scratch_shapes=[*staged, sems],
        compiler_params=params(),
        cost_estimate=cost(1),
        name="own",
    )(section, *got)
    ends = pl.pallas_call(
        unpack_kernel,
        in_specs=[SCALARS] + [near] * 4 + [ANYWHERE] * 3,
        out_specs=[ANYWHERE] * (3 + len(little)),
        out_shape=large + little,
        scratch_shapes=[pltpu.VMEM(v.shape, F32) for v in little]
        + [*staged, pltpu.VMEM((CUBE * SHORT, LANES), F32), sems],
        input_output_aliases={5: 0, 6: 1, 7: 2},
        compiler_params=params(),
        cost_estimate=cost(1.5),
        name="unpack",
    )(section, *got, *got_other, *begun)
    rest = list(ends[3:])
    for k, at in enumerate((5, 7, 11)):
        rest.insert(at, ends[k])
    rest = [v.reshape(s) for v, s in zip(rest, [()] + shapes)]
    for at in (1, 3, 9, 13):
        rest[at] = rest[at].T
    return (rest[0], frames_grad.transpose(2, 0, 1, 3), *rest[1:])


def solution(mesh):
    placed = (
        P(None, None, None, "batch"),
        P("batch"),
        P(None, "batch"),
        P("batch"),
        P(None, None, "batch"),
    ) + (P(),) * 14
    return jax.shard_map(
        local,
        mesh=mesh,
        in_specs=placed,
        out_specs=(P(), P("section", None, None, "batch")) + (P(),) * 14,
        check_vma=False,
    )
```

```python
import functools
import math

import jax
import jax.numpy as jnp
from jax import lax
from jax.experimental import pallas as pl
from jax.experimental.pallas import tpu as pltpu
from jax.sharding import PartitionSpec as P

BF16 = jnp.bfloat16
F32 = jnp.float32
EXACT = lax.Precision.HIGHEST
LANES = 128
VMEM_BYTES = 32 * 1024 * 1024
TILE = 16
REACH = 5
STEP = 3
COLS = 12
NEAR = 4
AT_VB, AT_OW, AT_HW, AT_LB, AT_SCALARS, AT_B1, AT_B2, AT_DEST = (
    slice(18, 19),
    slice(19, 20),
    slice(20, 22),
    slice(22, 23),
    slice(23, 24),
    slice(24, 25),
    slice(25, 26),
    26,
)
TABLE = 32
CUBE = 8
DRAW = 4
SHORT = 16


def dot(a, b, precision=None):
    return jnp.dot(a, b, preferred_element_type=F32, precision=precision)


def dot_rows(a, b, precision=None):
    return lax.dot_general(
        a, b, (((0,), (0,)), ((), ())), preferred_element_type=F32, precision=precision
    )


def dot_lanes(a, b, precision=None):
    return lax.dot_general(
        a, b, (((1,), (1,)), ((), ())), preferred_element_type=F32, precision=precision
    )


def iota(shape, axis):
    return lax.broadcasted_iota(jnp.int32, shape, axis)


def column(row):
    n = row.shape[1]
    wide = jnp.broadcast_to(row, (n, n))
    return jnp.sum(jnp.where(iota((n, n), 0) == iota((n, n), 1), wide, 0.0), axis=1, keepdims=True)


def row_of(col):
    n = col.shape[0]
    wide = jnp.broadcast_to(col, (n, n))
    return jnp.sum(jnp.where(iota((n, n), 0) == iota((n, n), 1), wide, 0.0), axis=0, keepdims=True)


def soft(x):
    t = jnp.tanh(0.5 * x)
    return jnp.maximum(x, 0.0) - jnp.log(0.5 + 0.5 * jnp.abs(t)), 0.5 + 0.5 * t


def silu_pair(x):
    s = 0.5 + 0.5 * jnp.tanh(0.5 * x)
    act = x * s
    return act, s + act * (1.0 - s)


def pixel_order(w1t):
    tap, pix = iota((256, 256), 0), iota((256, 256), 1)
    moves = ((tap >> 6) == (pix & 3)) & ((tap & 63) == (pix >> 2))
    return dot(w1t, moves.astype(F32).astype(BF16))


def frame_copies(section, far, here, sems):
    lanes = pl.ds(pl.multiple_of(section[0] * LANES, LANES), LANES)
    size = 4 * STEP

    def copy(g):
        rows = pl.ds(pl.multiple_of(g * size, size), size)
        return pltpu.make_async_copy(far.at[rows, :, :, lanes], here.at[rows], sems.at[g])

    return copy


def tile_rows(frames, row, j, cols):
    img, _, channels, _ = frames.shape
    flat = frames.reshape(img, img * channels, LANES)
    size = cols * channels
    end = min((j + 1) * size, img * channels)
    part = flat[pl.ds(row, 4), j * size : end, :]
    return part.reshape(4 * (end - j * size), LANES)


def encode_kernel(
    section,
    frames_far,
    w1t,
    w2t,
    lw_far,
    table,
    h1_far,
    s1_far,
    s2_far,
    h2,
    enc,
    s3,
    frames,
    lw,
    h1,
    s1,
    s2,
    band,
    edge,
    band2,
    bias1,
    bias2,
    held,
    held2,
    sems,
):
    blocks, side = h1.shape[:2]
    steps = blocks // STEP
    tiles = frames.shape[1] // TILE
    k1, k2 = w1t.shape[0], w2t.shape[0]
    reach_rows = REACH * k1
    arrives = frame_copies(section, frames_far, frames, sems.at[0])
    for g in range(steps):
        arrives(g).start()
    last_copies = [
        pltpu.make_async_copy(lw_far, lw, sems.at[3, 0]),
        pltpu.make_async_copy(s2, s2_far, sems.at[3, 1]),
    ]
    last_copies[0].start()

    def leaves(g):
        rows = pl.ds(g * STEP, STEP)
        return [
            pltpu.make_async_copy(h1.at[rows], h1_far.at[rows], sems.at[1, g]),
            pltpu.make_async_copy(s1.at[rows], s1_far.at[rows], sems.at[2, g]),
        ]

    inner = side // 2 - 1
    row_len = inner * k2
    two = 2 * k2 * 3

    def prepare():
        taps = pixel_order(w1t[...])
        edges = []
        for half in range(2):
            lines = [taps[:, 32 * (4 * half + u) : 32 * (4 * half + u + 1)] for u in range(4)]
            for place in range(REACH):
                pieces = []
                for line in lines:
                    start = 16 * (place - 1)
                    cut = line[:, max(0, -start) : min(32, 64 - start)]
                    start = max(start, 0)
                    pieces += [jnp.zeros((k1, start), F32)] if start else []
                    pieces.append(cut)
                    rest = 64 - start - cut.shape[1]
                    pieces += [jnp.zeros((k1, rest), F32)] if rest else []
                at = half * reach_rows + place * k1
                band[at : at + k1, :] = jnp.concatenate(pieces, axis=1).astype(BF16)
            edges.append(jnp.concatenate([line[:, 16:] for line in lines], axis=1))
        edge[...] = jnp.concatenate(edges, axis=0).astype(BF16)
        tap, pix = iota((256, LANES), 0), iota((256, LANES), 1)
        for half in range(2):
            for place in range(3):
                hit = (
                    ((tap & 15) == (pix & 15))
                    & ((tap >> 6) == (pix >> 6) + 2 * half)
                    & (((tap >> 4) & 3) == ((pix >> 4) & 3) + 2 - 2 * place)
                )
                at = (half * 3 + place) * k2
                taps = dot(w2t[...], hit.astype(F32).astype(BF16))
                band2[at : at + k2, :] = taps.astype(BF16)
        bias1[...] = jnp.broadcast_to(column(table[AT_B1, 0:k1]), bias1.shape)
        bias2[...] = jnp.broadcast_to(column(table[AT_B2, 0:k2]), bias2.shape)
        held[...] = jnp.zeros_like(held)
        held2[...] = jnp.zeros_like(held2)
        h1[...] = jnp.zeros_like(h1)

    def added(sums, x, value):
        sums[x] = sums[x] + value if x in sums else value

    def second_matmul(b):
        tiles = [
            h1[pl.ds(2 * b + 1, 2), 4 * j : 4 * j + 4].reshape(LANES, LANES)
            for j in range(side // 4)
        ]
        return dot(band2[...], jnp.concatenate(tiles, axis=1))

    def second_rows(b, got):
        low, high = {}, {}
        for j in range(side // 4):
            for place in range(3):
                x = 2 * j - 1 + place
                if 0 <= x < inner:
                    span = slice(j * LANES, (j + 1) * LANES)
                    at = place * k2
                    added(low, x, got[at : at + k2, span])
                    added(high, x, got[two // 2 + at : two // 2 + at + k2, span])
        row = jnp.maximum(b - 1, 0) * row_len
        for x in range(inner):
            value, slope = soft(held2[x] + high[x] + bias2[...])
            held2[x] = low[x]
            at = pl.ds(pl.multiple_of(row + x * k2, k2), k2)
            h2[at, :] = value.astype(BF16)
            s2[at, :] = slope.astype(BF16)

    def one_step(g, carry):
        def row(r):
            return pl.multiple_of(4 * (STEP * g + r), 4)

        arrives(g).wait()
        lows, highs = [{} for _ in range(STEP)], [{} for _ in range(STEP)]

        def place_tile(r, j, got):
            for place in range(REACH):
                x = 4 * j - 1 + place
                if 0 <= x < side:
                    at = place * k1
                    added(lows[r], x, got[at : at + k1])
                    added(highs[r], x, got[reach_rows + at : reach_rows + at + k1])

        def finish(r, xs):
            for x in xs:
                value, slope = soft(held[x] + highs[r][x] + bias1[...])
                held[x] = lows[r][x]
                h1[STEP * g + r, x] = value.astype(BF16)
                s1[STEP * g + r, x] = slope.astype(BF16)

        pair = jnp.maximum(g - 1, 0)
        units = [(lambda: second_matmul(pair), lambda got: second_rows(pair, got))]

        def edges():
            parts = [tile_rows(frames, row(r), tiles, TILE) for r in range(STEP)]
            return dot(edge[...], jnp.concatenate(parts, axis=1))

        def place_edges(got):
            for r in range(STEP):
                added(lows[r], side - 1, got[:k1, r * LANES : (r + 1) * LANES])
                added(highs[r], side - 1, got[k1:, r * LANES : (r + 1) * LANES])

        units.append((edges, place_edges))

        def full(spots):
            parts = [tile_rows(frames, row(r), j, TILE) for r, j in spots]
            return dot(band[...], jnp.concatenate(parts, axis=1))

        def place_full(got, spots, ready):
            for i, (r, j) in enumerate(spots):
                place_tile(r, j, got[:, i * LANES : (i + 1) * LANES])
            if ready:
                finish(*ready)

        for r in range(STEP):
            if r % 2 == 0:
                spots = [(k, tiles - 1) for k in (r, r + 1) if k < STEP]
                units.append(
                    (
                        functools.partial(full, spots),
                        functools.partial(place_full, spots=spots, ready=None),
                    )
                )
            done = 0
            for j in range(0, tiles - 1, 2):
                spots = [(r, j), (r, j + 1)]
                ready = side if j + 2 == tiles - 1 else 4 * j + 7
                units.append(
                    (
                        functools.partial(full, spots),
                        functools.partial(place_full, spots=spots, ready=(r, range(done, ready))),
                    )
                )
                done = ready
        waiting = None
        for issue, take in units:
            got = issue()
            if waiting is not None:
                waiting[0](waiting[1])
            waiting = (take, got)
        waiting[0](waiting[1])
        for copy in leaves(g):
            copy.start()
        return carry

    prepare()
    lax.fori_loop(0, steps, one_step, 0)
    for b in range(steps - 1, side // 2):
        second_rows(b, second_matmul(b))
    for copy in last_copies[1:]:
        copy.start()
    last_copies[0].wait()
    value, slope = soft(dot_rows(lw[...], h2[...]) + column(table[AT_LB, :]))
    enc[...] = value.astype(BF16)
    s3[...] = slope
    for g in range(steps):
        for copy in leaves(g):
            copy.wait()
    for copy in last_copies[1:]:
        copy.wait()


def three_parts(row):
    high = row.astype(BF16).astype(F32)
    middle = (row - high).astype(BF16).astype(F32)
    return jnp.concatenate([high, middle, row - high - middle], axis=0)


def with_ones(value):
    return jnp.concatenate([value, ones_rows(value.shape[1])], axis=0)


def ones_rows(lanes):
    return (iota((16, lanes), 0) < 3).astype(F32).astype(BF16)


def plan_kernel(
    section,
    slots,
    enc,
    s3,
    h2,
    branch_far,
    value_w,
    table,
    keep,
    send_one,
    send_two,
    small,
    g3,
    parts,
    bwt,
    vht,
    vhw,
    ow,
    mine,
    pre,
    dbr,
    dval,
    low,
    hid,
    gb,
    branch_w,
    sem,
    *,
    per_pair,
    depth,
):
    width = enc.shape[0]
    options = branch_w.shape[0]
    pairs = options // 2
    two = 2 * width
    sec = section[0]
    branch_copy = pltpu.make_async_copy(branch_far, branch_w, sem)
    branch_copy.start()

    count = slots.shape[0]
    dest = jnp.concatenate(
        [table[AT_DEST + k : AT_DEST + k + 1, :] for k in range(count // LANES)], axis=1
    )
    own = jnp.where(sec == 0, dest[:, :LANES], dest[:, LANES:])
    others = jnp.transpose(jnp.broadcast_to(dest, (LANES, count)))
    index = iota((count, LANES), 1) + sec * LANES
    earlier = (others == own) & (iota((count, LANES), 0) < index)
    rank = jnp.sum(earlier.astype(F32), axis=0, keepdims=True)
    bucket = own * float(per_pair) + rank
    chosen = (iota((count, LANES), 0).astype(F32) == bucket).astype(F32).astype(BF16)
    numbers = slots[...]
    high = numbers.astype(BF16)
    middle = (numbers - high.astype(F32)).astype(BF16)
    rest = (numbers - high.astype(F32) - middle.astype(F32)).astype(BF16)
    mine[...] = sum(dot_rows(v, chosen) for v in (rest, middle, high))[: mine.shape[0]]

    pad = jnp.zeros((13, width), F32)
    branch_copy.wait()
    for o in range(options):
        rows = [branch_w[o].astype(F32), three_parts(table[o : o + 1, :]), pad]
        bwt[o * width : (o + 1) * width, :] = jnp.transpose(
            jnp.concatenate(rows, axis=0)
        ).astype(BF16)
    scalars = table[AT_SCALARS, :]
    head_w = table[AT_HW, :]
    rows = [value_w[...].astype(F32), three_parts(table[AT_VB, :]), pad]
    vht[0:width, :] = jnp.transpose(jnp.concatenate(rows, axis=0)).astype(BF16)
    vht[width:, :] = jnp.zeros((16, width + 16), BF16)
    lane = iota((1, 16), 1)
    for k in range(2):
        bias = three_parts(jnp.broadcast_to(scalars[:, 1 + k : 2 + k], (1, 16)))
        bias = sum(jnp.where(lane == j, bias[j : j + 1], 0.0) for j in range(3))
        vht[width + k : width + k + 1, 0:width] = head_w[k : k + 1].astype(BF16)
        vht[width + k : width + k + 1, width:] = bias.astype(BF16)
    vhw[:, 0:width] = value_w[...]
    vhw[:, width:] = jnp.transpose(
        jnp.concatenate([head_w, jnp.zeros((14, width), F32)], axis=0)
    ).astype(BF16)
    ow[...] = jnp.broadcast_to(column(table[AT_OW, :]), (width, LANES))
    wide_ow = jnp.concatenate([ow[...], ow[...]], axis=1)

    labels = iota((options, LANES), 0).astype(F32)
    state = enc[...].astype(F32)
    rounded_all, saved = [], []
    for level in range(depth):
        picked = labels == mine[level : level + 1, :]
        rounded = state.astype(BF16)
        rounded_all.append(rounded)
        pre[...] = dot(bwt[...], with_ones(rounded))
        following = state
        reward, discount, value = [], [], []

        def value_part(t, got):
            act, slope = silu_pair(got[:width])
            dval[level, t] = slope
            hidden = act.astype(BF16)
            hid[level, t] = hidden
            worth = jnp.sum(hidden.astype(F32) * wide_ow, axis=0, keepdims=True)
            for k in range(2):
                span = slice(k * LANES, (k + 1) * LANES)
                value.append(worth[:, span])
                reward.append(got[width : width + 1, span])
                discount.append(got[width + 1 : width + 2, span])

        waiting = None
        for t in range(pairs):
            at = slice(t * two, (t + 1) * two)
            act, slope = silu_pair(pre[at, :])
            dbr[level, at, :] = slope
            left = state + act[:width]
            right = state + act[width:]
            following = jnp.where(picked[2 * t : 2 * t + 1], left, following)
            following = jnp.where(picked[2 * t + 1 : 2 * t + 2], right, following)
            both = with_ones(jnp.concatenate([left.astype(BF16), right.astype(BF16)], axis=1))
            low[level, t] = both
            got = dot(vht[...], both)
            if waiting is not None:
                value_part(*waiting)
            waiting = (t, got)
        value_part(*waiting)
        reward = jnp.concatenate(reward, axis=0)
        discount = jax.nn.sigmoid(jnp.concatenate(discount, axis=0))
        value = jnp.concatenate(value, axis=0) + scalars[:, 3:4]
        quality = reward + discount * value
        top = jnp.max(quality, axis=0, keepdims=True)
        shifted = jnp.exp(quality - top)
        total = jnp.sum(shifted, axis=0, keepdims=True)
        live = (mine[depth : depth + 1, :] > level).astype(F32)
        chosen = picked.astype(F32)

        def target(kind):
            at = depth + 1 + kind * depth + level
            return mine[at : at + 1, :]

        reward_gap = live * (jnp.sum(chosen * reward, axis=0, keepdims=True) - target(0))
        discount_gap = live * (jnp.sum(chosen * discount, axis=0, keepdims=True) - target(1))
        plan_gap = live * (top + jnp.log(total) - target(2))
        grad_quality = plan_gap * (shifted / total)
        head_two = (chosen * discount_gap + grad_quality * value) * discount * (1.0 - discount)
        saved.append(
            (
                picked,
                (chosen * reward_gap + grad_quality).astype(BF16).astype(F32),
                head_two.astype(BF16).astype(F32),
                (grad_quality * discount).astype(BF16).astype(F32),
                reward_gap * reward_gap + discount_gap * discount_gap + plan_gap * plan_gap,
            )
        )
        state = following

    out_sum = jnp.zeros((width, two), F32)
    value_sum = jnp.zeros((width + 16, width + 16), F32)
    grad_next = jnp.zeros((width, LANES), F32)
    line = iota((16, two), 0)
    for level in reversed(range(depth)):
        picked, head_one, head_two, grad_value, _ = saved[level]
        upward = jnp.zeros((width, LANES), F32)

        def branch_part(t, moved):
            at = slice(t * two, (t + 1) * two)
            left = moved[:, :LANES] + jnp.where(picked[2 * t : 2 * t + 1], grad_next, 0.0)
            right = moved[:, LANES:] + jnp.where(picked[2 * t + 1 : 2 * t + 2], grad_next, 0.0)
            grad_branch = jnp.concatenate([left, right], axis=0) * dbr[level, at, :]
            grad_branch = grad_branch.astype(BF16)
            gb[level, at, :] = grad_branch
            weights = jnp.concatenate([branch_w[2 * t], branch_w[2 * t + 1]], axis=1)
            return left + right + dot(weights, grad_branch)

        waiting = None
        for t in range(pairs):

            def across(rows):
                return jnp.concatenate(
                    [rows[2 * t : 2 * t + 1], rows[2 * t + 1 : 2 * t + 2]], axis=1
                )

            worth = across(grad_value)
            grad_pre = (worth * wide_ow * dval[level, t]).astype(BF16)
            out_sum = out_sum + hid[level, t].astype(F32) * worth
            heads = jnp.where(line == 0, across(head_one), 0.0)
            heads = jnp.where(line == 1, across(head_two), heads)
            heads = jnp.where(line == 2, worth, heads)
            stacked = jnp.concatenate([grad_pre, heads.astype(BF16)], axis=0)
            moved = dot(vhw[...], stacked)
            value_sum = value_sum + dot_lanes(stacked, low[level, t])
            if waiting is not None:
                upward = upward + branch_part(*waiting)
            waiting = (t, moved)
        upward = upward + branch_part(*waiting)
        grad_next = upward

    linear_rows = h2.shape[0]
    half = (linear_rows + options * width + width) // 2
    rest = linear_rows - half
    rounded = with_ones(jnp.concatenate(rounded_all, axis=1))
    small[...] = jnp.zeros_like(small)
    if half < keep.shape[0]:
        for k in range(2):
            parts[k, half:, :] = jnp.zeros((keep.shape[0] - half, LANES), BF16)
    for t in range(pairs):
        at = slice(t * two, (t + 1) * two)
        grads = jnp.concatenate([gb[level, at, :] for level in range(depth)], axis=1)
        got = dot_lanes(rounded, grads)
        for k in range(2):
            o = 2 * t + k
            span = slice(k * width, (k + 1) * width)
            rows = slice(rest + o * width, rest + (o + 1) * width)
            parts[1 - sec, rows, :] = got[:width, span].astype(BF16)
            small[o : o + 1, :] = got[width : width + 1, span]
    after = rest + options * width
    parts[1 - sec, after : after + width, :] = jnp.transpose(value_sum[:width, :width]).astype(BF16)

    grad_three = (grad_next.astype(BF16).astype(F32) * s3[...]).astype(BF16)
    g3[...] = grad_three
    chunk = linear_rows // 9
    for i in range(8):
        at = slice(i * chunk, (i + 1) * chunk)
        parts[sec, at, :] = dot_lanes(h2[at, :], grad_three).astype(BF16)
    last = dot_lanes(h2[8 * chunk :, :], grad_three).astype(BF16)
    parts[sec, 8 * chunk : half, :] = last[: half - 8 * chunk]
    parts[1 - sec, 0:rest, :] = last[half - 8 * chunk :]
    keep[...] = parts[0]
    send_one[...] = parts[1, : send_one.shape[0]]
    send_two[...] = parts[1, send_one.shape[0] :]

    small[AT_VB, :] = row_of(value_sum[:width, width : width + 1])
    small[AT_OW, :] = row_of(jnp.sum(out_sum, axis=1, keepdims=True))
    small[AT_HW, :] = value_sum[width : width + 2, :width]
    small[AT_LB, :] = row_of(jnp.sum(grad_three.astype(F32), axis=1, keepdims=True))
    loss = 0.5 * jnp.sum(sum(kept[4] for kept in saved), axis=1, keepdims=True)
    ends = [loss] + [value_sum[width + k : width + k + 1, width : width + 1] for k in range(3)]
    lane = iota((1, LANES), 1)
    line = jnp.zeros((1, LANES), F32)
    for k, end in enumerate(ends):
        line = jnp.where(lane == k, end, line)
    small[AT_SCALARS, :] = line


def back_kernel(g3, lw, s2, s1, h1, w2t, g1, c2, sums, t2, g2):
    side, k1 = s1.shape[1], s1.shape[2]
    k2 = w2t.shape[0]
    inner = side // 2 - 1
    row_len = inner * k2
    tap, pix = iota((LANES, 256), 1), iota((LANES, 256), 0)
    for yrel in range(2):
        for p in range(3):
            hit = (
                ((tap & 15) == (pix & 15))
                & ((tap >> 6) == (pix >> 6) + 2 * (1 - yrel))
                & (((tap >> 4) & 3) == ((pix >> 4) & 3) + 2 - 2 * p)
            )
            at = (yrel * 3 + p) * k2
            t2[:, at : at + k2] = dot_lanes(hit.astype(F32).astype(BF16), w2t[...]).astype(BF16)
    g2[0] = jnp.zeros(g2.shape[1:], BF16)
    g2[inner + 1] = jnp.zeros(g2.shape[1:], BF16)
    g1[0] = jnp.zeros(g1.shape[1:], BF16)
    g1[side + 1] = jnp.zeros(g1.shape[1:], BF16)
    zero = jnp.zeros((k2, LANES), BF16)
    total_one = jnp.zeros((k1, LANES), F32)
    total_two = jnp.zeros((k2, LANES), F32)
    for y in range(inner):
        at = slice(y * row_len, (y + 1) * row_len)
        grad = dot(lw[at, :], g3[...]) * s2[at, :].astype(F32)
        grad = grad.astype(BF16).reshape(inner, k2, LANES)
        g2[y + 1] = grad
        total_two = total_two + jnp.sum(grad.astype(F32), axis=0)
    reach, cols = 5, 8
    total = jnp.zeros((2 * reach * k2, 2 * cols * k1), F32)
    grads, tiles = [], []
    for b in range(side // 2):
        cut = []
        for j in range(side // 4):
            pieces = []
            for yrel in range(2):
                for p in range(3):
                    x = 2 * j - 1 + p
                    pieces.append(g2[b + yrel, x] if 0 <= x < inner else zero)
            cut.append(jnp.concatenate(pieces, axis=0))
        got = dot(t2[...], jnp.concatenate(cut, axis=1))
        for u in range(2):
            for j in range(side // 4):
                part = got[u * 64 : (u + 1) * 64, j * LANES : (j + 1) * LANES]
                slope = s1[2 * b + u + 1, 4 * j : 4 * j + 4].astype(F32)
                grad = (part.reshape(4, k1, LANES) * slope).astype(BF16)
                g1[2 * b + u + 1, 4 * j : 4 * j + 4] = grad
                total_one = total_one + jnp.sum(grad.astype(F32), axis=0)
        for j in range(-(-side // cols)):
            end = min((j + 1) * cols, side)
            tile = h1[2 * b + 1 : 2 * b + 3, j * cols : end]
            if end < (j + 1) * cols:
                rest = jnp.zeros((2, (j + 1) * cols - end, k1, LANES), BF16)
                tile = jnp.concatenate([tile, rest], axis=1)
            tiles.append(tile.reshape(2 * cols * k1, LANES))
            pieces = []
            for half in range(2):
                for p in range(reach):
                    x = 4 * j - 1 + p
                    pieces.append(g2[b + 1 - half, x] if 0 <= x < inner else zero)
            grads.append(jnp.concatenate(pieces, axis=0))
        if b % 2:
            total = total + dot_lanes(
                jnp.concatenate(grads, axis=1), jnp.concatenate(tiles, axis=1)
            )
            grads, tiles = [], []
    line = 4 * k1
    for half in range(2):
        for u in range(2):
            tap_row = jnp.zeros((k2, line), F32)
            for p in range(reach):
                at = (half * reach + p) * k2
                part = total[at : at + k2, u * 2 * line : (u + 1) * 2 * line]
                start = 2 * k1 * (p - 1)
                piece = part[:, max(start, 0) : min(start + line, 2 * line)]
                if start < 0:
                    piece = jnp.concatenate([jnp.zeros((k2, -start), F32), piece], axis=1)
                if start + line > 2 * line:
                    rest = jnp.zeros((k2, start - line), F32)
                    piece = jnp.concatenate([piece, rest], axis=1)
                tap_row = tap_row + piece
            at = (2 * half + u) * line
            c2[:, at : at + line] = tap_row
    sums[...] = jnp.zeros_like(sums)
    sums[0:1, 0:k1] = row_of(jnp.sum(total_one, axis=1, keepdims=True))
    sums[1:2, 0:k2] = row_of(jnp.sum(total_two, axis=1, keepdims=True))


def pixel_band(sec, w1t, channels):
    k1 = w1t.shape[0]
    rows = 64 * channels
    row, tap = iota((rows, 256), 0), iota((rows, 256), 1)
    moves = ((tap >> 6) == row % channels + sec * channels) & ((tap & 63) == row // channels)
    taps = dot_lanes(moves.astype(F32).astype(BF16), w1t)
    line, span = COLS * channels, 8 * channels
    blocks = {}
    for half in range(2):
        for p in range(NEAR):
            pieces = []
            for u in range(4):
                at = (4 * half + u) * span
                start = 4 * (p - 1) * channels
                cut = taps[at + max(0, -start) : at + min(span, line - start)]
                start = max(start, 0)
                pieces += [jnp.zeros((start, k1), F32)] if start else []
                pieces.append(cut)
                rest = line - start - cut.shape[0]
                pieces += [jnp.zeros((rest, k1), F32)] if rest else []
            blocks[half, p] = jnp.concatenate(pieces, axis=0)
    zero = jnp.zeros((4 * line, k1), F32)
    lines = []
    for r in range(STEP):
        cols = [
            blocks.get((r + 1 - yrel, p), zero) for yrel in range(STEP + 1) for p in range(NEAR)
        ]
        lines.append(jnp.concatenate(cols, axis=1))
    return jnp.concatenate(lines, axis=0).astype(BF16)


def first_kernel(
    section,
    frames_far,
    g1,
    w1t,
    other_far,
    after,
    c1,
    out,
    band,
    frames,
    acc,
    other,
    held,
    sems,
    draw_sems,
    *,
    draw,
):
    side, k1 = g1.shape[1], g1.shape[2]
    img, _, channels, _ = frames.shape
    steps = img // 4 // STEP
    arrives = frame_copies(section, frames_far, frames, sems)
    for g in range(steps):
        arrives(g).start()
    other_copy = pltpu.make_async_copy(
        other_far.at[0 : STEP * draw + 1], other, sems.at[steps]
    )
    other_copy.start()
    acc[...] = jnp.zeros_like(acc)
    zero = jnp.zeros((k1, LANES), BF16)

    def one_step(g, carry):
        arrives(g).wait()
        pixels, grads = [], []
        for j in range(img // COLS):
            rows = [pl.multiple_of(4 * (STEP * g + r), 4) for r in range(STEP)]
            pixels.append(
                jnp.concatenate([tile_rows(frames, row, j, COLS) for row in rows], axis=0)
            )
            pieces = []
            for yrel in range(STEP + 1):
                for p in range(NEAR):
                    x = 3 * j - 1 + p
                    pieces.append(g1[STEP * g + yrel, x] if 0 <= x < side else zero)
            grads.append(jnp.concatenate(pieces, axis=0))
        acc[...] += dot_lanes(jnp.concatenate(pixels, axis=1), jnp.concatenate(grads, axis=1))
        return carry

    lax.fori_loop(0, steps, one_step, 0)
    band[...] = pixel_band(section[0], w1t[...], out.shape[2])
    other_copy.wait()
    finish = draw_steps(section, band, g1, 0, other, 0, out, held, draw_sems, 0, draw)
    fold_first(acc, c1, channels, k1)
    finish()


def fold_first(acc, c1, channels, k1):
    line = COLS * channels
    step = 4 * channels
    taps = []
    for half in range(2):
        total = sum(
            acc[r * 4 * line : (r + 1) * 4 * line, :][
                :, (r + 1 - half) * NEAR * k1 : (r + 2 - half) * NEAR * k1
            ]
            for r in range(STEP)
        )
        for u in range(4):
            part = total[u * line : (u + 1) * line]
            cols = [part[:, p * k1 : (p + 1) * k1] for p in range(NEAR)]
            taps.append(cols[1][0:step] + cols[2][step : 2 * step] + cols[3][2 * step :])
            taps.append(cols[0][0:step] + cols[1][step : 2 * step] + cols[2][2 * step :])
    row, col = iota((256, 256), 0), iota((256, 256), 1)
    moves = ((row & 3) == (col >> 6)) & ((row >> 2) == (col & 63))
    grad = dot_rows(jnp.concatenate(taps, axis=0), moves.astype(F32), EXACT)
    for half in range(2):
        c1[half * k1 : (half + 1) * k1, :] = grad[:, half * LANES : (half + 1) * LANES].astype(BF16)


def draw_steps(section, band, mine, mine_at, other, other_at, out, held, sems, start, steps):
    side, k1 = mine.shape[1], mine.shape[2]
    img, channels = out.shape[1], out.shape[2]
    sec = section[0]
    line = COLS * channels
    flat = held.reshape(2, 2, 4 * STEP, img * channels, LANES)

    def writes(g):
        rows = slice(4 * STEP * (start + g), 4 * STEP * (start + g + 1))
        places = (sec * LANES, (1 - sec) * LANES)
        return [
            pltpu.make_async_copy(
                held.at[g % 2, k],
                out.at[rows, :, :, pl.ds(pl.multiple_of(places[k], LANES), LANES)],
                sems.at[g % 2, k],
            )
            for k in range(2)
        ]

    zero = jnp.zeros((k1, 2 * LANES), BF16)
    for g in range(steps):
        if g >= 2:
            for copy in writes(g - 2):
                copy.wait()
        for j in range(img // COLS):
            pieces = []
            for yrel in range(STEP + 1):
                for p in range(NEAR):
                    x, y = 3 * j - 1 + p, STEP * (start + g) + yrel
                    if 0 <= x < side:
                        pair = [mine[y - mine_at, x], other[y - other_at, x]]
                        pieces.append(jnp.concatenate(pair, axis=1))
                    else:
                        pieces.append(zero)
            got = dot(band[...], jnp.concatenate(pieces, axis=0))
            for k in range(4 * STEP):
                at = slice(k * line, (k + 1) * line)
                span = slice(j * line, (j + 1) * line)
                flat[g % 2, 0, k, span, :] = got[at, :LANES]
                flat[g % 2, 1, k, span, :] = got[at, LANES:]
        for copy in writes(g):
            copy.start()

    def finish():
        for g in range(max(steps - 2, 0), steps):
            for copy in writes(g):
                copy.wait()

    return finish


def pixels_kernel(section, band, mine, other_far, after, done, out, token, held, other, sems, *, start):
    steps = other.shape[0] // STEP
    fetch = pltpu.make_async_copy(
        other_far.at[STEP * start : STEP * (start + steps) + 1], other, sems.at[2, 0]
    )
    fetch.start()
    token[...] = jnp.zeros_like(token)
    fetch.wait()
    draw_steps(
        section, band, mine, 0, other, STEP * start, out, held, sems, start, steps
    )()


def two_parts(value):
    high = value.astype(BF16).astype(F32)
    return jnp.concatenate([high, value - high], axis=0).astype(BF16)


def one_part(pair):
    rows = pair.shape[0] // 2
    pair = pair.astype(F32)
    return pair[:rows] + pair[rows:]


def merge_kernel(keep, recv_one, recv_two, small, c2, sums, out_far, lines, out, sems):
    members = out.shape[0]
    size = keep.shape[0] // members
    k2 = c2.shape[0]
    lines[...] = jnp.zeros_like(lines)
    at = small.shape[0]
    lines[0:at, :] = small[...]
    for half in range(2):
        lines[at : at + k2, :] = c2[:, half * LANES : (half + 1) * LANES]
        at += k2
    lines[at : at + sums.shape[0], :] = sums[...]
    for k in range(members):
        at = slice(k * size, (k + 1) * size)
        recv, here = recv_one, k
        if k >= members // 2:
            recv, here = recv_two, k - members // 2
        got = recv[here * size : (here + 1) * size, :]
        out[k, 0:size, :] = (keep[at, :].astype(F32) + got.astype(F32)).astype(BF16)
        out[k, size:, :] = two_parts(lines[k * SHORT : (k + 1) * SHORT, :])
        pltpu.make_async_copy(out.at[k], out_far.at[k], sems.at[k]).start()
    for k in range(members):
        pltpu.make_async_copy(out.at[k], out_far.at[k], sems.at[k]).wait()


def cube_kernel(got, c1, out):
    members = got.shape[0]
    size = got.shape[1] - 2 * SHORT
    out[0:size, :] = sum(got[k, 0:size, :].astype(F32) for k in range(members)).astype(BF16)
    total = sum(one_part(got[k, size:, :]) for k in range(members))
    out[size : size + 2 * SHORT, :] = two_parts(total)
    out[size + 2 * SHORT :, :] = c1[...]


def add_kernel(a, b, after, out):
    size = a.shape[0] - 2 * SHORT - 32
    middle = slice(size, size + 2 * SHORT)
    for span in (slice(0, size), slice(size + 2 * SHORT, a.shape[0])):
        out[span, :] = (a[span, :].astype(F32) + b[span, :].astype(F32)).astype(BF16)
    out[middle, :] = two_parts(one_part(a[middle, :]) + one_part(b[middle, :]))


def relay_kernel(batch, *refs):
    parts, (one, two, out) = refs[:CUBE], refs[CUBE:]
    me = batch[0] % CUBE
    for k, part in enumerate(parts):
        out[me ^ k] = part[...]
    one[...] = out[: CUBE // 2]
    two[...] = out[CUBE // 2 :]


def piece_of(got, k):
    count = got[0].shape[0]
    return got[k // count].at[k % count]


def unpack_half(which, got, lw, bw, vw, stage, stage_b, sems):
    members = 2 * got[0].shape[0]
    size = stage.shape[0] // members
    linear_rows, width = lw.shape
    options = bw.shape[0]
    half = (linear_rows + options * width + width) // 2
    rest = linear_rows - half

    @pl.when(which == 0)
    def _():
        copies = []
        for k in range(members):
            start, end = k * size, min((k + 1) * size, half)
            stage[start:end, :] = piece_of(got, k)[0 : end - start, :].astype(F32)
            copies.append(
                pltpu.make_async_copy(stage.at[start:end], lw.at[start:end], sems.at[k])
            )
            copies[-1].start()
        for copy in copies:
            copy.wait()

    @pl.when(which == 1)
    def _():
        def rows(start, end):
            parts = []
            while start < end:
                k, at = start // size, start % size
                count = min(size - at, end - start)
                parts.append(piece_of(got, k)[at : at + count, :])
                start += count
            value = parts[0] if len(parts) == 1 else jnp.concatenate(parts, axis=0)
            return value.astype(F32)

        stage[0:rest, :] = rows(0, rest)
        copies = [pltpu.make_async_copy(stage.at[0:rest], lw.at[half:], sems.at[0])]
        copies[0].start()
        group = options // 3
        for o in range(options):
            stage_b[o] = rows(rest + o * width, rest + (o + 1) * width)
            if o % group == group - 1:
                part = slice(o + 1 - group, o + 1)
                copy = pltpu.make_async_copy(
                    stage_b.at[part], bw.at[part], sems.at[1 + o // group]
                )
                copy.start()
                copies.append(copy)
        at = rest + options * width
        stage[rest : rest + width, :] = rows(at, at + width)
        copies.append(
            pltpu.make_async_copy(stage.at[rest : rest + width], vw, sems.at[1 + options // group])
        )
        copies[-1].start()
        for copy in copies:
            copy.wait()


def own_kernel(section, one, two, lw, bw, vw, stage, stage_b, sems):
    unpack_half(section[0], (one, two), lw, bw, vw, stage, stage_b, sems)


def unpack_kernel(section, *refs):
    mine, other, refs = refs[0:2], refs[2:4], refs[4:]
    lw, bw, vw = refs[3:6]
    little = (len(refs) - 10) // 2
    far, near = refs[6 : 6 + little], refs[6 + little : 6 + 2 * little]
    loss, c1, b1, c2, b2, lb, bb, hw, hb, vb, ow, ob = near
    stage, stage_b, lines, sems = refs[-4:]
    options = bw.shape[0]
    k1, k2 = c1.shape[0], c2.shape[0]
    size = stage.shape[0] // CUBE
    grad = [jnp.zeros((k1, LANES), F32) for _ in range(2)]
    for k in range(CUBE):
        pair = slice(size, size + 2 * SHORT)
        at = slice(k * SHORT, (k + 1) * SHORT)
        views = piece_of(mine, k), piece_of(other, k)
        lines[at, :] = sum(one_part(v[pair, :]) for v in views)
        for view in views:
            for h in range(2):
                at = size + 2 * SHORT + h * k1
                grad[h] += view[at : at + k1, :].astype(F32)
    for part in range(2):
        c1[:, part * LANES : (part + 1) * LANES] = grad[part]
    bb[...] = lines[0:options, :]
    vb[...] = lines[AT_VB, :]
    ow[...] = lines[AT_OW, :]
    hw[...] = lines[AT_HW, :]
    lb[...] = lines[AT_LB, :]
    scalars = lines[AT_SCALARS, :]
    loss[...] = scalars[:, 0:1]
    hb[...] = scalars[:, 1:3]
    ob[...] = scalars[:, 3:4]
    at = TABLE
    for part in range(2):
        c2[:, part * LANES : (part + 1) * LANES] = lines[at : at + k2, :]
        at += k2
    b1[...] = lines[at : at + 1, 0:k1]
    b2[...] = lines[at + 1 : at + 2, 0:k2]
    copies = [
        pltpu.make_async_copy(a, b, sems.at[CUBE + k]) for k, (a, b) in enumerate(zip(near, far))
    ]
    for copy in copies:
        copy.start()
    unpack_half(1 - section[0], other, lw, bw, vw, stage, stage_b, sems)
    for copy in copies:
        copy.wait()


def numbers_kernel(
    options,
    depth,
    targets,
    destination,
    b1,
    b2,
    lb,
    bb,
    hw,
    vb,
    ow,
    hb,
    ob,
    out,
    table,
):
    levels, kinds = options.shape[0], targets.shape[0]
    slots = depth.shape[1]
    rows = [options[...].astype(F32), depth[...].astype(F32)]
    rows += [targets[k] for k in range(kinds)]
    rows.append(jnp.zeros((LANES - levels - 1 - kinds * levels, slots), F32))
    out[...] = jnp.transpose(jnp.concatenate(rows, axis=0))
    table[...] = jnp.zeros_like(table)
    table[0 : bb.shape[0], :] = bb[...]
    table[AT_VB, :] = vb[...]
    table[AT_OW, :] = ow[...].astype(F32)
    table[AT_HW, :] = hw[...].astype(F32)
    table[AT_LB, :] = lb[...]
    table[AT_B1, 0 : b1.shape[1]] = b1[...]
    table[AT_B2, 0 : b2.shape[1]] = b2[...]
    lane = iota((1, LANES), 1)
    scalars = jnp.zeros((1, LANES), F32)
    for k, value in ((1, hb[:, 0:1]), (2, hb[:, 1:2]), (3, ob[...])):
        scalars = jnp.where(lane == k, value, scalars)
    table[AT_SCALARS, :] = scalars
    for k in range(slots // LANES):
        part = destination[:, k * LANES : (k + 1) * LANES]
        table[AT_DEST + k : AT_DEST + k + 1, :] = part.astype(F32)


def whole(shape):
    zeros = (0,) * len(shape)
    return pl.BlockSpec(shape, lambda *_: zeros)


ANYWHERE = pl.BlockSpec(memory_space=pl.ANY)
SCALARS = pl.BlockSpec(memory_space=pltpu.SMEM)


def params():
    return pltpu.CompilerParams(vmem_limit_bytes=VMEM_BYTES)


def shape_of(*shape, dtype=F32):
    return jax.ShapeDtypeStruct(shape, dtype)


def cost(microseconds):
    return pl.CostEstimate(
        flops=int(1.1e9 * microseconds), bytes_accessed=int(3.6e6 * microseconds), transcendentals=0
    )


def stays(value):
    return pltpu.with_memory_space_constraint(value, pltpu.HBM)


def held_near(value):
    return pltpu.with_memory_space_constraint(value, pltpu.VMEM)


def encode(section, frames, w1t, w2t, lw, table):
    img = frames.shape[0]
    blocks = img // 4
    side = blocks - 1
    k1, k2, width = w1t.shape[0], w2t.shape[0], lw.shape[1]
    flat = lw.shape[0]
    vmem = pltpu.VMEM
    near = pl.BlockSpec(memory_space=vmem)
    grid_one = (blocks, side, k1, LANES)
    return pl.pallas_call(
        encode_kernel,
        in_specs=[SCALARS, ANYWHERE, near, near, ANYWHERE, near],
        out_specs=[ANYWHERE] * 3 + [near] * 3,
        out_shape=(
            pltpu.HBM(grid_one, BF16),
            pltpu.HBM(grid_one, BF16),
            pltpu.HBM((flat, LANES), BF16),
            shape_of(flat, LANES, dtype=BF16),
            shape_of(width, LANES, dtype=BF16),
            shape_of(width, LANES),
        ),
        scratch_shapes=[
            vmem((img, img, frames.shape[2], LANES), BF16),
            vmem(lw.shape, BF16),
            vmem(grid_one, BF16),
            vmem(grid_one, BF16),
            vmem((flat, LANES), BF16),
            vmem((2 * REACH * k1, 256), BF16),
            vmem((2 * k1, 64), BF16),
            vmem((6 * k2, LANES), BF16),
            vmem((k1, LANES), F32),
            vmem((k2, LANES), F32),
            vmem((side, k1, LANES), F32),
            vmem((side // 2 - 1, k2, LANES), F32),
            pltpu.SemaphoreType.DMA((4, max(blocks // STEP, 3))),
        ],
        compiler_params=params(),
        cost_estimate=cost(9),
        name="encode",
    )(section, frames, w1t, w2t, lw, table)


def plan(section, slots, enc, s3, h2, branch_w, value_w, table, per_pair, depth, half_rows):
    width = enc.shape[0]
    options = branch_w.shape[0]
    two = 2 * width
    pairs = options // 2
    outs = (
        shape_of(half_rows, LANES, dtype=BF16),
        shape_of(half_rows // 2, LANES, dtype=BF16),
        shape_of(half_rows // 2, LANES, dtype=BF16),
        shape_of(TABLE, LANES),
        shape_of(width, LANES, dtype=BF16),
    )
    vmem = pltpu.VMEM
    near = pl.BlockSpec(memory_space=vmem)
    return pl.pallas_call(
        functools.partial(plan_kernel, per_pair=per_pair, depth=depth),
        in_specs=[SCALARS, near, near, near, near, ANYWHERE, near, near],
        out_shape=outs,
        scratch_shapes=[
            vmem((2, half_rows, LANES), BF16),
            vmem((options * width, width + 16), BF16),
            vmem((width + 16, width + 16), BF16),
            vmem((width, width + 16), BF16),
            vmem((width, LANES), F32),
            vmem((16, LANES), F32),
            vmem((options * width, LANES), F32),
            vmem((depth, options * width, LANES), F32),
            vmem((depth, pairs, width, two), F32),
            vmem((depth, pairs, width + 16, two), BF16),
            vmem((depth, pairs, width, two), BF16),
            vmem((depth, options * width, LANES), BF16),
            vmem(branch_w.shape, BF16),
            pltpu.SemaphoreType.DMA,
        ],
        compiler_params=params(),
        cost_estimate=cost(11),
        name="plan",
    )(section, slots, enc, s3, h2, branch_w, value_w, table)


def back(g3, lw, s2, s1, h1, w2t):
    _, side, k1 = s1.shape[:3]
    k2 = w2t.shape[0]
    inner = side // 2 - 1
    padded = (side + 2, side, k1, LANES)
    near = pl.BlockSpec(memory_space=pltpu.VMEM)
    return pl.pallas_call(
        back_kernel,
        in_specs=[near] * 6,
        out_shape=(shape_of(*padded, dtype=BF16), shape_of(k2, 256), shape_of(8, LANES)),
        scratch_shapes=[
            pltpu.VMEM((LANES, 6 * k2), BF16),
            pltpu.VMEM((inner + 2, inner, k2, LANES), BF16),
        ],
        compiler_params=params(),
        cost_estimate=cost(25),
        name="back",
    )(g3, lw, s2, s1, h1, w2t)


def first(section, frames, g1, w1t, other, after, channels, draw):
    img, _, stack, _ = frames.shape
    k1 = g1.shape[2]
    band = (STEP * 4 * COLS * channels, (STEP + 1) * NEAR * k1)
    near = pl.BlockSpec(memory_space=pltpu.VMEM)
    return pl.pallas_call(
        functools.partial(first_kernel, draw=draw),
        in_specs=[SCALARS, ANYWHERE, near, near, ANYWHERE, ANYWHERE],
        out_specs=[near, ANYWHERE, near],
        out_shape=[
            shape_of(2 * k1, LANES, dtype=BF16),
            shape_of(img, img, channels, 2 * LANES),
            shape_of(*band, dtype=BF16),
        ],
        scratch_shapes=[
            pltpu.VMEM((img, img, stack, LANES), BF16),
            pltpu.VMEM((STEP * 4 * COLS * stack, (STEP + 1) * NEAR * k1), F32),
            pltpu.VMEM((STEP * draw + 1,) + g1.shape[1:], BF16),
            pltpu.VMEM((2, 2, 4 * STEP, img, channels, LANES), F32),
            pltpu.SemaphoreType.DMA((img // 4 // STEP + 1,)),
            pltpu.SemaphoreType.DMA((2, 2)),
        ],
        compiler_params=params(),
        cost_estimate=cost(45),
        name="first",
    )(section, frames, g1, w1t, other, after)


def pixels(section, band, mine, other, after, done, start):
    img, _, channels, _ = done.shape
    steps = img // 4 // STEP - start
    near = pl.BlockSpec(memory_space=pltpu.VMEM)
    return pl.pallas_call(
        functools.partial(pixels_kernel, start=start),
        in_specs=[SCALARS, near, near, ANYWHERE, ANYWHERE, ANYWHERE],
        out_specs=[ANYWHERE, near],
        out_shape=[shape_of(*done.shape), shape_of(8, LANES)],
        scratch_shapes=[
            pltpu.VMEM((2, 2, 4 * STEP, img, channels, LANES), F32),
            pltpu.VMEM((STEP * steps + 1,) + mine.shape[1:], BF16),
            pltpu.SemaphoreType.DMA((3, 2)),
        ],
        input_output_aliases={5: 0},
        compiler_params=params(),
        cost_estimate=cost(1 + 0.9 * steps),
        name="pixels",
    )(section, band, mine, other, after, done)


def small_call(
    kernel, outs, operands, scratch=(), name=None, place=None, after=(), weight=0.3, far=False
):
    specs = [pl.BlockSpec(memory_space=pltpu.VMEM)] * len(operands)
    if place is not None:
        operands = (*place, *operands)
        specs = [pl.BlockSpec(memory_space=pltpu.SMEM)] * len(place) + specs
    return pl.pallas_call(
        kernel,
        in_specs=specs + [ANYWHERE] * len(after),
        out_specs=jax.tree.map(
            lambda _: ANYWHERE if far else pl.BlockSpec(memory_space=pltpu.VMEM), outs
        ),
        out_shape=outs,
        scratch_shapes=list(scratch),
        compiler_params=params(),
        cost_estimate=cost(weight),
        name=name,
    )(*operands, *after)


def round_up(value, step):
    return -(-value // step) * step


def swapped(value):
    return lax.ppermute(value, "section", [(0, 1), (1, 0)])


def exchanged(value, groups=None):
    return lax.all_to_all(
        value, "batch", split_axis=0, concat_axis=0, axis_index_groups=groups, tiled=True
    )


def partner(value, distance):
    count = lax.axis_size("batch")
    return lax.ppermute(value, "batch", [(b, b ^ distance) for b in range(count)])


def local(
    frames,
    destination,
    options,
    depth,
    targets,
    conv_one,
    bias_one,
    conv_two,
    bias_two,
    linear_w,
    linear_b,
    branch_w,
    branch_b,
    head_w,
    head_b,
    value_w,
    value_b,
    out_w,
    out_b,
):
    section = lax.axis_index("section").astype(jnp.int32)[None]
    peers = lax.axis_size("batch")
    frame_count = frames.shape[3]
    per_pair = frame_count // peers
    levels = options.shape[0]
    frames = stays(frames.transpose(1, 2, 0, 3))
    w1t, w2t = stays(conv_one.T), stays(conv_two.T)
    branch_w, value_w = stays(branch_w), stays(value_w)
    encoder_params = (w1t, bias_one, w2t, bias_two, linear_w, linear_b)
    planner_params = (branch_w, branch_b, head_w.T, head_b, value_w, value_b, out_w.T, out_b)
    width = linear_w.shape[1]
    big_rows = linear_w.shape[0] + (branch_w.shape[0] + 1) * width
    size = round_up(-(-big_rows // (2 * CUBE)), 16)

    tiny = (bias_one, bias_two, linear_b, branch_b, head_w.T, value_b, out_w.T)
    tiny = [stays(v if v.ndim > 1 else v[None, :]) for v in tiny]
    numbers, table = pl.pallas_call(
        numbers_kernel,
        in_specs=[pl.BlockSpec(memory_space=pltpu.VMEM)] * (6 + len(tiny)),
        out_shape=[shape_of(frame_count, LANES), shape_of(TABLE, LANES)],
        compiler_params=params(),
        cost_estimate=cost(1),
        name="numbers",
    )(
        stays(options),
        stays(depth[None, :]),
        stays(targets),
        stays(destination[None, :]),
        *tiny,
        stays(head_b[None, :]),
        out_b[None, :],
    )
    slots = exchanged(numbers.reshape(peers, per_pair, LANES)).reshape(frame_count, LANES)

    h1, s1, s2, h2, enc, s3 = encode(section, frames, w1t, w2t, stays(linear_w), table)
    keep, send_one, send_two, small, g3 = plan(
        section, slots, enc, s3, h2, branch_w, value_w, table, per_pair, levels, CUBE * size
    )
    recv = swapped(send_one), swapped(send_two)
    channels = frames.shape[2] // lax.axis_size("section")
    g1, c2, sums = back(g3, linear_w, s2, s1, h1, w2t)
    other = swapped(g1)
    g1 = held_near(g1)
    cubes = [list(range(c, c + CUBE)) for c in range(0, peers, CUBE)]
    bf16 = functools.partial(shape_of, dtype=BF16)
    pieces = small_call(
        merge_kernel,
        bf16(CUBE, size + 2 * SHORT, LANES),
        (keep, *recv, small, c2, sums),
        [
            pltpu.VMEM((CUBE * SHORT, LANES), F32),
            pltpu.VMEM((CUBE, size + 2 * SHORT, LANES), BF16),
            pltpu.SemaphoreType.DMA((CUBE,)),
        ],
        name="merge",
        far=True,
        weight=30,
    )
    got = exchanged(pieces, cubes)
    c1, frames_grad, band = first(section, frames, g1, w1t, other, pieces, channels, DRAW)
    piece = bf16(size + 2 * SHORT + c1.shape[0], LANES)
    keep = small_call(cube_kernel, piece, (got, c1), name="cube")
    distance = CUBE
    while distance < peers:
        recv = partner(keep, distance)
        if distance == CUBE:
            frames_grad, token = pixels(section, band, g1, other, keep, frames_grad, DRAW)
        distance *= 2
        keep = small_call(add_kernel, piece, (keep, recv), name="add", after=(token,))
    parts = [keep] + [partner(keep, k) for k in range(1, CUBE)]
    place = (lax.axis_index("batch").astype(jnp.int32)[None],)
    got = small_call(
        relay_kernel,
        [bf16(CUBE // 2, *piece.shape)] * 2,
        parts,
        [pltpu.VMEM((CUBE, *piece.shape), BF16)],
        name="relay",
        place=place,
    )
    got_other = [swapped(v) for v in got]
    shapes = [p.shape for p in encoder_params + planner_params]
    near = pl.BlockSpec(memory_space=pltpu.VMEM)
    flat = [shape_of(*(v if len(v) > 1 else (1,) + v)) for v in [(1, 1)] + shapes]
    large = [flat[k] for k in (5, 7, 11)]
    staged = [
        pltpu.VMEM((CUBE * size, LANES), F32),
        pltpu.VMEM(branch_w.shape, F32),
    ]
    little = [v for k, v in enumerate(flat) if k not in (5, 7, 11)]
    sems = pltpu.SemaphoreType.DMA((CUBE + len(little),))
    begun = pl.pallas_call(
        own_kernel,
        in_specs=[SCALARS, near, near],
        out_specs=[ANYWHERE] * 3,
        out_shape=large,
        scratch_shapes=[*staged, sems],
        compiler_params=params(),
        cost_estimate=cost(1),
        name="own",
    )(section, *got)
    ends = pl.pallas_call(
        unpack_kernel,
        in_specs=[SCALARS] + [near] * 4 + [ANYWHERE] * 3,
        out_specs=[ANYWHERE] * (3 + len(little)),
        out_shape=large + little,
        scratch_shapes=[pltpu.VMEM(v.shape, F32) for v in little]
        + [*staged, pltpu.VMEM((CUBE * SHORT, LANES), F32), sems],
        input_output_aliases={5: 0, 6: 1, 7: 2},
        compiler_params=params(),
        cost_estimate=cost(1.5),
        name="unpack",
    )(section, *got, *got_other, *begun)
    rest = list(ends[3:])
    for k, at in enumerate((5, 7, 11)):
        rest.insert(at, ends[k])
    rest = [v.reshape(s) for v, s in zip(rest, [()] + shapes)]
    for at in (1, 3, 9, 13):
        rest[at] = rest[at].T
    return (rest[0], frames_grad.transpose(2, 0, 1, 3), *rest[1:])


def solution(mesh):
    placed = (
        P(None, None, None, "batch"),
        P("batch"),
        P(None, "batch"),
        P("batch"),
        P(None, None, "batch"),
    ) + (P(),) * 14
    return jax.shard_map(
        local,
        mesh=mesh,
        in_specs=placed,
        out_specs=(P(), P("section", None, None, "batch")) + (P(),) * 14,
        check_vma=False,
    )
```

```python
import functools
import math

import jax
import jax.numpy as jnp
from jax import lax
from jax.experimental import pallas as pl
from jax.experimental.pallas import tpu as pltpu
from jax.sharding import PartitionSpec as P

BF16 = jnp.bfloat16
F32 = jnp.float32
EXACT = lax.Precision.HIGHEST
LANES = 128
VMEM_BYTES = 32 * 1024 * 1024
TILE = 16
REACH = 5
STEP = 3
COLS = 12
NEAR = 4
AT_VB, AT_OW, AT_HW, AT_LB, AT_SCALARS, AT_B1, AT_B2, AT_DEST = (
    slice(18, 19),
    slice(19, 20),
    slice(20, 22),
    slice(22, 23),
    slice(23, 24),
    slice(24, 25),
    slice(25, 26),
    26,
)
TABLE = 32
CUBE = 8
DRAW = 4
SHORT = 16


def dot(a, b, precision=None):
    return jnp.dot(a, b, preferred_element_type=F32, precision=precision)


def dot_rows(a, b, precision=None):
    return lax.dot_general(
        a, b, (((0,), (0,)), ((), ())), preferred_element_type=F32, precision=precision
    )


def dot_lanes(a, b, precision=None):
    return lax.dot_general(
        a, b, (((1,), (1,)), ((), ())), preferred_element_type=F32, precision=precision
    )


def iota(shape, axis):
    return lax.broadcasted_iota(jnp.int32, shape, axis)


def column(row):
    n = row.shape[1]
    wide = jnp.broadcast_to(row, (n, n))
    return jnp.sum(jnp.where(iota((n, n), 0) == iota((n, n), 1), wide, 0.0), axis=1, keepdims=True)


def row_of(col):
    n = col.shape[0]
    wide = jnp.broadcast_to(col, (n, n))
    return jnp.sum(jnp.where(iota((n, n), 0) == iota((n, n), 1), wide, 0.0), axis=0, keepdims=True)


def soft(x):
    t = jnp.tanh(0.5 * x)
    return jnp.maximum(x, 0.0) - jnp.log(0.5 + 0.5 * jnp.abs(t)), 0.5 + 0.5 * t


def silu_pair(x):
    s = 0.5 + 0.5 * jnp.tanh(0.5 * x)
    act = x * s
    return act, s + act * (1.0 - s)


def pixel_order(w1t):
    tap, pix = iota((256, 256), 0), iota((256, 256), 1)
    moves = ((tap >> 6) == (pix & 3)) & ((tap & 63) == (pix >> 2))
    return dot(w1t, moves.astype(F32).astype(BF16))


def frame_copies(section, far, here, sems):
    lanes = pl.ds(pl.multiple_of(section[0] * LANES, LANES), LANES)
    size = 4 * STEP

    def copy(g):
        rows = pl.ds(pl.multiple_of(g * size, size), size)
        return pltpu.make_async_copy(far.at[rows, :, :, lanes], here.at[rows], sems.at[g])

    return copy


def tile_rows(frames, row, j, cols):
    img, _, channels, _ = frames.shape
    flat = frames.reshape(img, img * channels, LANES)
    size = cols * channels
    end = min((j + 1) * size, img * channels)
    part = flat[pl.ds(row, 4), j * size : end, :]
    return part.reshape(4 * (end - j * size), LANES)


def encode_kernel(
    section,
    frames_far,
    w1t,
    w2t,
    lw_far,
    table,
    h1_far,
    s1_far,
    s2_far,
    h2,
    enc,
    s3,
    frames,
    lw,
    h1,
    s1,
    s2,
    band,
    edge,
    band2,
    bias1,
    bias2,
    held,
    held2,
    sems,
):
    blocks, side = h1.shape[:2]
    steps = blocks // STEP
    tiles = frames.shape[1] // TILE
    k1, k2 = w1t.shape[0], w2t.shape[0]
    reach_rows = REACH * k1
    arrives = frame_copies(section, frames_far, frames, sems.at[0])
    for g in range(steps):
        arrives(g).start()
    last_copies = [
        pltpu.make_async_copy(lw_far, lw, sems.at[3, 0]),
        pltpu.make_async_copy(s2, s2_far, sems.at[3, 1]),
    ]
    last_copies[0].start()

    def leaves(g):
        rows = pl.ds(g * STEP, STEP)
        return [
            pltpu.make_async_copy(h1.at[rows], h1_far.at[rows], sems.at[1, g]),
            pltpu.make_async_copy(s1.at[rows], s1_far.at[rows], sems.at[2, g]),
        ]

    inner = side // 2 - 1
    row_len = inner * k2
    two = 2 * k2 * 3

    def prepare():
        taps = pixel_order(w1t[...])
        edges = []
        for half in range(2):
            lines = [taps[:, 32 * (4 * half + u) : 32 * (4 * half + u + 1)] for u in range(4)]
            for place in range(REACH):
                pieces = []
                for line in lines:
                    start = 16 * (place - 1)
                    cut = line[:, max(0, -start) : min(32, 64 - start)]
                    start = max(start, 0)
                    pieces += [jnp.zeros((k1, start), F32)] if start else []
                    pieces.append(cut)
                    rest = 64 - start - cut.shape[1]
                    pieces += [jnp.zeros((k1, rest), F32)] if rest else []
                at = half * reach_rows + place * k1
                band[at : at + k1, :] = jnp.concatenate(pieces, axis=1).astype(BF16)
            edges.append(jnp.concatenate([line[:, 16:] for line in lines], axis=1))
        edge[...] = jnp.concatenate(edges, axis=0).astype(BF16)
        tap, pix = iota((256, LANES), 0), iota((256, LANES), 1)
        for half in range(2):
            for place in range(3):
                hit = (
                    ((tap & 15) == (pix & 15))
                    & ((tap >> 6) == (pix >> 6) + 2 * half)
                    & (((tap >> 4) & 3) == ((pix >> 4) & 3) + 2 - 2 * place)
                )
                at = (half * 3 + place) * k2
                taps = dot(w2t[...], hit.astype(F32).astype(BF16))
                band2[at : at + k2, :] = taps.astype(BF16)
        bias1[...] = jnp.broadcast_to(column(table[AT_B1, 0:k1]), bias1.shape)
        bias2[...] = jnp.broadcast_to(column(table[AT_B2, 0:k2]), bias2.shape)
        h1[0] = jnp.zeros(h1.shape[1:], BF16)
        s1[0] = jnp.zeros(s1.shape[1:], BF16)

    def added(sums, x, value):
        sums[x] = sums[x] + value if x in sums else value

    def second_matmul(b):
        parts = [
            h1[2 * b + 1 : 2 * b + 3, 4 * j : 4 * j + 4].reshape(LANES, LANES)
            for j in range(side // 4)
        ]
        return dot(band2[...], jnp.concatenate(parts, axis=1))

    def second_rows(b, got):
        low, high = {}, {}
        for j in range(side // 4):
            for place in range(3):
                x = 2 * j - 1 + place
                if 0 <= x < inner:
                    span = slice(j * LANES, (j + 1) * LANES)
                    at = place * k2
                    added(low, x, got[at : at + k2, span])
                    added(high, x, got[two // 2 + at : two // 2 + at + k2, span])
        for x in range(inner):
            if b:
                value, slope = soft(held2[x] + high[x] + bias2[...])
                at = slice((b - 1) * row_len + x * k2, (b - 1) * row_len + (x + 1) * k2)
                h2[at, :] = value.astype(BF16)
                s2[at, :] = slope.astype(BF16)
            held2[x] = low[x]

    lows, highs = [{} for _ in range(blocks)], [{} for _ in range(blocks)]

    def place_tiles(spots, got):
        for i, (b, j) in enumerate(spots):
            part = got[:, i * LANES : (i + 1) * LANES]
            for place in range(REACH):
                x = 4 * j - 1 + place
                if 0 <= x < side:
                    at = place * k1
                    added(lows[b], x, part[at : at + k1])
                    added(highs[b], x, part[reach_rows + at : reach_rows + at + k1])

    def finish(b, xs):
        for x in xs:
            if b:
                value, slope = soft(held[x] + highs[b][x] + bias1[...])
                h1[b, x] = value.astype(BF16)
                s1[b, x] = slope.astype(BF16)
            held[x] = lows[b][x]

    def tile(b, j):
        return tile_rows(frames, 4 * b, j, TILE)

    def full(spots, ready=None):
        def issue():
            for b, _ in spots:
                if b % STEP == 0 and b not in arrived:
                    arrived.add(b)
                    arrives(b // STEP).wait()
            return dot(band[...], jnp.concatenate([tile(*spot) for spot in spots], axis=1))

        def take(got):
            place_tiles(spots, got)
            if ready:
                finish(*ready)

        return issue, take

    def edges(g):
        def issue():
            parts = [tile(STEP * g + r, tiles) for r in range(STEP)]
            return dot(edge[...], jnp.concatenate(parts, axis=1))

        def take(got):
            for r in range(STEP):
                span = slice(r * LANES, (r + 1) * LANES)
                added(lows[STEP * g + r], side - 1, got[:k1, span])
                added(highs[STEP * g + r], side - 1, got[k1:, span])

        return issue, take

    def leave(g):
        def take(_):
            for copy in leaves(g):
                copy.start()

        return (lambda: None), take

    total = {}

    def linear(row):
        def issue():
            at = slice(row * row_len, (row + 1) * row_len)
            return dot_rows(lw[at, :], h2[at, :])

        return issue, functools.partial(added, total, 0)

    arrived = set()
    units, later, summed = [], [], 0
    for b in range(blocks):
        mine = []
        if b % 2 == 0:
            mine.append(full([(k, tiles - 1) for k in (b, b + 1) if k < blocks]))
        if b % STEP == 0:
            mine.append(edges(b // STEP))
        done = 0
        for j in range(0, tiles - 1, 2):
            ready = side if j + 2 == tiles - 1 else 4 * j + 7
            mine.append(full([(b, j), (b, j + 1)], (b, range(done, ready))))
            done = ready
        units += mine[:1] + later + mine[1:]
        later = []
        if b % STEP == STEP - 1:
            later.append(leave(b // STEP))
        if b % 2 == 0 and b >= 2:
            pair = b // 2 - 1
            later.append(
                (functools.partial(second_matmul, pair), functools.partial(second_rows, pair))
            )
        if b % 2 == 1 and b >= 5:
            later.append(linear(summed))
            summed += 1
    nothing = (lambda: None), (lambda got: None)
    units += [nothing] + later + [nothing]
    units += [linear(row) for row in range(summed, inner)]

    prepare()
    last_copies[0].wait()
    waiting = None
    for issue, take in units:
        got = issue()
        if waiting is not None:
            waiting[0](waiting[1])
        waiting = (take, got)
    waiting[0](waiting[1])
    last_copies[1].start()
    value, slope = soft(total[0] + column(table[AT_LB, :]))
    enc[...] = value.astype(BF16)
    s3[...] = slope
    for g in range(steps):
        for copy in leaves(g):
            copy.wait()
    last_copies[1].wait()


def three_parts(row):
    high = row.astype(BF16).astype(F32)
    middle = (row - high).astype(BF16).astype(F32)
    return jnp.concatenate([high, middle, row - high - middle], axis=0)


def with_ones(value):
    return jnp.concatenate([value, ones_rows(value.shape[1])], axis=0)


def ones_rows(lanes):
    return (iota((16, lanes), 0) < 3).astype(F32).astype(BF16)


def plan_kernel(
    section,
    slots,
    enc,
    s3,
    h2,
    branch_far,
    value_w,
    table,
    keep,
    send_one,
    send_two,
    small,
    g3,
    parts,
    bwt,
    vht,
    vhw,
    ow,
    mine,
    dbr,
    dval,
    low,
    hid,
    gb,
    branch_w,
    sem,
    *,
    per_pair,
    depth,
):
    width = enc.shape[0]
    options = branch_w.shape[0]
    pairs = options // 2
    two = 2 * width
    sec = section[0]
    branch_copy = pltpu.make_async_copy(branch_far, branch_w, sem)
    branch_copy.start()

    count = slots.shape[0]
    dest = jnp.concatenate(
        [table[AT_DEST + k : AT_DEST + k + 1, :] for k in range(count // LANES)], axis=1
    )
    own = jnp.where(sec == 0, dest[:, :LANES], dest[:, LANES:])
    others = jnp.transpose(jnp.broadcast_to(dest, (LANES, count)))
    index = iota((count, LANES), 1) + sec * LANES
    earlier = (others == own) & (iota((count, LANES), 0) < index)
    rank = jnp.sum(earlier.astype(F32), axis=0, keepdims=True)
    bucket = own * float(per_pair) + rank
    chosen = (iota((count, LANES), 0).astype(F32) == bucket).astype(F32).astype(BF16)
    numbers = slots[...]
    high = numbers.astype(BF16)
    middle = (numbers - high.astype(F32)).astype(BF16)
    rest = (numbers - high.astype(F32) - middle.astype(F32)).astype(BF16)
    mine[...] = sum(dot_rows(v, chosen) for v in (rest, middle, high))[: mine.shape[0]]

    pad = jnp.zeros((13, width), F32)
    branch_copy.wait()
    for o in range(options):
        rows = [branch_w[o].astype(F32), three_parts(table[o : o + 1, :]), pad]
        bwt[o * width : (o + 1) * width, :] = jnp.transpose(
            jnp.concatenate(rows, axis=0)
        ).astype(BF16)
    scalars = table[AT_SCALARS, :]
    head_w = table[AT_HW, :]
    rows = [value_w[...].astype(F32), three_parts(table[AT_VB, :]), pad]
    vht[0:width, :] = jnp.transpose(jnp.concatenate(rows, axis=0)).astype(BF16)
    vht[width:, :] = jnp.zeros((16, width + 16), BF16)
    lane = iota((1, 16), 1)
    for k in range(2):
        bias = three_parts(jnp.broadcast_to(scalars[:, 1 + k : 2 + k], (1, 16)))
        bias = sum(jnp.where(lane == j, bias[j : j + 1], 0.0) for j in range(3))
        vht[width + k : width + k + 1, 0:width] = head_w[k : k + 1].astype(BF16)
        vht[width + k : width + k + 1, width:] = bias.astype(BF16)
    vhw[:, 0:width] = value_w[...]
    vhw[:, width:] = jnp.transpose(
        jnp.concatenate([head_w, jnp.zeros((14, width), F32)], axis=0)
    ).astype(BF16)
    ow[...] = jnp.broadcast_to(column(table[AT_OW, :]), (width, LANES))
    wide_ow = jnp.concatenate([ow[...], ow[...]], axis=1)

    labels = iota((options, LANES), 0).astype(F32)
    state = enc[...].astype(F32)
    rounded_all, saved = [], []

    def loss_terms(level, picked, reward, discount, value):
        reward = jnp.concatenate(reward, axis=0)
        discount = jax.nn.sigmoid(jnp.concatenate(discount, axis=0))
        value = jnp.concatenate(value, axis=0) + scalars[:, 3:4]
        quality = reward + discount * value
        top = jnp.max(quality, axis=0, keepdims=True)
        shifted = jnp.exp(quality - top)
        total = jnp.sum(shifted, axis=0, keepdims=True)
        live = (mine[depth : depth + 1, :] > level).astype(F32)
        chosen = picked.astype(F32)

        def target(kind):
            at = depth + 1 + kind * depth + level
            return mine[at : at + 1, :]

        reward_gap = live * (jnp.sum(chosen * reward, axis=0, keepdims=True) - target(0))
        discount_gap = live * (jnp.sum(chosen * discount, axis=0, keepdims=True) - target(1))
        plan_gap = live * (top + jnp.log(total) - target(2))
        grad_quality = plan_gap * (shifted / total)
        head_two = (chosen * discount_gap + grad_quality * value) * discount * (1.0 - discount)
        saved.append(
            (
                picked,
                (chosen * reward_gap + grad_quality).astype(BF16).astype(F32),
                head_two.astype(BF16).astype(F32),
                (grad_quality * discount).astype(BF16).astype(F32),
                reward_gap * reward_gap + discount_gap * discount_gap + plan_gap * plan_gap,
            )
        )

    def value_part(level, t, got, reward, discount, value):
        act, slope = silu_pair(got[:width])
        dval[level, t] = slope
        hidden = act.astype(BF16)
        hid[level, t] = hidden
        worth = jnp.sum(hidden.astype(F32) * wide_ow, axis=0, keepdims=True)
        for k in range(2):
            span = slice(k * LANES, (k + 1) * LANES)
            value.append(worth[:, span])
            reward.append(got[width : width + 1, span])
            discount.append(got[width + 1 : width + 2, span])

    waiting, ending = None, None
    for level in range(depth):
        picked = labels == mine[level : level + 1, :]
        rounded = state.astype(BF16)
        rounded_all.append(rounded)
        rounded = with_ones(rounded)
        following = state
        rows = ([], [], [])
        branch = dot(bwt[0:two, :], rounded)
        for t in range(pairs):
            at = slice(t * two, (t + 1) * two)
            upcoming = dot(bwt[(t + 1) * two : (t + 2) * two, :], rounded) if t + 1 < pairs else None
            act, slope = silu_pair(branch)
            dbr[level, at, :] = slope
            left = state + act[:width]
            right = state + act[width:]
            following = jnp.where(picked[2 * t : 2 * t + 1], left, following)
            following = jnp.where(picked[2 * t + 1 : 2 * t + 2], right, following)
            both = with_ones(jnp.concatenate([left.astype(BF16), right.astype(BF16)], axis=1))
            low[level, t] = both
            got = dot(vht[...], both)
            if waiting is not None:
                value_part(*waiting)
            waiting = (level, t, got, *rows)
            if t == 2 and ending is not None:
                loss_terms(*ending)
            branch = upcoming
        ending = (level, picked, *rows)
        state = following
    value_part(*waiting)
    loss_terms(*ending)

    out_sum = jnp.zeros((width, two), F32)
    value_sum = jnp.zeros((width + 16, width + 16), F32)
    line = iota((16, two), 0)
    grads_next = [jnp.zeros((width, LANES), F32)]

    def branch_part(level, t, moved, upward):
        picked, grad_next = saved[level][0], grads_next[-1]
        at = slice(t * two, (t + 1) * two)
        left = moved[:, :LANES] + jnp.where(picked[2 * t : 2 * t + 1], grad_next, 0.0)
        right = moved[:, LANES:] + jnp.where(picked[2 * t + 1 : 2 * t + 2], grad_next, 0.0)
        grad_branch = jnp.concatenate([left, right], axis=0) * dbr[level, at, :]
        grad_branch = grad_branch.astype(BF16)
        gb[level, at, :] = grad_branch
        weights = jnp.concatenate([branch_w[2 * t], branch_w[2 * t + 1]], axis=1)
        part = left + right + dot(weights, grad_branch)
        upward = part if upward is None else upward + part
        if t == pairs - 1:
            grads_next.append(upward)
            return None
        return upward

    waiting, upward = None, None
    for level in reversed(range(depth)):
        _, head_one, head_two, grad_value, _ = saved[level]
        for t in range(pairs):

            def across(rows):
                return jnp.concatenate(
                    [rows[2 * t : 2 * t + 1], rows[2 * t + 1 : 2 * t + 2]], axis=1
                )

            worth = across(grad_value)
            grad_pre = (worth * wide_ow * dval[level, t]).astype(BF16)
            out_sum = out_sum + hid[level, t].astype(F32) * worth
            heads = jnp.where(line == 0, across(head_one), 0.0)
            heads = jnp.where(line == 1, across(head_two), heads)
            heads = jnp.where(line == 2, worth, heads)
            stacked = jnp.concatenate([grad_pre, heads.astype(BF16)], axis=0)
            moved = dot(vhw[...], stacked)
            value_sum = value_sum + dot_lanes(stacked, low[level, t])
            if waiting is not None:
                upward = branch_part(*waiting, upward)
            waiting = (level, t, moved)
    branch_part(*waiting, upward)
    grad_next = grads_next[-1]

    linear_rows = h2.shape[0]
    half = (linear_rows + options * width + width) // 2
    rest = linear_rows - half
    rounded = with_ones(jnp.concatenate(rounded_all, axis=1))
    small[...] = jnp.zeros_like(small)
    if half < keep.shape[0]:
        for k in range(2):
            parts[k, half:, :] = jnp.zeros((keep.shape[0] - half, LANES), BF16)
    for t in range(pairs):
        at = slice(t * two, (t + 1) * two)
        grads = jnp.concatenate([gb[level, at, :] for level in range(depth)], axis=1)
        got = dot_lanes(rounded, grads)
        for k in range(2):
            o = 2 * t + k
            span = slice(k * width, (k + 1) * width)
            rows = slice(rest + o * width, rest + (o + 1) * width)
            parts[1 - sec, rows, :] = got[:width, span].astype(BF16)
            small[o : o + 1, :] = got[width : width + 1, span]
    after = rest + options * width
    parts[1 - sec, after : after + width, :] = jnp.transpose(value_sum[:width, :width]).astype(BF16)

    grad_three = (grad_next.astype(BF16).astype(F32) * s3[...]).astype(BF16)
    g3[...] = grad_three
    chunk = linear_rows // 9
    for i in range(8):
        at = slice(i * chunk, (i + 1) * chunk)
        parts[sec, at, :] = dot_lanes(h2[at, :], grad_three).astype(BF16)
    last = dot_lanes(h2[8 * chunk :, :], grad_three).astype(BF16)
    parts[sec, 8 * chunk : half, :] = last[: half - 8 * chunk]
    parts[1 - sec, 0:rest, :] = last[half - 8 * chunk :]
    keep[...] = parts[0]
    send_one[...] = parts[1, : send_one.shape[0]]
    send_two[...] = parts[1, send_one.shape[0] :]

    small[AT_VB, :] = row_of(value_sum[:width, width : width + 1])
    small[AT_OW, :] = row_of(jnp.sum(out_sum, axis=1, keepdims=True))
    small[AT_HW, :] = value_sum[width : width + 2, :width]
    small[AT_LB, :] = row_of(jnp.sum(grad_three.astype(F32), axis=1, keepdims=True))
    loss = 0.5 * jnp.sum(sum(kept[4] for kept in saved), axis=1, keepdims=True)
    ends = [loss] + [value_sum[width + k : width + k + 1, width : width + 1] for k in range(3)]
    lane = iota((1, LANES), 1)
    line = jnp.zeros((1, LANES), F32)
    for k, end in enumerate(ends):
        line = jnp.where(lane == k, end, line)
    small[AT_SCALARS, :] = line


def back_kernel(g3, lw, s2, s1, h1, w2t, g1, c2, sums, t2, g2):
    side, k1 = s1.shape[1], s1.shape[2]
    k2 = w2t.shape[0]
    inner = side // 2 - 1
    row_len = inner * k2
    tap, pix = iota((LANES, 256), 1), iota((LANES, 256), 0)
    for yrel in range(2):
        for p in range(3):
            hit = (
                ((tap & 15) == (pix & 15))
                & ((tap >> 6) == (pix >> 6) + 2 * (1 - yrel))
                & (((tap >> 4) & 3) == ((pix >> 4) & 3) + 2 - 2 * p)
            )
            at = (yrel * 3 + p) * k2
            t2[:, at : at + k2] = dot_lanes(hit.astype(F32).astype(BF16), w2t[...]).astype(BF16)
    g2[0] = jnp.zeros(g2.shape[1:], BF16)
    g2[inner + 1] = jnp.zeros(g2.shape[1:], BF16)
    g1[0] = jnp.zeros(g1.shape[1:], BF16)
    g1[side + 1] = jnp.zeros(g1.shape[1:], BF16)
    zero = jnp.zeros((k2, LANES), BF16)
    total_one = jnp.zeros((k1, LANES), F32)
    total_two = jnp.zeros((k2, LANES), F32)
    for y in range(inner):
        at = slice(y * row_len, (y + 1) * row_len)
        grad = dot(lw[at, :], g3[...]) * s2[at, :].astype(F32)
        grad = grad.astype(BF16).reshape(inner, k2, LANES)
        g2[y + 1] = grad
        total_two = total_two + jnp.sum(grad.astype(F32), axis=0)
    reach, cols = 5, 8
    total = jnp.zeros((2 * reach * k2, 2 * cols * k1), F32)
    grads, tiles = [], []
    for b in range(side // 2):
        cut = []
        for j in range(side // 4):
            pieces = []
            for yrel in range(2):
                for p in range(3):
                    x = 2 * j - 1 + p
                    pieces.append(g2[b + yrel, x] if 0 <= x < inner else zero)
            cut.append(jnp.concatenate(pieces, axis=0))
        got = dot(t2[...], jnp.concatenate(cut, axis=1))
        for u in range(2):
            for j in range(side // 4):
                part = got[u * 64 : (u + 1) * 64, j * LANES : (j + 1) * LANES]
                slope = s1[2 * b + u + 1, 4 * j : 4 * j + 4].astype(F32)
                grad = (part.reshape(4, k1, LANES) * slope).astype(BF16)
                g1[2 * b + u + 1, 4 * j : 4 * j + 4] = grad
                total_one = total_one + jnp.sum(grad.astype(F32), axis=0)
        for j in range(-(-side // cols)):
            end = min((j + 1) * cols, side)
            tile = h1[2 * b + 1 : 2 * b + 3, j * cols : end]
            if end < (j + 1) * cols:
                rest = jnp.zeros((2, (j + 1) * cols - end, k1, LANES), BF16)
                tile = jnp.concatenate([tile, rest], axis=1)
            tiles.append(tile.reshape(2 * cols * k1, LANES))
            pieces = []
            for half in range(2):
                for p in range(reach):
                    x = 4 * j - 1 + p
                    pieces.append(g2[b + 1 - half, x] if 0 <= x < inner else zero)
            grads.append(jnp.concatenate(pieces, axis=0))
        if b % 2:
            total = total + dot_lanes(
                jnp.concatenate(grads, axis=1), jnp.concatenate(tiles, axis=1)
            )
            grads, tiles = [], []
    line = 4 * k1
    for half in range(2):
        for u in range(2):
            tap_row = jnp.zeros((k2, line), F32)
            for p in range(reach):
                at = (half * reach + p) * k2
                part = total[at : at + k2, u * 2 * line : (u + 1) * 2 * line]
                start = 2 * k1 * (p - 1)
                piece = part[:, max(start, 0) : min(start + line, 2 * line)]
                if start < 0:
                    piece = jnp.concatenate([jnp.zeros((k2, -start), F32), piece], axis=1)
                if start + line > 2 * line:
                    rest = jnp.zeros((k2, start - line), F32)
                    piece = jnp.concatenate([piece, rest], axis=1)
                tap_row = tap_row + piece
            at = (2 * half + u) * line
            c2[:, at : at + line] = tap_row
    sums[...] = jnp.zeros_like(sums)
    sums[0:1, 0:k1] = row_of(jnp.sum(total_one, axis=1, keepdims=True))
    sums[1:2, 0:k2] = row_of(jnp.sum(total_two, axis=1, keepdims=True))


def pixel_band(sec, w1t, channels):
    k1 = w1t.shape[0]
    rows = 64 * channels
    row, tap = iota((rows, 256), 0), iota((rows, 256), 1)
    moves = ((tap >> 6) == row % channels + sec * channels) & ((tap & 63) == row // channels)
    taps = dot_lanes(moves.astype(F32).astype(BF16), w1t)
    line, span = COLS * channels, 8 * channels
    blocks = {}
    for half in range(2):
        for p in range(NEAR):
            pieces = []
            for u in range(4):
                at = (4 * half + u) * span
                start = 4 * (p - 1) * channels
                cut = taps[at + max(0, -start) : at + min(span, line - start)]
                start = max(start, 0)
                pieces += [jnp.zeros((start, k1), F32)] if start else []
                pieces.append(cut)
                rest = line - start - cut.shape[0]
                pieces += [jnp.zeros((rest, k1), F32)] if rest else []
            blocks[half, p] = jnp.concatenate(pieces, axis=0)
    zero = jnp.zeros((4 * line, k1), F32)
    lines = []
    for r in range(STEP):
        cols = [
            blocks.get((r + 1 - yrel, p), zero) for yrel in range(STEP + 1) for p in range(NEAR)
        ]
        lines.append(jnp.concatenate(cols, axis=1))
    return jnp.concatenate(lines, axis=0).astype(BF16)


def first_kernel(
    section,
    frames_far,
    g1,
    w1t,
    other_far,
    after,
    c1,
    out,
    band,
    frames,
    acc,
    other,
    held,
    sems,
    draw_sems,
    *,
    draw,
):
    side, k1 = g1.shape[1], g1.shape[2]
    img, _, channels, _ = frames.shape
    steps = img // 4 // STEP
    arrives = frame_copies(section, frames_far, frames, sems)
    for g in range(steps):
        arrives(g).start()
    other_copy = pltpu.make_async_copy(
        other_far.at[0 : STEP * draw + 1], other, sems.at[steps]
    )
    other_copy.start()
    acc[...] = jnp.zeros_like(acc)
    zero = jnp.zeros((k1, LANES), BF16)

    def one_step(g, carry):
        arrives(g).wait()
        pixels, grads = [], []
        for j in range(img // COLS):
            rows = [pl.multiple_of(4 * (STEP * g + r), 4) for r in range(STEP)]
            pixels.append(
                jnp.concatenate([tile_rows(frames, row, j, COLS) for row in rows], axis=0)
            )
            pieces = []
            for yrel in range(STEP + 1):
                for p in range(NEAR):
                    x = 3 * j - 1 + p
                    pieces.append(g1[STEP * g + yrel, x] if 0 <= x < side else zero)
            grads.append(jnp.concatenate(pieces, axis=0))
        acc[...] += dot_lanes(jnp.concatenate(pixels, axis=1), jnp.concatenate(grads, axis=1))
        return carry

    lax.fori_loop(0, steps, one_step, 0)
    band[...] = pixel_band(section[0], w1t[...], out.shape[2])
    other_copy.wait()
    finish = draw_steps(section, band, g1, 0, other, 0, out, held, draw_sems, 0, draw)
    fold_first(acc, c1, channels, k1)
    finish()


def fold_first(acc, c1, channels, k1):
    line = COLS * channels
    step = 4 * channels
    taps = []
    for half in range(2):
        total = sum(
            acc[r * 4 * line : (r + 1) * 4 * line, :][
                :, (r + 1 - half) * NEAR * k1 : (r + 2 - half) * NEAR * k1
            ]
            for r in range(STEP)
        )
        for u in range(4):
            part = total[u * line : (u + 1) * line]
            cols = [part[:, p * k1 : (p + 1) * k1] for p in range(NEAR)]
            taps.append(cols[1][0:step] + cols[2][step : 2 * step] + cols[3][2 * step :])
            taps.append(cols[0][0:step] + cols[1][step : 2 * step] + cols[2][2 * step :])
    row, col = iota((256, 256), 0), iota((256, 256), 1)
    moves = ((row & 3) == (col >> 6)) & ((row >> 2) == (col & 63))
    grad = dot_rows(jnp.concatenate(taps, axis=0), moves.astype(F32), EXACT)
    for half in range(2):
        c1[half * k1 : (half + 1) * k1, :] = grad[:, half * LANES : (half + 1) * LANES].astype(BF16)


def draw_steps(section, band, mine, mine_at, other, other_at, out, held, sems, start, steps):
    side, k1 = mine.shape[1], mine.shape[2]
    img, channels = out.shape[1], out.shape[2]
    sec = section[0]
    line = COLS * channels
    flat = held.reshape(2, 2, 4 * STEP, img * channels, LANES)

    def writes(g):
        rows = slice(4 * STEP * (start + g), 4 * STEP * (start + g + 1))
        places = (sec * LANES, (1 - sec) * LANES)
        return [
            pltpu.make_async_copy(
                held.at[g % 2, k],
                out.at[rows, :, :, pl.ds(pl.multiple_of(places[k], LANES), LANES)],
                sems.at[g % 2, k],
            )
            for k in range(2)
        ]

    zero = jnp.zeros((k1, 2 * LANES), BF16)
    for g in range(steps):
        if g >= 2:
            for copy in writes(g - 2):
                copy.wait()
        for j in range(img // COLS):
            pieces = []
            for yrel in range(STEP + 1):
                for p in range(NEAR):
                    x, y = 3 * j - 1 + p, STEP * (start + g) + yrel
                    if 0 <= x < side:
                        pair = [mine[y - mine_at, x], other[y - other_at, x]]
                        pieces.append(jnp.concatenate(pair, axis=1))
                    else:
                        pieces.append(zero)
            got = dot(band[...], jnp.concatenate(pieces, axis=0))
            for k in range(4 * STEP):
                at = slice(k * line, (k + 1) * line)
                span = slice(j * line, (j + 1) * line)
                flat[g % 2, 0, k, span, :] = got[at, :LANES]
                flat[g % 2, 1, k, span, :] = got[at, LANES:]
        for copy in writes(g):
            copy.start()

    def finish():
        for g in range(max(steps - 2, 0), steps):
            for copy in writes(g):
                copy.wait()

    return finish


def pixels_kernel(section, band, mine, other_far, after, done, out, token, held, other, sems, *, start):
    steps = other.shape[0] // STEP
    fetch = pltpu.make_async_copy(
        other_far.at[STEP * start : STEP * (start + steps) + 1], other, sems.at[2, 0]
    )
    fetch.start()
    token[...] = jnp.zeros_like(token)
    fetch.wait()
    draw_steps(
        section, band, mine, 0, other, STEP * start, out, held, sems, start, steps
    )()


def two_parts(value):
    high = value.astype(BF16).astype(F32)
    return jnp.concatenate([high, value - high], axis=0).astype(BF16)


def one_part(pair):
    rows = pair.shape[0] // 2
    pair = pair.astype(F32)
    return pair[:rows] + pair[rows:]


def merge_kernel(keep, recv_one, recv_two, small, c2, sums, out_far, lines, out, sems):
    members = out.shape[0]
    size = keep.shape[0] // members
    k2 = c2.shape[0]
    lines[...] = jnp.zeros_like(lines)
    at = small.shape[0]
    lines[0:at, :] = small[...]
    for half in range(2):
        lines[at : at + k2, :] = c2[:, half * LANES : (half + 1) * LANES]
        at += k2
    lines[at : at + sums.shape[0], :] = sums[...]
    for k in range(members):
        at = slice(k * size, (k + 1) * size)
        recv, here = recv_one, k
        if k >= members // 2:
            recv, here = recv_two, k - members // 2
        got = recv[here * size : (here + 1) * size, :]
        out[k, 0:size, :] = (keep[at, :].astype(F32) + got.astype(F32)).astype(BF16)
        out[k, size:, :] = two_parts(lines[k * SHORT : (k + 1) * SHORT, :])
        pltpu.make_async_copy(out.at[k], out_far.at[k], sems.at[k]).start()
    for k in range(members):
        pltpu.make_async_copy(out.at[k], out_far.at[k], sems.at[k]).wait()


def cube_kernel(got, c1, out):
    members = got.shape[0]
    size = got.shape[1] - 2 * SHORT
    out[0:size, :] = sum(got[k, 0:size, :].astype(F32) for k in range(members)).astype(BF16)
    total = sum(one_part(got[k, size:, :]) for k in range(members))
    out[size : size + 2 * SHORT, :] = two_parts(total)
    out[size + 2 * SHORT :, :] = c1[...]


def add_kernel(a, b, after, out):
    size = a.shape[0] - 2 * SHORT - 32
    middle = slice(size, size + 2 * SHORT)
    for span in (slice(0, size), slice(size + 2 * SHORT, a.shape[0])):
        out[span, :] = (a[span, :].astype(F32) + b[span, :].astype(F32)).astype(BF16)
    out[middle, :] = two_parts(one_part(a[middle, :]) + one_part(b[middle, :]))


def relay_kernel(batch, *refs):
    parts, (one, two, out) = refs[:CUBE], refs[CUBE:]
    me = batch[0] % CUBE
    for k, part in enumerate(parts):
        out[me ^ k] = part[...]
    one[...] = out[: CUBE // 2]
    two[...] = out[CUBE // 2 :]


def piece_of(got, k):
    count = got[0].shape[0]
    return got[k // count].at[k % count]


def unpack_half(which, got, lw, bw, vw, stage, stage_b, sems):
    members = 2 * got[0].shape[0]
    size = stage.shape[0] // members
    linear_rows, width = lw.shape
    options = bw.shape[0]
    half = (linear_rows + options * width + width) // 2
    rest = linear_rows - half

    @pl.when(which == 0)
    def _():
        copies = []
        for k in range(members):
            start, end = k * size, min((k + 1) * size, half)
            stage[start:end, :] = piece_of(got, k)[0 : end - start, :].astype(F32)
            copies.append(
                pltpu.make_async_copy(stage.at[start:end], lw.at[start:end], sems.at[k])
            )
            copies[-1].start()
        for copy in copies:
            copy.wait()

    @pl.when(which == 1)
    def _():
        def rows(start, end):
            parts = []
            while start < end:
                k, at = start // size, start % size
                count = min(size - at, end - start)
                parts.append(piece_of(got, k)[at : at + count, :])
                start += count
            value = parts[0] if len(parts) == 1 else jnp.concatenate(parts, axis=0)
            return value.astype(F32)

        stage[0:rest, :] = rows(0, rest)
        copies = [pltpu.make_async_copy(stage.at[0:rest], lw.at[half:], sems.at[0])]
        copies[0].start()
        group = options // 3
        for o in range(options):
            stage_b[o] = rows(rest + o * width, rest + (o + 1) * width)
            if o % group == group - 1:
                part = slice(o + 1 - group, o + 1)
                copy = pltpu.make_async_copy(
                    stage_b.at[part], bw.at[part], sems.at[1 + o // group]
                )
                copy.start()
                copies.append(copy)
        at = rest + options * width
        stage[rest : rest + width, :] = rows(at, at + width)
        copies.append(
            pltpu.make_async_copy(stage.at[rest : rest + width], vw, sems.at[1 + options // group])
        )
        copies[-1].start()
        for copy in copies:
            copy.wait()


def own_kernel(section, one, two, lw, bw, vw, stage, stage_b, sems):
    unpack_half(section[0], (one, two), lw, bw, vw, stage, stage_b, sems)


def unpack_kernel(section, *refs):
    mine, other, refs = refs[0:2], refs[2:4], refs[4:]
    lw, bw, vw = refs[3:6]
    little = (len(refs) - 10) // 2
    far, near = refs[6 : 6 + little], refs[6 + little : 6 + 2 * little]
    loss, c1, b1, c2, b2, lb, bb, hw, hb, vb, ow, ob = near
    stage, stage_b, lines, sems = refs[-4:]
    options = bw.shape[0]
    k1, k2 = c1.shape[0], c2.shape[0]
    size = stage.shape[0] // CUBE
    grad = [jnp.zeros((k1, LANES), F32) for _ in range(2)]
    for k in range(CUBE):
        pair = slice(size, size + 2 * SHORT)
        at = slice(k * SHORT, (k + 1) * SHORT)
        views = piece_of(mine, k), piece_of(other, k)
        lines[at, :] = sum(one_part(v[pair, :]) for v in views)
        for view in views:
            for h in range(2):
                at = size + 2 * SHORT + h * k1
                grad[h] += view[at : at + k1, :].astype(F32)
    for part in range(2):
        c1[:, part * LANES : (part + 1) * LANES] = grad[part]
    bb[...] = lines[0:options, :]
    vb[...] = lines[AT_VB, :]
    ow[...] = lines[AT_OW, :]
    hw[...] = lines[AT_HW, :]
    lb[...] = lines[AT_LB, :]
    scalars = lines[AT_SCALARS, :]
    loss[...] = scalars[:, 0:1]
    hb[...] = scalars[:, 1:3]
    ob[...] = scalars[:, 3:4]
    at = TABLE
    for part in range(2):
        c2[:, part * LANES : (part + 1) * LANES] = lines[at : at + k2, :]
        at += k2
    b1[...] = lines[at : at + 1, 0:k1]
    b2[...] = lines[at + 1 : at + 2, 0:k2]
    copies = [
        pltpu.make_async_copy(a, b, sems.at[CUBE + k]) for k, (a, b) in enumerate(zip(near, far))
    ]
    for copy in copies:
        copy.start()
    unpack_half(1 - section[0], other, lw, bw, vw, stage, stage_b, sems)
    for copy in copies:
        copy.wait()


def numbers_kernel(
    options,
    depth,
    targets,
    destination,
    b1,
    b2,
    lb,
    bb,
    hw,
    vb,
    ow,
    hb,
    ob,
    out,
    table,
):
    levels, kinds = options.shape[0], targets.shape[0]
    slots = depth.shape[1]
    rows = [options[...].astype(F32), depth[...].astype(F32)]
    rows += [targets[k] for k in range(kinds)]
    rows.append(jnp.zeros((LANES - levels - 1 - kinds * levels, slots), F32))
    out[...] = jnp.transpose(jnp.concatenate(rows, axis=0))
    table[...] = jnp.zeros_like(table)
    table[0 : bb.shape[0], :] = bb[...]
    table[AT_VB, :] = vb[...]
    table[AT_OW, :] = ow[...].astype(F32)
    table[AT_HW, :] = hw[...].astype(F32)
    table[AT_LB, :] = lb[...]
    table[AT_B1, 0 : b1.shape[1]] = b1[...]
    table[AT_B2, 0 : b2.shape[1]] = b2[...]
    lane = iota((1, LANES), 1)
    scalars = jnp.zeros((1, LANES), F32)
    for k, value in ((1, hb[:, 0:1]), (2, hb[:, 1:2]), (3, ob[...])):
        scalars = jnp.where(lane == k, value, scalars)
    table[AT_SCALARS, :] = scalars
    for k in range(slots // LANES):
        part = destination[:, k * LANES : (k + 1) * LANES]
        table[AT_DEST + k : AT_DEST + k + 1, :] = part.astype(F32)


def whole(shape):
    zeros = (0,) * len(shape)
    return pl.BlockSpec(shape, lambda *_: zeros)


ANYWHERE = pl.BlockSpec(memory_space=pl.ANY)
SCALARS = pl.BlockSpec(memory_space=pltpu.SMEM)


def params():
    return pltpu.CompilerParams(vmem_limit_bytes=VMEM_BYTES)


def shape_of(*shape, dtype=F32):
    return jax.ShapeDtypeStruct(shape, dtype)


def cost(microseconds):
    return pl.CostEstimate(
        flops=int(1.1e9 * microseconds), bytes_accessed=int(3.6e6 * microseconds), transcendentals=0
    )


def stays(value):
    return pltpu.with_memory_space_constraint(value, pltpu.HBM)


def held_near(value):
    return pltpu.with_memory_space_constraint(value, pltpu.VMEM)


def encode(section, frames, w1t, w2t, lw, table):
    img = frames.shape[0]
    blocks = img // 4
    side = blocks - 1
    k1, k2, width = w1t.shape[0], w2t.shape[0], lw.shape[1]
    flat = lw.shape[0]
    vmem = pltpu.VMEM
    near = pl.BlockSpec(memory_space=vmem)
    grid_one = (blocks, side, k1, LANES)
    return pl.pallas_call(
        encode_kernel,
        in_specs=[SCALARS, ANYWHERE, near, near, ANYWHERE, near],
        out_specs=[ANYWHERE] * 3 + [near] * 3,
        out_shape=(
            pltpu.HBM(grid_one, BF16),
            pltpu.HBM(grid_one, BF16),
            pltpu.HBM((flat, LANES), BF16),
            shape_of(flat, LANES, dtype=BF16),
            shape_of(width, LANES, dtype=BF16),
            shape_of(width, LANES),
        ),
        scratch_shapes=[
            vmem((img, img, frames.shape[2], LANES), BF16),
            vmem(lw.shape, BF16),
            vmem(grid_one, BF16),
            vmem(grid_one, BF16),
            vmem((flat, LANES), BF16),
            vmem((2 * REACH * k1, 256), BF16),
            vmem((2 * k1, 64), BF16),
            vmem((6 * k2, LANES), BF16),
            vmem((k1, LANES), F32),
            vmem((k2, LANES), F32),
            vmem((side, k1, LANES), F32),
            vmem((side // 2 - 1, k2, LANES), F32),
            pltpu.SemaphoreType.DMA((4, max(blocks // STEP, 3))),
        ],
        compiler_params=params(),
        cost_estimate=cost(9),
        name="encode",
    )(section, frames, w1t, w2t, lw, table)


def plan(section, slots, enc, s3, h2, branch_w, value_w, table, per_pair, depth, half_rows):
    width = enc.shape[0]
    options = branch_w.shape[0]
    two = 2 * width
    pairs = options // 2
    outs = (
        shape_of(half_rows, LANES, dtype=BF16),
        shape_of(half_rows // 2, LANES, dtype=BF16),
        shape_of(half_rows // 2, LANES, dtype=BF16),
        shape_of(TABLE, LANES),
        shape_of(width, LANES, dtype=BF16),
    )
    vmem = pltpu.VMEM
    near = pl.BlockSpec(memory_space=vmem)
    return pl.pallas_call(
        functools.partial(plan_kernel, per_pair=per_pair, depth=depth),
        in_specs=[SCALARS, near, near, near, near, ANYWHERE, near, near],
        out_shape=outs,
        scratch_shapes=[
            vmem((2, half_rows, LANES), BF16),
            vmem((options * width, width + 16), BF16),
            vmem((width + 16, width + 16), BF16),
            vmem((width, width + 16), BF16),
            vmem((width, LANES), F32),
            vmem((16, LANES), F32),
            vmem((depth, options * width, LANES), F32),
            vmem((depth, pairs, width, two), F32),
            vmem((depth, pairs, width + 16, two), BF16),
            vmem((depth, pairs, width, two), BF16),
            vmem((depth, options * width, LANES), BF16),
            vmem(branch_w.shape, BF16),
            pltpu.SemaphoreType.DMA,
        ],
        compiler_params=params(),
        cost_estimate=cost(11),
        name="plan",
    )(section, slots, enc, s3, h2, branch_w, value_w, table)


def back(g3, lw, s2, s1, h1, w2t):
    _, side, k1 = s1.shape[:3]
    k2 = w2t.shape[0]
    inner = side // 2 - 1
    padded = (side + 2, side, k1, LANES)
    near = pl.BlockSpec(memory_space=pltpu.VMEM)
    return pl.pallas_call(
        back_kernel,
        in_specs=[near] * 6,
        out_shape=(shape_of(*padded, dtype=BF16), shape_of(k2, 256), shape_of(8, LANES)),
        scratch_shapes=[
            pltpu.VMEM((LANES, 6 * k2), BF16),
            pltpu.VMEM((inner + 2, inner, k2, LANES), BF16),
        ],
        compiler_params=params(),
        cost_estimate=cost(25),
        name="back",
    )(g3, lw, s2, s1, h1, w2t)


def first(section, frames, g1, w1t, other, after, channels, draw):
    img, _, stack, _ = frames.shape
    k1 = g1.shape[2]
    band = (STEP * 4 * COLS * channels, (STEP + 1) * NEAR * k1)
    near = pl.BlockSpec(memory_space=pltpu.VMEM)
    return pl.pallas_call(
        functools.partial(first_kernel, draw=draw),
        in_specs=[SCALARS, ANYWHERE, near, near, ANYWHERE, ANYWHERE],
        out_specs=[near, ANYWHERE, near],
        out_shape=[
            shape_of(2 * k1, LANES, dtype=BF16),
            shape_of(img, img, channels, 2 * LANES),
            shape_of(*band, dtype=BF16),
        ],
        scratch_shapes=[
            pltpu.VMEM((img, img, stack, LANES), BF16),
            pltpu.VMEM((STEP * 4 * COLS * stack, (STEP + 1) * NEAR * k1), F32),
            pltpu.VMEM((STEP * draw + 1,) + g1.shape[1:], BF16),
            pltpu.VMEM((2, 2, 4 * STEP, img, channels, LANES), F32),
            pltpu.SemaphoreType.DMA((img // 4 // STEP + 1,)),
            pltpu.SemaphoreType.DMA((2, 2)),
        ],
        compiler_params=params(),
        cost_estimate=cost(45),
        name="first",
    )(section, frames, g1, w1t, other, after)


def pixels(section, band, mine, other, after, done, start):
    img, _, channels, _ = done.shape
    steps = img // 4 // STEP - start
    near = pl.BlockSpec(memory_space=pltpu.VMEM)
    return pl.pallas_call(
        functools.partial(pixels_kernel, start=start),
        in_specs=[SCALARS, near, near, ANYWHERE, ANYWHERE, ANYWHERE],
        out_specs=[ANYWHERE, near],
        out_shape=[shape_of(*done.shape), shape_of(8, LANES)],
        scratch_shapes=[
            pltpu.VMEM((2, 2, 4 * STEP, img, channels, LANES), F32),
            pltpu.VMEM((STEP * steps + 1,) + mine.shape[1:], BF16),
            pltpu.SemaphoreType.DMA((3, 2)),
        ],
        input_output_aliases={5: 0},
        compiler_params=params(),
        cost_estimate=cost(1 + 0.9 * steps),
        name="pixels",
    )(section, band, mine, other, after, done)


def small_call(
    kernel, outs, operands, scratch=(), name=None, place=None, after=(), weight=0.3, far=False
):
    specs = [pl.BlockSpec(memory_space=pltpu.VMEM)] * len(operands)
    if place is not None:
        operands = (*place, *operands)
        specs = [pl.BlockSpec(memory_space=pltpu.SMEM)] * len(place) + specs
    return pl.pallas_call(
        kernel,
        in_specs=specs + [ANYWHERE] * len(after),
        out_specs=jax.tree.map(
            lambda _: ANYWHERE if far else pl.BlockSpec(memory_space=pltpu.VMEM), outs
        ),
        out_shape=outs,
        scratch_shapes=list(scratch),
        compiler_params=params(),
        cost_estimate=cost(weight),
        name=name,
    )(*operands, *after)


def round_up(value, step):
    return -(-value // step) * step


def swapped(value):
    return lax.ppermute(value, "section", [(0, 1), (1, 0)])


def exchanged(value, groups=None):
    return lax.all_to_all(
        value, "batch", split_axis=0, concat_axis=0, axis_index_groups=groups, tiled=True
    )


def partner(value, distance):
    count = lax.axis_size("batch")
    return lax.ppermute(value, "batch", [(b, b ^ distance) for b in range(count)])


def local(
    frames,
    destination,
    options,
    depth,
    targets,
    conv_one,
    bias_one,
    conv_two,
    bias_two,
    linear_w,
    linear_b,
    branch_w,
    branch_b,
    head_w,
    head_b,
    value_w,
    value_b,
    out_w,
    out_b,
):
    section = lax.axis_index("section").astype(jnp.int32)[None]
    peers = lax.axis_size("batch")
    frame_count = frames.shape[3]
    per_pair = frame_count // peers
    levels = options.shape[0]
    frames = stays(frames.transpose(1, 2, 0, 3))
    w1t, w2t = stays(conv_one.T), stays(conv_two.T)
    branch_w, value_w = stays(branch_w), stays(value_w)
    encoder_params = (w1t, bias_one, w2t, bias_two, linear_w, linear_b)
    planner_params = (branch_w, branch_b, head_w.T, head_b, value_w, value_b, out_w.T, out_b)
    width = linear_w.shape[1]
    big_rows = linear_w.shape[0] + (branch_w.shape[0] + 1) * width
    size = round_up(-(-big_rows // (2 * CUBE)), 16)

    tiny = (bias_one, bias_two, linear_b, branch_b, head_w.T, value_b, out_w.T)
    tiny = [stays(v if v.ndim > 1 else v[None, :]) for v in tiny]
    numbers, table = pl.pallas_call(
        numbers_kernel,
        in_specs=[pl.BlockSpec(memory_space=pltpu.VMEM)] * (6 + len(tiny)),
        out_shape=[shape_of(frame_count, LANES), shape_of(TABLE, LANES)],
        compiler_params=params(),
        cost_estimate=cost(1),
        name="numbers",
    )(
        stays(options),
        stays(depth[None, :]),
        stays(targets),
        stays(destination[None, :]),
        *tiny,
        stays(head_b[None, :]),
        out_b[None, :],
    )
    slots = exchanged(numbers.reshape(peers, per_pair, LANES)).reshape(frame_count, LANES)

    h1, s1, s2, h2, enc, s3 = encode(section, frames, w1t, w2t, stays(linear_w), table)
    keep, send_one, send_two, small, g3 = plan(
        section, slots, enc, s3, h2, branch_w, value_w, table, per_pair, levels, CUBE * size
    )
    recv = swapped(send_one), swapped(send_two)
    channels = frames.shape[2] // lax.axis_size("section")
    g1, c2, sums = back(g3, linear_w, s2, s1, h1, w2t)
    other = swapped(g1)
    g1 = held_near(g1)
    cubes = [list(range(c, c + CUBE)) for c in range(0, peers, CUBE)]
    bf16 = functools.partial(shape_of, dtype=BF16)
    pieces = small_call(
        merge_kernel,
        bf16(CUBE, size + 2 * SHORT, LANES),
        (keep, *recv, small, c2, sums),
        [
            pltpu.VMEM((CUBE * SHORT, LANES), F32),
            pltpu.VMEM((CUBE, size + 2 * SHORT, LANES), BF16),
            pltpu.SemaphoreType.DMA((CUBE,)),
        ],
        name="merge",
        far=True,
        weight=30,
    )
    got = exchanged(pieces, cubes)
    c1, frames_grad, band = first(section, frames, g1, w1t, other, pieces, channels, DRAW)
    piece = bf16(size + 2 * SHORT + c1.shape[0], LANES)
    keep = small_call(cube_kernel, piece, (got, c1), name="cube")
    distance = CUBE
    while distance < peers:
        recv = partner(keep, distance)
        if distance == CUBE:
            frames_grad, token = pixels(section, band, g1, other, keep, frames_grad, DRAW)
        distance *= 2
        keep = small_call(add_kernel, piece, (keep, recv), name="add", after=(token,))
    parts = [keep] + [partner(keep, k) for k in range(1, CUBE)]
    place = (lax.axis_index("batch").astype(jnp.int32)[None],)
    got = small_call(
        relay_kernel,
        [bf16(CUBE // 2, *piece.shape)] * 2,
        parts,
        [pltpu.VMEM((CUBE, *piece.shape), BF16)],
        name="relay",
        place=place,
    )
    got_other = [swapped(v) for v in got]
    shapes = [p.shape for p in encoder_params + planner_params]
    near = pl.BlockSpec(memory_space=pltpu.VMEM)
    flat = [shape_of(*(v if len(v) > 1 else (1,) + v)) for v in [(1, 1)] + shapes]
    large = [flat[k] for k in (5, 7, 11)]
    staged = [
        pltpu.VMEM((CUBE * size, LANES), F32),
        pltpu.VMEM(branch_w.shape, F32),
    ]
    little = [v for k, v in enumerate(flat) if k not in (5, 7, 11)]
    sems = pltpu.SemaphoreType.DMA((CUBE + len(little),))
    begun = pl.pallas_call(
        own_kernel,
        in_specs=[SCALARS, near, near],
        out_specs=[ANYWHERE] * 3,
        out_shape=large,
        scratch_shapes=[*staged, sems],
        compiler_params=params(),
        cost_estimate=cost(1),
        name="own",
    )(section, *got)
    ends = pl.pallas_call(
        unpack_kernel,
        in_specs=[SCALARS] + [near] * 4 + [ANYWHERE] * 3,
        out_specs=[ANYWHERE] * (3 + len(little)),
        out_shape=large + little,
        scratch_shapes=[pltpu.VMEM(v.shape, F32) for v in little]
        + [*staged, pltpu.VMEM((CUBE * SHORT, LANES), F32), sems],
        input_output_aliases={5: 0, 6: 1, 7: 2},
        compiler_params=params(),
        cost_estimate=cost(1.5),
        name="unpack",
    )(section, *got, *got_other, *begun)
    rest = list(ends[3:])
    for k, at in enumerate((5, 7, 11)):
        rest.insert(at, ends[k])
    rest = [v.reshape(s) for v, s in zip(rest, [()] + shapes)]
    for at in (1, 3, 9, 13):
        rest[at] = rest[at].T
    return (rest[0], frames_grad.transpose(2, 0, 1, 3), *rest[1:])


def solution(mesh):
    placed = (
        P(None, None, None, "batch"),
        P("batch"),
        P(None, "batch"),
        P("batch"),
        P(None, None, "batch"),
    ) + (P(),) * 14
    return jax.shard_map(
        local,
        mesh=mesh,
        in_specs=placed,
        out_specs=(P(), P("section", None, None, "batch")) + (P(),) * 14,
        check_vma=False,
    )
```

```python
import functools
import math

import jax
import jax.numpy as jnp
from jax import lax
from jax.experimental import pallas as pl
from jax.experimental.pallas import tpu as pltpu
from jax.sharding import PartitionSpec as P

BF16 = jnp.bfloat16
F32 = jnp.float32
EXACT = lax.Precision.HIGHEST
LANES = 128
VMEM_BYTES = 32 * 1024 * 1024
TILE = 16
REACH = 5
STEP = 3
COLS = 12
NEAR = 4
AT_VB, AT_OW, AT_HW, AT_LB, AT_SCALARS, AT_B1, AT_B2, AT_DEST = (
    slice(18, 19),
    slice(19, 20),
    slice(20, 22),
    slice(22, 23),
    slice(23, 24),
    slice(24, 25),
    slice(25, 26),
    26,
)
TABLE = 32
CUBE = 8
DRAW = 4
SHORT = 16


def dot(a, b, precision=None):
    return jnp.dot(a, b, preferred_element_type=F32, precision=precision)


def dot_rows(a, b, precision=None):
    return lax.dot_general(
        a, b, (((0,), (0,)), ((), ())), preferred_element_type=F32, precision=precision
    )


def dot_lanes(a, b, precision=None):
    return lax.dot_general(
        a, b, (((1,), (1,)), ((), ())), preferred_element_type=F32, precision=precision
    )


def iota(shape, axis):
    return lax.broadcasted_iota(jnp.int32, shape, axis)


def column(row):
    n = row.shape[1]
    wide = jnp.broadcast_to(row, (n, n))
    return jnp.sum(jnp.where(iota((n, n), 0) == iota((n, n), 1), wide, 0.0), axis=1, keepdims=True)


def row_of(col):
    n = col.shape[0]
    wide = jnp.broadcast_to(col, (n, n))
    return jnp.sum(jnp.where(iota((n, n), 0) == iota((n, n), 1), wide, 0.0), axis=0, keepdims=True)


def soft(x):
    t = jnp.tanh(0.5 * x)
    return jnp.maximum(x, 0.0) - jnp.log(0.5 + 0.5 * jnp.abs(t)), 0.5 + 0.5 * t


def silu_pair(y):
    t = jnp.tanh(y)
    m = y * t
    return y + m, (1.0 + t) + (y - m * t)


def pixel_order(w1t):
    tap, pix = iota((256, 256), 0), iota((256, 256), 1)
    moves = ((tap >> 6) == (pix & 3)) & ((tap & 63) == (pix >> 2))
    return dot(w1t, moves.astype(F32).astype(BF16))


def frame_copies(section, far, here, sems, blocks):
    lanes = pl.ds(pl.multiple_of(section[0] * LANES, LANES), LANES)
    size = 4 * blocks

    def copy(g):
        rows = pl.ds(pl.multiple_of(g * size, size), size)
        return pltpu.make_async_copy(far.at[rows, :, :, lanes], here.at[rows], sems.at[g])

    return copy


def tile_rows(frames, row, j, cols):
    img, _, channels, _ = frames.shape
    flat = frames.reshape(img, img * channels, LANES)
    size = cols * channels
    end = min((j + 1) * size, img * channels)
    part = flat[pl.ds(row, 4), j * size : end, :]
    return part.reshape(4 * (end - j * size), LANES)


def encode_kernel(
    section,
    frames_far,
    w1t,
    w2t,
    lw_far,
    table,
    h1_far,
    s1_far,
    s2_far,
    h2,
    enc,
    s3,
    frames,
    lw,
    h1,
    s1,
    s2,
    band,
    edge,
    band2,
    bias1,
    bias2,
    held,
    held2,
    total,
    sems,
):
    blocks, side = h1.shape[:2]
    steps = blocks // 2
    tiles = frames.shape[1] // TILE
    k1, k2 = w1t.shape[0], w2t.shape[0]
    reach_rows = REACH * k1
    arrives = frame_copies(section, frames_far, frames, sems.at[0], 2)
    lanes = pl.ds(pl.multiple_of(section[0] * LANES, LANES), LANES)
    last_rows = slice(8 * steps, 4 * blocks)
    last_copies = [
        pltpu.make_async_copy(lw_far, lw, sems.at[3, 0]),
        pltpu.make_async_copy(s2, s2_far, sems.at[3, 1]),
        pltpu.make_async_copy(
            frames_far.at[last_rows, :, :, lanes], frames.at[last_rows], sems.at[3, 2]
        ),
    ]
    for g in range(steps):
        arrives(g).start()
        if g == 1:
            last_copies[0].start()
    last_copies[2].start()

    def leaves(first, count, g):
        rows = pl.ds(first, count)
        return [
            pltpu.make_async_copy(h1.at[rows], h1_far.at[rows], sems.at[1, g]),
            pltpu.make_async_copy(s1.at[rows], s1_far.at[rows], sems.at[2, g]),
        ]

    inner = side // 2 - 1
    row_len = inner * k2
    two = 2 * k2 * 3

    def prepare():
        taps = pixel_order(w1t[...])
        edges = []
        for half in range(2):
            lines = [taps[:, 32 * (4 * half + u) : 32 * (4 * half + u + 1)] for u in range(4)]
            for place in range(REACH):
                pieces = []
                for line in lines:
                    start = 16 * (place - 1)
                    cut = line[:, max(0, -start) : min(32, 64 - start)]
                    start = max(start, 0)
                    pieces += [jnp.zeros((k1, start), F32)] if start else []
                    pieces.append(cut)
                    rest = 64 - start - cut.shape[1]
                    pieces += [jnp.zeros((k1, rest), F32)] if rest else []
                at = half * reach_rows + place * k1
                band[at : at + k1, :] = jnp.concatenate(pieces, axis=1).astype(BF16)
            edges.append(jnp.concatenate([line[:, 16:] for line in lines], axis=1))
        edge[...] = jnp.concatenate(edges, axis=0).astype(BF16)
        tap, pix = iota((256, LANES), 0), iota((256, LANES), 1)
        for half in range(2):
            for place in range(3):
                hit = (
                    ((tap & 15) == (pix & 15))
                    & ((tap >> 6) == (pix >> 6) + 2 * half)
                    & (((tap >> 4) & 3) == ((pix >> 4) & 3) + 2 - 2 * place)
                )
                at = (half * 3 + place) * k2
                taps = dot(w2t[...], hit.astype(F32).astype(BF16))
                band2[at : at + k2, :] = taps.astype(BF16)
        bias1[...] = jnp.broadcast_to(column(table[AT_B1, 0:k1]), bias1.shape)
        bias2[...] = jnp.broadcast_to(column(table[AT_B2, 0:k2]), bias2.shape)
        held[...] = jnp.zeros_like(held)
        held2[...] = jnp.zeros_like(held2)
        h1[...] = jnp.zeros_like(h1)

    def added(sums, x, value):
        sums[x] = sums[x] + value if x in sums else value

    def second_matmul(b):
        parts = [
            h1[pl.ds(2 * b + 1, 2), 4 * j : 4 * j + 4].reshape(LANES, LANES)
            for j in range(side // 4)
        ]
        return dot(band2[...], jnp.concatenate(parts, axis=1))

    def second_rows(b, got):
        low, high = {}, {}
        for j in range(side // 4):
            for place in range(3):
                x = 2 * j - 1 + place
                if 0 <= x < inner:
                    span = slice(j * LANES, (j + 1) * LANES)
                    at = place * k2
                    added(low, x, got[at : at + k2, span])
                    added(high, x, got[two // 2 + at : two // 2 + at + k2, span])
        row = jnp.maximum(b - 1, 0) * row_len
        for x in range(inner):
            value, slope = soft(held2[x] + high[x] + bias2[...])
            held2[x] = low[x]
            at = pl.ds(pl.multiple_of(row + x * k2, k2), k2)
            h2[at, :] = value.astype(BF16)
            s2[at, :] = slope.astype(BF16)

    def linear(row):
        at = pl.ds(pl.multiple_of(row * row_len, row_len), row_len)
        return dot_rows(lw[at, :], h2[at, :])

    def run(units):
        waiting = None
        for issue, take in units:
            got = issue()
            if waiting is not None:
                waiting[0](waiting[1])
            waiting = (take, got)
        waiting[0](waiting[1])

    def first_units(start, count):
        lows, highs = [{} for _ in range(count)], [{} for _ in range(count)]

        def tile(r, j):
            return tile_rows(frames, pl.multiple_of(4 * (start + r), 4), j, TILE)

        def finish(r, xs):
            for x in xs:
                value, slope = soft(held[x] + highs[r][x] + bias1[...])
                held[x] = lows[r][x]
                h1[start + r, x] = value.astype(BF16)
                s1[start + r, x] = slope.astype(BF16)

        def full(spots, ready=None):
            def issue():
                return dot(band[...], jnp.concatenate([tile(*spot) for spot in spots], axis=1))

            def take(got):
                for i, (r, j) in enumerate(spots):
                    part = got[:, i * LANES : (i + 1) * LANES]
                    for place in range(REACH):
                        x = 4 * j - 1 + place
                        if 0 <= x < side:
                            at = place * k1
                            added(lows[r], x, part[at : at + k1])
                            added(highs[r], x, part[reach_rows + at : reach_rows + at + k1])
                if ready:
                    finish(*ready)

            return issue, take

        def edges():
            parts = [tile(r, tiles) for r in range(count)]
            return dot(edge[...], jnp.concatenate(parts, axis=1))

        def place_edges(got):
            for r in range(count):
                span = slice(r * LANES, (r + 1) * LANES)
                added(lows[r], side - 1, got[:k1, span])
                added(highs[r], side - 1, got[k1:, span])

        units = [(edges, place_edges), full([(r, tiles - 1) for r in range(count)])]
        for r in range(count):
            done = 0
            for j in range(0, tiles - 1, 2):
                ready = side if j + 2 == tiles - 1 else 4 * j + 7
                units.append(full([(r, j), (r, j + 1)], (r, range(done, ready))))
                done = ready
        return units

    def one_step(g, carry):
        arrives(g).wait()
        pair, row = jnp.maximum(g - 2, 0), jnp.maximum(g - 4, 0)

        def add_linear(got):
            total[...] += jnp.where(g >= 4, got, 0.0)

        units = [
            (lambda: linear(row), add_linear),
            (lambda: second_matmul(pair), lambda got: second_rows(pair, got)),
        ]
        run(units + first_units(2 * g, 2))
        for copy in leaves(2 * g, 2, g):
            copy.start()
        return carry

    prepare()
    total[...] = jnp.zeros_like(total)
    last_copies[0].wait()
    lax.fori_loop(0, steps, one_step, 0)
    last_copies[2].wait()
    late = side // 2 - 2
    units = [(lambda: second_matmul(late), lambda got: second_rows(late, got))]
    units += first_units(2 * steps, 1)
    run(units)
    for copy in leaves(2 * steps, 1, steps):
        copy.start()
    more = []
    run(
        [(lambda: second_matmul(late + 1), lambda got: second_rows(late + 1, got))]
        + [
            (functools.partial(linear, row), more.append)
            for row in range(steps - 4, inner - 1)
        ]
    )
    last_copies[1].start()
    more.append(linear(inner - 1))
    value, slope = soft(total[...] + sum(more) + column(table[AT_LB, :]))
    enc[...] = value.astype(BF16)
    s3[...] = slope
    for g in range(steps):
        for copy in leaves(2 * g, 2, g):
            copy.wait()
    for copy in leaves(2 * steps, 1, steps):
        copy.wait()
    last_copies[1].wait()


def three_parts(row):
    high = row.astype(BF16).astype(F32)
    middle = (row - high).astype(BF16).astype(F32)
    return jnp.concatenate([high, middle, row - high - middle], axis=0)


def with_ones(value):
    return jnp.concatenate([value, ones_rows(value.shape[1])], axis=0)


def ones_rows(lanes):
    return (iota((16, lanes), 0) < 3).astype(F32).astype(BF16)


def plan_kernel(
    section,
    slots,
    enc,
    s3,
    h2,
    branch_far,
    value_w,
    table,
    keep,
    send_one,
    send_two,
    small,
    g3,
    parts,
    bwt,
    vht,
    vhw,
    ow,
    mine,
    pre,
    dbr,
    dval,
    low,
    hid,
    gb,
    branch_w,
    sem,
    *,
    per_pair,
    depth,
):
    width = enc.shape[0]
    options = branch_w.shape[0]
    pairs = options // 2
    two = 2 * width
    sec = section[0]
    branch_copy = pltpu.make_async_copy(branch_far, branch_w, sem)
    branch_copy.start()

    count = slots.shape[0]
    dest = jnp.concatenate(
        [table[AT_DEST + k : AT_DEST + k + 1, :] for k in range(count // LANES)], axis=1
    )
    own = jnp.where(sec == 0, dest[:, :LANES], dest[:, LANES:])
    others = jnp.transpose(jnp.broadcast_to(dest, (LANES, count)))
    index = iota((count, LANES), 1) + sec * LANES
    earlier = (others == own) & (iota((count, LANES), 0) < index)
    rank = jnp.sum(earlier.astype(F32), axis=0, keepdims=True)
    bucket = own * float(per_pair) + rank
    chosen = (iota((count, LANES), 0).astype(F32) == bucket).astype(F32).astype(BF16)
    numbers = slots[...]
    high = numbers.astype(BF16)
    middle = (numbers - high.astype(F32)).astype(BF16)
    rest = (numbers - high.astype(F32) - middle.astype(F32)).astype(BF16)
    mine[...] = sum(dot_rows(v, chosen) for v in (rest, middle, high))[: mine.shape[0]]

    pad = jnp.zeros((13, width), F32)
    branch_copy.wait()
    for o in range(options):
        rows = [branch_w[o].astype(F32), three_parts(table[o : o + 1, :]), pad]
        bwt[o * width : (o + 1) * width, :] = jnp.transpose(
            0.5 * jnp.concatenate(rows, axis=0)
        ).astype(BF16)
    scalars = table[AT_SCALARS, :]
    head_w = table[AT_HW, :]
    rows = [value_w[...].astype(F32), three_parts(table[AT_VB, :]), pad]
    vht[0:width, :] = jnp.transpose(0.5 * jnp.concatenate(rows, axis=0)).astype(BF16)
    vht[width:, :] = jnp.zeros((16, width + 16), BF16)
    lane = iota((1, 16), 1)
    for k in range(2):
        bias = three_parts(jnp.broadcast_to(scalars[:, 1 + k : 2 + k], (1, 16)))
        bias = sum(jnp.where(lane == j, bias[j : j + 1], 0.0) for j in range(3))
        vht[width + k : width + k + 1, 0:width] = head_w[k : k + 1].astype(BF16)
        vht[width + k : width + k + 1, width:] = bias.astype(BF16)
    vhw[:, 0:width] = (0.5 * value_w[...].astype(F32)).astype(BF16)
    vhw[:, width:] = jnp.transpose(
        0.5 * jnp.concatenate([head_w, jnp.zeros((14, width), F32)], axis=0)
    ).astype(BF16)
    ow[...] = jnp.broadcast_to(column(table[AT_OW, :]), (width, LANES))
    wide_ow = jnp.concatenate([ow[...], ow[...]], axis=1)
    half_ow = 0.5 * wide_ow

    labels = iota((options, LANES), 0).astype(F32)
    state = enc[...].astype(F32)
    rounded_all, saved = [], []
    group = 3
    for level in range(depth):
        picked = labels == mine[level : level + 1, :]
        rounded = state.astype(BF16)
        rounded_all.append(rounded)
        met = with_ones(rounded)

        def branches(first):
            at = slice(first * two, (first + group) * two)
            pre[at, :] = dot(bwt[at, :], met)

        branches(0)
        following = state
        reward, discount, value = [], [], []

        def value_part(t, got):
            act, slope = silu_pair(got[:width])
            dval[level, t] = slope
            hidden = act.astype(BF16)
            hid[level, t] = hidden
            worth = jnp.sum(hidden.astype(F32) * wide_ow, axis=0, keepdims=True)
            for k in range(2):
                span = slice(k * LANES, (k + 1) * LANES)
                value.append(worth[:, span])
                reward.append(got[width : width + 1, span])
                discount.append(got[width + 1 : width + 2, span])

        waiting = None
        for first in range(0, pairs, group):
            if first + group < pairs:
                branches(first + group)
            boths = []
            for t in range(first, first + group):
                at = slice(t * two, (t + 1) * two)
                act, slope = silu_pair(pre[at, :])
                dbr[level, at, :] = slope
                left = state + act[:width]
                right = state + act[width:]
                following = jnp.where(picked[2 * t : 2 * t + 1], left, following)
                following = jnp.where(picked[2 * t + 1 : 2 * t + 2], right, following)
                both = with_ones(
                    jnp.concatenate([left.astype(BF16), right.astype(BF16)], axis=1)
                )
                low[level, t] = both
                boths.append(both)
            got = dot(vht[...], jnp.concatenate(boths, axis=1))
            if waiting is not None:
                for k in range(group):
                    value_part(waiting[0] + k, waiting[1][:, k * two : (k + 1) * two])
            waiting = (first, got)
        for k in range(group):
            value_part(waiting[0] + k, waiting[1][:, k * two : (k + 1) * two])
        reward = jnp.concatenate(reward, axis=0)
        discount = jax.nn.sigmoid(jnp.concatenate(discount, axis=0))
        value = jnp.concatenate(value, axis=0) + scalars[:, 3:4]
        quality = reward + discount * value
        top = jnp.max(quality, axis=0, keepdims=True)
        shifted = jnp.exp(quality - top)
        total = jnp.sum(shifted, axis=0, keepdims=True)
        live = (mine[depth : depth + 1, :] > level).astype(F32)
        chosen = picked.astype(F32)

        def target(kind):
            at = depth + 1 + kind * depth + level
            return mine[at : at + 1, :]

        reward_gap = live * (jnp.sum(chosen * reward, axis=0, keepdims=True) - target(0))
        discount_gap = live * (jnp.sum(chosen * discount, axis=0, keepdims=True) - target(1))
        plan_gap = live * (top + jnp.log(total) - target(2))
        grad_quality = plan_gap * (shifted / total)
        head_two = (chosen * discount_gap + grad_quality * value) * discount * (1.0 - discount)
        saved.append(
            (
                picked,
                (chosen * reward_gap + grad_quality).astype(BF16).astype(F32),
                head_two.astype(BF16).astype(F32),
                (grad_quality * discount).astype(BF16).astype(F32),
                reward_gap * reward_gap + discount_gap * discount_gap + plan_gap * plan_gap,
            )
        )
        state = following

    out_sum = jnp.zeros((16, width), F32)
    value_sum = jnp.zeros((width + 16, width + 16), F32)
    grad_next = None
    line = iota((16, two), 0)
    for level in reversed(range(depth)):
        picked, head_one, head_two, grad_value, _ = saved[level]
        upward = jnp.zeros((width, LANES), F32)

        def branch_part(t, moved):
            at = slice(t * two, (t + 1) * two)
            left, right = moved[:, :LANES], moved[:, LANES:]
            if grad_next is not None:
                left = left + jnp.where(picked[2 * t : 2 * t + 1], grad_next, 0.0)
                right = right + jnp.where(picked[2 * t + 1 : 2 * t + 2], grad_next, 0.0)
            grad_branch = jnp.concatenate([left, right], axis=0) * dbr[level, at, :]
            grad_branch = grad_branch.astype(BF16)
            gb[level, at, :] = grad_branch
            return left + right

        def group_part(first, moved):
            parts = [
                branch_part(first + k, moved[:, k * two : (k + 1) * two]) for k in range(group)
            ]
            at = slice(first * two, (first + group) * two)
            weights = [branch_w[o] for o in range(2 * first, 2 * (first + group))]
            return sum(parts), dot(jnp.concatenate(weights, axis=1), gb[level, at, :])

        waiting = None
        for first in range(0, pairs, group):
            stack = []
            for t in range(first, first + group):

                def across(rows):
                    return jnp.concatenate(
                        [rows[2 * t : 2 * t + 1], rows[2 * t + 1 : 2 * t + 2]], axis=1
                    )

                worth = across(grad_value)
                grad_pre = (worth * half_ow * dval[level, t]).astype(BF16)
                heads = jnp.where(line == 0, across(head_one), 0.0)
                heads = jnp.where(line == 1, across(head_two), heads)
                heads = jnp.where(line == 2, worth, heads)
                heads = heads.astype(BF16)
                out_sum = out_sum + dot_lanes(heads, hid[level, t])
                stack.append(jnp.concatenate([grad_pre, heads], axis=0))
            stack = jnp.concatenate(stack, axis=1)
            moved = dot(vhw[...], stack)
            lows = jnp.concatenate([low[level, first + k] for k in range(group)], axis=1)
            value_sum = value_sum + dot_lanes(stack, lows)
            if waiting is not None:
                one, other = group_part(*waiting)
                upward = upward + (one + 0.5 * other)
            waiting = (first, moved)
        one, other = group_part(*waiting)
        grad_next = upward + (one + 0.5 * other)

    linear_rows = h2.shape[0]
    half = (linear_rows + options * width + width) // 2
    rest = linear_rows - half
    rounded = with_ones(jnp.concatenate(rounded_all, axis=1))
    small[...] = jnp.zeros_like(small)
    if half < keep.shape[0]:
        for k in range(2):
            parts[k, half:, :] = jnp.zeros((keep.shape[0] - half, LANES), BF16)
    for t in range(pairs):
        at = slice(t * two, (t + 1) * two)
        grads = jnp.concatenate([gb[level, at, :] for level in range(depth)], axis=1)
        got = dot_lanes(rounded, grads)
        for k in range(2):
            o = 2 * t + k
            span = slice(k * width, (k + 1) * width)
            rows = slice(rest + o * width, rest + (o + 1) * width)
            parts[1 - sec, rows, :] = got[:width, span].astype(BF16)
            small[o : o + 1, :] = got[width : width + 1, span]
    after = rest + options * width
    parts[1 - sec, after : after + width, :] = jnp.transpose(value_sum[:width, :width]).astype(BF16)

    grad_three = ((2.0 * grad_next).astype(BF16).astype(F32) * s3[...]).astype(BF16)
    g3[...] = grad_three
    chunk = linear_rows // 9
    for i in range(8):
        at = slice(i * chunk, (i + 1) * chunk)
        parts[sec, at, :] = dot_lanes(h2[at, :], grad_three).astype(BF16)
    last = dot_lanes(h2[8 * chunk :, :], grad_three).astype(BF16)
    parts[sec, 8 * chunk : half, :] = last[: half - 8 * chunk]
    parts[1 - sec, 0:rest, :] = last[half - 8 * chunk :]
    keep[...] = parts[0]
    send_one[...] = parts[1, : send_one.shape[0]]
    send_two[...] = parts[1, send_one.shape[0] :]

    small[AT_VB, :] = row_of(value_sum[:width, width : width + 1])
    small[AT_OW, :] = out_sum[2:3]
    small[AT_HW, :] = value_sum[width : width + 2, :width]
    small[AT_LB, :] = row_of(jnp.sum(grad_three.astype(F32), axis=1, keepdims=True))
    loss = 0.5 * jnp.sum(sum(kept[4] for kept in saved), axis=1, keepdims=True)
    ends = [loss] + [value_sum[width + k : width + k + 1, width : width + 1] for k in range(3)]
    lane = iota((1, LANES), 1)
    line = jnp.zeros((1, LANES), F32)
    for k, end in enumerate(ends):
        line = jnp.where(lane == k, end, line)
    small[AT_SCALARS, :] = line


def back_kernel(g3, lw, s2, s1, h1, w2t, g1, c2, sums, t2, g2):
    side, k1 = s1.shape[1], s1.shape[2]
    k2 = w2t.shape[0]
    inner = side // 2 - 1
    row_len = inner * k2
    tap, pix = iota((LANES, 256), 1), iota((LANES, 256), 0)
    for yrel in range(2):
        for p in range(3):
            hit = (
                ((tap & 15) == (pix & 15))
                & ((tap >> 6) == (pix >> 6) + 2 * (1 - yrel))
                & (((tap >> 4) & 3) == ((pix >> 4) & 3) + 2 - 2 * p)
            )
            at = (yrel * 3 + p) * k2
            t2[:, at : at + k2] = dot_lanes(hit.astype(F32).astype(BF16), w2t[...]).astype(BF16)
    g2[0] = jnp.zeros(g2.shape[1:], BF16)
    g2[inner + 1] = jnp.zeros(g2.shape[1:], BF16)
    g1[0] = jnp.zeros(g1.shape[1:], BF16)
    g1[side + 1] = jnp.zeros(g1.shape[1:], BF16)
    zero = jnp.zeros((k2, LANES), BF16)
    total_one = jnp.zeros((k1, LANES), F32)
    total_two = jnp.zeros((k2, LANES), F32)
    for y in range(inner):
        at = slice(y * row_len, (y + 1) * row_len)
        grad = dot(lw[at, :], g3[...]) * s2[at, :].astype(F32)
        grad = grad.astype(BF16).reshape(inner, k2, LANES)
        g2[y + 1] = grad
        total_two = total_two + jnp.sum(grad.astype(F32), axis=0)
    reach, cols = 5, 8
    total = jnp.zeros((2 * reach * k2, 2 * cols * k1), F32)
    grads, tiles = [], []
    for b in range(side // 2):
        cut = []
        for j in range(side // 4):
            pieces = []
            for yrel in range(2):
                for p in range(3):
                    x = 2 * j - 1 + p
                    pieces.append(g2[b + yrel, x] if 0 <= x < inner else zero)
            cut.append(jnp.concatenate(pieces, axis=0))
        got = dot(t2[...], jnp.concatenate(cut, axis=1))
        for u in range(2):
            for j in range(side // 4):
                part = got[u * 64 : (u + 1) * 64, j * LANES : (j + 1) * LANES]
                slope = s1[2 * b + u + 1, 4 * j : 4 * j + 4].astype(F32)
                grad = (part.reshape(4, k1, LANES) * slope).astype(BF16)
                g1[2 * b + u + 1, 4 * j : 4 * j + 4] = grad
                total_one = total_one + jnp.sum(grad.astype(F32), axis=0)
        for j in range(-(-side // cols)):
            end = min((j + 1) * cols, side)
            tile = h1[2 * b + 1 : 2 * b + 3, j * cols : end]
            if end < (j + 1) * cols:
                rest = jnp.zeros((2, (j + 1) * cols - end, k1, LANES), BF16)
                tile = jnp.concatenate([tile, rest], axis=1)
            tiles.append(tile.reshape(2 * cols * k1, LANES))
            pieces = []
            for half in range(2):
                for p in range(reach):
                    x = 4 * j - 1 + p
                    pieces.append(g2[b + 1 - half, x] if 0 <= x < inner else zero)
            grads.append(jnp.concatenate(pieces, axis=0))
        if b % 2:
            total = total + dot_lanes(
                jnp.concatenate(grads, axis=1), jnp.concatenate(tiles, axis=1)
            )
            grads, tiles = [], []
    line = 4 * k1
    for half in range(2):
        for u in range(2):
            tap_row = jnp.zeros((k2, line), F32)
            for p in range(reach):
                at = (half * reach + p) * k2
                part = total[at : at + k2, u * 2 * line : (u + 1) * 2 * line]
                start = 2 * k1 * (p - 1)
                piece = part[:, max(start, 0) : min(start + line, 2 * line)]
                if start < 0:
                    piece = jnp.concatenate([jnp.zeros((k2, -start), F32), piece], axis=1)
                if start + line > 2 * line:
                    rest = jnp.zeros((k2, start - line), F32)
                    piece = jnp.concatenate([piece, rest], axis=1)
                tap_row = tap_row + piece
            at = (2 * half + u) * line
            c2[:, at : at + line] = tap_row
    sums[...] = jnp.zeros_like(sums)
    sums[0:1, 0:k1] = row_of(jnp.sum(total_one, axis=1, keepdims=True))
    sums[1:2, 0:k2] = row_of(jnp.sum(total_two, axis=1, keepdims=True))


def pixel_band(sec, w1t, channels):
    k1 = w1t.shape[0]
    rows = 64 * channels
    row, tap = iota((rows, 256), 0), iota((rows, 256), 1)
    moves = ((tap >> 6) == row % channels + sec * channels) & ((tap & 63) == row // channels)
    taps = dot_lanes(moves.astype(F32).astype(BF16), w1t)
    line, span = COLS * channels, 8 * channels
    blocks = {}
    for half in range(2):
        for p in range(NEAR):
            pieces = []
            for u in range(4):
                at = (4 * half + u) * span
                start = 4 * (p - 1) * channels
                cut = taps[at + max(0, -start) : at + min(span, line - start)]
                start = max(start, 0)
                pieces += [jnp.zeros((start, k1), F32)] if start else []
                pieces.append(cut)
                rest = line - start - cut.shape[0]
                pieces += [jnp.zeros((rest, k1), F32)] if rest else []
            blocks[half, p] = jnp.concatenate(pieces, axis=0)
    zero = jnp.zeros((4 * line, k1), F32)
    lines = []
    for r in range(STEP):
        cols = [
            blocks.get((r + 1 - yrel, p), zero) for yrel in range(STEP + 1) for p in range(NEAR)
        ]
        lines.append(jnp.concatenate(cols, axis=1))
    return jnp.concatenate(lines, axis=0).astype(BF16)


def first_kernel(
    section,
    frames_far,
    g1,
    w1t,
    other_far,
    after,
    c1,
    out,
    band,
    frames,
    acc,
    other,
    held,
    sems,
    draw_sems,
    *,
    draw,
):
    side, k1 = g1.shape[1], g1.shape[2]
    img, _, channels, _ = frames.shape
    steps = img // 4 // STEP
    arrives = frame_copies(section, frames_far, frames, sems, STEP)
    for g in range(steps):
        arrives(g).start()
    other_copy = pltpu.make_async_copy(
        other_far.at[0 : STEP * draw + 1], other, sems.at[steps]
    )
    other_copy.start()
    acc[...] = jnp.zeros_like(acc)
    zero = jnp.zeros((k1, LANES), BF16)

    def one_step(g, carry):
        arrives(g).wait()
        pixels, grads = [], []
        for j in range(img // COLS):
            rows = [pl.multiple_of(4 * (STEP * g + r), 4) for r in range(STEP)]
            pixels.append(
                jnp.concatenate([tile_rows(frames, row, j, COLS) for row in rows], axis=0)
            )
            pieces = []
            for yrel in range(STEP + 1):
                for p in range(NEAR):
                    x = 3 * j - 1 + p
                    pieces.append(g1[STEP * g + yrel, x] if 0 <= x < side else zero)
            grads.append(jnp.concatenate(pieces, axis=0))
        acc[...] += dot_lanes(jnp.concatenate(pixels, axis=1), jnp.concatenate(grads, axis=1))
        return carry

    lax.fori_loop(0, steps, one_step, 0)
    band[...] = pixel_band(section[0], w1t[...], out.shape[2])
    other_copy.wait()
    finish = draw_steps(section, band, g1, 0, other, 0, out, held, draw_sems, 0, draw)
    fold_first(acc, c1, channels, k1)
    finish()


def fold_first(acc, c1, channels, k1):
    line = COLS * channels
    step = 4 * channels
    taps = []
    for half in range(2):
        total = sum(
            acc[r * 4 * line : (r + 1) * 4 * line, :][
                :, (r + 1 - half) * NEAR * k1 : (r + 2 - half) * NEAR * k1
            ]
            for r in range(STEP)
        )
        for u in range(4):
            part = total[u * line : (u + 1) * line]
            cols = [part[:, p * k1 : (p + 1) * k1] for p in range(NEAR)]
            taps.append(cols[1][0:step] + cols[2][step : 2 * step] + cols[3][2 * step :])
            taps.append(cols[0][0:step] + cols[1][step : 2 * step] + cols[2][2 * step :])
    row, col = iota((256, 256), 0), iota((256, 256), 1)
    moves = ((row & 3) == (col >> 6)) & ((row >> 2) == (col & 63))
    grad = dot_rows(jnp.concatenate(taps, axis=0), moves.astype(F32), EXACT)
    for half in range(2):
        c1[half * k1 : (half + 1) * k1, :] = grad[:, half * LANES : (half + 1) * LANES].astype(BF16)


def draw_steps(section, band, mine, mine_at, other, other_at, out, held, sems, start, steps):
    side, k1 = mine.shape[1], mine.shape[2]
    img, channels = out.shape[1], out.shape[2]
    sec = section[0]
    line = COLS * channels
    flat = held.reshape(2, 2, 4 * STEP, img * channels, LANES)

    def writes(g):
        rows = slice(4 * STEP * (start + g), 4 * STEP * (start + g + 1))
        places = (sec * LANES, (1 - sec) * LANES)
        return [
            pltpu.make_async_copy(
                held.at[g % 2, k],
                out.at[rows, :, :, pl.ds(pl.multiple_of(places[k], LANES), LANES)],
                sems.at[g % 2, k],
            )
            for k in range(2)
        ]

    zero = jnp.zeros((k1, 2 * LANES), BF16)
    for g in range(steps):
        if g >= 2:
            for copy in writes(g - 2):
                copy.wait()
        for j in range(img // COLS):
            pieces = []
            for yrel in range(STEP + 1):
                for p in range(NEAR):
                    x, y = 3 * j - 1 + p, STEP * (start + g) + yrel
                    if 0 <= x < side:
                        pair = [mine[y - mine_at, x], other[y - other_at, x]]
                        pieces.append(jnp.concatenate(pair, axis=1))
                    else:
                        pieces.append(zero)
            got = dot(band[...], jnp.concatenate(pieces, axis=0))
            for k in range(4 * STEP):
                at = slice(k * line, (k + 1) * line)
                span = slice(j * line, (j + 1) * line)
                flat[g % 2, 0, k, span, :] = got[at, :LANES]
                flat[g % 2, 1, k, span, :] = got[at, LANES:]
        for copy in writes(g):
            copy.start()

    def finish():
        for g in range(max(steps - 2, 0), steps):
            for copy in writes(g):
                copy.wait()

    return finish


def pixels_kernel(section, band, mine, other_far, after, done, out, token, held, other, sems, *, start):
    steps = other.shape[0] // STEP
    fetch = pltpu.make_async_copy(
        other_far.at[STEP * start : STEP * (start + steps) + 1], other, sems.at[2, 0]
    )
    fetch.start()
    token[...] = jnp.zeros_like(token)
    fetch.wait()
    draw_steps(
        section, band, mine, 0, other, STEP * start, out, held, sems, start, steps
    )()


def two_parts(value):
    high = value.astype(BF16).astype(F32)
    return jnp.concatenate([high, value - high], axis=0).astype(BF16)


def one_part(pair):
    rows = pair.shape[0] // 2
    pair = pair.astype(F32)
    return pair[:rows] + pair[rows:]


def merge_kernel(keep, recv_one, recv_two, small, c2, sums, out_far, lines, out, sems):
    members = out.shape[0]
    size = keep.shape[0] // members
    k2 = c2.shape[0]
    lines[...] = jnp.zeros_like(lines)
    at = small.shape[0]
    lines[0:at, :] = small[...]
    for half in range(2):
        lines[at : at + k2, :] = c2[:, half * LANES : (half + 1) * LANES]
        at += k2
    lines[at : at + sums.shape[0], :] = sums[...]
    for k in range(members):
        at = slice(k * size, (k + 1) * size)
        recv, here = recv_one, k
        if k >= members // 2:
            recv, here = recv_two, k - members // 2
        got = recv[here * size : (here + 1) * size, :]
        out[k, 0:size, :] = (keep[at, :].astype(F32) + got.astype(F32)).astype(BF16)
        out[k, size:, :] = two_parts(lines[k * SHORT : (k + 1) * SHORT, :])
        pltpu.make_async_copy(out.at[k], out_far.at[k], sems.at[k]).start()
    for k in range(members):
        pltpu.make_async_copy(out.at[k], out_far.at[k], sems.at[k]).wait()


def cube_kernel(got, c1, out):
    members = got.shape[0]
    size = got.shape[1] - 2 * SHORT
    out[0:size, :] = sum(got[k, 0:size, :].astype(F32) for k in range(members)).astype(BF16)
    total = sum(one_part(got[k, size:, :]) for k in range(members))
    out[size : size + 2 * SHORT, :] = two_parts(total)
    out[size + 2 * SHORT :, :] = c1[...]


def add_kernel(a, b, after, out):
    size = a.shape[0] - 2 * SHORT - 32
    middle = slice(size, size + 2 * SHORT)
    for span in (slice(0, size), slice(size + 2 * SHORT, a.shape[0])):
        out[span, :] = (a[span, :].astype(F32) + b[span, :].astype(F32)).astype(BF16)
    out[middle, :] = two_parts(one_part(a[middle, :]) + one_part(b[middle, :]))


def relay_kernel(batch, *refs):
    parts, (one, two, out) = refs[:CUBE], refs[CUBE:]
    me = batch[0] % CUBE
    for k, part in enumerate(parts):
        out[me ^ k] = part[...]
    one[...] = out[: CUBE // 2]
    two[...] = out[CUBE // 2 :]


def piece_of(got, k):
    count = got[0].shape[0]
    return got[k // count].at[k % count]


def unpack_half(which, got, lw, bw, vw, stage, stage_b, sems):
    members = 2 * got[0].shape[0]
    size = stage.shape[0] // members
    linear_rows, width = lw.shape
    options = bw.shape[0]
    half = (linear_rows + options * width + width) // 2
    rest = linear_rows - half

    @pl.when(which == 0)
    def _():
        copies = []
        for k in range(members):
            start, end = k * size, min((k + 1) * size, half)
            stage[start:end, :] = piece_of(got, k)[0 : end - start, :].astype(F32)
            copies.append(
                pltpu.make_async_copy(stage.at[start:end], lw.at[start:end], sems.at[k])
            )
            copies[-1].start()
        for copy in copies:
            copy.wait()

    @pl.when(which == 1)
    def _():
        def rows(start, end):
            parts = []
            while start < end:
                k, at = start // size, start % size
                count = min(size - at, end - start)
                parts.append(piece_of(got, k)[at : at + count, :])
                start += count
            value = parts[0] if len(parts) == 1 else jnp.concatenate(parts, axis=0)
            return value.astype(F32)

        stage[0:rest, :] = rows(0, rest)
        copies = [pltpu.make_async_copy(stage.at[0:rest], lw.at[half:], sems.at[0])]
        copies[0].start()
        group = options // 3
        for o in range(options):
            stage_b[o] = rows(rest + o * width, rest + (o + 1) * width)
            if o % group == group - 1:
                part = slice(o + 1 - group, o + 1)
                copy = pltpu.make_async_copy(
                    stage_b.at[part], bw.at[part], sems.at[1 + o // group]
                )
                copy.start()
                copies.append(copy)
        at = rest + options * width
        stage[rest : rest + width, :] = rows(at, at + width)
        copies.append(
            pltpu.make_async_copy(stage.at[rest : rest + width], vw, sems.at[1 + options // group])
        )
        copies[-1].start()
        for copy in copies:
            copy.wait()


def own_kernel(section, one, two, lw, bw, vw, stage, stage_b, sems):
    unpack_half(section[0], (one, two), lw, bw, vw, stage, stage_b, sems)


def unpack_kernel(section, *refs):
    mine, other, refs = refs[0:2], refs[2:4], refs[4:]
    lw, bw, vw = refs[3:6]
    little = (len(refs) - 10) // 2
    far, near = refs[6 : 6 + little], refs[6 + little : 6 + 2 * little]
    loss, c1, b1, c2, b2, lb, bb, hw, hb, vb, ow, ob = near
    stage, stage_b, lines, sems = refs[-4:]
    options = bw.shape[0]
    k1, k2 = c1.shape[0], c2.shape[0]
    size = stage.shape[0] // CUBE
    grad = [jnp.zeros((k1, LANES), F32) for _ in range(2)]
    for k in range(CUBE):
        pair = slice(size, size + 2 * SHORT)
        at = slice(k * SHORT, (k + 1) * SHORT)
        views = piece_of(mine, k), piece_of(other, k)
        lines[at, :] = sum(one_part(v[pair, :]) for v in views)
        for view in views:
            for h in range(2):
                at = size + 2 * SHORT + h * k1
                grad[h] += view[at : at + k1, :].astype(F32)
    for part in range(2):
        c1[:, part * LANES : (part + 1) * LANES] = grad[part]
    bb[...] = lines[0:options, :]
    vb[...] = lines[AT_VB, :]
    ow[...] = lines[AT_OW, :]
    hw[...] = lines[AT_HW, :]
    lb[...] = lines[AT_LB, :]
    scalars = lines[AT_SCALARS, :]
    loss[...] = scalars[:, 0:1]
    hb[...] = scalars[:, 1:3]
    ob[...] = scalars[:, 3:4]
    at = TABLE
    for part in range(2):
        c2[:, part * LANES : (part + 1) * LANES] = lines[at : at + k2, :]
        at += k2
    b1[...] = lines[at : at + 1, 0:k1]
    b2[...] = lines[at + 1 : at + 2, 0:k2]
    copies = [
        pltpu.make_async_copy(a, b, sems.at[CUBE + k]) for k, (a, b) in enumerate(zip(near, far))
    ]
    for copy in copies:
        copy.start()
    unpack_half(1 - section[0], other, lw, bw, vw, stage, stage_b, sems)
    for copy in copies:
        copy.wait()


def numbers_kernel(
    options,
    depth,
    targets,
    destination,
    b1,
    b2,
    lb,
    bb,
    hw,
    vb,
    ow,
    hb,
    ob,
    out,
    table,
):
    levels, kinds = options.shape[0], targets.shape[0]
    slots = depth.shape[1]
    rows = [options[...].astype(F32), depth[...].astype(F32)]
    rows += [targets[k] for k in range(kinds)]
    rows.append(jnp.zeros((LANES - levels - 1 - kinds * levels, slots), F32))
    out[...] = jnp.transpose(jnp.concatenate(rows, axis=0))
    table[...] = jnp.zeros_like(table)
    table[0 : bb.shape[0], :] = bb[...]
    table[AT_VB, :] = vb[...]
    table[AT_OW, :] = ow[...].astype(F32)
    table[AT_HW, :] = hw[...].astype(F32)
    table[AT_LB, :] = lb[...]
    table[AT_B1, 0 : b1.shape[1]] = b1[...]
    table[AT_B2, 0 : b2.shape[1]] = b2[...]
    lane = iota((1, LANES), 1)
    scalars = jnp.zeros((1, LANES), F32)
    for k, value in ((1, hb[:, 0:1]), (2, hb[:, 1:2]), (3, ob[...])):
        scalars = jnp.where(lane == k, value, scalars)
    table[AT_SCALARS, :] = scalars
    for k in range(slots // LANES):
        part = destination[:, k * LANES : (k + 1) * LANES]
        table[AT_DEST + k : AT_DEST + k + 1, :] = part.astype(F32)


def whole(shape):
    zeros = (0,) * len(shape)
    return pl.BlockSpec(shape, lambda *_: zeros)


ANYWHERE = pl.BlockSpec(memory_space=pl.ANY)
SCALARS = pl.BlockSpec(memory_space=pltpu.SMEM)


def params():
    return pltpu.CompilerParams(vmem_limit_bytes=VMEM_BYTES)


def shape_of(*shape, dtype=F32):
    return jax.ShapeDtypeStruct(shape, dtype)


def cost(microseconds):
    return pl.CostEstimate(
        flops=int(1.1e9 * microseconds), bytes_accessed=int(3.6e6 * microseconds), transcendentals=0
    )


def stays(value):
    return pltpu.with_memory_space_constraint(value, pltpu.HBM)


def held_near(value):
    return pltpu.with_memory_space_constraint(value, pltpu.VMEM)


def encode(section, frames, w1t, w2t, lw, table):
    img = frames.shape[0]
    blocks = img // 4
    side = blocks - 1
    k1, k2, width = w1t.shape[0], w2t.shape[0], lw.shape[1]
    flat = lw.shape[0]
    vmem = pltpu.VMEM
    near = pl.BlockSpec(memory_space=vmem)
    grid_one = (blocks, side, k1, LANES)
    return pl.pallas_call(
        encode_kernel,
        in_specs=[SCALARS, ANYWHERE, near, near, ANYWHERE, near],
        out_specs=[ANYWHERE] * 3 + [near] * 3,
        out_shape=(
            pltpu.HBM(grid_one, BF16),
            pltpu.HBM(grid_one, BF16),
            pltpu.HBM((flat, LANES), BF16),
            shape_of(flat, LANES, dtype=BF16),
            shape_of(width, LANES, dtype=BF16),
            shape_of(width, LANES),
        ),
        scratch_shapes=[
            vmem((img, img, frames.shape[2], LANES), BF16),
            vmem(lw.shape, BF16),
            vmem(grid_one, BF16),
            vmem(grid_one, BF16),
            vmem((flat, LANES), BF16),
            vmem((2 * REACH * k1, 256), BF16),
            vmem((2 * k1, 64), BF16),
            vmem((6 * k2, LANES), BF16),
            vmem((k1, LANES), F32),
            vmem((k2, LANES), F32),
            vmem((side, k1, LANES), F32),
            vmem((side // 2 - 1, k2, LANES), F32),
            vmem((width, LANES), F32),
            pltpu.SemaphoreType.DMA((4, blocks // 2 + 1)),
        ],
        compiler_params=params(),
        cost_estimate=cost(9),
        name="encode",
    )(section, frames, w1t, w2t, lw, table)


def plan(section, slots, enc, s3, h2, branch_w, value_w, table, per_pair, depth, half_rows):
    width = enc.shape[0]
    options = branch_w.shape[0]
    two = 2 * width
    pairs = options // 2
    outs = (
        shape_of(half_rows, LANES, dtype=BF16),
        shape_of(half_rows // 2, LANES, dtype=BF16),
        shape_of(half_rows // 2, LANES, dtype=BF16),
        shape_of(TABLE, LANES),
        shape_of(width, LANES, dtype=BF16),
    )
    vmem = pltpu.VMEM
    near = pl.BlockSpec(memory_space=vmem)
    return pl.pallas_call(
        functools.partial(plan_kernel, per_pair=per_pair, depth=depth),
        in_specs=[SCALARS, near, near, near, near, ANYWHERE, near, near],
        out_shape=outs,
        scratch_shapes=[
            vmem((2, half_rows, LANES), BF16),
            vmem((options * width, width + 16), BF16),
            vmem((width + 16, width + 16), BF16),
            vmem((width, width + 16), BF16),
            vmem((width, LANES), F32),
            vmem((16, LANES), F32),
            vmem((options * width, LANES), F32),
            vmem((depth, options * width, LANES), F32),
            vmem((depth, pairs, width, two), F32),
            vmem((depth, pairs, width + 16, two), BF16),
            vmem((depth, pairs, width, two), BF16),
            vmem((depth, options * width, LANES), BF16),
            vmem(branch_w.shape, BF16),
            pltpu.SemaphoreType.DMA,
        ],
        compiler_params=params(),
        cost_estimate=cost(11),
        name="plan",
    )(section, slots, enc, s3, h2, branch_w, value_w, table)


def back(g3, lw, s2, s1, h1, w2t):
    _, side, k1 = s1.shape[:3]
    k2 = w2t.shape[0]
    inner = side // 2 - 1
    padded = (side + 2, side, k1, LANES)
    near = pl.BlockSpec(memory_space=pltpu.VMEM)
    return pl.pallas_call(
        back_kernel,
        in_specs=[near] * 6,
        out_shape=(shape_of(*padded, dtype=BF16), shape_of(k2, 256), shape_of(8, LANES)),
        scratch_shapes=[
            pltpu.VMEM((LANES, 6 * k2), BF16),
            pltpu.VMEM((inner + 2, inner, k2, LANES), BF16),
        ],
        compiler_params=params(),
        cost_estimate=cost(25),
        name="back",
    )(g3, lw, s2, s1, h1, w2t)


def first(section, frames, g1, w1t, other, after, channels, draw):
    img, _, stack, _ = frames.shape
    k1 = g1.shape[2]
    band = (STEP * 4 * COLS * channels, (STEP + 1) * NEAR * k1)
    near = pl.BlockSpec(memory_space=pltpu.VMEM)
    return pl.pallas_call(
        functools.partial(first_kernel, draw=draw),
        in_specs=[SCALARS, ANYWHERE, near, near, ANYWHERE, ANYWHERE],
        out_specs=[near, ANYWHERE, near],
        out_shape=[
            shape_of(2 * k1, LANES, dtype=BF16),
            shape_of(img, img, channels, 2 * LANES),
            shape_of(*band, dtype=BF16),
        ],
        scratch_shapes=[
            pltpu.VMEM((img, img, stack, LANES), BF16),
            pltpu.VMEM((STEP * 4 * COLS * stack, (STEP + 1) * NEAR * k1), F32),
            pltpu.VMEM((STEP * draw + 1,) + g1.shape[1:], BF16),
            pltpu.VMEM((2, 2, 4 * STEP, img, channels, LANES), F32),
            pltpu.SemaphoreType.DMA((img // 4 // STEP + 1,)),
            pltpu.SemaphoreType.DMA((2, 2)),
        ],
        compiler_params=params(),
        cost_estimate=cost(45),
        name="first",
    )(section, frames, g1, w1t, other, after)


def pixels(section, band, mine, other, after, done, start):
    img, _, channels, _ = done.shape
    steps = img // 4 // STEP - start
    near = pl.BlockSpec(memory_space=pltpu.VMEM)
    return pl.pallas_call(
        functools.partial(pixels_kernel, start=start),
        in_specs=[SCALARS, near, near, ANYWHERE, ANYWHERE, ANYWHERE],
        out_specs=[ANYWHERE, near],
        out_shape=[shape_of(*done.shape), shape_of(8, LANES)],
        scratch_shapes=[
            pltpu.VMEM((2, 2, 4 * STEP, img, channels, LANES), F32),
            pltpu.VMEM((STEP * steps + 1,) + mine.shape[1:], BF16),
            pltpu.SemaphoreType.DMA((3, 2)),
        ],
        input_output_aliases={5: 0},
        compiler_params=params(),
        cost_estimate=cost(1 + 0.9 * steps),
        name="pixels",
    )(section, band, mine, other, after, done)


def small_call(
    kernel, outs, operands, scratch=(), name=None, place=None, after=(), weight=0.3, far=False
):
    specs = [pl.BlockSpec(memory_space=pltpu.VMEM)] * len(operands)
    if place is not None:
        operands = (*place, *operands)
        specs = [pl.BlockSpec(memory_space=pltpu.SMEM)] * len(place) + specs
    return pl.pallas_call(
        kernel,
        in_specs=specs + [ANYWHERE] * len(after),
        out_specs=jax.tree.map(
            lambda _: ANYWHERE if far else pl.BlockSpec(memory_space=pltpu.VMEM), outs
        ),
        out_shape=outs,
        scratch_shapes=list(scratch),
        compiler_params=params(),
        cost_estimate=cost(weight),
        name=name,
    )(*operands, *after)


def round_up(value, step):
    return -(-value // step) * step


def swapped(value):
    return lax.ppermute(value, "section", [(0, 1), (1, 0)])


def exchanged(value, groups=None):
    return lax.all_to_all(
        value, "batch", split_axis=0, concat_axis=0, axis_index_groups=groups, tiled=True
    )


def partner(value, distance):
    count = lax.axis_size("batch")
    return lax.ppermute(value, "batch", [(b, b ^ distance) for b in range(count)])


def local(
    frames,
    destination,
    options,
    depth,
    targets,
    conv_one,
    bias_one,
    conv_two,
    bias_two,
    linear_w,
    linear_b,
    branch_w,
    branch_b,
    head_w,
    head_b,
    value_w,
    value_b,
    out_w,
    out_b,
):
    section = lax.axis_index("section").astype(jnp.int32)[None]
    peers = lax.axis_size("batch")
    frame_count = frames.shape[3]
    per_pair = frame_count // peers
    levels = options.shape[0]
    frames = stays(frames.transpose(1, 2, 0, 3))
    w1t, w2t = stays(conv_one.T), stays(conv_two.T)
    branch_w, value_w = stays(branch_w), stays(value_w)
    encoder_params = (w1t, bias_one, w2t, bias_two, linear_w, linear_b)
    planner_params = (branch_w, branch_b, head_w.T, head_b, value_w, value_b, out_w.T, out_b)
    width = linear_w.shape[1]
    big_rows = linear_w.shape[0] + (branch_w.shape[0] + 1) * width
    size = round_up(-(-big_rows // (2 * CUBE)), 16)

    tiny = (bias_one, bias_two, linear_b, branch_b, head_w.T, value_b, out_w.T)
    tiny = [stays(v if v.ndim > 1 else v[None, :]) for v in tiny]
    numbers, table = pl.pallas_call(
        numbers_kernel,
        in_specs=[pl.BlockSpec(memory_space=pltpu.VMEM)] * (6 + len(tiny)),
        out_shape=[shape_of(frame_count, LANES), shape_of(TABLE, LANES)],
        compiler_params=params(),
        cost_estimate=cost(1),
        name="numbers",
    )(
        stays(options),
        stays(depth[None, :]),
        stays(targets),
        stays(destination[None, :]),
        *tiny,
        stays(head_b[None, :]),
        out_b[None, :],
    )
    slots = exchanged(numbers.reshape(peers, per_pair, LANES)).reshape(frame_count, LANES)

    h1, s1, s2, h2, enc, s3 = encode(section, frames, w1t, w2t, stays(linear_w), table)
    keep, send_one, send_two, small, g3 = plan(
        section, slots, enc, s3, h2, branch_w, value_w, table, per_pair, levels, CUBE * size
    )
    recv = swapped(send_one), swapped(send_two)
    channels = frames.shape[2] // lax.axis_size("section")
    g1, c2, sums = back(g3, linear_w, s2, s1, h1, w2t)
    other = swapped(g1)
    g1 = held_near(g1)
    cubes = [list(range(c, c + CUBE)) for c in range(0, peers, CUBE)]
    bf16 = functools.partial(shape_of, dtype=BF16)
    pieces = small_call(
        merge_kernel,
        bf16(CUBE, size + 2 * SHORT, LANES),
        (keep, *recv, small, c2, sums),
        [
            pltpu.VMEM((CUBE * SHORT, LANES), F32),
            pltpu.VMEM((CUBE, size + 2 * SHORT, LANES), BF16),
            pltpu.SemaphoreType.DMA((CUBE,)),
        ],
        name="merge",
        far=True,
        weight=30,
    )
    got = exchanged(pieces, cubes)
    c1, frames_grad, band = first(section, frames, g1, w1t, other, pieces, channels, DRAW)
    piece = bf16(size + 2 * SHORT + c1.shape[0], LANES)
    keep = small_call(cube_kernel, piece, (got, c1), name="cube")
    distance = CUBE
    while distance < peers:
        recv = partner(keep, distance)
        if distance == CUBE:
            frames_grad, token = pixels(section, band, g1, other, keep, frames_grad, DRAW)
        distance *= 2
        keep = small_call(add_kernel, piece, (keep, recv), name="add", after=(token,))
    parts = [keep] + [partner(keep, k) for k in range(1, CUBE)]
    place = (lax.axis_index("batch").astype(jnp.int32)[None],)
    got = small_call(
        relay_kernel,
        [bf16(CUBE // 2, *piece.shape)] * 2,
        parts,
        [pltpu.VMEM((CUBE, *piece.shape), BF16)],
        name="relay",
        place=place,
    )
    got_other = [swapped(v) for v in got]
    shapes = [p.shape for p in encoder_params + planner_params]
    near = pl.BlockSpec(memory_space=pltpu.VMEM)
    flat = [shape_of(*(v if len(v) > 1 else (1,) + v)) for v in [(1, 1)] + shapes]
    large = [flat[k] for k in (5, 7, 11)]
    staged = [
        pltpu.VMEM((CUBE * size, LANES), F32),
        pltpu.VMEM(branch_w.shape, F32),
    ]
    little = [v for k, v in enumerate(flat) if k not in (5, 7, 11)]
    sems = pltpu.SemaphoreType.DMA((CUBE + len(little),))
    begun = pl.pallas_call(
        own_kernel,
        in_specs=[SCALARS, near, near],
        out_specs=[ANYWHERE] * 3,
        out_shape=large,
        scratch_shapes=[*staged, sems],
        compiler_params=params(),
        cost_estimate=cost(1),
        name="own",
    )(section, *got)
    ends = pl.pallas_call(
        unpack_kernel,
        in_specs=[SCALARS] + [near] * 4 + [ANYWHERE] * 3,
        out_specs=[ANYWHERE] * (3 + len(little)),
        out_shape=large + little,
        scratch_shapes=[pltpu.VMEM(v.shape, F32) for v in little]
        + [*staged, pltpu.VMEM((CUBE * SHORT, LANES), F32), sems],
        input_output_aliases={5: 0, 6: 1, 7: 2},
        compiler_params=params(),
        cost_estimate=cost(1.5),
        name="unpack",
    )(section, *got, *got_other, *begun)
    rest = list(ends[3:])
    for k, at in enumerate((5, 7, 11)):
        rest.insert(at, ends[k])
    rest = [v.reshape(s) for v, s in zip(rest, [()] + shapes)]
    for at in (1, 3, 9, 13):
        rest[at] = rest[at].T
    return (rest[0], frames_grad.transpose(2, 0, 1, 3), *rest[1:])


def solution(mesh):
    placed = (
        P(None, None, None, "batch"),
        P("batch"),
        P(None, "batch"),
        P("batch"),
        P(None, None, "batch"),
    ) + (P(),) * 14
    return jax.shard_map(
        local,
        mesh=mesh,
        in_specs=placed,
        out_specs=(P(), P("section", None, None, "batch")) + (P(),) * 14,
        check_vma=False,
    )
```

```python
import functools
import math

import jax
import jax.numpy as jnp
from jax import lax
from jax.experimental import pallas as pl
from jax.experimental.pallas import tpu as pltpu
from jax.sharding import PartitionSpec as P

BF16 = jnp.bfloat16
F32 = jnp.float32
EXACT = lax.Precision.HIGHEST
LANES = 128
VMEM_BYTES = 32 * 1024 * 1024
TILE = 16
REACH = 5
STEP = 3
COLS = 12
NEAR = 4
AT_VB, AT_OW, AT_HW, AT_LB, AT_SCALARS, AT_B1, AT_B2, AT_DEST = (
    slice(18, 19),
    slice(19, 20),
    slice(20, 22),
    slice(22, 23),
    slice(23, 24),
    slice(24, 25),
    slice(25, 26),
    26,
)
TABLE = 32
CUBE = 8
DRAW = 4
SHORT = 16


def dot(a, b, precision=None):
    return jnp.dot(a, b, preferred_element_type=F32, precision=precision)


def dot_rows(a, b, precision=None):
    return lax.dot_general(
        a, b, (((0,), (0,)), ((), ())), preferred_element_type=F32, precision=precision
    )


def dot_lanes(a, b, precision=None):
    return lax.dot_general(
        a, b, (((1,), (1,)), ((), ())), preferred_element_type=F32, precision=precision
    )


def iota(shape, axis):
    return lax.broadcasted_iota(jnp.int32, shape, axis)


def column(row):
    n = row.shape[1]
    wide = jnp.broadcast_to(row, (n, n))
    return jnp.sum(jnp.where(iota((n, n), 0) == iota((n, n), 1), wide, 0.0), axis=1, keepdims=True)


def row_of(col):
    n = col.shape[0]
    wide = jnp.broadcast_to(col, (n, n))
    return jnp.sum(jnp.where(iota((n, n), 0) == iota((n, n), 1), wide, 0.0), axis=0, keepdims=True)


def soft(x):
    t = jnp.tanh(0.5 * x)
    return jnp.maximum(x, 0.0) - jnp.log(0.5 + 0.5 * jnp.abs(t)), 0.5 + 0.5 * t


def silu_pair(y):
    t = jnp.tanh(y)
    m = y * t
    return y + m, (1.0 + t) + (y - m * t)


def pixel_order(w1t):
    tap, pix = iota((256, 256), 0), iota((256, 256), 1)
    moves = ((tap >> 6) == (pix & 3)) & ((tap & 63) == (pix >> 2))
    return dot(w1t, moves.astype(F32).astype(BF16))


def frame_copies(section, far, here, sems):
    lanes = pl.ds(pl.multiple_of(section[0] * LANES, LANES), LANES)
    size = 4 * STEP

    def copy(g):
        rows = pl.ds(pl.multiple_of(g * size, size), size)
        return pltpu.make_async_copy(far.at[rows, :, :, lanes], here.at[rows], sems.at[g])

    return copy


def tile_rows(frames, row, j, cols):
    img, _, channels, _ = frames.shape
    flat = frames.reshape(img, img * channels, LANES)
    size = cols * channels
    end = min((j + 1) * size, img * channels)
    part = flat[pl.ds(row, 4), j * size : end, :]
    return part.reshape(4 * (end - j * size), LANES)


def encode_kernel(
    section,
    frames_far,
    w1t,
    w2t,
    lw_far,
    table,
    h1_far,
    s1_far,
    s2_far,
    h2,
    enc,
    s3,
    frames,
    lw,
    h1,
    s1,
    s2,
    band,
    edge,
    band2,
    bias1,
    bias2,
    held,
    held2,
    sems,
):
    blocks, side = h1.shape[:2]
    steps = blocks // STEP
    tiles = frames.shape[1] // TILE
    k1, k2 = w1t.shape[0], w2t.shape[0]
    reach_rows = REACH * k1
    arrives = frame_copies(section, frames_far, frames, sems.at[0])
    for g in range(steps):
        arrives(g).start()
    last_copies = [
        pltpu.make_async_copy(lw_far, lw, sems.at[3, 0]),
        pltpu.make_async_copy(s2, s2_far, sems.at[3, 1]),
    ]
    last_copies[0].start()

    def leaves(g):
        rows = pl.ds(g * STEP, STEP)
        return [
            pltpu.make_async_copy(h1.at[rows], h1_far.at[rows], sems.at[1, g]),
            pltpu.make_async_copy(s1.at[rows], s1_far.at[rows], sems.at[2, g]),
        ]

    inner = side // 2 - 1
    row_len = inner * k2
    two = 2 * k2 * 3

    def prepare():
        taps = pixel_order(w1t[...])
        edges = []
        for half in range(2):
            lines = [taps[:, 32 * (4 * half + u) : 32 * (4 * half + u + 1)] for u in range(4)]
            for place in range(REACH):
                pieces = []
                for line in lines:
                    start = 16 * (place - 1)
                    cut = line[:, max(0, -start) : min(32, 64 - start)]
                    start = max(start, 0)
                    pieces += [jnp.zeros((k1, start), F32)] if start else []
                    pieces.append(cut)
                    rest = 64 - start - cut.shape[1]
                    pieces += [jnp.zeros((k1, rest), F32)] if rest else []
                at = half * reach_rows + place * k1
                band[at : at + k1, :] = jnp.concatenate(pieces, axis=1).astype(BF16)
            edges.append(jnp.concatenate([line[:, 16:] for line in lines], axis=1))
        edge[...] = jnp.concatenate(edges, axis=0).astype(BF16)
        tap, pix = iota((256, LANES), 0), iota((256, LANES), 1)
        for half in range(2):
            for place in range(3):
                hit = (
                    ((tap & 15) == (pix & 15))
                    & ((tap >> 6) == (pix >> 6) + 2 * half)
                    & (((tap >> 4) & 3) == ((pix >> 4) & 3) + 2 - 2 * place)
                )
                at = (half * 3 + place) * k2
                taps = dot(w2t[...], hit.astype(F32).astype(BF16))
                band2[at : at + k2, :] = taps.astype(BF16)
        bias1[...] = jnp.broadcast_to(column(table[AT_B1, 0:k1]), bias1.shape)
        bias2[...] = jnp.broadcast_to(column(table[AT_B2, 0:k2]), bias2.shape)
        held[...] = jnp.zeros_like(held)
        held2[...] = jnp.zeros_like(held2)
        h1[...] = jnp.zeros_like(h1)

    def added(sums, x, value):
        sums[x] = sums[x] + value if x in sums else value

    def second_matmul(b):
        tiles = [
            h1[pl.ds(2 * b + 1, 2), 4 * j : 4 * j + 4].reshape(LANES, LANES)
            for j in range(side // 4)
        ]
        return dot(band2[...], jnp.concatenate(tiles, axis=1))

    def second_rows(b, got):
        low, high = {}, {}
        for j in range(side // 4):
            for place in range(3):
                x = 2 * j - 1 + place
                if 0 <= x < inner:
                    span = slice(j * LANES, (j + 1) * LANES)
                    at = place * k2
                    added(low, x, got[at : at + k2, span])
                    added(high, x, got[two // 2 + at : two // 2 + at + k2, span])
        row = jnp.maximum(b - 1, 0) * row_len
        for x in range(inner):
            value, slope = soft(held2[x] + high[x] + bias2[...])
            held2[x] = low[x]
            at = pl.ds(pl.multiple_of(row + x * k2, k2), k2)
            h2[at, :] = value.astype(BF16)
            s2[at, :] = slope.astype(BF16)

    def one_step(g, carry):
        def row(r):
            return pl.multiple_of(4 * (STEP * g + r), 4)

        arrives(g).wait()
        lows, highs = [{} for _ in range(STEP)], [{} for _ in range(STEP)]

        def place_tile(r, j, got):
            for place in range(REACH):
                x = 4 * j - 1 + place
                if 0 <= x < side:
                    at = place * k1
                    added(lows[r], x, got[at : at + k1])
                    added(highs[r], x, got[reach_rows + at : reach_rows + at + k1])

        def finish(r, xs):
            for x in xs:
                value, slope = soft(held[x] + highs[r][x] + bias1[...])
                held[x] = lows[r][x]
                h1[STEP * g + r, x] = value.astype(BF16)
                s1[STEP * g + r, x] = slope.astype(BF16)

        pair = jnp.maximum(g - 1, 0)
        units = [(lambda: second_matmul(pair), lambda got: second_rows(pair, got))]

        def edges():
            parts = [tile_rows(frames, row(r), tiles, TILE) for r in range(STEP)]
            return dot(edge[...], jnp.concatenate(parts, axis=1))

        def place_edges(got):
            for r in range(STEP):
                added(lows[r], side - 1, got[:k1, r * LANES : (r + 1) * LANES])
                added(highs[r], side - 1, got[k1:, r * LANES : (r + 1) * LANES])

        units.append((edges, place_edges))

        def full(spots):
            parts = [tile_rows(frames, row(r), j, TILE) for r, j in spots]
            return dot(band[...], jnp.concatenate(parts, axis=1))

        def place_full(got, spots, ready):
            for i, (r, j) in enumerate(spots):
                place_tile(r, j, got[:, i * LANES : (i + 1) * LANES])
            if ready:
                finish(*ready)

        for r in range(STEP):
            if r % 2 == 0:
                spots = [(k, tiles - 1) for k in (r, r + 1) if k < STEP]
                units.append(
                    (
                        functools.partial(full, spots),
                        functools.partial(place_full, spots=spots, ready=None),
                    )
                )
            done = 0
            for j in range(0, tiles - 1, 2):
                spots = [(r, j), (r, j + 1)]
                ready = side if j + 2 == tiles - 1 else 4 * j + 7
                units.append(
                    (
                        functools.partial(full, spots),
                        functools.partial(place_full, spots=spots, ready=(r, range(done, ready))),
                    )
                )
                done = ready
        waiting = None
        for issue, take in units:
            got = issue()
            if waiting is not None:
                waiting[0](waiting[1])
            waiting = (take, got)
        waiting[0](waiting[1])
        for copy in leaves(g):
            copy.start()
        return carry

    prepare()
    lax.fori_loop(0, steps, one_step, 0)
    for b in range(steps - 1, side // 2):
        second_rows(b, second_matmul(b))
    for copy in last_copies[1:]:
        copy.start()
    last_copies[0].wait()
    value, slope = soft(dot_rows(lw[...], h2[...]) + column(table[AT_LB, :]))
    enc[...] = value.astype(BF16)
    s3[...] = slope
    for g in range(steps):
        for copy in leaves(g):
            copy.wait()
    for copy in last_copies[1:]:
        copy.wait()


def three_parts(row):
    high = row.astype(BF16).astype(F32)
    middle = (row - high).astype(BF16).astype(F32)
    return jnp.concatenate([high, middle, row - high - middle], axis=0)


def with_ones(value):
    return jnp.concatenate([value, ones_rows(value.shape[1])], axis=0)


def ones_rows(lanes):
    return (iota((16, lanes), 0) < 3).astype(F32).astype(BF16)


def plan_kernel(
    section,
    slots,
    enc,
    s3,
    h2,
    branch_far,
    value_w,
    table,
    keep,
    send_one,
    send_two,
    small,
    g3,
    parts,
    bwt,
    vht,
    vhw,
    ow,
    mine,
    pre,
    dbr,
    dval,
    low,
    hid,
    gb,
    rounded_all,
    saved,
    losses,
    out_all,
    value_all,
    branch_w,
    sem,
    *,
    per_pair,
    depth,
):
    width = enc.shape[0]
    options = branch_w.shape[0]
    pairs = options // 2
    two = 2 * width
    sec = section[0]
    branch_copy = pltpu.make_async_copy(branch_far, branch_w, sem)
    branch_copy.start()

    count = slots.shape[0]
    dest = jnp.concatenate(
        [table[AT_DEST + k : AT_DEST + k + 1, :] for k in range(count // LANES)], axis=1
    )
    own = jnp.where(sec == 0, dest[:, :LANES], dest[:, LANES:])
    others = jnp.transpose(jnp.broadcast_to(dest, (LANES, count)))
    index = iota((count, LANES), 1) + sec * LANES
    earlier = (others == own) & (iota((count, LANES), 0) < index)
    rank = jnp.sum(earlier.astype(F32), axis=0, keepdims=True)
    bucket = own * float(per_pair) + rank
    chosen = (iota((count, LANES), 0).astype(F32) == bucket).astype(F32).astype(BF16)
    numbers = slots[...]
    high = numbers.astype(BF16)
    middle = (numbers - high.astype(F32)).astype(BF16)
    rest = (numbers - high.astype(F32) - middle.astype(F32)).astype(BF16)
    mine[...] = sum(dot_rows(v, chosen) for v in (rest, middle, high))[: mine.shape[0]]

    pad = jnp.zeros((13, width), F32)
    branch_copy.wait()
    for o in range(options):
        rows = [branch_w[o].astype(F32), three_parts(table[o : o + 1, :]), pad]
        bwt[o * width : (o + 1) * width, :] = jnp.transpose(
            0.5 * jnp.concatenate(rows, axis=0)
        ).astype(BF16)
    scalars = table[AT_SCALARS, :]
    head_w = table[AT_HW, :]
    rows = [value_w[...].astype(F32), three_parts(table[AT_VB, :]), pad]
    vht[0:width, :] = jnp.transpose(0.5 * jnp.concatenate(rows, axis=0)).astype(BF16)
    vht[width:, :] = jnp.zeros((16, width + 16), BF16)
    lane = iota((1, 16), 1)
    for k in range(2):
        bias = three_parts(jnp.broadcast_to(scalars[:, 1 + k : 2 + k], (1, 16)))
        bias = sum(jnp.where(lane == j, bias[j : j + 1], 0.0) for j in range(3))
        vht[width + k : width + k + 1, 0:width] = head_w[k : k + 1].astype(BF16)
        vht[width + k : width + k + 1, width:] = bias.astype(BF16)
    vhw[:, 0:width] = (0.5 * value_w[...].astype(F32)).astype(BF16)
    vhw[:, width:] = jnp.transpose(
        0.5 * jnp.concatenate([head_w, jnp.zeros((14, width), F32)], axis=0)
    ).astype(BF16)
    ow[...] = jnp.broadcast_to(column(table[AT_OW, :]), (width, LANES))
    wide_ow = jnp.concatenate([ow[...], ow[...]], axis=1)
    half_ow = 0.5 * wide_ow

    labels = iota((options, LANES), 0).astype(F32)
    group = 3

    def ahead(level, state):
        picked = labels == mine[pl.ds(level, 1), :]
        rounded = state.astype(BF16)
        rounded_all[level] = rounded
        met = with_ones(rounded)

        def branches(first):
            at = slice(first * two, (first + group) * two)
            pre[at, :] = dot(bwt[at, :], met)

        branches(0)
        following = state
        reward, discount, value = [], [], []

        def value_part(t, got):
            act, slope = silu_pair(got[:width])
            dval[level, t] = slope
            hidden = act.astype(BF16)
            hid[level, t] = hidden
            worth = jnp.sum(hidden.astype(F32) * wide_ow, axis=0, keepdims=True)
            for k in range(2):
                span = slice(k * LANES, (k + 1) * LANES)
                value.append(worth[:, span])
                reward.append(got[width : width + 1, span])
                discount.append(got[width + 1 : width + 2, span])

        waiting = None
        for first in range(0, pairs, group):
            if first + group < pairs:
                branches(first + group)
            boths = []
            for t in range(first, first + group):
                at = slice(t * two, (t + 1) * two)
                act, slope = silu_pair(pre[at, :])
                dbr[level, at, :] = slope
                left = state + act[:width]
                right = state + act[width:]
                following = jnp.where(picked[2 * t : 2 * t + 1], left, following)
                following = jnp.where(picked[2 * t + 1 : 2 * t + 2], right, following)
                both = with_ones(
                    jnp.concatenate([left.astype(BF16), right.astype(BF16)], axis=1)
                )
                low[level, t] = both
                boths.append(both)
            got = dot(vht[...], jnp.concatenate(boths, axis=1))
            if waiting is not None:
                for k in range(group):
                    value_part(waiting[0] + k, waiting[1][:, k * two : (k + 1) * two])
            waiting = (first, got)
        for k in range(group):
            value_part(waiting[0] + k, waiting[1][:, k * two : (k + 1) * two])
        reward = jnp.concatenate(reward, axis=0)
        discount = jax.nn.sigmoid(jnp.concatenate(discount, axis=0))
        value = jnp.concatenate(value, axis=0) + scalars[:, 3:4]
        quality = reward + discount * value
        top = jnp.max(quality, axis=0, keepdims=True)
        shifted = jnp.exp(quality - top)
        total = jnp.sum(shifted, axis=0, keepdims=True)
        live = (mine[depth : depth + 1, :] > level.astype(F32)).astype(F32)
        chosen = picked.astype(F32)

        def target(kind):
            return mine[pl.ds(depth + 1 + kind * depth + level, 1), :]

        reward_gap = live * (jnp.sum(chosen * reward, axis=0, keepdims=True) - target(0))
        discount_gap = live * (jnp.sum(chosen * discount, axis=0, keepdims=True) - target(1))
        plan_gap = live * (top + jnp.log(total) - target(2))
        grad_quality = plan_gap * (shifted / total)
        head_two = (chosen * discount_gap + grad_quality * value) * discount * (1.0 - discount)
        saved[level, 0] = chosen
        saved[level, 1] = (chosen * reward_gap + grad_quality).astype(BF16).astype(F32)
        saved[level, 2] = head_two.astype(BF16).astype(F32)
        saved[level, 3] = (grad_quality * discount).astype(BF16).astype(F32)
        losses[...] += reward_gap * reward_gap + discount_gap * discount_gap + plan_gap * plan_gap
        return following

    losses[...] = jnp.zeros_like(losses)
    lax.fori_loop(0, depth, ahead, enc[...].astype(F32))

    line = iota((16, two), 0)
    out_all[...] = jnp.zeros_like(out_all)
    value_all[...] = jnp.zeros_like(value_all)

    def behind(turn, grad_next):
        level = depth - 1 - turn
        picked = saved[level, 0] > 0.0
        head_one, head_two, grad_value = (saved[level, k] for k in (1, 2, 3))
        out_sum = jnp.zeros((16, width), F32)
        value_sum = jnp.zeros((width + 16, width + 16), F32)
        upward = jnp.zeros((width, LANES), F32)

        def branch_part(t, moved):
            at = slice(t * two, (t + 1) * two)
            left, right = moved[:, :LANES], moved[:, LANES:]
            left = left + jnp.where(picked[2 * t : 2 * t + 1], grad_next, 0.0)
            right = right + jnp.where(picked[2 * t + 1 : 2 * t + 2], grad_next, 0.0)
            grad_branch = jnp.concatenate([left, right], axis=0) * dbr[level, at, :]
            grad_branch = grad_branch.astype(BF16)
            gb[level, at, :] = grad_branch
            return left + right

        def group_part(first, moved):
            parts = [
                branch_part(first + k, moved[:, k * two : (k + 1) * two]) for k in range(group)
            ]
            at = slice(first * two, (first + group) * two)
            weights = [branch_w[o] for o in range(2 * first, 2 * (first + group))]
            return sum(parts), dot(jnp.concatenate(weights, axis=1), gb[level, at, :])

        waiting = None
        for first in range(0, pairs, group):
            stack = []
            for t in range(first, first + group):

                def across(rows):
                    return jnp.concatenate(
                        [rows[2 * t : 2 * t + 1], rows[2 * t + 1 : 2 * t + 2]], axis=1
                    )

                worth = across(grad_value)
                grad_pre = (worth * half_ow * dval[level, t]).astype(BF16)
                heads = jnp.where(line == 0, across(head_one), 0.0)
                heads = jnp.where(line == 1, across(head_two), heads)
                heads = jnp.where(line == 2, worth, heads)
                heads = heads.astype(BF16)
                out_sum = out_sum + dot_lanes(heads, hid[level, t])
                stack.append(jnp.concatenate([grad_pre, heads], axis=0))
            stack = jnp.concatenate(stack, axis=1)
            moved = dot(vhw[...], stack)
            lows = jnp.concatenate([low[level, first + k] for k in range(group)], axis=1)
            value_sum = value_sum + dot_lanes(stack, lows)
            if waiting is not None:
                one, other = group_part(*waiting)
                upward = upward + (one + 0.5 * other)
            waiting = (first, moved)
        one, other = group_part(*waiting)
        out_all[...] += out_sum
        value_all[...] += value_sum
        return upward + (one + 0.5 * other)

    grad_next = lax.fori_loop(0, depth, behind, jnp.zeros((width, LANES), F32))
    out_sum, value_sum = out_all[...], value_all[...]

    linear_rows = h2.shape[0]
    half = (linear_rows + options * width + width) // 2
    rest = linear_rows - half
    rounded = with_ones(jnp.concatenate([rounded_all[k] for k in range(depth)], axis=1))
    small[...] = jnp.zeros_like(small)
    if half < keep.shape[0]:
        for k in range(2):
            parts[k, half:, :] = jnp.zeros((keep.shape[0] - half, LANES), BF16)
    for t in range(pairs):
        at = slice(t * two, (t + 1) * two)
        grads = jnp.concatenate([gb[level, at, :] for level in range(depth)], axis=1)
        got = dot_lanes(rounded, grads)
        for k in range(2):
            o = 2 * t + k
            span = slice(k * width, (k + 1) * width)
            rows = slice(rest + o * width, rest + (o + 1) * width)
            parts[1 - sec, rows, :] = got[:width, span].astype(BF16)
            small[o : o + 1, :] = got[width : width + 1, span]
    after = rest + options * width
    parts[1 - sec, after : after + width, :] = jnp.transpose(value_sum[:width, :width]).astype(BF16)

    grad_three = ((2.0 * grad_next).astype(BF16).astype(F32) * s3[...]).astype(BF16)
    g3[...] = grad_three
    chunk = linear_rows // 9
    for i in range(8):
        at = slice(i * chunk, (i + 1) * chunk)
        parts[sec, at, :] = dot_lanes(h2[at, :], grad_three).astype(BF16)
    last = dot_lanes(h2[8 * chunk :, :], grad_three).astype(BF16)
    parts[sec, 8 * chunk : half, :] = last[: half - 8 * chunk]
    parts[1 - sec, 0:rest, :] = last[half - 8 * chunk :]
    keep[...] = parts[0]
    send_one[...] = parts[1, : send_one.shape[0]]
    send_two[...] = parts[1, send_one.shape[0] :]

    small[AT_VB, :] = row_of(value_sum[:width, width : width + 1])
    small[AT_OW, :] = out_sum[2:3]
    small[AT_HW, :] = value_sum[width : width + 2, :width]
    small[AT_LB, :] = row_of(jnp.sum(grad_three.astype(F32), axis=1, keepdims=True))
    loss = 0.5 * jnp.sum(losses[...], axis=1, keepdims=True)
    ends = [loss] + [value_sum[width + k : width + k + 1, width : width + 1] for k in range(3)]
    lane = iota((1, LANES), 1)
    line = jnp.zeros((1, LANES), F32)
    for k, end in enumerate(ends):
        line = jnp.where(lane == k, end, line)
    small[AT_SCALARS, :] = line


def back_kernel(g3, lw, s2, s1, h1, w2t, g1, c2, sums, t2, g2):
    side, k1 = s1.shape[1], s1.shape[2]
    k2 = w2t.shape[0]
    inner = side // 2 - 1
    row_len = inner * k2
    tap, pix = iota((LANES, 256), 1), iota((LANES, 256), 0)
    for yrel in range(2):
        for p in range(3):
            hit = (
                ((tap & 15) == (pix & 15))
                & ((tap >> 6) == (pix >> 6) + 2 * (1 - yrel))
                & (((tap >> 4) & 3) == ((pix >> 4) & 3) + 2 - 2 * p)
            )
            at = (yrel * 3 + p) * k2
            t2[:, at : at + k2] = dot_lanes(hit.astype(F32).astype(BF16), w2t[...]).astype(BF16)
    g2[0] = jnp.zeros(g2.shape[1:], BF16)
    g2[inner + 1] = jnp.zeros(g2.shape[1:], BF16)
    g1[0] = jnp.zeros(g1.shape[1:], BF16)
    g1[side + 1] = jnp.zeros(g1.shape[1:], BF16)
    zero = jnp.zeros((k2, LANES), BF16)
    total_one = jnp.zeros((k1, LANES), F32)
    total_two = jnp.zeros((k2, LANES), F32)
    for y in range(inner):
        at = slice(y * row_len, (y + 1) * row_len)
        grad = dot(lw[at, :], g3[...]) * s2[at, :].astype(F32)
        grad = grad.astype(BF16).reshape(inner, k2, LANES)
        g2[y + 1] = grad
        total_two = total_two + jnp.sum(grad.astype(F32), axis=0)
    reach, cols = 5, 8
    total = jnp.zeros((2 * reach * k2, 2 * cols * k1), F32)
    grads, tiles = [], []
    for b in range(side // 2):
        cut = []
        for j in range(side // 4):
            pieces = []
            for yrel in range(2):
                for p in range(3):
                    x = 2 * j - 1 + p
                    pieces.append(g2[b + yrel, x] if 0 <= x < inner else zero)
            cut.append(jnp.concatenate(pieces, axis=0))
        got = dot(t2[...], jnp.concatenate(cut, axis=1))
        for u in range(2):
            for j in range(side // 4):
                part = got[u * 64 : (u + 1) * 64, j * LANES : (j + 1) * LANES]
                slope = s1[2 * b + u + 1, 4 * j : 4 * j + 4].astype(F32)
                grad = (part.reshape(4, k1, LANES) * slope).astype(BF16)
                g1[2 * b + u + 1, 4 * j : 4 * j + 4] = grad
                total_one = total_one + jnp.sum(grad.astype(F32), axis=0)
        for j in range(-(-side // cols)):
            end = min((j + 1) * cols, side)
            tile = h1[2 * b + 1 : 2 * b + 3, j * cols : end]
            if end < (j + 1) * cols:
                rest = jnp.zeros((2, (j + 1) * cols - end, k1, LANES), BF16)
                tile = jnp.concatenate([tile, rest], axis=1)
            tiles.append(tile.reshape(2 * cols * k1, LANES))
            pieces = []
            for half in range(2):
                for p in range(reach):
                    x = 4 * j - 1 + p
                    pieces.append(g2[b + 1 - half, x] if 0 <= x < inner else zero)
            grads.append(jnp.concatenate(pieces, axis=0))
        if b % 2:
            total = total + dot_lanes(
                jnp.concatenate(grads, axis=1), jnp.concatenate(tiles, axis=1)
            )
            grads, tiles = [], []
    line = 4 * k1
    for half in range(2):
        for u in range(2):
            tap_row = jnp.zeros((k2, line), F32)
            for p in range(reach):
                at = (half * reach + p) * k2
                part = total[at : at + k2, u * 2 * line : (u + 1) * 2 * line]
                start = 2 * k1 * (p - 1)
                piece = part[:, max(start, 0) : min(start + line, 2 * line)]
                if start < 0:
                    piece = jnp.concatenate([jnp.zeros((k2, -start), F32), piece], axis=1)
                if start + line > 2 * line:
                    rest = jnp.zeros((k2, start - line), F32)
                    piece = jnp.concatenate([piece, rest], axis=1)
                tap_row = tap_row + piece
            at = (2 * half + u) * line
            c2[:, at : at + line] = tap_row
    sums[...] = jnp.zeros_like(sums)
    sums[0:1, 0:k1] = row_of(jnp.sum(total_one, axis=1, keepdims=True))
    sums[1:2, 0:k2] = row_of(jnp.sum(total_two, axis=1, keepdims=True))


def pixel_band(sec, w1t, channels):
    k1 = w1t.shape[0]
    rows = 64 * channels
    row, tap = iota((rows, 256), 0), iota((rows, 256), 1)
    moves = ((tap >> 6) == row % channels + sec * channels) & ((tap & 63) == row // channels)
    taps = dot_lanes(moves.astype(F32).astype(BF16), w1t)
    line, span = COLS * channels, 8 * channels
    blocks = {}
    for half in range(2):
        for p in range(NEAR):
            pieces = []
            for u in range(4):
                at = (4 * half + u) * span
                start = 4 * (p - 1) * channels
                cut = taps[at + max(0, -start) : at + min(span, line - start)]
                start = max(start, 0)
                pieces += [jnp.zeros((start, k1), F32)] if start else []
                pieces.append(cut)
                rest = line - start - cut.shape[0]
                pieces += [jnp.zeros((rest, k1), F32)] if rest else []
            blocks[half, p] = jnp.concatenate(pieces, axis=0)
    zero = jnp.zeros((4 * line, k1), F32)
    lines = []
    for r in range(STEP):
        cols = [
            blocks.get((r + 1 - yrel, p), zero) for yrel in range(STEP + 1) for p in range(NEAR)
        ]
        lines.append(jnp.concatenate(cols, axis=1))
    return jnp.concatenate(lines, axis=0).astype(BF16)


def first_kernel(
    section,
    frames_far,
    g1,
    w1t,
    other_far,
    after,
    c1,
    out,
    band,
    frames,
    acc,
    other,
    held,
    sems,
    draw_sems,
    *,
    draw,
):
    side, k1 = g1.shape[1], g1.shape[2]
    img, _, channels, _ = frames.shape
    steps = img // 4 // STEP
    arrives = frame_copies(section, frames_far, frames, sems)
    for g in range(steps):
        arrives(g).start()
    other_copy = pltpu.make_async_copy(
        other_far.at[0 : STEP * draw + 1], other, sems.at[steps]
    )
    other_copy.start()
    acc[...] = jnp.zeros_like(acc)
    zero = jnp.zeros((k1, LANES), BF16)

    def one_step(g, carry):
        arrives(g).wait()
        pixels, grads = [], []
        for j in range(img // COLS):
            rows = [pl.multiple_of(4 * (STEP * g + r), 4) for r in range(STEP)]
            pixels.append(
                jnp.concatenate([tile_rows(frames, row, j, COLS) for row in rows], axis=0)
            )
            pieces = []
            for yrel in range(STEP + 1):
                for p in range(NEAR):
                    x = 3 * j - 1 + p
                    pieces.append(g1[STEP * g + yrel, x] if 0 <= x < side else zero)
            grads.append(jnp.concatenate(pieces, axis=0))
        acc[...] += dot_lanes(jnp.concatenate(pixels, axis=1), jnp.concatenate(grads, axis=1))
        return carry

    lax.fori_loop(0, steps, one_step, 0)
    band[...] = pixel_band(section[0], w1t[...], out.shape[2])
    other_copy.wait()
    finish = draw_steps(section, band, g1, 0, other, 0, out, held, draw_sems, 0, draw)
    fold_first(acc, c1, channels, k1)
    finish()


def fold_first(acc, c1, channels, k1):
    line = COLS * channels
    step = 4 * channels
    taps = []
    for half in range(2):
        total = sum(
            acc[r * 4 * line : (r + 1) * 4 * line, :][
                :, (r + 1 - half) * NEAR * k1 : (r + 2 - half) * NEAR * k1
            ]
            for r in range(STEP)
        )
        for u in range(4):
            part = total[u * line : (u + 1) * line]
            cols = [part[:, p * k1 : (p + 1) * k1] for p in range(NEAR)]
            taps.append(cols[1][0:step] + cols[2][step : 2 * step] + cols[3][2 * step :])
            taps.append(cols[0][0:step] + cols[1][step : 2 * step] + cols[2][2 * step :])
    row, col = iota((256, 256), 0), iota((256, 256), 1)
    moves = ((row & 3) == (col >> 6)) & ((row >> 2) == (col & 63))
    grad = dot_rows(jnp.concatenate(taps, axis=0), moves.astype(F32), EXACT)
    for half in range(2):
        c1[half * k1 : (half + 1) * k1, :] = grad[:, half * LANES : (half + 1) * LANES].astype(BF16)


def draw_steps(section, band, mine, mine_at, other, other_at, out, held, sems, start, steps):
    side, k1 = mine.shape[1], mine.shape[2]
    img, channels = out.shape[1], out.shape[2]
    sec = section[0]
    line = COLS * channels
    flat = held.reshape(2, 2, 4 * STEP, img * channels, LANES)

    def writes(g):
        rows = slice(4 * STEP * (start + g), 4 * STEP * (start + g + 1))
        places = (sec * LANES, (1 - sec) * LANES)
        return [
            pltpu.make_async_copy(
                held.at[g % 2, k],
                out.at[rows, :, :, pl.ds(pl.multiple_of(places[k], LANES), LANES)],
                sems.at[g % 2, k],
            )
            for k in range(2)
        ]

    zero = jnp.zeros((k1, 2 * LANES), BF16)
    for g in range(steps):
        if g >= 2:
            for copy in writes(g - 2):
                copy.wait()
        for j in range(img // COLS):
            pieces = []
            for yrel in range(STEP + 1):
                for p in range(NEAR):
                    x, y = 3 * j - 1 + p, STEP * (start + g) + yrel
                    if 0 <= x < side:
                        pair = [mine[y - mine_at, x], other[y - other_at, x]]
                        pieces.append(jnp.concatenate(pair, axis=1))
                    else:
                        pieces.append(zero)
            got = dot(band[...], jnp.concatenate(pieces, axis=0))
            for k in range(4 * STEP):
                at = slice(k * line, (k + 1) * line)
                span = slice(j * line, (j + 1) * line)
                flat[g % 2, 0, k, span, :] = got[at, :LANES]
                flat[g % 2, 1, k, span, :] = got[at, LANES:]
        for copy in writes(g):
            copy.start()

    def finish():
        for g in range(max(steps - 2, 0), steps):
            for copy in writes(g):
                copy.wait()

    return finish


def pixels_kernel(section, band, mine, other_far, after, done, out, token, held, other, sems, *, start):
    steps = other.shape[0] // STEP
    fetch = pltpu.make_async_copy(
        other_far.at[STEP * start : STEP * (start + steps) + 1], other, sems.at[2, 0]
    )
    fetch.start()
    token[...] = jnp.zeros_like(token)
    fetch.wait()
    draw_steps(
        section, band, mine, 0, other, STEP * start, out, held, sems, start, steps
    )()


def two_parts(value):
    high = value.astype(BF16).astype(F32)
    return jnp.concatenate([high, value - high], axis=0).astype(BF16)


def one_part(pair):
    rows = pair.shape[0] // 2
    pair = pair.astype(F32)
    return pair[:rows] + pair[rows:]


def merge_kernel(keep, recv_one, recv_two, small, c2, sums, out_far, lines, out, sems):
    members = out.shape[0]
    size = keep.shape[0] // members
    k2 = c2.shape[0]
    lines[...] = jnp.zeros_like(lines)
    at = small.shape[0]
    lines[0:at, :] = small[...]
    for half in range(2):
        lines[at : at + k2, :] = c2[:, half * LANES : (half + 1) * LANES]
        at += k2
    lines[at : at + sums.shape[0], :] = sums[...]
    for k in range(members):
        at = slice(k * size, (k + 1) * size)
        recv, here = recv_one, k
        if k >= members // 2:
            recv, here = recv_two, k - members // 2
        got = recv[here * size : (here + 1) * size, :]
        out[k, 0:size, :] = (keep[at, :].astype(F32) + got.astype(F32)).astype(BF16)
        out[k, size:, :] = two_parts(lines[k * SHORT : (k + 1) * SHORT, :])
        pltpu.make_async_copy(out.at[k], out_far.at[k], sems.at[k]).start()
    for k in range(members):
        pltpu.make_async_copy(out.at[k], out_far.at[k], sems.at[k]).wait()


def cube_kernel(got, c1, out):
    members = got.shape[0]
    size = got.shape[1] - 2 * SHORT
    out[0:size, :] = sum(got[k, 0:size, :].astype(F32) for k in range(members)).astype(BF16)
    total = sum(one_part(got[k, size:, :]) for k in range(members))
    out[size : size + 2 * SHORT, :] = two_parts(total)
    out[size + 2 * SHORT :, :] = c1[...]


def add_kernel(a, b, after, out):
    size = a.shape[0] - 2 * SHORT - 32
    middle = slice(size, size + 2 * SHORT)
    for span in (slice(0, size), slice(size + 2 * SHORT, a.shape[0])):
        out[span, :] = (a[span, :].astype(F32) + b[span, :].astype(F32)).astype(BF16)
    out[middle, :] = two_parts(one_part(a[middle, :]) + one_part(b[middle, :]))


def relay_kernel(batch, *refs):
    parts, (one, two, out) = refs[:CUBE], refs[CUBE:]
    me = batch[0] % CUBE
    for k, part in enumerate(parts):
        out[me ^ k] = part[...]
    one[...] = out[: CUBE // 2]
    two[...] = out[CUBE // 2 :]


def piece_of(got, k):
    count = got[0].shape[0]
    return got[k // count].at[k % count]


def unpack_half(which, got, lw, bw, vw, stage, stage_b, sems):
    members = 2 * got[0].shape[0]
    size = stage.shape[0] // members
    linear_rows, width = lw.shape
    options = bw.shape[0]
    half = (linear_rows + options * width + width) // 2
    rest = linear_rows - half

    @pl.when(which == 0)
    def _():
        copies = []
        for k in range(members):
            start, end = k * size, min((k + 1) * size, half)
            stage[start:end, :] = piece_of(got, k)[0 : end - start, :].astype(F32)
            copies.append(
                pltpu.make_async_copy(stage.at[start:end], lw.at[start:end], sems.at[k])
            )
            copies[-1].start()
        for copy in copies:
            copy.wait()

    @pl.when(which == 1)
    def _():
        def rows(start, end):
            parts = []
            while start < end:
                k, at = start // size, start % size
                count = min(size - at, end - start)
                parts.append(piece_of(got, k)[at : at + count, :])
                start += count
            value = parts[0] if len(parts) == 1 else jnp.concatenate(parts, axis=0)
            return value.astype(F32)

        stage[0:rest, :] = rows(0, rest)
        copies = [pltpu.make_async_copy(stage.at[0:rest], lw.at[half:], sems.at[0])]
        copies[0].start()
        group = options // 3
        for o in range(options):
            stage_b[o] = rows(rest + o * width, rest + (o + 1) * width)
            if o % group == group - 1:
                part = slice(o + 1 - group, o + 1)
                copy = pltpu.make_async_copy(
                    stage_b.at[part], bw.at[part], sems.at[1 + o // group]
                )
                copy.start()
                copies.append(copy)
        at = rest + options * width
        stage[rest : rest + width, :] = rows(at, at + width)
        copies.append(
            pltpu.make_async_copy(stage.at[rest : rest + width], vw, sems.at[1 + options // group])
        )
        copies[-1].start()
        for copy in copies:
            copy.wait()


def own_kernel(section, one, two, lw, bw, vw, stage, stage_b, sems):
    unpack_half(section[0], (one, two), lw, bw, vw, stage, stage_b, sems)


def unpack_kernel(section, *refs):
    mine, other, refs = refs[0:2], refs[2:4], refs[4:]
    lw, bw, vw = refs[3:6]
    little = (len(refs) - 10) // 2
    far, near = refs[6 : 6 + little], refs[6 + little : 6 + 2 * little]
    loss, c1, b1, c2, b2, lb, bb, hw, hb, vb, ow, ob = near
    stage, stage_b, lines, sems = refs[-4:]
    options = bw.shape[0]
    k1, k2 = c1.shape[0], c2.shape[0]
    size = stage.shape[0] // CUBE
    grad = [jnp.zeros((k1, LANES), F32) for _ in range(2)]
    for k in range(CUBE):
        pair = slice(size, size + 2 * SHORT)
        at = slice(k * SHORT, (k + 1) * SHORT)
        views = piece_of(mine, k), piece_of(other, k)
        lines[at, :] = sum(one_part(v[pair, :]) for v in views)
        for view in views:
            for h in range(2):
                at = size + 2 * SHORT + h * k1
                grad[h] += view[at : at + k1, :].astype(F32)
    for part in range(2):
        c1[:, part * LANES : (part + 1) * LANES] = grad[part]
    bb[...] = lines[0:options, :]
    vb[...] = lines[AT_VB, :]
    ow[...] = lines[AT_OW, :]
    hw[...] = lines[AT_HW, :]
    lb[...] = lines[AT_LB, :]
    scalars = lines[AT_SCALARS, :]
    loss[...] = scalars[:, 0:1]
    hb[...] = scalars[:, 1:3]
    ob[...] = scalars[:, 3:4]
    at = TABLE
    for part in range(2):
        c2[:, part * LANES : (part + 1) * LANES] = lines[at : at + k2, :]
        at += k2
    b1[...] = lines[at : at + 1, 0:k1]
    b2[...] = lines[at + 1 : at + 2, 0:k2]
    copies = [
        pltpu.make_async_copy(a, b, sems.at[CUBE + k]) for k, (a, b) in enumerate(zip(near, far))
    ]
    for copy in copies:
        copy.start()
    unpack_half(1 - section[0], other, lw, bw, vw, stage, stage_b, sems)
    for copy in copies:
        copy.wait()


def numbers_kernel(
    options,
    depth,
    targets,
    destination,
    b1,
    b2,
    lb,
    bb,
    hw,
    vb,
    ow,
    hb,
    ob,
    out,
    table,
):
    levels, kinds = options.shape[0], targets.shape[0]
    slots = depth.shape[1]
    rows = [options[...].astype(F32), depth[...].astype(F32)]
    rows += [targets[k] for k in range(kinds)]
    rows.append(jnp.zeros((LANES - levels - 1 - kinds * levels, slots), F32))
    out[...] = jnp.transpose(jnp.concatenate(rows, axis=0))
    table[...] = jnp.zeros_like(table)
    table[0 : bb.shape[0], :] = bb[...]
    table[AT_VB, :] = vb[...]
    table[AT_OW, :] = ow[...].astype(F32)
    table[AT_HW, :] = hw[...].astype(F32)
    table[AT_LB, :] = lb[...]
    table[AT_B1, 0 : b1.shape[1]] = b1[...]
    table[AT_B2, 0 : b2.shape[1]] = b2[...]
    lane = iota((1, LANES), 1)
    scalars = jnp.zeros((1, LANES), F32)
    for k, value in ((1, hb[:, 0:1]), (2, hb[:, 1:2]), (3, ob[...])):
        scalars = jnp.where(lane == k, value, scalars)
    table[AT_SCALARS, :] = scalars
    for k in range(slots // LANES):
        part = destination[:, k * LANES : (k + 1) * LANES]
        table[AT_DEST + k : AT_DEST + k + 1, :] = part.astype(F32)


def whole(shape):
    zeros = (0,) * len(shape)
    return pl.BlockSpec(shape, lambda *_: zeros)


ANYWHERE = pl.BlockSpec(memory_space=pl.ANY)
SCALARS = pl.BlockSpec(memory_space=pltpu.SMEM)


def params():
    return pltpu.CompilerParams(vmem_limit_bytes=VMEM_BYTES)


def shape_of(*shape, dtype=F32):
    return jax.ShapeDtypeStruct(shape, dtype)


def cost(microseconds):
    return pl.CostEstimate(
        flops=int(1.1e9 * microseconds), bytes_accessed=int(3.6e6 * microseconds), transcendentals=0
    )


def stays(value):
    return pltpu.with_memory_space_constraint(value, pltpu.HBM)


def held_near(value):
    return pltpu.with_memory_space_constraint(value, pltpu.VMEM)


def encode(section, frames, w1t, w2t, lw, table):
    img = frames.shape[0]
    blocks = img // 4
    side = blocks - 1
    k1, k2, width = w1t.shape[0], w2t.shape[0], lw.shape[1]
    flat = lw.shape[0]
    vmem = pltpu.VMEM
    near = pl.BlockSpec(memory_space=vmem)
    grid_one = (blocks, side, k1, LANES)
    return pl.pallas_call(
        encode_kernel,
        in_specs=[SCALARS, ANYWHERE, near, near, ANYWHERE, near],
        out_specs=[ANYWHERE] * 3 + [near] * 3,
        out_shape=(
            pltpu.HBM(grid_one, BF16),
            pltpu.HBM(grid_one, BF16),
            pltpu.HBM((flat, LANES), BF16),
            shape_of(flat, LANES, dtype=BF16),
            shape_of(width, LANES, dtype=BF16),
            shape_of(width, LANES),
        ),
        scratch_shapes=[
            vmem((img, img, frames.shape[2], LANES), BF16),
            vmem(lw.shape, BF16),
            vmem(grid_one, BF16),
            vmem(grid_one, BF16),
            vmem((flat, LANES), BF16),
            vmem((2 * REACH * k1, 256), BF16),
            vmem((2 * k1, 64), BF16),
            vmem((6 * k2, LANES), BF16),
            vmem((k1, LANES), F32),
            vmem((k2, LANES), F32),
            vmem((side, k1, LANES), F32),
            vmem((side // 2 - 1, k2, LANES), F32),
            pltpu.SemaphoreType.DMA((4, max(blocks // STEP, 3))),
        ],
        compiler_params=params(),
        cost_estimate=cost(9),
        name="encode",
    )(section, frames, w1t, w2t, lw, table)


def plan(section, slots, enc, s3, h2, branch_w, value_w, table, per_pair, depth, half_rows):
    width = enc.shape[0]
    options = branch_w.shape[0]
    two = 2 * width
    pairs = options // 2
    outs = (
        shape_of(half_rows, LANES, dtype=BF16),
        shape_of(half_rows // 2, LANES, dtype=BF16),
        shape_of(half_rows // 2, LANES, dtype=BF16),
        shape_of(TABLE, LANES),
        shape_of(width, LANES, dtype=BF16),
    )
    vmem = pltpu.VMEM
    near = pl.BlockSpec(memory_space=vmem)
    return pl.pallas_call(
        functools.partial(plan_kernel, per_pair=per_pair, depth=depth),
        in_specs=[SCALARS, near, near, near, near, ANYWHERE, near, near],
        out_shape=outs,
        scratch_shapes=[
            vmem((2, half_rows, LANES), BF16),
            vmem((options * width, width + 16), BF16),
            vmem((width + 16, width + 16), BF16),
            vmem((width, width + 16), BF16),
            vmem((width, LANES), F32),
            vmem((16, LANES), F32),
            vmem((options * width, LANES), F32),
            vmem((depth, options * width, LANES), F32),
            vmem((depth, pairs, width, two), F32),
            vmem((depth, pairs, width + 16, two), BF16),
            vmem((depth, pairs, width, two), BF16),
            vmem((depth, options * width, LANES), BF16),
            vmem((depth, width, LANES), BF16),
            vmem((depth, 4, options, LANES), F32),
            vmem((1, LANES), F32),
            vmem((16, width), F32),
            vmem((width + 16, width + 16), F32),
            vmem(branch_w.shape, BF16),
            pltpu.SemaphoreType.DMA,
        ],
        compiler_params=params(),
        cost_estimate=cost(11),
        name="plan",
    )(section, slots, enc, s3, h2, branch_w, value_w, table)


def back(g3, lw, s2, s1, h1, w2t):
    _, side, k1 = s1.shape[:3]
    k2 = w2t.shape[0]
    inner = side // 2 - 1
    padded = (side + 2, side, k1, LANES)
    near = pl.BlockSpec(memory_space=pltpu.VMEM)
    return pl.pallas_call(
        back_kernel,
        in_specs=[near] * 6,
        out_shape=(shape_of(*padded, dtype=BF16), shape_of(k2, 256), shape_of(8, LANES)),
        scratch_shapes=[
            pltpu.VMEM((LANES, 6 * k2), BF16),
            pltpu.VMEM((inner + 2, inner, k2, LANES), BF16),
        ],
        compiler_params=params(),
        cost_estimate=cost(25),
        name="back",
    )(g3, lw, s2, s1, h1, w2t)


def first(section, frames, g1, w1t, other, after, channels, draw):
    img, _, stack, _ = frames.shape
    k1 = g1.shape[2]
    band = (STEP * 4 * COLS * channels, (STEP + 1) * NEAR * k1)
    near = pl.BlockSpec(memory_space=pltpu.VMEM)
    return pl.pallas_call(
        functools.partial(first_kernel, draw=draw),
        in_specs=[SCALARS, ANYWHERE, near, near, ANYWHERE, ANYWHERE],
        out_specs=[near, ANYWHERE, near],
        out_shape=[
            shape_of(2 * k1, LANES, dtype=BF16),
            shape_of(img, img, channels, 2 * LANES),
            shape_of(*band, dtype=BF16),
        ],
        scratch_shapes=[
            pltpu.VMEM((img, img, stack, LANES), BF16),
            pltpu.VMEM((STEP * 4 * COLS * stack, (STEP + 1) * NEAR * k1), F32),
            pltpu.VMEM((STEP * draw + 1,) + g1.shape[1:], BF16),
            pltpu.VMEM((2, 2, 4 * STEP, img, channels, LANES), F32),
            pltpu.SemaphoreType.DMA((img // 4 // STEP + 1,)),
            pltpu.SemaphoreType.DMA((2, 2)),
        ],
        compiler_params=params(),
        cost_estimate=cost(45),
        name="first",
    )(section, frames, g1, w1t, other, after)


def pixels(section, band, mine, other, after, done, start):
    img, _, channels, _ = done.shape
    steps = img // 4 // STEP - start
    near = pl.BlockSpec(memory_space=pltpu.VMEM)
    return pl.pallas_call(
        functools.partial(pixels_kernel, start=start),
        in_specs=[SCALARS, near, near, ANYWHERE, ANYWHERE, ANYWHERE],
        out_specs=[ANYWHERE, near],
        out_shape=[shape_of(*done.shape), shape_of(8, LANES)],
        scratch_shapes=[
            pltpu.VMEM((2, 2, 4 * STEP, img, channels, LANES), F32),
            pltpu.VMEM((STEP * steps + 1,) + mine.shape[1:], BF16),
            pltpu.SemaphoreType.DMA((3, 2)),
        ],
        input_output_aliases={5: 0},
        compiler_params=params(),
        cost_estimate=cost(1 + 0.9 * steps),
        name="pixels",
    )(section, band, mine, other, after, done)


def small_call(
    kernel, outs, operands, scratch=(), name=None, place=None, after=(), weight=0.3, far=False
):
    specs = [pl.BlockSpec(memory_space=pltpu.VMEM)] * len(operands)
    if place is not None:
        operands = (*place, *operands)
        specs = [pl.BlockSpec(memory_space=pltpu.SMEM)] * len(place) + specs
    return pl.pallas_call(
        kernel,
        in_specs=specs + [ANYWHERE] * len(after),
        out_specs=jax.tree.map(
            lambda _: ANYWHERE if far else pl.BlockSpec(memory_space=pltpu.VMEM), outs
        ),
        out_shape=outs,
        scratch_shapes=list(scratch),
        compiler_params=params(),
        cost_estimate=cost(weight),
        name=name,
    )(*operands, *after)


def round_up(value, step):
    return -(-value // step) * step


def swapped(value):
    return lax.ppermute(value, "section", [(0, 1), (1, 0)])


def exchanged(value, groups=None):
    return lax.all_to_all(
        value, "batch", split_axis=0, concat_axis=0, axis_index_groups=groups, tiled=True
    )


def partner(value, distance):
    count = lax.axis_size("batch")
    return lax.ppermute(value, "batch", [(b, b ^ distance) for b in range(count)])


def local(
    frames,
    destination,
    options,
    depth,
    targets,
    conv_one,
    bias_one,
    conv_two,
    bias_two,
    linear_w,
    linear_b,
    branch_w,
    branch_b,
    head_w,
    head_b,
    value_w,
    value_b,
    out_w,
    out_b,
):
    section = lax.axis_index("section").astype(jnp.int32)[None]
    peers = lax.axis_size("batch")
    frame_count = frames.shape[3]
    per_pair = frame_count // peers
    levels = options.shape[0]
    frames = stays(frames.transpose(1, 2, 0, 3))
    w1t, w2t = stays(conv_one.T), stays(conv_two.T)
    branch_w, value_w = stays(branch_w), stays(value_w)
    encoder_params = (w1t, bias_one, w2t, bias_two, linear_w, linear_b)
    planner_params = (branch_w, branch_b, head_w.T, head_b, value_w, value_b, out_w.T, out_b)
    width = linear_w.shape[1]
    big_rows = linear_w.shape[0] + (branch_w.shape[0] + 1) * width
    size = round_up(-(-big_rows // (2 * CUBE)), 16)

    tiny = (bias_one, bias_two, linear_b, branch_b, head_w.T, value_b, out_w.T)
    tiny = [stays(v if v.ndim > 1 else v[None, :]) for v in tiny]
    numbers, table = pl.pallas_call(
        numbers_kernel,
        in_specs=[pl.BlockSpec(memory_space=pltpu.VMEM)] * (6 + len(tiny)),
        out_shape=[shape_of(frame_count, LANES), shape_of(TABLE, LANES)],
        compiler_params=params(),
        cost_estimate=cost(1),
        name="numbers",
    )(
        stays(options),
        stays(depth[None, :]),
        stays(targets),
        stays(destination[None, :]),
        *tiny,
        stays(head_b[None, :]),
        out_b[None, :],
    )
    slots = exchanged(numbers.reshape(peers, per_pair, LANES)).reshape(frame_count, LANES)

    h1, s1, s2, h2, enc, s3 = encode(section, frames, w1t, w2t, stays(linear_w), table)
    keep, send_one, send_two, small, g3 = plan(
        section, slots, enc, s3, h2, branch_w, value_w, table, per_pair, levels, CUBE * size
    )
    recv = swapped(send_one), swapped(send_two)
    channels = frames.shape[2] // lax.axis_size("section")
    g1, c2, sums = back(g3, linear_w, s2, s1, h1, w2t)
    other = swapped(g1)
    g1 = held_near(g1)
    cubes = [list(range(c, c + CUBE)) for c in range(0, peers, CUBE)]
    bf16 = functools.partial(shape_of, dtype=BF16)
    pieces = small_call(
        merge_kernel,
        bf16(CUBE, size + 2 * SHORT, LANES),
        (keep, *recv, small, c2, sums),
        [
            pltpu.VMEM((CUBE * SHORT, LANES), F32),
            pltpu.VMEM((CUBE, size + 2 * SHORT, LANES), BF16),
            pltpu.SemaphoreType.DMA((CUBE,)),
        ],
        name="merge",
        far=True,
        weight=30,
    )
    got = exchanged(pieces, cubes)
    c1, frames_grad, band = first(section, frames, g1, w1t, other, pieces, channels, DRAW)
    piece = bf16(size + 2 * SHORT + c1.shape[0], LANES)
    keep = small_call(cube_kernel, piece, (got, c1), name="cube")
    distance = CUBE
    while distance < peers:
        recv = partner(keep, distance)
        if distance == CUBE:
            frames_grad, token = pixels(section, band, g1, other, keep, frames_grad, DRAW)
        distance *= 2
        keep = small_call(add_kernel, piece, (keep, recv), name="add", after=(token,))
    parts = [keep] + [partner(keep, k) for k in range(1, CUBE)]
    place = (lax.axis_index("batch").astype(jnp.int32)[None],)
    got = small_call(
        relay_kernel,
        [bf16(CUBE // 2, *piece.shape)] * 2,
        parts,
        [pltpu.VMEM((CUBE, *piece.shape), BF16)],
        name="relay",
        place=place,
    )
    got_other = [swapped(v) for v in got]
    shapes = [p.shape for p in encoder_params + planner_params]
    near = pl.BlockSpec(memory_space=pltpu.VMEM)
    flat = [shape_of(*(v if len(v) > 1 else (1,) + v)) for v in [(1, 1)] + shapes]
    large = [flat[k] for k in (5, 7, 11)]
    staged = [
        pltpu.VMEM((CUBE * size, LANES), F32),
        pltpu.VMEM(branch_w.shape, F32),
    ]
    little = [v for k, v in enumerate(flat) if k not in (5, 7, 11)]
    sems = pltpu.SemaphoreType.DMA((CUBE + len(little),))
    begun = pl.pallas_call(
        own_kernel,
        in_specs=[SCALARS, near, near],
        out_specs=[ANYWHERE] * 3,
        out_shape=large,
        scratch_shapes=[*staged, sems],
        compiler_params=params(),
        cost_estimate=cost(1),
        name="own",
    )(section, *got)
    ends = pl.pallas_call(
        unpack_kernel,
        in_specs=[SCALARS] + [near] * 4 + [ANYWHERE] * 3,
        out_specs=[ANYWHERE] * (3 + len(little)),
        out_shape=large + little,
        scratch_shapes=[pltpu.VMEM(v.shape, F32) for v in little]
        + [*staged, pltpu.VMEM((CUBE * SHORT, LANES), F32), sems],
        input_output_aliases={5: 0, 6: 1, 7: 2},
        compiler_params=params(),
        cost_estimate=cost(1.5),
        name="unpack",
    )(section, *got, *got_other, *begun)
    rest = list(ends[3:])
    for k, at in enumerate((5, 7, 11)):
        rest.insert(at, ends[k])
    rest = [v.reshape(s) for v, s in zip(rest, [()] + shapes)]
    for at in (1, 3, 9, 13):
        rest[at] = rest[at].T
    return (rest[0], frames_grad.transpose(2, 0, 1, 3), *rest[1:])


def solution(mesh):
    placed = (
        P(None, None, None, "batch"),
        P("batch"),
        P(None, "batch"),
        P("batch"),
        P(None, None, "batch"),
    ) + (P(),) * 14
    return jax.shard_map(
        local,
        mesh=mesh,
        in_specs=placed,
        out_specs=(P(), P("section", None, None, "batch")) + (P(),) * 14,
        check_vma=False,
    )
```

```python
import functools
import math

import jax
import jax.numpy as jnp
from jax import lax
from jax.experimental import pallas as pl
from jax.experimental.pallas import tpu as pltpu
from jax.sharding import PartitionSpec as P

BF16 = jnp.bfloat16
F32 = jnp.float32
EXACT = lax.Precision.HIGHEST
LANES = 128
VMEM_BYTES = 32 * 1024 * 1024
TILE = 16
REACH = 5
STEP = 3
COLS = 12
NEAR = 4
AT_VB, AT_OW, AT_HW, AT_LB, AT_SCALARS, AT_B1, AT_B2, AT_DEST = (
    slice(18, 19),
    slice(19, 20),
    slice(20, 22),
    slice(22, 23),
    slice(23, 24),
    slice(24, 25),
    slice(25, 26),
    26,
)
TABLE = 32
CUBE = 8
DRAW = 4
SHORT = 16


def dot(a, b, precision=None):
    return jnp.dot(a, b, preferred_element_type=F32, precision=precision)


def dot_rows(a, b, precision=None):
    return lax.dot_general(
        a, b, (((0,), (0,)), ((), ())), preferred_element_type=F32, precision=precision
    )


def dot_lanes(a, b, precision=None):
    return lax.dot_general(
        a, b, (((1,), (1,)), ((), ())), preferred_element_type=F32, precision=precision
    )


def iota(shape, axis):
    return lax.broadcasted_iota(jnp.int32, shape, axis)


def column(row):
    n = row.shape[1]
    wide = jnp.broadcast_to(row, (n, n))
    return jnp.sum(jnp.where(iota((n, n), 0) == iota((n, n), 1), wide, 0.0), axis=1, keepdims=True)


def row_of(col):
    n = col.shape[0]
    wide = jnp.broadcast_to(col, (n, n))
    return jnp.sum(jnp.where(iota((n, n), 0) == iota((n, n), 1), wide, 0.0), axis=0, keepdims=True)


def soft(x):
    t = jnp.tanh(0.5 * x)
    return jnp.maximum(x, 0.0) - jnp.log(0.5 + 0.5 * jnp.abs(t)), 0.5 + 0.5 * t


def silu_pair(y):
    t = jnp.tanh(y)
    m = y * t
    return y + m, (1.0 + t) + (y - m * t)


def pixel_order(w1t):
    tap, pix = iota((256, 256), 0), iota((256, 256), 1)
    moves = ((tap >> 6) == (pix & 3)) & ((tap & 63) == (pix >> 2))
    return dot(w1t, moves.astype(F32).astype(BF16))


def frame_copies(section, far, here, sems):
    lanes = pl.ds(pl.multiple_of(section[0] * LANES, LANES), LANES)
    size = 4 * STEP

    def copy(g):
        rows = pl.ds(pl.multiple_of(g * size, size), size)
        return pltpu.make_async_copy(far.at[rows, :, :, lanes], here.at[rows], sems.at[g])

    return copy


def tile_rows(frames, row, j, cols):
    img, _, channels, _ = frames.shape
    flat = frames.reshape(img, img * channels, LANES)
    size = cols * channels
    end = min((j + 1) * size, img * channels)
    part = flat[pl.ds(row, 4), j * size : end, :]
    return part.reshape(4 * (end - j * size), LANES)


def encode_kernel(
    section,
    frames_far,
    w1t,
    w2t,
    lw_far,
    table,
    h1_far,
    s1_far,
    s2_far,
    h2,
    enc,
    s3,
    frames,
    lw,
    h1,
    s1,
    s2,
    band,
    edge,
    band2,
    bias1,
    bias2,
    held,
    held2,
    sems,
):
    blocks, side = h1.shape[:2]
    steps = blocks // STEP
    tiles = frames.shape[1] // TILE
    k1, k2 = w1t.shape[0], w2t.shape[0]
    reach_rows = REACH * k1
    arrives = frame_copies(section, frames_far, frames, sems.at[0])
    for g in range(steps):
        arrives(g).start()
    last_copies = [
        pltpu.make_async_copy(lw_far, lw, sems.at[3, 0]),
        pltpu.make_async_copy(s2, s2_far, sems.at[3, 1]),
    ]
    last_copies[0].start()

    def leaves(g):
        rows = pl.ds(g * STEP, STEP)
        return [
            pltpu.make_async_copy(h1.at[rows], h1_far.at[rows], sems.at[1, g]),
            pltpu.make_async_copy(s1.at[rows], s1_far.at[rows], sems.at[2, g]),
        ]

    inner = side // 2 - 1
    row_len = inner * k2
    two = 2 * k2 * 3

    def prepare():
        taps = pixel_order(w1t[...])
        edges = []
        for half in range(2):
            lines = [taps[:, 32 * (4 * half + u) : 32 * (4 * half + u + 1)] for u in range(4)]
            for place in range(REACH):
                pieces = []
                for line in lines:
                    start = 16 * (place - 1)
                    cut = line[:, max(0, -start) : min(32, 64 - start)]
                    start = max(start, 0)
                    pieces += [jnp.zeros((k1, start), F32)] if start else []
                    pieces.append(cut)
                    rest = 64 - start - cut.shape[1]
                    pieces += [jnp.zeros((k1, rest), F32)] if rest else []
                at = half * reach_rows + place * k1
                band[at : at + k1, :] = jnp.concatenate(pieces, axis=1).astype(BF16)
            edges.append(jnp.concatenate([line[:, 16:] for line in lines], axis=1))
        edge[...] = jnp.concatenate(edges, axis=0).astype(BF16)
        tap, pix = iota((256, LANES), 0), iota((256, LANES), 1)
        for half in range(2):
            for place in range(3):
                hit = (
                    ((tap & 15) == (pix & 15))
                    & ((tap >> 6) == (pix >> 6) + 2 * half)
                    & (((tap >> 4) & 3) == ((pix >> 4) & 3) + 2 - 2 * place)
                )
                at = (half * 3 + place) * k2
                taps = dot(w2t[...], hit.astype(F32).astype(BF16))
                band2[at : at + k2, :] = taps.astype(BF16)
        bias1[...] = jnp.broadcast_to(column(table[AT_B1, 0:k1]), bias1.shape)
        bias2[...] = jnp.broadcast_to(column(table[AT_B2, 0:k2]), bias2.shape)
        held[...] = jnp.zeros_like(held)
        held2[...] = jnp.zeros_like(held2)
        h1[...] = jnp.zeros_like(h1)

    def added(sums, x, value):
        sums[x] = sums[x] + value if x in sums else value

    def second_matmul(b):
        tiles = [
            h1[pl.ds(2 * b + 1, 2), 4 * j : 4 * j + 4].reshape(LANES, LANES)
            for j in range(side // 4)
        ]
        return dot(band2[...], jnp.concatenate(tiles, axis=1))

    def second_rows(b, got):
        low, high = {}, {}
        for j in range(side // 4):
            for place in range(3):
                x = 2 * j - 1 + place
                if 0 <= x < inner:
                    span = slice(j * LANES, (j + 1) * LANES)
                    at = place * k2
                    added(low, x, got[at : at + k2, span])
                    added(high, x, got[two // 2 + at : two // 2 + at + k2, span])
        row = jnp.maximum(b - 1, 0) * row_len
        for x in range(inner):
            value, slope = soft(held2[x] + high[x] + bias2[...])
            held2[x] = low[x]
            at = pl.ds(pl.multiple_of(row + x * k2, k2), k2)
            h2[at, :] = value.astype(BF16)
            s2[at, :] = slope.astype(BF16)

    def one_step(g, carry):
        def row(r):
            return pl.multiple_of(4 * (STEP * g + r), 4)

        arrives(g).wait()
        lows, highs = [{} for _ in range(STEP)], [{} for _ in range(STEP)]

        def place_tile(r, j, got):
            for place in range(REACH):
                x = 4 * j - 1 + place
                if 0 <= x < side:
                    at = place * k1
                    added(lows[r], x, got[at : at + k1])
                    added(highs[r], x, got[reach_rows + at : reach_rows + at + k1])

        def finish(r, xs):
            for x in xs:
                value, slope = soft(held[x] + highs[r][x] + bias1[...])
                held[x] = lows[r][x]
                h1[STEP * g + r, x] = value.astype(BF16)
                s1[STEP * g + r, x] = slope.astype(BF16)

        pair = jnp.maximum(g - 1, 0)
        units = [(lambda: second_matmul(pair), lambda got: second_rows(pair, got))]

        def edges():
            parts = [tile_rows(frames, row(r), tiles, TILE) for r in range(STEP)]
            return dot(edge[...], jnp.concatenate(parts, axis=1))

        def place_edges(got):
            for r in range(STEP):
                added(lows[r], side - 1, got[:k1, r * LANES : (r + 1) * LANES])
                added(highs[r], side - 1, got[k1:, r * LANES : (r + 1) * LANES])

        units.append((edges, place_edges))

        def full(spots):
            parts = [tile_rows(frames, row(r), j, TILE) for r, j in spots]
            return dot(band[...], jnp.concatenate(parts, axis=1))

        def place_full(got, spots, ready):
            for i, (r, j) in enumerate(spots):
                place_tile(r, j, got[:, i * LANES : (i + 1) * LANES])
            if ready:
                finish(*ready)

        for r in range(STEP):
            if r % 2 == 0:
                spots = [(k, tiles - 1) for k in (r, r + 1) if k < STEP]
                units.append(
                    (
                        functools.partial(full, spots),
                        functools.partial(place_full, spots=spots, ready=None),
                    )
                )
            done = 0
            for j in range(0, tiles - 1, 2):
                spots = [(r, j), (r, j + 1)]
                ready = side if j + 2 == tiles - 1 else 4 * j + 7
                units.append(
                    (
                        functools.partial(full, spots),
                        functools.partial(place_full, spots=spots, ready=(r, range(done, ready))),
                    )
                )
                done = ready
        waiting = None
        for issue, take in units:
            got = issue()
            if waiting is not None:
                waiting[0](waiting[1])
            waiting = (take, got)
        waiting[0](waiting[1])
        for copy in leaves(g):
            copy.start()
        return carry

    prepare()
    lax.fori_loop(0, steps, one_step, 0)
    for b in range(steps - 1, side // 2):
        second_rows(b, second_matmul(b))
    for copy in last_copies[1:]:
        copy.start()
    last_copies[0].wait()
    value, slope = soft(dot_rows(lw[...], h2[...]) + column(table[AT_LB, :]))
    enc[...] = value.astype(BF16)
    s3[...] = slope
    for g in range(steps):
        for copy in leaves(g):
            copy.wait()
    for copy in last_copies[1:]:
        copy.wait()


def three_parts(row):
    high = row.astype(BF16).astype(F32)
    middle = (row - high).astype(BF16).astype(F32)
    return jnp.concatenate([high, middle, row - high - middle], axis=0)


def with_ones(value):
    return jnp.concatenate([value, ones_rows(value.shape[1])], axis=0)


def ones_rows(lanes):
    return (iota((16, lanes), 0) < 3).astype(F32).astype(BF16)


def plan_kernel(
    section,
    slots,
    enc,
    s3,
    h2,
    branch_far,
    value_w,
    table,
    keep,
    send_one,
    send_two,
    small,
    g3,
    parts,
    bwt,
    vht,
    vhw,
    ow,
    mine,
    dbr,
    dval,
    low,
    hid,
    gb,
    rounded_all,
    saved,
    losses,
    rows,
    value_all,
    branch_w,
    sem,
    *,
    per_pair,
    depth,
):
    width = enc.shape[0]
    options = branch_w.shape[0]
    pairs = options // 2
    two = 2 * width
    sec = section[0]
    branch_copy = pltpu.make_async_copy(branch_far, branch_w, sem)
    branch_copy.start()

    count = slots.shape[0]
    dest = jnp.concatenate(
        [table[AT_DEST + k : AT_DEST + k + 1, :] for k in range(count // LANES)], axis=1
    )
    own = jnp.where(sec == 0, dest[:, :LANES], dest[:, LANES:])
    others = jnp.transpose(jnp.broadcast_to(dest, (LANES, count)))
    index = iota((count, LANES), 1) + sec * LANES
    earlier = (others == own) & (iota((count, LANES), 0) < index)
    rank = jnp.sum(earlier.astype(F32), axis=0, keepdims=True)
    bucket = own * float(per_pair) + rank
    chosen = (iota((count, LANES), 0).astype(F32) == bucket).astype(F32).astype(BF16)
    numbers = slots[...]
    high = numbers.astype(BF16)
    middle = (numbers - high.astype(F32)).astype(BF16)
    rest = (numbers - high.astype(F32) - middle.astype(F32)).astype(BF16)
    mine[...] = sum(dot_rows(v, chosen) for v in (rest, middle, high))[: mine.shape[0]]

    pad = jnp.zeros((13, width), F32)
    branch_copy.wait()
    for o in range(options):
        stack = [branch_w[o].astype(F32), three_parts(table[o : o + 1, :]), pad]
        bwt[o * width : (o + 1) * width, :] = jnp.transpose(
            0.5 * jnp.concatenate(stack, axis=0)
        ).astype(BF16)
    scalars = table[AT_SCALARS, :]
    head_w = table[AT_HW, :]
    stack = [value_w[...].astype(F32), three_parts(table[AT_VB, :]), pad]
    vht[0:width, :] = jnp.transpose(0.5 * jnp.concatenate(stack, axis=0)).astype(BF16)
    vht[width:, :] = jnp.zeros((16, width + 16), BF16)
    lane = iota((1, 16), 1)
    for k in range(2):
        bias = three_parts(jnp.broadcast_to(scalars[:, 1 + k : 2 + k], (1, 16)))
        bias = sum(jnp.where(lane == j, bias[j : j + 1], 0.0) for j in range(3))
        vht[width + k : width + k + 1, 0:width] = head_w[k : k + 1].astype(BF16)
        vht[width + k : width + k + 1, width:] = bias.astype(BF16)
    vhw[:, 0:width] = (0.5 * value_w[...].astype(F32)).astype(BF16)
    vhw[:, width:] = jnp.transpose(
        0.5 * jnp.concatenate([head_w, jnp.zeros((14, width), F32)], axis=0)
    ).astype(BF16)
    ow[...] = jnp.broadcast_to(column(table[AT_OW, :]), (width, LANES))
    wide_ow = jnp.concatenate([ow[...], ow[...]], axis=1)
    half_ow = 0.5 * wide_ow

    labels = iota((options, LANES), 0).astype(F32)
    losses[...] = jnp.zeros_like(losses)
    value_all[...] = jnp.zeros_like(value_all)

    def pair_rows(t):
        return pl.ds(pl.multiple_of(t * two, two), two)

    def row_pair(ref, t):
        return jnp.concatenate([ref[pl.ds(2 * t, 1), :], ref[pl.ds(2 * t + 1, 1), :]], axis=1)

    def ahead(level, state):
        picked = labels == mine[level : level + 1, :]
        chosen = picked.astype(F32)
        saved[level, 0] = chosen
        rounded = state.astype(BF16)
        rounded_all[level] = rounded
        met = with_ones(rounded)

        def one_pair(t, following):
            act, slope = silu_pair(dot(bwt[pair_rows(t), :], met))
            dbr[level, pair_rows(t), :] = slope
            left = state + act[:width]
            right = state + act[width:]
            picks = saved.at[level, 0]
            following = jnp.where(picks[pl.ds(2 * t, 1), :] > 0.0, left, following)
            following = jnp.where(picks[pl.ds(2 * t + 1, 1), :] > 0.0, right, following)
            both = with_ones(jnp.concatenate([left.astype(BF16), right.astype(BF16)], axis=1))
            low[level, t] = both
            got = dot(vht[...], both)
            act, slope = silu_pair(got[:width])
            dval[level, t] = slope
            hidden = act.astype(BF16)
            hid[level, t] = hidden
            worth = jnp.sum(hidden.astype(F32) * wide_ow, axis=0, keepdims=True)
            for k in range(2):
                span = slice(k * LANES, (k + 1) * LANES)
                at = pl.ds(2 * t + k, 1)
                rows[0, at, :] = got[width : width + 1, span]
                rows[1, at, :] = got[width + 1 : width + 2, span]
                rows[2, at, :] = worth[:, span]
            return following

        following = lax.fori_loop(0, pairs, one_pair, state)
        reward = rows[0]
        discount = jax.nn.sigmoid(rows[1])
        value = rows[2] + scalars[:, 3:4]
        quality = reward + discount * value
        top = jnp.max(quality, axis=0, keepdims=True)
        shifted = jnp.exp(quality - top)
        total = jnp.sum(shifted, axis=0, keepdims=True)
        live = (mine[depth : depth + 1, :] > level).astype(F32)

        def target(kind):
            at = depth + 1 + kind * depth + level
            return mine[at : at + 1, :]

        reward_gap = live * (jnp.sum(chosen * reward, axis=0, keepdims=True) - target(0))
        discount_gap = live * (jnp.sum(chosen * discount, axis=0, keepdims=True) - target(1))
        plan_gap = live * (top + jnp.log(total) - target(2))
        grad_quality = plan_gap * (shifted / total)
        head_two = (chosen * discount_gap + grad_quality * value) * discount * (1.0 - discount)
        saved[level, 1] = (chosen * reward_gap + grad_quality).astype(BF16).astype(F32)
        saved[level, 2] = head_two.astype(BF16).astype(F32)
        saved[level, 3] = (grad_quality * discount).astype(BF16).astype(F32)
        losses[...] += reward_gap * reward_gap + discount_gap * discount_gap + plan_gap * plan_gap
        return following

    def behind(level, grad_next, out_sum):
        def one_pair(t, carry):
            upward, out_sum = carry
            worth = row_pair(saved.at[level, 3], t)
            grad_pre = (worth * half_ow * dval[level, t]).astype(BF16)
            heads = jnp.where(line == 0, row_pair(saved.at[level, 1], t), 0.0)
            heads = jnp.where(line == 1, row_pair(saved.at[level, 2], t), heads)
            heads = jnp.where(line == 2, worth, heads).astype(BF16)
            out_sum = out_sum + dot_lanes(heads, hid[level, t])
            stacked = jnp.concatenate([grad_pre, heads], axis=0)
            value_all[...] += dot_lanes(stacked, low[level, t])
            moved = dot(vhw[...], stacked)
            left, right = moved[:, :LANES], moved[:, LANES:]
            if grad_next is not None:
                picks = saved.at[level, 0]
                left = left + jnp.where(picks[pl.ds(2 * t, 1), :] > 0.0, grad_next, 0.0)
                right = right + jnp.where(picks[pl.ds(2 * t + 1, 1), :] > 0.0, grad_next, 0.0)
            grad_branch = jnp.concatenate([left, right], axis=0) * dbr[level, pair_rows(t), :]
            grad_branch = grad_branch.astype(BF16)
            gb[level, pair_rows(t), :] = grad_branch
            weights = jnp.concatenate([branch_w[2 * t], branch_w[2 * t + 1]], axis=1)
            return upward + (left + right + 0.5 * dot(weights, grad_branch)), out_sum

        return lax.fori_loop(0, pairs, one_pair, (jnp.zeros((width, LANES), F32), out_sum))

    state = enc[...].astype(F32)
    for level in range(depth):
        state = ahead(level, state)
    line = iota((16, two), 0)
    grad_next, out_sum = None, jnp.zeros((16, width), F32)
    for level in reversed(range(depth)):
        grad_next, out_sum = behind(level, grad_next, out_sum)
    value_sum = value_all[...]

    linear_rows = h2.shape[0]
    half = (linear_rows + options * width + width) // 2
    rest = linear_rows - half
    rounded = with_ones(jnp.concatenate([rounded_all[k] for k in range(depth)], axis=1))
    small[...] = jnp.zeros_like(small)
    if half < keep.shape[0]:
        for k in range(2):
            parts[k, half:, :] = jnp.zeros((keep.shape[0] - half, LANES), BF16)
    for t in range(pairs):
        at = slice(t * two, (t + 1) * two)
        grads = jnp.concatenate([gb[level, at, :] for level in range(depth)], axis=1)
        got = dot_lanes(rounded, grads)
        for k in range(2):
            o = 2 * t + k
            span = slice(k * width, (k + 1) * width)
            here = slice(rest + o * width, rest + (o + 1) * width)
            parts[1 - sec, here, :] = got[:width, span].astype(BF16)
            small[o : o + 1, :] = got[width : width + 1, span]
    after = rest + options * width
    parts[1 - sec, after : after + width, :] = jnp.transpose(value_sum[:width, :width]).astype(BF16)

    grad_three = ((2.0 * grad_next).astype(BF16).astype(F32) * s3[...]).astype(BF16)
    g3[...] = grad_three
    chunk = linear_rows // 9
    for i in range(8):
        at = slice(i * chunk, (i + 1) * chunk)
        parts[sec, at, :] = dot_lanes(h2[at, :], grad_three).astype(BF16)
    last = dot_lanes(h2[8 * chunk :, :], grad_three).astype(BF16)
    parts[sec, 8 * chunk : half, :] = last[: half - 8 * chunk]
    parts[1 - sec, 0:rest, :] = last[half - 8 * chunk :]
    keep[...] = parts[0]
    send_one[...] = parts[1, : send_one.shape[0]]
    send_two[...] = parts[1, send_one.shape[0] :]

    small[AT_VB, :] = row_of(value_sum[:width, width : width + 1])
    small[AT_OW, :] = out_sum[2:3]
    small[AT_HW, :] = value_sum[width : width + 2, :width]
    small[AT_LB, :] = row_of(jnp.sum(grad_three.astype(F32), axis=1, keepdims=True))
    loss = 0.5 * jnp.sum(losses[...], axis=1, keepdims=True)
    ends = [loss] + [value_sum[width + k : width + k + 1, width : width + 1] for k in range(3)]
    lane = iota((1, LANES), 1)
    line = jnp.zeros((1, LANES), F32)
    for k, end in enumerate(ends):
        line = jnp.where(lane == k, end, line)
    small[AT_SCALARS, :] = line


def back_kernel(g3, lw, s2, s1, h1, w2t, g1, c2, sums, t2, g2):
    side, k1 = s1.shape[1], s1.shape[2]
    k2 = w2t.shape[0]
    inner = side // 2 - 1
    row_len = inner * k2
    tap, pix = iota((LANES, 256), 1), iota((LANES, 256), 0)
    for yrel in range(2):
        for p in range(3):
            hit = (
                ((tap & 15) == (pix & 15))
                & ((tap >> 6) == (pix >> 6) + 2 * (1 - yrel))
                & (((tap >> 4) & 3) == ((pix >> 4) & 3) + 2 - 2 * p)
            )
            at = (yrel * 3 + p) * k2
            t2[:, at : at + k2] = dot_lanes(hit.astype(F32).astype(BF16), w2t[...]).astype(BF16)
    g2[0] = jnp.zeros(g2.shape[1:], BF16)
    g2[inner + 1] = jnp.zeros(g2.shape[1:], BF16)
    g1[0] = jnp.zeros(g1.shape[1:], BF16)
    g1[side + 1] = jnp.zeros(g1.shape[1:], BF16)
    zero = jnp.zeros((k2, LANES), BF16)
    total_one = jnp.zeros((k1, LANES), F32)
    total_two = jnp.zeros((k2, LANES), F32)
    for y in range(inner):
        at = slice(y * row_len, (y + 1) * row_len)
        grad = dot(lw[at, :], g3[...]) * s2[at, :].astype(F32)
        grad = grad.astype(BF16).reshape(inner, k2, LANES)
        g2[y + 1] = grad
        total_two = total_two + jnp.sum(grad.astype(F32), axis=0)
    reach, cols = 5, 8
    total = jnp.zeros((2 * reach * k2, 2 * cols * k1), F32)
    grads, tiles = [], []
    for b in range(side // 2):
        cut = []
        for j in range(side // 4):
            pieces = []
            for yrel in range(2):
                for p in range(3):
                    x = 2 * j - 1 + p
                    pieces.append(g2[b + yrel, x] if 0 <= x < inner else zero)
            cut.append(jnp.concatenate(pieces, axis=0))
        got = dot(t2[...], jnp.concatenate(cut, axis=1))
        for u in range(2):
            for j in range(side // 4):
                part = got[u * 64 : (u + 1) * 64, j * LANES : (j + 1) * LANES]
                slope = s1[2 * b + u + 1, 4 * j : 4 * j + 4].astype(F32)
                grad = (part.reshape(4, k1, LANES) * slope).astype(BF16)
                g1[2 * b + u + 1, 4 * j : 4 * j + 4] = grad
                total_one = total_one + jnp.sum(grad.astype(F32), axis=0)
        for j in range(-(-side // cols)):
            end = min((j + 1) * cols, side)
            tile = h1[2 * b + 1 : 2 * b + 3, j * cols : end]
            if end < (j + 1) * cols:
                rest = jnp.zeros((2, (j + 1) * cols - end, k1, LANES), BF16)
                tile = jnp.concatenate([tile, rest], axis=1)
            tiles.append(tile.reshape(2 * cols * k1, LANES))
            pieces = []
            for half in range(2):
                for p in range(reach):
                    x = 4 * j - 1 + p
                    pieces.append(g2[b + 1 - half, x] if 0 <= x < inner else zero)
            grads.append(jnp.concatenate(pieces, axis=0))
        if b % 2:
            total = total + dot_lanes(
                jnp.concatenate(grads, axis=1), jnp.concatenate(tiles, axis=1)
            )
            grads, tiles = [], []
    line = 4 * k1
    for half in range(2):
        for u in range(2):
            tap_row = jnp.zeros((k2, line), F32)
            for p in range(reach):
                at = (half * reach + p) * k2
                part = total[at : at + k2, u * 2 * line : (u + 1) * 2 * line]
                start = 2 * k1 * (p - 1)
                piece = part[:, max(start, 0) : min(start + line, 2 * line)]
                if start < 0:
                    piece = jnp.concatenate([jnp.zeros((k2, -start), F32), piece], axis=1)
                if start + line > 2 * line:
                    rest = jnp.zeros((k2, start - line), F32)
                    piece = jnp.concatenate([piece, rest], axis=1)
                tap_row = tap_row + piece
            at = (2 * half + u) * line
            c2[:, at : at + line] = tap_row
    sums[...] = jnp.zeros_like(sums)
    sums[0:1, 0:k1] = row_of(jnp.sum(total_one, axis=1, keepdims=True))
    sums[1:2, 0:k2] = row_of(jnp.sum(total_two, axis=1, keepdims=True))


def pixel_band(sec, w1t, channels):
    k1 = w1t.shape[0]
    rows = 64 * channels
    row, tap = iota((rows, 256), 0), iota((rows, 256), 1)
    moves = ((tap >> 6) == row % channels + sec * channels) & ((tap & 63) == row // channels)
    taps = dot_lanes(moves.astype(F32).astype(BF16), w1t)
    line, span = COLS * channels, 8 * channels
    blocks = {}
    for half in range(2):
        for p in range(NEAR):
            pieces = []
            for u in range(4):
                at = (4 * half + u) * span
                start = 4 * (p - 1) * channels
                cut = taps[at + max(0, -start) : at + min(span, line - start)]
                start = max(start, 0)
                pieces += [jnp.zeros((start, k1), F32)] if start else []
                pieces.append(cut)
                rest = line - start - cut.shape[0]
                pieces += [jnp.zeros((rest, k1), F32)] if rest else []
            blocks[half, p] = jnp.concatenate(pieces, axis=0)
    zero = jnp.zeros((4 * line, k1), F32)
    lines = []
    for r in range(STEP):
        cols = [
            blocks.get((r + 1 - yrel, p), zero) for yrel in range(STEP + 1) for p in range(NEAR)
        ]
        lines.append(jnp.concatenate(cols, axis=1))
    return jnp.concatenate(lines, axis=0).astype(BF16)


def first_kernel(
    section,
    frames_far,
    g1,
    w1t,
    other_far,
    after,
    c1,
    out,
    band,
    frames,
    acc,
    other,
    held,
    sems,
    draw_sems,
    *,
    draw,
):
    side, k1 = g1.shape[1], g1.shape[2]
    img, _, channels, _ = frames.shape
    steps = img // 4 // STEP
    arrives = frame_copies(section, frames_far, frames, sems)
    for g in range(steps):
        arrives(g).start()
    other_copy = pltpu.make_async_copy(
        other_far.at[0 : STEP * draw + 1], other, sems.at[steps]
    )
    other_copy.start()
    acc[...] = jnp.zeros_like(acc)
    zero = jnp.zeros((k1, LANES), BF16)

    def one_step(g, carry):
        arrives(g).wait()
        pixels, grads = [], []
        for j in range(img // COLS):
            rows = [pl.multiple_of(4 * (STEP * g + r), 4) for r in range(STEP)]
            pixels.append(
                jnp.concatenate([tile_rows(frames, row, j, COLS) for row in rows], axis=0)
            )
            pieces = []
            for yrel in range(STEP + 1):
                for p in range(NEAR):
                    x = 3 * j - 1 + p
                    pieces.append(g1[STEP * g + yrel, x] if 0 <= x < side else zero)
            grads.append(jnp.concatenate(pieces, axis=0))
        acc[...] += dot_lanes(jnp.concatenate(pixels, axis=1), jnp.concatenate(grads, axis=1))
        return carry

    lax.fori_loop(0, steps, one_step, 0)
    band[...] = pixel_band(section[0], w1t[...], out.shape[2])
    other_copy.wait()
    finish = draw_steps(section, band, g1, 0, other, 0, out, held, draw_sems, 0, draw)
    fold_first(acc, c1, channels, k1)
    finish()


def fold_first(acc, c1, channels, k1):
    line = COLS * channels
    step = 4 * channels
    taps = []
    for half in range(2):
        total = sum(
            acc[r * 4 * line : (r + 1) * 4 * line, :][
                :, (r + 1 - half) * NEAR * k1 : (r + 2 - half) * NEAR * k1
            ]
            for r in range(STEP)
        )
        for u in range(4):
            part = total[u * line : (u + 1) * line]
            cols = [part[:, p * k1 : (p + 1) * k1] for p in range(NEAR)]
            taps.append(cols[1][0:step] + cols[2][step : 2 * step] + cols[3][2 * step :])
            taps.append(cols[0][0:step] + cols[1][step : 2 * step] + cols[2][2 * step :])
    row, col = iota((256, 256), 0), iota((256, 256), 1)
    moves = ((row & 3) == (col >> 6)) & ((row >> 2) == (col & 63))
    grad = dot_rows(jnp.concatenate(taps, axis=0), moves.astype(F32), EXACT)
    for half in range(2):
        c1[half * k1 : (half + 1) * k1, :] = grad[:, half * LANES : (half + 1) * LANES].astype(BF16)


def draw_steps(section, band, mine, mine_at, other, other_at, out, held, sems, start, steps):
    side, k1 = mine.shape[1], mine.shape[2]
    img, channels = out.shape[1], out.shape[2]
    sec = section[0]
    line = COLS * channels
    flat = held.reshape(2, 2, 4 * STEP, img * channels, LANES)

    def writes(g):
        rows = slice(4 * STEP * (start + g), 4 * STEP * (start + g + 1))
        places = (sec * LANES, (1 - sec) * LANES)
        return [
            pltpu.make_async_copy(
                held.at[g % 2, k],
                out.at[rows, :, :, pl.ds(pl.multiple_of(places[k], LANES), LANES)],
                sems.at[g % 2, k],
            )
            for k in range(2)
        ]

    zero = jnp.zeros((k1, 2 * LANES), BF16)
    for g in range(steps):
        if g >= 2:
            for copy in writes(g - 2):
                copy.wait()
        for j in range(img // COLS):
            pieces = []
            for yrel in range(STEP + 1):
                for p in range(NEAR):
                    x, y = 3 * j - 1 + p, STEP * (start + g) + yrel
                    if 0 <= x < side:
                        pair = [mine[y - mine_at, x], other[y - other_at, x]]
                        pieces.append(jnp.concatenate(pair, axis=1))
                    else:
                        pieces.append(zero)
            got = dot(band[...], jnp.concatenate(pieces, axis=0))
            for k in range(4 * STEP):
                at = slice(k * line, (k + 1) * line)
                span = slice(j * line, (j + 1) * line)
                flat[g % 2, 0, k, span, :] = got[at, :LANES]
                flat[g % 2, 1, k, span, :] = got[at, LANES:]
        for copy in writes(g):
            copy.start()

    def finish():
        for g in range(max(steps - 2, 0), steps):
            for copy in writes(g):
                copy.wait()

    return finish


def pixels_kernel(section, band, mine, other_far, after, done, out, token, held, other, sems, *, start):
    steps = other.shape[0] // STEP
    fetch = pltpu.make_async_copy(
        other_far.at[STEP * start : STEP * (start + steps) + 1], other, sems.at[2, 0]
    )
    fetch.start()
    token[...] = jnp.zeros_like(token)
    fetch.wait()
    draw_steps(
        section, band, mine, 0, other, STEP * start, out, held, sems, start, steps
    )()


def two_parts(value):
    high = value.astype(BF16).astype(F32)
    return jnp.concatenate([high, value - high], axis=0).astype(BF16)


def one_part(pair):
    rows = pair.shape[0] // 2
    pair = pair.astype(F32)
    return pair[:rows] + pair[rows:]


def merge_kernel(keep, recv_one, recv_two, small, c2, sums, out_far, lines, out, sems):
    members = out.shape[0]
    size = keep.shape[0] // members
    k2 = c2.shape[0]
    lines[...] = jnp.zeros_like(lines)
    at = small.shape[0]
    lines[0:at, :] = small[...]
    for half in range(2):
        lines[at : at + k2, :] = c2[:, half * LANES : (half + 1) * LANES]
        at += k2
    lines[at : at + sums.shape[0], :] = sums[...]
    for k in range(members):
        at = slice(k * size, (k + 1) * size)
        recv, here = recv_one, k
        if k >= members // 2:
            recv, here = recv_two, k - members // 2
        got = recv[here * size : (here + 1) * size, :]
        out[k, 0:size, :] = (keep[at, :].astype(F32) + got.astype(F32)).astype(BF16)
        out[k, size:, :] = two_parts(lines[k * SHORT : (k + 1) * SHORT, :])
        pltpu.make_async_copy(out.at[k], out_far.at[k], sems.at[k]).start()
    for k in range(members):
        pltpu.make_async_copy(out.at[k], out_far.at[k], sems.at[k]).wait()


def cube_kernel(got, c1, out):
    members = got.shape[0]
    size = got.shape[1] - 2 * SHORT
    out[0:size, :] = sum(got[k, 0:size, :].astype(F32) for k in range(members)).astype(BF16)
    total = sum(one_part(got[k, size:, :]) for k in range(members))
    out[size : size + 2 * SHORT, :] = two_parts(total)
    out[size + 2 * SHORT :, :] = c1[...]


def add_kernel(a, b, after, out):
    size = a.shape[0] - 2 * SHORT - 32
    middle = slice(size, size + 2 * SHORT)
    for span in (slice(0, size), slice(size + 2 * SHORT, a.shape[0])):
        out[span, :] = (a[span, :].astype(F32) + b[span, :].astype(F32)).astype(BF16)
    out[middle, :] = two_parts(one_part(a[middle, :]) + one_part(b[middle, :]))


def relay_kernel(batch, *refs):
    parts, (one, two, out) = refs[:CUBE], refs[CUBE:]
    me = batch[0] % CUBE
    for k, part in enumerate(parts):
        out[me ^ k] = part[...]
    one[...] = out[: CUBE // 2]
    two[...] = out[CUBE // 2 :]


def piece_of(got, k):
    count = got[0].shape[0]
    return got[k // count].at[k % count]


def unpack_half(which, got, lw, bw, vw, stage, stage_b, sems):
    members = 2 * got[0].shape[0]
    size = stage.shape[0] // members
    linear_rows, width = lw.shape
    options = bw.shape[0]
    half = (linear_rows + options * width + width) // 2
    rest = linear_rows - half

    @pl.when(which == 0)
    def _():
        copies = []
        for k in range(members):
            start, end = k * size, min((k + 1) * size, half)
            stage[start:end, :] = piece_of(got, k)[0 : end - start, :].astype(F32)
            copies.append(
                pltpu.make_async_copy(stage.at[start:end], lw.at[start:end], sems.at[k])
            )
            copies[-1].start()
        for copy in copies:
            copy.wait()

    @pl.when(which == 1)
    def _():
        def rows(start, end):
            parts = []
            while start < end:
                k, at = start // size, start % size
                count = min(size - at, end - start)
                parts.append(piece_of(got, k)[at : at + count, :])
                start += count
            value = parts[0] if len(parts) == 1 else jnp.concatenate(parts, axis=0)
            return value.astype(F32)

        stage[0:rest, :] = rows(0, rest)
        copies = [pltpu.make_async_copy(stage.at[0:rest], lw.at[half:], sems.at[0])]
        copies[0].start()
        group = options // 3
        for o in range(options):
            stage_b[o] = rows(rest + o * width, rest + (o + 1) * width)
            if o % group == group - 1:
                part = slice(o + 1 - group, o + 1)
                copy = pltpu.make_async_copy(
                    stage_b.at[part], bw.at[part], sems.at[1 + o // group]
                )
                copy.start()
                copies.append(copy)
        at = rest + options * width
        stage[rest : rest + width, :] = rows(at, at + width)
        copies.append(
            pltpu.make_async_copy(stage.at[rest : rest + width], vw, sems.at[1 + options // group])
        )
        copies[-1].start()
        for copy in copies:
            copy.wait()


def own_kernel(section, one, two, lw, bw, vw, stage, stage_b, sems):
    unpack_half(section[0], (one, two), lw, bw, vw, stage, stage_b, sems)


def unpack_kernel(section, *refs):
    mine, other, refs = refs[0:2], refs[2:4], refs[4:]
    lw, bw, vw = refs[3:6]
    little = (len(refs) - 10) // 2
    far, near = refs[6 : 6 + little], refs[6 + little : 6 + 2 * little]
    loss, c1, b1, c2, b2, lb, bb, hw, hb, vb, ow, ob = near
    stage, stage_b, lines, sems = refs[-4:]
    options = bw.shape[0]
    k1, k2 = c1.shape[0], c2.shape[0]
    size = stage.shape[0] // CUBE
    grad = [jnp.zeros((k1, LANES), F32) for _ in range(2)]
    for k in range(CUBE):
        pair = slice(size, size + 2 * SHORT)
        at = slice(k * SHORT, (k + 1) * SHORT)
        views = piece_of(mine, k), piece_of(other, k)
        lines[at, :] = sum(one_part(v[pair, :]) for v in views)
        for view in views:
            for h in range(2):
                at = size + 2 * SHORT + h * k1
                grad[h] += view[at : at + k1, :].astype(F32)
    for part in range(2):
        c1[:, part * LANES : (part + 1) * LANES] = grad[part]
    bb[...] = lines[0:options, :]
    vb[...] = lines[AT_VB, :]
    ow[...] = lines[AT_OW, :]
    hw[...] = lines[AT_HW, :]
    lb[...] = lines[AT_LB, :]
    scalars = lines[AT_SCALARS, :]
    loss[...] = scalars[:, 0:1]
    hb[...] = scalars[:, 1:3]
    ob[...] = scalars[:, 3:4]
    at = TABLE
    for part in range(2):
        c2[:, part * LANES : (part + 1) * LANES] = lines[at : at + k2, :]
        at += k2
    b1[...] = lines[at : at + 1, 0:k1]
    b2[...] = lines[at + 1 : at + 2, 0:k2]
    copies = [
        pltpu.make_async_copy(a, b, sems.at[CUBE + k]) for k, (a, b) in enumerate(zip(near, far))
    ]
    for copy in copies:
        copy.start()
    unpack_half(1 - section[0], other, lw, bw, vw, stage, stage_b, sems)
    for copy in copies:
        copy.wait()


def numbers_kernel(
    options,
    depth,
    targets,
    destination,
    b1,
    b2,
    lb,
    bb,
    hw,
    vb,
    ow,
    hb,
    ob,
    out,
    table,
):
    levels, kinds = options.shape[0], targets.shape[0]
    slots = depth.shape[1]
    rows = [options[...].astype(F32), depth[...].astype(F32)]
    rows += [targets[k] for k in range(kinds)]
    rows.append(jnp.zeros((LANES - levels - 1 - kinds * levels, slots), F32))
    out[...] = jnp.transpose(jnp.concatenate(rows, axis=0))
    table[...] = jnp.zeros_like(table)
    table[0 : bb.shape[0], :] = bb[...]
    table[AT_VB, :] = vb[...]
    table[AT_OW, :] = ow[...].astype(F32)
    table[AT_HW, :] = hw[...].astype(F32)
    table[AT_LB, :] = lb[...]
    table[AT_B1, 0 : b1.shape[1]] = b1[...]
    table[AT_B2, 0 : b2.shape[1]] = b2[...]
    lane = iota((1, LANES), 1)
    scalars = jnp.zeros((1, LANES), F32)
    for k, value in ((1, hb[:, 0:1]), (2, hb[:, 1:2]), (3, ob[...])):
        scalars = jnp.where(lane == k, value, scalars)
    table[AT_SCALARS, :] = scalars
    for k in range(slots // LANES):
        part = destination[:, k * LANES : (k + 1) * LANES]
        table[AT_DEST + k : AT_DEST + k + 1, :] = part.astype(F32)


def whole(shape):
    zeros = (0,) * len(shape)
    return pl.BlockSpec(shape, lambda *_: zeros)


ANYWHERE = pl.BlockSpec(memory_space=pl.ANY)
SCALARS = pl.BlockSpec(memory_space=pltpu.SMEM)


def params():
    return pltpu.CompilerParams(vmem_limit_bytes=VMEM_BYTES)


def shape_of(*shape, dtype=F32):
    return jax.ShapeDtypeStruct(shape, dtype)


def cost(microseconds):
    return pl.CostEstimate(
        flops=int(1.1e9 * microseconds), bytes_accessed=int(3.6e6 * microseconds), transcendentals=0
    )


def stays(value):
    return pltpu.with_memory_space_constraint(value, pltpu.HBM)


def held_near(value):
    return pltpu.with_memory_space_constraint(value, pltpu.VMEM)


def encode(section, frames, w1t, w2t, lw, table):
    img = frames.shape[0]
    blocks = img // 4
    side = blocks - 1
    k1, k2, width = w1t.shape[0], w2t.shape[0], lw.shape[1]
    flat = lw.shape[0]
    vmem = pltpu.VMEM
    near = pl.BlockSpec(memory_space=vmem)
    grid_one = (blocks, side, k1, LANES)
    return pl.pallas_call(
        encode_kernel,
        in_specs=[SCALARS, ANYWHERE, near, near, ANYWHERE, near],
        out_specs=[ANYWHERE] * 3 + [near] * 3,
        out_shape=(
            pltpu.HBM(grid_one, BF16),
            pltpu.HBM(grid_one, BF16),
            pltpu.HBM((flat, LANES), BF16),
            shape_of(flat, LANES, dtype=BF16),
            shape_of(width, LANES, dtype=BF16),
            shape_of(width, LANES),
        ),
        scratch_shapes=[
            vmem((img, img, frames.shape[2], LANES), BF16),
            vmem(lw.shape, BF16),
            vmem(grid_one, BF16),
            vmem(grid_one, BF16),
            vmem((flat, LANES), BF16),
            vmem((2 * REACH * k1, 256), BF16),
            vmem((2 * k1, 64), BF16),
            vmem((6 * k2, LANES), BF16),
            vmem((k1, LANES), F32),
            vmem((k2, LANES), F32),
            vmem((side, k1, LANES), F32),
            vmem((side // 2 - 1, k2, LANES), F32),
            pltpu.SemaphoreType.DMA((4, max(blocks // STEP, 3))),
        ],
        compiler_params=params(),
        cost_estimate=cost(9),
        name="encode",
    )(section, frames, w1t, w2t, lw, table)


def plan(section, slots, enc, s3, h2, branch_w, value_w, table, per_pair, depth, half_rows):
    width = enc.shape[0]
    options = branch_w.shape[0]
    two = 2 * width
    pairs = options // 2
    outs = (
        shape_of(half_rows, LANES, dtype=BF16),
        shape_of(half_rows // 2, LANES, dtype=BF16),
        shape_of(half_rows // 2, LANES, dtype=BF16),
        shape_of(TABLE, LANES),
        shape_of(width, LANES, dtype=BF16),
    )
    vmem = pltpu.VMEM
    near = pl.BlockSpec(memory_space=vmem)
    return pl.pallas_call(
        functools.partial(plan_kernel, per_pair=per_pair, depth=depth),
        in_specs=[SCALARS, near, near, near, near, ANYWHERE, near, near],
        out_shape=outs,
        scratch_shapes=[
            vmem((2, half_rows, LANES), BF16),
            vmem((options * width, width + 16), BF16),
            vmem((width + 16, width + 16), BF16),
            vmem((width, width + 16), BF16),
            vmem((width, LANES), F32),
            vmem((16, LANES), F32),
            vmem((depth, options * width, LANES), F32),
            vmem((depth, pairs, width, two), F32),
            vmem((depth, pairs, width + 16, two), BF16),
            vmem((depth, pairs, width, two), BF16),
            vmem((depth, options * width, LANES), BF16),
            vmem((depth, width, LANES), BF16),
            vmem((depth, 4, options, LANES), F32),
            vmem((1, LANES), F32),
            vmem((3, options, LANES), F32),
            vmem((width + 16, width + 16), F32),
            vmem(branch_w.shape, BF16),
            pltpu.SemaphoreType.DMA,
        ],
        compiler_params=params(),
        cost_estimate=cost(11),
        name="plan",
    )(section, slots, enc, s3, h2, branch_w, value_w, table)


def back(g3, lw, s2, s1, h1, w2t):
    _, side, k1 = s1.shape[:3]
    k2 = w2t.shape[0]
    inner = side // 2 - 1
    padded = (side + 2, side, k1, LANES)
    near = pl.BlockSpec(memory_space=pltpu.VMEM)
    return pl.pallas_call(
        back_kernel,
        in_specs=[near] * 6,
        out_shape=(shape_of(*padded, dtype=BF16), shape_of(k2, 256), shape_of(8, LANES)),
        scratch_shapes=[
            pltpu.VMEM((LANES, 6 * k2), BF16),
            pltpu.VMEM((inner + 2, inner, k2, LANES), BF16),
        ],
        compiler_params=params(),
        cost_estimate=cost(25),
        name="back",
    )(g3, lw, s2, s1, h1, w2t)


def first(section, frames, g1, w1t, other, after, channels, draw):
    img, _, stack, _ = frames.shape
    k1 = g1.shape[2]
    band = (STEP * 4 * COLS * channels, (STEP + 1) * NEAR * k1)
    near = pl.BlockSpec(memory_space=pltpu.VMEM)
    return pl.pallas_call(
        functools.partial(first_kernel, draw=draw),
        in_specs=[SCALARS, ANYWHERE, near, near, ANYWHERE, ANYWHERE],
        out_specs=[near, ANYWHERE, near],
        out_shape=[
            shape_of(2 * k1, LANES, dtype=BF16),
            shape_of(img, img, channels, 2 * LANES),
            shape_of(*band, dtype=BF16),
        ],
        scratch_shapes=[
            pltpu.VMEM((img, img, stack, LANES), BF16),
            pltpu.VMEM((STEP * 4 * COLS * stack, (STEP + 1) * NEAR * k1), F32),
            pltpu.VMEM((STEP * draw + 1,) + g1.shape[1:], BF16),
            pltpu.VMEM((2, 2, 4 * STEP, img, channels, LANES), F32),
            pltpu.SemaphoreType.DMA((img // 4 // STEP + 1,)),
            pltpu.SemaphoreType.DMA((2, 2)),
        ],
        compiler_params=params(),
        cost_estimate=cost(45),
        name="first",
    )(section, frames, g1, w1t, other, after)


def pixels(section, band, mine, other, after, done, start):
    img, _, channels, _ = done.shape
    steps = img // 4 // STEP - start
    near = pl.BlockSpec(memory_space=pltpu.VMEM)
    return pl.pallas_call(
        functools.partial(pixels_kernel, start=start),
        in_specs=[SCALARS, near, near, ANYWHERE, ANYWHERE, ANYWHERE],
        out_specs=[ANYWHERE, near],
        out_shape=[shape_of(*done.shape), shape_of(8, LANES)],
        scratch_shapes=[
            pltpu.VMEM((2, 2, 4 * STEP, img, channels, LANES), F32),
            pltpu.VMEM((STEP * steps + 1,) + mine.shape[1:], BF16),
            pltpu.SemaphoreType.DMA((3, 2)),
        ],
        input_output_aliases={5: 0},
        compiler_params=params(),
        cost_estimate=cost(1 + 0.9 * steps),
        name="pixels",
    )(section, band, mine, other, after, done)


def small_call(
    kernel, outs, operands, scratch=(), name=None, place=None, after=(), weight=0.3, far=False
):
    specs = [pl.BlockSpec(memory_space=pltpu.VMEM)] * len(operands)
    if place is not None:
        operands = (*place, *operands)
        specs = [pl.BlockSpec(memory_space=pltpu.SMEM)] * len(place) + specs
    return pl.pallas_call(
        kernel,
        in_specs=specs + [ANYWHERE] * len(after),
        out_specs=jax.tree.map(
            lambda _: ANYWHERE if far else pl.BlockSpec(memory_space=pltpu.VMEM), outs
        ),
        out_shape=outs,
        scratch_shapes=list(scratch),
        compiler_params=params(),
        cost_estimate=cost(weight),
        name=name,
    )(*operands, *after)


def round_up(value, step):
    return -(-value // step) * step


def swapped(value):
    return lax.ppermute(value, "section", [(0, 1), (1, 0)])


def exchanged(value, groups=None):
    return lax.all_to_all(
        value, "batch", split_axis=0, concat_axis=0, axis_index_groups=groups, tiled=True
    )


def partner(value, distance):
    count = lax.axis_size("batch")
    return lax.ppermute(value, "batch", [(b, b ^ distance) for b in range(count)])


def local(
    frames,
    destination,
    options,
    depth,
    targets,
    conv_one,
    bias_one,
    conv_two,
    bias_two,
    linear_w,
    linear_b,
    branch_w,
    branch_b,
    head_w,
    head_b,
    value_w,
    value_b,
    out_w,
    out_b,
):
    section = lax.axis_index("section").astype(jnp.int32)[None]
    peers = lax.axis_size("batch")
    frame_count = frames.shape[3]
    per_pair = frame_count // peers
    levels = options.shape[0]
    frames = stays(frames.transpose(1, 2, 0, 3))
    w1t, w2t = stays(conv_one.T), stays(conv_two.T)
    branch_w, value_w = stays(branch_w), stays(value_w)
    encoder_params = (w1t, bias_one, w2t, bias_two, linear_w, linear_b)
    planner_params = (branch_w, branch_b, head_w.T, head_b, value_w, value_b, out_w.T, out_b)
    width = linear_w.shape[1]
    big_rows = linear_w.shape[0] + (branch_w.shape[0] + 1) * width
    size = round_up(-(-big_rows // (2 * CUBE)), 16)

    tiny = (bias_one, bias_two, linear_b, branch_b, head_w.T, value_b, out_w.T)
    tiny = [stays(v if v.ndim > 1 else v[None, :]) for v in tiny]
    numbers, table = pl.pallas_call(
        numbers_kernel,
        in_specs=[pl.BlockSpec(memory_space=pltpu.VMEM)] * (6 + len(tiny)),
        out_shape=[shape_of(frame_count, LANES), shape_of(TABLE, LANES)],
        compiler_params=params(),
        cost_estimate=cost(1),
        name="numbers",
    )(
        stays(options),
        stays(depth[None, :]),
        stays(targets),
        stays(destination[None, :]),
        *tiny,
        stays(head_b[None, :]),
        out_b[None, :],
    )
    slots = exchanged(numbers.reshape(peers, per_pair, LANES)).reshape(frame_count, LANES)

    h1, s1, s2, h2, enc, s3 = encode(section, frames, w1t, w2t, stays(linear_w), table)
    keep, send_one, send_two, small, g3 = plan(
        section, slots, enc, s3, h2, branch_w, value_w, table, per_pair, levels, CUBE * size
    )
    recv = swapped(send_one), swapped(send_two)
    channels = frames.shape[2] // lax.axis_size("section")
    g1, c2, sums = back(g3, linear_w, s2, s1, h1, w2t)
    other = swapped(g1)
    g1 = held_near(g1)
    cubes = [list(range(c, c + CUBE)) for c in range(0, peers, CUBE)]
    bf16 = functools.partial(shape_of, dtype=BF16)
    pieces = small_call(
        merge_kernel,
        bf16(CUBE, size + 2 * SHORT, LANES),
        (keep, *recv, small, c2, sums),
        [
            pltpu.VMEM((CUBE * SHORT, LANES), F32),
            pltpu.VMEM((CUBE, size + 2 * SHORT, LANES), BF16),
            pltpu.SemaphoreType.DMA((CUBE,)),
        ],
        name="merge",
        far=True,
        weight=30,
    )
    got = exchanged(pieces, cubes)
    c1, frames_grad, band = first(section, frames, g1, w1t, other, pieces, channels, DRAW)
    piece = bf16(size + 2 * SHORT + c1.shape[0], LANES)
    keep = small_call(cube_kernel, piece, (got, c1), name="cube")
    distance = CUBE
    while distance < peers:
        recv = partner(keep, distance)
        if distance == CUBE:
            frames_grad, token = pixels(section, band, g1, other, keep, frames_grad, DRAW)
        distance *= 2
        keep = small_call(add_kernel, piece, (keep, recv), name="add", after=(token,))
    parts = [keep] + [partner(keep, k) for k in range(1, CUBE)]
    place = (lax.axis_index("batch").astype(jnp.int32)[None],)
    got = small_call(
        relay_kernel,
        [bf16(CUBE // 2, *piece.shape)] * 2,
        parts,
        [pltpu.VMEM((CUBE, *piece.shape), BF16)],
        name="relay",
        place=place,
    )
    got_other = [swapped(v) for v in got]
    shapes = [p.shape for p in encoder_params + planner_params]
    near = pl.BlockSpec(memory_space=pltpu.VMEM)
    flat = [shape_of(*(v if len(v) > 1 else (1,) + v)) for v in [(1, 1)] + shapes]
    large = [flat[k] for k in (5, 7, 11)]
    staged = [
        pltpu.VMEM((CUBE * size, LANES), F32),
        pltpu.VMEM(branch_w.shape, F32),
    ]
    little = [v for k, v in enumerate(flat) if k not in (5, 7, 11)]
    sems = pltpu.SemaphoreType.DMA((CUBE + len(little),))
    begun = pl.pallas_call(
        own_kernel,
        in_specs=[SCALARS, near, near],
        out_specs=[ANYWHERE] * 3,
        out_shape=large,
        scratch_shapes=[*staged, sems],
        compiler_params=params(),
        cost_estimate=cost(1),
        name="own",
    )(section, *got)
    ends = pl.pallas_call(
        unpack_kernel,
        in_specs=[SCALARS] + [near] * 4 + [ANYWHERE] * 3,
        out_specs=[ANYWHERE] * (3 + len(little)),
        out_shape=large + little,
        scratch_shapes=[pltpu.VMEM(v.shape, F32) for v in little]
        + [*staged, pltpu.VMEM((CUBE * SHORT, LANES), F32), sems],
        input_output_aliases={5: 0, 6: 1, 7: 2},
        compiler_params=params(),
        cost_estimate=cost(1.5),
        name="unpack",
    )(section, *got, *got_other, *begun)
    rest = list(ends[3:])
    for k, at in enumerate((5, 7, 11)):
        rest.insert(at, ends[k])
    rest = [v.reshape(s) for v, s in zip(rest, [()] + shapes)]
    for at in (1, 3, 9, 13):
        rest[at] = rest[at].T
    return (rest[0], frames_grad.transpose(2, 0, 1, 3), *rest[1:])


def solution(mesh):
    placed = (
        P(None, None, None, "batch"),
        P("batch"),
        P(None, "batch"),
        P("batch"),
        P(None, None, "batch"),
    ) + (P(),) * 14
    return jax.shard_map(
        local,
        mesh=mesh,
        in_specs=placed,
        out_specs=(P(), P("section", None, None, "batch")) + (P(),) * 14,
        check_vma=False,
    )
```

```python
import functools
import math

import jax
import jax.numpy as jnp
from jax import lax
from jax.experimental import pallas as pl
from jax.experimental.pallas import tpu as pltpu
from jax.sharding import PartitionSpec as P

BF16 = jnp.bfloat16
F32 = jnp.float32
EXACT = lax.Precision.HIGHEST
LANES = 128
VMEM_BYTES = 32 * 1024 * 1024
TILE = 16
REACH = 5
STEP = 3
COLS = 12
NEAR = 4
AT_VB, AT_OW, AT_HW, AT_LB, AT_SCALARS, AT_B1, AT_B2, AT_DEST = (
    slice(18, 19),
    slice(19, 20),
    slice(20, 22),
    slice(22, 23),
    slice(23, 24),
    slice(24, 25),
    slice(25, 26),
    26,
)
TABLE = 32
CUBE = 8
DRAW = 4
SHORT = 16


def dot(a, b, precision=None):
    return jnp.dot(a, b, preferred_element_type=F32, precision=precision)


def dot_rows(a, b, precision=None):
    return lax.dot_general(
        a, b, (((0,), (0,)), ((), ())), preferred_element_type=F32, precision=precision
    )


def dot_lanes(a, b, precision=None):
    return lax.dot_general(
        a, b, (((1,), (1,)), ((), ())), preferred_element_type=F32, precision=precision
    )


def iota(shape, axis):
    return lax.broadcasted_iota(jnp.int32, shape, axis)


def column(row):
    n = row.shape[1]
    wide = jnp.broadcast_to(row, (n, n))
    return jnp.sum(jnp.where(iota((n, n), 0) == iota((n, n), 1), wide, 0.0), axis=1, keepdims=True)


def row_of(col):
    n = col.shape[0]
    wide = jnp.broadcast_to(col, (n, n))
    return jnp.sum(jnp.where(iota((n, n), 0) == iota((n, n), 1), wide, 0.0), axis=0, keepdims=True)


def soft(x):
    t = jnp.tanh(0.5 * x)
    return jnp.maximum(x, 0.0) - jnp.log(0.5 + 0.5 * jnp.abs(t)), 0.5 + 0.5 * t


def silu_pair(y):
    t = jnp.tanh(y)
    m = y * t
    return y + m, (1.0 + t) + (y - m * t)


def pixel_order(w1t):
    tap, pix = iota((256, 256), 0), iota((256, 256), 1)
    moves = ((tap >> 6) == (pix & 3)) & ((tap & 63) == (pix >> 2))
    return dot(w1t, moves.astype(F32).astype(BF16))


def frame_copies(section, far, here, sems):
    lanes = pl.ds(pl.multiple_of(section[0] * LANES, LANES), LANES)
    size = 4 * STEP

    def copy(g, part=None):
        rows = pl.ds(pl.multiple_of(g * size, size), size)
        if part is not None:
            rows = slice(g * size + 2 * part, g * size + 2 * part + 2)
        return pltpu.make_async_copy(far.at[rows, :, :, lanes], here.at[rows], sems.at[g])

    return copy


def start_frames(arrives, steps):
    for part in range(2 * STEP):
        arrives(0, part).start()
    for g in range(1, steps):
        arrives(g).start()


def tile_rows(frames, row, j, cols):
    img, _, channels, _ = frames.shape
    flat = frames.reshape(img, img * channels, LANES)
    size = cols * channels
    end = min((j + 1) * size, img * channels)
    part = flat[pl.ds(row, 4), j * size : end, :]
    return part.reshape(4 * (end - j * size), LANES)


def encode_kernel(
    section,
    frames_far,
    w1t,
    w2t,
    lw_far,
    table,
    h1_far,
    s1_far,
    s2_far,
    h2,
    enc,
    s3,
    frames,
    lw,
    h1,
    s1,
    s2,
    band,
    edge,
    band2,
    bias1,
    bias2,
    held,
    held2,
    sems,
):
    blocks, side = h1.shape[:2]
    steps = blocks // STEP
    tiles = frames.shape[1] // TILE
    k1, k2 = w1t.shape[0], w2t.shape[0]
    reach_rows = REACH * k1
    arrives = frame_copies(section, frames_far, frames, sems.at[0])
    start_frames(arrives, steps)
    last_copies = [
        pltpu.make_async_copy(lw_far, lw, sems.at[3, 0]),
        pltpu.make_async_copy(s2, s2_far, sems.at[3, 1]),
    ]
    last_copies[0].start()

    def leaves(g):
        rows = pl.ds(g * STEP, STEP)
        return [
            pltpu.make_async_copy(h1.at[rows], h1_far.at[rows], sems.at[1, g]),
            pltpu.make_async_copy(s1.at[rows], s1_far.at[rows], sems.at[2, g]),
        ]

    inner = side // 2 - 1
    row_len = inner * k2
    two = 2 * k2 * 3

    def prepare():
        taps = pixel_order(w1t[...])
        edges = []
        for half in range(2):
            lines = [taps[:, 32 * (4 * half + u) : 32 * (4 * half + u + 1)] for u in range(4)]
            for place in range(REACH):
                pieces = []
                for line in lines:
                    start = 16 * (place - 1)
                    cut = line[:, max(0, -start) : min(32, 64 - start)]
                    start = max(start, 0)
                    pieces += [jnp.zeros((k1, start), F32)] if start else []
                    pieces.append(cut)
                    rest = 64 - start - cut.shape[1]
                    pieces += [jnp.zeros((k1, rest), F32)] if rest else []
                at = half * reach_rows + place * k1
                band[at : at + k1, :] = jnp.concatenate(pieces, axis=1).astype(BF16)
            edges.append(jnp.concatenate([line[:, 16:] for line in lines], axis=1))
        edge[...] = jnp.concatenate(edges, axis=0).astype(BF16)
        tap, pix = iota((256, LANES), 0), iota((256, LANES), 1)
        for half in range(2):
            for place in range(3):
                hit = (
                    ((tap & 15) == (pix & 15))
                    & ((tap >> 6) == (pix >> 6) + 2 * half)
                    & (((tap >> 4) & 3) == ((pix >> 4) & 3) + 2 - 2 * place)
                )
                at = (half * 3 + place) * k2
                taps = dot(w2t[...], hit.astype(F32).astype(BF16))
                band2[at : at + k2, :] = taps.astype(BF16)
        bias1[...] = jnp.broadcast_to(column(table[AT_B1, 0:k1]), bias1.shape)
        bias2[...] = jnp.broadcast_to(column(table[AT_B2, 0:k2]), bias2.shape)
        held[...] = jnp.zeros_like(held)
        held2[...] = jnp.zeros_like(held2)
        h1[...] = jnp.zeros_like(h1)

    def added(sums, x, value):
        sums[x] = sums[x] + value if x in sums else value

    def second_matmul(b):
        tiles = [
            h1[pl.ds(2 * b + 1, 2), 4 * j : 4 * j + 4].reshape(LANES, LANES)
            for j in range(side // 4)
        ]
        return dot(band2[...], jnp.concatenate(tiles, axis=1))

    def second_rows(b, got):
        low, high = {}, {}
        for j in range(side // 4):
            for place in range(3):
                x = 2 * j - 1 + place
                if 0 <= x < inner:
                    span = slice(j * LANES, (j + 1) * LANES)
                    at = place * k2
                    added(low, x, got[at : at + k2, span])
                    added(high, x, got[two // 2 + at : two // 2 + at + k2, span])
        row = jnp.maximum(b - 1, 0) * row_len
        for x in range(inner):
            value, slope = soft(held2[x] + high[x] + bias2[...])
            held2[x] = low[x]
            at = pl.ds(pl.multiple_of(row + x * k2, k2), k2)
            h2[at, :] = value.astype(BF16)
            s2[at, :] = slope.astype(BF16)

    def one_step(g, carry):
        def row(r):
            return pl.multiple_of(4 * (STEP * g + r), 4)

        arrives(g).wait()
        lows, highs = [{} for _ in range(STEP)], [{} for _ in range(STEP)]

        def place_tile(r, j, got):
            for place in range(REACH):
                x = 4 * j - 1 + place
                if 0 <= x < side:
                    at = place * k1
                    added(lows[r], x, got[at : at + k1])
                    added(highs[r], x, got[reach_rows + at : reach_rows + at + k1])

        def finish(r, xs):
            for x in xs:
                value, slope = soft(held[x] + highs[r][x] + bias1[...])
                held[x] = lows[r][x]
                h1[STEP * g + r, x] = value.astype(BF16)
                s1[STEP * g + r, x] = slope.astype(BF16)

        pair = jnp.maximum(g - 1, 0)
        units = [(lambda: second_matmul(pair), lambda got: second_rows(pair, got))]

        def edges():
            parts = [tile_rows(frames, row(r), tiles, TILE) for r in range(STEP)]
            return dot(edge[...], jnp.concatenate(parts, axis=1))

        def place_edges(got):
            for r in range(STEP):
                added(lows[r], side - 1, got[:k1, r * LANES : (r + 1) * LANES])
                added(highs[r], side - 1, got[k1:, r * LANES : (r + 1) * LANES])

        units.append((edges, place_edges))

        def full(spots):
            parts = [tile_rows(frames, row(r), j, TILE) for r, j in spots]
            return dot(band[...], jnp.concatenate(parts, axis=1))

        def place_full(got, spots, ready):
            for i, (r, j) in enumerate(spots):
                place_tile(r, j, got[:, i * LANES : (i + 1) * LANES])
            if ready:
                finish(*ready)

        for r in range(STEP):
            if r % 2 == 0:
                spots = [(k, tiles - 1) for k in (r, r + 1) if k < STEP]
                units.append(
                    (
                        functools.partial(full, spots),
                        functools.partial(place_full, spots=spots, ready=None),
                    )
                )
            done = 0
            for j in range(0, tiles - 1, 2):
                spots = [(r, j), (r, j + 1)]
                ready = side if j + 2 == tiles - 1 else 4 * j + 7
                units.append(
                    (
                        functools.partial(full, spots),
                        functools.partial(place_full, spots=spots, ready=(r, range(done, ready))),
                    )
                )
                done = ready
        waiting = None
        for issue, take in units:
            got = issue()
            if waiting is not None:
                waiting[0](waiting[1])
            waiting = (take, got)
        waiting[0](waiting[1])
        for copy in leaves(g):
            copy.start()
        return carry

    prepare()
    lax.fori_loop(0, steps, one_step, 0)
    for b in range(steps - 1, side // 2):
        second_rows(b, second_matmul(b))
    for copy in last_copies[1:]:
        copy.start()
    last_copies[0].wait()
    value, slope = soft(dot_rows(lw[...], h2[...]) + column(table[AT_LB, :]))
    enc[...] = value.astype(BF16)
    s3[...] = slope
    for g in range(steps):
        for copy in leaves(g):
            copy.wait()
    for copy in last_copies[1:]:
        copy.wait()


def three_parts(row):
    high = row.astype(BF16).astype(F32)
    middle = (row - high).astype(BF16).astype(F32)
    return jnp.concatenate([high, middle, row - high - middle], axis=0)


def with_ones(value):
    return jnp.concatenate([value, ones_rows(value.shape[1])], axis=0)


def ones_rows(lanes):
    return (iota((16, lanes), 0) < 3).astype(F32).astype(BF16)


def plan_kernel(
    section,
    slots,
    enc,
    s3,
    h2,
    branch_far,
    value_w,
    table,
    keep,
    send_one,
    send_two,
    small,
    g3,
    parts,
    bwt,
    vht,
    vhw,
    ow,
    mine,
    pre,
    dbr,
    dval,
    low,
    hid,
    gb,
    branch_w,
    sem,
    *,
    per_pair,
    depth,
):
    width = enc.shape[0]
    options = branch_w.shape[0]
    pairs = options // 2
    two = 2 * width
    sec = section[0]
    branch_copy = pltpu.make_async_copy(branch_far, branch_w, sem)
    branch_copy.start()

    count = slots.shape[0]
    dest = jnp.concatenate(
        [table[AT_DEST + k : AT_DEST + k + 1, :] for k in range(count // LANES)], axis=1
    )
    own = jnp.where(sec == 0, dest[:, :LANES], dest[:, LANES:])
    others = jnp.transpose(jnp.broadcast_to(dest, (LANES, count)))
    index = iota((count, LANES), 1) + sec * LANES
    earlier = (others == own) & (iota((count, LANES), 0) < index)
    rank = jnp.sum(earlier.astype(F32), axis=0, keepdims=True)
    bucket = own * float(per_pair) + rank
    chosen = (iota((count, LANES), 0).astype(F32) == bucket).astype(F32).astype(BF16)
    numbers = slots[...]
    high = numbers.astype(BF16)
    middle = (numbers - high.astype(F32)).astype(BF16)
    rest = (numbers - high.astype(F32) - middle.astype(F32)).astype(BF16)
    mine[...] = sum(dot_rows(v, chosen) for v in (rest, middle, high))[: mine.shape[0]]

    pad = jnp.zeros((13, width), F32)
    branch_copy.wait()
    for o in range(options):
        rows = [branch_w[o].astype(F32), three_parts(table[o : o + 1, :]), pad]
        bwt[o * width : (o + 1) * width, :] = jnp.transpose(
            0.5 * jnp.concatenate(rows, axis=0)
        ).astype(BF16)
    scalars = table[AT_SCALARS, :]
    head_w = table[AT_HW, :]
    rows = [value_w[...].astype(F32), three_parts(table[AT_VB, :]), pad]
    vht[0:width, :] = jnp.transpose(0.5 * jnp.concatenate(rows, axis=0)).astype(BF16)
    vht[width:, :] = jnp.zeros((16, width + 16), BF16)
    lane = iota((1, 16), 1)
    for k in range(2):
        bias = three_parts(jnp.broadcast_to(scalars[:, 1 + k : 2 + k], (1, 16)))
        bias = sum(jnp.where(lane == j, bias[j : j + 1], 0.0) for j in range(3))
        vht[width + k : width + k + 1, 0:width] = head_w[k : k + 1].astype(BF16)
        vht[width + k : width + k + 1, width:] = bias.astype(BF16)
    vhw[:, 0:width] = (0.5 * value_w[...].astype(F32)).astype(BF16)
    vhw[:, width:] = jnp.transpose(
        0.5 * jnp.concatenate([head_w, jnp.zeros((14, width), F32)], axis=0)
    ).astype(BF16)
    ow[...] = jnp.broadcast_to(column(table[AT_OW, :]), (width, LANES))
    wide_ow = jnp.concatenate([ow[...], ow[...]], axis=1)
    half_ow = 0.5 * wide_ow

    labels = iota((options, LANES), 0).astype(F32)
    state = enc[...].astype(F32)
    rounded_all, saved = [], []
    group = 3
    for level in range(depth):
        picked = labels == mine[level : level + 1, :]
        rounded = state.astype(BF16)
        rounded_all.append(rounded)
        met = with_ones(rounded)

        def branches(first):
            at = slice(first * two, (first + group) * two)
            pre[at, :] = dot(bwt[at, :], met)

        branches(0)
        following = state
        reward, discount, value = [], [], []

        def value_part(t, got):
            act, slope = silu_pair(got[:width])
            dval[level, t] = slope
            hidden = act.astype(BF16)
            hid[level, t] = hidden
            worth = jnp.sum(hidden.astype(F32) * wide_ow, axis=0, keepdims=True)
            for k in range(2):
                span = slice(k * LANES, (k + 1) * LANES)
                value.append(worth[:, span])
                reward.append(got[width : width + 1, span])
                discount.append(got[width + 1 : width + 2, span])

        waiting = None
        for first in range(0, pairs, group):
            if first + group < pairs:
                branches(first + group)
            boths = []
            for t in range(first, first + group):
                at = slice(t * two, (t + 1) * two)
                act, slope = silu_pair(pre[at, :])
                dbr[level, at, :] = slope
                left = state + act[:width]
                right = state + act[width:]
                following = jnp.where(picked[2 * t : 2 * t + 1], left, following)
                following = jnp.where(picked[2 * t + 1 : 2 * t + 2], right, following)
                both = with_ones(
                    jnp.concatenate([left.astype(BF16), right.astype(BF16)], axis=1)
                )
                low[level, t] = both
                boths.append(both)
            got = dot(vht[...], jnp.concatenate(boths, axis=1))
            if waiting is not None:
                for k in range(group):
                    value_part(waiting[0] + k, waiting[1][:, k * two : (k + 1) * two])
            waiting = (first, got)
        for k in range(group):
            value_part(waiting[0] + k, waiting[1][:, k * two : (k + 1) * two])
        reward = jnp.concatenate(reward, axis=0)
        discount = jax.nn.sigmoid(jnp.concatenate(discount, axis=0))
        value = jnp.concatenate(value, axis=0) + scalars[:, 3:4]
        quality = reward + discount * value
        top = jnp.max(quality, axis=0, keepdims=True)
        shifted = jnp.exp(quality - top)
        total = jnp.sum(shifted, axis=0, keepdims=True)
        live = (mine[depth : depth + 1, :] > level).astype(F32)
        chosen = picked.astype(F32)

        def target(kind):
            at = depth + 1 + kind * depth + level
            return mine[at : at + 1, :]

        reward_gap = live * (jnp.sum(chosen * reward, axis=0, keepdims=True) - target(0))
        discount_gap = live * (jnp.sum(chosen * discount, axis=0, keepdims=True) - target(1))
        plan_gap = live * (top + jnp.log(total) - target(2))
        grad_quality = plan_gap * (shifted / total)
        head_two = (chosen * discount_gap + grad_quality * value) * discount * (1.0 - discount)
        saved.append(
            (
                picked,
                (chosen * reward_gap + grad_quality).astype(BF16).astype(F32),
                head_two.astype(BF16).astype(F32),
                (grad_quality * discount).astype(BF16).astype(F32),
                reward_gap * reward_gap + discount_gap * discount_gap + plan_gap * plan_gap,
            )
        )
        state = following

    out_sum = jnp.zeros((16, width), F32)
    value_sum = jnp.zeros((width + 16, width + 16), F32)
    grad_next = None
    line = iota((16, two), 0)
    for level in reversed(range(depth)):
        picked, head_one, head_two, grad_value, _ = saved[level]
        upward = jnp.zeros((width, LANES), F32)

        def branch_part(t, moved):
            at = slice(t * two, (t + 1) * two)
            left, right = moved[:, :LANES], moved[:, LANES:]
            if grad_next is not None:
                left = left + jnp.where(picked[2 * t : 2 * t + 1], grad_next, 0.0)
                right = right + jnp.where(picked[2 * t + 1 : 2 * t + 2], grad_next, 0.0)
            grad_branch = jnp.concatenate([left, right], axis=0) * dbr[level, at, :]
            grad_branch = grad_branch.astype(BF16)
            gb[level, at, :] = grad_branch
            return left + right

        def group_part(first, moved):
            parts = [
                branch_part(first + k, moved[:, k * two : (k + 1) * two]) for k in range(group)
            ]
            at = slice(first * two, (first + group) * two)
            weights = [branch_w[o] for o in range(2 * first, 2 * (first + group))]
            return sum(parts), dot(jnp.concatenate(weights, axis=1), gb[level, at, :])

        waiting = None
        for first in range(0, pairs, group):
            stack = []
            for t in range(first, first + group):

                def across(rows):
                    return jnp.concatenate(
                        [rows[2 * t : 2 * t + 1], rows[2 * t + 1 : 2 * t + 2]], axis=1
                    )

                worth = across(grad_value)
                grad_pre = (worth * half_ow * dval[level, t]).astype(BF16)
                heads = jnp.where(line == 0, across(head_one), 0.0)
                heads = jnp.where(line == 1, across(head_two), heads)
                heads = jnp.where(line == 2, worth, heads)
                heads = heads.astype(BF16)
                out_sum = out_sum + dot_lanes(heads, hid[level, t])
                stack.append(jnp.concatenate([grad_pre, heads], axis=0))
            stack = jnp.concatenate(stack, axis=1)
            moved = dot(vhw[...], stack)
            lows = jnp.concatenate([low[level, first + k] for k in range(group)], axis=1)
            value_sum = value_sum + dot_lanes(stack, lows)
            if waiting is not None:
                one, other = group_part(*waiting)
                upward = upward + (one + 0.5 * other)
            waiting = (first, moved)
        one, other = group_part(*waiting)
        grad_next = upward + (one + 0.5 * other)

    linear_rows = h2.shape[0]
    half = (linear_rows + options * width + width) // 2
    rest = linear_rows - half
    rounded = with_ones(jnp.concatenate(rounded_all, axis=1))
    small[...] = jnp.zeros_like(small)
    if half < keep.shape[0]:
        for k in range(2):
            parts[k, half:, :] = jnp.zeros((keep.shape[0] - half, LANES), BF16)
    for t in range(pairs):
        at = slice(t * two, (t + 1) * two)
        grads = jnp.concatenate([gb[level, at, :] for level in range(depth)], axis=1)
        got = dot_lanes(rounded, grads)
        for k in range(2):
            o = 2 * t + k
            span = slice(k * width, (k + 1) * width)
            rows = slice(rest + o * width, rest + (o + 1) * width)
            parts[1 - sec, rows, :] = got[:width, span].astype(BF16)
            small[o : o + 1, :] = got[width : width + 1, span]
    after = rest + options * width
    parts[1 - sec, after : after + width, :] = jnp.transpose(value_sum[:width, :width]).astype(BF16)

    grad_three = ((2.0 * grad_next).astype(BF16).astype(F32) * s3[...]).astype(BF16)
    g3[...] = grad_three
    chunk = linear_rows // 9
    for i in range(8):
        at = slice(i * chunk, (i + 1) * chunk)
        parts[sec, at, :] = dot_lanes(h2[at, :], grad_three).astype(BF16)
    last = dot_lanes(h2[8 * chunk :, :], grad_three).astype(BF16)
    parts[sec, 8 * chunk : half, :] = last[: half - 8 * chunk]
    parts[1 - sec, 0:rest, :] = last[half - 8 * chunk :]
    keep[...] = parts[0]
    send_one[...] = parts[1, : send_one.shape[0]]
    send_two[...] = parts[1, send_one.shape[0] :]

    small[AT_VB, :] = row_of(value_sum[:width, width : width + 1])
    small[AT_OW, :] = out_sum[2:3]
    small[AT_HW, :] = value_sum[width : width + 2, :width]
    small[AT_LB, :] = row_of(jnp.sum(grad_three.astype(F32), axis=1, keepdims=True))
    loss = 0.5 * jnp.sum(sum(kept[4] for kept in saved), axis=1, keepdims=True)
    ends = [loss] + [value_sum[width + k : width + k + 1, width : width + 1] for k in range(3)]
    lane = iota((1, LANES), 1)
    line = jnp.zeros((1, LANES), F32)
    for k, end in enumerate(ends):
        line = jnp.where(lane == k, end, line)
    small[AT_SCALARS, :] = line


def back_kernel(g3, lw, s2, s1, h1, w2t, g1, c2, sums, t2, g2):
    side, k1 = s1.shape[1], s1.shape[2]
    k2 = w2t.shape[0]
    inner = side // 2 - 1
    row_len = inner * k2
    tap, pix = iota((LANES, 256), 1), iota((LANES, 256), 0)
    for yrel in range(2):
        for p in range(3):
            hit = (
                ((tap & 15) == (pix & 15))
                & ((tap >> 6) == (pix >> 6) + 2 * (1 - yrel))
                & (((tap >> 4) & 3) == ((pix >> 4) & 3) + 2 - 2 * p)
            )
            at = (yrel * 3 + p) * k2
            t2[:, at : at + k2] = dot_lanes(hit.astype(F32).astype(BF16), w2t[...]).astype(BF16)
    g2[0] = jnp.zeros(g2.shape[1:], BF16)
    g2[inner + 1] = jnp.zeros(g2.shape[1:], BF16)
    g1[0] = jnp.zeros(g1.shape[1:], BF16)
    g1[side + 1] = jnp.zeros(g1.shape[1:], BF16)
    zero = jnp.zeros((k2, LANES), BF16)
    total_one = jnp.zeros((k1, LANES), F32)
    total_two = jnp.zeros((k2, LANES), F32)
    for y in range(inner):
        at = slice(y * row_len, (y + 1) * row_len)
        grad = dot(lw[at, :], g3[...]) * s2[at, :].astype(F32)
        grad = grad.astype(BF16).reshape(inner, k2, LANES)
        g2[y + 1] = grad
        total_two = total_two + jnp.sum(grad.astype(F32), axis=0)
    reach, cols = 5, 8
    total = jnp.zeros((2 * reach * k2, 2 * cols * k1), F32)
    grads, tiles = [], []
    for b in range(side // 2):
        cut = []
        for j in range(side // 4):
            pieces = []
            for yrel in range(2):
                for p in range(3):
                    x = 2 * j - 1 + p
                    pieces.append(g2[b + yrel, x] if 0 <= x < inner else zero)
            cut.append(jnp.concatenate(pieces, axis=0))
        got = dot(t2[...], jnp.concatenate(cut, axis=1))
        for u in range(2):
            for j in range(side // 4):
                part = got[u * 64 : (u + 1) * 64, j * LANES : (j + 1) * LANES]
                slope = s1[2 * b + u + 1, 4 * j : 4 * j + 4].astype(F32)
                grad = (part.reshape(4, k1, LANES) * slope).astype(BF16)
                g1[2 * b + u + 1, 4 * j : 4 * j + 4] = grad
                total_one = total_one + jnp.sum(grad.astype(F32), axis=0)
        for j in range(-(-side // cols)):
            end = min((j + 1) * cols, side)
            tile = h1[2 * b + 1 : 2 * b + 3, j * cols : end]
            if end < (j + 1) * cols:
                rest = jnp.zeros((2, (j + 1) * cols - end, k1, LANES), BF16)
                tile = jnp.concatenate([tile, rest], axis=1)
            tiles.append(tile.reshape(2 * cols * k1, LANES))
            pieces = []
            for half in range(2):
                for p in range(reach):
                    x = 4 * j - 1 + p
                    pieces.append(g2[b + 1 - half, x] if 0 <= x < inner else zero)
            grads.append(jnp.concatenate(pieces, axis=0))
        if b % 2:
            total = total + dot_lanes(
                jnp.concatenate(grads, axis=1), jnp.concatenate(tiles, axis=1)
            )
            grads, tiles = [], []
    line = 4 * k1
    for half in range(2):
        for u in range(2):
            tap_row = jnp.zeros((k2, line), F32)
            for p in range(reach):
                at = (half * reach + p) * k2
                part = total[at : at + k2, u * 2 * line : (u + 1) * 2 * line]
                start = 2 * k1 * (p - 1)
                piece = part[:, max(start, 0) : min(start + line, 2 * line)]
                if start < 0:
                    piece = jnp.concatenate([jnp.zeros((k2, -start), F32), piece], axis=1)
                if start + line > 2 * line:
                    rest = jnp.zeros((k2, start - line), F32)
                    piece = jnp.concatenate([piece, rest], axis=1)
                tap_row = tap_row + piece
            at = (2 * half + u) * line
            c2[:, at : at + line] = tap_row
    sums[...] = jnp.zeros_like(sums)
    sums[0:1, 0:k1] = row_of(jnp.sum(total_one, axis=1, keepdims=True))
    sums[1:2, 0:k2] = row_of(jnp.sum(total_two, axis=1, keepdims=True))


def pixel_band(sec, w1t, channels):
    k1 = w1t.shape[0]
    rows = 64 * channels
    row, tap = iota((rows, 256), 0), iota((rows, 256), 1)
    moves = ((tap >> 6) == row % channels + sec * channels) & ((tap & 63) == row // channels)
    taps = dot_lanes(moves.astype(F32).astype(BF16), w1t)
    line, span = COLS * channels, 8 * channels
    blocks = {}
    for half in range(2):
        for p in range(NEAR):
            pieces = []
            for u in range(4):
                at = (4 * half + u) * span
                start = 4 * (p - 1) * channels
                cut = taps[at + max(0, -start) : at + min(span, line - start)]
                start = max(start, 0)
                pieces += [jnp.zeros((start, k1), F32)] if start else []
                pieces.append(cut)
                rest = line - start - cut.shape[0]
                pieces += [jnp.zeros((rest, k1), F32)] if rest else []
            blocks[half, p] = jnp.concatenate(pieces, axis=0)
    zero = jnp.zeros((4 * line, k1), F32)
    lines = []
    for r in range(STEP):
        cols = [
            blocks.get((r + 1 - yrel, p), zero) for yrel in range(STEP + 1) for p in range(NEAR)
        ]
        lines.append(jnp.concatenate(cols, axis=1))
    return jnp.concatenate(lines, axis=0).astype(BF16)


def first_kernel(
    section,
    frames_far,
    g1,
    w1t,
    other_far,
    after,
    c1,
    out,
    band,
    frames,
    acc,
    other,
    held,
    sems,
    draw_sems,
    *,
    draw,
):
    side, k1 = g1.shape[1], g1.shape[2]
    img, _, channels, _ = frames.shape
    steps = img // 4 // STEP
    arrives = frame_copies(section, frames_far, frames, sems)
    start_frames(arrives, steps)
    other_copy = pltpu.make_async_copy(
        other_far.at[0 : STEP * draw + 1], other, sems.at[steps]
    )
    other_copy.start()
    acc[...] = jnp.zeros_like(acc)
    zero = jnp.zeros((k1, LANES), BF16)

    def one_step(g, carry):
        arrives(g).wait()
        pixels, grads = [], []
        for j in range(img // COLS):
            rows = [pl.multiple_of(4 * (STEP * g + r), 4) for r in range(STEP)]
            pixels.append(
                jnp.concatenate([tile_rows(frames, row, j, COLS) for row in rows], axis=0)
            )
            pieces = []
            for yrel in range(STEP + 1):
                for p in range(NEAR):
                    x = 3 * j - 1 + p
                    pieces.append(g1[STEP * g + yrel, x] if 0 <= x < side else zero)
            grads.append(jnp.concatenate(pieces, axis=0))
        acc[...] += dot_lanes(jnp.concatenate(pixels, axis=1), jnp.concatenate(grads, axis=1))
        return carry

    lax.fori_loop(0, steps, one_step, 0)
    band[...] = pixel_band(section[0], w1t[...], out.shape[2])
    other_copy.wait()
    finish = draw_steps(section, band, g1, 0, other, 0, out, held, draw_sems, 0, draw)
    fold_first(acc, c1, channels, k1)
    finish()


def fold_first(acc, c1, channels, k1):
    line = COLS * channels
    step = 4 * channels
    taps = []
    for half in range(2):
        total = sum(
            acc[r * 4 * line : (r + 1) * 4 * line, :][
                :, (r + 1 - half) * NEAR * k1 : (r + 2 - half) * NEAR * k1
            ]
            for r in range(STEP)
        )
        for u in range(4):
            part = total[u * line : (u + 1) * line]
            cols = [part[:, p * k1 : (p + 1) * k1] for p in range(NEAR)]
            taps.append(cols[1][0:step] + cols[2][step : 2 * step] + cols[3][2 * step :])
            taps.append(cols[0][0:step] + cols[1][step : 2 * step] + cols[2][2 * step :])
    row, col = iota((256, 256), 0), iota((256, 256), 1)
    moves = ((row & 3) == (col >> 6)) & ((row >> 2) == (col & 63))
    grad = dot_rows(jnp.concatenate(taps, axis=0), moves.astype(F32), EXACT)
    for half in range(2):
        c1[half * k1 : (half + 1) * k1, :] = grad[:, half * LANES : (half + 1) * LANES].astype(BF16)


def draw_steps(section, band, mine, mine_at, other, other_at, out, held, sems, start, steps):
    side, k1 = mine.shape[1], mine.shape[2]
    img, channels = out.shape[1], out.shape[2]
    sec = section[0]
    line = COLS * channels
    flat = held.reshape(2, 2, 4 * STEP, img * channels, LANES)

    def writes(g):
        rows = slice(4 * STEP * (start + g), 4 * STEP * (start + g + 1))
        places = (sec * LANES, (1 - sec) * LANES)
        return [
            pltpu.make_async_copy(
                held.at[g % 2, k],
                out.at[rows, :, :, pl.ds(pl.multiple_of(places[k], LANES), LANES)],
                sems.at[g % 2, k],
            )
            for k in range(2)
        ]

    zero = jnp.zeros((k1, 2 * LANES), BF16)
    for g in range(steps):
        if g >= 2:
            for copy in writes(g - 2):
                copy.wait()
        for j in range(img // COLS):
            pieces = []
            for yrel in range(STEP + 1):
                for p in range(NEAR):
                    x, y = 3 * j - 1 + p, STEP * (start + g) + yrel
                    if 0 <= x < side:
                        pair = [mine[y - mine_at, x], other[y - other_at, x]]
                        pieces.append(jnp.concatenate(pair, axis=1))
                    else:
                        pieces.append(zero)
            got = dot(band[...], jnp.concatenate(pieces, axis=0))
            for k in range(4 * STEP):
                at = slice(k * line, (k + 1) * line)
                span = slice(j * line, (j + 1) * line)
                flat[g % 2, 0, k, span, :] = got[at, :LANES]
                flat[g % 2, 1, k, span, :] = got[at, LANES:]
        for copy in writes(g):
            copy.start()

    def finish():
        for g in range(max(steps - 2, 0), steps):
            for copy in writes(g):
                copy.wait()

    return finish


def pixels_kernel(section, band, mine, other_far, after, done, out, token, held, other, sems, *, start):
    steps = other.shape[0] // STEP
    fetch = pltpu.make_async_copy(
        other_far.at[STEP * start : STEP * (start + steps) + 1], other, sems.at[2, 0]
    )
    fetch.start()
    token[...] = jnp.zeros_like(token)
    fetch.wait()
    draw_steps(
        section, band, mine, 0, other, STEP * start, out, held, sems, start, steps
    )()


def two_parts(value):
    high = value.astype(BF16).astype(F32)
    return jnp.concatenate([high, value - high], axis=0).astype(BF16)


def one_part(pair):
    rows = pair.shape[0] // 2
    pair = pair.astype(F32)
    return pair[:rows] + pair[rows:]


def merge_kernel(keep, recv_one, recv_two, small, c2, sums, out_far, lines, out, sems):
    members = out.shape[0]
    size = keep.shape[0] // members
    k2 = c2.shape[0]
    lines[...] = jnp.zeros_like(lines)
    at = small.shape[0]
    lines[0:at, :] = small[...]
    for half in range(2):
        lines[at : at + k2, :] = c2[:, half * LANES : (half + 1) * LANES]
        at += k2
    lines[at : at + sums.shape[0], :] = sums[...]
    for k in range(members):
        at = slice(k * size, (k + 1) * size)
        recv, here = recv_one, k
        if k >= members // 2:
            recv, here = recv_two, k - members // 2
        got = recv[here * size : (here + 1) * size, :]
        out[k, 0:size, :] = (keep[at, :].astype(F32) + got.astype(F32)).astype(BF16)
        out[k, size:, :] = two_parts(lines[k * SHORT : (k + 1) * SHORT, :])
        pltpu.make_async_copy(out.at[k], out_far.at[k], sems.at[k]).start()
    for k in range(members):
        pltpu.make_async_copy(out.at[k], out_far.at[k], sems.at[k]).wait()


def cube_kernel(got, c1, out):
    members = got.shape[0]
    size = got.shape[1] - 2 * SHORT
    out[0:size, :] = sum(got[k, 0:size, :].astype(F32) for k in range(members)).astype(BF16)
    total = sum(one_part(got[k, size:, :]) for k in range(members))
    out[size : size + 2 * SHORT, :] = two_parts(total)
    out[size + 2 * SHORT :, :] = c1[...]


def add_kernel(a, b, after, out):
    size = a.shape[0] - 2 * SHORT - 32
    middle = slice(size, size + 2 * SHORT)
    for span in (slice(0, size), slice(size + 2 * SHORT, a.shape[0])):
        out[span, :] = (a[span, :].astype(F32) + b[span, :].astype(F32)).astype(BF16)
    out[middle, :] = two_parts(one_part(a[middle, :]) + one_part(b[middle, :]))


def relay_kernel(batch, *refs):
    parts, (one, two, out) = refs[:CUBE], refs[CUBE:]
    me = batch[0] % CUBE
    for k, part in enumerate(parts):
        out[me ^ k] = part[...]
    one[...] = out[: CUBE // 2]
    two[...] = out[CUBE // 2 :]


def piece_of(got, k):
    count = got[0].shape[0]
    return got[k // count].at[k % count]


def unpack_half(which, got, lw, bw, vw, stage, stage_b, sems):
    members = 2 * got[0].shape[0]
    size = stage.shape[0] // members
    linear_rows, width = lw.shape
    options = bw.shape[0]
    half = (linear_rows + options * width + width) // 2
    rest = linear_rows - half
    group = options // 3

    def first_copies():
        spans = [(k * size, min((k + 1) * size, half)) for k in range(members)]
        return [
            pltpu.make_async_copy(stage.at[a:b], lw.at[a:b], sems.at[k])
            for k, (a, b) in enumerate(spans)
        ]

    def second_copies():
        copies = [pltpu.make_async_copy(stage.at[0:rest], lw.at[half:], sems.at[0])]
        for k in range(options // group):
            part = slice(k * group, (k + 1) * group)
            copies.append(pltpu.make_async_copy(stage_b.at[part], bw.at[part], sems.at[1 + k]))
        last = stage.at[rest : rest + width]
        copies.append(pltpu.make_async_copy(last, vw, sems.at[len(copies)]))
        return copies

    @pl.when(which == 0)
    def _():
        for k, copy in enumerate(first_copies()):
            start, end = k * size, min((k + 1) * size, half)
            stage[start:end, :] = piece_of(got, k)[0 : end - start, :].astype(F32)
            copy.start()

    @pl.when(which == 1)
    def _():
        def rows(start, end):
            parts = []
            while start < end:
                k, at = start // size, start % size
                count = min(size - at, end - start)
                parts.append(piece_of(got, k)[at : at + count, :])
                start += count
            value = parts[0] if len(parts) == 1 else jnp.concatenate(parts, axis=0)
            return value.astype(F32)

        copies = second_copies()
        stage[0:rest, :] = rows(0, rest)
        copies[0].start()
        for o in range(options):
            stage_b[o] = rows(rest + o * width, rest + (o + 1) * width)
            if o % group == group - 1:
                copies[1 + o // group].start()
        at = rest + options * width
        stage[rest : rest + width, :] = rows(at, at + width)
        copies[-1].start()

    def finish():
        for half_at, copies in ((0, first_copies), (1, second_copies)):

            @pl.when(which == half_at)
            def _():
                for copy in copies():
                    copy.wait()

    return finish


def own_kernel(section, one, two, lw, bw, vw, stage, stage_b, sems):
    unpack_half(section[0], (one, two), lw, bw, vw, stage, stage_b, sems)()


def unpack_kernel(section, *refs):
    mine, other, refs = refs[0:2], refs[2:4], refs[4:]
    lw, bw, vw = refs[3:6]
    little = (len(refs) - 10) // 2
    far, near = refs[6 : 6 + little], refs[6 + little : 6 + 2 * little]
    loss, c1, b1, c2, b2, lb, bb, hw, hb, vb, ow, ob = near
    stage, stage_b, lines, sems = refs[-4:]
    options = bw.shape[0]
    k1, k2 = c1.shape[0], c2.shape[0]
    size = stage.shape[0] // CUBE
    finish = unpack_half(1 - section[0], other, lw, bw, vw, stage, stage_b, sems)
    grad = [jnp.zeros((k1, LANES), F32) for _ in range(2)]
    for k in range(CUBE):
        pair = slice(size, size + 2 * SHORT)
        at = slice(k * SHORT, (k + 1) * SHORT)
        views = piece_of(mine, k), piece_of(other, k)
        lines[at, :] = sum(one_part(v[pair, :]) for v in views)
        for view in views:
            for h in range(2):
                at = size + 2 * SHORT + h * k1
                grad[h] += view[at : at + k1, :].astype(F32)
    for part in range(2):
        c1[:, part * LANES : (part + 1) * LANES] = grad[part]
    bb[...] = lines[0:options, :]
    vb[...] = lines[AT_VB, :]
    ow[...] = lines[AT_OW, :]
    hw[...] = lines[AT_HW, :]
    lb[...] = lines[AT_LB, :]
    scalars = lines[AT_SCALARS, :]
    loss[...] = scalars[:, 0:1]
    hb[...] = scalars[:, 1:3]
    ob[...] = scalars[:, 3:4]
    at = TABLE
    for part in range(2):
        c2[:, part * LANES : (part + 1) * LANES] = lines[at : at + k2, :]
        at += k2
    b1[...] = lines[at : at + 1, 0:k1]
    b2[...] = lines[at + 1 : at + 2, 0:k2]
    copies = [
        pltpu.make_async_copy(a, b, sems.at[CUBE + k]) for k, (a, b) in enumerate(zip(near, far))
    ]
    for copy in copies:
        copy.start()
    finish()
    for copy in copies:
        copy.wait()


def numbers_kernel(
    options,
    depth,
    targets,
    destination,
    b1,
    b2,
    lb,
    bb,
    hw,
    vb,
    ow,
    hb,
    ob,
    out,
    table,
):
    levels, kinds = options.shape[0], targets.shape[0]
    slots = depth.shape[1]
    rows = [options[...].astype(F32), depth[...].astype(F32)]
    rows += [targets[k] for k in range(kinds)]
    rows.append(jnp.zeros((LANES - levels - 1 - kinds * levels, slots), F32))
    out[...] = jnp.transpose(jnp.concatenate(rows, axis=0))
    table[...] = jnp.zeros_like(table)
    table[0 : bb.shape[0], :] = bb[...]
    table[AT_VB, :] = vb[...]
    table[AT_OW, :] = ow[...].astype(F32)
    table[AT_HW, :] = hw[...].astype(F32)
    table[AT_LB, :] = lb[...]
    table[AT_B1, 0 : b1.shape[1]] = b1[...]
    table[AT_B2, 0 : b2.shape[1]] = b2[...]
    lane = iota((1, LANES), 1)
    scalars = jnp.zeros((1, LANES), F32)
    for k, value in ((1, hb[:, 0:1]), (2, hb[:, 1:2]), (3, ob[...])):
        scalars = jnp.where(lane == k, value, scalars)
    table[AT_SCALARS, :] = scalars
    for k in range(slots // LANES):
        part = destination[:, k * LANES : (k + 1) * LANES]
        table[AT_DEST + k : AT_DEST + k + 1, :] = part.astype(F32)


def whole(shape):
    zeros = (0,) * len(shape)
    return pl.BlockSpec(shape, lambda *_: zeros)


ANYWHERE = pl.BlockSpec(memory_space=pl.ANY)
SCALARS = pl.BlockSpec(memory_space=pltpu.SMEM)


def params():
    return pltpu.CompilerParams(vmem_limit_bytes=VMEM_BYTES)


def shape_of(*shape, dtype=F32):
    return jax.ShapeDtypeStruct(shape, dtype)


def cost(microseconds):
    return pl.CostEstimate(
        flops=int(1.1e9 * microseconds), bytes_accessed=int(3.6e6 * microseconds), transcendentals=0
    )


def stays(value):
    return pltpu.with_memory_space_constraint(value, pltpu.HBM)


def held_near(value):
    return pltpu.with_memory_space_constraint(value, pltpu.VMEM)


def encode(section, frames, w1t, w2t, lw, table):
    img = frames.shape[0]
    blocks = img // 4
    side = blocks - 1
    k1, k2, width = w1t.shape[0], w2t.shape[0], lw.shape[1]
    flat = lw.shape[0]
    vmem = pltpu.VMEM
    near = pl.BlockSpec(memory_space=vmem)
    grid_one = (blocks, side, k1, LANES)
    return pl.pallas_call(
        encode_kernel,
        in_specs=[SCALARS, ANYWHERE, near, near, ANYWHERE, near],
        out_specs=[ANYWHERE] * 3 + [near] * 3,
        out_shape=(
            pltpu.HBM(grid_one, BF16),
            pltpu.HBM(grid_one, BF16),
            pltpu.HBM((flat, LANES), BF16),
            shape_of(flat, LANES, dtype=BF16),
            shape_of(width, LANES, dtype=BF16),
            shape_of(width, LANES),
        ),
        scratch_shapes=[
            vmem((img, img, frames.shape[2], LANES), BF16),
            vmem(lw.shape, BF16),
            vmem(grid_one, BF16),
            vmem(grid_one, BF16),
            vmem((flat, LANES), BF16),
            vmem((2 * REACH * k1, 256), BF16),
            vmem((2 * k1, 64), BF16),
            vmem((6 * k2, LANES), BF16),
            vmem((k1, LANES), F32),
            vmem((k2, LANES), F32),
            vmem((side, k1, LANES), F32),
            vmem((side // 2 - 1, k2, LANES), F32),
            pltpu.SemaphoreType.DMA((4, max(blocks // STEP, 3))),
        ],
        compiler_params=params(),
        cost_estimate=cost(9),
        name="encode",
    )(section, frames, w1t, w2t, lw, table)


def plan(section, slots, enc, s3, h2, branch_w, value_w, table, per_pair, depth, half_rows):
    width = enc.shape[0]
    options = branch_w.shape[0]
    two = 2 * width
    pairs = options // 2
    outs = (
        shape_of(half_rows, LANES, dtype=BF16),
        shape_of(half_rows // 2, LANES, dtype=BF16),
        shape_of(half_rows // 2, LANES, dtype=BF16),
        shape_of(TABLE, LANES),
        shape_of(width, LANES, dtype=BF16),
    )
    vmem = pltpu.VMEM
    near = pl.BlockSpec(memory_space=vmem)
    return pl.pallas_call(
        functools.partial(plan_kernel, per_pair=per_pair, depth=depth),
        in_specs=[SCALARS, near, near, near, near, ANYWHERE, near, near],
        out_shape=outs,
        scratch_shapes=[
            vmem((2, half_rows, LANES), BF16),
            vmem((options * width, width + 16), BF16),
            vmem((width + 16, width + 16), BF16),
            vmem((width, width + 16), BF16),
            vmem((width, LANES), F32),
            vmem((16, LANES), F32),
            vmem((options * width, LANES), F32),
            vmem((depth, options * width, LANES), F32),
            vmem((depth, pairs, width, two), F32),
            vmem((depth, pairs, width + 16, two), BF16),
            vmem((depth, pairs, width, two), BF16),
            vmem((depth, options * width, LANES), BF16),
            vmem(branch_w.shape, BF16),
            pltpu.SemaphoreType.DMA,
        ],
        compiler_params=params(),
        cost_estimate=cost(11),
        name="plan",
    )(section, slots, enc, s3, h2, branch_w, value_w, table)


def back(g3, lw, s2, s1, h1, w2t):
    _, side, k1 = s1.shape[:3]
    k2 = w2t.shape[0]
    inner = side // 2 - 1
    padded = (side + 2, side, k1, LANES)
    near = pl.BlockSpec(memory_space=pltpu.VMEM)
    return pl.pallas_call(
        back_kernel,
        in_specs=[near] * 6,
        out_shape=(shape_of(*padded, dtype=BF16), shape_of(k2, 256), shape_of(8, LANES)),
        scratch_shapes=[
            pltpu.VMEM((LANES, 6 * k2), BF16),
            pltpu.VMEM((inner + 2, inner, k2, LANES), BF16),
        ],
        compiler_params=params(),
        cost_estimate=cost(25),
        name="back",
    )(g3, lw, s2, s1, h1, w2t)


def first(section, frames, g1, w1t, other, after, channels, draw):
    img, _, stack, _ = frames.shape
    k1 = g1.shape[2]
    band = (STEP * 4 * COLS * channels, (STEP + 1) * NEAR * k1)
    near = pl.BlockSpec(memory_space=pltpu.VMEM)
    return pl.pallas_call(
        functools.partial(first_kernel, draw=draw),
        in_specs=[SCALARS, ANYWHERE, near, near, ANYWHERE, ANYWHERE],
        out_specs=[near, ANYWHERE, near],
        out_shape=[
            shape_of(2 * k1, LANES, dtype=BF16),
            shape_of(img, img, channels, 2 * LANES),
            shape_of(*band, dtype=BF16),
        ],
        scratch_shapes=[
            pltpu.VMEM((img, img, stack, LANES), BF16),
            pltpu.VMEM((STEP * 4 * COLS * stack, (STEP + 1) * NEAR * k1), F32),
            pltpu.VMEM((STEP * draw + 1,) + g1.shape[1:], BF16),
            pltpu.VMEM((2, 2, 4 * STEP, img, channels, LANES), F32),
            pltpu.SemaphoreType.DMA((img // 4 // STEP + 1,)),
            pltpu.SemaphoreType.DMA((2, 2)),
        ],
        compiler_params=params(),
        cost_estimate=cost(45),
        name="first",
    )(section, frames, g1, w1t, other, after)


def pixels(section, band, mine, other, after, done, start):
    img, _, channels, _ = done.shape
    steps = img // 4 // STEP - start
    near = pl.BlockSpec(memory_space=pltpu.VMEM)
    return pl.pallas_call(
        functools.partial(pixels_kernel, start=start),
        in_specs=[SCALARS, near, near, ANYWHERE, ANYWHERE, ANYWHERE],
        out_specs=[ANYWHERE, near],
        out_shape=[shape_of(*done.shape), shape_of(8, LANES)],
        scratch_shapes=[
            pltpu.VMEM((2, 2, 4 * STEP, img, channels, LANES), F32),
            pltpu.VMEM((STEP * steps + 1,) + mine.shape[1:], BF16),
            pltpu.SemaphoreType.DMA((3, 2)),
        ],
        input_output_aliases={5: 0},
        compiler_params=params(),
        cost_estimate=cost(1 + 0.9 * steps),
        name="pixels",
    )(section, band, mine, other, after, done)


def small_call(
    kernel, outs, operands, scratch=(), name=None, place=None, after=(), weight=0.3, far=False
):
    specs = [pl.BlockSpec(memory_space=pltpu.VMEM)] * len(operands)
    if place is not None:
        operands = (*place, *operands)
        specs = [pl.BlockSpec(memory_space=pltpu.SMEM)] * len(place) + specs
    return pl.pallas_call(
        kernel,
        in_specs=specs + [ANYWHERE] * len(after),
        out_specs=jax.tree.map(
            lambda _: ANYWHERE if far else pl.BlockSpec(memory_space=pltpu.VMEM), outs
        ),
        out_shape=outs,
        scratch_shapes=list(scratch),
        compiler_params=params(),
        cost_estimate=cost(weight),
        name=name,
    )(*operands, *after)


def round_up(value, step):
    return -(-value // step) * step


def swapped(value):
    return lax.ppermute(value, "section", [(0, 1), (1, 0)])


def exchanged(value, groups=None):
    return lax.all_to_all(
        value, "batch", split_axis=0, concat_axis=0, axis_index_groups=groups, tiled=True
    )


def partner(value, distance):
    count = lax.axis_size("batch")
    return lax.ppermute(value, "batch", [(b, b ^ distance) for b in range(count)])


def local(
    frames,
    destination,
    options,
    depth,
    targets,
    conv_one,
    bias_one,
    conv_two,
    bias_two,
    linear_w,
    linear_b,
    branch_w,
    branch_b,
    head_w,
    head_b,
    value_w,
    value_b,
    out_w,
    out_b,
):
    section = lax.axis_index("section").astype(jnp.int32)[None]
    peers = lax.axis_size("batch")
    frame_count = frames.shape[3]
    per_pair = frame_count // peers
    levels = options.shape[0]
    frames = stays(frames.transpose(1, 2, 0, 3))
    w1t, w2t = stays(conv_one.T), stays(conv_two.T)
    branch_w, value_w = stays(branch_w), stays(value_w)
    encoder_params = (w1t, bias_one, w2t, bias_two, linear_w, linear_b)
    planner_params = (branch_w, branch_b, head_w.T, head_b, value_w, value_b, out_w.T, out_b)
    width = linear_w.shape[1]
    big_rows = linear_w.shape[0] + (branch_w.shape[0] + 1) * width
    size = round_up(-(-big_rows // (2 * CUBE)), 16)

    tiny = (bias_one, bias_two, linear_b, branch_b, head_w.T, value_b, out_w.T)
    tiny = [stays(v if v.ndim > 1 else v[None, :]) for v in tiny]
    numbers, table = pl.pallas_call(
        numbers_kernel,
        in_specs=[pl.BlockSpec(memory_space=pltpu.VMEM)] * (6 + len(tiny)),
        out_shape=[shape_of(frame_count, LANES), shape_of(TABLE, LANES)],
        compiler_params=params(),
        cost_estimate=cost(1),
        name="numbers",
    )(
        stays(options),
        stays(depth[None, :]),
        stays(targets),
        stays(destination[None, :]),
        *tiny,
        stays(head_b[None, :]),
        out_b[None, :],
    )
    slots = exchanged(numbers.reshape(peers, per_pair, LANES)).reshape(frame_count, LANES)

    h1, s1, s2, h2, enc, s3 = encode(section, frames, w1t, w2t, stays(linear_w), table)
    keep, send_one, send_two, small, g3 = plan(
        section, slots, enc, s3, h2, branch_w, value_w, table, per_pair, levels, CUBE * size
    )
    recv = swapped(send_one), swapped(send_two)
    channels = frames.shape[2] // lax.axis_size("section")
    g1, c2, sums = back(g3, linear_w, s2, s1, h1, w2t)
    other = swapped(g1)
    g1 = held_near(g1)
    cubes = [list(range(c, c + CUBE)) for c in range(0, peers, CUBE)]
    bf16 = functools.partial(shape_of, dtype=BF16)
    pieces = small_call(
        merge_kernel,
        bf16(CUBE, size + 2 * SHORT, LANES),
        (keep, *recv, small, c2, sums),
        [
            pltpu.VMEM((CUBE * SHORT, LANES), F32),
            pltpu.VMEM((CUBE, size + 2 * SHORT, LANES), BF16),
            pltpu.SemaphoreType.DMA((CUBE,)),
        ],
        name="merge",
        far=True,
        weight=30,
    )
    got = exchanged(pieces, cubes)
    c1, frames_grad, band = first(section, frames, g1, w1t, other, pieces, channels, DRAW)
    piece = bf16(size + 2 * SHORT + c1.shape[0], LANES)
    keep = small_call(cube_kernel, piece, (got, c1), name="cube")
    distance = CUBE
    while distance < peers:
        recv = partner(keep, distance)
        if distance == CUBE:
            frames_grad, token = pixels(section, band, g1, other, keep, frames_grad, DRAW)
        distance *= 2
        keep = small_call(add_kernel, piece, (keep, recv), name="add", after=(token,))
    parts = [keep] + [partner(keep, k) for k in range(1, CUBE)]
    place = (lax.axis_index("batch").astype(jnp.int32)[None],)
    got = small_call(
        relay_kernel,
        [bf16(CUBE // 2, *piece.shape)] * 2,
        parts,
        [pltpu.VMEM((CUBE, *piece.shape), BF16)],
        name="relay",
        place=place,
    )
    got_other = [swapped(v) for v in got]
    shapes = [p.shape for p in encoder_params + planner_params]
    near = pl.BlockSpec(memory_space=pltpu.VMEM)
    flat = [shape_of(*(v if len(v) > 1 else (1,) + v)) for v in [(1, 1)] + shapes]
    large = [flat[k] for k in (5, 7, 11)]
    staged = [
        pltpu.VMEM((CUBE * size, LANES), F32),
        pltpu.VMEM(branch_w.shape, F32),
    ]
    little = [v for k, v in enumerate(flat) if k not in (5, 7, 11)]
    sems = pltpu.SemaphoreType.DMA((CUBE + len(little),))
    begun = pl.pallas_call(
        own_kernel,
        in_specs=[SCALARS, near, near],
        out_specs=[ANYWHERE] * 3,
        out_shape=large,
        scratch_shapes=[*staged, sems],
        compiler_params=params(),
        cost_estimate=cost(1),
        name="own",
    )(section, *got)
    ends = pl.pallas_call(
        unpack_kernel,
        in_specs=[SCALARS] + [near] * 4 + [ANYWHERE] * 3,
        out_specs=[ANYWHERE] * (3 + len(little)),
        out_shape=large + little,
        scratch_shapes=[pltpu.VMEM(v.shape, F32) for v in little]
        + [*staged, pltpu.VMEM((CUBE * SHORT, LANES), F32), sems],
        input_output_aliases={5: 0, 6: 1, 7: 2},
        compiler_params=params(),
        cost_estimate=cost(1.5),
        name="unpack",
    )(section, *got, *got_other, *begun)
    rest = list(ends[3:])
    for k, at in enumerate((5, 7, 11)):
        rest.insert(at, ends[k])
    rest = [v.reshape(s) for v, s in zip(rest, [()] + shapes)]
    for at in (1, 3, 9, 13):
        rest[at] = rest[at].T
    return (rest[0], frames_grad.transpose(2, 0, 1, 3), *rest[1:])


def solution(mesh):
    placed = (
        P(None, None, None, "batch"),
        P("batch"),
        P(None, "batch"),
        P("batch"),
        P(None, None, "batch"),
    ) + (P(),) * 14
    return jax.shard_map(
        local,
        mesh=mesh,
        in_specs=placed,
        out_specs=(P(), P("section", None, None, "batch")) + (P(),) * 14,
        check_vma=False,
    )
```

```python
import functools
import math

import jax
import jax.numpy as jnp
from jax import lax
from jax.experimental import pallas as pl
from jax.experimental.pallas import tpu as pltpu
from jax.sharding import PartitionSpec as P

BF16 = jnp.bfloat16
F32 = jnp.float32
EXACT = lax.Precision.HIGHEST
LANES = 128
VMEM_BYTES = 32 * 1024 * 1024
TILE = 16
REACH = 5
STEP = 3
COLS = 12
NEAR = 4
AT_VB, AT_OW, AT_HW, AT_LB, AT_SCALARS, AT_B1, AT_B2, AT_DEST = (
    slice(18, 19),
    slice(19, 20),
    slice(20, 22),
    slice(22, 23),
    slice(23, 24),
    slice(24, 25),
    slice(25, 26),
    26,
)
TABLE = 32
CUBE = 8
DRAW = 3
DRAW_ACROSS = 3
SHORT = 16


def dot(a, b, precision=None):
    return jnp.dot(a, b, preferred_element_type=F32, precision=precision)


def dot_rows(a, b, precision=None):
    return lax.dot_general(
        a, b, (((0,), (0,)), ((), ())), preferred_element_type=F32, precision=precision
    )


def dot_lanes(a, b, precision=None):
    return lax.dot_general(
        a, b, (((1,), (1,)), ((), ())), preferred_element_type=F32, precision=precision
    )


def iota(shape, axis):
    return lax.broadcasted_iota(jnp.int32, shape, axis)


def column(row):
    n = row.shape[1]
    wide = jnp.broadcast_to(row, (n, n))
    return jnp.sum(jnp.where(iota((n, n), 0) == iota((n, n), 1), wide, 0.0), axis=1, keepdims=True)


def row_of(col):
    n = col.shape[0]
    wide = jnp.broadcast_to(col, (n, n))
    return jnp.sum(jnp.where(iota((n, n), 0) == iota((n, n), 1), wide, 0.0), axis=0, keepdims=True)


def soft(x):
    t = jnp.tanh(0.5 * x)
    return jnp.maximum(x, 0.0) - jnp.log(0.5 + 0.5 * jnp.abs(t)), 0.5 + 0.5 * t


def silu_pair(y):
    t = jnp.tanh(y)
    m = y * t
    return y + m, (1.0 + t) + (y - m * t)


def pixel_order(w1t):
    tap, pix = iota((256, 256), 0), iota((256, 256), 1)
    moves = ((tap >> 6) == (pix & 3)) & ((tap & 63) == (pix >> 2))
    return dot(w1t, moves.astype(F32).astype(BF16))


def frame_copies(section, far, here, sems):
    lanes = pl.ds(pl.multiple_of(section[0] * LANES, LANES), LANES)
    size = 4 * STEP

    def copy(g):
        rows = pl.ds(pl.multiple_of(g * size, size), size)
        return pltpu.make_async_copy(far.at[rows, :, :, lanes], here.at[rows], sems.at[g])

    return copy


def tile_rows(frames, row, j, cols):
    img, _, channels, _ = frames.shape
    flat = frames.reshape(img, img * channels, LANES)
    size = cols * channels
    end = min((j + 1) * size, img * channels)
    part = flat[pl.ds(row, 4), j * size : end, :]
    return part.reshape(4 * (end - j * size), LANES)


def encode_kernel(
    section,
    frames_far,
    w1t,
    w2t,
    lw_far,
    table,
    h1_far,
    s1_far,
    s2_far,
    h2,
    enc,
    s3,
    frames,
    lw,
    h1,
    s1,
    s2,
    band,
    edge,
    band2,
    bias1,
    bias2,
    held,
    held2,
    sems,
):
    blocks, side = h1.shape[:2]
    steps = blocks // STEP
    tiles = frames.shape[1] // TILE
    k1, k2 = w1t.shape[0], w2t.shape[0]
    reach_rows = REACH * k1
    arrives = frame_copies(section, frames_far, frames, sems.at[0])
    for g in range(steps):
        arrives(g).start()
    last_copies = [
        pltpu.make_async_copy(lw_far, lw, sems.at[3, 0]),
        pltpu.make_async_copy(s2, s2_far, sems.at[3, 1]),
    ]
    last_copies[0].start()

    def leaves(g):
        rows = pl.ds(g * STEP, STEP)
        return [
            pltpu.make_async_copy(h1.at[rows], h1_far.at[rows], sems.at[1, g]),
            pltpu.make_async_copy(s1.at[rows], s1_far.at[rows], sems.at[2, g]),
        ]

    inner = side // 2 - 1
    row_len = inner * k2
    two = 2 * k2 * 3

    def prepare():
        taps = pixel_order(w1t[...])
        edges = []
        for half in range(2):
            lines = [taps[:, 32 * (4 * half + u) : 32 * (4 * half + u + 1)] for u in range(4)]
            for place in range(REACH):
                pieces = []
                for line in lines:
                    start = 16 * (place - 1)
                    cut = line[:, max(0, -start) : min(32, 64 - start)]
                    start = max(start, 0)
                    pieces += [jnp.zeros((k1, start), F32)] if start else []
                    pieces.append(cut)
                    rest = 64 - start - cut.shape[1]
                    pieces += [jnp.zeros((k1, rest), F32)] if rest else []
                at = half * reach_rows + place * k1
                band[at : at + k1, :] = jnp.concatenate(pieces, axis=1).astype(BF16)
            edges.append(jnp.concatenate([line[:, 16:] for line in lines], axis=1))
        edge[...] = jnp.concatenate(edges, axis=0).astype(BF16)
        taps = w2t[...].astype(F32)
        blank = jnp.zeros((k2, 2 * k1), F32)
        for half in range(2):
            lines = [taps[:, 4 * k1 * (2 * half + u) : 4 * k1 * (2 * half + u + 1)] for u in range(2)]
            pieces = (
                [v for line in lines for v in (line[:, 2 * k1 :], blank)],
                lines,
                [v for line in lines for v in (blank, line[:, : 2 * k1])],
            )
            for place in range(3):
                at = (half * 3 + place) * k2
                band2[at : at + k2, :] = jnp.concatenate(pieces[place], axis=1).astype(BF16)
        bias1[...] = jnp.broadcast_to(column(table[AT_B1, 0:k1]), bias1.shape)
        bias2[...] = jnp.broadcast_to(column(table[AT_B2, 0:k2]), bias2.shape)
        held[...] = jnp.zeros_like(held)
        held2[...] = jnp.zeros_like(held2)
        h1[...] = jnp.zeros_like(h1)

    def added(sums, x, value):
        sums[x] = sums[x] + value if x in sums else value

    def second_matmul(b):
        tiles = [
            h1[pl.ds(2 * b + 1, 2), 4 * j : 4 * j + 4].reshape(LANES, LANES)
            for j in range(side // 4)
        ]
        return dot(band2[...], jnp.concatenate(tiles, axis=1))

    def second_rows(b, got):
        low, high = {}, {}
        for j in range(side // 4):
            for place in range(3):
                x = 2 * j - 1 + place
                if 0 <= x < inner:
                    span = slice(j * LANES, (j + 1) * LANES)
                    at = place * k2
                    added(low, x, got[at : at + k2, span])
                    added(high, x, got[two // 2 + at : two // 2 + at + k2, span])
        row = jnp.maximum(b - 1, 0) * row_len
        for x in range(inner):
            value, slope = soft(held2[x] + high[x] + bias2[...])
            held2[x] = low[x]
            at = pl.ds(pl.multiple_of(row + x * k2, k2), k2)
            h2[at, :] = value.astype(BF16)
            s2[at, :] = slope.astype(BF16)

    def one_step(g, carry):
        def row(r):
            return pl.multiple_of(4 * (STEP * g + r), 4)

        arrives(g).wait()
        lows, highs = [{} for _ in range(STEP)], [{} for _ in range(STEP)]

        def place_tile(r, j, got):
            for place in range(REACH):
                x = 4 * j - 1 + place
                if 0 <= x < side:
                    at = place * k1
                    added(lows[r], x, got[at : at + k1])
                    added(highs[r], x, got[reach_rows + at : reach_rows + at + k1])

        def finish(r, xs):
            for x in xs:
                value, slope = soft(held[x] + highs[r][x] + bias1[...])
                held[x] = lows[r][x]
                h1[STEP * g + r, x] = value.astype(BF16)
                s1[STEP * g + r, x] = slope.astype(BF16)

        pair = jnp.maximum(g - 1, 0)
        units = [(lambda: second_matmul(pair), lambda got: second_rows(pair, got))]

        def edges():
            parts = [tile_rows(frames, row(r), tiles, TILE) for r in range(STEP)]
            return dot(edge[...], jnp.concatenate(parts, axis=1))

        def place_edges(got):
            for r in range(STEP):
                added(lows[r], side - 1, got[:k1, r * LANES : (r + 1) * LANES])
                added(highs[r], side - 1, got[k1:, r * LANES : (r + 1) * LANES])

        units.append((edges, place_edges))

        def full(spots):
            parts = [tile_rows(frames, row(r), j, TILE) for r, j in spots]
            return dot(band[...], jnp.concatenate(parts, axis=1))

        def place_full(got, spots, ready):
            for i, (r, j) in enumerate(spots):
                place_tile(r, j, got[:, i * LANES : (i + 1) * LANES])
            if ready:
                finish(*ready)

        for r in range(STEP):
            if r % 2 == 0:
                spots = [(k, tiles - 1) for k in (r, r + 1) if k < STEP]
                units.append(
                    (
                        functools.partial(full, spots),
                        functools.partial(place_full, spots=spots, ready=None),
                    )
                )
            done = 0
            for j in range(0, tiles - 1, 2):
                spots = [(r, j), (r, j + 1)]
                ready = side if j + 2 == tiles - 1 else 4 * j + 7
                units.append(
                    (
                        functools.partial(full, spots),
                        functools.partial(place_full, spots=spots, ready=(r, range(done, ready))),
                    )
                )
                done = ready
        waiting = None
        for issue, take in units:
            got = issue()
            if waiting is not None:
                waiting[0](waiting[1])
            waiting = (take, got)
        waiting[0](waiting[1])
        for copy in leaves(g):
            copy.start()
        return carry

    prepare()
    lax.fori_loop(0, steps, one_step, 0)
    last_copies[0].wait()
    early = (steps - 2) * row_len
    waiting = None
    for b in range(steps - 1, side // 2):
        got = second_matmul(b)
        if waiting is None:
            total = dot_rows(lw[0:early, :], h2[0:early, :]) + column(table[AT_LB, :])
        else:
            second_rows(*waiting)
        waiting = (b, got)
    second_rows(*waiting)
    for copy in last_copies[1:]:
        copy.start()
    value, slope = soft(total + dot_rows(lw[early:, :], h2[early:, :]))
    enc[...] = value.astype(BF16)
    s3[...] = slope
    for g in range(steps):
        for copy in leaves(g):
            copy.wait()
    for copy in last_copies[1:]:
        copy.wait()


def three_parts(row):
    high = row.astype(BF16).astype(F32)
    middle = (row - high).astype(BF16).astype(F32)
    return jnp.concatenate([high, middle, row - high - middle], axis=0)


def with_ones(value):
    return jnp.concatenate([value, ones_rows(value.shape[1])], axis=0)


def ones_rows(lanes):
    return (iota((16, lanes), 0) < 3).astype(F32).astype(BF16)


def plan_kernel(
    section,
    slots,
    enc,
    s3,
    h2,
    branch_far,
    value_w,
    table,
    keep,
    send_one,
    send_two,
    small,
    g3,
    parts,
    bwt,
    vht,
    vhw,
    ow,
    mine,
    pre,
    dbr,
    dval,
    low,
    hid,
    gb,
    branch_w,
    sem,
    *,
    per_pair,
    depth,
):
    width = enc.shape[0]
    options = branch_w.shape[0]
    pairs = options // 2
    two = 2 * width
    sec = section[0]
    branch_copy = pltpu.make_async_copy(branch_far, branch_w, sem)
    branch_copy.start()

    count = slots.shape[0]
    dest = jnp.concatenate(
        [table[AT_DEST + k : AT_DEST + k + 1, :] for k in range(count // LANES)], axis=1
    )
    own = jnp.where(sec == 0, dest[:, :LANES], dest[:, LANES:])
    others = jnp.transpose(jnp.broadcast_to(dest, (LANES, count)))
    index = iota((count, LANES), 1) + sec * LANES
    earlier = (others == own) & (iota((count, LANES), 0) < index)
    rank = jnp.sum(earlier.astype(F32), axis=0, keepdims=True)
    bucket = own * float(per_pair) + rank
    chosen = (iota((count, LANES), 0).astype(F32) == bucket).astype(F32).astype(BF16)
    numbers = slots[:, : mine.shape[0]]
    high = numbers.astype(BF16)
    middle = (numbers - high.astype(F32)).astype(BF16)
    rest = (numbers - high.astype(F32) - middle.astype(F32)).astype(BF16)
    mine[...] = sum(dot_rows(v, chosen) for v in (rest, middle, high))

    pad = jnp.zeros((13, width), F32)
    branch_copy.wait()
    for o in range(options):
        rows = [branch_w[o].astype(F32), three_parts(table[o : o + 1, :]), pad]
        bwt[o * width : (o + 1) * width, :] = jnp.transpose(
            0.5 * jnp.concatenate(rows, axis=0)
        ).astype(BF16)
    scalars = table[AT_SCALARS, :]
    head_w = table[AT_HW, :]
    rows = [value_w[...].astype(F32), three_parts(table[AT_VB, :]), pad]
    vht[0:width, :] = jnp.transpose(0.5 * jnp.concatenate(rows, axis=0)).astype(BF16)
    vht[width:, :] = jnp.zeros((16, width + 16), BF16)
    lane = iota((1, 16), 1)
    for k in range(2):
        bias = three_parts(jnp.broadcast_to(scalars[:, 1 + k : 2 + k], (1, 16)))
        bias = sum(jnp.where(lane == j, bias[j : j + 1], 0.0) for j in range(3))
        vht[width + k : width + k + 1, 0:width] = head_w[k : k + 1].astype(BF16)
        vht[width + k : width + k + 1, width:] = bias.astype(BF16)
    vhw[:, 0:width] = (0.5 * value_w[...].astype(F32)).astype(BF16)
    vhw[:, width:] = jnp.transpose(
        0.5 * jnp.concatenate([head_w, jnp.zeros((14, width), F32)], axis=0)
    ).astype(BF16)
    ow[...] = jnp.broadcast_to(column(table[AT_OW, :]), (width, LANES))
    wide_ow = jnp.concatenate([ow[...], ow[...]], axis=1)
    half_ow = 0.5 * wide_ow

    labels = iota((options, LANES), 0).astype(F32)
    state = enc[...].astype(F32)
    rounded_all, saved = [], []
    group = 3
    for level in range(depth):
        picked = labels == mine[level : level + 1, :]
        rounded = state.astype(BF16)
        rounded_all.append(rounded)
        met = with_ones(rounded)

        def branches(first):
            at = slice(first * two, (first + group) * two)
            pre[at, :] = dot(bwt[at, :], met)

        branches(0)
        following = state
        reward, discount, value = [], [], []

        def value_part(t, got):
            act, slope = silu_pair(got[:width])
            dval[level, t] = slope
            hidden = act.astype(BF16)
            hid[level, t] = hidden
            worth = jnp.sum(hidden.astype(F32) * wide_ow, axis=0, keepdims=True)
            for k in range(2):
                span = slice(k * LANES, (k + 1) * LANES)
                value.append(worth[:, span])
                reward.append(got[width : width + 1, span])
                discount.append(got[width + 1 : width + 2, span])

        waiting = None
        for first in range(0, pairs, group):
            if first + group < pairs:
                branches(first + group)
            boths = []
            for t in range(first, first + group):
                at = slice(t * two, (t + 1) * two)
                act, slope = silu_pair(pre[at, :])
                dbr[level, at, :] = slope
                left = state + act[:width]
                right = state + act[width:]
                following = jnp.where(picked[2 * t : 2 * t + 1], left, following)
                following = jnp.where(picked[2 * t + 1 : 2 * t + 2], right, following)
                both = with_ones(
                    jnp.concatenate([left.astype(BF16), right.astype(BF16)], axis=1)
                )
                low[level, t] = both
                boths.append(both)
            got = dot(vht[...], jnp.concatenate(boths, axis=1))
            if waiting is not None:
                for k in range(group):
                    value_part(waiting[0] + k, waiting[1][:, k * two : (k + 1) * two])
            waiting = (first, got)
        for k in range(group):
            value_part(waiting[0] + k, waiting[1][:, k * two : (k + 1) * two])
        reward = jnp.concatenate(reward, axis=0)
        discount = jax.nn.sigmoid(jnp.concatenate(discount, axis=0))
        value = jnp.concatenate(value, axis=0) + scalars[:, 3:4]
        quality = reward + discount * value
        top = jnp.max(quality, axis=0, keepdims=True)
        shifted = jnp.exp(quality - top)
        total = jnp.sum(shifted, axis=0, keepdims=True)
        live = (mine[depth : depth + 1, :] > level).astype(F32)
        chosen = picked.astype(F32)

        def target(kind):
            at = depth + 1 + kind * depth + level
            return mine[at : at + 1, :]

        reward_gap = live * (jnp.sum(chosen * reward, axis=0, keepdims=True) - target(0))
        discount_gap = live * (jnp.sum(chosen * discount, axis=0, keepdims=True) - target(1))
        plan_gap = live * (top + jnp.log(total) - target(2))
        grad_quality = plan_gap * (shifted / total)
        head_two = (chosen * discount_gap + grad_quality * value) * discount * (1.0 - discount)
        saved.append(
            (
                picked,
                (chosen * reward_gap + grad_quality).astype(BF16).astype(F32),
                head_two.astype(BF16).astype(F32),
                (grad_quality * discount).astype(BF16).astype(F32),
                reward_gap * reward_gap + discount_gap * discount_gap + plan_gap * plan_gap,
            )
        )
        state = following

    out_sum = jnp.zeros((16, width), F32)
    value_sum = jnp.zeros((width + 16, width + 16), F32)
    grad_next = None
    line = iota((16, two), 0)
    for level in reversed(range(depth)):
        picked, head_one, head_two, grad_value, _ = saved[level]
        upward = jnp.zeros((width, LANES), F32)

        def branch_part(t, moved):
            at = slice(t * two, (t + 1) * two)
            left, right = moved[:, :LANES], moved[:, LANES:]
            if grad_next is not None:
                left = left + jnp.where(picked[2 * t : 2 * t + 1], grad_next, 0.0)
                right = right + jnp.where(picked[2 * t + 1 : 2 * t + 2], grad_next, 0.0)
            grad_branch = jnp.concatenate([left, right], axis=0) * dbr[level, at, :]
            grad_branch = grad_branch.astype(BF16)
            gb[level, at, :] = grad_branch
            return left + right

        def group_part(first, moved):
            parts = [
                branch_part(first + k, moved[:, k * two : (k + 1) * two]) for k in range(group)
            ]
            at = slice(first * two, (first + group) * two)
            weights = [branch_w[o] for o in range(2 * first, 2 * (first + group))]
            return sum(parts), dot(jnp.concatenate(weights, axis=1), gb[level, at, :])

        waiting = None
        for first in range(0, pairs, group):
            stack = []
            for t in range(first, first + group):

                def across(rows):
                    return jnp.concatenate(
                        [rows[2 * t : 2 * t + 1], rows[2 * t + 1 : 2 * t + 2]], axis=1
                    )

                worth = across(grad_value)
                grad_pre = (worth * half_ow * dval[level, t]).astype(BF16)
                heads = jnp.where(line == 0, across(head_one), 0.0)
                heads = jnp.where(line == 1, across(head_two), heads)
                heads = jnp.where(line == 2, worth, heads)
                heads = heads.astype(BF16)
                out_sum = out_sum + dot_lanes(heads, hid[level, t])
                stack.append(jnp.concatenate([grad_pre, heads], axis=0))
            stack = jnp.concatenate(stack, axis=1)
            moved = dot(vhw[...], stack)
            if waiting is not None:
                one, other = group_part(*waiting)
                upward = upward + (one + 0.5 * other)
            waiting = (first, moved)
            lows = jnp.concatenate([low[level, first + k] for k in range(group)], axis=1)
            value_sum = value_sum + dot_lanes(stack, lows)
        one, other = group_part(*waiting)
        grad_next = upward + (one + 0.5 * other)

    linear_rows = h2.shape[0]
    half = (linear_rows + options * width + width) // 2
    rest = linear_rows - half
    rounded = with_ones(jnp.concatenate(rounded_all, axis=1))
    small[...] = jnp.zeros_like(small)
    if half < keep.shape[0]:
        for k in range(2):
            parts[k, half:, :] = jnp.zeros((keep.shape[0] - half, LANES), BF16)
    for t in range(pairs):
        at = slice(t * two, (t + 1) * two)
        grads = jnp.concatenate([gb[level, at, :] for level in range(depth)], axis=1)
        got = dot_lanes(rounded, grads)
        for k in range(2):
            o = 2 * t + k
            span = slice(k * width, (k + 1) * width)
            rows = slice(rest + o * width, rest + (o + 1) * width)
            parts[1 - sec, rows, :] = got[:width, span].astype(BF16)
            small[o : o + 1, :] = got[width : width + 1, span]
    after = rest + options * width
    parts[1 - sec, after : after + width, :] = jnp.transpose(value_sum[:width, :width]).astype(BF16)

    grad_three = ((2.0 * grad_next).astype(BF16).astype(F32) * s3[...]).astype(BF16)
    g3[...] = grad_three
    chunk = linear_rows // 9
    for i in range(8):
        at = slice(i * chunk, (i + 1) * chunk)
        parts[sec, at, :] = dot_lanes(h2[at, :], grad_three).astype(BF16)
    last = dot_lanes(h2[8 * chunk :, :], grad_three).astype(BF16)
    parts[sec, 8 * chunk : half, :] = last[: half - 8 * chunk]
    parts[1 - sec, 0:rest, :] = last[half - 8 * chunk :]
    keep[...] = parts[0]
    send_one[...] = parts[1, : send_one.shape[0]]
    send_two[...] = parts[1, send_one.shape[0] :]

    small[AT_VB, :] = row_of(value_sum[:width, width : width + 1])
    small[AT_OW, :] = out_sum[2:3]
    small[AT_HW, :] = value_sum[width : width + 2, :width]
    small[AT_LB, :] = row_of(jnp.sum(grad_three.astype(F32), axis=1, keepdims=True))
    loss = 0.5 * jnp.sum(sum(kept[4] for kept in saved), axis=1, keepdims=True)
    ends = [loss] + [value_sum[width + k : width + k + 1, width : width + 1] for k in range(3)]
    lane = iota((1, LANES), 1)
    line = jnp.zeros((1, LANES), F32)
    for k, end in enumerate(ends):
        line = jnp.where(lane == k, end, line)
    small[AT_SCALARS, :] = line


def back_kernel(g3, lw, s2, s1, h1, w2t, g1, c2, sums, t2, g2):
    side, k1 = s1.shape[1], s1.shape[2]
    k2 = w2t.shape[0]
    inner = side // 2 - 1
    row_len = inner * k2
    tap, pix = iota((LANES, 256), 1), iota((LANES, 256), 0)
    for yrel in range(2):
        for p in range(3):
            hit = (
                ((tap & 15) == (pix & 15))
                & ((tap >> 6) == (pix >> 6) + 2 * (1 - yrel))
                & (((tap >> 4) & 3) == ((pix >> 4) & 3) + 2 - 2 * p)
            )
            at = (yrel * 3 + p) * k2
            t2[:, at : at + k2] = dot_lanes(hit.astype(F32).astype(BF16), w2t[...]).astype(BF16)
    g2[0] = jnp.zeros(g2.shape[1:], BF16)
    g2[inner + 1] = jnp.zeros(g2.shape[1:], BF16)
    g1[0] = jnp.zeros(g1.shape[1:], BF16)
    g1[side + 1] = jnp.zeros(g1.shape[1:], BF16)
    zero = jnp.zeros((k2, LANES), BF16)
    total_one = jnp.zeros((k1, LANES), F32)
    total_two = jnp.zeros((k2, LANES), F32)
    for y in range(inner):
        at = slice(y * row_len, (y + 1) * row_len)
        grad = dot(lw[at, :], g3[...]) * s2[at, :].astype(F32)
        grad = grad.astype(BF16).reshape(inner, k2, LANES)
        g2[y + 1] = grad
        total_two = total_two + jnp.sum(grad.astype(F32), axis=0)
    reach, cols = 5, 8
    total = jnp.zeros((2 * reach * k2, 2 * cols * k1), F32)
    grads, tiles = [], []
    for b in range(side // 2):
        cut = []
        for j in range(side // 4):
            pieces = []
            for yrel in range(2):
                for p in range(3):
                    x = 2 * j - 1 + p
                    pieces.append(g2[b + yrel, x] if 0 <= x < inner else zero)
            cut.append(jnp.concatenate(pieces, axis=0))
        got = dot(t2[...], jnp.concatenate(cut, axis=1))
        for u in range(2):
            for j in range(side // 4):
                part = got[u * 64 : (u + 1) * 64, j * LANES : (j + 1) * LANES]
                slope = s1[2 * b + u + 1, 4 * j : 4 * j + 4].astype(F32)
                grad = (part.reshape(4, k1, LANES) * slope).astype(BF16)
                g1[2 * b + u + 1, 4 * j : 4 * j + 4] = grad
                total_one = total_one + jnp.sum(grad.astype(F32), axis=0)
        for j in range(-(-side // cols)):
            end = min((j + 1) * cols, side)
            tile = h1[2 * b + 1 : 2 * b + 3, j * cols : end]
            if end < (j + 1) * cols:
                rest = jnp.zeros((2, (j + 1) * cols - end, k1, LANES), BF16)
                tile = jnp.concatenate([tile, rest], axis=1)
            tiles.append(tile.reshape(2 * cols * k1, LANES))
            pieces = []
            for half in range(2):
                for p in range(reach):
                    x = 4 * j - 1 + p
                    pieces.append(g2[b + 1 - half, x] if 0 <= x < inner else zero)
            grads.append(jnp.concatenate(pieces, axis=0))
        if b % 2:
            total = total + dot_lanes(
                jnp.concatenate(grads, axis=1), jnp.concatenate(tiles, axis=1)
            )
            grads, tiles = [], []
    line = 4 * k1
    for half in range(2):
        for u in range(2):
            tap_row = jnp.zeros((k2, line), F32)
            for p in range(reach):
                at = (half * reach + p) * k2
                part = total[at : at + k2, u * 2 * line : (u + 1) * 2 * line]
                start = 2 * k1 * (p - 1)
                piece = part[:, max(start, 0) : min(start + line, 2 * line)]
                if start < 0:
                    piece = jnp.concatenate([jnp.zeros((k2, -start), F32), piece], axis=1)
                if start + line > 2 * line:
                    rest = jnp.zeros((k2, start - line), F32)
                    piece = jnp.concatenate([piece, rest], axis=1)
                tap_row = tap_row + piece
            at = (2 * half + u) * line
            c2[:, at : at + line] = tap_row
    sums[...] = jnp.zeros_like(sums)
    sums[0:1, 0:k1] = row_of(jnp.sum(total_one, axis=1, keepdims=True))
    sums[1:2, 0:k2] = row_of(jnp.sum(total_two, axis=1, keepdims=True))


def pixel_band(sec, w1t, channels):
    k1 = w1t.shape[0]
    rows = 64 * channels
    row, tap = iota((rows, 256), 0), iota((rows, 256), 1)
    moves = ((tap >> 6) == row % channels + sec * channels) & ((tap & 63) == row // channels)
    taps = dot_lanes(moves.astype(F32).astype(BF16), w1t)
    line, span = COLS * channels, 8 * channels
    blocks = {}
    for half in range(2):
        for p in range(NEAR):
            pieces = []
            for u in range(4):
                at = (4 * half + u) * span
                start = 4 * (p - 1) * channels
                cut = taps[at + max(0, -start) : at + min(span, line - start)]
                start = max(start, 0)
                pieces += [jnp.zeros((start, k1), F32)] if start else []
                pieces.append(cut)
                rest = line - start - cut.shape[0]
                pieces += [jnp.zeros((rest, k1), F32)] if rest else []
            blocks[half, p] = jnp.concatenate(pieces, axis=0)
    zero = jnp.zeros((4 * line, k1), F32)
    lines = []
    for r in range(STEP):
        cols = [
            blocks.get((r + 1 - yrel, p), zero) for yrel in range(STEP + 1) for p in range(NEAR)
        ]
        lines.append(jnp.concatenate(cols, axis=1))
    return jnp.concatenate(lines, axis=0).astype(BF16)


def first_kernel(
    section,
    frames_far,
    g1,
    w1t,
    other_far,
    after,
    c1,
    out,
    band,
    frames,
    acc,
    other,
    held,
    sems,
    draw_sems,
    *,
    draw,
):
    side, k1 = g1.shape[1], g1.shape[2]
    img, _, channels, _ = frames.shape
    steps = img // 4 // STEP
    arrives = frame_copies(section, frames_far, frames, sems)
    for g in range(steps):
        arrives(g).start()
    other_copy = pltpu.make_async_copy(
        other_far.at[0 : STEP * draw + 1], other, sems.at[steps]
    )
    other_copy.start()
    acc[...] = jnp.zeros_like(acc)
    zero = jnp.zeros((k1, LANES), BF16)

    def one_step(g, carry):
        arrives(g).wait()
        pixels, grads = [], []
        for j in range(img // COLS):
            rows = [pl.multiple_of(4 * (STEP * g + r), 4) for r in range(STEP)]
            pixels.append(
                jnp.concatenate([tile_rows(frames, row, j, COLS) for row in rows], axis=0)
            )
            pieces = []
            for yrel in range(STEP + 1):
                for p in range(NEAR):
                    x = 3 * j - 1 + p
                    pieces.append(g1[STEP * g + yrel, x] if 0 <= x < side else zero)
            grads.append(jnp.concatenate(pieces, axis=0))
        acc[...] += dot_lanes(jnp.concatenate(pixels, axis=1), jnp.concatenate(grads, axis=1))
        return carry

    lax.fori_loop(0, steps, one_step, 0)
    band[...] = pixel_band(section[0], w1t[...], out.shape[2])
    other_copy.wait()
    finish = draw_steps(section, band, g1, 0, other, 0, out, held, draw_sems, 0, draw)
    fold_first(acc, c1, channels, k1)
    finish()


def fold_first(acc, c1, channels, k1):
    line = COLS * channels
    step = 4 * channels
    taps = []
    for half in range(2):
        total = sum(
            acc[r * 4 * line : (r + 1) * 4 * line, :][
                :, (r + 1 - half) * NEAR * k1 : (r + 2 - half) * NEAR * k1
            ]
            for r in range(STEP)
        )
        for u in range(4):
            part = total[u * line : (u + 1) * line]
            cols = [part[:, p * k1 : (p + 1) * k1] for p in range(NEAR)]
            taps.append(cols[1][0:step] + cols[2][step : 2 * step] + cols[3][2 * step :])
            taps.append(cols[0][0:step] + cols[1][step : 2 * step] + cols[2][2 * step :])
    row, col = iota((256, 256), 0), iota((256, 256), 1)
    moves = ((row & 3) == (col >> 6)) & ((row >> 2) == (col & 63))
    grad = dot_rows(jnp.concatenate(taps, axis=0), moves.astype(F32), EXACT)
    for half in range(2):
        c1[half * k1 : (half + 1) * k1, :] = grad[:, half * LANES : (half + 1) * LANES].astype(BF16)


def draw_steps(section, band, mine, mine_at, other, other_at, out, held, sems, start, steps):
    side, k1 = mine.shape[1], mine.shape[2]
    img, channels = out.shape[1], out.shape[2]
    sec = section[0]
    line = COLS * channels
    flat = held.reshape(2, 2, 4 * STEP, img * channels, LANES)

    def writes(g):
        rows = slice(4 * STEP * (start + g), 4 * STEP * (start + g + 1))
        places = (sec * LANES, (1 - sec) * LANES)
        return [
            pltpu.make_async_copy(
                held.at[g % 2, k],
                out.at[rows, :, :, pl.ds(pl.multiple_of(places[k], LANES), LANES)],
                sems.at[g % 2, k],
            )
            for k in range(2)
        ]

    zero = jnp.zeros((k1, 2 * LANES), BF16)
    for g in range(steps):
        if g >= 2:
            for copy in writes(g - 2):
                copy.wait()
        for j in range(img // COLS):
            pieces = []
            for yrel in range(STEP + 1):
                for p in range(NEAR):
                    x, y = 3 * j - 1 + p, STEP * (start + g) + yrel
                    if 0 <= x < side:
                        pair = [mine[y - mine_at, x], other[y - other_at, x]]
                        pieces.append(jnp.concatenate(pair, axis=1))
                    else:
                        pieces.append(zero)
            got = dot(band[...], jnp.concatenate(pieces, axis=0))
            for k in range(4 * STEP):
                at = slice(k * line, (k + 1) * line)
                span = slice(j * line, (j + 1) * line)
                flat[g % 2, 0, k, span, :] = got[at, :LANES]
                flat[g % 2, 1, k, span, :] = got[at, LANES:]
        for copy in writes(g):
            copy.start()

    def finish():
        for g in range(max(steps - 2, 0), steps):
            for copy in writes(g):
                copy.wait()

    return finish


def pixels_kernel(section, band, mine, other_far, after, done, out, token, held, other, sems, *, start):
    steps = other.shape[0] // STEP
    fetch = pltpu.make_async_copy(
        other_far.at[STEP * start : STEP * (start + steps) + 1], other, sems.at[2, 0]
    )
    fetch.start()
    token[...] = jnp.zeros_like(token)
    fetch.wait()
    draw_steps(
        section, band, mine, 0, other, STEP * start, out, held, sems, start, steps
    )()


def two_parts(value):
    high = value.astype(BF16).astype(F32)
    return jnp.concatenate([high, value - high], axis=0).astype(BF16)


def one_part(pair):
    rows = pair.shape[0] // 2
    pair = pair.astype(F32)
    return pair[:rows] + pair[rows:]


def merge_kernel(keep, recv_one, recv_two, small, c2, sums, out_far, lines, out, sems):
    members = out.shape[0]
    size = keep.shape[0] // members
    k2 = c2.shape[0]
    lines[...] = jnp.zeros_like(lines)
    at = small.shape[0]
    lines[0:at, :] = small[...]
    for half in range(2):
        lines[at : at + k2, :] = c2[:, half * LANES : (half + 1) * LANES]
        at += k2
    lines[at : at + sums.shape[0], :] = sums[...]
    for k in range(members):
        at = slice(k * size, (k + 1) * size)
        recv, here = recv_one, k
        if k >= members // 2:
            recv, here = recv_two, k - members // 2
        got = recv[here * size : (here + 1) * size, :]
        out[k, 0:size, :] = (keep[at, :].astype(F32) + got.astype(F32)).astype(BF16)
        out[k, size:, :] = two_parts(lines[k * SHORT : (k + 1) * SHORT, :])
        pltpu.make_async_copy(out.at[k], out_far.at[k], sems.at[k]).start()
    for k in range(members):
        pltpu.make_async_copy(out.at[k], out_far.at[k], sems.at[k]).wait()


def cube_kernel(got, c1, out):
    members = got.shape[0]
    size = got.shape[1] - 2 * SHORT
    out[0:size, :] = sum(got[k, 0:size, :].astype(F32) for k in range(members)).astype(BF16)
    total = sum(one_part(got[k, size:, :]) for k in range(members))
    out[size : size + 2 * SHORT, :] = two_parts(total)
    out[size + 2 * SHORT :, :] = c1[...]


def add_kernel(a, b, after, out):
    size = a.shape[0] - 2 * SHORT - 32
    middle = slice(size, size + 2 * SHORT)
    for span in (slice(0, size), slice(size + 2 * SHORT, a.shape[0])):
        out[span, :] = (a[span, :].astype(F32) + b[span, :].astype(F32)).astype(BF16)
    out[middle, :] = two_parts(one_part(a[middle, :]) + one_part(b[middle, :]))


def relay_kernel(batch, *refs):
    parts, (one, two, out) = refs[:CUBE], refs[-3:]
    me = batch[0] % CUBE
    for k, part in enumerate(parts):
        out[me ^ k] = part[...]
    one[...] = out[: CUBE // 2]
    two[...] = out[CUBE // 2 :]


def piece_of(got, k):
    count = got[0].shape[0]
    return got[k // count].at[k % count]


def unpack_half(which, got, lw, bw, vw, stage, stage_b, sems):
    members = 2 * got[0].shape[0]
    size = stage.shape[0] // members
    linear_rows, width = lw.shape
    options = bw.shape[0]
    half = (linear_rows + options * width + width) // 2
    rest = linear_rows - half
    group = options // 3

    def first_copies():
        spans = [(k * size, min((k + 1) * size, half)) for k in range(members)]
        return [
            pltpu.make_async_copy(stage.at[a:b], lw.at[a:b], sems.at[k])
            for k, (a, b) in enumerate(spans)
        ]

    def second_copies():
        copies = [pltpu.make_async_copy(stage.at[0:rest], lw.at[half:], sems.at[0])]
        for k in range(options // group):
            part = slice(k * group, (k + 1) * group)
            copies.append(pltpu.make_async_copy(stage_b.at[part], bw.at[part], sems.at[1 + k]))
        last = stage.at[rest : rest + width]
        copies.append(pltpu.make_async_copy(last, vw, sems.at[len(copies)]))
        return copies

    @pl.when(which == 0)
    def _():
        for k, copy in enumerate(first_copies()):
            start, end = k * size, min((k + 1) * size, half)
            stage[start:end, :] = piece_of(got, k)[0 : end - start, :].astype(F32)
            copy.start()

    @pl.when(which == 1)
    def _():
        def rows(start, end):
            parts = []
            while start < end:
                k, at = start // size, start % size
                count = min(size - at, end - start)
                parts.append(piece_of(got, k)[at : at + count, :])
                start += count
            value = parts[0] if len(parts) == 1 else jnp.concatenate(parts, axis=0)
            return value.astype(F32)

        copies = second_copies()
        stage[0:rest, :] = rows(0, rest)
        copies[0].start()
        for o in range(options):
            stage_b[o] = rows(rest + o * width, rest + (o + 1) * width)
            if o % group == group - 1:
                copies[1 + o // group].start()
        at = rest + options * width
        stage[rest : rest + width, :] = rows(at, at + width)
        copies[-1].start()

    def finish():
        for half_at, copies in ((0, first_copies), (1, second_copies)):

            @pl.when(which == half_at)
            def _():
                for copy in copies():
                    copy.wait()

    return finish


def own_kernel(section, one, two, lw, bw, vw, stage, stage_b, sems):
    unpack_half(section[0], (one, two), lw, bw, vw, stage, stage_b, sems)()


def unpack_kernel(section, *refs):
    mine, other, refs = refs[0:2], refs[2:4], refs[4:]
    lw, bw, vw = refs[3:6]
    little = (len(refs) - 10) // 2
    far, near = refs[6 : 6 + little], refs[6 + little : 6 + 2 * little]
    loss, c1, b1, c2, b2, lb, bb, hw, hb, vb, ow, ob = near
    stage, stage_b, lines, sems = refs[-4:]
    options = bw.shape[0]
    k1, k2 = c1.shape[0], c2.shape[0]
    size = stage.shape[0] // CUBE
    finish = unpack_half(1 - section[0], other, lw, bw, vw, stage, stage_b, sems)
    grad = [jnp.zeros((k1, LANES), F32) for _ in range(2)]
    for k in range(CUBE):
        pair = slice(size, size + 2 * SHORT)
        at = slice(k * SHORT, (k + 1) * SHORT)
        views = piece_of(mine, k), piece_of(other, k)
        lines[at, :] = sum(one_part(v[pair, :]) for v in views)
        for view in views:
            for h in range(2):
                at = size + 2 * SHORT + h * k1
                grad[h] += view[at : at + k1, :].astype(F32)
    for part in range(2):
        c1[:, part * LANES : (part + 1) * LANES] = grad[part]
    bb[...] = lines[0:options, :]
    vb[...] = lines[AT_VB, :]
    ow[...] = lines[AT_OW, :]
    hw[...] = lines[AT_HW, :]
    lb[...] = lines[AT_LB, :]
    scalars = lines[AT_SCALARS, :]
    loss[...] = scalars[:, 0:1]
    hb[...] = scalars[:, 1:3]
    ob[...] = scalars[:, 3:4]
    at = TABLE
    for part in range(2):
        c2[:, part * LANES : (part + 1) * LANES] = lines[at : at + k2, :]
        at += k2
    b1[...] = lines[at : at + 1, 0:k1]
    b2[...] = lines[at + 1 : at + 2, 0:k2]
    copies = [
        pltpu.make_async_copy(a, b, sems.at[CUBE + k]) for k, (a, b) in enumerate(zip(near, far))
    ]
    for copy in copies:
        copy.start()
    finish()
    for copy in copies:
        copy.wait()


def numbers_kernel(
    options,
    depth,
    targets,
    destination,
    b1,
    b2,
    lb,
    bb,
    hw,
    vb,
    ow,
    hb,
    ob,
    out,
    table,
):
    levels, kinds = options.shape[0], targets.shape[0]
    slots = depth.shape[1]
    rows = [options[...].astype(F32), depth[...].astype(F32)]
    rows += [targets[k] for k in range(kinds)]
    rows.append(jnp.zeros((LANES - levels - 1 - kinds * levels, slots), F32))
    out[...] = jnp.transpose(jnp.concatenate(rows, axis=0))
    table[...] = jnp.zeros_like(table)
    table[0 : bb.shape[0], :] = bb[...]
    table[AT_VB, :] = vb[...]
    table[AT_OW, :] = ow[...].astype(F32)
    table[AT_HW, :] = hw[...].astype(F32)
    table[AT_LB, :] = lb[...]
    table[AT_B1, 0 : b1.shape[1]] = b1[...]
    table[AT_B2, 0 : b2.shape[1]] = b2[...]
    lane = iota((1, LANES), 1)
    scalars = jnp.zeros((1, LANES), F32)
    for k, value in ((1, hb[:, 0:1]), (2, hb[:, 1:2]), (3, ob[...])):
        scalars = jnp.where(lane == k, value, scalars)
    table[AT_SCALARS, :] = scalars
    for k in range(slots // LANES):
        part = destination[:, k * LANES : (k + 1) * LANES]
        table[AT_DEST + k : AT_DEST + k + 1, :] = part.astype(F32)


def whole(shape):
    zeros = (0,) * len(shape)
    return pl.BlockSpec(shape, lambda *_: zeros)


ANYWHERE = pl.BlockSpec(memory_space=pl.ANY)
SCALARS = pl.BlockSpec(memory_space=pltpu.SMEM)


def params():
    return pltpu.CompilerParams(vmem_limit_bytes=VMEM_BYTES)


def shape_of(*shape, dtype=F32):
    return jax.ShapeDtypeStruct(shape, dtype)


def cost(microseconds):
    return pl.CostEstimate(
        flops=int(1.1e9 * microseconds), bytes_accessed=int(3.6e6 * microseconds), transcendentals=0
    )


def stays(value):
    return pltpu.with_memory_space_constraint(value, pltpu.HBM)


def held_near(value):
    return pltpu.with_memory_space_constraint(value, pltpu.VMEM)


def encode(section, frames, w1t, w2t, lw, table):
    img = frames.shape[0]
    blocks = img // 4
    side = blocks - 1
    k1, k2, width = w1t.shape[0], w2t.shape[0], lw.shape[1]
    flat = lw.shape[0]
    vmem = pltpu.VMEM
    near = pl.BlockSpec(memory_space=vmem)
    grid_one = (blocks, side, k1, LANES)
    return pl.pallas_call(
        encode_kernel,
        in_specs=[SCALARS, ANYWHERE, near, near, ANYWHERE, near],
        out_specs=[ANYWHERE] * 3 + [near] * 3,
        out_shape=(
            pltpu.HBM(grid_one, BF16),
            pltpu.HBM(grid_one, BF16),
            pltpu.HBM((flat, LANES), BF16),
            shape_of(flat, LANES, dtype=BF16),
            shape_of(width, LANES, dtype=BF16),
            shape_of(width, LANES),
        ),
        scratch_shapes=[
            vmem((img, img, frames.shape[2], LANES), BF16),
            vmem(lw.shape, BF16),
            vmem(grid_one, BF16),
            vmem(grid_one, BF16),
            vmem((flat, LANES), BF16),
            vmem((2 * REACH * k1, 256), BF16),
            vmem((2 * k1, 64), BF16),
            vmem((6 * k2, LANES), BF16),
            vmem((k1, LANES), F32),
            vmem((k2, LANES), F32),
            vmem((side, k1, LANES), F32),
            vmem((side // 2 - 1, k2, LANES), F32),
            pltpu.SemaphoreType.DMA((4, max(blocks // STEP, 3))),
        ],
        compiler_params=params(),
        cost_estimate=cost(9),
        name="encode",
    )(section, frames, w1t, w2t, lw, table)


def plan(section, slots, enc, s3, h2, branch_w, value_w, table, per_pair, depth, half_rows):
    width = enc.shape[0]
    options = branch_w.shape[0]
    two = 2 * width
    pairs = options // 2
    outs = (
        shape_of(half_rows, LANES, dtype=BF16),
        shape_of(half_rows // 2, LANES, dtype=BF16),
        shape_of(half_rows // 2, LANES, dtype=BF16),
        shape_of(TABLE, LANES),
        shape_of(width, LANES, dtype=BF16),
    )
    vmem = pltpu.VMEM
    near = pl.BlockSpec(memory_space=vmem)
    return pl.pallas_call(
        functools.partial(plan_kernel, per_pair=per_pair, depth=depth),
        in_specs=[SCALARS, near, near, near, near, ANYWHERE, near, near],
        out_shape=outs,
        scratch_shapes=[
            vmem((2, half_rows, LANES), BF16),
            vmem((options * width, width + 16), BF16),
            vmem((width + 16, width + 16), BF16),
            vmem((width, width + 16), BF16),
            vmem((width, LANES), F32),
            vmem((16, LANES), F32),
            vmem((options * width, LANES), F32),
            vmem((depth, options * width, LANES), F32),
            vmem((depth, pairs, width, two), F32),
            vmem((depth, pairs, width + 16, two), BF16),
            vmem((depth, pairs, width, two), BF16),
            vmem((depth, options * width, LANES), BF16),
            vmem(branch_w.shape, BF16),
            pltpu.SemaphoreType.DMA,
        ],
        compiler_params=params(),
        cost_estimate=cost(11),
        name="plan",
    )(section, slots, enc, s3, h2, branch_w, value_w, table)


def back(g3, lw, s2, s1, h1, w2t):
    _, side, k1 = s1.shape[:3]
    k2 = w2t.shape[0]
    inner = side // 2 - 1
    padded = (side + 2, side, k1, LANES)
    near = pl.BlockSpec(memory_space=pltpu.VMEM)
    return pl.pallas_call(
        back_kernel,
        in_specs=[near] * 6,
        out_shape=(shape_of(*padded, dtype=BF16), shape_of(k2, 256), shape_of(8, LANES)),
        scratch_shapes=[
            pltpu.VMEM((LANES, 6 * k2), BF16),
            pltpu.VMEM((inner + 2, inner, k2, LANES), BF16),
        ],
        compiler_params=params(),
        cost_estimate=cost(25),
        name="back",
    )(g3, lw, s2, s1, h1, w2t)


def first(section, frames, g1, w1t, other, after, channels, draw):
    img, _, stack, _ = frames.shape
    k1 = g1.shape[2]
    band = (STEP * 4 * COLS * channels, (STEP + 1) * NEAR * k1)
    near = pl.BlockSpec(memory_space=pltpu.VMEM)
    return pl.pallas_call(
        functools.partial(first_kernel, draw=draw),
        in_specs=[SCALARS, ANYWHERE, near, near, ANYWHERE, ANYWHERE],
        out_specs=[near, ANYWHERE, near],
        out_shape=[
            shape_of(2 * k1, LANES, dtype=BF16),
            shape_of(img, img, channels, 2 * LANES),
            shape_of(*band, dtype=BF16),
        ],
        scratch_shapes=[
            pltpu.VMEM((img, img, stack, LANES), BF16),
            pltpu.VMEM((STEP * 4 * COLS * stack, (STEP + 1) * NEAR * k1), F32),
            pltpu.VMEM((STEP * draw + 1,) + g1.shape[1:], BF16),
            pltpu.VMEM((2, 2, 4 * STEP, img, channels, LANES), F32),
            pltpu.SemaphoreType.DMA((img // 4 // STEP + 1,)),
            pltpu.SemaphoreType.DMA((2, 2)),
        ],
        compiler_params=params(),
        cost_estimate=cost(45),
        name="first",
    )(section, frames, g1, w1t, other, after)


def pixels(section, band, mine, other, after, done, start, steps):
    img, _, channels, _ = done.shape
    near = pl.BlockSpec(memory_space=pltpu.VMEM)
    return pl.pallas_call(
        functools.partial(pixels_kernel, start=start),
        in_specs=[SCALARS, near, near, ANYWHERE, ANYWHERE, ANYWHERE],
        out_specs=[ANYWHERE, near],
        out_shape=[shape_of(*done.shape), shape_of(8, LANES)],
        scratch_shapes=[
            pltpu.VMEM((2, 2, 4 * STEP, img, channels, LANES), F32),
            pltpu.VMEM((STEP * steps + 1,) + mine.shape[1:], BF16),
            pltpu.SemaphoreType.DMA((3, 2)),
        ],
        input_output_aliases={5: 0},
        compiler_params=params(),
        cost_estimate=cost(1 + 0.9 * steps),
        name="pixels",
    )(section, band, mine, other, after, done)


def small_call(
    kernel, outs, operands, scratch=(), name=None, place=None, after=(), weight=0.3, far=False
):
    specs = [pl.BlockSpec(memory_space=pltpu.VMEM)] * len(operands)
    if place is not None:
        operands = (*place, *operands)
        specs = [pl.BlockSpec(memory_space=pltpu.SMEM)] * len(place) + specs
    return pl.pallas_call(
        kernel,
        in_specs=specs + [ANYWHERE] * len(after),
        out_specs=jax.tree.map(
            lambda _: ANYWHERE if far else pl.BlockSpec(memory_space=pltpu.VMEM), outs
        ),
        out_shape=outs,
        scratch_shapes=list(scratch),
        compiler_params=params(),
        cost_estimate=cost(weight),
        name=name,
    )(*operands, *after)


def round_up(value, step):
    return -(-value // step) * step


def swapped(value):
    return lax.ppermute(value, "section", [(0, 1), (1, 0)])


def exchanged(value, groups=None):
    return lax.all_to_all(
        value, "batch", split_axis=0, concat_axis=0, axis_index_groups=groups, tiled=True
    )


def partner(value, distance):
    count = lax.axis_size("batch")
    return lax.ppermute(value, "batch", [(b, b ^ distance) for b in range(count)])


def local(
    frames,
    destination,
    options,
    depth,
    targets,
    conv_one,
    bias_one,
    conv_two,
    bias_two,
    linear_w,
    linear_b,
    branch_w,
    branch_b,
    head_w,
    head_b,
    value_w,
    value_b,
    out_w,
    out_b,
):
    section = lax.axis_index("section").astype(jnp.int32)[None]
    peers = lax.axis_size("batch")
    frame_count = frames.shape[3]
    per_pair = frame_count // peers
    levels = options.shape[0]
    frames = stays(frames.transpose(1, 2, 0, 3))
    w1t, w2t = stays(conv_one.T), stays(conv_two.T)
    branch_w, value_w = stays(branch_w), stays(value_w)
    encoder_params = (w1t, bias_one, w2t, bias_two, linear_w, linear_b)
    planner_params = (branch_w, branch_b, head_w.T, head_b, value_w, value_b, out_w.T, out_b)
    width = linear_w.shape[1]
    big_rows = linear_w.shape[0] + (branch_w.shape[0] + 1) * width
    size = round_up(-(-big_rows // (2 * CUBE)), 16)

    tiny = (bias_one, bias_two, linear_b, branch_b, head_w.T, value_b, out_w.T)
    tiny = [stays(v if v.ndim > 1 else v[None, :]) for v in tiny]
    numbers, table = pl.pallas_call(
        numbers_kernel,
        in_specs=[pl.BlockSpec(memory_space=pltpu.VMEM)] * (6 + len(tiny)),
        out_shape=[shape_of(frame_count, LANES), shape_of(TABLE, LANES)],
        compiler_params=params(),
        cost_estimate=cost(1),
        name="numbers",
    )(
        stays(options),
        stays(depth[None, :]),
        stays(targets),
        stays(destination[None, :]),
        *tiny,
        stays(head_b[None, :]),
        out_b[None, :],
    )
    slots = exchanged(numbers.reshape(peers, per_pair, LANES)).reshape(frame_count, LANES)

    h1, s1, s2, h2, enc, s3 = encode(section, frames, w1t, w2t, stays(linear_w), table)
    keep, send_one, send_two, small, g3 = plan(
        section, slots, enc, s3, h2, branch_w, value_w, table, per_pair, levels, CUBE * size
    )
    recv = swapped(send_one), swapped(send_two)
    channels = frames.shape[2] // lax.axis_size("section")
    g1, c2, sums = back(g3, linear_w, s2, s1, h1, w2t)
    other = swapped(g1)
    g1 = held_near(g1)
    cubes = [list(range(c, c + CUBE)) for c in range(0, peers, CUBE)]
    bf16 = functools.partial(shape_of, dtype=BF16)
    pieces = small_call(
        merge_kernel,
        bf16(CUBE, size + 2 * SHORT, LANES),
        (keep, *recv, small, c2, sums),
        [
            pltpu.VMEM((CUBE * SHORT, LANES), F32),
            pltpu.VMEM((CUBE, size + 2 * SHORT, LANES), BF16),
            pltpu.SemaphoreType.DMA((CUBE,)),
        ],
        name="merge",
        far=True,
        weight=30,
    )
    got = exchanged(pieces, cubes)
    c1, frames_grad, band = first(section, frames, g1, w1t, other, pieces, channels, DRAW)
    piece = bf16(size + 2 * SHORT + c1.shape[0], LANES)
    keep = small_call(cube_kernel, piece, (got, c1), name="cube")
    distance = CUBE
    while distance < peers:
        recv = partner(keep, distance)
        if distance == CUBE:
            frames_grad, token = pixels(
                section, band, g1, other, keep, frames_grad, DRAW, DRAW_ACROSS
            )
        distance *= 2
        keep = small_call(add_kernel, piece, (keep, recv), name="add", after=(token,))
    parts = [keep] + [partner(keep, k) for k in range(1, CUBE)]
    place = (lax.axis_index("batch").astype(jnp.int32)[None],)
    drawn = DRAW + DRAW_ACROSS
    left = frames.shape[0] // 4 // STEP - drawn
    frames_grad, token = pixels(section, band, g1, other, keep, frames_grad, drawn, left)
    got = small_call(
        relay_kernel,
        [bf16(CUBE // 2, *piece.shape)] * 2,
        parts,
        [pltpu.VMEM((CUBE, *piece.shape), BF16)],
        name="relay",
        place=place,
        after=(token,),
    )
    got_other = [swapped(v) for v in got]
    shapes = [p.shape for p in encoder_params + planner_params]
    near = pl.BlockSpec(memory_space=pltpu.VMEM)
    flat = [shape_of(*(v if len(v) > 1 else (1,) + v)) for v in [(1, 1)] + shapes]
    large = [flat[k] for k in (5, 7, 11)]
    staged = [
        pltpu.VMEM((CUBE * size, LANES), F32),
        pltpu.VMEM(branch_w.shape, F32),
    ]
    little = [v for k, v in enumerate(flat) if k not in (5, 7, 11)]
    sems = pltpu.SemaphoreType.DMA((CUBE + len(little),))
    begun = pl.pallas_call(
        own_kernel,
        in_specs=[SCALARS, near, near],
        out_specs=[ANYWHERE] * 3,
        out_shape=large,
        scratch_shapes=[*staged, sems],
        compiler_params=params(),
        cost_estimate=cost(1),
        name="own",
    )(section, *got)
    ends = pl.pallas_call(
        unpack_kernel,
        in_specs=[SCALARS] + [near] * 4 + [ANYWHERE] * 3,
        out_specs=[ANYWHERE] * (3 + len(little)),
        out_shape=large + little,
        scratch_shapes=[pltpu.VMEM(v.shape, F32) for v in little]
        + [*staged, pltpu.VMEM((CUBE * SHORT, LANES), F32), sems],
        input_output_aliases={5: 0, 6: 1, 7: 2},
        compiler_params=params(),
        cost_estimate=cost(1.5),
        name="unpack",
    )(section, *got, *got_other, *begun)
    rest = list(ends[3:])
    for k, at in enumerate((5, 7, 11)):
        rest.insert(at, ends[k])
    rest = [v.reshape(s) for v, s in zip(rest, [()] + shapes)]
    for at in (1, 3, 9, 13):
        rest[at] = rest[at].T
    return (rest[0], frames_grad.transpose(2, 0, 1, 3), *rest[1:])


def solution(mesh):
    placed = (
        P(None, None, None, "batch"),
        P("batch"),
        P(None, "batch"),
        P("batch"),
        P(None, None, "batch"),
    ) + (P(),) * 14
    return jax.shard_map(
        local,
        mesh=mesh,
        in_specs=placed,
        out_specs=(P(), P("section", None, None, "batch")) + (P(),) * 14,
        check_vma=False,
    )
```

```python
import functools
import math

import jax
import jax.numpy as jnp
from jax import lax
from jax.experimental import pallas as pl
from jax.experimental.pallas import tpu as pltpu
from jax.sharding import PartitionSpec as P

BF16 = jnp.bfloat16
F32 = jnp.float32
EXACT = lax.Precision.HIGHEST
LANES = 128
VMEM_BYTES = 32 * 1024 * 1024
TILE = 16
REACH = 5
STEP = 3
COLS = 12
NEAR = 4
AT_VB, AT_OW, AT_HW, AT_LB, AT_SCALARS, AT_B1, AT_B2, AT_DEST = (
    slice(18, 19),
    slice(19, 20),
    slice(20, 22),
    slice(22, 23),
    slice(23, 24),
    slice(24, 25),
    slice(25, 26),
    26,
)
TABLE = 32
CUBE = 8
DRAW = 4
SHORT = 16


def dot(a, b, precision=None):
    return jnp.dot(a, b, preferred_element_type=F32, precision=precision)


def dot_rows(a, b, precision=None):
    return lax.dot_general(
        a, b, (((0,), (0,)), ((), ())), preferred_element_type=F32, precision=precision
    )


def dot_lanes(a, b, precision=None):
    return lax.dot_general(
        a, b, (((1,), (1,)), ((), ())), preferred_element_type=F32, precision=precision
    )


def iota(shape, axis):
    return lax.broadcasted_iota(jnp.int32, shape, axis)


def column(row):
    n = row.shape[1]
    wide = jnp.broadcast_to(row, (n, n))
    return jnp.sum(jnp.where(iota((n, n), 0) == iota((n, n), 1), wide, 0.0), axis=1, keepdims=True)


def row_of(col):
    n = col.shape[0]
    wide = jnp.broadcast_to(col, (n, n))
    return jnp.sum(jnp.where(iota((n, n), 0) == iota((n, n), 1), wide, 0.0), axis=0, keepdims=True)


def soft(x):
    t = jnp.tanh(0.5 * x)
    return jnp.maximum(x, 0.0) - jnp.log(0.5 + 0.5 * jnp.abs(t)), 0.5 + 0.5 * t


def silu_pair(y):
    t = jnp.tanh(y)
    m = y * t
    return y + m, (1.0 + t) + (y - m * t)


def pixel_order(w1t):
    tap, pix = iota((256, 256), 0), iota((256, 256), 1)
    moves = ((tap >> 6) == (pix & 3)) & ((tap & 63) == (pix >> 2))
    return dot(w1t, moves.astype(F32).astype(BF16))


def frame_copies(section, far, here, sems):
    lanes = pl.ds(pl.multiple_of(section[0] * LANES, LANES), LANES)
    size = 4 * STEP

    def copy(g):
        rows = pl.ds(pl.multiple_of(g * size, size), size)
        return pltpu.make_async_copy(far.at[rows, :, :, lanes], here.at[rows], sems.at[g])

    return copy


def tile_rows(frames, row, j, cols):
    img, _, channels, _ = frames.shape
    flat = frames.reshape(img, img * channels, LANES)
    size = cols * channels
    end = min((j + 1) * size, img * channels)
    part = flat[pl.ds(row, 4), j * size : end, :]
    return part.reshape(4 * (end - j * size), LANES)


def encode_kernel(
    section,
    frames_far,
    w1t,
    w2t,
    lw_far,
    table,
    h1_far,
    s1_far,
    s2_far,
    h2,
    enc,
    s3,
    frames,
    lw,
    h1,
    s1,
    s2,
    band,
    edge,
    band2,
    bias1,
    bias2,
    held,
    held2,
    sems,
):
    blocks, side = h1.shape[:2]
    steps = blocks // STEP
    tiles = frames.shape[1] // TILE
    k1, k2 = w1t.shape[0], w2t.shape[0]
    reach_rows = REACH * k1
    arrives = frame_copies(section, frames_far, frames, sems.at[0])
    for g in range(steps):
        arrives(g).start()
    last_copies = [
        pltpu.make_async_copy(lw_far, lw, sems.at[3, 0]),
        pltpu.make_async_copy(s2, s2_far, sems.at[3, 1]),
    ]
    last_copies[0].start()

    def leaves(g):
        rows = pl.ds(g * STEP, STEP)
        return [
            pltpu.make_async_copy(h1.at[rows], h1_far.at[rows], sems.at[1, g]),
            pltpu.make_async_copy(s1.at[rows], s1_far.at[rows], sems.at[2, g]),
        ]

    inner = side // 2 - 1
    row_len = inner * k2
    two = 2 * k2 * 3

    def prepare():
        taps = pixel_order(w1t[...])
        edges = []
        for half in range(2):
            lines = [taps[:, 32 * (4 * half + u) : 32 * (4 * half + u + 1)] for u in range(4)]
            for place in range(REACH):
                pieces = []
                for line in lines:
                    start = 16 * (place - 1)
                    cut = line[:, max(0, -start) : min(32, 64 - start)]
                    start = max(start, 0)
                    pieces += [jnp.zeros((k1, start), F32)] if start else []
                    pieces.append(cut)
                    rest = 64 - start - cut.shape[1]
                    pieces += [jnp.zeros((k1, rest), F32)] if rest else []
                at = half * reach_rows + place * k1
                band[at : at + k1, :] = jnp.concatenate(pieces, axis=1).astype(BF16)
            edges.append(jnp.concatenate([line[:, 16:] for line in lines], axis=1))
        edge[...] = jnp.concatenate(edges, axis=0).astype(BF16)
        tap, pix = iota((256, LANES), 0), iota((256, LANES), 1)
        for half in range(2):
            for place in range(3):
                hit = (
                    ((tap & 15) == (pix & 15))
                    & ((tap >> 6) == (pix >> 6) + 2 * half)
                    & (((tap >> 4) & 3) == ((pix >> 4) & 3) + 2 - 2 * place)
                )
                at = (half * 3 + place) * k2
                taps = dot(w2t[...], hit.astype(F32).astype(BF16))
                band2[at : at + k2, :] = taps.astype(BF16)
        bias1[...] = jnp.broadcast_to(column(table[AT_B1, 0:k1]), bias1.shape)
        bias2[...] = jnp.broadcast_to(column(table[AT_B2, 0:k2]), bias2.shape)
        held[...] = jnp.zeros_like(held)
        held2[...] = jnp.zeros_like(held2)
        h1[...] = jnp.zeros_like(h1)

    def added(sums, x, value):
        sums[x] = sums[x] + value if x in sums else value

    def second_matmul(b):
        tiles = [
            h1[pl.ds(2 * b + 1, 2), 4 * j : 4 * j + 4].reshape(LANES, LANES)
            for j in range(side // 4)
        ]
        return dot(band2[...], jnp.concatenate(tiles, axis=1))

    def second_rows(b, got):
        low, high = {}, {}
        for j in range(side // 4):
            for place in range(3):
                x = 2 * j - 1 + place
                if 0 <= x < inner:
                    span = slice(j * LANES, (j + 1) * LANES)
                    at = place * k2
                    added(low, x, got[at : at + k2, span])
                    added(high, x, got[two // 2 + at : two // 2 + at + k2, span])
        row = jnp.maximum(b - 1, 0) * row_len
        for x in range(inner):
            value, slope = soft(held2[x] + high[x] + bias2[...])
            held2[x] = low[x]
            at = pl.ds(pl.multiple_of(row + x * k2, k2), k2)
            h2[at, :] = value.astype(BF16)
            s2[at, :] = slope.astype(BF16)

    def one_step(g, carry):
        def row(r):
            return pl.multiple_of(4 * (STEP * g + r), 4)

        arrives(g).wait()
        lows, highs = [{} for _ in range(STEP)], [{} for _ in range(STEP)]

        def place_tile(r, j, got):
            for place in range(REACH):
                x = 4 * j - 1 + place
                if 0 <= x < side:
                    at = place * k1
                    added(lows[r], x, got[at : at + k1])
                    added(highs[r], x, got[reach_rows + at : reach_rows + at + k1])

        def finish(r, xs):
            for x in xs:
                value, slope = soft(held[x] + highs[r][x] + bias1[...])
                held[x] = lows[r][x]
                h1[STEP * g + r, x] = value.astype(BF16)
                s1[STEP * g + r, x] = slope.astype(BF16)

        pair = jnp.maximum(g - 1, 0)
        units = [(lambda: second_matmul(pair), lambda got: second_rows(pair, got))]

        def edges():
            parts = [tile_rows(frames, row(r), tiles, TILE) for r in range(STEP)]
            return dot(edge[...], jnp.concatenate(parts, axis=1))

        def place_edges(got):
            for r in range(STEP):
                added(lows[r], side - 1, got[:k1, r * LANES : (r + 1) * LANES])
                added(highs[r], side - 1, got[k1:, r * LANES : (r + 1) * LANES])

        units.append((edges, place_edges))

        def full(spots):
            parts = [tile_rows(frames, row(r), j, TILE) for r, j in spots]
            return dot(band[...], jnp.concatenate(parts, axis=1))

        def place_full(got, spots, ready):
            for i, (r, j) in enumerate(spots):
                place_tile(r, j, got[:, i * LANES : (i + 1) * LANES])
            if ready:
                finish(*ready)

        for r in range(STEP):
            if r % 2 == 0:
                spots = [(k, tiles - 1) for k in (r, r + 1) if k < STEP]
                units.append(
                    (
                        functools.partial(full, spots),
                        functools.partial(place_full, spots=spots, ready=None),
                    )
                )
            done = 0
            for j in range(0, tiles - 1, 2):
                spots = [(r, j), (r, j + 1)]
                ready = side if j + 2 == tiles - 1 else 4 * j + 7
                units.append(
                    (
                        functools.partial(full, spots),
                        functools.partial(place_full, spots=spots, ready=(r, range(done, ready))),
                    )
                )
                done = ready
        waiting = None
        for issue, take in units:
            got = issue()
            if waiting is not None:
                waiting[0](waiting[1])
            waiting = (take, got)
        waiting[0](waiting[1])
        for copy in leaves(g):
            copy.start()
        return carry

    prepare()
    lax.fori_loop(0, steps, one_step, 0)
    for b in range(steps - 1, side // 2):
        second_rows(b, second_matmul(b))
    for copy in last_copies[1:]:
        copy.start()
    last_copies[0].wait()
    value, slope = soft(dot_rows(lw[...], h2[...]) + column(table[AT_LB, :]))
    enc[...] = value.astype(BF16)
    s3[...] = slope
    for g in range(steps):
        for copy in leaves(g):
            copy.wait()
    for copy in last_copies[1:]:
        copy.wait()


def three_parts(row):
    high = row.astype(BF16).astype(F32)
    middle = (row - high).astype(BF16).astype(F32)
    return jnp.concatenate([high, middle, row - high - middle], axis=0)


def with_ones(value):
    return jnp.concatenate([value, ones_rows(value.shape[1])], axis=0)


def ones_rows(lanes):
    return (iota((16, lanes), 0) < 3).astype(F32).astype(BF16)


def plan_kernel(
    section,
    slots,
    enc,
    s3,
    h2,
    branch_far,
    value_w,
    table,
    keep,
    send_one,
    send_two,
    small,
    g3,
    parts,
    bwt,
    vht,
    vhw,
    ow,
    mine,
    pre,
    dbr,
    dval,
    low,
    hid,
    gb,
    branch_w,
    sem,
    *,
    per_pair,
    depth,
):
    width = enc.shape[0]
    options = branch_w.shape[0]
    pairs = options // 2
    two = 2 * width
    sec = section[0]
    branch_copy = pltpu.make_async_copy(branch_far, branch_w, sem)
    branch_copy.start()

    count = slots.shape[0]
    dest = jnp.concatenate(
        [table[AT_DEST + k : AT_DEST + k + 1, :] for k in range(count // LANES)], axis=1
    )
    own = jnp.where(sec == 0, dest[:, :LANES], dest[:, LANES:])
    others = jnp.transpose(jnp.broadcast_to(dest, (LANES, count)))
    index = iota((count, LANES), 1) + sec * LANES
    earlier = (others == own) & (iota((count, LANES), 0) < index)
    rank = jnp.sum(earlier.astype(F32), axis=0, keepdims=True)
    bucket = own * float(per_pair) + rank
    chosen = (iota((count, LANES), 0).astype(F32) == bucket).astype(F32).astype(BF16)
    numbers = slots[:, : mine.shape[0]]
    high = numbers.astype(BF16)
    middle = (numbers - high.astype(F32)).astype(BF16)
    rest = (numbers - high.astype(F32) - middle.astype(F32)).astype(BF16)
    mine[...] = sum(dot_rows(v, chosen) for v in (rest, middle, high))

    pad = jnp.zeros((13, width), F32)
    branch_copy.wait()
    for o in range(options):
        rows = [branch_w[o].astype(F32), three_parts(table[o : o + 1, :]), pad]
        bwt[o * width : (o + 1) * width, :] = jnp.transpose(
            0.5 * jnp.concatenate(rows, axis=0)
        ).astype(BF16)
    scalars = table[AT_SCALARS, :]
    head_w = table[AT_HW, :]
    rows = [value_w[...].astype(F32), three_parts(table[AT_VB, :]), pad]
    vht[0:width, :] = jnp.transpose(0.5 * jnp.concatenate(rows, axis=0)).astype(BF16)
    vht[width:, :] = jnp.zeros((16, width + 16), BF16)
    lane = iota((1, 16), 1)
    for k in range(2):
        bias = three_parts(jnp.broadcast_to(scalars[:, 1 + k : 2 + k], (1, 16)))
        bias = sum(jnp.where(lane == j, bias[j : j + 1], 0.0) for j in range(3))
        vht[width + k : width + k + 1, 0:width] = head_w[k : k + 1].astype(BF16)
        vht[width + k : width + k + 1, width:] = bias.astype(BF16)
    vhw[:, 0:width] = (0.5 * value_w[...].astype(F32)).astype(BF16)
    vhw[:, width:] = jnp.transpose(
        0.5 * jnp.concatenate([head_w, jnp.zeros((14, width), F32)], axis=0)
    ).astype(BF16)
    ow[...] = jnp.broadcast_to(column(table[AT_OW, :]), (width, LANES))
    wide_ow = jnp.concatenate([ow[...], ow[...]], axis=1)
    half_ow = 0.5 * wide_ow

    labels = iota((options, LANES), 0).astype(F32)
    state = enc[...].astype(F32)
    rounded_all, saved = [], []
    group = 3
    for level in range(depth):
        picked = labels == mine[level : level + 1, :]
        rounded = state.astype(BF16)
        rounded_all.append(rounded)
        met = with_ones(rounded)

        def branches(first):
            at = slice(first * two, (first + group) * two)
            pre[at, :] = dot(bwt[at, :], met)

        branches(0)
        following = state
        reward, discount, value = [], [], []

        def value_part(t, got):
            act, slope = silu_pair(got[:width])
            dval[level, t] = slope
            hidden = act.astype(BF16)
            hid[level, t] = hidden
            worth = jnp.sum(hidden.astype(F32) * wide_ow, axis=0, keepdims=True)
            for k in range(2):
                span = slice(k * LANES, (k + 1) * LANES)
                value.append(worth[:, span])
                reward.append(got[width : width + 1, span])
                discount.append(got[width + 1 : width + 2, span])

        waiting = None
        for first in range(0, pairs, group):
            if first + group < pairs:
                branches(first + group)
            boths = []
            for t in range(first, first + group):
                at = slice(t * two, (t + 1) * two)
                act, slope = silu_pair(pre[at, :])
                dbr[level, at, :] = slope
                left = state + act[:width]
                right = state + act[width:]
                following = jnp.where(picked[2 * t : 2 * t + 1], left, following)
                following = jnp.where(picked[2 * t + 1 : 2 * t + 2], right, following)
                both = with_ones(
                    jnp.concatenate([left.astype(BF16), right.astype(BF16)], axis=1)
                )
                low[level, t] = both
                boths.append(both)
            got = dot(vht[...], jnp.concatenate(boths, axis=1))
            if waiting is not None:
                for k in range(group):
                    value_part(waiting[0] + k, waiting[1][:, k * two : (k + 1) * two])
            waiting = (first, got)
        for k in range(group):
            value_part(waiting[0] + k, waiting[1][:, k * two : (k + 1) * two])
        reward = jnp.concatenate(reward, axis=0)
        discount = jax.nn.sigmoid(jnp.concatenate(discount, axis=0))
        value = jnp.concatenate(value, axis=0) + scalars[:, 3:4]
        quality = reward + discount * value
        top = jnp.max(quality, axis=0, keepdims=True)
        shifted = jnp.exp(quality - top)
        total = jnp.sum(shifted, axis=0, keepdims=True)
        live = (mine[depth : depth + 1, :] > level).astype(F32)
        chosen = picked.astype(F32)

        def target(kind):
            at = depth + 1 + kind * depth + level
            return mine[at : at + 1, :]

        reward_gap = live * (jnp.sum(chosen * reward, axis=0, keepdims=True) - target(0))
        discount_gap = live * (jnp.sum(chosen * discount, axis=0, keepdims=True) - target(1))
        plan_gap = live * (top + jnp.log(total) - target(2))
        grad_quality = plan_gap * (shifted / total)
        head_two = (chosen * discount_gap + grad_quality * value) * discount * (1.0 - discount)
        saved.append(
            (
                picked,
                (chosen * reward_gap + grad_quality).astype(BF16).astype(F32),
                head_two.astype(BF16).astype(F32),
                (grad_quality * discount).astype(BF16).astype(F32),
                reward_gap * reward_gap + discount_gap * discount_gap + plan_gap * plan_gap,
            )
        )
        state = following

    out_sum = jnp.zeros((16, width), F32)
    value_sum = jnp.zeros((width + 16, width + 16), F32)
    grad_next = None
    line = iota((16, two), 0)
    for level in reversed(range(depth)):
        picked, head_one, head_two, grad_value, _ = saved[level]
        upward = jnp.zeros((width, LANES), F32)

        def branch_part(t, moved):
            at = slice(t * two, (t + 1) * two)
            left, right = moved[:, :LANES], moved[:, LANES:]
            if grad_next is not None:
                left = left + jnp.where(picked[2 * t : 2 * t + 1], grad_next, 0.0)
                right = right + jnp.where(picked[2 * t + 1 : 2 * t + 2], grad_next, 0.0)
            grad_branch = jnp.concatenate([left, right], axis=0) * dbr[level, at, :]
            grad_branch = grad_branch.astype(BF16)
            gb[level, at, :] = grad_branch
            return left + right

        def group_part(first, moved):
            parts = [
                branch_part(first + k, moved[:, k * two : (k + 1) * two]) for k in range(group)
            ]
            at = slice(first * two, (first + group) * two)
            weights = [branch_w[o] for o in range(2 * first, 2 * (first + group))]
            return sum(parts), dot(jnp.concatenate(weights, axis=1), gb[level, at, :])

        waiting = None
        for first in range(0, pairs, group):
            stack = []
            for t in range(first, first + group):

                def across(rows):
                    return jnp.concatenate(
                        [rows[2 * t : 2 * t + 1], rows[2 * t + 1 : 2 * t + 2]], axis=1
                    )

                worth = across(grad_value)
                grad_pre = (worth * half_ow * dval[level, t]).astype(BF16)
                heads = jnp.where(line == 0, across(head_one), 0.0)
                heads = jnp.where(line == 1, across(head_two), heads)
                heads = jnp.where(line == 2, worth, heads)
                heads = heads.astype(BF16)
                out_sum = out_sum + dot_lanes(heads, hid[level, t])
                stack.append(jnp.concatenate([grad_pre, heads], axis=0))
            stack = jnp.concatenate(stack, axis=1)
            moved = dot(vhw[...], stack)
            if waiting is not None:
                one, other = group_part(*waiting)
                upward = upward + (one + 0.5 * other)
            waiting = (first, moved)
            lows = jnp.concatenate([low[level, first + k] for k in range(group)], axis=1)
            value_sum = value_sum + dot_lanes(stack, lows)
        one, other = group_part(*waiting)
        grad_next = upward + (one + 0.5 * other)

    linear_rows = h2.shape[0]
    half = (linear_rows + options * width + width) // 2
    rest = linear_rows - half
    rounded = with_ones(jnp.concatenate(rounded_all, axis=1))
    small[...] = jnp.zeros_like(small)
    if half < keep.shape[0]:
        for k in range(2):
            parts[k, half:, :] = jnp.zeros((keep.shape[0] - half, LANES), BF16)
    for t in range(pairs):
        at = slice(t * two, (t + 1) * two)
        grads = jnp.concatenate([gb[level, at, :] for level in range(depth)], axis=1)
        got = dot_lanes(rounded, grads)
        for k in range(2):
            o = 2 * t + k
            span = slice(k * width, (k + 1) * width)
            rows = slice(rest + o * width, rest + (o + 1) * width)
            parts[1 - sec, rows, :] = got[:width, span].astype(BF16)
            small[o : o + 1, :] = got[width : width + 1, span]
    after = rest + options * width
    parts[1 - sec, after : after + width, :] = jnp.transpose(value_sum[:width, :width]).astype(BF16)

    grad_three = ((2.0 * grad_next).astype(BF16).astype(F32) * s3[...]).astype(BF16)
    g3[...] = grad_three
    chunk = linear_rows // 9
    for i in range(8):
        at = slice(i * chunk, (i + 1) * chunk)
        parts[sec, at, :] = dot_lanes(h2[at, :], grad_three).astype(BF16)
    last = dot_lanes(h2[8 * chunk :, :], grad_three).astype(BF16)
    parts[sec, 8 * chunk : half, :] = last[: half - 8 * chunk]
    parts[1 - sec, 0:rest, :] = last[half - 8 * chunk :]
    keep[...] = parts[0]
    send_one[...] = parts[1, : send_one.shape[0]]
    send_two[...] = parts[1, send_one.shape[0] :]

    small[AT_VB, :] = row_of(value_sum[:width, width : width + 1])
    small[AT_OW, :] = out_sum[2:3]
    small[AT_HW, :] = value_sum[width : width + 2, :width]
    small[AT_LB, :] = row_of(jnp.sum(grad_three.astype(F32), axis=1, keepdims=True))
    loss = 0.5 * jnp.sum(sum(kept[4] for kept in saved), axis=1, keepdims=True)
    ends = [loss] + [value_sum[width + k : width + k + 1, width : width + 1] for k in range(3)]
    lane = iota((1, LANES), 1)
    line = jnp.zeros((1, LANES), F32)
    for k, end in enumerate(ends):
        line = jnp.where(lane == k, end, line)
    small[AT_SCALARS, :] = line


def back_kernel(g3, lw, s2, s1, h1, w2t, g1, c2, sums, t2, g2):
    side, k1 = s1.shape[1], s1.shape[2]
    k2 = w2t.shape[0]
    inner = side // 2 - 1
    row_len = inner * k2
    tap, pix = iota((LANES, 256), 1), iota((LANES, 256), 0)
    for yrel in range(2):
        for p in range(3):
            hit = (
                ((tap & 15) == (pix & 15))
                & ((tap >> 6) == (pix >> 6) + 2 * (1 - yrel))
                & (((tap >> 4) & 3) == ((pix >> 4) & 3) + 2 - 2 * p)
            )
            at = (yrel * 3 + p) * k2
            t2[:, at : at + k2] = dot_lanes(hit.astype(F32).astype(BF16), w2t[...]).astype(BF16)
    g2[0] = jnp.zeros(g2.shape[1:], BF16)
    g2[inner + 1] = jnp.zeros(g2.shape[1:], BF16)
    g1[0] = jnp.zeros(g1.shape[1:], BF16)
    g1[side + 1] = jnp.zeros(g1.shape[1:], BF16)
    zero = jnp.zeros((k2, LANES), BF16)
    total_one = jnp.zeros((k1, LANES), F32)
    total_two = jnp.zeros((k2, LANES), F32)
    for y in range(inner):
        at = slice(y * row_len, (y + 1) * row_len)
        grad = dot(lw[at, :], g3[...]) * s2[at, :].astype(F32)
        grad = grad.astype(BF16).reshape(inner, k2, LANES)
        g2[y + 1] = grad
        total_two = total_two + jnp.sum(grad.astype(F32), axis=0)
    reach, cols = 5, 8
    total = jnp.zeros((2 * reach * k2, 2 * cols * k1), F32)
    grads, tiles = [], []
    for b in range(side // 2):
        cut = []
        for j in range(side // 4):
            pieces = []
            for yrel in range(2):
                for p in range(3):
                    x = 2 * j - 1 + p
                    pieces.append(g2[b + yrel, x] if 0 <= x < inner else zero)
            cut.append(jnp.concatenate(pieces, axis=0))
        got = dot(t2[...], jnp.concatenate(cut, axis=1))
        for u in range(2):
            for j in range(side // 4):
                part = got[u * 64 : (u + 1) * 64, j * LANES : (j + 1) * LANES]
                slope = s1[2 * b + u + 1, 4 * j : 4 * j + 4].astype(F32)
                grad = (part.reshape(4, k1, LANES) * slope).astype(BF16)
                g1[2 * b + u + 1, 4 * j : 4 * j + 4] = grad
                total_one = total_one + jnp.sum(grad.astype(F32), axis=0)
        for j in range(-(-side // cols)):
            end = min((j + 1) * cols, side)
            tile = h1[2 * b + 1 : 2 * b + 3, j * cols : end]
            if end < (j + 1) * cols:
                rest = jnp.zeros((2, (j + 1) * cols - end, k1, LANES), BF16)
                tile = jnp.concatenate([tile, rest], axis=1)
            tiles.append(tile.reshape(2 * cols * k1, LANES))
            pieces = []
            for half in range(2):
                for p in range(reach):
                    x = 4 * j - 1 + p
                    pieces.append(g2[b + 1 - half, x] if 0 <= x < inner else zero)
            grads.append(jnp.concatenate(pieces, axis=0))
        if b % 2:
            total = total + dot_lanes(
                jnp.concatenate(grads, axis=1), jnp.concatenate(tiles, axis=1)
            )
            grads, tiles = [], []
    line = 4 * k1
    for half in range(2):
        for u in range(2):
            tap_row = jnp.zeros((k2, line), F32)
            for p in range(reach):
                at = (half * reach + p) * k2
                part = total[at : at + k2, u * 2 * line : (u + 1) * 2 * line]
                start = 2 * k1 * (p - 1)
                piece = part[:, max(start, 0) : min(start + line, 2 * line)]
                if start < 0:
                    piece = jnp.concatenate([jnp.zeros((k2, -start), F32), piece], axis=1)
                if start + line > 2 * line:
                    rest = jnp.zeros((k2, start - line), F32)
                    piece = jnp.concatenate([piece, rest], axis=1)
                tap_row = tap_row + piece
            at = (2 * half + u) * line
            c2[:, at : at + line] = tap_row
    sums[...] = jnp.zeros_like(sums)
    sums[0:1, 0:k1] = row_of(jnp.sum(total_one, axis=1, keepdims=True))
    sums[1:2, 0:k2] = row_of(jnp.sum(total_two, axis=1, keepdims=True))


def pixel_band(sec, w1t, channels):
    k1 = w1t.shape[0]
    rows = 64 * channels
    row, tap = iota((rows, 256), 0), iota((rows, 256), 1)
    moves = ((tap >> 6) == row % channels + sec * channels) & ((tap & 63) == row // channels)
    taps = dot_lanes(moves.astype(F32).astype(BF16), w1t)
    line, span = COLS * channels, 8 * channels
    blocks = {}
    for half in range(2):
        for p in range(NEAR):
            pieces = []
            for u in range(4):
                at = (4 * half + u) * span
                start = 4 * (p - 1) * channels
                cut = taps[at + max(0, -start) : at + min(span, line - start)]
                start = max(start, 0)
                pieces += [jnp.zeros((start, k1), F32)] if start else []
                pieces.append(cut)
                rest = line - start - cut.shape[0]
                pieces += [jnp.zeros((rest, k1), F32)] if rest else []
            blocks[half, p] = jnp.concatenate(pieces, axis=0)
    zero = jnp.zeros((4 * line, k1), F32)
    lines = []
    for r in range(STEP):
        cols = [
            blocks.get((r + 1 - yrel, p), zero) for yrel in range(STEP + 1) for p in range(NEAR)
        ]
        lines.append(jnp.concatenate(cols, axis=1))
    return jnp.concatenate(lines, axis=0).astype(BF16)


def first_kernel(
    section,
    frames_far,
    g1,
    w1t,
    other_far,
    after,
    c1,
    out,
    band,
    frames,
    acc,
    other,
    held,
    sems,
    draw_sems,
    *,
    draw,
):
    side, k1 = g1.shape[1], g1.shape[2]
    img, _, channels, _ = frames.shape
    steps = img // 4 // STEP
    arrives = frame_copies(section, frames_far, frames, sems)
    for g in range(steps):
        arrives(g).start()
    other_copy = pltpu.make_async_copy(
        other_far.at[0 : STEP * draw + 1], other, sems.at[steps]
    )
    other_copy.start()
    acc[...] = jnp.zeros_like(acc)
    zero = jnp.zeros((k1, LANES), BF16)

    def one_step(g, carry):
        arrives(g).wait()
        pixels, grads = [], []
        for j in range(img // COLS):
            rows = [pl.multiple_of(4 * (STEP * g + r), 4) for r in range(STEP)]
            pixels.append(
                jnp.concatenate([tile_rows(frames, row, j, COLS) for row in rows], axis=0)
            )
            pieces = []
            for yrel in range(STEP + 1):
                for p in range(NEAR):
                    x = 3 * j - 1 + p
                    pieces.append(g1[STEP * g + yrel, x] if 0 <= x < side else zero)
            grads.append(jnp.concatenate(pieces, axis=0))
        acc[...] += dot_lanes(jnp.concatenate(pixels, axis=1), jnp.concatenate(grads, axis=1))
        return carry

    lax.fori_loop(0, steps, one_step, 0)
    band[...] = pixel_band(section[0], w1t[...], out.shape[2])
    other_copy.wait()
    finish = draw_steps(section, band, g1, 0, other, 0, out, held, draw_sems, 0, draw)
    fold_first(acc, c1, channels, k1)
    finish()


def fold_first(acc, c1, channels, k1):
    line = COLS * channels
    step = 4 * channels
    taps = []
    for half in range(2):
        total = sum(
            acc[r * 4 * line : (r + 1) * 4 * line, :][
                :, (r + 1 - half) * NEAR * k1 : (r + 2 - half) * NEAR * k1
            ]
            for r in range(STEP)
        )
        for u in range(4):
            part = total[u * line : (u + 1) * line]
            cols = [part[:, p * k1 : (p + 1) * k1] for p in range(NEAR)]
            taps.append(cols[1][0:step] + cols[2][step : 2 * step] + cols[3][2 * step :])
            taps.append(cols[0][0:step] + cols[1][step : 2 * step] + cols[2][2 * step :])
    row, col = iota((256, 256), 0), iota((256, 256), 1)
    moves = ((row & 3) == (col >> 6)) & ((row >> 2) == (col & 63))
    grad = dot_rows(jnp.concatenate(taps, axis=0), moves.astype(F32), EXACT)
    for half in range(2):
        c1[half * k1 : (half + 1) * k1, :] = grad[:, half * LANES : (half + 1) * LANES].astype(BF16)


def draw_steps(section, band, mine, mine_at, other, other_at, out, held, sems, start, steps):
    side, k1 = mine.shape[1], mine.shape[2]
    img, channels = out.shape[1], out.shape[2]
    sec = section[0]
    line = COLS * channels
    flat = held.reshape(2, 2, 4 * STEP, img * channels, LANES)

    def writes(g):
        rows = slice(4 * STEP * (start + g), 4 * STEP * (start + g + 1))
        places = (sec * LANES, (1 - sec) * LANES)
        return [
            pltpu.make_async_copy(
                held.at[g % 2, k],
                out.at[rows, :, :, pl.ds(pl.multiple_of(places[k], LANES), LANES)],
                sems.at[g % 2, k],
            )
            for k in range(2)
        ]

    zero = jnp.zeros((k1, 2 * LANES), BF16)
    for g in range(steps):
        if g >= 2:
            for copy in writes(g - 2):
                copy.wait()
        for j in range(img // COLS):
            pieces = []
            for yrel in range(STEP + 1):
                for p in range(NEAR):
                    x, y = 3 * j - 1 + p, STEP * (start + g) + yrel
                    if 0 <= x < side:
                        pair = [mine[y - mine_at, x], other[y - other_at, x]]
                        pieces.append(jnp.concatenate(pair, axis=1))
                    else:
                        pieces.append(zero)
            got = dot(band[...], jnp.concatenate(pieces, axis=0))
            for k in range(4 * STEP):
                at = slice(k * line, (k + 1) * line)
                span = slice(j * line, (j + 1) * line)
                flat[g % 2, 0, k, span, :] = got[at, :LANES]
                flat[g % 2, 1, k, span, :] = got[at, LANES:]
        for copy in writes(g):
            copy.start()

    def finish():
        for g in range(max(steps - 2, 0), steps):
            for copy in writes(g):
                copy.wait()

    return finish


def pixels_kernel(section, band, mine, other_far, after, done, out, token, held, other, sems, *, start):
    steps = other.shape[0] // STEP
    fetch = pltpu.make_async_copy(
        other_far.at[STEP * start : STEP * (start + steps) + 1], other, sems.at[2, 0]
    )
    fetch.start()
    token[...] = jnp.zeros_like(token)
    fetch.wait()
    draw_steps(
        section, band, mine, 0, other, STEP * start, out, held, sems, start, steps
    )()


def two_parts(value):
    high = value.astype(BF16).astype(F32)
    return jnp.concatenate([high, value - high], axis=0).astype(BF16)


def one_part(pair):
    rows = pair.shape[0] // 2
    pair = pair.astype(F32)
    return pair[:rows] + pair[rows:]


def merge_kernel(keep, recv_one, recv_two, small, c2, sums, out_far, lines, out, sems):
    members = out.shape[0]
    size = keep.shape[0] // members
    lines[...] = small[...]
    lines[AT_B1, :] = sums[0:1, :]
    lines[AT_B2, :] = sums[1:2, :]
    for k in range(members):
        at = slice(k * size, (k + 1) * size)
        recv, here = recv_one, k
        if k >= members // 2:
            recv, here = recv_two, k - members // 2
        got = recv[here * size : (here + 1) * size, :]
        out[k, 0:size, :] = (keep[at, :].astype(F32) + got.astype(F32)).astype(BF16)
        if k < members // 2:
            rows, span = c2_place(k)
            out[k, size:, :] = c2[rows, span].astype(BF16)
        else:
            out[k, size:, :] = two_parts(lines[table_place(k), :])
        pltpu.make_async_copy(out.at[k], out_far.at[k], sems.at[k]).start()
    for k in range(members):
        pltpu.make_async_copy(out.at[k], out_far.at[k], sems.at[k]).wait()


def c2_place(k):
    return slice(k % 2 * SHORT, (k % 2 + 1) * SHORT), slice(k // 2 * LANES, (k // 2 + 1) * LANES)


def table_place(k):
    at = (k - CUBE // 2) * SHORT // 2
    return slice(at, at + SHORT // 2)


def riders(batch, parts):
    plain = sum(p.astype(F32) for p in parts).astype(BF16)
    fine = two_parts(sum(one_part(p) for p in parts))
    return jnp.where(batch[0] % CUBE < CUBE // 2, plain.astype(F32), fine.astype(F32)).astype(BF16)


def cube_kernel(batch, got, c1, out):
    members = got.shape[0]
    size = got.shape[1] - SHORT
    out[0:size, :] = sum(got[k, 0:size, :].astype(F32) for k in range(members)).astype(BF16)
    out[size : size + SHORT, :] = riders(batch, [got[k, size:, :] for k in range(members)])
    out[size + SHORT :, :] = c1[...]


def add_kernel(batch, a, b, after, out):
    size = a.shape[0] - SHORT - 32
    for span in (slice(0, size), slice(size + SHORT, a.shape[0])):
        out[span, :] = (a[span, :].astype(F32) + b[span, :].astype(F32)).astype(BF16)
    ride = slice(size, size + SHORT)
    out[ride, :] = riders(batch, [a[ride, :], b[ride, :]])


def relay_kernel(batch, *refs):
    parts, (one, two, out) = refs[:CUBE], refs[-3:]
    me = batch[0] % CUBE
    for k, part in enumerate(parts):
        out[me ^ k] = part[...]
    one[...] = out[: CUBE // 2]
    two[...] = out[CUBE // 2 :]


def piece_of(got, k):
    count = got[0].shape[0]
    return got[k // count].at[k % count]


def unpack_half(which, got, lw, bw, vw, stage, stage_b, sems):
    members = 2 * got[0].shape[0]
    size = stage.shape[0] // members
    linear_rows, width = lw.shape
    options = bw.shape[0]
    half = (linear_rows + options * width + width) // 2
    rest = linear_rows - half
    group = options // 3

    def first_copies():
        spans = [(k * size, min((k + 1) * size, half)) for k in range(members)]
        return [
            pltpu.make_async_copy(stage.at[a:b], lw.at[a:b], sems.at[k])
            for k, (a, b) in enumerate(spans)
        ]

    def second_copies():
        copies = [pltpu.make_async_copy(stage.at[0:rest], lw.at[half:], sems.at[0])]
        for k in range(options // group):
            part = slice(k * group, (k + 1) * group)
            copies.append(pltpu.make_async_copy(stage_b.at[part], bw.at[part], sems.at[1 + k]))
        last = stage.at[rest : rest + width]
        copies.append(pltpu.make_async_copy(last, vw, sems.at[len(copies)]))
        return copies

    @pl.when(which == 0)
    def _():
        for k, copy in enumerate(first_copies()):
            start, end = k * size, min((k + 1) * size, half)
            stage[start:end, :] = piece_of(got, k)[0 : end - start, :].astype(F32)
            copy.start()

    @pl.when(which == 1)
    def _():
        def rows(start, end):
            parts = []
            while start < end:
                k, at = start // size, start % size
                count = min(size - at, end - start)
                parts.append(piece_of(got, k)[at : at + count, :])
                start += count
            value = parts[0] if len(parts) == 1 else jnp.concatenate(parts, axis=0)
            return value.astype(F32)

        copies = second_copies()
        stage[0:rest, :] = rows(0, rest)
        copies[0].start()
        for o in range(options):
            stage_b[o] = rows(rest + o * width, rest + (o + 1) * width)
            if o % group == group - 1:
                copies[1 + o // group].start()
        at = rest + options * width
        stage[rest : rest + width, :] = rows(at, at + width)
        copies[-1].start()

    def finish():
        for half_at, copies in ((0, first_copies), (1, second_copies)):

            @pl.when(which == half_at)
            def _():
                for copy in copies():
                    copy.wait()

    return finish


def own_kernel(section, one, two, lw, bw, vw, stage, stage_b, sems):
    unpack_half(section[0], (one, two), lw, bw, vw, stage, stage_b, sems)()


def unpack_kernel(section, *refs):
    mine, other, refs = refs[0:2], refs[2:4], refs[4:]
    lw, bw, vw = refs[3:6]
    little = (len(refs) - 10) // 2
    far, near = refs[6 : 6 + little], refs[6 + little : 6 + 2 * little]
    loss, c1, b1, c2, b2, lb, bb, hw, hb, vb, ow, ob = near
    stage, stage_b, lines, sems = refs[-4:]
    options = bw.shape[0]
    k1, k2 = c1.shape[0], c2.shape[0]
    size = stage.shape[0] // CUBE
    finish = unpack_half(1 - section[0], other, lw, bw, vw, stage, stage_b, sems)
    grad = [jnp.zeros((k1, LANES), F32) for _ in range(2)]
    ride = slice(size, size + SHORT)
    for k in range(CUBE):
        views = piece_of(mine, k), piece_of(other, k)
        if k < CUBE // 2:
            c2[c2_place(k)] = sum(v[ride, :].astype(F32) for v in views)
        else:
            lines[table_place(k), :] = sum(one_part(v[ride, :]) for v in views)
        for view in views:
            for h in range(2):
                at = size + SHORT + h * k1
                grad[h] += view[at : at + k1, :].astype(F32)
    for part in range(2):
        c1[:, part * LANES : (part + 1) * LANES] = grad[part]
    bb[...] = lines[0:options, :]
    vb[...] = lines[AT_VB, :]
    ow[...] = lines[AT_OW, :]
    hw[...] = lines[AT_HW, :]
    lb[...] = lines[AT_LB, :]
    scalars = lines[AT_SCALARS, :]
    loss[...] = scalars[:, 0:1]
    hb[...] = scalars[:, 1:3]
    ob[...] = scalars[:, 3:4]
    b1[...] = lines[AT_B1, 0:k1]
    b2[...] = lines[AT_B2, 0:k2]
    copies = [
        pltpu.make_async_copy(a, b, sems.at[CUBE + k]) for k, (a, b) in enumerate(zip(near, far))
    ]
    for copy in copies:
        copy.start()
    finish()
    for copy in copies:
        copy.wait()


def numbers_kernel(
    options,
    depth,
    targets,
    destination,
    b1,
    b2,
    lb,
    bb,
    hw,
    vb,
    ow,
    hb,
    ob,
    out,
    table,
):
    levels, kinds = options.shape[0], targets.shape[0]
    slots = depth.shape[1]
    rows = [options[...].astype(F32), depth[...].astype(F32)]
    rows += [targets[k] for k in range(kinds)]
    rows.append(jnp.zeros((LANES - levels - 1 - kinds * levels, slots), F32))
    out[...] = jnp.transpose(jnp.concatenate(rows, axis=0))
    table[...] = jnp.zeros_like(table)
    table[0 : bb.shape[0], :] = bb[...]
    table[AT_VB, :] = vb[...]
    table[AT_OW, :] = ow[...].astype(F32)
    table[AT_HW, :] = hw[...].astype(F32)
    table[AT_LB, :] = lb[...]
    table[AT_B1, 0 : b1.shape[1]] = b1[...]
    table[AT_B2, 0 : b2.shape[1]] = b2[...]
    lane = iota((1, LANES), 1)
    scalars = jnp.zeros((1, LANES), F32)
    for k, value in ((1, hb[:, 0:1]), (2, hb[:, 1:2]), (3, ob[...])):
        scalars = jnp.where(lane == k, value, scalars)
    table[AT_SCALARS, :] = scalars
    for k in range(slots // LANES):
        part = destination[:, k * LANES : (k + 1) * LANES]
        table[AT_DEST + k : AT_DEST + k + 1, :] = part.astype(F32)


def whole(shape):
    zeros = (0,) * len(shape)
    return pl.BlockSpec(shape, lambda *_: zeros)


ANYWHERE = pl.BlockSpec(memory_space=pl.ANY)
SCALARS = pl.BlockSpec(memory_space=pltpu.SMEM)


def params():
    return pltpu.CompilerParams(vmem_limit_bytes=VMEM_BYTES)


def shape_of(*shape, dtype=F32):
    return jax.ShapeDtypeStruct(shape, dtype)


def cost(microseconds):
    return pl.CostEstimate(
        flops=int(1.1e9 * microseconds), bytes_accessed=int(3.6e6 * microseconds), transcendentals=0
    )


def stays(value):
    return pltpu.with_memory_space_constraint(value, pltpu.HBM)


def held_near(value):
    return pltpu.with_memory_space_constraint(value, pltpu.VMEM)


def encode(section, frames, w1t, w2t, lw, table):
    img = frames.shape[0]
    blocks = img // 4
    side = blocks - 1
    k1, k2, width = w1t.shape[0], w2t.shape[0], lw.shape[1]
    flat = lw.shape[0]
    vmem = pltpu.VMEM
    near = pl.BlockSpec(memory_space=vmem)
    grid_one = (blocks, side, k1, LANES)
    return pl.pallas_call(
        encode_kernel,
        in_specs=[SCALARS, ANYWHERE, near, near, ANYWHERE, near],
        out_specs=[ANYWHERE] * 3 + [near] * 3,
        out_shape=(
            pltpu.HBM(grid_one, BF16),
            pltpu.HBM(grid_one, BF16),
            pltpu.HBM((flat, LANES), BF16),
            shape_of(flat, LANES, dtype=BF16),
            shape_of(width, LANES, dtype=BF16),
            shape_of(width, LANES),
        ),
        scratch_shapes=[
            vmem((img, img, frames.shape[2], LANES), BF16),
            vmem(lw.shape, BF16),
            vmem(grid_one, BF16),
            vmem(grid_one, BF16),
            vmem((flat, LANES), BF16),
            vmem((2 * REACH * k1, 256), BF16),
            vmem((2 * k1, 64), BF16),
            vmem((6 * k2, LANES), BF16),
            vmem((k1, LANES), F32),
            vmem((k2, LANES), F32),
            vmem((side, k1, LANES), F32),
            vmem((side // 2 - 1, k2, LANES), F32),
            pltpu.SemaphoreType.DMA((4, max(blocks // STEP, 3))),
        ],
        compiler_params=params(),
        cost_estimate=cost(9),
        name="encode",
    )(section, frames, w1t, w2t, lw, table)


def plan(section, slots, enc, s3, h2, branch_w, value_w, table, per_pair, depth, half_rows):
    width = enc.shape[0]
    options = branch_w.shape[0]
    two = 2 * width
    pairs = options // 2
    outs = (
        shape_of(half_rows, LANES, dtype=BF16),
        shape_of(half_rows // 2, LANES, dtype=BF16),
        shape_of(half_rows // 2, LANES, dtype=BF16),
        shape_of(TABLE, LANES),
        shape_of(width, LANES, dtype=BF16),
    )
    vmem = pltpu.VMEM
    near = pl.BlockSpec(memory_space=vmem)
    return pl.pallas_call(
        functools.partial(plan_kernel, per_pair=per_pair, depth=depth),
        in_specs=[SCALARS, near, near, near, near, ANYWHERE, near, near],
        out_shape=outs,
        scratch_shapes=[
            vmem((2, half_rows, LANES), BF16),
            vmem((options * width, width + 16), BF16),
            vmem((width + 16, width + 16), BF16),
            vmem((width, width + 16), BF16),
            vmem((width, LANES), F32),
            vmem((16, LANES), F32),
            vmem((options * width, LANES), F32),
            vmem((depth, options * width, LANES), F32),
            vmem((depth, pairs, width, two), F32),
            vmem((depth, pairs, width + 16, two), BF16),
            vmem((depth, pairs, width, two), BF16),
            vmem((depth, options * width, LANES), BF16),
            vmem(branch_w.shape, BF16),
            pltpu.SemaphoreType.DMA,
        ],
        compiler_params=params(),
        cost_estimate=cost(11),
        name="plan",
    )(section, slots, enc, s3, h2, branch_w, value_w, table)


def back(g3, lw, s2, s1, h1, w2t):
    _, side, k1 = s1.shape[:3]
    k2 = w2t.shape[0]
    inner = side // 2 - 1
    padded = (side + 2, side, k1, LANES)
    near = pl.BlockSpec(memory_space=pltpu.VMEM)
    return pl.pallas_call(
        back_kernel,
        in_specs=[near] * 6,
        out_shape=(shape_of(*padded, dtype=BF16), shape_of(k2, 256), shape_of(8, LANES)),
        scratch_shapes=[
            pltpu.VMEM((LANES, 6 * k2), BF16),
            pltpu.VMEM((inner + 2, inner, k2, LANES), BF16),
        ],
        compiler_params=params(),
        cost_estimate=cost(25),
        name="back",
    )(g3, lw, s2, s1, h1, w2t)


def first(section, frames, g1, w1t, other, after, channels, draw):
    img, _, stack, _ = frames.shape
    k1 = g1.shape[2]
    band = (STEP * 4 * COLS * channels, (STEP + 1) * NEAR * k1)
    near = pl.BlockSpec(memory_space=pltpu.VMEM)
    return pl.pallas_call(
        functools.partial(first_kernel, draw=draw),
        in_specs=[SCALARS, ANYWHERE, near, near, ANYWHERE, ANYWHERE],
        out_specs=[near, ANYWHERE, near],
        out_shape=[
            shape_of(2 * k1, LANES, dtype=BF16),
            shape_of(img, img, channels, 2 * LANES),
            shape_of(*band, dtype=BF16),
        ],
        scratch_shapes=[
            pltpu.VMEM((img, img, stack, LANES), BF16),
            pltpu.VMEM((STEP * 4 * COLS * stack, (STEP + 1) * NEAR * k1), F32),
            pltpu.VMEM((STEP * draw + 1,) + g1.shape[1:], BF16),
            pltpu.VMEM((2, 2, 4 * STEP, img, channels, LANES), F32),
            pltpu.SemaphoreType.DMA((img // 4 // STEP + 1,)),
            pltpu.SemaphoreType.DMA((2, 2)),
        ],
        compiler_params=params(),
        cost_estimate=cost(45),
        name="first",
    )(section, frames, g1, w1t, other, after)


def pixels(section, band, mine, other, after, done, start, steps):
    img, _, channels, _ = done.shape
    near = pl.BlockSpec(memory_space=pltpu.VMEM)
    return pl.pallas_call(
        functools.partial(pixels_kernel, start=start),
        in_specs=[SCALARS, near, near, ANYWHERE, ANYWHERE, ANYWHERE],
        out_specs=[ANYWHERE, near],
        out_shape=[shape_of(*done.shape), shape_of(8, LANES)],
        scratch_shapes=[
            pltpu.VMEM((2, 2, 4 * STEP, img, channels, LANES), F32),
            pltpu.VMEM((STEP * steps + 1,) + mine.shape[1:], BF16),
            pltpu.SemaphoreType.DMA((3, 2)),
        ],
        input_output_aliases={5: 0},
        compiler_params=params(),
        cost_estimate=cost(1 + 0.9 * steps),
        name="pixels",
    )(section, band, mine, other, after, done)


def small_call(
    kernel, outs, operands, scratch=(), name=None, place=None, after=(), weight=0.3, far=False
):
    specs = [pl.BlockSpec(memory_space=pltpu.VMEM)] * len(operands)
    if place is not None:
        operands = (*place, *operands)
        specs = [pl.BlockSpec(memory_space=pltpu.SMEM)] * len(place) + specs
    return pl.pallas_call(
        kernel,
        in_specs=specs + [ANYWHERE] * len(after),
        out_specs=jax.tree.map(
            lambda _: ANYWHERE if far else pl.BlockSpec(memory_space=pltpu.VMEM), outs
        ),
        out_shape=outs,
        scratch_shapes=list(scratch),
        compiler_params=params(),
        cost_estimate=cost(weight),
        name=name,
    )(*operands, *after)


def round_up(value, step):
    return -(-value // step) * step


def swapped(value):
    return lax.ppermute(value, "section", [(0, 1), (1, 0)])


def exchanged(value, groups=None):
    return lax.all_to_all(
        value, "batch", split_axis=0, concat_axis=0, axis_index_groups=groups, tiled=True
    )


def partner(value, distance):
    count = lax.axis_size("batch")
    return lax.ppermute(value, "batch", [(b, b ^ distance) for b in range(count)])


def local(
    frames,
    destination,
    options,
    depth,
    targets,
    conv_one,
    bias_one,
    conv_two,
    bias_two,
    linear_w,
    linear_b,
    branch_w,
    branch_b,
    head_w,
    head_b,
    value_w,
    value_b,
    out_w,
    out_b,
):
    section = lax.axis_index("section").astype(jnp.int32)[None]
    peers = lax.axis_size("batch")
    frame_count = frames.shape[3]
    per_pair = frame_count // peers
    levels = options.shape[0]
    frames = stays(frames.transpose(1, 2, 0, 3))
    w1t, w2t = stays(conv_one.T), stays(conv_two.T)
    branch_w, value_w = stays(branch_w), stays(value_w)
    encoder_params = (w1t, bias_one, w2t, bias_two, linear_w, linear_b)
    planner_params = (branch_w, branch_b, head_w.T, head_b, value_w, value_b, out_w.T, out_b)
    width = linear_w.shape[1]
    big_rows = linear_w.shape[0] + (branch_w.shape[0] + 1) * width
    size = round_up(-(-big_rows // (2 * CUBE)), 16)

    tiny = (bias_one, bias_two, linear_b, branch_b, head_w.T, value_b, out_w.T)
    tiny = [stays(v if v.ndim > 1 else v[None, :]) for v in tiny]
    numbers, table = pl.pallas_call(
        numbers_kernel,
        in_specs=[pl.BlockSpec(memory_space=pltpu.VMEM)] * (6 + len(tiny)),
        out_shape=[shape_of(frame_count, LANES), shape_of(TABLE, LANES)],
        compiler_params=params(),
        cost_estimate=cost(1),
        name="numbers",
    )(
        stays(options),
        stays(depth[None, :]),
        stays(targets),
        stays(destination[None, :]),
        *tiny,
        stays(head_b[None, :]),
        out_b[None, :],
    )
    slots = exchanged(numbers.reshape(peers, per_pair, LANES)).reshape(frame_count, LANES)

    h1, s1, s2, h2, enc, s3 = encode(section, frames, w1t, w2t, stays(linear_w), table)
    keep, send_one, send_two, small, g3 = plan(
        section, slots, enc, s3, h2, branch_w, value_w, table, per_pair, levels, CUBE * size
    )
    recv = swapped(send_one), swapped(send_two)
    channels = frames.shape[2] // lax.axis_size("section")
    g1, c2, sums = back(g3, linear_w, s2, s1, h1, w2t)
    other = swapped(g1)
    g1 = held_near(g1)
    place = (lax.axis_index("batch").astype(jnp.int32)[None],)
    cubes = [list(range(c, c + CUBE)) for c in range(0, peers, CUBE)]
    bf16 = functools.partial(shape_of, dtype=BF16)
    pieces = small_call(
        merge_kernel,
        bf16(CUBE, size + SHORT, LANES),
        (keep, *recv, small, c2, sums),
        [
            pltpu.VMEM((TABLE, LANES), F32),
            pltpu.VMEM((CUBE, size + SHORT, LANES), BF16),
            pltpu.SemaphoreType.DMA((CUBE,)),
        ],
        name="merge",
        far=True,
        weight=30,
    )
    got = exchanged(pieces, cubes)
    c1, frames_grad, band = first(section, frames, g1, w1t, other, pieces, channels, DRAW)
    piece = bf16(size + SHORT + c1.shape[0], LANES)
    keep = small_call(cube_kernel, piece, (got, c1), name="cube", place=place)
    distance = CUBE
    while distance < peers:
        recv = partner(keep, distance)
        if distance == CUBE:
            left = frames.shape[0] // 4 // STEP - DRAW
            frames_grad, token = pixels(
                section, band, g1, other, keep, frames_grad, DRAW, left
            )
        distance *= 2
        keep = small_call(
            add_kernel, piece, (keep, recv), name="add", place=place, after=(token,)
        )
    parts = [keep] + [partner(keep, k) for k in range(1, CUBE)]
    got = small_call(
        relay_kernel,
        [bf16(CUBE // 2, *piece.shape)] * 2,
        parts,
        [pltpu.VMEM((CUBE, *piece.shape), BF16)],
        name="relay",
        place=place,
    )
    got_other = [swapped(v) for v in got]
    shapes = [p.shape for p in encoder_params + planner_params]
    near = pl.BlockSpec(memory_space=pltpu.VMEM)
    flat = [shape_of(*(v if len(v) > 1 else (1,) + v)) for v in [(1, 1)] + shapes]
    large = [flat[k] for k in (5, 7, 11)]
    staged = [
        pltpu.VMEM((CUBE * size, LANES), F32),
        pltpu.VMEM(branch_w.shape, F32),
    ]
    little = [v for k, v in enumerate(flat) if k not in (5, 7, 11)]
    sems = pltpu.SemaphoreType.DMA((CUBE + len(little),))
    begun = pl.pallas_call(
        own_kernel,
        in_specs=[SCALARS, near, near],
        out_specs=[ANYWHERE] * 3,
        out_shape=large,
        scratch_shapes=[*staged, sems],
        compiler_params=params(),
        cost_estimate=cost(1),
        name="own",
    )(section, *got)
    ends = pl.pallas_call(
        unpack_kernel,
        in_specs=[SCALARS] + [near] * 4 + [ANYWHERE] * 3,
        out_specs=[ANYWHERE] * (3 + len(little)),
        out_shape=large + little,
        scratch_shapes=[pltpu.VMEM(v.shape, F32) for v in little]
        + [*staged, pltpu.VMEM((TABLE, LANES), F32), sems],
        input_output_aliases={5: 0, 6: 1, 7: 2},
        compiler_params=params(),
        cost_estimate=cost(1.5),
        name="unpack",
    )(section, *got, *got_other, *begun)
    rest = list(ends[3:])
    for k, at in enumerate((5, 7, 11)):
        rest.insert(at, ends[k])
    rest = [v.reshape(s) for v, s in zip(rest, [()] + shapes)]
    for at in (1, 3, 9, 13):
        rest[at] = rest[at].T
    return (rest[0], frames_grad.transpose(2, 0, 1, 3), *rest[1:])


def solution(mesh):
    placed = (
        P(None, None, None, "batch"),
        P("batch"),
        P(None, "batch"),
        P("batch"),
        P(None, None, "batch"),
    ) + (P(),) * 14
    return jax.shard_map(
        local,
        mesh=mesh,
        in_specs=placed,
        out_specs=(P(), P("section", None, None, "batch")) + (P(),) * 14,
        check_vma=False,
    )
```

```python
import functools
import math

import jax
import jax.numpy as jnp
from jax import lax
from jax.experimental import pallas as pl
from jax.experimental.pallas import tpu as pltpu
from jax.sharding import PartitionSpec as P

BF16 = jnp.bfloat16
F32 = jnp.float32
EXACT = lax.Precision.HIGHEST
LANES = 128
VMEM_BYTES = 32 * 1024 * 1024
TILE = 16
REACH = 5
STEP = 3
COLS = 12
NEAR = 4
AT_VB, AT_OW, AT_HW, AT_LB, AT_SCALARS, AT_B1, AT_B2, AT_DEST = (
    slice(18, 19),
    slice(19, 20),
    slice(20, 22),
    slice(22, 23),
    slice(23, 24),
    slice(24, 25),
    slice(25, 26),
    26,
)
TABLE = 32
CUBE = 8
DRAW = 3
DRAW_ACROSS = 3
SHORT = 16


def dot(a, b, precision=None):
    return jnp.dot(a, b, preferred_element_type=F32, precision=precision)


def dot_rows(a, b, precision=None):
    return lax.dot_general(
        a, b, (((0,), (0,)), ((), ())), preferred_element_type=F32, precision=precision
    )


def dot_lanes(a, b, precision=None):
    return lax.dot_general(
        a, b, (((1,), (1,)), ((), ())), preferred_element_type=F32, precision=precision
    )


def iota(shape, axis):
    return lax.broadcasted_iota(jnp.int32, shape, axis)


def column(row):
    n = row.shape[1]
    wide = jnp.broadcast_to(row, (n, n))
    return jnp.sum(jnp.where(iota((n, n), 0) == iota((n, n), 1), wide, 0.0), axis=1, keepdims=True)


def row_of(col):
    n = col.shape[0]
    wide = jnp.broadcast_to(col, (n, n))
    return jnp.sum(jnp.where(iota((n, n), 0) == iota((n, n), 1), wide, 0.0), axis=0, keepdims=True)


def soft(x):
    t = jnp.tanh(0.5 * x)
    return jnp.maximum(x, 0.0) - jnp.log(0.5 + 0.5 * jnp.abs(t)), 1.0 + t


def silu_pair(y):
    t = jnp.tanh(y)
    m = y * t
    return y + m, (1.0 + t) + (y - m * t)


def pixel_order(w1t):
    tap, pix = iota((256, 256), 0), iota((256, 256), 1)
    moves = ((tap >> 6) == (pix & 3)) & ((tap & 63) == (pix >> 2))
    return dot(w1t, moves.astype(F32).astype(BF16))


def frame_copies(section, far, here, sems):
    lanes = pl.ds(pl.multiple_of(section[0] * LANES, LANES), LANES)
    size = 4 * STEP

    def copy(g):
        rows = pl.ds(pl.multiple_of(g * size, size), size)
        return pltpu.make_async_copy(far.at[rows, :, :, lanes], here.at[rows], sems.at[g])

    return copy


def tile_rows(frames, row, j, cols):
    img, _, channels, _ = frames.shape
    flat = frames.reshape(img, img * channels, LANES)
    size = cols * channels
    end = min((j + 1) * size, img * channels)
    part = flat[pl.ds(row, 4), j * size : end, :]
    return part.reshape(4 * (end - j * size), LANES)


def encode_kernel(
    section,
    frames_far,
    w1t,
    w2t,
    lw_far,
    table,
    h1_far,
    s1_far,
    s2_far,
    h2,
    enc,
    s3,
    frames,
    lw,
    h1,
    s1,
    s2,
    band,
    edge,
    band2,
    bias1,
    bias2,
    held,
    held2,
    sems,
):
    blocks, side = h1.shape[:2]
    steps = blocks // STEP
    tiles = frames.shape[1] // TILE
    k1, k2 = w1t.shape[0], w2t.shape[0]
    reach_rows = REACH * k1
    arrives = frame_copies(section, frames_far, frames, sems.at[0])
    for g in range(steps):
        arrives(g).start()
    last_copies = [
        pltpu.make_async_copy(lw_far, lw, sems.at[3, 0]),
        pltpu.make_async_copy(s2, s2_far, sems.at[3, 1]),
    ]
    last_copies[0].start()

    def leaves(g):
        rows = pl.ds(g * STEP, STEP)
        return [
            pltpu.make_async_copy(h1.at[rows], h1_far.at[rows], sems.at[1, g]),
            pltpu.make_async_copy(s1.at[rows], s1_far.at[rows], sems.at[2, g]),
        ]

    inner = side // 2 - 1
    row_len = inner * k2
    two = 2 * k2 * 3

    def prepare():
        taps = pixel_order(w1t[...])
        edges = []
        for half in range(2):
            lines = [taps[:, 32 * (4 * half + u) : 32 * (4 * half + u + 1)] for u in range(4)]
            for place in range(REACH):
                pieces = []
                for line in lines:
                    start = 16 * (place - 1)
                    cut = line[:, max(0, -start) : min(32, 64 - start)]
                    start = max(start, 0)
                    pieces += [jnp.zeros((k1, start), F32)] if start else []
                    pieces.append(cut)
                    rest = 64 - start - cut.shape[1]
                    pieces += [jnp.zeros((k1, rest), F32)] if rest else []
                at = half * reach_rows + place * k1
                band[at : at + k1, :] = jnp.concatenate(pieces, axis=1).astype(BF16)
            edges.append(jnp.concatenate([line[:, 16:] for line in lines], axis=1))
        edge[...] = jnp.concatenate(edges, axis=0).astype(BF16)
        tap, pix = iota((256, LANES), 0), iota((256, LANES), 1)
        for half in range(2):
            for place in range(3):
                hit = (
                    ((tap & 15) == (pix & 15))
                    & ((tap >> 6) == (pix >> 6) + 2 * half)
                    & (((tap >> 4) & 3) == ((pix >> 4) & 3) + 2 - 2 * place)
                )
                at = (half * 3 + place) * k2
                taps = dot(w2t[...], hit.astype(F32).astype(BF16))
                band2[at : at + k2, :] = taps.astype(BF16)
        bias1[...] = jnp.broadcast_to(column(table[AT_B1, 0:k1]), bias1.shape)
        bias2[...] = jnp.broadcast_to(column(table[AT_B2, 0:k2]), bias2.shape)
        held[...] = jnp.zeros_like(held)
        held2[...] = jnp.zeros_like(held2)
        h1[...] = jnp.zeros_like(h1)

    def added(sums, x, value):
        sums[x] = sums[x] + value if x in sums else value

    def second_matmul(b):
        tiles = [
            h1[pl.ds(2 * b + 1, 2), 4 * j : 4 * j + 4].reshape(LANES, LANES)
            for j in range(side // 4)
        ]
        return dot(band2[...], jnp.concatenate(tiles, axis=1))

    def second_rows(b, got):
        low, high = {}, {}
        for j in range(side // 4):
            for place in range(3):
                x = 2 * j - 1 + place
                if 0 <= x < inner:
                    span = slice(j * LANES, (j + 1) * LANES)
                    at = place * k2
                    added(low, x, got[at : at + k2, span])
                    added(high, x, got[two // 2 + at : two // 2 + at + k2, span])
        row = jnp.maximum(b - 1, 0) * row_len
        for x in range(inner):
            value, slope = soft(held2[x] + high[x] + bias2[...])
            held2[x] = low[x]
            at = pl.ds(pl.multiple_of(row + x * k2, k2), k2)
            h2[at, :] = value.astype(BF16)
            s2[at, :] = slope.astype(BF16)

    def one_step(g, carry):
        def row(r):
            return pl.multiple_of(4 * (STEP * g + r), 4)

        arrives(g).wait()
        lows, highs = [{} for _ in range(STEP)], [{} for _ in range(STEP)]

        def place_tile(r, j, got):
            for place in range(REACH):
                x = 4 * j - 1 + place
                if 0 <= x < side:
                    at = place * k1
                    added(lows[r], x, got[at : at + k1])
                    added(highs[r], x, got[reach_rows + at : reach_rows + at + k1])

        def finish(r, xs):
            for x in xs:
                value, slope = soft(held[x] + highs[r][x] + bias1[...])
                held[x] = lows[r][x]
                h1[STEP * g + r, x] = value.astype(BF16)
                s1[STEP * g + r, x] = slope.astype(BF16)

        pair = jnp.maximum(g - 1, 0)
        units = [(lambda: second_matmul(pair), lambda got: second_rows(pair, got))]

        def edges():
            parts = [tile_rows(frames, row(r), tiles, TILE) for r in range(STEP)]
            return dot(edge[...], jnp.concatenate(parts, axis=1))

        def place_edges(got):
            for r in range(STEP):
                added(lows[r], side - 1, got[:k1, r * LANES : (r + 1) * LANES])
                added(highs[r], side - 1, got[k1:, r * LANES : (r + 1) * LANES])

        units.append((edges, place_edges))

        def full(spots):
            parts = [tile_rows(frames, row(r), j, TILE) for r, j in spots]
            return dot(band[...], jnp.concatenate(parts, axis=1))

        def place_full(got, spots, ready):
            for i, (r, j) in enumerate(spots):
                place_tile(r, j, got[:, i * LANES : (i + 1) * LANES])
            if ready:
                finish(*ready)

        for r in range(STEP):
            if r % 2 == 0:
                spots = [(k, tiles - 1) for k in (r, r + 1) if k < STEP]
                units.append(
                    (
                        functools.partial(full, spots),
                        functools.partial(place_full, spots=spots, ready=None),
                    )
                )
            done = 0
            for j in range(0, tiles - 1, 2):
                spots = [(r, j), (r, j + 1)]
                ready = side if j + 2 == tiles - 1 else 4 * j + 7
                units.append(
                    (
                        functools.partial(full, spots),
                        functools.partial(place_full, spots=spots, ready=(r, range(done, ready))),
                    )
                )
                done = ready
        waiting = None
        for issue, take in units:
            got = issue()
            if waiting is not None:
                waiting[0](waiting[1])
            waiting = (take, got)
        waiting[0](waiting[1])
        for copy in leaves(g):
            copy.start()
        return carry

    prepare()
    lax.fori_loop(0, steps, one_step, 0)
    for b in range(steps - 1, side // 2):
        second_rows(b, second_matmul(b))
    for copy in last_copies[1:]:
        copy.start()
    last_copies[0].wait()
    value, slope = soft(dot_rows(lw[...], h2[...]) + column(table[AT_LB, :]))
    enc[...] = value.astype(BF16)
    s3[...] = 0.5 * slope
    for g in range(steps):
        for copy in leaves(g):
            copy.wait()
    for copy in last_copies[1:]:
        copy.wait()


def three_parts(row):
    high = row.astype(BF16).astype(F32)
    middle = (row - high).astype(BF16).astype(F32)
    return jnp.concatenate([high, middle, row - high - middle], axis=0)


def with_ones(value):
    return jnp.concatenate([value, ones_rows(value.shape[1])], axis=0)


def ones_rows(lanes):
    return (iota((16, lanes), 0) < 3).astype(F32).astype(BF16)


def plan_kernel(
    section,
    slots,
    enc,
    s3,
    h2,
    branch_far,
    value_w,
    table,
    keep,
    send_one,
    send_two,
    small,
    g3,
    parts,
    bwt,
    vht,
    vhw,
    ow,
    mine,
    pre,
    dbr,
    dval,
    low,
    hid,
    gb,
    branch_w,
    sem,
    *,
    per_pair,
    depth,
):
    width = enc.shape[0]
    options = branch_w.shape[0]
    pairs = options // 2
    two = 2 * width
    sec = section[0]
    branch_copy = pltpu.make_async_copy(branch_far, branch_w, sem)
    branch_copy.start()

    count = slots.shape[0]
    dest = jnp.concatenate(
        [table[AT_DEST + k : AT_DEST + k + 1, :] for k in range(count // LANES)], axis=1
    )
    own = jnp.where(sec == 0, dest[:, :LANES], dest[:, LANES:])
    others = jnp.transpose(jnp.broadcast_to(dest, (LANES, count)))
    index = iota((count, LANES), 1) + sec * LANES
    earlier = (others == own) & (iota((count, LANES), 0) < index)
    rank = jnp.sum(earlier.astype(F32), axis=0, keepdims=True)
    bucket = own * float(per_pair) + rank
    chosen = (iota((count, LANES), 0).astype(F32) == bucket).astype(F32).astype(BF16)
    numbers = slots[:, : mine.shape[0]]
    high = numbers.astype(BF16)
    middle = (numbers - high.astype(F32)).astype(BF16)
    rest = (numbers - high.astype(F32) - middle.astype(F32)).astype(BF16)
    mine[...] = sum(dot_rows(v, chosen) for v in (rest, middle, high))

    pad = jnp.zeros((13, width), F32)
    branch_copy.wait()
    for o in range(options):
        rows = [branch_w[o].astype(F32), three_parts(table[o : o + 1, :]), pad]
        bwt[o * width : (o + 1) * width, :] = jnp.transpose(
            0.5 * jnp.concatenate(rows, axis=0)
        ).astype(BF16)
    scalars = table[AT_SCALARS, :]
    head_w = table[AT_HW, :]
    rows = [value_w[...].astype(F32), three_parts(table[AT_VB, :]), pad]
    vht[0:width, :] = jnp.transpose(0.5 * jnp.concatenate(rows, axis=0)).astype(BF16)
    vht[width:, :] = jnp.zeros((16, width + 16), BF16)
    lane = iota((1, 16), 1)
    for k in range(2):
        bias = three_parts(jnp.broadcast_to(scalars[:, 1 + k : 2 + k], (1, 16)))
        bias = sum(jnp.where(lane == j, bias[j : j + 1], 0.0) for j in range(3))
        vht[width + k : width + k + 1, 0:width] = head_w[k : k + 1].astype(BF16)
        vht[width + k : width + k + 1, width:] = bias.astype(BF16)
    vhw[:, 0:width] = (0.5 * value_w[...].astype(F32)).astype(BF16)
    vhw[:, width:] = jnp.transpose(
        0.5 * jnp.concatenate([head_w, jnp.zeros((14, width), F32)], axis=0)
    ).astype(BF16)
    ow[...] = jnp.broadcast_to(column(table[AT_OW, :]), (width, LANES))
    wide_ow = jnp.concatenate([ow[...], ow[...]], axis=1)
    half_ow = 0.5 * wide_ow

    labels = iota((options, LANES), 0).astype(F32)
    state = enc[...].astype(F32)
    rounded_all, saved = [], []
    group = 3
    for level in range(depth):
        picked = labels == mine[level : level + 1, :]
        rounded = state.astype(BF16)
        rounded_all.append(rounded)
        met = with_ones(rounded)

        def branches(first):
            at = slice(first * two, (first + group) * two)
            pre[at, :] = dot(bwt[at, :], met)

        branches(0)
        following = state
        reward, discount, value = [], [], []

        def value_part(t, got):
            act, slope = silu_pair(got[:width])
            dval[level, t] = slope
            hidden = act.astype(BF16)
            hid[level, t] = hidden
            worth = jnp.sum(hidden.astype(F32) * wide_ow, axis=0, keepdims=True)
            for k in range(2):
                span = slice(k * LANES, (k + 1) * LANES)
                value.append(worth[:, span])
                reward.append(got[width : width + 1, span])
                discount.append(got[width + 1 : width + 2, span])

        waiting = None
        for first in range(0, pairs, group):
            if first + group < pairs:
                branches(first + group)
            boths = []
            for t in range(first, first + group):
                at = slice(t * two, (t + 1) * two)
                act, slope = silu_pair(pre[at, :])
                dbr[level, at, :] = slope
                left = state + act[:width]
                right = state + act[width:]
                following = jnp.where(picked[2 * t : 2 * t + 1], left, following)
                following = jnp.where(picked[2 * t + 1 : 2 * t + 2], right, following)
                both = with_ones(
                    jnp.concatenate([left.astype(BF16), right.astype(BF16)], axis=1)
                )
                low[level, t] = both
                boths.append(both)
            got = dot(vht[...], jnp.concatenate(boths, axis=1))
            if waiting is not None:
                for k in range(group):
                    value_part(waiting[0] + k, waiting[1][:, k * two : (k + 1) * two])
            waiting = (first, got)
        for k in range(group):
            value_part(waiting[0] + k, waiting[1][:, k * two : (k + 1) * two])
        reward = jnp.concatenate(reward, axis=0)
        discount = jax.nn.sigmoid(jnp.concatenate(discount, axis=0))
        value = jnp.concatenate(value, axis=0) + scalars[:, 3:4]
        quality = reward + discount * value
        top = jnp.max(quality, axis=0, keepdims=True)
        shifted = jnp.exp(quality - top)
        total = jnp.sum(shifted, axis=0, keepdims=True)
        live = (mine[depth : depth + 1, :] > level).astype(F32)
        chosen = picked.astype(F32)

        def target(kind):
            at = depth + 1 + kind * depth + level
            return mine[at : at + 1, :]

        reward_gap = live * (jnp.sum(chosen * reward, axis=0, keepdims=True) - target(0))
        discount_gap = live * (jnp.sum(chosen * discount, axis=0, keepdims=True) - target(1))
        plan_gap = live * (top + jnp.log(total) - target(2))
        grad_quality = plan_gap * (shifted / total)
        head_two = (chosen * discount_gap + grad_quality * value) * discount * (1.0 - discount)
        saved.append(
            (
                picked,
                (chosen * reward_gap + grad_quality).astype(BF16).astype(F32),
                head_two.astype(BF16).astype(F32),
                (grad_quality * discount).astype(BF16).astype(F32),
                reward_gap * reward_gap + discount_gap * discount_gap + plan_gap * plan_gap,
            )
        )
        state = following

    out_sum = jnp.zeros((16, width), F32)
    value_sum = jnp.zeros((width + 16, width + 16), F32)
    grad_next = None
    line = iota((16, two), 0)
    for level in reversed(range(depth)):
        picked, head_one, head_two, grad_value, _ = saved[level]
        upward = jnp.zeros((width, LANES), F32)

        def branch_part(t, moved):
            at = slice(t * two, (t + 1) * two)
            left, right = moved[:, :LANES], moved[:, LANES:]
            if grad_next is not None:
                left = left + jnp.where(picked[2 * t : 2 * t + 1], grad_next, 0.0)
                right = right + jnp.where(picked[2 * t + 1 : 2 * t + 2], grad_next, 0.0)
            grad_branch = jnp.concatenate([left, right], axis=0) * dbr[level, at, :]
            grad_branch = grad_branch.astype(BF16)
            gb[level, at, :] = grad_branch
            return left + right

        def group_part(first, moved):
            parts = [
                branch_part(first + k, moved[:, k * two : (k + 1) * two]) for k in range(group)
            ]
            at = slice(first * two, (first + group) * two)
            weights = [branch_w[o] for o in range(2 * first, 2 * (first + group))]
            return sum(parts), dot(jnp.concatenate(weights, axis=1), gb[level, at, :])

        waiting = None
        for first in range(0, pairs, group):
            stack = []
            for t in range(first, first + group):

                def across(rows):
                    return jnp.concatenate(
                        [rows[2 * t : 2 * t + 1], rows[2 * t + 1 : 2 * t + 2]], axis=1
                    )

                worth = across(grad_value)
                grad_pre = (worth * half_ow * dval[level, t]).astype(BF16)
                heads = jnp.where(line == 0, across(head_one), 0.0)
                heads = jnp.where(line == 1, across(head_two), heads)
                heads = jnp.where(line == 2, worth, heads)
                heads = heads.astype(BF16)
                out_sum = out_sum + dot_lanes(heads, hid[level, t])
                stack.append(jnp.concatenate([grad_pre, heads], axis=0))
            stack = jnp.concatenate(stack, axis=1)
            moved = dot(vhw[...], stack)
            if waiting is not None:
                one, other = group_part(*waiting)
                upward = upward + (one + 0.5 * other)
            waiting = (first, moved)
            lows = jnp.concatenate([low[level, first + k] for k in range(group)], axis=1)
            value_sum = value_sum + dot_lanes(stack, lows)
        one, other = group_part(*waiting)
        grad_next = upward + (one + 0.5 * other)

    linear_rows = h2.shape[0]
    half = (linear_rows + options * width + width) // 2
    rest = linear_rows - half
    rounded = with_ones(jnp.concatenate(rounded_all, axis=1))
    small[...] = jnp.zeros_like(small)
    if half < keep.shape[0]:
        for k in range(2):
            parts[k, half:, :] = jnp.zeros((keep.shape[0] - half, LANES), BF16)
    for t in range(pairs):
        at = slice(t * two, (t + 1) * two)
        grads = jnp.concatenate([gb[level, at, :] for level in range(depth)], axis=1)
        got = dot_lanes(rounded, grads)
        for k in range(2):
            o = 2 * t + k
            span = slice(k * width, (k + 1) * width)
            rows = slice(rest + o * width, rest + (o + 1) * width)
            parts[1 - sec, rows, :] = got[:width, span].astype(BF16)
            small[o : o + 1, :] = got[width : width + 1, span]
    after = rest + options * width
    parts[1 - sec, after : after + width, :] = jnp.transpose(value_sum[:width, :width]).astype(BF16)

    grad_three = ((2.0 * grad_next).astype(BF16).astype(F32) * s3[...]).astype(BF16)
    g3[...] = grad_three
    chunk = linear_rows // 9
    for i in range(8):
        at = slice(i * chunk, (i + 1) * chunk)
        parts[sec, at, :] = dot_lanes(h2[at, :], grad_three).astype(BF16)
    last = dot_lanes(h2[8 * chunk :, :], grad_three).astype(BF16)
    parts[sec, 8 * chunk : half, :] = last[: half - 8 * chunk]
    parts[1 - sec, 0:rest, :] = last[half - 8 * chunk :]
    keep[...] = parts[0]
    send_one[...] = parts[1, : send_one.shape[0]]
    send_two[...] = parts[1, send_one.shape[0] :]

    small[AT_VB, :] = row_of(value_sum[:width, width : width + 1])
    small[AT_OW, :] = out_sum[2:3]
    small[AT_HW, :] = value_sum[width : width + 2, :width]
    small[AT_LB, :] = row_of(jnp.sum(grad_three.astype(F32), axis=1, keepdims=True))
    loss = 0.5 * jnp.sum(sum(kept[4] for kept in saved), axis=1, keepdims=True)
    ends = [loss] + [value_sum[width + k : width + k + 1, width : width + 1] for k in range(3)]
    lane = iota((1, LANES), 1)
    line = jnp.zeros((1, LANES), F32)
    for k, end in enumerate(ends):
        line = jnp.where(lane == k, end, line)
    small[AT_SCALARS, :] = line


def back_kernel(g3, lw, s2, s1, h1, w2t, g1, c2, sums, t2, g2):
    side, k1 = s1.shape[1], s1.shape[2]
    k2 = w2t.shape[0]
    inner = side // 2 - 1
    row_len = inner * k2
    half_g3 = (0.5 * g3[...].astype(F32)).astype(BF16)
    tap, pix = iota((LANES, 256), 1), iota((LANES, 256), 0)
    for yrel in range(2):
        for p in range(3):
            hit = (
                ((tap & 15) == (pix & 15))
                & ((tap >> 6) == (pix >> 6) + 2 * (1 - yrel))
                & (((tap >> 4) & 3) == ((pix >> 4) & 3) + 2 - 2 * p)
            )
            at = (yrel * 3 + p) * k2
            taps = dot_lanes(hit.astype(F32).astype(BF16), w2t[...])
            t2[:, at : at + k2] = (0.5 * taps).astype(BF16)
    g2[0] = jnp.zeros(g2.shape[1:], BF16)
    g2[inner + 1] = jnp.zeros(g2.shape[1:], BF16)
    g1[0] = jnp.zeros(g1.shape[1:], BF16)
    g1[side + 1] = jnp.zeros(g1.shape[1:], BF16)
    zero = jnp.zeros((k2, LANES), BF16)
    total_one = jnp.zeros((k1, LANES), F32)
    total_two = jnp.zeros((k2, LANES), F32)
    for y in range(inner):
        at = slice(y * row_len, (y + 1) * row_len)
        grad = dot(lw[at, :], half_g3) * s2[at, :].astype(F32)
        grad = grad.astype(BF16).reshape(inner, k2, LANES)
        g2[y + 1] = grad
        total_two = total_two + jnp.sum(grad.astype(F32), axis=0)
    reach, cols = 5, 8
    total = jnp.zeros((2 * reach * k2, 2 * cols * k1), F32)
    grads, tiles = [], []
    for b in range(side // 2):
        cut = []
        for j in range(side // 4):
            pieces = []
            for yrel in range(2):
                for p in range(3):
                    x = 2 * j - 1 + p
                    pieces.append(g2[b + yrel, x] if 0 <= x < inner else zero)
            cut.append(jnp.concatenate(pieces, axis=0))
        got = dot(t2[...], jnp.concatenate(cut, axis=1))
        for u in range(2):
            for j in range(side // 4):
                part = got[u * 64 : (u + 1) * 64, j * LANES : (j + 1) * LANES]
                slope = s1[2 * b + u + 1, 4 * j : 4 * j + 4].astype(F32)
                grad = (part.reshape(4, k1, LANES) * slope).astype(BF16)
                g1[2 * b + u + 1, 4 * j : 4 * j + 4] = grad
                total_one = total_one + jnp.sum(grad.astype(F32), axis=0)
        for j in range(-(-side // cols)):
            end = min((j + 1) * cols, side)
            tile = h1[2 * b + 1 : 2 * b + 3, j * cols : end]
            if end < (j + 1) * cols:
                rest = jnp.zeros((2, (j + 1) * cols - end, k1, LANES), BF16)
                tile = jnp.concatenate([tile, rest], axis=1)
            tiles.append(tile.reshape(2 * cols * k1, LANES))
            pieces = []
            for half in range(2):
                for p in range(reach):
                    x = 4 * j - 1 + p
                    pieces.append(g2[b + 1 - half, x] if 0 <= x < inner else zero)
            grads.append(jnp.concatenate(pieces, axis=0))
        if b % 2:
            total = total + dot_lanes(
                jnp.concatenate(grads, axis=1), jnp.concatenate(tiles, axis=1)
            )
            grads, tiles = [], []
    line = 4 * k1
    for half in range(2):
        for u in range(2):
            tap_row = jnp.zeros((k2, line), F32)
            for p in range(reach):
                at = (half * reach + p) * k2
                part = total[at : at + k2, u * 2 * line : (u + 1) * 2 * line]
                start = 2 * k1 * (p - 1)
                piece = part[:, max(start, 0) : min(start + line, 2 * line)]
                if start < 0:
                    piece = jnp.concatenate([jnp.zeros((k2, -start), F32), piece], axis=1)
                if start + line > 2 * line:
                    rest = jnp.zeros((k2, start - line), F32)
                    piece = jnp.concatenate([piece, rest], axis=1)
                tap_row = tap_row + piece
            at = (2 * half + u) * line
            c2[:, at : at + line] = tap_row
    sums[...] = jnp.zeros_like(sums)
    sums[0:1, 0:k1] = row_of(jnp.sum(total_one, axis=1, keepdims=True))
    sums[1:2, 0:k2] = row_of(jnp.sum(total_two, axis=1, keepdims=True))


def pixel_band(sec, w1t, channels):
    k1 = w1t.shape[0]
    rows = 64 * channels
    row, tap = iota((rows, 256), 0), iota((rows, 256), 1)
    moves = ((tap >> 6) == row % channels + sec * channels) & ((tap & 63) == row // channels)
    taps = dot_lanes(moves.astype(F32).astype(BF16), w1t)
    line, span = COLS * channels, 8 * channels
    blocks = {}
    for half in range(2):
        for p in range(NEAR):
            pieces = []
            for u in range(4):
                at = (4 * half + u) * span
                start = 4 * (p - 1) * channels
                cut = taps[at + max(0, -start) : at + min(span, line - start)]
                start = max(start, 0)
                pieces += [jnp.zeros((start, k1), F32)] if start else []
                pieces.append(cut)
                rest = line - start - cut.shape[0]
                pieces += [jnp.zeros((rest, k1), F32)] if rest else []
            blocks[half, p] = jnp.concatenate(pieces, axis=0)
    zero = jnp.zeros((4 * line, k1), F32)
    lines = []
    for r in range(STEP):
        cols = [
            blocks.get((r + 1 - yrel, p), zero) for yrel in range(STEP + 1) for p in range(NEAR)
        ]
        lines.append(jnp.concatenate(cols, axis=1))
    return jnp.concatenate(lines, axis=0).astype(BF16)


def first_kernel(
    section,
    frames_far,
    g1,
    w1t,
    other_far,
    after,
    c1,
    out,
    band,
    frames,
    acc,
    other,
    held,
    sems,
    draw_sems,
    *,
    draw,
):
    side, k1 = g1.shape[1], g1.shape[2]
    img, _, channels, _ = frames.shape
    steps = img // 4 // STEP
    arrives = frame_copies(section, frames_far, frames, sems)
    for g in range(steps):
        arrives(g).start()
    other_copy = pltpu.make_async_copy(
        other_far.at[0 : STEP * draw + 1], other, sems.at[steps]
    )
    other_copy.start()
    acc[...] = jnp.zeros_like(acc)
    zero = jnp.zeros((k1, LANES), BF16)

    def one_step(g, carry):
        arrives(g).wait()
        pixels, grads = [], []
        for j in range(img // COLS):
            rows = [pl.multiple_of(4 * (STEP * g + r), 4) for r in range(STEP)]
            pixels.append(
                jnp.concatenate([tile_rows(frames, row, j, COLS) for row in rows], axis=0)
            )
            pieces = []
            for yrel in range(STEP + 1):
                for p in range(NEAR):
                    x = 3 * j - 1 + p
                    pieces.append(g1[STEP * g + yrel, x] if 0 <= x < side else zero)
            grads.append(jnp.concatenate(pieces, axis=0))
        acc[...] += dot_lanes(jnp.concatenate(pixels, axis=1), jnp.concatenate(grads, axis=1))
        return carry

    lax.fori_loop(0, steps, one_step, 0)
    band[...] = pixel_band(section[0], w1t[...], out.shape[2])
    other_copy.wait()
    finish = draw_steps(section, band, g1, 0, other, 0, out, held, draw_sems, 0, draw)
    fold_first(acc, c1, channels, k1)
    finish()


def fold_first(acc, c1, channels, k1):
    line = COLS * channels
    step = 4 * channels
    taps = []
    for half in range(2):
        total = sum(
            acc[r * 4 * line : (r + 1) * 4 * line, :][
                :, (r + 1 - half) * NEAR * k1 : (r + 2 - half) * NEAR * k1
            ]
            for r in range(STEP)
        )
        for u in range(4):
            part = total[u * line : (u + 1) * line]
            cols = [part[:, p * k1 : (p + 1) * k1] for p in range(NEAR)]
            taps.append(cols[1][0:step] + cols[2][step : 2 * step] + cols[3][2 * step :])
            taps.append(cols[0][0:step] + cols[1][step : 2 * step] + cols[2][2 * step :])
    row, col = iota((256, 256), 0), iota((256, 256), 1)
    moves = ((row & 3) == (col >> 6)) & ((row >> 2) == (col & 63))
    grad = dot_rows(jnp.concatenate(taps, axis=0), moves.astype(F32), EXACT)
    for half in range(2):
        c1[half * k1 : (half + 1) * k1, :] = grad[:, half * LANES : (half + 1) * LANES].astype(BF16)


def draw_steps(section, band, mine, mine_at, other, other_at, out, held, sems, start, steps):
    side, k1 = mine.shape[1], mine.shape[2]
    img, channels = out.shape[1], out.shape[2]
    sec = section[0]
    line = COLS * channels
    flat = held.reshape(2, 2, 4 * STEP, img * channels, LANES)

    def writes(g):
        rows = slice(4 * STEP * (start + g), 4 * STEP * (start + g + 1))
        places = (sec * LANES, (1 - sec) * LANES)
        return [
            pltpu.make_async_copy(
                held.at[g % 2, k],
                out.at[rows, :, :, pl.ds(pl.multiple_of(places[k], LANES), LANES)],
                sems.at[g % 2, k],
            )
            for k in range(2)
        ]

    zero = jnp.zeros((k1, 2 * LANES), BF16)
    for g in range(steps):
        if g >= 2:
            for copy in writes(g - 2):
                copy.wait()
        for j in range(img // COLS):
            pieces = []
            for yrel in range(STEP + 1):
                for p in range(NEAR):
                    x, y = 3 * j - 1 + p, STEP * (start + g) + yrel
                    if 0 <= x < side:
                        pair = [mine[y - mine_at, x], other[y - other_at, x]]
                        pieces.append(jnp.concatenate(pair, axis=1))
                    else:
                        pieces.append(zero)
            got = dot(band[...], jnp.concatenate(pieces, axis=0))
            for k in range(4 * STEP):
                at = slice(k * line, (k + 1) * line)
                span = slice(j * line, (j + 1) * line)
                flat[g % 2, 0, k, span, :] = got[at, :LANES]
                flat[g % 2, 1, k, span, :] = got[at, LANES:]
        for copy in writes(g):
            copy.start()

    def finish():
        for g in range(max(steps - 2, 0), steps):
            for copy in writes(g):
                copy.wait()

    return finish


def pixels_kernel(section, band, mine, other_far, after, done, out, token, held, other, sems, *, start):
    steps = other.shape[0] // STEP
    fetch = pltpu.make_async_copy(
        other_far.at[STEP * start : STEP * (start + steps) + 1], other, sems.at[2, 0]
    )
    fetch.start()
    token[...] = jnp.zeros_like(token)
    fetch.wait()
    draw_steps(
        section, band, mine, 0, other, STEP * start, out, held, sems, start, steps
    )()


def two_parts(value):
    high = value.astype(BF16).astype(F32)
    return jnp.concatenate([high, value - high], axis=0).astype(BF16)


def one_part(pair):
    rows = pair.shape[0] // 2
    pair = pair.astype(F32)
    return pair[:rows] + pair[rows:]


def merge_kernel(keep, recv_one, recv_two, small, c2, sums, out_far, lines, out, sems):
    members = out.shape[0]
    size = keep.shape[0] // members
    lines[...] = small[...]
    lines[AT_B1, :] = sums[0:1, :]
    lines[AT_B2, :] = sums[1:2, :]
    for k in range(members):
        at = slice(k * size, (k + 1) * size)
        recv, here = recv_one, k
        if k >= members // 2:
            recv, here = recv_two, k - members // 2
        got = recv[here * size : (here + 1) * size, :]
        out[k, 0:size, :] = keep[at, :] + got
        if k < members // 2:
            rows, span = c2_place(k)
            out[k, size:, :] = c2[rows, span].astype(BF16)
        else:
            out[k, size:, :] = two_parts(lines[table_place(k), :])
        pltpu.make_async_copy(out.at[k], out_far.at[k], sems.at[k]).start()
    for k in range(members):
        pltpu.make_async_copy(out.at[k], out_far.at[k], sems.at[k]).wait()


def c2_place(k):
    return slice(k % 2 * SHORT, (k % 2 + 1) * SHORT), slice(k // 2 * LANES, (k // 2 + 1) * LANES)


def table_place(k):
    at = (k - CUBE // 2) * SHORT // 2
    return slice(at, at + SHORT // 2)


def riders(batch, parts):
    plain = sum(p.astype(F32) for p in parts).astype(BF16)
    fine = two_parts(sum(one_part(p) for p in parts))
    return jnp.where(batch[0] % CUBE < CUBE // 2, plain.astype(F32), fine.astype(F32)).astype(BF16)


def cube_kernel(batch, got, c1, out):
    members = got.shape[0]
    size = got.shape[1] - SHORT
    out[0:size, :] = sum(got[k, 0:size, :].astype(F32) for k in range(members)).astype(BF16)
    out[size : size + SHORT, :] = riders(batch, [got[k, size:, :] for k in range(members)])
    out[size + SHORT :, :] = c1[...]


def add_kernel(batch, a, b, after, out):
    size = a.shape[0] - SHORT - 32
    for span in (slice(0, size), slice(size + SHORT, a.shape[0])):
        out[span, :] = (a[span, :].astype(F32) + b[span, :].astype(F32)).astype(BF16)
    ride = slice(size, size + SHORT)
    out[ride, :] = riders(batch, [a[ride, :], b[ride, :]])


def relay_kernel(batch, *refs):
    parts, (one, two, out) = refs[:CUBE], refs[-3:]
    me = batch[0] % CUBE
    for k, part in enumerate(parts):
        out[me ^ k] = part[...]
    one[...] = out[: CUBE // 2]
    two[...] = out[CUBE // 2 :]


def piece_of(got, k):
    count = got[0].shape[0]
    return got[k // count].at[k % count]


def unpack_half(which, got, lw, bw, vw, stage, stage_b, sems):
    members = 2 * got[0].shape[0]
    size = stage.shape[0] // members
    linear_rows, width = lw.shape
    options = bw.shape[0]
    half = (linear_rows + options * width + width) // 2
    rest = linear_rows - half
    group = options // 3

    def first_copies():
        spans = [(k * size, min((k + 1) * size, half)) for k in range(members)]
        return [
            pltpu.make_async_copy(stage.at[a:b], lw.at[a:b], sems.at[k])
            for k, (a, b) in enumerate(spans)
        ]

    def second_copies():
        copies = [pltpu.make_async_copy(stage.at[0:rest], lw.at[half:], sems.at[0])]
        for k in range(options // group):
            part = slice(k * group, (k + 1) * group)
            copies.append(pltpu.make_async_copy(stage_b.at[part], bw.at[part], sems.at[1 + k]))
        last = stage.at[rest : rest + width]
        copies.append(pltpu.make_async_copy(last, vw, sems.at[len(copies)]))
        return copies

    @pl.when(which == 0)
    def _():
        for k, copy in enumerate(first_copies()):
            start, end = k * size, min((k + 1) * size, half)
            stage[start:end, :] = piece_of(got, k)[0 : end - start, :].astype(F32)
            copy.start()

    @pl.when(which == 1)
    def _():
        def rows(start, end):
            parts = []
            while start < end:
                k, at = start // size, start % size
                count = min(size - at, end - start)
                parts.append(piece_of(got, k)[at : at + count, :])
                start += count
            value = parts[0] if len(parts) == 1 else jnp.concatenate(parts, axis=0)
            return value.astype(F32)

        copies = second_copies()
        stage[0:rest, :] = rows(0, rest)
        copies[0].start()
        for o in range(options):
            stage_b[o] = rows(rest + o * width, rest + (o + 1) * width)
            if o % group == group - 1:
                copies[1 + o // group].start()
        at = rest + options * width
        stage[rest : rest + width, :] = rows(at, at + width)
        copies[-1].start()

    def finish():
        for half_at, copies in ((0, first_copies), (1, second_copies)):

            @pl.when(which == half_at)
            def _():
                for copy in copies():
                    copy.wait()

    return finish


def own_kernel(section, one, two, lw, bw, vw, stage, stage_b, sems):
    unpack_half(section[0], (one, two), lw, bw, vw, stage, stage_b, sems)()


def unpack_kernel(section, *refs):
    mine, other, refs = refs[0:2], refs[2:4], refs[4:]
    lw, bw, vw = refs[3:6]
    little = (len(refs) - 10) // 2
    far, near = refs[6 : 6 + little], refs[6 + little : 6 + 2 * little]
    loss, c1, b1, c2, b2, lb, bb, hw, hb, vb, ow, ob = near
    stage, stage_b, lines, sems = refs[-4:]
    options = bw.shape[0]
    k1, k2 = c1.shape[0], c2.shape[0]
    size = stage.shape[0] // CUBE
    finish = unpack_half(1 - section[0], other, lw, bw, vw, stage, stage_b, sems)
    grad = [jnp.zeros((k1, LANES), F32) for _ in range(2)]
    ride = slice(size, size + SHORT)
    for k in range(CUBE):
        views = piece_of(mine, k), piece_of(other, k)
        if k < CUBE // 2:
            c2[c2_place(k)] = sum(v[ride, :].astype(F32) for v in views)
        else:
            lines[table_place(k), :] = sum(one_part(v[ride, :]) for v in views)
        for view in views:
            for h in range(2):
                at = size + SHORT + h * k1
                grad[h] += view[at : at + k1, :].astype(F32)
    for part in range(2):
        c1[:, part * LANES : (part + 1) * LANES] = grad[part]
    bb[...] = lines[0:options, :]
    vb[...] = lines[AT_VB, :]
    ow[...] = lines[AT_OW, :]
    hw[...] = lines[AT_HW, :]
    lb[...] = lines[AT_LB, :]
    scalars = lines[AT_SCALARS, :]
    loss[...] = scalars[:, 0:1]
    hb[...] = scalars[:, 1:3]
    ob[...] = scalars[:, 3:4]
    b1[...] = lines[AT_B1, 0:k1]
    b2[...] = lines[AT_B2, 0:k2]
    copies = [
        pltpu.make_async_copy(a, b, sems.at[CUBE + k]) for k, (a, b) in enumerate(zip(near, far))
    ]
    for copy in copies:
        copy.start()
    finish()
    for copy in copies:
        copy.wait()


def numbers_kernel(
    options,
    depth,
    targets,
    destination,
    b1,
    b2,
    lb,
    bb,
    hw,
    vb,
    ow,
    hb,
    ob,
    out,
    table,
):
    levels, kinds = options.shape[0], targets.shape[0]
    slots = depth.shape[1]
    rows = [options[...].astype(F32), depth[...].astype(F32)]
    rows += [targets[k] for k in range(kinds)]
    rows.append(jnp.zeros((LANES - levels - 1 - kinds * levels, slots), F32))
    out[...] = jnp.transpose(jnp.concatenate(rows, axis=0))
    table[...] = jnp.zeros_like(table)
    table[0 : bb.shape[0], :] = bb[...]
    table[AT_VB, :] = vb[...]
    table[AT_OW, :] = ow[...].astype(F32)
    table[AT_HW, :] = hw[...].astype(F32)
    table[AT_LB, :] = lb[...]
    table[AT_B1, 0 : b1.shape[1]] = b1[...]
    table[AT_B2, 0 : b2.shape[1]] = b2[...]
    lane = iota((1, LANES), 1)
    scalars = jnp.zeros((1, LANES), F32)
    for k, value in ((1, hb[:, 0:1]), (2, hb[:, 1:2]), (3, ob[...])):
        scalars = jnp.where(lane == k, value, scalars)
    table[AT_SCALARS, :] = scalars
    for k in range(slots // LANES):
        part = destination[:, k * LANES : (k + 1) * LANES]
        table[AT_DEST + k : AT_DEST + k + 1, :] = part.astype(F32)


def whole(shape):
    zeros = (0,) * len(shape)
    return pl.BlockSpec(shape, lambda *_: zeros)


ANYWHERE = pl.BlockSpec(memory_space=pl.ANY)
SCALARS = pl.BlockSpec(memory_space=pltpu.SMEM)


def params():
    return pltpu.CompilerParams(vmem_limit_bytes=VMEM_BYTES)


def shape_of(*shape, dtype=F32):
    return jax.ShapeDtypeStruct(shape, dtype)


def cost(microseconds):
    return pl.CostEstimate(
        flops=int(1.1e9 * microseconds), bytes_accessed=int(3.6e6 * microseconds), transcendentals=0
    )


def stays(value):
    return pltpu.with_memory_space_constraint(value, pltpu.HBM)


def held_near(value):
    return pltpu.with_memory_space_constraint(value, pltpu.VMEM)


def encode(section, frames, w1t, w2t, lw, table):
    img = frames.shape[0]
    blocks = img // 4
    side = blocks - 1
    k1, k2, width = w1t.shape[0], w2t.shape[0], lw.shape[1]
    flat = lw.shape[0]
    vmem = pltpu.VMEM
    near = pl.BlockSpec(memory_space=vmem)
    grid_one = (blocks, side, k1, LANES)
    return pl.pallas_call(
        encode_kernel,
        in_specs=[SCALARS, ANYWHERE, near, near, ANYWHERE, near],
        out_specs=[ANYWHERE] * 3 + [near] * 3,
        out_shape=(
            pltpu.HBM(grid_one, BF16),
            pltpu.HBM(grid_one, BF16),
            pltpu.HBM((flat, LANES), BF16),
            shape_of(flat, LANES, dtype=BF16),
            shape_of(width, LANES, dtype=BF16),
            shape_of(width, LANES),
        ),
        scratch_shapes=[
            vmem((img, img, frames.shape[2], LANES), BF16),
            vmem(lw.shape, BF16),
            vmem(grid_one, BF16),
            vmem(grid_one, BF16),
            vmem((flat, LANES), BF16),
            vmem((2 * REACH * k1, 256), BF16),
            vmem((2 * k1, 64), BF16),
            vmem((6 * k2, LANES), BF16),
            vmem((k1, LANES), F32),
            vmem((k2, LANES), F32),
            vmem((side, k1, LANES), F32),
            vmem((side // 2 - 1, k2, LANES), F32),
            pltpu.SemaphoreType.DMA((4, max(blocks // STEP, 3))),
        ],
        compiler_params=params(),
        cost_estimate=cost(9),
        name="encode",
    )(section, frames, w1t, w2t, lw, table)


def plan(section, slots, enc, s3, h2, branch_w, value_w, table, per_pair, depth, half_rows):
    width = enc.shape[0]
    options = branch_w.shape[0]
    two = 2 * width
    pairs = options // 2
    outs = (
        shape_of(half_rows, LANES, dtype=BF16),
        shape_of(half_rows // 2, LANES, dtype=BF16),
        shape_of(half_rows // 2, LANES, dtype=BF16),
        shape_of(TABLE, LANES),
        shape_of(width, LANES, dtype=BF16),
    )
    vmem = pltpu.VMEM
    near = pl.BlockSpec(memory_space=vmem)
    return pl.pallas_call(
        functools.partial(plan_kernel, per_pair=per_pair, depth=depth),
        in_specs=[SCALARS, near, near, near, near, ANYWHERE, near, near],
        out_shape=outs,
        scratch_shapes=[
            vmem((2, half_rows, LANES), BF16),
            vmem((options * width, width + 16), BF16),
            vmem((width + 16, width + 16), BF16),
            vmem((width, width + 16), BF16),
            vmem((width, LANES), F32),
            vmem((16, LANES), F32),
            vmem((options * width, LANES), F32),
            vmem((depth, options * width, LANES), F32),
            vmem((depth, pairs, width, two), F32),
            vmem((depth, pairs, width + 16, two), BF16),
            vmem((depth, pairs, width, two), BF16),
            vmem((depth, options * width, LANES), BF16),
            vmem(branch_w.shape, BF16),
            pltpu.SemaphoreType.DMA,
        ],
        compiler_params=params(),
        cost_estimate=cost(11),
        name="plan",
    )(section, slots, enc, s3, h2, branch_w, value_w, table)


def back(g3, lw, s2, s1, h1, w2t):
    _, side, k1 = s1.shape[:3]
    k2 = w2t.shape[0]
    inner = side // 2 - 1
    padded = (side + 2, side, k1, LANES)
    near = pl.BlockSpec(memory_space=pltpu.VMEM)
    return pl.pallas_call(
        back_kernel,
        in_specs=[near] * 6,
        out_shape=(shape_of(*padded, dtype=BF16), shape_of(k2, 256), shape_of(8, LANES)),
        scratch_shapes=[
            pltpu.VMEM((LANES, 6 * k2), BF16),
            pltpu.VMEM((inner + 2, inner, k2, LANES), BF16),
        ],
        compiler_params=params(),
        cost_estimate=cost(25),
        name="back",
    )(g3, lw, s2, s1, h1, w2t)


def first(section, frames, g1, w1t, other, after, channels, draw):
    img, _, stack, _ = frames.shape
    k1 = g1.shape[2]
    band = (STEP * 4 * COLS * channels, (STEP + 1) * NEAR * k1)
    near = pl.BlockSpec(memory_space=pltpu.VMEM)
    return pl.pallas_call(
        functools.partial(first_kernel, draw=draw),
        in_specs=[SCALARS, ANYWHERE, near, near, ANYWHERE, ANYWHERE],
        out_specs=[near, ANYWHERE, near],
        out_shape=[
            shape_of(2 * k1, LANES, dtype=BF16),
            shape_of(img, img, channels, 2 * LANES),
            shape_of(*band, dtype=BF16),
        ],
        scratch_shapes=[
            pltpu.VMEM((img, img, stack, LANES), BF16),
            pltpu.VMEM((STEP * 4 * COLS * stack, (STEP + 1) * NEAR * k1), F32),
            pltpu.VMEM((STEP * draw + 1,) + g1.shape[1:], BF16),
            pltpu.VMEM((2, 2, 4 * STEP, img, channels, LANES), F32),
            pltpu.SemaphoreType.DMA((img // 4 // STEP + 1,)),
            pltpu.SemaphoreType.DMA((2, 2)),
        ],
        compiler_params=params(),
        cost_estimate=cost(45),
        name="first",
    )(section, frames, g1, w1t, other, after)


def pixels(section, band, mine, other, after, done, start, steps):
    img, _, channels, _ = done.shape
    near = pl.BlockSpec(memory_space=pltpu.VMEM)
    return pl.pallas_call(
        functools.partial(pixels_kernel, start=start),
        in_specs=[SCALARS, near, near, ANYWHERE, ANYWHERE, ANYWHERE],
        out_specs=[ANYWHERE, near],
        out_shape=[shape_of(*done.shape), shape_of(8, LANES)],
        scratch_shapes=[
            pltpu.VMEM((2, 2, 4 * STEP, img, channels, LANES), F32),
            pltpu.VMEM((STEP * steps + 1,) + mine.shape[1:], BF16),
            pltpu.SemaphoreType.DMA((3, 2)),
        ],
        input_output_aliases={5: 0},
        compiler_params=params(),
        cost_estimate=cost(1 + 0.9 * steps),
        name="pixels",
    )(section, band, mine, other, after, done)


def small_call(
    kernel, outs, operands, scratch=(), name=None, place=None, after=(), weight=0.3, far=False
):
    specs = [pl.BlockSpec(memory_space=pltpu.VMEM)] * len(operands)
    if place is not None:
        operands = (*place, *operands)
        specs = [pl.BlockSpec(memory_space=pltpu.SMEM)] * len(place) + specs
    return pl.pallas_call(
        kernel,
        in_specs=specs + [ANYWHERE] * len(after),
        out_specs=jax.tree.map(
            lambda _: ANYWHERE if far else pl.BlockSpec(memory_space=pltpu.VMEM), outs
        ),
        out_shape=outs,
        scratch_shapes=list(scratch),
        compiler_params=params(),
        cost_estimate=cost(weight),
        name=name,
    )(*operands, *after)


def round_up(value, step):
    return -(-value // step) * step


def swapped(value):
    return lax.ppermute(value, "section", [(0, 1), (1, 0)])


def exchanged(value, groups=None):
    return lax.all_to_all(
        value, "batch", split_axis=0, concat_axis=0, axis_index_groups=groups, tiled=True
    )


def partner(value, distance):
    count = lax.axis_size("batch")
    return lax.ppermute(value, "batch", [(b, b ^ distance) for b in range(count)])


def local(
    frames,
    destination,
    options,
    depth,
    targets,
    conv_one,
    bias_one,
    conv_two,
    bias_two,
    linear_w,
    linear_b,
    branch_w,
    branch_b,
    head_w,
    head_b,
    value_w,
    value_b,
    out_w,
    out_b,
):
    section = lax.axis_index("section").astype(jnp.int32)[None]
    peers = lax.axis_size("batch")
    frame_count = frames.shape[3]
    per_pair = frame_count // peers
    levels = options.shape[0]
    frames = stays(frames.transpose(1, 2, 0, 3))
    w1t, w2t = stays(conv_one.T), stays(conv_two.T)
    branch_w, value_w = stays(branch_w), stays(value_w)
    encoder_params = (w1t, bias_one, w2t, bias_two, linear_w, linear_b)
    planner_params = (branch_w, branch_b, head_w.T, head_b, value_w, value_b, out_w.T, out_b)
    width = linear_w.shape[1]
    big_rows = linear_w.shape[0] + (branch_w.shape[0] + 1) * width
    size = round_up(-(-big_rows // (2 * CUBE)), 16)

    tiny = (bias_one, bias_two, linear_b, branch_b, head_w.T, value_b, out_w.T)
    tiny = [stays(v if v.ndim > 1 else v[None, :]) for v in tiny]
    numbers, table = pl.pallas_call(
        numbers_kernel,
        in_specs=[pl.BlockSpec(memory_space=pltpu.VMEM)] * (6 + len(tiny)),
        out_shape=[shape_of(frame_count, LANES), shape_of(TABLE, LANES)],
        compiler_params=params(),
        cost_estimate=cost(1),
        name="numbers",
    )(
        stays(options),
        stays(depth[None, :]),
        stays(targets),
        stays(destination[None, :]),
        *tiny,
        stays(head_b[None, :]),
        out_b[None, :],
    )
    slots = exchanged(numbers.reshape(peers, per_pair, LANES)).reshape(frame_count, LANES)

    h1, s1, s2, h2, enc, s3 = encode(section, frames, w1t, w2t, stays(linear_w), table)
    keep, send_one, send_two, small, g3 = plan(
        section, slots, enc, s3, h2, branch_w, value_w, table, per_pair, levels, CUBE * size
    )
    recv = swapped(send_one), swapped(send_two)
    channels = frames.shape[2] // lax.axis_size("section")
    g1, c2, sums = back(g3, linear_w, s2, s1, h1, w2t)
    other = swapped(g1)
    g1 = held_near(g1)
    place = (lax.axis_index("batch").astype(jnp.int32)[None],)
    cubes = [list(range(c, c + CUBE)) for c in range(0, peers, CUBE)]
    bf16 = functools.partial(shape_of, dtype=BF16)
    pieces = small_call(
        merge_kernel,
        bf16(CUBE, size + SHORT, LANES),
        (keep, *recv, small, c2, sums),
        [
            pltpu.VMEM((TABLE, LANES), F32),
            pltpu.VMEM((CUBE, size + SHORT, LANES), BF16),
            pltpu.SemaphoreType.DMA((CUBE,)),
        ],
        name="merge",
        far=True,
        weight=30,
    )
    got = exchanged(pieces, cubes)
    c1, frames_grad, band = first(section, frames, g1, w1t, other, pieces, channels, DRAW)
    piece = bf16(size + SHORT + c1.shape[0], LANES)
    keep = small_call(cube_kernel, piece, (got, c1), name="cube", place=place)
    distance = CUBE
    while distance < peers:
        recv = partner(keep, distance)
        if distance == CUBE:
            frames_grad, token = pixels(
                section, band, g1, other, keep, frames_grad, DRAW, DRAW_ACROSS
            )
        distance *= 2
        keep = small_call(
            add_kernel, piece, (keep, recv), name="add", place=place, after=(token,)
        )
    parts = [keep] + [partner(keep, k) for k in range(1, CUBE)]
    drawn = DRAW + DRAW_ACROSS
    left = frames.shape[0] // 4 // STEP - drawn
    frames_grad, token = pixels(section, band, g1, other, keep, frames_grad, drawn, left)
    got = small_call(
        relay_kernel,
        [bf16(CUBE // 2, *piece.shape)] * 2,
        parts,
        [pltpu.VMEM((CUBE, *piece.shape), BF16)],
        name="relay",
        place=place,
        after=(token,),
    )
    got_other = [swapped(v) for v in got]
    shapes = [p.shape for p in encoder_params + planner_params]
    near = pl.BlockSpec(memory_space=pltpu.VMEM)
    flat = [shape_of(*(v if len(v) > 1 else (1,) + v)) for v in [(1, 1)] + shapes]
    large = [flat[k] for k in (5, 7, 11)]
    staged = [
        pltpu.VMEM((CUBE * size, LANES), F32),
        pltpu.VMEM(branch_w.shape, F32),
    ]
    little = [v for k, v in enumerate(flat) if k not in (5, 7, 11)]
    sems = pltpu.SemaphoreType.DMA((CUBE + len(little),))
    begun = pl.pallas_call(
        own_kernel,
        in_specs=[SCALARS, near, near],
        out_specs=[ANYWHERE] * 3,
        out_shape=large,
        scratch_shapes=[*staged, sems],
        compiler_params=params(),
        cost_estimate=cost(1),
        name="own",
    )(section, *got)
    ends = pl.pallas_call(
        unpack_kernel,
        in_specs=[SCALARS] + [near] * 4 + [ANYWHERE] * 3,
        out_specs=[ANYWHERE] * (3 + len(little)),
        out_shape=large + little,
        scratch_shapes=[pltpu.VMEM(v.shape, F32) for v in little]
        + [*staged, pltpu.VMEM((TABLE, LANES), F32), sems],
        input_output_aliases={5: 0, 6: 1, 7: 2},
        compiler_params=params(),
        cost_estimate=cost(1.5),
        name="unpack",
    )(section, *got, *got_other, *begun)
    rest = list(ends[3:])
    for k, at in enumerate((5, 7, 11)):
        rest.insert(at, ends[k])
    rest = [v.reshape(s) for v, s in zip(rest, [()] + shapes)]
    for at in (1, 3, 9, 13):
        rest[at] = rest[at].T
    return (rest[0], frames_grad.transpose(2, 0, 1, 3), *rest[1:])


def solution(mesh):
    placed = (
        P(None, None, None, "batch"),
        P("batch"),
        P(None, "batch"),
        P("batch"),
        P(None, None, "batch"),
    ) + (P(),) * 14
    return jax.shard_map(
        local,
        mesh=mesh,
        in_specs=placed,
        out_specs=(P(), P("section", None, None, "batch")) + (P(),) * 14,
        check_vma=False,
    )
```

```python
import functools
import math

import jax
import jax.numpy as jnp
from jax import lax
from jax.experimental import pallas as pl
from jax.experimental.pallas import tpu as pltpu
from jax.sharding import PartitionSpec as P

BF16 = jnp.bfloat16
F32 = jnp.float32
EXACT = lax.Precision.HIGHEST
LANES = 128
VMEM_BYTES = 32 * 1024 * 1024
TILE = 16
REACH = 5
STEP = 3
COLS = 12
NEAR = 4
AT_VB, AT_OW, AT_HW, AT_LB, AT_SCALARS, AT_B1, AT_B2, AT_DEST = (
    slice(18, 19),
    slice(19, 20),
    slice(20, 22),
    slice(22, 23),
    slice(23, 24),
    slice(24, 25),
    slice(25, 26),
    26,
)
TABLE = 32
CUBE = 8
TURNS = (0, 4, 3, 2, 5, 1, 6, 7)
DRAW = 3
DRAW_ACROSS = 3
SHORT = 16


def dot(a, b, precision=None):
    return jnp.dot(a, b, preferred_element_type=F32, precision=precision)


def dot_rows(a, b, precision=None):
    return lax.dot_general(
        a, b, (((0,), (0,)), ((), ())), preferred_element_type=F32, precision=precision
    )


def dot_lanes(a, b, precision=None):
    return lax.dot_general(
        a, b, (((1,), (1,)), ((), ())), preferred_element_type=F32, precision=precision
    )


def iota(shape, axis):
    return lax.broadcasted_iota(jnp.int32, shape, axis)


def column(row):
    n = row.shape[1]
    wide = jnp.broadcast_to(row, (n, n))
    return jnp.sum(jnp.where(iota((n, n), 0) == iota((n, n), 1), wide, 0.0), axis=1, keepdims=True)


def row_of(col):
    n = col.shape[0]
    wide = jnp.broadcast_to(col, (n, n))
    return jnp.sum(jnp.where(iota((n, n), 0) == iota((n, n), 1), wide, 0.0), axis=0, keepdims=True)


def soft(x):
    t = jnp.tanh(0.5 * x)
    return jnp.maximum(x, 0.0) - jnp.log(0.5 + 0.5 * jnp.abs(t)), 1.0 + t


def silu_pair(y):
    t = jnp.tanh(y)
    m = y * t
    return y + m, (1.0 + t) + (y - m * t)


def pixel_order(w1t):
    tap, pix = iota((256, 256), 0), iota((256, 256), 1)
    moves = ((tap >> 6) == (pix & 3)) & ((tap & 63) == (pix >> 2))
    return dot(w1t, moves.astype(F32).astype(BF16))


def frame_copies(section, far, here, sems):
    lanes = pl.ds(pl.multiple_of(section[0] * LANES, LANES), LANES)
    size = 4 * STEP

    def copy(g):
        rows = pl.ds(pl.multiple_of(g * size, size), size)
        return pltpu.make_async_copy(far.at[rows, :, :, lanes], here.at[rows], sems.at[g])

    return copy


def tile_rows(frames, row, j, cols):
    img, _, channels, _ = frames.shape
    flat = frames.reshape(img, img * channels, LANES)
    size = cols * channels
    end = min((j + 1) * size, img * channels)
    part = flat[pl.ds(row, 4), j * size : end, :]
    return part.reshape(4 * (end - j * size), LANES)


def encode_kernel(
    section,
    frames_far,
    w1t,
    w2t,
    lw_far,
    table,
    h1_far,
    s1_far,
    s2_far,
    h2,
    enc,
    s3,
    frames,
    lw,
    h1,
    s1,
    s2,
    band,
    edge,
    band2,
    bias1,
    bias2,
    held,
    held2,
    sems,
):
    blocks, side = h1.shape[:2]
    steps = blocks // STEP
    tiles = frames.shape[1] // TILE
    k1, k2 = w1t.shape[0], w2t.shape[0]
    reach_rows = REACH * k1
    arrives = frame_copies(section, frames_far, frames, sems.at[0])
    for g in range(steps):
        arrives(g).start()
    last_copies = [
        pltpu.make_async_copy(lw_far, lw, sems.at[3, 0]),
        pltpu.make_async_copy(s2, s2_far, sems.at[3, 1]),
    ]
    last_copies[0].start()

    def leaves(g):
        rows = pl.ds(g * STEP, STEP)
        return [
            pltpu.make_async_copy(h1.at[rows], h1_far.at[rows], sems.at[1, g]),
            pltpu.make_async_copy(s1.at[rows], s1_far.at[rows], sems.at[2, g]),
        ]

    inner = side // 2 - 1
    row_len = inner * k2
    two = 2 * k2 * 3

    def prepare():
        taps = pixel_order(w1t[...])
        edges = []
        for half in range(2):
            lines = [taps[:, 32 * (4 * half + u) : 32 * (4 * half + u + 1)] for u in range(4)]
            for place in range(REACH):
                pieces = []
                for line in lines:
                    start = 16 * (place - 1)
                    cut = line[:, max(0, -start) : min(32, 64 - start)]
                    start = max(start, 0)
                    pieces += [jnp.zeros((k1, start), F32)] if start else []
                    pieces.append(cut)
                    rest = 64 - start - cut.shape[1]
                    pieces += [jnp.zeros((k1, rest), F32)] if rest else []
                at = half * reach_rows + place * k1
                band[at : at + k1, :] = jnp.concatenate(pieces, axis=1).astype(BF16)
            edges.append(jnp.concatenate([line[:, 16:] for line in lines], axis=1))
        edge[...] = jnp.concatenate(edges, axis=0).astype(BF16)
        tap, pix = iota((256, LANES), 0), iota((256, LANES), 1)
        for half in range(2):
            for place in range(3):
                hit = (
                    ((tap & 15) == (pix & 15))
                    & ((tap >> 6) == (pix >> 6) + 2 * half)
                    & (((tap >> 4) & 3) == ((pix >> 4) & 3) + 2 - 2 * place)
                )
                at = (half * 3 + place) * k2
                taps = dot(w2t[...], hit.astype(F32).astype(BF16))
                band2[at : at + k2, :] = taps.astype(BF16)
        bias1[...] = jnp.broadcast_to(column(table[AT_B1, 0:k1]), bias1.shape)
        bias2[...] = jnp.broadcast_to(column(table[AT_B2, 0:k2]), bias2.shape)
        held[...] = jnp.zeros_like(held)
        held2[...] = jnp.zeros_like(held2)
        h1[...] = jnp.zeros_like(h1)

    def added(sums, x, value):
        sums[x] = sums[x] + value if x in sums else value

    def second_matmul(b):
        tiles = [
            h1[pl.ds(2 * b + 1, 2), 4 * j : 4 * j + 4].reshape(LANES, LANES)
            for j in range(side // 4)
        ]
        return dot(band2[...], jnp.concatenate(tiles, axis=1))

    def second_rows(b, got):
        low, high = {}, {}
        for j in range(side // 4):
            for place in range(3):
                x = 2 * j - 1 + place
                if 0 <= x < inner:
                    span = slice(j * LANES, (j + 1) * LANES)
                    at = place * k2
                    added(low, x, got[at : at + k2, span])
                    added(high, x, got[two // 2 + at : two // 2 + at + k2, span])
        row = jnp.maximum(b - 1, 0) * row_len
        for x in range(inner):
            value, slope = soft(held2[x] + high[x] + bias2[...])
            held2[x] = low[x]
            at = pl.ds(pl.multiple_of(row + x * k2, k2), k2)
            h2[at, :] = value.astype(BF16)
            s2[at, :] = slope.astype(BF16)

    def one_step(g, carry):
        def row(r):
            return pl.multiple_of(4 * (STEP * g + r), 4)

        arrives(g).wait()
        lows, highs = [{} for _ in range(STEP)], [{} for _ in range(STEP)]

        def place_tile(r, j, got):
            for place in range(REACH):
                x = 4 * j - 1 + place
                if 0 <= x < side:
                    at = place * k1
                    added(lows[r], x, got[at : at + k1])
                    added(highs[r], x, got[reach_rows + at : reach_rows + at + k1])

        def finish(r, xs):
            for x in xs:
                value, slope = soft(held[x] + highs[r][x] + bias1[...])
                held[x] = lows[r][x]
                h1[STEP * g + r, x] = value.astype(BF16)
                s1[STEP * g + r, x] = slope.astype(BF16)

        pair = jnp.maximum(g - 1, 0)
        units = [(lambda: second_matmul(pair), lambda got: second_rows(pair, got))]

        def edges():
            parts = [tile_rows(frames, row(r), tiles, TILE) for r in range(STEP)]
            return dot(edge[...], jnp.concatenate(parts, axis=1))

        def place_edges(got):
            for r in range(STEP):
                added(lows[r], side - 1, got[:k1, r * LANES : (r + 1) * LANES])
                added(highs[r], side - 1, got[k1:, r * LANES : (r + 1) * LANES])

        units.append((edges, place_edges))

        def full(spots):
            parts = [tile_rows(frames, row(r), j, TILE) for r, j in spots]
            return dot(band[...], jnp.concatenate(parts, axis=1))

        def place_full(got, spots, ready):
            for i, (r, j) in enumerate(spots):
                place_tile(r, j, got[:, i * LANES : (i + 1) * LANES])
            if ready:
                finish(*ready)

        for r in range(STEP):
            if r % 2 == 0:
                spots = [(k, tiles - 1) for k in (r, r + 1) if k < STEP]
                units.append(
                    (
                        functools.partial(full, spots),
                        functools.partial(place_full, spots=spots, ready=None),
                    )
                )
            done = 0
            for j in range(0, tiles - 1, 2):
                spots = [(r, j), (r, j + 1)]
                ready = side if j + 2 == tiles - 1 else 4 * j + 7
                units.append(
                    (
                        functools.partial(full, spots),
                        functools.partial(place_full, spots=spots, ready=(r, range(done, ready))),
                    )
                )
                done = ready
        waiting = None
        for issue, take in units:
            got = issue()
            if waiting is not None:
                waiting[0](waiting[1])
            waiting = (take, got)
        waiting[0](waiting[1])
        for copy in leaves(g):
            copy.start()
        return carry

    prepare()
    lax.fori_loop(0, steps, one_step, 0)
    for b in range(steps - 1, side // 2):
        second_rows(b, second_matmul(b))
    for copy in last_copies[1:]:
        copy.start()
    last_copies[0].wait()
    value, slope = soft(dot_rows(lw[...], h2[...]) + column(table[AT_LB, :]))
    enc[...] = value.astype(BF16)
    s3[...] = 0.5 * slope
    for g in range(steps):
        for copy in leaves(g):
            copy.wait()
    for copy in last_copies[1:]:
        copy.wait()


def three_parts(row):
    high = row.astype(BF16).astype(F32)
    middle = (row - high).astype(BF16).astype(F32)
    return jnp.concatenate([high, middle, row - high - middle], axis=0)


def with_ones(value):
    return jnp.concatenate([value, ones_rows(value.shape[1])], axis=0)


def ones_rows(lanes):
    return (iota((16, lanes), 0) < 3).astype(F32).astype(BF16)


def plan_kernel(
    section,
    slots,
    enc,
    s3,
    h2,
    branch_far,
    value_w,
    table,
    keep,
    send_one,
    send_two,
    small,
    g3,
    parts,
    bwt,
    vht,
    vhw,
    ow,
    mine,
    pre,
    dbr,
    dval,
    low,
    hid,
    gb,
    branch_w,
    sem,
    *,
    per_pair,
    depth,
):
    width = enc.shape[0]
    options = branch_w.shape[0]
    pairs = options // 2
    two = 2 * width
    sec = section[0]
    branch_copy = pltpu.make_async_copy(branch_far, branch_w, sem)
    branch_copy.start()

    count = slots.shape[0]
    dest = jnp.concatenate(
        [table[AT_DEST + k : AT_DEST + k + 1, :] for k in range(count // LANES)], axis=1
    )
    own = jnp.where(sec == 0, dest[:, :LANES], dest[:, LANES:])
    others = jnp.transpose(jnp.broadcast_to(dest, (LANES, count)))
    index = iota((count, LANES), 1) + sec * LANES
    earlier = (others == own) & (iota((count, LANES), 0) < index)
    rank = jnp.sum(earlier.astype(F32), axis=0, keepdims=True)
    bucket = own * float(per_pair) + rank
    chosen = (iota((count, LANES), 0).astype(F32) == bucket).astype(F32).astype(BF16)
    numbers = slots[:, : mine.shape[0]]
    high = numbers.astype(BF16)
    middle = (numbers - high.astype(F32)).astype(BF16)
    rest = (numbers - high.astype(F32) - middle.astype(F32)).astype(BF16)
    mine[...] = sum(dot_rows(v, chosen) for v in (rest, middle, high))

    pad = jnp.zeros((13, width), F32)
    branch_copy.wait()
    for o in range(options):
        rows = [branch_w[o].astype(F32), three_parts(table[o : o + 1, :]), pad]
        bwt[o * width : (o + 1) * width, :] = jnp.transpose(
            0.5 * jnp.concatenate(rows, axis=0)
        ).astype(BF16)
    scalars = table[AT_SCALARS, :]
    head_w = table[AT_HW, :]
    rows = [value_w[...].astype(F32), three_parts(table[AT_VB, :]), pad]
    vht[0:width, :] = jnp.transpose(0.5 * jnp.concatenate(rows, axis=0)).astype(BF16)
    vht[width:, :] = jnp.zeros((16, width + 16), BF16)
    lane = iota((1, 16), 1)
    for k in range(2):
        bias = three_parts(jnp.broadcast_to(scalars[:, 1 + k : 2 + k], (1, 16)))
        bias = sum(jnp.where(lane == j, bias[j : j + 1], 0.0) for j in range(3))
        vht[width + k : width + k + 1, 0:width] = head_w[k : k + 1].astype(BF16)
        vht[width + k : width + k + 1, width:] = bias.astype(BF16)
    vhw[:, 0:width] = (0.5 * value_w[...].astype(F32)).astype(BF16)
    vhw[:, width:] = jnp.transpose(
        0.5 * jnp.concatenate([head_w, jnp.zeros((14, width), F32)], axis=0)
    ).astype(BF16)
    ow[...] = jnp.broadcast_to(column(table[AT_OW, :]), (width, LANES))
    wide_ow = jnp.concatenate([ow[...], ow[...]], axis=1)
    half_ow = 0.5 * wide_ow

    labels = iota((options, LANES), 0).astype(F32)
    state = enc[...].astype(F32)
    rounded_all, saved = [], []
    group = 3
    for level in range(depth):
        picked = labels == mine[level : level + 1, :]
        rounded = state.astype(BF16)
        rounded_all.append(rounded)
        met = with_ones(rounded)

        def branches(first):
            at = slice(first * two, (first + group) * two)
            pre[at, :] = dot(bwt[at, :], met)

        branches(0)
        following = state
        reward, discount, value = [], [], []

        def value_part(t, got):
            act, slope = silu_pair(got[:width])
            dval[level, t] = slope
            hidden = act.astype(BF16)
            hid[level, t] = hidden
            worth = jnp.sum(hidden.astype(F32) * wide_ow, axis=0, keepdims=True)
            for k in range(2):
                span = slice(k * LANES, (k + 1) * LANES)
                value.append(worth[:, span])
                reward.append(got[width : width + 1, span])
                discount.append(got[width + 1 : width + 2, span])

        waiting = None
        for first in range(0, pairs, group):
            if first + group < pairs:
                branches(first + group)
            boths = []
            for t in range(first, first + group):
                at = slice(t * two, (t + 1) * two)
                act, slope = silu_pair(pre[at, :])
                dbr[level, at, :] = slope
                left = state + act[:width]
                right = state + act[width:]
                following = jnp.where(picked[2 * t : 2 * t + 1], left, following)
                following = jnp.where(picked[2 * t + 1 : 2 * t + 2], right, following)
                both = with_ones(
                    jnp.concatenate([left.astype(BF16), right.astype(BF16)], axis=1)
                )
                low[level, t] = both
                boths.append(both)
            got = dot(vht[...], jnp.concatenate(boths, axis=1))
            if waiting is not None:
                for k in range(group):
                    value_part(waiting[0] + k, waiting[1][:, k * two : (k + 1) * two])
            waiting = (first, got)
        for k in range(group):
            value_part(waiting[0] + k, waiting[1][:, k * two : (k + 1) * two])
        reward = jnp.concatenate(reward, axis=0)
        discount = jax.nn.sigmoid(jnp.concatenate(discount, axis=0))
        value = jnp.concatenate(value, axis=0) + scalars[:, 3:4]
        quality = reward + discount * value
        top = jnp.max(quality, axis=0, keepdims=True)
        shifted = jnp.exp(quality - top)
        total = jnp.sum(shifted, axis=0, keepdims=True)
        live = (mine[depth : depth + 1, :] > level).astype(F32)
        chosen = picked.astype(F32)

        def target(kind):
            at = depth + 1 + kind * depth + level
            return mine[at : at + 1, :]

        reward_gap = live * (jnp.sum(chosen * reward, axis=0, keepdims=True) - target(0))
        discount_gap = live * (jnp.sum(chosen * discount, axis=0, keepdims=True) - target(1))
        plan_gap = live * (top + jnp.log(total) - target(2))
        grad_quality = plan_gap * (shifted / total)
        head_two = (chosen * discount_gap + grad_quality * value) * discount * (1.0 - discount)
        saved.append(
            (
                picked,
                (chosen * reward_gap + grad_quality).astype(BF16).astype(F32),
                head_two.astype(BF16).astype(F32),
                (grad_quality * discount).astype(BF16).astype(F32),
                reward_gap * reward_gap + discount_gap * discount_gap + plan_gap * plan_gap,
            )
        )
        state = following

    out_sum = jnp.zeros((16, width), F32)
    value_sum = jnp.zeros((width + 16, width + 16), F32)
    grad_next = None
    line = iota((16, two), 0)
    for level in reversed(range(depth)):
        picked, head_one, head_two, grad_value, _ = saved[level]
        upward = jnp.zeros((width, LANES), F32)

        def branch_part(t, moved):
            at = slice(t * two, (t + 1) * two)
            left, right = moved[:, :LANES], moved[:, LANES:]
            if grad_next is not None:
                left = left + jnp.where(picked[2 * t : 2 * t + 1], grad_next, 0.0)
                right = right + jnp.where(picked[2 * t + 1 : 2 * t + 2], grad_next, 0.0)
            grad_branch = jnp.concatenate([left, right], axis=0) * dbr[level, at, :]
            grad_branch = grad_branch.astype(BF16)
            gb[level, at, :] = grad_branch
            return left + right

        def group_part(first, moved):
            parts = [
                branch_part(first + k, moved[:, k * two : (k + 1) * two]) for k in range(group)
            ]
            at = slice(first * two, (first + group) * two)
            weights = [branch_w[o] for o in range(2 * first, 2 * (first + group))]
            return sum(parts), dot(jnp.concatenate(weights, axis=1), gb[level, at, :])

        waiting = None
        for first in range(0, pairs, group):
            stack = []
            for t in range(first, first + group):

                def across(rows):
                    return jnp.concatenate(
                        [rows[2 * t : 2 * t + 1], rows[2 * t + 1 : 2 * t + 2]], axis=1
                    )

                worth = across(grad_value)
                grad_pre = (worth * half_ow * dval[level, t]).astype(BF16)
                heads = jnp.where(line == 0, across(head_one), 0.0)
                heads = jnp.where(line == 1, across(head_two), heads)
                heads = jnp.where(line == 2, worth, heads)
                heads = heads.astype(BF16)
                out_sum = out_sum + dot_lanes(heads, hid[level, t])
                stack.append(jnp.concatenate([grad_pre, heads], axis=0))
            stack = jnp.concatenate(stack, axis=1)
            moved = dot(vhw[...], stack)
            if waiting is not None:
                one, other = group_part(*waiting)
                upward = upward + (one + 0.5 * other)
            waiting = (first, moved)
            lows = jnp.concatenate([low[level, first + k] for k in range(group)], axis=1)
            value_sum = value_sum + dot_lanes(stack, lows)
        one, other = group_part(*waiting)
        grad_next = upward + (one + 0.5 * other)

    linear_rows = h2.shape[0]
    half = (linear_rows + options * width + width) // 2
    rest = linear_rows - half
    rounded = with_ones(jnp.concatenate(rounded_all, axis=1))
    small[...] = jnp.zeros_like(small)
    if half < keep.shape[0]:
        for k in range(2):
            parts[k, half:, :] = jnp.zeros((keep.shape[0] - half, LANES), BF16)
    for t in range(pairs):
        at = slice(t * two, (t + 1) * two)
        grads = jnp.concatenate([gb[level, at, :] for level in range(depth)], axis=1)
        got = dot_lanes(rounded, grads)
        for k in range(2):
            o = 2 * t + k
            span = slice(k * width, (k + 1) * width)
            rows = slice(rest + o * width, rest + (o + 1) * width)
            parts[1 - sec, rows, :] = got[:width, span].astype(BF16)
            small[o : o + 1, :] = got[width : width + 1, span]
    after = rest + options * width
    parts[1 - sec, after : after + width, :] = jnp.transpose(value_sum[:width, :width]).astype(BF16)

    grad_three = ((2.0 * grad_next).astype(BF16).astype(F32) * s3[...]).astype(BF16)
    g3[...] = grad_three
    chunk = linear_rows // 9
    for i in range(8):
        at = slice(i * chunk, (i + 1) * chunk)
        parts[sec, at, :] = dot_lanes(h2[at, :], grad_three).astype(BF16)
    last = dot_lanes(h2[8 * chunk :, :], grad_three).astype(BF16)
    parts[sec, 8 * chunk : half, :] = last[: half - 8 * chunk]
    parts[1 - sec, 0:rest, :] = last[half - 8 * chunk :]
    keep[...] = parts[0]
    send_one[...] = parts[1, : send_one.shape[0]]
    send_two[...] = parts[1, send_one.shape[0] :]

    small[AT_VB, :] = row_of(value_sum[:width, width : width + 1])
    small[AT_OW, :] = out_sum[2:3]
    small[AT_HW, :] = value_sum[width : width + 2, :width]
    small[AT_LB, :] = row_of(jnp.sum(grad_three.astype(F32), axis=1, keepdims=True))
    loss = 0.5 * jnp.sum(sum(kept[4] for kept in saved), axis=1, keepdims=True)
    ends = [loss] + [value_sum[width + k : width + k + 1, width : width + 1] for k in range(3)]
    lane = iota((1, LANES), 1)
    line = jnp.zeros((1, LANES), F32)
    for k, end in enumerate(ends):
        line = jnp.where(lane == k, end, line)
    small[AT_SCALARS, :] = line


def back_kernel(g3, lw, s2, s1, h1, w2t, g1, c2, sums, t2, g2):
    side, k1 = s1.shape[1], s1.shape[2]
    k2 = w2t.shape[0]
    inner = side // 2 - 1
    row_len = inner * k2
    half_g3 = (0.5 * g3[...].astype(F32)).astype(BF16)
    tap, pix = iota((LANES, 256), 1), iota((LANES, 256), 0)
    for yrel in range(2):
        for p in range(3):
            hit = (
                ((tap & 15) == (pix & 15))
                & ((tap >> 6) == (pix >> 6) + 2 * (1 - yrel))
                & (((tap >> 4) & 3) == ((pix >> 4) & 3) + 2 - 2 * p)
            )
            at = (yrel * 3 + p) * k2
            taps = dot_lanes(hit.astype(F32).astype(BF16), w2t[...])
            t2[:, at : at + k2] = (0.5 * taps).astype(BF16)
    g2[0] = jnp.zeros(g2.shape[1:], BF16)
    g2[inner + 1] = jnp.zeros(g2.shape[1:], BF16)
    g1[0] = jnp.zeros(g1.shape[1:], BF16)
    g1[side + 1] = jnp.zeros(g1.shape[1:], BF16)
    zero = jnp.zeros((k2, LANES), BF16)
    total_one = jnp.zeros((k1, LANES), F32)
    total_two = jnp.zeros((k2, LANES), F32)
    for y in range(inner):
        at = slice(y * row_len, (y + 1) * row_len)
        grad = dot(lw[at, :], half_g3) * s2[at, :].astype(F32)
        grad = grad.astype(BF16).reshape(inner, k2, LANES)
        g2[y + 1] = grad
        total_two = total_two + jnp.sum(grad.astype(F32), axis=0)
    reach, cols = 5, 8
    total = jnp.zeros((2 * reach * k2, 2 * cols * k1), F32)
    grads, tiles = [], []
    for b in range(side // 2):
        cut = []
        for j in range(side // 4):
            pieces = []
            for yrel in range(2):
                for p in range(3):
                    x = 2 * j - 1 + p
                    pieces.append(g2[b + yrel, x] if 0 <= x < inner else zero)
            cut.append(jnp.concatenate(pieces, axis=0))
        got = dot(t2[...], jnp.concatenate(cut, axis=1))
        for u in range(2):
            for j in range(side // 4):
                part = got[u * 64 : (u + 1) * 64, j * LANES : (j + 1) * LANES]
                slope = s1[2 * b + u + 1, 4 * j : 4 * j + 4].astype(F32)
                grad = (part.reshape(4, k1, LANES) * slope).astype(BF16)
                g1[2 * b + u + 1, 4 * j : 4 * j + 4] = grad
                total_one = total_one + jnp.sum(grad.astype(F32), axis=0)
        for j in range(-(-side // cols)):
            end = min((j + 1) * cols, side)
            tile = h1[2 * b + 1 : 2 * b + 3, j * cols : end]
            if end < (j + 1) * cols:
                rest = jnp.zeros((2, (j + 1) * cols - end, k1, LANES), BF16)
                tile = jnp.concatenate([tile, rest], axis=1)
            tiles.append(tile.reshape(2 * cols * k1, LANES))
            pieces = []
            for half in range(2):
                for p in range(reach):
                    x = 4 * j - 1 + p
                    pieces.append(g2[b + 1 - half, x] if 0 <= x < inner else zero)
            grads.append(jnp.concatenate(pieces, axis=0))
        if b % 2:
            total = total + dot_lanes(
                jnp.concatenate(grads, axis=1), jnp.concatenate(tiles, axis=1)
            )
            grads, tiles = [], []
    line = 4 * k1
    for half in range(2):
        for u in range(2):
            tap_row = jnp.zeros((k2, line), F32)
            for p in range(reach):
                at = (half * reach + p) * k2
                part = total[at : at + k2, u * 2 * line : (u + 1) * 2 * line]
                start = 2 * k1 * (p - 1)
                piece = part[:, max(start, 0) : min(start + line, 2 * line)]
                if start < 0:
                    piece = jnp.concatenate([jnp.zeros((k2, -start), F32), piece], axis=1)
                if start + line > 2 * line:
                    rest = jnp.zeros((k2, start - line), F32)
                    piece = jnp.concatenate([piece, rest], axis=1)
                tap_row = tap_row + piece
            at = (2 * half + u) * line
            c2[:, at : at + line] = tap_row
    sums[...] = jnp.zeros_like(sums)
    sums[0:1, 0:k1] = row_of(jnp.sum(total_one, axis=1, keepdims=True))
    sums[1:2, 0:k2] = row_of(jnp.sum(total_two, axis=1, keepdims=True))


def pixel_band(sec, w1t, channels):
    k1 = w1t.shape[0]
    rows = 64 * channels
    row, tap = iota((rows, 256), 0), iota((rows, 256), 1)
    moves = ((tap >> 6) == row % channels + sec * channels) & ((tap & 63) == row // channels)
    taps = dot_lanes(moves.astype(F32).astype(BF16), w1t)
    line, span = COLS * channels, 8 * channels
    blocks = {}
    for half in range(2):
        for p in range(NEAR):
            pieces = []
            for u in range(4):
                at = (4 * half + u) * span
                start = 4 * (p - 1) * channels
                cut = taps[at + max(0, -start) : at + min(span, line - start)]
                start = max(start, 0)
                pieces += [jnp.zeros((start, k1), F32)] if start else []
                pieces.append(cut)
                rest = line - start - cut.shape[0]
                pieces += [jnp.zeros((rest, k1), F32)] if rest else []
            blocks[half, p] = jnp.concatenate(pieces, axis=0)
    zero = jnp.zeros((4 * line, k1), F32)
    lines = []
    for r in range(STEP):
        cols = [
            blocks.get((r + 1 - yrel, p), zero) for yrel in range(STEP + 1) for p in range(NEAR)
        ]
        lines.append(jnp.concatenate(cols, axis=1))
    return jnp.concatenate(lines, axis=0).astype(BF16)


def first_kernel(
    section,
    frames_far,
    g1,
    w1t,
    other_far,
    after,
    c1,
    out,
    band,
    frames,
    acc,
    other,
    held,
    sems,
    draw_sems,
    *,
    draw,
):
    side, k1 = g1.shape[1], g1.shape[2]
    img, _, channels, _ = frames.shape
    steps = img // 4 // STEP
    arrives = frame_copies(section, frames_far, frames, sems)
    for g in range(steps):
        arrives(g).start()
    other_copy = pltpu.make_async_copy(
        other_far.at[0 : STEP * draw + 1], other, sems.at[steps]
    )
    other_copy.start()
    acc[...] = jnp.zeros_like(acc)
    zero = jnp.zeros((k1, LANES), BF16)

    def one_step(g, carry):
        arrives(g).wait()
        pixels, grads = [], []
        for j in range(img // COLS):
            rows = [pl.multiple_of(4 * (STEP * g + r), 4) for r in range(STEP)]
            pixels.append(
                jnp.concatenate([tile_rows(frames, row, j, COLS) for row in rows], axis=0)
            )
            pieces = []
            for yrel in range(STEP + 1):
                for p in range(NEAR):
                    x = 3 * j - 1 + p
                    pieces.append(g1[STEP * g + yrel, x] if 0 <= x < side else zero)
            grads.append(jnp.concatenate(pieces, axis=0))
        acc[...] += dot_lanes(jnp.concatenate(pixels, axis=1), jnp.concatenate(grads, axis=1))
        return carry

    lax.fori_loop(0, steps, one_step, 0)
    band[...] = pixel_band(section[0], w1t[...], out.shape[2])
    other_copy.wait()
    finish = draw_steps(section, band, g1, 0, other, 0, out, held, draw_sems, 0, draw)
    fold_first(acc, c1, channels, k1)
    finish()


def fold_first(acc, c1, channels, k1):
    line = COLS * channels
    step = 4 * channels
    taps = []
    for half in range(2):
        total = sum(
            acc[r * 4 * line : (r + 1) * 4 * line, :][
                :, (r + 1 - half) * NEAR * k1 : (r + 2 - half) * NEAR * k1
            ]
            for r in range(STEP)
        )
        for u in range(4):
            part = total[u * line : (u + 1) * line]
            cols = [part[:, p * k1 : (p + 1) * k1] for p in range(NEAR)]
            taps.append(cols[1][0:step] + cols[2][step : 2 * step] + cols[3][2 * step :])
            taps.append(cols[0][0:step] + cols[1][step : 2 * step] + cols[2][2 * step :])
    row, col = iota((256, 256), 0), iota((256, 256), 1)
    moves = ((row & 3) == (col >> 6)) & ((row >> 2) == (col & 63))
    grad = dot_rows(jnp.concatenate(taps, axis=0), moves.astype(F32), EXACT)
    for half in range(2):
        c1[half * k1 : (half + 1) * k1, :] = grad[:, half * LANES : (half + 1) * LANES].astype(BF16)


def draw_steps(section, band, mine, mine_at, other, other_at, out, held, sems, start, steps):
    side, k1 = mine.shape[1], mine.shape[2]
    img, channels = out.shape[1], out.shape[2]
    sec = section[0]
    line = COLS * channels
    flat = held.reshape(2, 2, 4 * STEP, img * channels, LANES)

    def writes(g):
        rows = slice(4 * STEP * (start + g), 4 * STEP * (start + g + 1))
        places = (sec * LANES, (1 - sec) * LANES)
        return [
            pltpu.make_async_copy(
                held.at[g % 2, k],
                out.at[rows, :, :, pl.ds(pl.multiple_of(places[k], LANES), LANES)],
                sems.at[g % 2, k],
            )
            for k in range(2)
        ]

    zero = jnp.zeros((k1, 2 * LANES), BF16)
    for g in range(steps):
        if g >= 2:
            for copy in writes(g - 2):
                copy.wait()
        for j in range(img // COLS):
            pieces = []
            for yrel in range(STEP + 1):
                for p in range(NEAR):
                    x, y = 3 * j - 1 + p, STEP * (start + g) + yrel
                    if 0 <= x < side:
                        pair = [mine[y - mine_at, x], other[y - other_at, x]]
                        pieces.append(jnp.concatenate(pair, axis=1))
                    else:
                        pieces.append(zero)
            got = dot(band[...], jnp.concatenate(pieces, axis=0))
            for k in range(4 * STEP):
                at = slice(k * line, (k + 1) * line)
                span = slice(j * line, (j + 1) * line)
                flat[g % 2, 0, k, span, :] = got[at, :LANES]
                flat[g % 2, 1, k, span, :] = got[at, LANES:]
        for copy in writes(g):
            copy.start()

    def finish():
        for g in range(max(steps - 2, 0), steps):
            for copy in writes(g):
                copy.wait()

    return finish


def pixels_kernel(section, band, mine, other_far, after, done, out, token, held, other, sems, *, start):
    steps = other.shape[0] // STEP
    fetch = pltpu.make_async_copy(
        other_far.at[STEP * start : STEP * (start + steps) + 1], other, sems.at[2, 0]
    )
    fetch.start()
    token[...] = jnp.zeros_like(token)
    fetch.wait()
    draw_steps(
        section, band, mine, 0, other, STEP * start, out, held, sems, start, steps
    )()


def two_parts(value):
    high = value.astype(BF16).astype(F32)
    return jnp.concatenate([high, value - high], axis=0).astype(BF16)


def one_part(pair):
    rows = pair.shape[0] // 2
    pair = pair.astype(F32)
    return pair[:rows] + pair[rows:]


def merge_kernel(keep, recv_one, recv_two, small, c2, sums, out_far, lines, out, sems):
    members = out.shape[0]
    size = keep.shape[0] // members
    lines[...] = small[...]
    lines[AT_B1, :] = sums[0:1, :]
    lines[AT_B2, :] = sums[1:2, :]
    for k in range(members):
        at = slice(k * size, (k + 1) * size)
        recv, here = recv_one, k
        if k >= members // 2:
            recv, here = recv_two, k - members // 2
        got = recv[here * size : (here + 1) * size, :]
        out[k, 0:size, :] = keep[at, :] + got
        if k < members // 2:
            rows, span = c2_place(k)
            out[k, size:, :] = c2[rows, span].astype(BF16)
        else:
            out[k, size:, :] = two_parts(lines[table_place(k), :])
        pltpu.make_async_copy(out.at[k], out_far.at[k], sems.at[k]).start()
    for k in range(members):
        pltpu.make_async_copy(out.at[k], out_far.at[k], sems.at[k]).wait()


def c2_place(k):
    return slice(k % 2 * SHORT, (k % 2 + 1) * SHORT), slice(k // 2 * LANES, (k // 2 + 1) * LANES)


def table_place(k):
    at = (k - CUBE // 2) * SHORT // 2
    return slice(at, at + SHORT // 2)


def riders(batch, parts):
    plain = sum(p.astype(F32) for p in parts).astype(BF16)
    fine = two_parts(sum(one_part(p) for p in parts))
    return jnp.where(batch[0] % CUBE < CUBE // 2, plain.astype(F32), fine.astype(F32)).astype(BF16)


def cube_kernel(batch, got, c1, out):
    members = got.shape[0]
    size = got.shape[1] - SHORT
    out[0:size, :] = sum(got[k, 0:size, :].astype(F32) for k in range(members)).astype(BF16)
    out[size : size + SHORT, :] = riders(batch, [got[k, size:, :] for k in range(members)])
    out[size + SHORT :, :] = c1[...]


def add_kernel(batch, a, b, after, out):
    size = a.shape[0] - SHORT - 32
    for span in (slice(0, size), slice(size + SHORT, a.shape[0])):
        out[span, :] = (a[span, :].astype(F32) + b[span, :].astype(F32)).astype(BF16)
    ride = slice(size, size + SHORT)
    out[ride, :] = riders(batch, [a[ride, :], b[ride, :]])


def relay_kernel(batch, *refs):
    parts, (one, two, out) = refs[:CUBE], refs[-3:]
    me = batch[0] % CUBE
    for k, part in zip(TURNS, parts):
        out[me ^ k] = part[...]
    one[...] = out[: CUBE // 2]
    two[...] = out[CUBE // 2 :]


def piece_of(got, k):
    count = got[0].shape[0]
    return got[k // count].at[k % count]


def unpack_half(which, got, lw, bw, vw, stage, stage_b, sems):
    members = 2 * got[0].shape[0]
    size = stage.shape[0] // members
    linear_rows, width = lw.shape
    options = bw.shape[0]
    half = (linear_rows + options * width + width) // 2
    rest = linear_rows - half
    group = options // 3

    def first_copies():
        spans = [(k * size, min((k + 1) * size, half)) for k in range(members)]
        return [
            pltpu.make_async_copy(stage.at[a:b], lw.at[a:b], sems.at[k])
            for k, (a, b) in enumerate(spans)
        ]

    def second_copies():
        copies = [pltpu.make_async_copy(stage.at[0:rest], lw.at[half:], sems.at[0])]
        for k in range(options // group):
            part = slice(k * group, (k + 1) * group)
            copies.append(pltpu.make_async_copy(stage_b.at[part], bw.at[part], sems.at[1 + k]))
        last = stage.at[rest : rest + width]
        copies.append(pltpu.make_async_copy(last, vw, sems.at[len(copies)]))
        return copies

    @pl.when(which == 0)
    def _():
        for k, copy in enumerate(first_copies()):
            start, end = k * size, min((k + 1) * size, half)
            stage[start:end, :] = piece_of(got, k)[0 : end - start, :].astype(F32)
            copy.start()

    @pl.when(which == 1)
    def _():
        def rows(start, end):
            parts = []
            while start < end:
                k, at = start // size, start % size
                count = min(size - at, end - start)
                parts.append(piece_of(got, k)[at : at + count, :])
                start += count
            value = parts[0] if len(parts) == 1 else jnp.concatenate(parts, axis=0)
            return value.astype(F32)

        copies = second_copies()
        stage[0:rest, :] = rows(0, rest)
        copies[0].start()
        for o in range(options):
            stage_b[o] = rows(rest + o * width, rest + (o + 1) * width)
            if o % group == group - 1:
                copies[1 + o // group].start()
        at = rest + options * width
        stage[rest : rest + width, :] = rows(at, at + width)
        copies[-1].start()

    def finish():
        for half_at, copies in ((0, first_copies), (1, second_copies)):

            @pl.when(which == half_at)
            def _():
                for copy in copies():
                    copy.wait()

    return finish


def own_kernel(section, one, two, lw, bw, vw, stage, stage_b, sems):
    unpack_half(section[0], (one, two), lw, bw, vw, stage, stage_b, sems)()


def unpack_kernel(section, *refs):
    mine, other, refs = refs[0:2], refs[2:4], refs[4:]
    lw, bw, vw = refs[3:6]
    little = (len(refs) - 10) // 2
    far, near = refs[6 : 6 + little], refs[6 + little : 6 + 2 * little]
    loss, c1, b1, c2, b2, lb, bb, hw, hb, vb, ow, ob = near
    stage, stage_b, lines, sems = refs[-4:]
    options = bw.shape[0]
    k1, k2 = c1.shape[0], c2.shape[0]
    size = stage.shape[0] // CUBE
    finish = unpack_half(1 - section[0], other, lw, bw, vw, stage, stage_b, sems)
    grad = [jnp.zeros((k1, LANES), F32) for _ in range(2)]
    ride = slice(size, size + SHORT)
    for k in range(CUBE):
        views = piece_of(mine, k), piece_of(other, k)
        if k < CUBE // 2:
            c2[c2_place(k)] = sum(v[ride, :].astype(F32) for v in views)
        else:
            lines[table_place(k), :] = sum(one_part(v[ride, :]) for v in views)
        for view in views:
            for h in range(2):
                at = size + SHORT + h * k1
                grad[h] += view[at : at + k1, :].astype(F32)
    for part in range(2):
        c1[:, part * LANES : (part + 1) * LANES] = grad[part]
    bb[...] = lines[0:options, :]
    vb[...] = lines[AT_VB, :]
    ow[...] = lines[AT_OW, :]
    hw[...] = lines[AT_HW, :]
    lb[...] = lines[AT_LB, :]
    scalars = lines[AT_SCALARS, :]
    loss[...] = scalars[:, 0:1]
    hb[...] = scalars[:, 1:3]
    ob[...] = scalars[:, 3:4]
    b1[...] = lines[AT_B1, 0:k1]
    b2[...] = lines[AT_B2, 0:k2]
    copies = [
        pltpu.make_async_copy(a, b, sems.at[CUBE + k]) for k, (a, b) in enumerate(zip(near, far))
    ]
    for copy in copies:
        copy.start()
    finish()
    for copy in copies:
        copy.wait()


def numbers_kernel(
    options,
    depth,
    targets,
    destination,
    b1,
    b2,
    lb,
    bb,
    hw,
    vb,
    ow,
    hb,
    ob,
    out,
    table,
):
    levels, kinds = options.shape[0], targets.shape[0]
    slots = depth.shape[1]
    rows = [options[...].astype(F32), depth[...].astype(F32)]
    rows += [targets[k] for k in range(kinds)]
    rows.append(jnp.zeros((LANES - levels - 1 - kinds * levels, slots), F32))
    out[...] = jnp.transpose(jnp.concatenate(rows, axis=0))
    table[...] = jnp.zeros_like(table)
    table[0 : bb.shape[0], :] = bb[...]
    table[AT_VB, :] = vb[...]
    table[AT_OW, :] = ow[...].astype(F32)
    table[AT_HW, :] = hw[...].astype(F32)
    table[AT_LB, :] = lb[...]
    table[AT_B1, 0 : b1.shape[1]] = b1[...]
    table[AT_B2, 0 : b2.shape[1]] = b2[...]
    lane = iota((1, LANES), 1)
    scalars = jnp.zeros((1, LANES), F32)
    for k, value in ((1, hb[:, 0:1]), (2, hb[:, 1:2]), (3, ob[...])):
        scalars = jnp.where(lane == k, value, scalars)
    table[AT_SCALARS, :] = scalars
    for k in range(slots // LANES):
        part = destination[:, k * LANES : (k + 1) * LANES]
        table[AT_DEST + k : AT_DEST + k + 1, :] = part.astype(F32)


def whole(shape):
    zeros = (0,) * len(shape)
    return pl.BlockSpec(shape, lambda *_: zeros)


ANYWHERE = pl.BlockSpec(memory_space=pl.ANY)
SCALARS = pl.BlockSpec(memory_space=pltpu.SMEM)


def params():
    return pltpu.CompilerParams(vmem_limit_bytes=VMEM_BYTES)


def shape_of(*shape, dtype=F32):
    return jax.ShapeDtypeStruct(shape, dtype)


def cost(microseconds):
    return pl.CostEstimate(
        flops=int(1.1e9 * microseconds), bytes_accessed=int(3.6e6 * microseconds), transcendentals=0
    )


def stays(value):
    return pltpu.with_memory_space_constraint(value, pltpu.HBM)


def held_near(value):
    return pltpu.with_memory_space_constraint(value, pltpu.VMEM)


def encode(section, frames, w1t, w2t, lw, table):
    img = frames.shape[0]
    blocks = img // 4
    side = blocks - 1
    k1, k2, width = w1t.shape[0], w2t.shape[0], lw.shape[1]
    flat = lw.shape[0]
    vmem = pltpu.VMEM
    near = pl.BlockSpec(memory_space=vmem)
    grid_one = (blocks, side, k1, LANES)
    return pl.pallas_call(
        encode_kernel,
        in_specs=[SCALARS, ANYWHERE, near, near, ANYWHERE, near],
        out_specs=[ANYWHERE] * 3 + [near] * 3,
        out_shape=(
            pltpu.HBM(grid_one, BF16),
            pltpu.HBM(grid_one, BF16),
            pltpu.HBM((flat, LANES), BF16),
            shape_of(flat, LANES, dtype=BF16),
            shape_of(width, LANES, dtype=BF16),
            shape_of(width, LANES),
        ),
        scratch_shapes=[
            vmem((img, img, frames.shape[2], LANES), BF16),
            vmem(lw.shape, BF16),
            vmem(grid_one, BF16),
            vmem(grid_one, BF16),
            vmem((flat, LANES), BF16),
            vmem((2 * REACH * k1, 256), BF16),
            vmem((2 * k1, 64), BF16),
            vmem((6 * k2, LANES), BF16),
            vmem((k1, LANES), F32),
            vmem((k2, LANES), F32),
            vmem((side, k1, LANES), F32),
            vmem((side // 2 - 1, k2, LANES), F32),
            pltpu.SemaphoreType.DMA((4, max(blocks // STEP, 3))),
        ],
        compiler_params=params(),
        cost_estimate=cost(9),
        name="encode",
    )(section, frames, w1t, w2t, lw, table)


def plan(section, slots, enc, s3, h2, branch_w, value_w, table, per_pair, depth, half_rows):
    width = enc.shape[0]
    options = branch_w.shape[0]
    two = 2 * width
    pairs = options // 2
    outs = (
        shape_of(half_rows, LANES, dtype=BF16),
        shape_of(half_rows // 2, LANES, dtype=BF16),
        shape_of(half_rows // 2, LANES, dtype=BF16),
        shape_of(TABLE, LANES),
        shape_of(width, LANES, dtype=BF16),
    )
    vmem = pltpu.VMEM
    near = pl.BlockSpec(memory_space=vmem)
    return pl.pallas_call(
        functools.partial(plan_kernel, per_pair=per_pair, depth=depth),
        in_specs=[SCALARS, near, near, near, near, ANYWHERE, near, near],
        out_shape=outs,
        scratch_shapes=[
            vmem((2, half_rows, LANES), BF16),
            vmem((options * width, width + 16), BF16),
            vmem((width + 16, width + 16), BF16),
            vmem((width, width + 16), BF16),
            vmem((width, LANES), F32),
            vmem((16, LANES), F32),
            vmem((options * width, LANES), F32),
            vmem((depth, options * width, LANES), F32),
            vmem((depth, pairs, width, two), F32),
            vmem((depth, pairs, width + 16, two), BF16),
            vmem((depth, pairs, width, two), BF16),
            vmem((depth, options * width, LANES), BF16),
            vmem(branch_w.shape, BF16),
            pltpu.SemaphoreType.DMA,
        ],
        compiler_params=params(),
        cost_estimate=cost(11),
        name="plan",
    )(section, slots, enc, s3, h2, branch_w, value_w, table)


def back(g3, lw, s2, s1, h1, w2t):
    _, side, k1 = s1.shape[:3]
    k2 = w2t.shape[0]
    inner = side // 2 - 1
    padded = (side + 2, side, k1, LANES)
    near = pl.BlockSpec(memory_space=pltpu.VMEM)
    return pl.pallas_call(
        back_kernel,
        in_specs=[near] * 6,
        out_shape=(shape_of(*padded, dtype=BF16), shape_of(k2, 256), shape_of(8, LANES)),
        scratch_shapes=[
            pltpu.VMEM((LANES, 6 * k2), BF16),
            pltpu.VMEM((inner + 2, inner, k2, LANES), BF16),
        ],
        compiler_params=params(),
        cost_estimate=cost(25),
        name="back",
    )(g3, lw, s2, s1, h1, w2t)


def first(section, frames, g1, w1t, other, after, channels, draw):
    img, _, stack, _ = frames.shape
    k1 = g1.shape[2]
    band = (STEP * 4 * COLS * channels, (STEP + 1) * NEAR * k1)
    near = pl.BlockSpec(memory_space=pltpu.VMEM)
    return pl.pallas_call(
        functools.partial(first_kernel, draw=draw),
        in_specs=[SCALARS, ANYWHERE, near, near, ANYWHERE, ANYWHERE],
        out_specs=[near, ANYWHERE, near],
        out_shape=[
            shape_of(2 * k1, LANES, dtype=BF16),
            shape_of(img, img, channels, 2 * LANES),
            shape_of(*band, dtype=BF16),
        ],
        scratch_shapes=[
            pltpu.VMEM((img, img, stack, LANES), BF16),
            pltpu.VMEM((STEP * 4 * COLS * stack, (STEP + 1) * NEAR * k1), F32),
            pltpu.VMEM((STEP * draw + 1,) + g1.shape[1:], BF16),
            pltpu.VMEM((2, 2, 4 * STEP, img, channels, LANES), F32),
            pltpu.SemaphoreType.DMA((img // 4 // STEP + 1,)),
            pltpu.SemaphoreType.DMA((2, 2)),
        ],
        compiler_params=params(),
        cost_estimate=cost(45),
        name="first",
    )(section, frames, g1, w1t, other, after)


def pixels(section, band, mine, other, after, done, start, steps):
    img, _, channels, _ = done.shape
    near = pl.BlockSpec(memory_space=pltpu.VMEM)
    return pl.pallas_call(
        functools.partial(pixels_kernel, start=start),
        in_specs=[SCALARS, near, near, ANYWHERE, ANYWHERE, ANYWHERE],
        out_specs=[ANYWHERE, near],
        out_shape=[shape_of(*done.shape), shape_of(8, LANES)],
        scratch_shapes=[
            pltpu.VMEM((2, 2, 4 * STEP, img, channels, LANES), F32),
            pltpu.VMEM((STEP * steps + 1,) + mine.shape[1:], BF16),
            pltpu.SemaphoreType.DMA((3, 2)),
        ],
        input_output_aliases={5: 0},
        compiler_params=params(),
        cost_estimate=cost(1 + 0.9 * steps),
        name="pixels",
    )(section, band, mine, other, after, done)


def small_call(
    kernel, outs, operands, scratch=(), name=None, place=None, after=(), weight=0.3, far=False
):
    specs = [pl.BlockSpec(memory_space=pltpu.VMEM)] * len(operands)
    if place is not None:
        operands = (*place, *operands)
        specs = [pl.BlockSpec(memory_space=pltpu.SMEM)] * len(place) + specs
    return pl.pallas_call(
        kernel,
        in_specs=specs + [ANYWHERE] * len(after),
        out_specs=jax.tree.map(
            lambda _: ANYWHERE if far else pl.BlockSpec(memory_space=pltpu.VMEM), outs
        ),
        out_shape=outs,
        scratch_shapes=list(scratch),
        compiler_params=params(),
        cost_estimate=cost(weight),
        name=name,
    )(*operands, *after)


def round_up(value, step):
    return -(-value // step) * step


def swapped(value):
    return lax.ppermute(value, "section", [(0, 1), (1, 0)])


def exchanged(value, groups=None):
    return lax.all_to_all(
        value, "batch", split_axis=0, concat_axis=0, axis_index_groups=groups, tiled=True
    )


def partner(value, distance):
    count = lax.axis_size("batch")
    return lax.ppermute(value, "batch", [(b, b ^ distance) for b in range(count)])


def local(
    frames,
    destination,
    options,
    depth,
    targets,
    conv_one,
    bias_one,
    conv_two,
    bias_two,
    linear_w,
    linear_b,
    branch_w,
    branch_b,
    head_w,
    head_b,
    value_w,
    value_b,
    out_w,
    out_b,
):
    section = lax.axis_index("section").astype(jnp.int32)[None]
    peers = lax.axis_size("batch")
    frame_count = frames.shape[3]
    per_pair = frame_count // peers
    levels = options.shape[0]
    frames = stays(frames.transpose(1, 2, 0, 3))
    w1t, w2t = stays(conv_one.T), stays(conv_two.T)
    branch_w, value_w = stays(branch_w), stays(value_w)
    encoder_params = (w1t, bias_one, w2t, bias_two, linear_w, linear_b)
    planner_params = (branch_w, branch_b, head_w.T, head_b, value_w, value_b, out_w.T, out_b)
    width = linear_w.shape[1]
    big_rows = linear_w.shape[0] + (branch_w.shape[0] + 1) * width
    size = round_up(-(-big_rows // (2 * CUBE)), 16)

    tiny = (bias_one, bias_two, linear_b, branch_b, head_w.T, value_b, out_w.T)
    tiny = [stays(v if v.ndim > 1 else v[None, :]) for v in tiny]
    numbers, table = pl.pallas_call(
        numbers_kernel,
        in_specs=[pl.BlockSpec(memory_space=pltpu.VMEM)] * (6 + len(tiny)),
        out_shape=[shape_of(frame_count, LANES), shape_of(TABLE, LANES)],
        compiler_params=params(),
        cost_estimate=cost(1),
        name="numbers",
    )(
        stays(options),
        stays(depth[None, :]),
        stays(targets),
        stays(destination[None, :]),
        *tiny,
        stays(head_b[None, :]),
        out_b[None, :],
    )
    slots = exchanged(numbers.reshape(peers, per_pair, LANES)).reshape(frame_count, LANES)

    h1, s1, s2, h2, enc, s3 = encode(section, frames, w1t, w2t, stays(linear_w), table)
    keep, send_one, send_two, small, g3 = plan(
        section, slots, enc, s3, h2, branch_w, value_w, table, per_pair, levels, CUBE * size
    )
    recv = swapped(send_one), swapped(send_two)
    channels = frames.shape[2] // lax.axis_size("section")
    g1, c2, sums = back(g3, linear_w, s2, s1, h1, w2t)
    other = swapped(g1)
    g1 = held_near(g1)
    place = (lax.axis_index("batch").astype(jnp.int32)[None],)
    cubes = [list(range(c, c + CUBE)) for c in range(0, peers, CUBE)]
    bf16 = functools.partial(shape_of, dtype=BF16)
    pieces = small_call(
        merge_kernel,
        bf16(CUBE, size + SHORT, LANES),
        (keep, *recv, small, c2, sums),
        [
            pltpu.VMEM((TABLE, LANES), F32),
            pltpu.VMEM((CUBE, size + SHORT, LANES), BF16),
            pltpu.SemaphoreType.DMA((CUBE,)),
        ],
        name="merge",
        far=True,
        weight=30,
    )
    got = exchanged(pieces, cubes)
    c1, frames_grad, band = first(section, frames, g1, w1t, other, pieces, channels, DRAW)
    piece = bf16(size + SHORT + c1.shape[0], LANES)
    keep = small_call(cube_kernel, piece, (got, c1), name="cube", place=place)
    distance = CUBE
    while distance < peers:
        recv = partner(keep, distance)
        if distance == CUBE:
            frames_grad, token = pixels(
                section, band, g1, other, keep, frames_grad, DRAW, DRAW_ACROSS
            )
        distance *= 2
        keep = small_call(
            add_kernel, piece, (keep, recv), name="add", place=place, after=(token,)
        )
    parts = [partner(keep, k) if k else keep for k in TURNS]
    drawn = DRAW + DRAW_ACROSS
    left = frames.shape[0] // 4 // STEP - drawn
    frames_grad, token = pixels(section, band, g1, other, keep, frames_grad, drawn, left)
    got = small_call(
        relay_kernel,
        [bf16(CUBE // 2, *piece.shape)] * 2,
        parts,
        [pltpu.VMEM((CUBE, *piece.shape), BF16)],
        name="relay",
        place=place,
        after=(token,),
    )
    got_other = [swapped(v) for v in got]
    shapes = [p.shape for p in encoder_params + planner_params]
    near = pl.BlockSpec(memory_space=pltpu.VMEM)
    flat = [shape_of(*(v if len(v) > 1 else (1,) + v)) for v in [(1, 1)] + shapes]
    large = [flat[k] for k in (5, 7, 11)]
    staged = [
        pltpu.VMEM((CUBE * size, LANES), F32),
        pltpu.VMEM(branch_w.shape, F32),
    ]
    little = [v for k, v in enumerate(flat) if k not in (5, 7, 11)]
    sems = pltpu.SemaphoreType.DMA((CUBE + len(little),))
    begun = pl.pallas_call(
        own_kernel,
        in_specs=[SCALARS, near, near],
        out_specs=[ANYWHERE] * 3,
        out_shape=large,
        scratch_shapes=[*staged, sems],
        compiler_params=params(),
        cost_estimate=cost(1),
        name="own",
    )(section, *got)
    ends = pl.pallas_call(
        unpack_kernel,
        in_specs=[SCALARS] + [near] * 4 + [ANYWHERE] * 3,
        out_specs=[ANYWHERE] * (3 + len(little)),
        out_shape=large + little,
        scratch_shapes=[pltpu.VMEM(v.shape, F32) for v in little]
        + [*staged, pltpu.VMEM((TABLE, LANES), F32), sems],
        input_output_aliases={5: 0, 6: 1, 7: 2},
        compiler_params=params(),
        cost_estimate=cost(1.5),
        name="unpack",
    )(section, *got, *got_other, *begun)
    rest = list(ends[3:])
    for k, at in enumerate((5, 7, 11)):
        rest.insert(at, ends[k])
    rest = [v.reshape(s) for v, s in zip(rest, [()] + shapes)]
    for at in (1, 3, 9, 13):
        rest[at] = rest[at].T
    return (rest[0], frames_grad.transpose(2, 0, 1, 3), *rest[1:])


def solution(mesh):
    placed = (
        P(None, None, None, "batch"),
        P("batch"),
        P(None, "batch"),
        P("batch"),
        P(None, None, "batch"),
    ) + (P(),) * 14
    return jax.shard_map(
        local,
        mesh=mesh,
        in_specs=placed,
        out_specs=(P(), P("section", None, None, "batch")) + (P(),) * 14,
        check_vma=False,
    )
```

```python
import functools
import math

import jax
import jax.numpy as jnp
from jax import lax
from jax.experimental import pallas as pl
from jax.experimental.pallas import tpu as pltpu
from jax.sharding import PartitionSpec as P

BF16 = jnp.bfloat16
F32 = jnp.float32
EXACT = lax.Precision.HIGHEST
LANES = 128
VMEM_BYTES = 32 * 1024 * 1024
TILE = 16
REACH = 5
STEP = 3
COLS = 12
NEAR = 4
AT_VB, AT_OW, AT_HW, AT_LB, AT_SCALARS, AT_B1, AT_B2, AT_DEST = (
    slice(18, 19),
    slice(19, 20),
    slice(20, 22),
    slice(22, 23),
    slice(23, 24),
    slice(24, 25),
    slice(25, 26),
    26,
)
TABLE = 32
CUBE = 8
TURNS = (0, 4, 3, 2, 5, 1, 6, 7)
DRAW = 4
SHORT = 16


def dot(a, b, precision=None):
    return jnp.dot(a, b, preferred_element_type=F32, precision=precision)


def dot_rows(a, b, precision=None):
    return lax.dot_general(
        a, b, (((0,), (0,)), ((), ())), preferred_element_type=F32, precision=precision
    )


def dot_lanes(a, b, precision=None):
    return lax.dot_general(
        a, b, (((1,), (1,)), ((), ())), preferred_element_type=F32, precision=precision
    )


def iota(shape, axis):
    return lax.broadcasted_iota(jnp.int32, shape, axis)


def column(row):
    n = row.shape[1]
    wide = jnp.broadcast_to(row, (n, n))
    return jnp.sum(jnp.where(iota((n, n), 0) == iota((n, n), 1), wide, 0.0), axis=1, keepdims=True)


def row_of(col):
    n = col.shape[0]
    wide = jnp.broadcast_to(col, (n, n))
    return jnp.sum(jnp.where(iota((n, n), 0) == iota((n, n), 1), wide, 0.0), axis=0, keepdims=True)


def soft(x):
    t = jnp.tanh(0.5 * x)
    return jnp.maximum(x, 0.0) - jnp.log(0.5 + 0.5 * jnp.abs(t)), 1.0 + t


def silu_pair(y):
    t = jnp.tanh(y)
    m = y * t
    return y + m, (1.0 + t) + (y - m * t)


def pixel_order(w1t):
    tap, pix = iota((256, 256), 0), iota((256, 256), 1)
    moves = ((tap >> 6) == (pix & 3)) & ((tap & 63) == (pix >> 2))
    return dot(w1t, moves.astype(F32).astype(BF16))


def frame_copies(section, far, here, sems):
    lanes = pl.ds(pl.multiple_of(section[0] * LANES, LANES), LANES)
    size = 4 * STEP

    def copy(g):
        rows = pl.ds(pl.multiple_of(g * size, size), size)
        return pltpu.make_async_copy(far.at[rows, :, :, lanes], here.at[rows], sems.at[g])

    return copy


def tile_rows(frames, row, j, cols):
    img, _, channels, _ = frames.shape
    flat = frames.reshape(img, img * channels, LANES)
    size = cols * channels
    end = min((j + 1) * size, img * channels)
    part = flat[pl.ds(row, 4), j * size : end, :]
    return part.reshape(4 * (end - j * size), LANES)


def encode_kernel(
    section,
    frames_far,
    w1t,
    w2t,
    lw_far,
    table,
    h1_far,
    s1_far,
    s2_far,
    h2,
    enc,
    s3,
    frames,
    lw,
    h1,
    s1,
    s2,
    band,
    edge,
    band2,
    bias1,
    bias2,
    held,
    held2,
    sems,
):
    blocks, side = h1.shape[:2]
    steps = blocks // STEP
    tiles = frames.shape[1] // TILE
    k1, k2 = w1t.shape[0], w2t.shape[0]
    reach_rows = REACH * k1
    arrives = frame_copies(section, frames_far, frames, sems.at[0])
    for g in range(steps):
        arrives(g).start()
    last_copies = [
        pltpu.make_async_copy(lw_far, lw, sems.at[3, 0]),
        pltpu.make_async_copy(s2, s2_far, sems.at[3, 1]),
    ]
    last_copies[0].start()

    def leaves(g):
        rows = pl.ds(g * STEP, STEP)
        return [
            pltpu.make_async_copy(h1.at[rows], h1_far.at[rows], sems.at[1, g]),
            pltpu.make_async_copy(s1.at[rows], s1_far.at[rows], sems.at[2, g]),
        ]

    inner = side // 2 - 1
    row_len = inner * k2
    two = 2 * k2 * 3

    def prepare():
        taps = pixel_order(w1t[...])
        edges = []
        for half in range(2):
            lines = [taps[:, 32 * (4 * half + u) : 32 * (4 * half + u + 1)] for u in range(4)]
            for place in range(REACH):
                pieces = []
                for line in lines:
                    start = 16 * (place - 1)
                    cut = line[:, max(0, -start) : min(32, 64 - start)]
                    start = max(start, 0)
                    pieces += [jnp.zeros((k1, start), F32)] if start else []
                    pieces.append(cut)
                    rest = 64 - start - cut.shape[1]
                    pieces += [jnp.zeros((k1, rest), F32)] if rest else []
                at = half * reach_rows + place * k1
                band[at : at + k1, :] = jnp.concatenate(pieces, axis=1).astype(BF16)
            edges.append(jnp.concatenate([line[:, 16:] for line in lines], axis=1))
        edge[...] = jnp.concatenate(edges, axis=0).astype(BF16)
        tap, pix = iota((256, LANES), 0), iota((256, LANES), 1)
        for half in range(2):
            for place in range(3):
                hit = (
                    ((tap & 15) == (pix & 15))
                    & ((tap >> 6) == (pix >> 6) + 2 * half)
                    & (((tap >> 4) & 3) == ((pix >> 4) & 3) + 2 - 2 * place)
                )
                at = (half * 3 + place) * k2
                taps = dot(w2t[...], hit.astype(F32).astype(BF16))
                band2[at : at + k2, :] = taps.astype(BF16)
        bias1[...] = jnp.broadcast_to(column(table[AT_B1, 0:k1]), bias1.shape)
        bias2[...] = jnp.broadcast_to(column(table[AT_B2, 0:k2]), bias2.shape)
        held[...] = jnp.zeros_like(held)
        held2[...] = jnp.zeros_like(held2)
        h1[...] = jnp.zeros_like(h1)

    def added(sums, x, value):
        sums[x] = sums[x] + value if x in sums else value

    def second_matmul(b):
        tiles = [
            h1[pl.ds(2 * b + 1, 2), 4 * j : 4 * j + 4].reshape(LANES, LANES)
            for j in range(side // 4)
        ]
        return dot(band2[...], jnp.concatenate(tiles, axis=1))

    def second_rows(b, got):
        low, high = {}, {}
        for j in range(side // 4):
            for place in range(3):
                x = 2 * j - 1 + place
                if 0 <= x < inner:
                    span = slice(j * LANES, (j + 1) * LANES)
                    at = place * k2
                    added(low, x, got[at : at + k2, span])
                    added(high, x, got[two // 2 + at : two // 2 + at + k2, span])
        row = jnp.maximum(b - 1, 0) * row_len
        for x in range(inner):
            value, slope = soft(held2[x] + high[x] + bias2[...])
            held2[x] = low[x]
            at = pl.ds(pl.multiple_of(row + x * k2, k2), k2)
            h2[at, :] = value.astype(BF16)
            s2[at, :] = slope.astype(BF16)

    def one_step(g, carry):
        def row(r):
            return pl.multiple_of(4 * (STEP * g + r), 4)

        arrives(g).wait()
        lows, highs = [{} for _ in range(STEP)], [{} for _ in range(STEP)]

        def place_tile(r, j, got):
            for place in range(REACH):
                x = 4 * j - 1 + place
                if 0 <= x < side:
                    at = place * k1
                    added(lows[r], x, got[at : at + k1])
                    added(highs[r], x, got[reach_rows + at : reach_rows + at + k1])

        def finish(r, xs):
            for x in xs:
                value, slope = soft(held[x] + highs[r][x] + bias1[...])
                held[x] = lows[r][x]
                h1[STEP * g + r, x] = value.astype(BF16)
                s1[STEP * g + r, x] = slope.astype(BF16)

        pair = jnp.maximum(g - 1, 0)
        units = [(lambda: second_matmul(pair), lambda got: second_rows(pair, got))]

        def edges():
            parts = [tile_rows(frames, row(r), tiles, TILE) for r in range(STEP)]
            return dot(edge[...], jnp.concatenate(parts, axis=1))

        def place_edges(got):
            for r in range(STEP):
                added(lows[r], side - 1, got[:k1, r * LANES : (r + 1) * LANES])
                added(highs[r], side - 1, got[k1:, r * LANES : (r + 1) * LANES])

        units.append((edges, place_edges))

        def full(spots):
            parts = [tile_rows(frames, row(r), j, TILE) for r, j in spots]
            return dot(band[...], jnp.concatenate(parts, axis=1))

        def place_full(got, spots, ready):
            for i, (r, j) in enumerate(spots):
                place_tile(r, j, got[:, i * LANES : (i + 1) * LANES])
            if ready:
                finish(*ready)

        for r in range(STEP):
            if r % 2 == 0:
                spots = [(k, tiles - 1) for k in (r, r + 1) if k < STEP]
                units.append(
                    (
                        functools.partial(full, spots),
                        functools.partial(place_full, spots=spots, ready=None),
                    )
                )
            done = 0
            for j in range(0, tiles - 1, 2):
                spots = [(r, j), (r, j + 1)]
                ready = side if j + 2 == tiles - 1 else 4 * j + 7
                units.append(
                    (
                        functools.partial(full, spots),
                        functools.partial(place_full, spots=spots, ready=(r, range(done, ready))),
                    )
                )
                done = ready
        waiting = None
        for issue, take in units:
            got = issue()
            if waiting is not None:
                waiting[0](waiting[1])
            waiting = (take, got)
        waiting[0](waiting[1])
        for copy in leaves(g):
            copy.start()
        return carry

    prepare()
    lax.fori_loop(0, steps, one_step, 0)
    for b in range(steps - 1, side // 2):
        second_rows(b, second_matmul(b))
    for copy in last_copies[1:]:
        copy.start()
    last_copies[0].wait()
    value, slope = soft(dot_rows(lw[...], h2[...]) + column(table[AT_LB, :]))
    enc[...] = value.astype(BF16)
    s3[...] = 0.5 * slope
    for g in range(steps):
        for copy in leaves(g):
            copy.wait()
    for copy in last_copies[1:]:
        copy.wait()


def three_parts(row):
    high = row.astype(BF16).astype(F32)
    middle = (row - high).astype(BF16).astype(F32)
    return jnp.concatenate([high, middle, row - high - middle], axis=0)


def with_ones(value):
    return jnp.concatenate([value, ones_rows(value.shape[1])], axis=0)


def ones_rows(lanes):
    return (iota((16, lanes), 0) < 3).astype(F32).astype(BF16)


def plan_kernel(
    section,
    slots,
    enc,
    s3,
    h2,
    branch_far,
    value_w,
    table,
    keep,
    send_one,
    send_two,
    small,
    g3,
    parts,
    bwt,
    vht,
    vhw,
    ow,
    mine,
    pre,
    dbr,
    dval,
    low,
    hid,
    gb,
    branch_w,
    sem,
    *,
    per_pair,
    depth,
):
    width = enc.shape[0]
    options = branch_w.shape[0]
    pairs = options // 2
    two = 2 * width
    sec = section[0]
    branch_copy = pltpu.make_async_copy(branch_far, branch_w, sem)
    branch_copy.start()

    count = slots.shape[0]
    dest = jnp.concatenate(
        [table[AT_DEST + k : AT_DEST + k + 1, :] for k in range(count // LANES)], axis=1
    )
    own = jnp.where(sec == 0, dest[:, :LANES], dest[:, LANES:])
    others = jnp.transpose(jnp.broadcast_to(dest, (LANES, count)))
    index = iota((count, LANES), 1) + sec * LANES
    earlier = (others == own) & (iota((count, LANES), 0) < index)
    rank = jnp.sum(earlier.astype(F32), axis=0, keepdims=True)
    bucket = own * float(per_pair) + rank
    chosen = (iota((count, LANES), 0).astype(F32) == bucket).astype(F32).astype(BF16)
    numbers = slots[:, : mine.shape[0]]
    high = numbers.astype(BF16)
    middle = (numbers - high.astype(F32)).astype(BF16)
    rest = (numbers - high.astype(F32) - middle.astype(F32)).astype(BF16)
    mine[...] = sum(dot_rows(v, chosen) for v in (rest, middle, high))

    pad = jnp.zeros((13, width), F32)
    branch_copy.wait()
    for o in range(options):
        rows = [branch_w[o].astype(F32), three_parts(table[o : o + 1, :]), pad]
        bwt[o * width : (o + 1) * width, :] = jnp.transpose(
            0.5 * jnp.concatenate(rows, axis=0)
        ).astype(BF16)
    scalars = table[AT_SCALARS, :]
    head_w = table[AT_HW, :]
    rows = [value_w[...].astype(F32), three_parts(table[AT_VB, :]), pad]
    vht[0:width, :] = jnp.transpose(0.5 * jnp.concatenate(rows, axis=0)).astype(BF16)
    vht[width:, :] = jnp.zeros((16, width + 16), BF16)
    lane = iota((1, 16), 1)
    for k in range(2):
        bias = three_parts(jnp.broadcast_to(scalars[:, 1 + k : 2 + k], (1, 16)))
        bias = sum(jnp.where(lane == j, bias[j : j + 1], 0.0) for j in range(3))
        vht[width + k : width + k + 1, 0:width] = head_w[k : k + 1].astype(BF16)
        vht[width + k : width + k + 1, width:] = bias.astype(BF16)
    vhw[:, 0:width] = (0.5 * value_w[...].astype(F32)).astype(BF16)
    vhw[:, width:] = jnp.transpose(
        0.5 * jnp.concatenate([head_w, jnp.zeros((14, width), F32)], axis=0)
    ).astype(BF16)
    ow[...] = jnp.broadcast_to(column(table[AT_OW, :]), (width, LANES))
    wide_ow = jnp.concatenate([ow[...], ow[...]], axis=1)
    half_ow = 0.5 * wide_ow

    labels = iota((options, LANES), 0).astype(F32)
    state = enc[...].astype(F32)
    rounded_all, saved = [], []
    group = 3
    for level in range(depth):
        picked = labels == mine[level : level + 1, :]
        rounded = state.astype(BF16)
        rounded_all.append(rounded)
        met = with_ones(rounded)

        def branches(first):
            at = slice(first * two, (first + group) * two)
            pre[at, :] = dot(bwt[at, :], met)

        branches(0)
        following = state
        reward, discount, value = [], [], []

        def value_part(t, got):
            act, slope = silu_pair(got[:width])
            dval[level, t] = slope
            hidden = act.astype(BF16)
            hid[level, t] = hidden
            worth = jnp.sum(hidden.astype(F32) * wide_ow, axis=0, keepdims=True)
            for k in range(2):
                span = slice(k * LANES, (k + 1) * LANES)
                value.append(worth[:, span])
                reward.append(got[width : width + 1, span])
                discount.append(got[width + 1 : width + 2, span])

        waiting = None
        for first in range(0, pairs, group):
            if first + group < pairs:
                branches(first + group)
            boths = []
            for t in range(first, first + group):
                at = slice(t * two, (t + 1) * two)
                act, slope = silu_pair(pre[at, :])
                dbr[level, at, :] = slope
                left = state + act[:width]
                right = state + act[width:]
                following = jnp.where(picked[2 * t : 2 * t + 1], left, following)
                following = jnp.where(picked[2 * t + 1 : 2 * t + 2], right, following)
                both = with_ones(
                    jnp.concatenate([left.astype(BF16), right.astype(BF16)], axis=1)
                )
                low[level, t] = both
                boths.append(both)
            got = dot(vht[...], jnp.concatenate(boths, axis=1))
            if waiting is not None:
                for k in range(group):
                    value_part(waiting[0] + k, waiting[1][:, k * two : (k + 1) * two])
            waiting = (first, got)
        for k in range(group):
            value_part(waiting[0] + k, waiting[1][:, k * two : (k + 1) * two])
        reward = jnp.concatenate(reward, axis=0)
        discount = jax.nn.sigmoid(jnp.concatenate(discount, axis=0))
        value = jnp.concatenate(value, axis=0) + scalars[:, 3:4]
        quality = reward + discount * value
        top = jnp.max(quality, axis=0, keepdims=True)
        shifted = jnp.exp(quality - top)
        total = jnp.sum(shifted, axis=0, keepdims=True)
        live = (mine[depth : depth + 1, :] > level).astype(F32)
        chosen = picked.astype(F32)

        def target(kind):
            at = depth + 1 + kind * depth + level
            return mine[at : at + 1, :]

        reward_gap = live * (jnp.sum(chosen * reward, axis=0, keepdims=True) - target(0))
        discount_gap = live * (jnp.sum(chosen * discount, axis=0, keepdims=True) - target(1))
        plan_gap = live * (top + jnp.log(total) - target(2))
        grad_quality = plan_gap * (shifted / total)
        head_two = (chosen * discount_gap + grad_quality * value) * discount * (1.0 - discount)
        saved.append(
            (
                picked,
                (chosen * reward_gap + grad_quality).astype(BF16).astype(F32),
                head_two.astype(BF16).astype(F32),
                (grad_quality * discount).astype(BF16).astype(F32),
                reward_gap * reward_gap + discount_gap * discount_gap + plan_gap * plan_gap,
            )
        )
        state = following

    out_sum = jnp.zeros((16, width), F32)
    value_sum = jnp.zeros((width + 16, width + 16), F32)
    grad_next = None
    line = iota((16, two), 0)
    for level in reversed(range(depth)):
        picked, head_one, head_two, grad_value, _ = saved[level]
        upward = jnp.zeros((width, LANES), F32)

        def branch_part(t, moved):
            at = slice(t * two, (t + 1) * two)
            left, right = moved[:, :LANES], moved[:, LANES:]
            if grad_next is not None:
                left = left + jnp.where(picked[2 * t : 2 * t + 1], grad_next, 0.0)
                right = right + jnp.where(picked[2 * t + 1 : 2 * t + 2], grad_next, 0.0)
            grad_branch = jnp.concatenate([left, right], axis=0) * dbr[level, at, :]
            grad_branch = grad_branch.astype(BF16)
            gb[level, at, :] = grad_branch
            return left + right

        def group_part(first, moved):
            parts = [
                branch_part(first + k, moved[:, k * two : (k + 1) * two]) for k in range(group)
            ]
            at = slice(first * two, (first + group) * two)
            weights = [branch_w[o] for o in range(2 * first, 2 * (first + group))]
            return sum(parts), dot(jnp.concatenate(weights, axis=1), gb[level, at, :])

        waiting = None
        for first in range(0, pairs, group):
            stack = []
            for t in range(first, first + group):

                def across(rows):
                    return jnp.concatenate(
                        [rows[2 * t : 2 * t + 1], rows[2 * t + 1 : 2 * t + 2]], axis=1
                    )

                worth = across(grad_value)
                grad_pre = (worth * half_ow * dval[level, t]).astype(BF16)
                heads = jnp.where(line == 0, across(head_one), 0.0)
                heads = jnp.where(line == 1, across(head_two), heads)
                heads = jnp.where(line == 2, worth, heads)
                heads = heads.astype(BF16)
                out_sum = out_sum + dot_lanes(heads, hid[level, t])
                stack.append(jnp.concatenate([grad_pre, heads], axis=0))
            stack = jnp.concatenate(stack, axis=1)
            moved = dot(vhw[...], stack)
            if waiting is not None:
                one, other = group_part(*waiting)
                upward = upward + (one + 0.5 * other)
            waiting = (first, moved)
            lows = jnp.concatenate([low[level, first + k] for k in range(group)], axis=1)
            value_sum = value_sum + dot_lanes(stack, lows)
        one, other = group_part(*waiting)
        grad_next = upward + (one + 0.5 * other)

    linear_rows = h2.shape[0]
    half = (linear_rows + options * width + width) // 2
    rest = linear_rows - half
    rounded = with_ones(jnp.concatenate(rounded_all, axis=1))
    small[...] = jnp.zeros_like(small)
    if half < keep.shape[0]:
        for k in range(2):
            parts[k, half:, :] = jnp.zeros((keep.shape[0] - half, LANES), BF16)
    for t in range(pairs):
        at = slice(t * two, (t + 1) * two)
        grads = jnp.concatenate([gb[level, at, :] for level in range(depth)], axis=1)
        got = dot_lanes(rounded, grads)
        for k in range(2):
            o = 2 * t + k
            span = slice(k * width, (k + 1) * width)
            rows = slice(rest + o * width, rest + (o + 1) * width)
            parts[1 - sec, rows, :] = got[:width, span].astype(BF16)
            small[o : o + 1, :] = got[width : width + 1, span]
    after = rest + options * width
    parts[1 - sec, after : after + width, :] = jnp.transpose(value_sum[:width, :width]).astype(BF16)

    grad_three = ((2.0 * grad_next).astype(BF16).astype(F32) * s3[...]).astype(BF16)
    g3[...] = grad_three
    chunk = linear_rows // 9
    for i in range(8):
        at = slice(i * chunk, (i + 1) * chunk)
        parts[sec, at, :] = dot_lanes(h2[at, :], grad_three).astype(BF16)
    last = dot_lanes(h2[8 * chunk :, :], grad_three).astype(BF16)
    parts[sec, 8 * chunk : half, :] = last[: half - 8 * chunk]
    parts[1 - sec, 0:rest, :] = last[half - 8 * chunk :]
    keep[...] = parts[0]
    send_one[...] = parts[1, : send_one.shape[0]]
    send_two[...] = parts[1, send_one.shape[0] :]

    small[AT_VB, :] = row_of(value_sum[:width, width : width + 1])
    small[AT_OW, :] = out_sum[2:3]
    small[AT_HW, :] = value_sum[width : width + 2, :width]
    small[AT_LB, :] = row_of(jnp.sum(grad_three.astype(F32), axis=1, keepdims=True))
    loss = 0.5 * jnp.sum(sum(kept[4] for kept in saved), axis=1, keepdims=True)
    ends = [loss] + [value_sum[width + k : width + k + 1, width : width + 1] for k in range(3)]
    lane = iota((1, LANES), 1)
    line = jnp.zeros((1, LANES), F32)
    for k, end in enumerate(ends):
        line = jnp.where(lane == k, end, line)
    small[AT_SCALARS, :] = line


def back_kernel(g3, lw, s2, s1, h1, w2t, g1, c2, sums, t2, g2):
    side, k1 = s1.shape[1], s1.shape[2]
    k2 = w2t.shape[0]
    inner = side // 2 - 1
    row_len = inner * k2
    half_g3 = (0.5 * g3[...].astype(F32)).astype(BF16)
    tap, pix = iota((LANES, 256), 1), iota((LANES, 256), 0)
    for yrel in range(2):
        for p in range(3):
            hit = (
                ((tap & 15) == (pix & 15))
                & ((tap >> 6) == (pix >> 6) + 2 * (1 - yrel))
                & (((tap >> 4) & 3) == ((pix >> 4) & 3) + 2 - 2 * p)
            )
            at = (yrel * 3 + p) * k2
            taps = dot_lanes(hit.astype(F32).astype(BF16), w2t[...])
            t2[:, at : at + k2] = (0.5 * taps).astype(BF16)
    g2[0] = jnp.zeros(g2.shape[1:], BF16)
    g2[inner + 1] = jnp.zeros(g2.shape[1:], BF16)
    g1[0] = jnp.zeros(g1.shape[1:], BF16)
    g1[side + 1] = jnp.zeros(g1.shape[1:], BF16)
    zero = jnp.zeros((k2, LANES), BF16)
    total_one = jnp.zeros((k1, LANES), F32)
    total_two = jnp.zeros((k2, LANES), F32)
    for y in range(inner):
        at = slice(y * row_len, (y + 1) * row_len)
        grad = dot(lw[at, :], half_g3) * s2[at, :].astype(F32)
        grad = grad.astype(BF16).reshape(inner, k2, LANES)
        g2[y + 1] = grad
        total_two = total_two + jnp.sum(grad.astype(F32), axis=0)
    reach, cols = 5, 8
    total = jnp.zeros((2 * reach * k2, 2 * cols * k1), F32)
    grads, tiles = [], []
    for b in range(side // 2):
        cut = []
        for j in range(side // 4):
            pieces = []
            for yrel in range(2):
                for p in range(3):
                    x = 2 * j - 1 + p
                    pieces.append(g2[b + yrel, x] if 0 <= x < inner else zero)
            cut.append(jnp.concatenate(pieces, axis=0))
        got = dot(t2[...], jnp.concatenate(cut, axis=1))
        for u in range(2):
            for j in range(side // 4):
                part = got[u * 64 : (u + 1) * 64, j * LANES : (j + 1) * LANES]
                slope = s1[2 * b + u + 1, 4 * j : 4 * j + 4].astype(F32)
                grad = (part.reshape(4, k1, LANES) * slope).astype(BF16)
                g1[2 * b + u + 1, 4 * j : 4 * j + 4] = grad
                total_one = total_one + jnp.sum(grad.astype(F32), axis=0)
        for j in range(-(-side // cols)):
            end = min((j + 1) * cols, side)
            tile = h1[2 * b + 1 : 2 * b + 3, j * cols : end]
            if end < (j + 1) * cols:
                rest = jnp.zeros((2, (j + 1) * cols - end, k1, LANES), BF16)
                tile = jnp.concatenate([tile, rest], axis=1)
            tiles.append(tile.reshape(2 * cols * k1, LANES))
            pieces = []
            for half in range(2):
                for p in range(reach):
                    x = 4 * j - 1 + p
                    pieces.append(g2[b + 1 - half, x] if 0 <= x < inner else zero)
            grads.append(jnp.concatenate(pieces, axis=0))
        if b % 2:
            total = total + dot_lanes(
                jnp.concatenate(grads, axis=1), jnp.concatenate(tiles, axis=1)
            )
            grads, tiles = [], []
    line = 4 * k1
    for half in range(2):
        for u in range(2):
            tap_row = jnp.zeros((k2, line), F32)
            for p in range(reach):
                at = (half * reach + p) * k2
                part = total[at : at + k2, u * 2 * line : (u + 1) * 2 * line]
                start = 2 * k1 * (p - 1)
                piece = part[:, max(start, 0) : min(start + line, 2 * line)]
                if start < 0:
                    piece = jnp.concatenate([jnp.zeros((k2, -start), F32), piece], axis=1)
                if start + line > 2 * line:
                    rest = jnp.zeros((k2, start - line), F32)
                    piece = jnp.concatenate([piece, rest], axis=1)
                tap_row = tap_row + piece
            at = (2 * half + u) * line
            c2[:, at : at + line] = tap_row
    sums[...] = jnp.zeros_like(sums)
    sums[0:1, 0:k1] = row_of(jnp.sum(total_one, axis=1, keepdims=True))
    sums[1:2, 0:k2] = row_of(jnp.sum(total_two, axis=1, keepdims=True))


def pixel_band(sec, w1t, channels):
    k1 = w1t.shape[0]
    rows = 64 * channels
    row, tap = iota((rows, 256), 0), iota((rows, 256), 1)
    moves = ((tap >> 6) == row % channels + sec * channels) & ((tap & 63) == row // channels)
    taps = dot_lanes(moves.astype(F32).astype(BF16), w1t)
    line, span = COLS * channels, 8 * channels
    blocks = {}
    for half in range(2):
        for p in range(NEAR):
            pieces = []
            for u in range(4):
                at = (4 * half + u) * span
                start = 4 * (p - 1) * channels
                cut = taps[at + max(0, -start) : at + min(span, line - start)]
                start = max(start, 0)
                pieces += [jnp.zeros((start, k1), F32)] if start else []
                pieces.append(cut)
                rest = line - start - cut.shape[0]
                pieces += [jnp.zeros((rest, k1), F32)] if rest else []
            blocks[half, p] = jnp.concatenate(pieces, axis=0)
    zero = jnp.zeros((4 * line, k1), F32)
    lines = []
    for r in range(STEP):
        cols = [
            blocks.get((r + 1 - yrel, p), zero) for yrel in range(STEP + 1) for p in range(NEAR)
        ]
        lines.append(jnp.concatenate(cols, axis=1))
    return jnp.concatenate(lines, axis=0).astype(BF16)


def first_kernel(
    section,
    frames_far,
    g1,
    w1t,
    other_far,
    after,
    c1,
    out,
    band,
    frames,
    acc,
    other,
    held,
    sems,
    draw_sems,
    *,
    draw,
):
    side, k1 = g1.shape[1], g1.shape[2]
    img, _, channels, _ = frames.shape
    steps = img // 4 // STEP
    arrives = frame_copies(section, frames_far, frames, sems)
    for g in range(steps):
        arrives(g).start()
    other_copy = pltpu.make_async_copy(
        other_far.at[0 : STEP * draw + 1], other, sems.at[steps]
    )
    other_copy.start()
    acc[...] = jnp.zeros_like(acc)
    zero = jnp.zeros((k1, LANES), BF16)

    def one_step(g, carry):
        arrives(g).wait()
        pixels, grads = [], []
        for j in range(img // COLS):
            rows = [pl.multiple_of(4 * (STEP * g + r), 4) for r in range(STEP)]
            pixels.append(
                jnp.concatenate([tile_rows(frames, row, j, COLS) for row in rows], axis=0)
            )
            pieces = []
            for yrel in range(STEP + 1):
                for p in range(NEAR):
                    x = 3 * j - 1 + p
                    pieces.append(g1[STEP * g + yrel, x] if 0 <= x < side else zero)
            grads.append(jnp.concatenate(pieces, axis=0))
        acc[...] += dot_lanes(jnp.concatenate(pixels, axis=1), jnp.concatenate(grads, axis=1))
        return carry

    lax.fori_loop(0, steps, one_step, 0)
    band[...] = pixel_band(section[0], w1t[...], out.shape[2])
    other_copy.wait()
    finish = draw_steps(section, band, g1, 0, other, 0, out, held, draw_sems, 0, draw)
    fold_first(acc, c1, channels, k1)
    finish()


def fold_first(acc, c1, channels, k1):
    line = COLS * channels
    step = 4 * channels
    taps = []
    for half in range(2):
        total = sum(
            acc[r * 4 * line : (r + 1) * 4 * line, :][
                :, (r + 1 - half) * NEAR * k1 : (r + 2 - half) * NEAR * k1
            ]
            for r in range(STEP)
        )
        for u in range(4):
            part = total[u * line : (u + 1) * line]
            cols = [part[:, p * k1 : (p + 1) * k1] for p in range(NEAR)]
            taps.append(cols[1][0:step] + cols[2][step : 2 * step] + cols[3][2 * step :])
            taps.append(cols[0][0:step] + cols[1][step : 2 * step] + cols[2][2 * step :])
    row, col = iota((256, 256), 0), iota((256, 256), 1)
    moves = ((row & 3) == (col >> 6)) & ((row >> 2) == (col & 63))
    grad = dot_rows(jnp.concatenate(taps, axis=0), moves.astype(F32), EXACT)
    for half in range(2):
        c1[half * k1 : (half + 1) * k1, :] = grad[:, half * LANES : (half + 1) * LANES].astype(BF16)


def draw_steps(section, band, mine, mine_at, other, other_at, out, held, sems, start, steps):
    side, k1 = mine.shape[1], mine.shape[2]
    img, channels = out.shape[1], out.shape[2]
    sec = section[0]
    line = COLS * channels
    flat = held.reshape(2, 2, 4 * STEP, img * channels, LANES)

    def writes(g):
        rows = slice(4 * STEP * (start + g), 4 * STEP * (start + g + 1))
        places = (sec * LANES, (1 - sec) * LANES)
        return [
            pltpu.make_async_copy(
                held.at[g % 2, k],
                out.at[rows, :, :, pl.ds(pl.multiple_of(places[k], LANES), LANES)],
                sems.at[g % 2, k],
            )
            for k in range(2)
        ]

    zero = jnp.zeros((k1, 2 * LANES), BF16)
    for g in range(steps):
        if g >= 2:
            for copy in writes(g - 2):
                copy.wait()
        for j in range(img // COLS):
            pieces = []
            for yrel in range(STEP + 1):
                for p in range(NEAR):
                    x, y = 3 * j - 1 + p, STEP * (start + g) + yrel
                    if 0 <= x < side:
                        pair = [mine[y - mine_at, x], other[y - other_at, x]]
                        pieces.append(jnp.concatenate(pair, axis=1))
                    else:
                        pieces.append(zero)
            got = dot(band[...], jnp.concatenate(pieces, axis=0))
            for k in range(4 * STEP):
                at = slice(k * line, (k + 1) * line)
                span = slice(j * line, (j + 1) * line)
                flat[g % 2, 0, k, span, :] = got[at, :LANES]
                flat[g % 2, 1, k, span, :] = got[at, LANES:]
        for copy in writes(g):
            copy.start()

    def finish():
        for g in range(max(steps - 2, 0), steps):
            for copy in writes(g):
                copy.wait()

    return finish


def pixels_kernel(section, band, mine, other_far, after, done, out, token, held, other, sems, *, start):
    steps = other.shape[0] // STEP
    fetch = pltpu.make_async_copy(
        other_far.at[STEP * start : STEP * (start + steps) + 1], other, sems.at[2, 0]
    )
    fetch.start()
    token[...] = jnp.zeros_like(token)
    fetch.wait()
    draw_steps(
        section, band, mine, 0, other, STEP * start, out, held, sems, start, steps
    )()


def two_parts(value):
    high = value.astype(BF16).astype(F32)
    return jnp.concatenate([high, value - high], axis=0).astype(BF16)


def one_part(pair):
    rows = pair.shape[0] // 2
    pair = pair.astype(F32)
    return pair[:rows] + pair[rows:]


def merge_kernel(keep, recv_one, recv_two, small, c2, sums, out_far, lines, out, sems):
    members = out.shape[0]
    size = keep.shape[0] // members
    lines[...] = small[...]
    lines[AT_B1, :] = sums[0:1, :]
    lines[AT_B2, :] = sums[1:2, :]
    for k in range(members):
        at = slice(k * size, (k + 1) * size)
        recv, here = recv_one, k
        if k >= members // 2:
            recv, here = recv_two, k - members // 2
        got = recv[here * size : (here + 1) * size, :]
        out[k, 0:size, :] = keep[at, :] + got
        if k < members // 2:
            rows, span = c2_place(k)
            out[k, size:, :] = c2[rows, span].astype(BF16)
        else:
            out[k, size:, :] = two_parts(lines[table_place(k), :])
        pltpu.make_async_copy(out.at[k], out_far.at[k], sems.at[k]).start()
    for k in range(members):
        pltpu.make_async_copy(out.at[k], out_far.at[k], sems.at[k]).wait()


def c2_place(k):
    return slice(k % 2 * SHORT, (k % 2 + 1) * SHORT), slice(k // 2 * LANES, (k // 2 + 1) * LANES)


def table_place(k):
    at = (k - CUBE // 2) * SHORT // 2
    return slice(at, at + SHORT // 2)


def riders(batch, parts):
    plain = sum(p.astype(F32) for p in parts).astype(BF16)
    fine = two_parts(sum(one_part(p) for p in parts))
    return jnp.where(batch[0] % CUBE < CUBE // 2, plain.astype(F32), fine.astype(F32)).astype(BF16)


def cube_kernel(batch, got, c1, out):
    members = got.shape[0]
    size = got.shape[1] - SHORT
    out[0:size, :] = sum(got[k, 0:size, :].astype(F32) for k in range(members)).astype(BF16)
    out[size : size + SHORT, :] = riders(batch, [got[k, size:, :] for k in range(members)])
    out[size + SHORT :, :] = c1[...]


def add_kernel(batch, a, b, after, out):
    size = a.shape[0] - SHORT - 32
    for span in (slice(0, size), slice(size + SHORT, a.shape[0])):
        out[span, :] = (a[span, :].astype(F32) + b[span, :].astype(F32)).astype(BF16)
    ride = slice(size, size + SHORT)
    out[ride, :] = riders(batch, [a[ride, :], b[ride, :]])


def relay_kernel(batch, *refs):
    parts, (one, two, out) = refs[:CUBE], refs[-3:]
    me = batch[0] % CUBE
    for k, part in zip(TURNS, parts):
        out[me ^ k] = part[...]
    one[...] = out[: CUBE // 2]
    two[...] = out[CUBE // 2 :]


def piece_of(got, k):
    count = got[0].shape[0]
    return got[k // count].at[k % count]


def unpack_half(which, got, lw, bw, vw, stage, stage_b, sems):
    members = 2 * got[0].shape[0]
    size = stage.shape[0] // members
    linear_rows, width = lw.shape
    options = bw.shape[0]
    half = (linear_rows + options * width + width) // 2
    rest = linear_rows - half
    group = options // 3

    def first_copies():
        spans = [(k * size, min((k + 1) * size, half)) for k in range(members)]
        return [
            pltpu.make_async_copy(stage.at[a:b], lw.at[a:b], sems.at[k])
            for k, (a, b) in enumerate(spans)
        ]

    def second_copies():
        copies = [pltpu.make_async_copy(stage.at[0:rest], lw.at[half:], sems.at[0])]
        for k in range(options // group):
            part = slice(k * group, (k + 1) * group)
            copies.append(pltpu.make_async_copy(stage_b.at[part], bw.at[part], sems.at[1 + k]))
        last = stage.at[rest : rest + width]
        copies.append(pltpu.make_async_copy(last, vw, sems.at[len(copies)]))
        return copies

    @pl.when(which == 0)
    def _():
        for k, copy in enumerate(first_copies()):
            start, end = k * size, min((k + 1) * size, half)
            stage[start:end, :] = piece_of(got, k)[0 : end - start, :].astype(F32)
            copy.start()

    @pl.when(which == 1)
    def _():
        def rows(start, end):
            parts = []
            while start < end:
                k, at = start // size, start % size
                count = min(size - at, end - start)
                parts.append(piece_of(got, k)[at : at + count, :])
                start += count
            value = parts[0] if len(parts) == 1 else jnp.concatenate(parts, axis=0)
            return value.astype(F32)

        copies = second_copies()
        stage[0:rest, :] = rows(0, rest)
        copies[0].start()
        for o in range(options):
            stage_b[o] = rows(rest + o * width, rest + (o + 1) * width)
            if o % group == group - 1:
                copies[1 + o // group].start()
        at = rest + options * width
        stage[rest : rest + width, :] = rows(at, at + width)
        copies[-1].start()

    def finish():
        for half_at, copies in ((0, first_copies), (1, second_copies)):

            @pl.when(which == half_at)
            def _():
                for copy in copies():
                    copy.wait()

    return finish


def own_kernel(section, one, two, lw, bw, vw, stage, stage_b, sems):
    unpack_half(section[0], (one, two), lw, bw, vw, stage, stage_b, sems)()


def unpack_kernel(section, *refs):
    mine, other, refs = refs[0:2], refs[2:4], refs[4:]
    lw, bw, vw = refs[3:6]
    little = (len(refs) - 10) // 2
    far, near = refs[6 : 6 + little], refs[6 + little : 6 + 2 * little]
    loss, c1, b1, c2, b2, lb, bb, hw, hb, vb, ow, ob = near
    stage, stage_b, lines, sems = refs[-4:]
    options = bw.shape[0]
    k1, k2 = c1.shape[0], c2.shape[0]
    size = stage.shape[0] // CUBE
    finish = unpack_half(1 - section[0], other, lw, bw, vw, stage, stage_b, sems)
    grad = [jnp.zeros((k1, LANES), F32) for _ in range(2)]
    ride = slice(size, size + SHORT)
    for k in range(CUBE):
        views = piece_of(mine, k), piece_of(other, k)
        if k < CUBE // 2:
            c2[c2_place(k)] = sum(v[ride, :].astype(F32) for v in views)
        else:
            lines[table_place(k), :] = sum(one_part(v[ride, :]) for v in views)
        for view in views:
            for h in range(2):
                at = size + SHORT + h * k1
                grad[h] += view[at : at + k1, :].astype(F32)
    for part in range(2):
        c1[:, part * LANES : (part + 1) * LANES] = grad[part]
    bb[...] = lines[0:options, :]
    vb[...] = lines[AT_VB, :]
    ow[...] = lines[AT_OW, :]
    hw[...] = lines[AT_HW, :]
    lb[...] = lines[AT_LB, :]
    scalars = lines[AT_SCALARS, :]
    loss[...] = scalars[:, 0:1]
    hb[...] = scalars[:, 1:3]
    ob[...] = scalars[:, 3:4]
    b1[...] = lines[AT_B1, 0:k1]
    b2[...] = lines[AT_B2, 0:k2]
    copies = [
        pltpu.make_async_copy(a, b, sems.at[CUBE + k]) for k, (a, b) in enumerate(zip(near, far))
    ]
    for copy in copies:
        copy.start()
    finish()
    for copy in copies:
        copy.wait()


def numbers_kernel(
    options,
    depth,
    targets,
    destination,
    b1,
    b2,
    lb,
    bb,
    hw,
    vb,
    ow,
    hb,
    ob,
    out,
    table,
):
    levels, kinds = options.shape[0], targets.shape[0]
    slots = depth.shape[1]
    rows = [options[...].astype(F32), depth[...].astype(F32)]
    rows += [targets[k] for k in range(kinds)]
    rows.append(jnp.zeros((LANES - levels - 1 - kinds * levels, slots), F32))
    out[...] = jnp.transpose(jnp.concatenate(rows, axis=0))
    table[...] = jnp.zeros_like(table)
    table[0 : bb.shape[0], :] = bb[...]
    table[AT_VB, :] = vb[...]
    table[AT_OW, :] = ow[...].astype(F32)
    table[AT_HW, :] = hw[...].astype(F32)
    table[AT_LB, :] = lb[...]
    table[AT_B1, 0 : b1.shape[1]] = b1[...]
    table[AT_B2, 0 : b2.shape[1]] = b2[...]
    lane = iota((1, LANES), 1)
    scalars = jnp.zeros((1, LANES), F32)
    for k, value in ((1, hb[:, 0:1]), (2, hb[:, 1:2]), (3, ob[...])):
        scalars = jnp.where(lane == k, value, scalars)
    table[AT_SCALARS, :] = scalars
    for k in range(slots // LANES):
        part = destination[:, k * LANES : (k + 1) * LANES]
        table[AT_DEST + k : AT_DEST + k + 1, :] = part.astype(F32)


def whole(shape):
    zeros = (0,) * len(shape)
    return pl.BlockSpec(shape, lambda *_: zeros)


ANYWHERE = pl.BlockSpec(memory_space=pl.ANY)
SCALARS = pl.BlockSpec(memory_space=pltpu.SMEM)


def params():
    return pltpu.CompilerParams(vmem_limit_bytes=VMEM_BYTES)


def shape_of(*shape, dtype=F32):
    return jax.ShapeDtypeStruct(shape, dtype)


def cost(microseconds):
    return pl.CostEstimate(
        flops=int(1.1e9 * microseconds), bytes_accessed=int(3.6e6 * microseconds), transcendentals=0
    )


def stays(value):
    return pltpu.with_memory_space_constraint(value, pltpu.HBM)


def held_near(value):
    return pltpu.with_memory_space_constraint(value, pltpu.VMEM)


def encode(section, frames, w1t, w2t, lw, table):
    img = frames.shape[0]
    blocks = img // 4
    side = blocks - 1
    k1, k2, width = w1t.shape[0], w2t.shape[0], lw.shape[1]
    flat = lw.shape[0]
    vmem = pltpu.VMEM
    near = pl.BlockSpec(memory_space=vmem)
    grid_one = (blocks, side, k1, LANES)
    return pl.pallas_call(
        encode_kernel,
        in_specs=[SCALARS, ANYWHERE, near, near, ANYWHERE, near],
        out_specs=[ANYWHERE] * 3 + [near] * 3,
        out_shape=(
            pltpu.HBM(grid_one, BF16),
            pltpu.HBM(grid_one, BF16),
            pltpu.HBM((flat, LANES), BF16),
            shape_of(flat, LANES, dtype=BF16),
            shape_of(width, LANES, dtype=BF16),
            shape_of(width, LANES),
        ),
        scratch_shapes=[
            vmem((img, img, frames.shape[2], LANES), BF16),
            vmem(lw.shape, BF16),
            vmem(grid_one, BF16),
            vmem(grid_one, BF16),
            vmem((flat, LANES), BF16),
            vmem((2 * REACH * k1, 256), BF16),
            vmem((2 * k1, 64), BF16),
            vmem((6 * k2, LANES), BF16),
            vmem((k1, LANES), F32),
            vmem((k2, LANES), F32),
            vmem((side, k1, LANES), F32),
            vmem((side // 2 - 1, k2, LANES), F32),
            pltpu.SemaphoreType.DMA((4, max(blocks // STEP, 3))),
        ],
        compiler_params=params(),
        cost_estimate=cost(9),
        name="encode",
    )(section, frames, w1t, w2t, lw, table)


def plan(section, slots, enc, s3, h2, branch_w, value_w, table, per_pair, depth, half_rows):
    width = enc.shape[0]
    options = branch_w.shape[0]
    two = 2 * width
    pairs = options // 2
    outs = (
        shape_of(half_rows, LANES, dtype=BF16),
        shape_of(half_rows // 2, LANES, dtype=BF16),
        shape_of(half_rows // 2, LANES, dtype=BF16),
        shape_of(TABLE, LANES),
        shape_of(width, LANES, dtype=BF16),
    )
    vmem = pltpu.VMEM
    near = pl.BlockSpec(memory_space=vmem)
    return pl.pallas_call(
        functools.partial(plan_kernel, per_pair=per_pair, depth=depth),
        in_specs=[SCALARS, near, near, near, near, ANYWHERE, near, near],
        out_shape=outs,
        scratch_shapes=[
            vmem((2, half_rows, LANES), BF16),
            vmem((options * width, width + 16), BF16),
            vmem((width + 16, width + 16), BF16),
            vmem((width, width + 16), BF16),
            vmem((width, LANES), F32),
            vmem((16, LANES), F32),
            vmem((options * width, LANES), F32),
            vmem((depth, options * width, LANES), F32),
            vmem((depth, pairs, width, two), F32),
            vmem((depth, pairs, width + 16, two), BF16),
            vmem((depth, pairs, width, two), BF16),
            vmem((depth, options * width, LANES), BF16),
            vmem(branch_w.shape, BF16),
            pltpu.SemaphoreType.DMA,
        ],
        compiler_params=params(),
        cost_estimate=cost(11),
        name="plan",
    )(section, slots, enc, s3, h2, branch_w, value_w, table)


def back(g3, lw, s2, s1, h1, w2t):
    _, side, k1 = s1.shape[:3]
    k2 = w2t.shape[0]
    inner = side // 2 - 1
    padded = (side + 2, side, k1, LANES)
    near = pl.BlockSpec(memory_space=pltpu.VMEM)
    return pl.pallas_call(
        back_kernel,
        in_specs=[near] * 6,
        out_shape=(shape_of(*padded, dtype=BF16), shape_of(k2, 256), shape_of(8, LANES)),
        scratch_shapes=[
            pltpu.VMEM((LANES, 6 * k2), BF16),
            pltpu.VMEM((inner + 2, inner, k2, LANES), BF16),
        ],
        compiler_params=params(),
        cost_estimate=cost(25),
        name="back",
    )(g3, lw, s2, s1, h1, w2t)


def first(section, frames, g1, w1t, other, after, channels, draw):
    img, _, stack, _ = frames.shape
    k1 = g1.shape[2]
    band = (STEP * 4 * COLS * channels, (STEP + 1) * NEAR * k1)
    near = pl.BlockSpec(memory_space=pltpu.VMEM)
    return pl.pallas_call(
        functools.partial(first_kernel, draw=draw),
        in_specs=[SCALARS, ANYWHERE, near, near, ANYWHERE, ANYWHERE],
        out_specs=[near, ANYWHERE, near],
        out_shape=[
            shape_of(2 * k1, LANES, dtype=BF16),
            shape_of(img, img, channels, 2 * LANES),
            shape_of(*band, dtype=BF16),
        ],
        scratch_shapes=[
            pltpu.VMEM((img, img, stack, LANES), BF16),
            pltpu.VMEM((STEP * 4 * COLS * stack, (STEP + 1) * NEAR * k1), F32),
            pltpu.VMEM((STEP * draw + 1,) + g1.shape[1:], BF16),
            pltpu.VMEM((2, 2, 4 * STEP, img, channels, LANES), F32),
            pltpu.SemaphoreType.DMA((img // 4 // STEP + 1,)),
            pltpu.SemaphoreType.DMA((2, 2)),
        ],
        compiler_params=params(),
        cost_estimate=cost(45),
        name="first",
    )(section, frames, g1, w1t, other, after)


def pixels(section, band, mine, other, after, done, start, steps):
    img, _, channels, _ = done.shape
    near = pl.BlockSpec(memory_space=pltpu.VMEM)
    return pl.pallas_call(
        functools.partial(pixels_kernel, start=start),
        in_specs=[SCALARS, near, near, ANYWHERE, ANYWHERE, ANYWHERE],
        out_specs=[ANYWHERE, near],
        out_shape=[shape_of(*done.shape), shape_of(8, LANES)],
        scratch_shapes=[
            pltpu.VMEM((2, 2, 4 * STEP, img, channels, LANES), F32),
            pltpu.VMEM((STEP * steps + 1,) + mine.shape[1:], BF16),
            pltpu.SemaphoreType.DMA((3, 2)),
        ],
        input_output_aliases={5: 0},
        compiler_params=params(),
        cost_estimate=cost(1 + 0.9 * steps),
        name="pixels",
    )(section, band, mine, other, after, done)


def small_call(
    kernel, outs, operands, scratch=(), name=None, place=None, after=(), weight=0.3, far=False
):
    specs = [pl.BlockSpec(memory_space=pltpu.VMEM)] * len(operands)
    if place is not None:
        operands = (*place, *operands)
        specs = [pl.BlockSpec(memory_space=pltpu.SMEM)] * len(place) + specs
    return pl.pallas_call(
        kernel,
        in_specs=specs + [ANYWHERE] * len(after),
        out_specs=jax.tree.map(
            lambda _: ANYWHERE if far else pl.BlockSpec(memory_space=pltpu.VMEM), outs
        ),
        out_shape=outs,
        scratch_shapes=list(scratch),
        compiler_params=params(),
        cost_estimate=cost(weight),
        name=name,
    )(*operands, *after)


def round_up(value, step):
    return -(-value // step) * step


def swapped(value):
    return lax.ppermute(value, "section", [(0, 1), (1, 0)])


def exchanged(value, groups=None):
    return lax.all_to_all(
        value, "batch", split_axis=0, concat_axis=0, axis_index_groups=groups, tiled=True
    )


def partner(value, distance):
    count = lax.axis_size("batch")
    return lax.ppermute(value, "batch", [(b, b ^ distance) for b in range(count)])


def local(
    frames,
    destination,
    options,
    depth,
    targets,
    conv_one,
    bias_one,
    conv_two,
    bias_two,
    linear_w,
    linear_b,
    branch_w,
    branch_b,
    head_w,
    head_b,
    value_w,
    value_b,
    out_w,
    out_b,
):
    section = lax.axis_index("section").astype(jnp.int32)[None]
    peers = lax.axis_size("batch")
    frame_count = frames.shape[3]
    per_pair = frame_count // peers
    levels = options.shape[0]
    frames = stays(frames.transpose(1, 2, 0, 3))
    w1t, w2t = stays(conv_one.T), stays(conv_two.T)
    branch_w, value_w = stays(branch_w), stays(value_w)
    encoder_params = (w1t, bias_one, w2t, bias_two, linear_w, linear_b)
    planner_params = (branch_w, branch_b, head_w.T, head_b, value_w, value_b, out_w.T, out_b)
    width = linear_w.shape[1]
    big_rows = linear_w.shape[0] + (branch_w.shape[0] + 1) * width
    size = round_up(-(-big_rows // (2 * CUBE)), 16)

    tiny = (bias_one, bias_two, linear_b, branch_b, head_w.T, value_b, out_w.T)
    tiny = [stays(v if v.ndim > 1 else v[None, :]) for v in tiny]
    numbers, table = pl.pallas_call(
        numbers_kernel,
        in_specs=[pl.BlockSpec(memory_space=pltpu.VMEM)] * (6 + len(tiny)),
        out_shape=[shape_of(frame_count, LANES), shape_of(TABLE, LANES)],
        compiler_params=params(),
        cost_estimate=cost(1),
        name="numbers",
    )(
        stays(options),
        stays(depth[None, :]),
        stays(targets),
        stays(destination[None, :]),
        *tiny,
        stays(head_b[None, :]),
        out_b[None, :],
    )
    slots = exchanged(numbers.reshape(peers, per_pair, LANES)).reshape(frame_count, LANES)

    h1, s1, s2, h2, enc, s3 = encode(section, frames, w1t, w2t, stays(linear_w), table)
    keep, send_one, send_two, small, g3 = plan(
        section, slots, enc, s3, h2, branch_w, value_w, table, per_pair, levels, CUBE * size
    )
    recv = swapped(send_one), swapped(send_two)
    channels = frames.shape[2] // lax.axis_size("section")
    g1, c2, sums = back(g3, linear_w, s2, s1, h1, w2t)
    other = swapped(g1)
    g1 = held_near(g1)
    place = (lax.axis_index("batch").astype(jnp.int32)[None],)
    cubes = [list(range(c, c + CUBE)) for c in range(0, peers, CUBE)]
    bf16 = functools.partial(shape_of, dtype=BF16)
    pieces = small_call(
        merge_kernel,
        bf16(CUBE, size + SHORT, LANES),
        (keep, *recv, small, c2, sums),
        [
            pltpu.VMEM((TABLE, LANES), F32),
            pltpu.VMEM((CUBE, size + SHORT, LANES), BF16),
            pltpu.SemaphoreType.DMA((CUBE,)),
        ],
        name="merge",
        far=True,
        weight=30,
    )
    got = exchanged(pieces, cubes)
    c1, frames_grad, band = first(section, frames, g1, w1t, other, pieces, channels, DRAW)
    piece = bf16(size + SHORT + c1.shape[0], LANES)
    keep = small_call(cube_kernel, piece, (got, c1), name="cube", place=place)
    distance = CUBE
    while distance < peers:
        recv = partner(keep, distance)
        if distance == CUBE:
            left = frames.shape[0] // 4 // STEP - DRAW
            frames_grad, token = pixels(
                section, band, g1, other, keep, frames_grad, DRAW, left
            )
        distance *= 2
        keep = small_call(
            add_kernel, piece, (keep, recv), name="add", place=place, after=(token,)
        )
    parts = [partner(keep, k) if k else keep for k in TURNS]
    got = small_call(
        relay_kernel,
        [bf16(CUBE // 2, *piece.shape)] * 2,
        parts,
        [pltpu.VMEM((CUBE, *piece.shape), BF16)],
        name="relay",
        place=place,
    )
    got_other = [swapped(v) for v in got]
    shapes = [p.shape for p in encoder_params + planner_params]
    near = pl.BlockSpec(memory_space=pltpu.VMEM)
    flat = [shape_of(*(v if len(v) > 1 else (1,) + v)) for v in [(1, 1)] + shapes]
    large = [flat[k] for k in (5, 7, 11)]
    staged = [
        pltpu.VMEM((CUBE * size, LANES), F32),
        pltpu.VMEM(branch_w.shape, F32),
    ]
    little = [v for k, v in enumerate(flat) if k not in (5, 7, 11)]
    sems = pltpu.SemaphoreType.DMA((CUBE + len(little),))
    begun = pl.pallas_call(
        own_kernel,
        in_specs=[SCALARS, near, near],
        out_specs=[ANYWHERE] * 3,
        out_shape=large,
        scratch_shapes=[*staged, sems],
        compiler_params=params(),
        cost_estimate=cost(1),
        name="own",
    )(section, *got)
    ends = pl.pallas_call(
        unpack_kernel,
        in_specs=[SCALARS] + [near] * 4 + [ANYWHERE] * 3,
        out_specs=[ANYWHERE] * (3 + len(little)),
        out_shape=large + little,
        scratch_shapes=[pltpu.VMEM(v.shape, F32) for v in little]
        + [*staged, pltpu.VMEM((TABLE, LANES), F32), sems],
        input_output_aliases={5: 0, 6: 1, 7: 2},
        compiler_params=params(),
        cost_estimate=cost(1.5),
        name="unpack",
    )(section, *got, *got_other, *begun)
    rest = list(ends[3:])
    for k, at in enumerate((5, 7, 11)):
        rest.insert(at, ends[k])
    rest = [v.reshape(s) for v, s in zip(rest, [()] + shapes)]
    for at in (1, 3, 9, 13):
        rest[at] = rest[at].T
    return (rest[0], frames_grad.transpose(2, 0, 1, 3), *rest[1:])


def solution(mesh):
    placed = (
        P(None, None, None, "batch"),
        P("batch"),
        P(None, "batch"),
        P("batch"),
        P(None, None, "batch"),
    ) + (P(),) * 14
    return jax.shard_map(
        local,
        mesh=mesh,
        in_specs=placed,
        out_specs=(P(), P("section", None, None, "batch")) + (P(),) * 14,
        check_vma=False,
    )
```

```python
import functools
import math

import jax
import jax.numpy as jnp
from jax import lax
from jax.experimental import pallas as pl
from jax.experimental.pallas import tpu as pltpu
from jax.sharding import PartitionSpec as P

BF16 = jnp.bfloat16
F32 = jnp.float32
EXACT = lax.Precision.HIGHEST
LANES = 128
VMEM_BYTES = 32 * 1024 * 1024
TILE = 16
REACH = 5
STEP = 3
COLS = 12
NEAR = 4
AT_VB, AT_OW, AT_HW, AT_LB, AT_SCALARS, AT_B1, AT_B2, AT_DEST = (
    slice(18, 19),
    slice(19, 20),
    slice(20, 22),
    slice(22, 23),
    slice(23, 24),
    slice(24, 25),
    slice(25, 26),
    26,
)
TABLE = 32
CUBE = 8
TURNS = (0, 4, 3, 2, 5, 1, 6, 7)
DRAW = 3
DRAW_ACROSS = 3
SHORT = 16


def dot(a, b, precision=None):
    return jnp.dot(a, b, preferred_element_type=F32, precision=precision)


def dot_rows(a, b, precision=None):
    return lax.dot_general(
        a, b, (((0,), (0,)), ((), ())), preferred_element_type=F32, precision=precision
    )


def dot_lanes(a, b, precision=None):
    return lax.dot_general(
        a, b, (((1,), (1,)), ((), ())), preferred_element_type=F32, precision=precision
    )


def iota(shape, axis):
    return lax.broadcasted_iota(jnp.int32, shape, axis)


def column(row):
    n = row.shape[1]
    wide = jnp.broadcast_to(row, (n, n))
    return jnp.sum(jnp.where(iota((n, n), 0) == iota((n, n), 1), wide, 0.0), axis=1, keepdims=True)


def row_of(col):
    n = col.shape[0]
    wide = jnp.broadcast_to(col, (n, n))
    return jnp.sum(jnp.where(iota((n, n), 0) == iota((n, n), 1), wide, 0.0), axis=0, keepdims=True)


def soft(x):
    t = jnp.tanh(0.5 * x)
    return jnp.maximum(x, 0.0) - jnp.log(0.5 + 0.5 * jnp.abs(t)), 1.0 + t


def silu_pair(y):
    t = jnp.tanh(y)
    m = y * t
    return y + m, (1.0 + t) + (y - m * t)


def pixel_order(w1t):
    tap, pix = iota((256, 256), 0), iota((256, 256), 1)
    moves = ((tap >> 6) == (pix & 3)) & ((tap & 63) == (pix >> 2))
    return dot(w1t, moves.astype(F32).astype(BF16))


def frame_copies(section, far, here, sems):
    lanes = pl.ds(pl.multiple_of(section[0] * LANES, LANES), LANES)
    size = 4 * STEP

    def copy(g):
        rows = pl.ds(pl.multiple_of(g * size, size), size)
        return pltpu.make_async_copy(far.at[rows, :, :, lanes], here.at[rows], sems.at[g])

    return copy


def tile_rows(frames, row, j, cols):
    img, _, channels, _ = frames.shape
    flat = frames.reshape(img, img * channels, LANES)
    size = cols * channels
    end = min((j + 1) * size, img * channels)
    part = flat[pl.ds(row, 4), j * size : end, :]
    return part.reshape(4 * (end - j * size), LANES)


def encode_kernel(
    section,
    frames_far,
    w1t,
    w2t,
    lw_far,
    table,
    h1_far,
    s1_far,
    s2_far,
    h2,
    enc,
    s3,
    frames,
    lw,
    h1,
    s1,
    s2,
    band,
    edge,
    band2,
    bias1,
    bias2,
    held,
    held2,
    sems,
):
    blocks, side = h1.shape[:2]
    steps = blocks // STEP
    tiles = frames.shape[1] // TILE
    k1, k2 = w1t.shape[0], w2t.shape[0]
    reach_rows = REACH * k1
    arrives = frame_copies(section, frames_far, frames, sems.at[0])
    for g in range(steps):
        arrives(g).start()
    last_copies = [
        pltpu.make_async_copy(lw_far, lw, sems.at[3, 0]),
        pltpu.make_async_copy(s2, s2_far, sems.at[3, 1]),
    ]
    last_copies[0].start()

    def leaves(g):
        rows = pl.ds(g * STEP, STEP)
        return [
            pltpu.make_async_copy(h1.at[rows], h1_far.at[rows], sems.at[1, g]),
            pltpu.make_async_copy(s1.at[rows], s1_far.at[rows], sems.at[2, g]),
        ]

    inner = side // 2 - 1
    row_len = inner * k2
    two = 2 * k2 * 3

    def prepare():
        taps = pixel_order(w1t[...])
        edges = []
        for half in range(2):
            lines = [taps[:, 32 * (4 * half + u) : 32 * (4 * half + u + 1)] for u in range(4)]
            for place in range(REACH):
                pieces = []
                for line in lines:
                    start = 16 * (place - 1)
                    cut = line[:, max(0, -start) : min(32, 64 - start)]
                    start = max(start, 0)
                    pieces += [jnp.zeros((k1, start), F32)] if start else []
                    pieces.append(cut)
                    rest = 64 - start - cut.shape[1]
                    pieces += [jnp.zeros((k1, rest), F32)] if rest else []
                at = half * reach_rows + place * k1
                band[at : at + k1, :] = jnp.concatenate(pieces, axis=1).astype(BF16)
            edges.append(jnp.concatenate([line[:, 16:] for line in lines], axis=1))
        edge[...] = jnp.concatenate(edges, axis=0).astype(BF16)
        taps = w2t[...].astype(F32)
        blank = jnp.zeros((k2, 2 * k1), F32)
        for half in range(2):
            lines = [taps[:, 4 * k1 * (2 * half + u) : 4 * k1 * (2 * half + u + 1)] for u in range(2)]
            pieces = (
                [v for line in lines for v in (line[:, 2 * k1 :], blank)],
                lines,
                [v for line in lines for v in (blank, line[:, : 2 * k1])],
            )
            for place in range(3):
                at = (half * 3 + place) * k2
                band2[at : at + k2, :] = jnp.concatenate(pieces[place], axis=1).astype(BF16)
        bias1[...] = jnp.broadcast_to(column(table[AT_B1, 0:k1]), bias1.shape)
        bias2[...] = jnp.broadcast_to(column(table[AT_B2, 0:k2]), bias2.shape)
        held[...] = jnp.zeros_like(held)
        held2[...] = jnp.zeros_like(held2)
        h1[...] = jnp.zeros_like(h1)

    def added(sums, x, value):
        sums[x] = sums[x] + value if x in sums else value

    def second_matmul(b):
        tiles = [
            h1[pl.ds(2 * b + 1, 2), 4 * j : 4 * j + 4].reshape(LANES, LANES)
            for j in range(side // 4)
        ]
        return dot(band2[...], jnp.concatenate(tiles, axis=1))

    def second_rows(b, got):
        low, high = {}, {}
        for j in range(side // 4):
            for place in range(3):
                x = 2 * j - 1 + place
                if 0 <= x < inner:
                    span = slice(j * LANES, (j + 1) * LANES)
                    at = place * k2
                    added(low, x, got[at : at + k2, span])
                    added(high, x, got[two // 2 + at : two // 2 + at + k2, span])
        row = jnp.maximum(b - 1, 0) * row_len
        for x in range(inner):
            value, slope = soft(held2[x] + high[x] + bias2[...])
            held2[x] = low[x]
            at = pl.ds(pl.multiple_of(row + x * k2, k2), k2)
            h2[at, :] = value.astype(BF16)
            s2[at, :] = slope.astype(BF16)

    def one_step(g, carry):
        def row(r):
            return pl.multiple_of(4 * (STEP * g + r), 4)

        arrives(g).wait()
        lows, highs = [{} for _ in range(STEP)], [{} for _ in range(STEP)]

        def place_tile(r, j, got):
            for place in range(REACH):
                x = 4 * j - 1 + place
                if 0 <= x < side:
                    at = place * k1
                    added(lows[r], x, got[at : at + k1])
                    added(highs[r], x, got[reach_rows + at : reach_rows + at + k1])

        def finish(r, xs):
            for x in xs:
                value, slope = soft(held[x] + highs[r][x] + bias1[...])
                held[x] = lows[r][x]
                h1[STEP * g + r, x] = value.astype(BF16)
                s1[STEP * g + r, x] = slope.astype(BF16)

        pair = jnp.maximum(g - 1, 0)
        units = [(lambda: second_matmul(pair), lambda got: second_rows(pair, got))]

        def edges():
            parts = [tile_rows(frames, row(r), tiles, TILE) for r in range(STEP)]
            return dot(edge[...], jnp.concatenate(parts, axis=1))

        def place_edges(got):
            for r in range(STEP):
                added(lows[r], side - 1, got[:k1, r * LANES : (r + 1) * LANES])
                added(highs[r], side - 1, got[k1:, r * LANES : (r + 1) * LANES])

        units.append((edges, place_edges))

        def full(spots):
            parts = [tile_rows(frames, row(r), j, TILE) for r, j in spots]
            return dot(band[...], jnp.concatenate(parts, axis=1))

        def place_full(got, spots, ready):
            for i, (r, j) in enumerate(spots):
                place_tile(r, j, got[:, i * LANES : (i + 1) * LANES])
            if ready:
                finish(*ready)

        for r in range(STEP):
            if r % 2 == 0:
                spots = [(k, tiles - 1) for k in (r, r + 1) if k < STEP]
                units.append(
                    (
                        functools.partial(full, spots),
                        functools.partial(place_full, spots=spots, ready=None),
                    )
                )
            done = 0
            for j in range(0, tiles - 1, 2):
                spots = [(r, j), (r, j + 1)]
                ready = side if j + 2 == tiles - 1 else 4 * j + 7
                units.append(
                    (
                        functools.partial(full, spots),
                        functools.partial(place_full, spots=spots, ready=(r, range(done, ready))),
                    )
                )
                done = ready
        waiting = None
        for issue, take in units:
            got = issue()
            if waiting is not None:
                waiting[0](waiting[1])
            waiting = (take, got)
        waiting[0](waiting[1])
        for copy in leaves(g):
            copy.start()
        return carry

    prepare()
    lax.fori_loop(0, steps, one_step, 0)
    for b in range(steps - 1, side // 2):
        second_rows(b, second_matmul(b))
    for copy in last_copies[1:]:
        copy.start()
    last_copies[0].wait()
    value, slope = soft(dot_rows(lw[...], h2[...]) + column(table[AT_LB, :]))
    enc[...] = value.astype(BF16)
    s3[...] = 0.5 * slope
    for g in range(steps):
        for copy in leaves(g):
            copy.wait()
    for copy in last_copies[1:]:
        copy.wait()


def three_parts(row):
    high = row.astype(BF16).astype(F32)
    middle = (row - high).astype(BF16).astype(F32)
    return jnp.concatenate([high, middle, row - high - middle], axis=0)


def with_ones(value):
    return jnp.concatenate([value, ones_rows(value.shape[1])], axis=0)


def ones_rows(lanes):
    return (iota((16, lanes), 0) < 3).astype(F32).astype(BF16)


def plan_kernel(
    section,
    slots,
    enc,
    s3,
    h2,
    branch_far,
    value_w,
    table,
    keep,
    send_one,
    send_two,
    small,
    g3,
    parts,
    bwt,
    vht,
    vhw,
    ow,
    mine,
    pre,
    dbr,
    dval,
    low,
    hid,
    gb,
    branch_w,
    sem,
    *,
    per_pair,
    depth,
):
    width = enc.shape[0]
    options = branch_w.shape[0]
    pairs = options // 2
    two = 2 * width
    sec = section[0]
    branch_copy = pltpu.make_async_copy(branch_far, branch_w, sem)
    branch_copy.start()

    count = slots.shape[0]
    dest = jnp.concatenate(
        [table[AT_DEST + k : AT_DEST + k + 1, :] for k in range(count // LANES)], axis=1
    )
    own = jnp.where(sec == 0, dest[:, :LANES], dest[:, LANES:])
    others = jnp.transpose(jnp.broadcast_to(dest, (LANES, count)))
    index = iota((count, LANES), 1) + sec * LANES
    earlier = (others == own) & (iota((count, LANES), 0) < index)
    rank = jnp.sum(earlier.astype(F32), axis=0, keepdims=True)
    bucket = own * float(per_pair) + rank
    chosen = (iota((count, LANES), 0).astype(F32) == bucket).astype(F32).astype(BF16)
    numbers = slots[:, : mine.shape[0]]
    high = numbers.astype(BF16)
    middle = (numbers - high.astype(F32)).astype(BF16)
    rest = (numbers - high.astype(F32) - middle.astype(F32)).astype(BF16)
    mine[...] = sum(dot_rows(v, chosen) for v in (rest, middle, high))

    pad = jnp.zeros((13, width), F32)
    branch_copy.wait()
    for o in range(options):
        rows = [branch_w[o].astype(F32), three_parts(table[o : o + 1, :]), pad]
        bwt[o * width : (o + 1) * width, :] = jnp.transpose(
            0.5 * jnp.concatenate(rows, axis=0)
        ).astype(BF16)
    scalars = table[AT_SCALARS, :]
    head_w = table[AT_HW, :]
    rows = [value_w[...].astype(F32), three_parts(table[AT_VB, :]), pad]
    vht[0:width, :] = jnp.transpose(0.5 * jnp.concatenate(rows, axis=0)).astype(BF16)
    vht[width:, :] = jnp.zeros((16, width + 16), BF16)
    lane = iota((1, 16), 1)
    for k in range(2):
        bias = three_parts(jnp.broadcast_to(scalars[:, 1 + k : 2 + k], (1, 16)))
        bias = sum(jnp.where(lane == j, bias[j : j + 1], 0.0) for j in range(3))
        vht[width + k : width + k + 1, 0:width] = head_w[k : k + 1].astype(BF16)
        vht[width + k : width + k + 1, width:] = bias.astype(BF16)
    vhw[:, 0:width] = (0.5 * value_w[...].astype(F32)).astype(BF16)
    vhw[:, width:] = jnp.transpose(
        0.5 * jnp.concatenate([head_w, jnp.zeros((14, width), F32)], axis=0)
    ).astype(BF16)
    ow[...] = jnp.broadcast_to(column(table[AT_OW, :]), (width, LANES))
    wide_ow = jnp.concatenate([ow[...], ow[...]], axis=1)
    half_ow = 0.5 * wide_ow

    labels = iota((options, LANES), 0).astype(F32)
    state = enc[...].astype(F32)
    rounded_all, saved = [], []
    group = 3
    for level in range(depth):
        picked = labels == mine[level : level + 1, :]
        rounded = state.astype(BF16)
        rounded_all.append(rounded)
        met = with_ones(rounded)

        def branches(first):
            at = slice(first * two, (first + group) * two)
            pre[at, :] = dot(bwt[at, :], met)

        branches(0)
        following = state
        reward, discount, value = [], [], []

        def value_part(t, got):
            act, slope = silu_pair(got[:width])
            dval[level, t] = slope
            hidden = act.astype(BF16)
            hid[level, t] = hidden
            worth = jnp.sum(hidden.astype(F32) * wide_ow, axis=0, keepdims=True)
            for k in range(2):
                span = slice(k * LANES, (k + 1) * LANES)
                value.append(worth[:, span])
                reward.append(got[width : width + 1, span])
                discount.append(got[width + 1 : width + 2, span])

        waiting = None
        for first in range(0, pairs, group):
            if first + group < pairs:
                branches(first + group)
            boths = []
            for t in range(first, first + group):
                at = slice(t * two, (t + 1) * two)
                act, slope = silu_pair(pre[at, :])
                dbr[level, at, :] = slope
                left = state + act[:width]
                right = state + act[width:]
                following = jnp.where(picked[2 * t : 2 * t + 1], left, following)
                following = jnp.where(picked[2 * t + 1 : 2 * t + 2], right, following)
                both = with_ones(
                    jnp.concatenate([left.astype(BF16), right.astype(BF16)], axis=1)
                )
                low[level, t] = both
                boths.append(both)
            got = dot(vht[...], jnp.concatenate(boths, axis=1))
            if waiting is not None:
                for k in range(group):
                    value_part(waiting[0] + k, waiting[1][:, k * two : (k + 1) * two])
            waiting = (first, got)
        for k in range(group):
            value_part(waiting[0] + k, waiting[1][:, k * two : (k + 1) * two])
        reward = jnp.concatenate(reward, axis=0)
        discount = jax.nn.sigmoid(jnp.concatenate(discount, axis=0))
        value = jnp.concatenate(value, axis=0) + scalars[:, 3:4]
        quality = reward + discount * value
        top = jnp.max(quality, axis=0, keepdims=True)
        shifted = jnp.exp(quality - top)
        total = jnp.sum(shifted, axis=0, keepdims=True)
        live = (mine[depth : depth + 1, :] > level).astype(F32)
        chosen = picked.astype(F32)

        def target(kind):
            at = depth + 1 + kind * depth + level
            return mine[at : at + 1, :]

        reward_gap = live * (jnp.sum(chosen * reward, axis=0, keepdims=True) - target(0))
        discount_gap = live * (jnp.sum(chosen * discount, axis=0, keepdims=True) - target(1))
        plan_gap = live * (top + jnp.log(total) - target(2))
        grad_quality = plan_gap * (shifted / total)
        head_two = (chosen * discount_gap + grad_quality * value) * discount * (1.0 - discount)
        saved.append(
            (
                picked,
                (chosen * reward_gap + grad_quality).astype(BF16).astype(F32),
                head_two.astype(BF16).astype(F32),
                (grad_quality * discount).astype(BF16).astype(F32),
                reward_gap * reward_gap + discount_gap * discount_gap + plan_gap * plan_gap,
            )
        )
        state = following

    out_sum = jnp.zeros((16, width), F32)
    value_sum = jnp.zeros((width + 16, width + 16), F32)
    grad_next = None
    line = iota((16, two), 0)
    for level in reversed(range(depth)):
        picked, head_one, head_two, grad_value, _ = saved[level]
        upward = jnp.zeros((width, LANES), F32)

        def branch_part(t, moved):
            at = slice(t * two, (t + 1) * two)
            left, right = moved[:, :LANES], moved[:, LANES:]
            if grad_next is not None:
                left = left + jnp.where(picked[2 * t : 2 * t + 1], grad_next, 0.0)
                right = right + jnp.where(picked[2 * t + 1 : 2 * t + 2], grad_next, 0.0)
            grad_branch = jnp.concatenate([left, right], axis=0) * dbr[level, at, :]
            grad_branch = grad_branch.astype(BF16)
            gb[level, at, :] = grad_branch
            return left + right

        def group_part(first, moved):
            parts = [
                branch_part(first + k, moved[:, k * two : (k + 1) * two]) for k in range(group)
            ]
            at = slice(first * two, (first + group) * two)
            weights = [branch_w[o] for o in range(2 * first, 2 * (first + group))]
            return sum(parts), dot(jnp.concatenate(weights, axis=1), gb[level, at, :])

        waiting = None
        for first in range(0, pairs, group):
            stack = []
            for t in range(first, first + group):

                def across(rows):
                    return jnp.concatenate(
                        [rows[2 * t : 2 * t + 1], rows[2 * t + 1 : 2 * t + 2]], axis=1
                    )

                worth = across(grad_value)
                grad_pre = (worth * half_ow * dval[level, t]).astype(BF16)
                heads = jnp.where(line == 0, across(head_one), 0.0)
                heads = jnp.where(line == 1, across(head_two), heads)
                heads = jnp.where(line == 2, worth, heads)
                heads = heads.astype(BF16)
                out_sum = out_sum + dot_lanes(heads, hid[level, t])
                stack.append(jnp.concatenate([grad_pre, heads], axis=0))
            stack = jnp.concatenate(stack, axis=1)
            moved = dot(vhw[...], stack)
            if waiting is not None:
                one, other = group_part(*waiting)
                upward = upward + (one + 0.5 * other)
            waiting = (first, moved)
            lows = jnp.concatenate([low[level, first + k] for k in range(group)], axis=1)
            value_sum = value_sum + dot_lanes(stack, lows)
        one, other = group_part(*waiting)
        grad_next = upward + (one + 0.5 * other)

    linear_rows = h2.shape[0]
    half = (linear_rows + options * width + width) // 2
    rest = linear_rows - half
    rounded = with_ones(jnp.concatenate(rounded_all, axis=1))
    small[...] = jnp.zeros_like(small)
    if half < keep.shape[0]:
        for k in range(2):
            parts[k, half:, :] = jnp.zeros((keep.shape[0] - half, LANES), BF16)
    for t in range(pairs):
        at = slice(t * two, (t + 1) * two)
        grads = jnp.concatenate([gb[level, at, :] for level in range(depth)], axis=1)
        got = dot_lanes(rounded, grads)
        for k in range(2):
            o = 2 * t + k
            span = slice(k * width, (k + 1) * width)
            rows = slice(rest + o * width, rest + (o + 1) * width)
            parts[1 - sec, rows, :] = got[:width, span].astype(BF16)
            small[o : o + 1, :] = got[width : width + 1, span]
    after = rest + options * width
    parts[1 - sec, after : after + width, :] = jnp.transpose(value_sum[:width, :width]).astype(BF16)

    grad_three = ((2.0 * grad_next).astype(BF16).astype(F32) * s3[...]).astype(BF16)
    g3[...] = grad_three
    chunk = linear_rows // 9
    for i in range(8):
        at = slice(i * chunk, (i + 1) * chunk)
        parts[sec, at, :] = dot_lanes(h2[at, :], grad_three).astype(BF16)
    last = dot_lanes(h2[8 * chunk :, :], grad_three).astype(BF16)
    parts[sec, 8 * chunk : half, :] = last[: half - 8 * chunk]
    parts[1 - sec, 0:rest, :] = last[half - 8 * chunk :]
    keep[...] = parts[0]
    send_one[...] = parts[1, : send_one.shape[0]]
    send_two[...] = parts[1, send_one.shape[0] :]

    small[AT_VB, :] = row_of(value_sum[:width, width : width + 1])
    small[AT_OW, :] = out_sum[2:3]
    small[AT_HW, :] = value_sum[width : width + 2, :width]
    small[AT_LB, :] = row_of(jnp.sum(grad_three.astype(F32), axis=1, keepdims=True))
    loss = 0.5 * jnp.sum(sum(kept[4] for kept in saved), axis=1, keepdims=True)
    ends = [loss] + [value_sum[width + k : width + k + 1, width : width + 1] for k in range(3)]
    lane = iota((1, LANES), 1)
    line = jnp.zeros((1, LANES), F32)
    for k, end in enumerate(ends):
        line = jnp.where(lane == k, end, line)
    small[AT_SCALARS, :] = line


def back_kernel(g3, lw, s2, s1, h1, w2t, g1, c2, sums, t2, g2):
    side, k1 = s1.shape[1], s1.shape[2]
    k2 = w2t.shape[0]
    inner = side // 2 - 1
    row_len = inner * k2
    half_g3 = (0.5 * g3[...].astype(F32)).astype(BF16)
    tap, pix = iota((LANES, 256), 1), iota((LANES, 256), 0)
    for yrel in range(2):
        for p in range(3):
            hit = (
                ((tap & 15) == (pix & 15))
                & ((tap >> 6) == (pix >> 6) + 2 * (1 - yrel))
                & (((tap >> 4) & 3) == ((pix >> 4) & 3) + 2 - 2 * p)
            )
            at = (yrel * 3 + p) * k2
            taps = dot_lanes(hit.astype(F32).astype(BF16), w2t[...])
            t2[:, at : at + k2] = (0.5 * taps).astype(BF16)
    g2[0] = jnp.zeros(g2.shape[1:], BF16)
    g2[inner + 1] = jnp.zeros(g2.shape[1:], BF16)
    g1[0] = jnp.zeros(g1.shape[1:], BF16)
    g1[side + 1] = jnp.zeros(g1.shape[1:], BF16)
    zero = jnp.zeros((k2, LANES), BF16)
    total_one = jnp.zeros((k1, LANES), F32)
    total_two = jnp.zeros((k2, LANES), F32)
    for y in range(inner):
        at = slice(y * row_len, (y + 1) * row_len)
        grad = dot(lw[at, :], half_g3) * s2[at, :].astype(F32)
        grad = grad.astype(BF16).reshape(inner, k2, LANES)
        g2[y + 1] = grad
        total_two = total_two + jnp.sum(grad.astype(F32), axis=0)
    reach, cols = 5, 8
    total = jnp.zeros((2 * reach * k2, 2 * cols * k1), F32)
    grads, tiles = [], []
    for b in range(side // 2):
        cut = []
        for j in range(side // 4):
            pieces = []
            for yrel in range(2):
                for p in range(3):
                    x = 2 * j - 1 + p
                    pieces.append(g2[b + yrel, x] if 0 <= x < inner else zero)
            cut.append(jnp.concatenate(pieces, axis=0))
        got = dot(t2[...], jnp.concatenate(cut, axis=1))
        for u in range(2):
            for j in range(side // 4):
                part = got[u * 64 : (u + 1) * 64, j * LANES : (j + 1) * LANES]
                slope = s1[2 * b + u + 1, 4 * j : 4 * j + 4].astype(F32)
                grad = (part.reshape(4, k1, LANES) * slope).astype(BF16)
                g1[2 * b + u + 1, 4 * j : 4 * j + 4] = grad
                total_one = total_one + jnp.sum(grad.astype(F32), axis=0)
        for j in range(-(-side // cols)):
            end = min((j + 1) * cols, side)
            tile = h1[2 * b + 1 : 2 * b + 3, j * cols : end]
            if end < (j + 1) * cols:
                rest = jnp.zeros((2, (j + 1) * cols - end, k1, LANES), BF16)
                tile = jnp.concatenate([tile, rest], axis=1)
            tiles.append(tile.reshape(2 * cols * k1, LANES))
            pieces = []
            for half in range(2):
                for p in range(reach):
                    x = 4 * j - 1 + p
                    pieces.append(g2[b + 1 - half, x] if 0 <= x < inner else zero)
            grads.append(jnp.concatenate(pieces, axis=0))
        if b % 2:
            total = total + dot_lanes(
                jnp.concatenate(grads, axis=1), jnp.concatenate(tiles, axis=1)
            )
            grads, tiles = [], []
    line = 4 * k1
    for half in range(2):
        for u in range(2):
            tap_row = jnp.zeros((k2, line), F32)
            for p in range(reach):
                at = (half * reach + p) * k2
                part = total[at : at + k2, u * 2 * line : (u + 1) * 2 * line]
                start = 2 * k1 * (p - 1)
                piece = part[:, max(start, 0) : min(start + line, 2 * line)]
                if start < 0:
                    piece = jnp.concatenate([jnp.zeros((k2, -start), F32), piece], axis=1)
                if start + line > 2 * line:
                    rest = jnp.zeros((k2, start - line), F32)
                    piece = jnp.concatenate([piece, rest], axis=1)
                tap_row = tap_row + piece
            at = (2 * half + u) * line
            c2[:, at : at + line] = tap_row
    sums[...] = jnp.zeros_like(sums)
    sums[0:1, 0:k1] = row_of(jnp.sum(total_one, axis=1, keepdims=True))
    sums[1:2, 0:k2] = row_of(jnp.sum(total_two, axis=1, keepdims=True))


def pixel_band(sec, w1t, channels):
    k1 = w1t.shape[0]
    rows = 64 * channels
    row, tap = iota((rows, 256), 0), iota((rows, 256), 1)
    moves = ((tap >> 6) == row % channels + sec * channels) & ((tap & 63) == row // channels)
    taps = dot_lanes(moves.astype(F32).astype(BF16), w1t)
    line, span = COLS * channels, 8 * channels
    blocks = {}
    for half in range(2):
        for p in range(NEAR):
            pieces = []
            for u in range(4):
                at = (4 * half + u) * span
                start = 4 * (p - 1) * channels
                cut = taps[at + max(0, -start) : at + min(span, line - start)]
                start = max(start, 0)
                pieces += [jnp.zeros((start, k1), F32)] if start else []
                pieces.append(cut)
                rest = line - start - cut.shape[0]
                pieces += [jnp.zeros((rest, k1), F32)] if rest else []
            blocks[half, p] = jnp.concatenate(pieces, axis=0)
    zero = jnp.zeros((4 * line, k1), F32)
    lines = []
    for r in range(STEP):
        cols = [
            blocks.get((r + 1 - yrel, p), zero) for yrel in range(STEP + 1) for p in range(NEAR)
        ]
        lines.append(jnp.concatenate(cols, axis=1))
    return jnp.concatenate(lines, axis=0).astype(BF16)


def first_kernel(
    section,
    frames_far,
    g1,
    w1t,
    other_far,
    after,
    c1,
    out,
    band,
    frames,
    acc,
    other,
    held,
    sems,
    draw_sems,
    *,
    draw,
):
    side, k1 = g1.shape[1], g1.shape[2]
    img, _, channels, _ = frames.shape
    steps = img // 4 // STEP
    arrives = frame_copies(section, frames_far, frames, sems)
    for g in range(steps):
        arrives(g).start()
    other_copy = pltpu.make_async_copy(
        other_far.at[0 : STEP * draw + 1], other, sems.at[steps]
    )
    other_copy.start()
    acc[...] = jnp.zeros_like(acc)
    zero = jnp.zeros((k1, LANES), BF16)

    def one_step(g, carry):
        arrives(g).wait()
        pixels, grads = [], []
        for j in range(img // COLS):
            rows = [pl.multiple_of(4 * (STEP * g + r), 4) for r in range(STEP)]
            pixels.append(
                jnp.concatenate([tile_rows(frames, row, j, COLS) for row in rows], axis=0)
            )
            pieces = []
            for yrel in range(STEP + 1):
                for p in range(NEAR):
                    x = 3 * j - 1 + p
                    pieces.append(g1[STEP * g + yrel, x] if 0 <= x < side else zero)
            grads.append(jnp.concatenate(pieces, axis=0))
        acc[...] += dot_lanes(jnp.concatenate(pixels, axis=1), jnp.concatenate(grads, axis=1))
        return carry

    lax.fori_loop(0, steps, one_step, 0)
    band[...] = pixel_band(section[0], w1t[...], out.shape[2])
    other_copy.wait()
    finish = draw_steps(section, band, g1, 0, other, 0, out, held, draw_sems, 0, draw)
    fold_first(acc, c1, channels, k1)
    finish()


def fold_first(acc, c1, channels, k1):
    line = COLS * channels
    step = 4 * channels
    taps = []
    for half in range(2):
        total = sum(
            acc[r * 4 * line : (r + 1) * 4 * line, :][
                :, (r + 1 - half) * NEAR * k1 : (r + 2 - half) * NEAR * k1
            ]
            for r in range(STEP)
        )
        for u in range(4):
            part = total[u * line : (u + 1) * line]
            cols = [part[:, p * k1 : (p + 1) * k1] for p in range(NEAR)]
            taps.append(cols[1][0:step] + cols[2][step : 2 * step] + cols[3][2 * step :])
            taps.append(cols[0][0:step] + cols[1][step : 2 * step] + cols[2][2 * step :])
    row, col = iota((256, 256), 0), iota((256, 256), 1)
    moves = ((row & 3) == (col >> 6)) & ((row >> 2) == (col & 63))
    grad = dot_rows(jnp.concatenate(taps, axis=0), moves.astype(F32), EXACT)
    for half in range(2):
        c1[half * k1 : (half + 1) * k1, :] = grad[:, half * LANES : (half + 1) * LANES].astype(BF16)


def draw_steps(section, band, mine, mine_at, other, other_at, out, held, sems, start, steps):
    side, k1 = mine.shape[1], mine.shape[2]
    img, channels = out.shape[1], out.shape[2]
    sec = section[0]
    line = COLS * channels
    flat = held.reshape(2, 2, 4 * STEP, img * channels, LANES)

    def writes(g):
        rows = slice(4 * STEP * (start + g), 4 * STEP * (start + g + 1))
        places = (sec * LANES, (1 - sec) * LANES)
        return [
            pltpu.make_async_copy(
                held.at[g % 2, k],
                out.at[rows, :, :, pl.ds(pl.multiple_of(places[k], LANES), LANES)],
                sems.at[g % 2, k],
            )
            for k in range(2)
        ]

    zero = jnp.zeros((k1, 2 * LANES), BF16)
    for g in range(steps):
        if g >= 2:
            for copy in writes(g - 2):
                copy.wait()
        for j in range(img // COLS):
            pieces = []
            for yrel in range(STEP + 1):
                for p in range(NEAR):
                    x, y = 3 * j - 1 + p, STEP * (start + g) + yrel
                    if 0 <= x < side:
                        pair = [mine[y - mine_at, x], other[y - other_at, x]]
                        pieces.append(jnp.concatenate(pair, axis=1))
                    else:
                        pieces.append(zero)
            got = dot(band[...], jnp.concatenate(pieces, axis=0))
            for k in range(4 * STEP):
                at = slice(k * line, (k + 1) * line)
                span = slice(j * line, (j + 1) * line)
                flat[g % 2, 0, k, span, :] = got[at, :LANES]
                flat[g % 2, 1, k, span, :] = got[at, LANES:]
        for copy in writes(g):
            copy.start()

    def finish():
        for g in range(max(steps - 2, 0), steps):
            for copy in writes(g):
                copy.wait()

    return finish


def pixels_kernel(section, band, mine, other_far, after, done, out, token, held, other, sems, *, start):
    steps = other.shape[0] // STEP
    fetch = pltpu.make_async_copy(
        other_far.at[STEP * start : STEP * (start + steps) + 1], other, sems.at[2, 0]
    )
    fetch.start()
    token[...] = jnp.zeros_like(token)
    fetch.wait()
    draw_steps(
        section, band, mine, 0, other, STEP * start, out, held, sems, start, steps
    )()


def two_parts(value):
    high = value.astype(BF16).astype(F32)
    return jnp.concatenate([high, value - high], axis=0).astype(BF16)


def one_part(pair):
    rows = pair.shape[0] // 2
    pair = pair.astype(F32)
    return pair[:rows] + pair[rows:]


def merge_kernel(keep, recv_one, recv_two, small, c2, sums, out_far, lines, out, sems):
    members = out.shape[0]
    size = keep.shape[0] // members
    lines[...] = small[...]
    lines[AT_B1, :] = sums[0:1, :]
    lines[AT_B2, :] = sums[1:2, :]
    for k in range(members):
        at = slice(k * size, (k + 1) * size)
        recv, here = recv_one, k
        if k >= members // 2:
            recv, here = recv_two, k - members // 2
        got = recv[here * size : (here + 1) * size, :]
        out[k, 0:size, :] = keep[at, :] + got
        if k < members // 2:
            rows, span = c2_place(k)
            out[k, size:, :] = c2[rows, span].astype(BF16)
        else:
            out[k, size:, :] = two_parts(lines[table_place(k), :])
        pltpu.make_async_copy(out.at[k], out_far.at[k], sems.at[k]).start()
    for k in range(members):
        pltpu.make_async_copy(out.at[k], out_far.at[k], sems.at[k]).wait()


def c2_place(k):
    return slice(k % 2 * SHORT, (k % 2 + 1) * SHORT), slice(k // 2 * LANES, (k // 2 + 1) * LANES)


def table_place(k):
    at = (k - CUBE // 2) * SHORT // 2
    return slice(at, at + SHORT // 2)


def riders(batch, parts):
    plain = sum(p.astype(F32) for p in parts).astype(BF16)
    fine = two_parts(sum(one_part(p) for p in parts))
    return jnp.where(batch[0] % CUBE < CUBE // 2, plain.astype(F32), fine.astype(F32)).astype(BF16)


def cube_kernel(batch, got, c1, out):
    members = got.shape[0]
    size = got.shape[1] - SHORT
    out[0:size, :] = sum(got[k, 0:size, :].astype(F32) for k in range(members)).astype(BF16)
    out[size : size + SHORT, :] = riders(batch, [got[k, size:, :] for k in range(members)])
    out[size + SHORT :, :] = c1[...]


def add_kernel(batch, a, b, after, out):
    size = a.shape[0] - SHORT - 32
    for span in (slice(0, size), slice(size + SHORT, a.shape[0])):
        out[span, :] = (a[span, :].astype(F32) + b[span, :].astype(F32)).astype(BF16)
    ride = slice(size, size + SHORT)
    out[ride, :] = riders(batch, [a[ride, :], b[ride, :]])


def relay_kernel(batch, *refs):
    parts, (one, two, out) = refs[:CUBE], refs[-3:]
    me = batch[0] % CUBE
    for k, part in zip(TURNS, parts):
        out[me ^ k] = part[...]
    one[...] = out[: CUBE // 2]
    two[...] = out[CUBE // 2 :]


def piece_of(got, k):
    count = got[0].shape[0]
    return got[k // count].at[k % count]


def unpack_half(which, got, lw, bw, vw, stage, stage_b, sems):
    members = 2 * got[0].shape[0]
    size = stage.shape[0] // members
    linear_rows, width = lw.shape
    options = bw.shape[0]
    half = (linear_rows + options * width + width) // 2
    rest = linear_rows - half
    group = options // 3

    def first_copies():
        spans = [(k * size, min((k + 1) * size, half)) for k in range(members)]
        return [
            pltpu.make_async_copy(stage.at[a:b], lw.at[a:b], sems.at[k])
            for k, (a, b) in enumerate(spans)
        ]

    def second_copies():
        copies = [pltpu.make_async_copy(stage.at[0:rest], lw.at[half:], sems.at[0])]
        for k in range(options // group):
            part = slice(k * group, (k + 1) * group)
            copies.append(pltpu.make_async_copy(stage_b.at[part], bw.at[part], sems.at[1 + k]))
        last = stage.at[rest : rest + width]
        copies.append(pltpu.make_async_copy(last, vw, sems.at[len(copies)]))
        return copies

    @pl.when(which == 0)
    def _():
        for k, copy in enumerate(first_copies()):
            start, end = k * size, min((k + 1) * size, half)
            stage[start:end, :] = piece_of(got, k)[0 : end - start, :].astype(F32)
            copy.start()

    @pl.when(which == 1)
    def _():
        def rows(start, end):
            parts = []
            while start < end:
                k, at = start // size, start % size
                count = min(size - at, end - start)
                parts.append(piece_of(got, k)[at : at + count, :])
                start += count
            value = parts[0] if len(parts) == 1 else jnp.concatenate(parts, axis=0)
            return value.astype(F32)

        copies = second_copies()
        stage[0:rest, :] = rows(0, rest)
        copies[0].start()
        for o in range(options):
            stage_b[o] = rows(rest + o * width, rest + (o + 1) * width)
            if o % group == group - 1:
                copies[1 + o // group].start()
        at = rest + options * width
        stage[rest : rest + width, :] = rows(at, at + width)
        copies[-1].start()

    def finish():
        for half_at, copies in ((0, first_copies), (1, second_copies)):

            @pl.when(which == half_at)
            def _():
                for copy in copies():
                    copy.wait()

    return finish


def own_kernel(section, one, two, lw, bw, vw, stage, stage_b, sems):
    unpack_half(section[0], (one, two), lw, bw, vw, stage, stage_b, sems)()


def unpack_kernel(section, *refs):
    mine, other, refs = refs[0:2], refs[2:4], refs[4:]
    lw, bw, vw = refs[3:6]
    little = (len(refs) - 10) // 2
    far, near = refs[6 : 6 + little], refs[6 + little : 6 + 2 * little]
    loss, c1, b1, c2, b2, lb, bb, hw, hb, vb, ow, ob = near
    stage, stage_b, lines, sems = refs[-4:]
    options = bw.shape[0]
    k1, k2 = c1.shape[0], c2.shape[0]
    size = stage.shape[0] // CUBE
    finish = unpack_half(1 - section[0], other, lw, bw, vw, stage, stage_b, sems)
    grad = [jnp.zeros((k1, LANES), F32) for _ in range(2)]
    ride = slice(size, size + SHORT)
    for k in range(CUBE):
        views = piece_of(mine, k), piece_of(other, k)
        if k < CUBE // 2:
            c2[c2_place(k)] = sum(v[ride, :].astype(F32) for v in views)
        else:
            lines[table_place(k), :] = sum(one_part(v[ride, :]) for v in views)
        for view in views:
            for h in range(2):
                at = size + SHORT + h * k1
                grad[h] += view[at : at + k1, :].astype(F32)
    for part in range(2):
        c1[:, part * LANES : (part + 1) * LANES] = grad[part]
    bb[...] = lines[0:options, :]
    vb[...] = lines[AT_VB, :]
    ow[...] = lines[AT_OW, :]
    hw[...] = lines[AT_HW, :]
    lb[...] = lines[AT_LB, :]
    scalars = lines[AT_SCALARS, :]
    loss[...] = scalars[:, 0:1]
    hb[...] = scalars[:, 1:3]
    ob[...] = scalars[:, 3:4]
    b1[...] = lines[AT_B1, 0:k1]
    b2[...] = lines[AT_B2, 0:k2]
    copies = [
        pltpu.make_async_copy(a, b, sems.at[CUBE + k]) for k, (a, b) in enumerate(zip(near, far))
    ]
    for copy in copies:
        copy.start()
    finish()
    for copy in copies:
        copy.wait()


def numbers_kernel(
    options,
    depth,
    targets,
    destination,
    b1,
    b2,
    lb,
    bb,
    hw,
    vb,
    ow,
    hb,
    ob,
    out,
    table,
):
    levels, kinds = options.shape[0], targets.shape[0]
    slots = depth.shape[1]
    rows = [options[...].astype(F32), depth[...].astype(F32)]
    rows += [targets[k] for k in range(kinds)]
    rows.append(jnp.zeros((LANES - levels - 1 - kinds * levels, slots), F32))
    out[...] = jnp.transpose(jnp.concatenate(rows, axis=0))
    table[...] = jnp.zeros_like(table)
    table[0 : bb.shape[0], :] = bb[...]
    table[AT_VB, :] = vb[...]
    table[AT_OW, :] = ow[...].astype(F32)
    table[AT_HW, :] = hw[...].astype(F32)
    table[AT_LB, :] = lb[...]
    table[AT_B1, 0 : b1.shape[1]] = b1[...]
    table[AT_B2, 0 : b2.shape[1]] = b2[...]
    lane = iota((1, LANES), 1)
    scalars = jnp.zeros((1, LANES), F32)
    for k, value in ((1, hb[:, 0:1]), (2, hb[:, 1:2]), (3, ob[...])):
        scalars = jnp.where(lane == k, value, scalars)
    table[AT_SCALARS, :] = scalars
    for k in range(slots // LANES):
        part = destination[:, k * LANES : (k + 1) * LANES]
        table[AT_DEST + k : AT_DEST + k + 1, :] = part.astype(F32)


def whole(shape):
    zeros = (0,) * len(shape)
    return pl.BlockSpec(shape, lambda *_: zeros)


ANYWHERE = pl.BlockSpec(memory_space=pl.ANY)
SCALARS = pl.BlockSpec(memory_space=pltpu.SMEM)


def params():
    return pltpu.CompilerParams(vmem_limit_bytes=VMEM_BYTES)


def shape_of(*shape, dtype=F32):
    return jax.ShapeDtypeStruct(shape, dtype)


def cost(microseconds):
    return pl.CostEstimate(
        flops=int(1.1e9 * microseconds), bytes_accessed=int(3.6e6 * microseconds), transcendentals=0
    )


def stays(value):
    return pltpu.with_memory_space_constraint(value, pltpu.HBM)


def held_near(value):
    return pltpu.with_memory_space_constraint(value, pltpu.VMEM)


def encode(section, frames, w1t, w2t, lw, table):
    img = frames.shape[0]
    blocks = img // 4
    side = blocks - 1
    k1, k2, width = w1t.shape[0], w2t.shape[0], lw.shape[1]
    flat = lw.shape[0]
    vmem = pltpu.VMEM
    near = pl.BlockSpec(memory_space=vmem)
    grid_one = (blocks, side, k1, LANES)
    return pl.pallas_call(
        encode_kernel,
        in_specs=[SCALARS, ANYWHERE, near, near, ANYWHERE, near],
        out_specs=[ANYWHERE] * 3 + [near] * 3,
        out_shape=(
            pltpu.HBM(grid_one, BF16),
            pltpu.HBM(grid_one, BF16),
            pltpu.HBM((flat, LANES), BF16),
            shape_of(flat, LANES, dtype=BF16),
            shape_of(width, LANES, dtype=BF16),
            shape_of(width, LANES),
        ),
        scratch_shapes=[
            vmem((img, img, frames.shape[2], LANES), BF16),
            vmem(lw.shape, BF16),
            vmem(grid_one, BF16),
            vmem(grid_one, BF16),
            vmem((flat, LANES), BF16),
            vmem((2 * REACH * k1, 256), BF16),
            vmem((2 * k1, 64), BF16),
            vmem((6 * k2, LANES), BF16),
            vmem((k1, LANES), F32),
            vmem((k2, LANES), F32),
            vmem((side, k1, LANES), F32),
            vmem((side // 2 - 1, k2, LANES), F32),
            pltpu.SemaphoreType.DMA((4, max(blocks // STEP, 3))),
        ],
        compiler_params=params(),
        cost_estimate=cost(9),
        name="encode",
    )(section, frames, w1t, w2t, lw, table)


def plan(section, slots, enc, s3, h2, branch_w, value_w, table, per_pair, depth, half_rows):
    width = enc.shape[0]
    options = branch_w.shape[0]
    two = 2 * width
    pairs = options // 2
    outs = (
        shape_of(half_rows, LANES, dtype=BF16),
        shape_of(half_rows // 2, LANES, dtype=BF16),
        shape_of(half_rows // 2, LANES, dtype=BF16),
        shape_of(TABLE, LANES),
        shape_of(width, LANES, dtype=BF16),
    )
    vmem = pltpu.VMEM
    near = pl.BlockSpec(memory_space=vmem)
    return pl.pallas_call(
        functools.partial(plan_kernel, per_pair=per_pair, depth=depth),
        in_specs=[SCALARS, near, near, near, near, ANYWHERE, near, near],
        out_shape=outs,
        scratch_shapes=[
            vmem((2, half_rows, LANES), BF16),
            vmem((options * width, width + 16), BF16),
            vmem((width + 16, width + 16), BF16),
            vmem((width, width + 16), BF16),
            vmem((width, LANES), F32),
            vmem((16, LANES), F32),
            vmem((options * width, LANES), F32),
            vmem((depth, options * width, LANES), F32),
            vmem((depth, pairs, width, two), F32),
            vmem((depth, pairs, width + 16, two), BF16),
            vmem((depth, pairs, width, two), BF16),
            vmem((depth, options * width, LANES), BF16),
            vmem(branch_w.shape, BF16),
            pltpu.SemaphoreType.DMA,
        ],
        compiler_params=params(),
        cost_estimate=cost(11),
        name="plan",
    )(section, slots, enc, s3, h2, branch_w, value_w, table)


def back(g3, lw, s2, s1, h1, w2t):
    _, side, k1 = s1.shape[:3]
    k2 = w2t.shape[0]
    inner = side // 2 - 1
    padded = (side + 2, side, k1, LANES)
    near = pl.BlockSpec(memory_space=pltpu.VMEM)
    return pl.pallas_call(
        back_kernel,
        in_specs=[near] * 6,
        out_shape=(shape_of(*padded, dtype=BF16), shape_of(k2, 256), shape_of(8, LANES)),
        scratch_shapes=[
            pltpu.VMEM((LANES, 6 * k2), BF16),
            pltpu.VMEM((inner + 2, inner, k2, LANES), BF16),
        ],
        compiler_params=params(),
        cost_estimate=cost(25),
        name="back",
    )(g3, lw, s2, s1, h1, w2t)


def first(section, frames, g1, w1t, other, after, channels, draw):
    img, _, stack, _ = frames.shape
    k1 = g1.shape[2]
    band = (STEP * 4 * COLS * channels, (STEP + 1) * NEAR * k1)
    near = pl.BlockSpec(memory_space=pltpu.VMEM)
    return pl.pallas_call(
        functools.partial(first_kernel, draw=draw),
        in_specs=[SCALARS, ANYWHERE, near, near, ANYWHERE, ANYWHERE],
        out_specs=[near, ANYWHERE, near],
        out_shape=[
            shape_of(2 * k1, LANES, dtype=BF16),
            shape_of(img, img, channels, 2 * LANES),
            shape_of(*band, dtype=BF16),
        ],
        scratch_shapes=[
            pltpu.VMEM((img, img, stack, LANES), BF16),
            pltpu.VMEM((STEP * 4 * COLS * stack, (STEP + 1) * NEAR * k1), F32),
            pltpu.VMEM((STEP * draw + 1,) + g1.shape[1:], BF16),
            pltpu.VMEM((2, 2, 4 * STEP, img, channels, LANES), F32),
            pltpu.SemaphoreType.DMA((img // 4 // STEP + 1,)),
            pltpu.SemaphoreType.DMA((2, 2)),
        ],
        compiler_params=params(),
        cost_estimate=cost(45),
        name="first",
    )(section, frames, g1, w1t, other, after)


def pixels(section, band, mine, other, after, done, start, steps):
    img, _, channels, _ = done.shape
    near = pl.BlockSpec(memory_space=pltpu.VMEM)
    return pl.pallas_call(
        functools.partial(pixels_kernel, start=start),
        in_specs=[SCALARS, near, near, ANYWHERE, ANYWHERE, ANYWHERE],
        out_specs=[ANYWHERE, near],
        out_shape=[shape_of(*done.shape), shape_of(8, LANES)],
        scratch_shapes=[
            pltpu.VMEM((2, 2, 4 * STEP, img, channels, LANES), F32),
            pltpu.VMEM((STEP * steps + 1,) + mine.shape[1:], BF16),
            pltpu.SemaphoreType.DMA((3, 2)),
        ],
        input_output_aliases={5: 0},
        compiler_params=params(),
        cost_estimate=cost(1 + 0.9 * steps),
        name="pixels",
    )(section, band, mine, other, after, done)


def small_call(
    kernel, outs, operands, scratch=(), name=None, place=None, after=(), weight=0.3, far=False
):
    specs = [pl.BlockSpec(memory_space=pltpu.VMEM)] * len(operands)
    if place is not None:
        operands = (*place, *operands)
        specs = [pl.BlockSpec(memory_space=pltpu.SMEM)] * len(place) + specs
    return pl.pallas_call(
        kernel,
        in_specs=specs + [ANYWHERE] * len(after),
        out_specs=jax.tree.map(
            lambda _: ANYWHERE if far else pl.BlockSpec(memory_space=pltpu.VMEM), outs
        ),
        out_shape=outs,
        scratch_shapes=list(scratch),
        compiler_params=params(),
        cost_estimate=cost(weight),
        name=name,
    )(*operands, *after)


def round_up(value, step):
    return -(-value // step) * step


def swapped(value):
    return lax.ppermute(value, "section", [(0, 1), (1, 0)])


def exchanged(value, groups=None):
    return lax.all_to_all(
        value, "batch", split_axis=0, concat_axis=0, axis_index_groups=groups, tiled=True
    )


def partner(value, distance):
    count = lax.axis_size("batch")
    return lax.ppermute(value, "batch", [(b, b ^ distance) for b in range(count)])


def local(
    frames,
    destination,
    options,
    depth,
    targets,
    conv_one,
    bias_one,
    conv_two,
    bias_two,
    linear_w,
    linear_b,
    branch_w,
    branch_b,
    head_w,
    head_b,
    value_w,
    value_b,
    out_w,
    out_b,
):
    section = lax.axis_index("section").astype(jnp.int32)[None]
    peers = lax.axis_size("batch")
    frame_count = frames.shape[3]
    per_pair = frame_count // peers
    levels = options.shape[0]
    frames = stays(frames.transpose(1, 2, 0, 3))
    w1t, w2t = stays(conv_one.T), stays(conv_two.T)
    branch_w, value_w = stays(branch_w), stays(value_w)
    encoder_params = (w1t, bias_one, w2t, bias_two, linear_w, linear_b)
    planner_params = (branch_w, branch_b, head_w.T, head_b, value_w, value_b, out_w.T, out_b)
    width = linear_w.shape[1]
    big_rows = linear_w.shape[0] + (branch_w.shape[0] + 1) * width
    size = round_up(-(-big_rows // (2 * CUBE)), 16)

    tiny = (bias_one, bias_two, linear_b, branch_b, head_w.T, value_b, out_w.T)
    tiny = [stays(v if v.ndim > 1 else v[None, :]) for v in tiny]
    numbers, table = pl.pallas_call(
        numbers_kernel,
        in_specs=[pl.BlockSpec(memory_space=pltpu.VMEM)] * (6 + len(tiny)),
        out_shape=[shape_of(frame_count, LANES), shape_of(TABLE, LANES)],
        compiler_params=params(),
        cost_estimate=cost(1),
        name="numbers",
    )(
        stays(options),
        stays(depth[None, :]),
        stays(targets),
        stays(destination[None, :]),
        *tiny,
        stays(head_b[None, :]),
        out_b[None, :],
    )
    slots = exchanged(numbers.reshape(peers, per_pair, LANES)).reshape(frame_count, LANES)

    h1, s1, s2, h2, enc, s3 = encode(section, frames, w1t, w2t, stays(linear_w), table)
    keep, send_one, send_two, small, g3 = plan(
        section, slots, enc, s3, h2, branch_w, value_w, table, per_pair, levels, CUBE * size
    )
    recv = swapped(send_one), swapped(send_two)
    channels = frames.shape[2] // lax.axis_size("section")
    g1, c2, sums = back(g3, linear_w, s2, s1, h1, w2t)
    other = swapped(g1)
    g1 = held_near(g1)
    place = (lax.axis_index("batch").astype(jnp.int32)[None],)
    cubes = [list(range(c, c + CUBE)) for c in range(0, peers, CUBE)]
    bf16 = functools.partial(shape_of, dtype=BF16)
    pieces = small_call(
        merge_kernel,
        bf16(CUBE, size + SHORT, LANES),
        (keep, *recv, small, c2, sums),
        [
            pltpu.VMEM((TABLE, LANES), F32),
            pltpu.VMEM((CUBE, size + SHORT, LANES), BF16),
            pltpu.SemaphoreType.DMA((CUBE,)),
        ],
        name="merge",
        far=True,
        weight=30,
    )
    got = exchanged(pieces, cubes)
    c1, frames_grad, band = first(section, frames, g1, w1t, other, pieces, channels, DRAW)
    piece = bf16(size + SHORT + c1.shape[0], LANES)
    keep = small_call(cube_kernel, piece, (got, c1), name="cube", place=place)
    distance = CUBE
    while distance < peers:
        recv = partner(keep, distance)
        if distance == CUBE:
            frames_grad, token = pixels(
                section, band, g1, other, keep, frames_grad, DRAW, DRAW_ACROSS
            )
        distance *= 2
        keep = small_call(
            add_kernel, piece, (keep, recv), name="add", place=place, after=(token,)
        )
    parts = [partner(keep, k) if k else keep for k in TURNS]
    drawn = DRAW + DRAW_ACROSS
    left = frames.shape[0] // 4 // STEP - drawn
    frames_grad, token = pixels(section, band, g1, other, keep, frames_grad, drawn, left)
    got = small_call(
        relay_kernel,
        [bf16(CUBE // 2, *piece.shape)] * 2,
        parts,
        [pltpu.VMEM((CUBE, *piece.shape), BF16)],
        name="relay",
        place=place,
        after=(token,),
    )
    got_other = [swapped(v) for v in got]
    shapes = [p.shape for p in encoder_params + planner_params]
    near = pl.BlockSpec(memory_space=pltpu.VMEM)
    flat = [shape_of(*(v if len(v) > 1 else (1,) + v)) for v in [(1, 1)] + shapes]
    large = [flat[k] for k in (5, 7, 11)]
    staged = [
        pltpu.VMEM((CUBE * size, LANES), F32),
        pltpu.VMEM(branch_w.shape, F32),
    ]
    little = [v for k, v in enumerate(flat) if k not in (5, 7, 11)]
    sems = pltpu.SemaphoreType.DMA((CUBE + len(little),))
    begun = pl.pallas_call(
        own_kernel,
        in_specs=[SCALARS, near, near],
        out_specs=[ANYWHERE] * 3,
        out_shape=large,
        scratch_shapes=[*staged, sems],
        compiler_params=params(),
        cost_estimate=cost(1),
        name="own",
    )(section, *got)
    ends = pl.pallas_call(
        unpack_kernel,
        in_specs=[SCALARS] + [near] * 4 + [ANYWHERE] * 3,
        out_specs=[ANYWHERE] * (3 + len(little)),
        out_shape=large + little,
        scratch_shapes=[pltpu.VMEM(v.shape, F32) for v in little]
        + [*staged, pltpu.VMEM((TABLE, LANES), F32), sems],
        input_output_aliases={5: 0, 6: 1, 7: 2},
        compiler_params=params(),
        cost_estimate=cost(1.5),
        name="unpack",
    )(section, *got, *got_other, *begun)
    rest = list(ends[3:])
    for k, at in enumerate((5, 7, 11)):
        rest.insert(at, ends[k])
    rest = [v.reshape(s) for v, s in zip(rest, [()] + shapes)]
    for at in (1, 3, 9, 13):
        rest[at] = rest[at].T
    return (rest[0], frames_grad.transpose(2, 0, 1, 3), *rest[1:])


def solution(mesh):
    placed = (
        P(None, None, None, "batch"),
        P("batch"),
        P(None, "batch"),
        P("batch"),
        P(None, None, "batch"),
    ) + (P(),) * 14
    return jax.shard_map(
        local,
        mesh=mesh,
        in_specs=placed,
        out_specs=(P(), P("section", None, None, "batch")) + (P(),) * 14,
        check_vma=False,
    )
```
